32 devices in a mesh: rows: 2 (over core), batch: 16 (over z, y, x).
Axes of the slice: x: 2, y: 2, z: 4, core: 2. Of those that a mesh axis runs over, the one named last changes fastest.
Arguments:
- images: bfloat16 [32, 56, 56, 256], P('batch', 'rows'), may hold values from -6 to 6
- w_1a: bfloat16 [256, 128], replicated, may hold values from -0.375 to 0.375
- w_1b: bfloat16 [3, 3, 128, 128], replicated, may hold values from -0.1875 to 0.1875
- w_1c: bfloat16 [128, 512], replicated, may hold values from -0.5 to 0.5
- w_1p: bfloat16 [256, 512], replicated, may hold values from -0.375 to 0.375
- w_2a: bfloat16 [512, 128], replicated, may hold values from -0.25 to 0.25
- w_2b: bfloat16 [3, 3, 128, 128], replicated, may hold values from -0.1875 to 0.1875
- w_2c: bfloat16 [128, 512], replicated, may hold values from -0.5 to 0.5
- norm_1a: float32 [2, 3, 128], replicated, may hold values from 0.5 to 1.5
- norm_1b: float32 [2, 3, 128], replicated, may hold values from 0.5 to 1.5
- norm_1c: float32 [2, 3, 512], replicated, may hold values from 0.5 to 1.5
- norm_1p: float32 [2, 3, 512], replicated, may hold values from 0.5 to 1.5
- norm_2a: float32 [2, 3, 128], replicated, may hold values from 0.5 to 1.5
- norm_2b: float32 [2, 3, 128], replicated, may hold values from 0.5 to 1.5
- norm_2c: float32 [2, 3, 512], replicated, may hold values from 0.5 to 1.5
- cotangent: bfloat16 [32, 28, 28, 512], P(('batch', 'rows')), may hold values from -6 to 6
- group: int32 [32], P('batch'), may hold values from 0 to 2, as said below
- width: int32 [3], replicated, may hold values from 2 to 4
- gate: int32 [3], replicated, may hold values from 0 to 4, as said below
Outputs:
- result: bfloat16 [32, 28, 28, 512], P(('batch', 'rows'))
- grad_images: bfloat16 [32, 56, 56, 256], P('batch', 'rows')
- grad_w_1a: float32 [256, 128], replicated
- grad_w_1b: float32 [3, 3, 128, 128], replicated
- grad_w_1c: float32 [128, 512], replicated
- grad_w_1p: float32 [256, 512], replicated
- grad_w_2a: float32 [512, 128], replicated
- grad_w_2b: float32 [3, 3, 128, 128], replicated
- grad_w_2c: float32 [128, 512], replicated
- grad_norm_1a: float32 [2, 3, 128], replicated
- grad_norm_1b: float32 [2, 3, 128], replicated
- grad_norm_1c: float32 [2, 3, 512], replicated
- grad_norm_1p: float32 [2, 3, 512], replicated
- grad_norm_2a: float32 [2, 3, 128], replicated
- grad_norm_2b: float32 [2, 3, 128], replicated
- grad_norm_2c: float32 [2, 3, 512], replicated
The draws below stay inside these ranges and needn't reach their ends.
Inputs may be any that keep to these rules, and one draw needn't show every extreme that they name: Every group holds at least one image. One group has gate 0, one has gate 4, the third 1 to 3.
All inputs are finite; a program needn't handle non-finite values.
Results may differ from the reference program's by a relative error of at most 0.015.
Values may be sent and summed in bfloat16 or wider, within the bound.
No kernel may reach another device: no remote copies, remote signals or barrier semaphores. Data moves between devices by JAX's collectives and lax.ppermute only.
A program may use at most 128 MiB of HBM per device.

```python
import jax
import jax.numpy as jnp
from jax import lax

C_IN = 256
C_MID = 128
C_OUT = 512
GROUPS = 3
HIN = 56
HOUT = 28
IMAGES = 32


def draw_group(key, part):
    key = jax.random.fold_in(key, 11)
    levels = jax.random.randint(jax.random.fold_in(key, 1), (IMAGES,), 0, 9)
    labels = jnp.where(levels < 1, 0, jnp.where(levels < 6, 1, 2)).astype(jnp.int32)
    ordering = jax.random.permutation(jax.random.fold_in(key, 2), IMAGES)
    labels = labels.at[ordering[:GROUPS]].set(jnp.arange(GROUPS, dtype=jnp.int32))
    return labels


def draw_gate(key, part):
    key = jax.random.fold_in(key, 23)
    ordering = jax.random.permutation(jax.random.fold_in(key, 1), GROUPS)
    middle = jax.random.randint(jax.random.fold_in(key, 2), (), 1, 4).astype(jnp.int32)
    levels = jnp.stack([jnp.int32(0), jnp.int32(4), middle]).astype(jnp.int32)
    return jnp.zeros((GROUPS,), jnp.int32).at[ordering].set(levels)


def level_of(own_key, dims, cuts, smallest, top_value):
    factor_of, own = 1.0, jax.random.fold_in(own_key, 6)
    for dim, parts in cuts:
        heights = jnp.exp(jax.random.uniform(jax.random.fold_in(own, dim), (parts,), jnp.float32, smallest / len(cuts), top_value / len(cuts)))
        factor_of = factor_of * jnp.repeat(heights, dims[dim] // parts).reshape([-1 if axis == dim else 1 for axis in range(len(dims))])
    return factor_of


def centred(rng, extent, spread, most, split=(), kind=jnp.bfloat16):
    factor_of = level_of(rng, extent, split, -0.22, 0.18) if split else 1.0
    drawn = jax.random.normal(rng, extent, jnp.float32) * spread * factor_of
    return jnp.minimum(jnp.maximum(drawn, -most), most).astype(kind)


def setup_inputs(seed: int = 0) -> dict:
    key_of = jax.random.split(jax.random.key(seed), 20)
    return {
        "images": centred(key_of[0], (IMAGES, HIN, HIN, C_IN), 1.0, 6.0, ((0, 16), (1, 2))),
        "w_1a": centred(key_of[1], (C_IN, C_MID), C_IN ** -0.5, 0.375),
        "w_1b": centred(key_of[2], (3, 3, C_MID, C_MID), (9 * C_MID) ** -0.5, 0.1875),
        "w_1c": centred(key_of[3], (C_MID, C_OUT), C_MID ** -0.5, 0.5),
        "w_1p": centred(key_of[4], (C_IN, C_OUT), C_IN ** -0.5, 0.375),
        "w_2a": centred(key_of[5], (C_OUT, C_MID), C_OUT ** -0.5, 0.25),
        "w_2b": centred(key_of[6], (3, 3, C_MID, C_MID), (9 * C_MID) ** -0.5, 0.1875),
        "w_2c": centred(key_of[7], (C_MID, C_OUT), C_MID ** -0.5, 0.5),
        "norm_1a": jnp.clip(jax.random.uniform(key_of[8], (2, GROUPS, C_MID), jnp.float32, 0.5, 1.5), 0.5, 1.5),
        "norm_1b": jnp.clip(jax.random.uniform(key_of[9], (2, GROUPS, C_MID), jnp.float32, 0.5, 1.5), 0.5, 1.5),
        "norm_1c": jnp.clip(jax.random.uniform(key_of[10], (2, GROUPS, C_OUT), jnp.float32, 0.5, 1.5), 0.5, 1.5),
        "norm_1p": jnp.clip(jax.random.uniform(key_of[11], (2, GROUPS, C_OUT), jnp.float32, 0.5, 1.5), 0.5, 1.5),
        "norm_2a": jnp.clip(jax.random.uniform(key_of[12], (2, GROUPS, C_MID), jnp.float32, 0.5, 1.5), 0.5, 1.5),
        "norm_2b": jnp.clip(jax.random.uniform(key_of[13], (2, GROUPS, C_MID), jnp.float32, 0.5, 1.5), 0.5, 1.5),
        "norm_2c": jnp.clip(jax.random.uniform(key_of[14], (2, GROUPS, C_OUT), jnp.float32, 0.5, 1.5), 0.5, 1.5),
        "cotangent": centred(key_of[15], (IMAGES, HOUT, HOUT, C_OUT), 1.0, 6.0, ((0, 32),)),
        "group": draw_group(jax.random.fold_in(key_of[19], 71), 0),
        "width": jax.random.randint(key_of[17], (GROUPS,), 2, 5).astype(jnp.int32),
        "gate": draw_gate(jax.random.fold_in(key_of[19], 71), 0),
    }


@jax.custom_vjp
def low(v):
    return lax.optimization_barrier(v.astype(jnp.bfloat16)).astype(jnp.float32)

@jax.custom_vjp
def low_back(v):
    return v

def low_keep(v):
    return (low(v), None)

def low_pass(kept, grad):
    return (grad,)

def back_keep(v):
    return (v, None)

def back_low(kept, grad):
    return (low(grad),)
low.defvjp(low_keep, low_pass)
low_back.defvjp(back_keep, back_low)
HIGHEST = lax.Precision.HIGHEST

def project(values, kernel):
    return jnp.einsum('nhwc,cd->nhwd', values, kernel, precision=HIGHEST)

def convolve(values, kernel, stride):
    return lax.conv_general_dilated(values, kernel, (stride, stride), ((1, 1), (1, 1)), dimension_numbers=('NHWC', 'HWIO', 'NHWC'), precision=HIGHEST)

def per_image(onehot, table):
    return jnp.dot(onehot, table, precision=HIGHEST)[:, None, None, :]

def group_norm(values, onehot, params):
    pixels = lax.optimization_barrier(jnp.sum(onehot, axis=0)) * (values.shape[1] * values.shape[2])
    first_sum = jnp.dot(onehot.T, lax.optimization_barrier(jnp.sum(values, axis=(1, 2))), precision=HIGHEST)
    second_sum = jnp.dot(onehot.T, lax.optimization_barrier(jnp.sum(values * values, axis=(1, 2))), precision=HIGHEST)
    means = first_sum / pixels[:, None]
    scales = lax.rsqrt(second_sum / pixels[:, None] - means * means + 1e-05)
    normed = (values - per_image(onehot, means)) * per_image(onehot, scales)
    return normed * per_image(onehot, params[0]) + per_image(onehot, params[1])

def reference(images, w_1a, w_1b, w_1c, w_1p, w_2a, w_2b, w_2c, norm_1a, norm_1b, norm_1c, norm_1p, norm_2a, norm_2b, norm_2c, cotangent, group, width, gate):
    onehot = (group[:, None] == jnp.arange(GROUPS, dtype=jnp.int32)[None, :]).astype(jnp.float32)
    img_width = jnp.dot(onehot, width.astype(jnp.float32), precision=HIGHEST)
    channel = jnp.arange(C_MID, dtype=jnp.float32)
    chan_mask = (channel[None, :] < C_MID // 4 * img_width[:, None]).astype(jnp.float32)[:, None, None, :]
    img_gate = 0.25 * jnp.dot(onehot, gate.astype(jnp.float32), precision=HIGHEST)[:, None, None, None]

    def forward(inputs, kern_1a, kern_1b, kern_1c, kern_1p, kern_2a, kern_2b, kern_2c, par_1a, par_1b, par_1c, par_1p, par_2a, par_2b, par_2c):
        z_1a = low_back(project(inputs, kern_1a))
        act_1a = low(chan_mask * jax.nn.silu(group_norm(z_1a, onehot, par_1a)))
        z_1b = low_back(convolve(act_1a, kern_1b, 2))
        act_1b = low(chan_mask * jax.nn.silu(group_norm(z_1b, onehot, par_1b)))
        z_1c = low_back(project(act_1b, kern_1c))
        z_1p = low_back(project(inputs[:, ::2, ::2], kern_1p))
        pre_2 = group_norm(z_1c, onehot, par_1c) + group_norm(z_1p, onehot, par_1p)
        joined = low_back(low(jax.nn.silu(pre_2)))
        z_2a = low_back(project(joined, kern_2a))
        act_2a = low(chan_mask * jax.nn.silu(group_norm(z_2a, onehot, par_2a)))
        z_2b = low_back(convolve(act_2a, kern_2b, 1))
        act_2b = low(chan_mask * jax.nn.silu(group_norm(z_2b, onehot, par_2b)))
        z_2c = low_back(project(act_2b, kern_2c))
        return jax.nn.silu(joined + img_gate * group_norm(z_2c, onehot, par_2c))
    floats = [images, w_1a, w_1b, w_1c, w_1p, w_2a, w_2b, w_2c, norm_1a, norm_1b, norm_1c, norm_1p, norm_2a, norm_2b, norm_2c]
    floats = [item.astype(jnp.float32) for item in floats]
    outcome, pullback = jax.vjp(forward, *floats)
    grads = pullback(cotangent.astype(jnp.float32))
    return (outcome.astype(jnp.bfloat16), grads[0].astype(jnp.bfloat16), grads[1], grads[2], grads[3], grads[4], grads[5], grads[6], grads[7], grads[8], grads[9], grads[10], grads[11], grads[12], grads[13], grads[14])
```

```python
import functools

import jax
import jax.numpy as jnp
from jax import lax
from jax.experimental import pallas as pl
from jax.experimental.pallas import tpu as pltpu
from jax.sharding import PartitionSpec as P

EPSILON = 1e-05
F32 = jnp.float32
BF16 = jnp.bfloat16
AXES = ("rows", "batch")
VMEM_LIMIT = 40 * 1024 * 1024
LANES = 128
COLS = 32


def full(memory=pltpu.VMEM):
    return pl.BlockSpec(memory_space=memory)


def stage(kernel, outs, scratch=(), flops=0, smem=(0,)):
    def call(*args):
        return pl.pallas_call(
            kernel,
            out_shape=tuple(jax.ShapeDtypeStruct(s, d) for s, d in outs),
            in_specs=[full(pltpu.SMEM if i in smem else pltpu.VMEM) for i in range(len(args))],
            out_specs=tuple(full() for _ in outs),
            scratch_shapes=list(scratch),
            compiler_params=pltpu.CompilerParams(vmem_limit_bytes=VMEM_LIMIT),
            cost_estimate=pl.CostEstimate(
                flops=flops, bytes_accessed=4 * 1024 * 1024, transcendentals=0
            ),
            name=kernel.func.__name__ if isinstance(kernel, functools.partial) else kernel.__name__,
        )(*args)

    return call


def sigmoid(v):
    return 0.5 * jnp.tanh(0.5 * v) + 0.5


def fold(x):
    return (x[0:8] + x[8:16]) + (x[16:24] + x[24:32])


def row(total, stat):
    blocks = total.shape[0]
    pieces = [total[j : j + 1, LANES * stat : LANES * (stat + 1)] for j in range(blocks)]
    return pieces[0] if blocks == 1 else jnp.concatenate(pieces, axis=1)


def spread(out_ref, rows):
    blocks = out_ref.shape[1]
    for stat, values in enumerate(rows):
        for j in range(blocks):
            piece = values[:, LANES * j : LANES * (j + 1)]
            out_ref[:, j : j + 1, LANES * stat : LANES * (stat + 1)] = jnp.broadcast_to(
                piece[None], (out_ref.shape[0], 1, LANES)
            )


def group_sum(got_ref, labels, label):
    same = (labels == label).astype(F32)
    stats = got_ref.shape[2] // LANES
    parts = [
        jnp.sum(got_ref[:, :, LANES * s : LANES * (s + 1)] * same, axis=0) for s in range(stats)
    ]
    return jnp.concatenate(parts, axis=1) if stats > 1 else parts[0]


def group_count(labels, label):
    return jnp.sum((labels == label).astype(F32), axis=0)


def tiled(values, channels):
    return jnp.concatenate([values] * (channels // LANES), axis=1) if channels > LANES else values


def moments(first, second, pixels):
    mean = first / pixels
    return mean, lax.rsqrt(second / pixels - mean * mean + EPSILON)


def gain_of(norm_ref, group):
    return norm_ref[0, pl.ds(group, 1), :]


def shift_of(norm_ref, group):
    return norm_ref[1, pl.ds(group, 1), :]


def valid_cols(channels):
    return lax.broadcasted_iota(jnp.int32, (COLS, channels), 0) < COLS - 4


def chan_mask(limit, channels):
    return lax.broadcasted_iota(jnp.int32, (1, channels), 1) < limit


def flat(x):
    return x.reshape(x.shape[0] * x.shape[1], x.shape[2])


def mm(a, b):
    return jnp.dot(a, b, preferred_element_type=F32)


def mm_nt(a, b):
    return lax.dot_general(a, b, (((1,), (1,)), ((), ())), preferred_element_type=F32)


def mm_tn(a, b):
    return lax.dot_general(a, b, (((0,), (0,)), ((), ())), preferred_element_type=F32)


def zeros8(channels):
    return jnp.zeros((8, channels), F32)


def down(x):
    return jnp.sum(x, axis=0, keepdims=True)


OWN, OTHER, HALF, LIMIT, GATE = range(5)


def prepare(w1b, w2b, w_cur, w_up, b_even, b_odd, b_same):
    n = LANES
    for k, (y, x) in enumerate(((1, 1), (1, 2), (1, 0), (2, 1), (2, 2), (2, 0))):
        w_cur[n * k : n * (k + 1), :] = w1b[y, x]
    for k, (y, x) in enumerate(((0, 1), (0, 2), (0, 0))):
        w_up[n * k : n * (k + 1), :] = w1b[y, x]
    nothing = jnp.zeros((n, n), BF16)
    b_even[0:n, 0:n] = w1b[1, 1]
    b_even[0:n, n : 2 * n] = nothing
    b_even[n : 2 * n, 0:n] = w1b[1, 2]
    b_even[n : 2 * n, n : 2 * n] = w1b[1, 0]
    for k, top in ((0, 2), (1, 0)):
        b_odd[0:n, 2 * n * k : 2 * n * k + n] = w1b[top, 1]
        b_odd[0:n, 2 * n * k + n : 2 * n * (k + 1)] = nothing
        b_odd[n : 2 * n, 2 * n * k : 2 * n * k + n] = w1b[top, 2]
        b_odd[n : 2 * n, 2 * n * k + n : 2 * n * (k + 1)] = w1b[top, 0]
    for y in range(3):
        for x in range(3):
            b_same[y, :, n * x : n * (x + 1)] = w2b[y, x]


def widen(source, x_pad):
    rows, cols, chans = source.shape
    gap = x_pad.shape[1] - cols

    def put(i, carry):
        x_pad[i, 0:cols, :] = source[i]
        x_pad[i, cols : cols + gap, :] = jnp.zeros((gap, chans), BF16)
        return carry

    lax.fori_loop(0, rows, put, 0, unroll=4)


def first_project(x_pad, w, z):
    rows = x_pad.shape[0]
    step = rows // 4
    sums, squares = zeros8(LANES), zeros8(LANES)
    for c in range(4):
        values = mm(flat(x_pad[step * c : step * (c + 1)]), w[...])
        z[step * c : step * (c + 1)] = values.reshape(step, x_pad.shape[1], LANES)
        parts = values.reshape(-1, 8, LANES)
        sums = sums + jnp.sum(parts, axis=0)
        squares = squares + jnp.sum(parts * parts, axis=0)
    return sums, squares


def f1_own(scal, images, w, x_pad, z, part):
    widen(images.at[scal[HALF]], x_pad)
    sums, squares = first_project(x_pad, w, z)
    part[0] = sums
    part[1] = squares


def f1_other(scal, received, w, part, x_pad, z, send):
    widen(received, x_pad)
    sums, squares = first_project(x_pad, w, z)
    label = jnp.full((1, LANES), scal[OWN].astype(F32))
    spread(send, [down(sums + part[0]), down(squares + part[1]), label])


def f1_strided(scal, x_own, x_oth, w, xee, z, stats, wide):
    half = scal[HALF]
    rows = x_own.shape[0] // 2
    for k, x_pad in enumerate((x_own, x_oth)):
        first = rows * (half if k == 0 else 1 - half)

        def put(i, carry, x_pad=x_pad, first=first):
            for b in range(wide.shape[0]):
                lanes = slice(LANES * b, LANES * (b + 1))
                wide[b] = x_pad[2 * i, :, lanes].astype(F32)
                xee[first + i, :, lanes] = wide[b, pl.ds(0, COLS, stride=2), :].astype(BF16)
            return carry

        lax.fori_loop(0, rows, put, 0, unroll=2)
    total = 2 * rows
    step = total // 7
    chans = z.shape[2]
    sums, squares = zeros8(chans), zeros8(chans)
    for c in range(7):
        values = mm(flat(xee[step * c : step * (c + 1)]), w[...])
        z[step * c : step * (c + 1)] = values.reshape(step, COLS, chans)
        parts = values.reshape(-1, 8, chans)
        sums = sums + jnp.sum(parts, axis=0)
        squares = squares + jnp.sum(parts * parts, axis=0)
    stats[0] = down(sums)
    stats[1] = down(squares)


def scale_shift(got, labels, scal, norm, pixels, slot=0):
    label = scal[OWN].astype(F32)
    total = group_sum(got, labels, label)
    chans = norm.shape[2]
    count = tiled(group_count(labels, label), chans) * pixels
    mean, rstd = moments(row(total, 2 * slot), row(total, 2 * slot + 1), count)
    gain, shift = gain_of(norm, scal[OWN]), shift_of(norm, scal[OWN])
    return mean, rstd, gain, shift, count


def conv_stats(z, pieces, send):
    keep = valid_cols(LANES)[None]
    rows = z.shape[0]
    step = rows // 4
    sums, squares = zeros8(LANES), zeros8(LANES)
    for c in range(4):
        values = None
        for source, first, lane, weight in pieces:
            term = mm(flat(source[first + step * c : first + step * (c + 1), :, lane:]), weight)
            values = term if values is None else values + term
        values = jnp.where(keep, values.reshape(step, COLS, LANES), 0.0)
        z[step * c : step * (c + 1)] = values
        parts = values.reshape(-1, 8, LANES)
        sums = sums + jnp.sum(parts, axis=0)
        squares = squares + jnp.sum(parts * parts, axis=0)
    spread(send, [down(sums), down(squares)])


def f2(scal, got, z_own, z_oth, norm, w_cur, w_up, xs, z, send, labels, keeps):
    marks = got[:, :, 2 * LANES : 3 * LANES]
    labels[...] = marks
    rows = xs.shape[0] - 1
    pixels = 4.0 * rows * (COLS - 4)
    mean, rstd, gain, shift, _ = scale_shift(got, marks, scal, norm, pixels)
    keeps[0:1, :] = mean
    keeps[1:2, :] = rstd
    other = scal[OTHER].astype(F32)
    total = group_sum(got, marks, other)
    count = group_count(marks, other) * pixels
    mean_2, rstd_2 = moments(row(total, 0), row(total, 1), count)
    keeps[2:3, :] = mean_2
    keeps[3:4, :] = rstd_2
    scale = rstd * gain
    bias = shift - mean * scale
    keep = valid_cols(LANES) & chan_mask(scal[LIMIT], LANES)
    half = scal[HALF]
    xs[0] = jnp.zeros(xs.shape[1:], BF16)
    n = LANES
    for k, zz in enumerate((z_own, z_oth)):
        first = 1 + (rows // 2) * (half if k == 0 else 1 - half)

        def put(i, carry, zz=zz, first=first):
            lane = 0
            for a in (0, 1):
                for b in (0, 1):
                    v = zz[2 * i + a, pl.ds(b, COLS, stride=2), :] * scale + bias
                    act = jnp.where(keep, v * sigmoid(v), 0.0)
                    xs[first + i, :, lane : lane + n] = act.astype(BF16)
                    lane += n
                    if b == 1:
                        moved = pltpu.roll(act, 1, 0)
                        xs[first + i, :, lane : lane + n] = moved.astype(BF16)
                        lane += n
            return carry

        lax.fori_loop(0, rows // 2, put, 0, unroll=2)
    conv_stats(z, ((xs, 1, 0, w_cur[...]), (xs, 0, 3 * n, w_up[...])), send)


def expand(act, w, z, send, extra=()):
    rows, chans = z.shape[0], z.shape[2]
    step = rows // 7
    sums, squares = zeros8(chans), zeros8(chans)
    for c in range(7):
        values = mm(flat(act[step * c : step * (c + 1)]), w[...])
        z[step * c : step * (c + 1)] = values.reshape(step, COLS, chans)
        parts = values.reshape(-1, 8, chans)
        sums = sums + jnp.sum(parts, axis=0)
        squares = squares + jnp.sum(parts * parts, axis=0)
    spread(send, [down(sums), down(squares), *extra])


def activate(scal, got, labels, z_in, norm, act, keeps):
    rows = z_in.shape[0]
    pixels = 1.0 * rows * (COLS - 4)
    mean, rstd, gain, shift, _ = scale_shift(got, labels[...], scal, norm, pixels)
    keeps[0:1, :] = mean
    keeps[1:2, :] = rstd
    scale = rstd * gain
    bias = shift - mean * scale
    keep = valid_cols(LANES) & chan_mask(scal[LIMIT], LANES)

    def put(i, carry):
        v = z_in[i] * scale + bias
        act[i] = jnp.where(keep, v * sigmoid(v), 0.0).astype(BF16)
        return carry

    lax.fori_loop(0, rows, put, 0, unroll=4)


def f3(scal, got, labels, z_in, norm, w, stats_p, act, z, send, keeps):
    activate(scal, got, labels, z_in, norm, act, keeps)
    expand(act, w, z, send, (stats_p[0], stats_p[1]))


def f4(scal, got, labels, zc, zp, norm_c, norm_p, w, joined, slope, z, send, keeps):
    rows, chans = zc.shape[0], zc.shape[2]
    pixels = 1.0 * rows * (COLS - 4)
    label = scal[OWN].astype(F32)
    marks = labels[...]
    total = group_sum(got, marks, label)
    count = tiled(group_count(marks, label), chans) * pixels
    mean_c, rstd_c = moments(row(total, 0), row(total, 1), count)
    mean_p, rstd_p = moments(row(total, 2), row(total, 3), count)
    for k, v in enumerate((mean_c, rstd_c, mean_p, rstd_p)):
        keeps[k : k + 1, :] = v
    group = scal[OWN]
    scale_c = rstd_c * gain_of(norm_c, group)
    scale_p = rstd_p * gain_of(norm_p, group)
    bias = (shift_of(norm_c, group) - mean_c * scale_c) + (
        shift_of(norm_p, group) - mean_p * scale_p
    )
    keep = valid_cols(chans)

    def put(i, carry):
        v = zc[i] * scale_c + zp[i] * scale_p + bias
        s = sigmoid(v)
        joined[i] = jnp.where(keep, v * s, 0.0).astype(BF16)
        slope[i] = s * (1.0 + v * (1.0 - s))
        return carry

    lax.fori_loop(0, rows, put, 0, unroll=2)
    step = rows // 4
    sums, squares = zeros8(LANES), zeros8(LANES)
    for c in range(4):
        values = mm(flat(joined[step * c : step * (c + 1)]), w[...])
        z[step * c : step * (c + 1)] = values.reshape(step, COLS, LANES)
        parts = values.reshape(-1, 8, LANES)
        sums = sums + jnp.sum(parts, axis=0)
        squares = squares + jnp.sum(parts * parts, axis=0)
    spread(send, [down(sums), down(squares)])


def f5(scal, got, labels, z_in, norm, w, x3, z, send, keeps):
    rows = z_in.shape[0]
    pixels = 1.0 * rows * (COLS - 4)
    mean, rstd, gain, shift, _ = scale_shift(got, labels[...], scal, norm, pixels)
    keeps[0:1, :] = mean
    keeps[1:2, :] = rstd
    scale = rstd * gain
    bias = shift - mean * scale
    keep = valid_cols(LANES) & chan_mask(scal[LIMIT], LANES)
    x3[0] = jnp.zeros(x3.shape[1:], BF16)
    x3[rows + 1] = jnp.zeros(x3.shape[1:], BF16)
    n = LANES

    def put(i, carry):
        v = z_in[i] * scale + bias
        act = jnp.where(keep, v * sigmoid(v), 0.0)
        x3[i + 1, :, 0:n] = pltpu.roll(act, 1, 0).astype(BF16)
        x3[i + 1, :, n : 2 * n] = act.astype(BF16)
        x3[i + 1, :, 2 * n : 3 * n] = pltpu.roll(act, COLS - 1, 0).astype(BF16)
        return carry

    lax.fori_loop(0, rows, put, 0, unroll=2)
    conv_stats(z, tuple((x3, y, 0, w[y]) for y in range(3)), send)


def f6(scal, got, labels, z_in, norm, w, act, z, send, keeps):
    activate(scal, got, labels, z_in, norm, act, keeps)
    expand(act, w, z, send)


def b7(scal, got, labels, joined, z, norm, cot, result, grad_pre, send, keeps):
    rows, chans = z.shape[0], z.shape[2]
    cols = COLS - 4
    pixels = 1.0 * rows * cols
    mean, rstd, gain, shift, _ = scale_shift(got, labels[...], scal, norm, pixels)
    keeps[0:1, :] = mean
    keeps[1:2, :] = rstd
    gate = 0.25 * scal[GATE].astype(F32)
    scale = rstd * gain * gate
    bias = (shift - mean * rstd * gain) * gate

    def put(i, carry):
        sums, products = carry
        zz = z[i, 0:cols, :]
        v = joined[i, 0:cols, :].astype(F32) + zz * scale + bias
        s = sigmoid(v)
        result[i] = (v * s).astype(BF16)
        g = cot[i].astype(F32) * (s * (1.0 + v * (1.0 - s)))
        grad_pre[i, 0:cols, :] = g
        grad_pre[i, cols:COLS, :] = jnp.zeros((COLS - cols, chans), F32)
        return sums + down(g), products + down(g * (zz - mean))

    start = jnp.zeros((1, chans), F32)
    sums, products = lax.fori_loop(0, rows, put, (start, start), unroll=2)
    spread(send, [sums * gate, products * rstd * gate])


def backward_norm(scal, got, labels, norm, keeps, pixels, grad_norm, slots=(0, 1)):
    marks = labels[...]
    chans = norm.shape[2]
    own_shift = jnp.zeros((1, chans), F32)
    own_gain = jnp.zeros((1, chans), F32)
    group = scal[OWN]
    for g in range(norm.shape[1]):
        total = group_sum(got, marks, float(g))
        shift_sum, gain_sum = row(total, slots[0]), row(total, slots[1])
        grad_norm[0, g : g + 1, :] = gain_sum
        grad_norm[1, g : g + 1, :] = shift_sum
        mine = group == g
        own_shift = jnp.where(mine, shift_sum, own_shift)
        own_gain = jnp.where(mine, gain_sum, own_gain)
    count = tiled(group_count(marks, group.astype(F32)), chans) * pixels
    mean, rstd = keeps[0:1, :], keeps[1:2, :]
    a = rstd * gain_of(norm, group)
    return mean, a, -(a * rstd) * own_gain / count, -a * own_shift / count


def slope_sums(scal, d, z_in, norm, keeps, dout, send):
    rows = z_in.shape[0]
    mean, rstd = keeps[0:1, :], keeps[1:2, :]
    group = scal[OWN]
    scale = rstd * gain_of(norm, group)
    bias = shift_of(norm, group) - mean * scale
    keep = valid_cols(LANES) & chan_mask(scal[LIMIT], LANES)

    def put(i, carry):
        sums, products = carry
        zz = z_in[i]
        v = zz * scale + bias
        s = sigmoid(v)
        g = jnp.where(keep, d[i] * (s * (1.0 + v * (1.0 - s))), 0.0)
        dout[i] = g
        return sums + fold(g), products + fold(g * (zz - mean))

    sums, products = lax.fori_loop(
        0, rows, put, (zeros8(LANES), zeros8(LANES)), unroll=4
    )
    spread(send, [down(sums), down(products) * rstd])


def b8(
    scal, got, labels, grad_pre, z, norm, keeps, w, z_in, norm_in, keeps_in,
    dz, dout, send, grad_norm, d,
):
    rows, chans = z.shape[0], z.shape[2]
    pixels = 1.0 * rows * (COLS - 4)
    mean, a, b, c = backward_norm(scal, got, labels, norm, keeps, pixels, grad_norm)
    a = a * (0.25 * scal[GATE].astype(F32))
    keep = valid_cols(chans)

    def put(i, carry):
        v = a * grad_pre[i] + b * (z[i] - mean) + c
        dz[i] = jnp.where(keep, v, 0.0).astype(BF16)
        return carry

    lax.fori_loop(0, rows, put, 0, unroll=2)
    d[...] = mm_nt(flat(dz[...]), w[...]).reshape(d.shape)
    slope_sums(scal, d, z_in, norm_in, keeps_in, dout, send)


def b9(
    scal, got, labels, dout_in, z, norm, keeps, b_same, z_in, norm_in, keeps_in,
    dz, dout, send, grad_norm, d3, d,
):
    rows = z.shape[0]
    pixels = 1.0 * rows * (COLS - 4)
    mean, a, b, c = backward_norm(scal, got, labels, norm, keeps, pixels, grad_norm)
    keep = valid_cols(LANES)
    n = LANES
    d3[0] = jnp.zeros(d3.shape[1:], BF16)
    d3[rows + 1] = jnp.zeros(d3.shape[1:], BF16)

    def put(i, carry):
        v = a * dout_in[i] + b * (z[i] - mean) + c
        v = jnp.where(keep, v, 0.0)
        d3[i + 1, :, 0:n] = pltpu.roll(v, COLS - 1, 0).astype(BF16)
        low = v.astype(BF16)
        d3[i + 1, :, n : 2 * n] = low
        dz[i] = low
        d3[i + 1, :, 2 * n : 3 * n] = pltpu.roll(v, 1, 0).astype(BF16)
        return carry

    lax.fori_loop(0, rows, put, 0, unroll=2)
    step = rows // 4
    for k in range(4):
        value = None
        for y in range(3):
            first = 2 - y + step * k
            term = mm_nt(flat(d3[first : first + step]), b_same[y])
            value = term if value is None else value + term
        d[step * k : step * (k + 1)] = value.reshape(step, COLS, LANES)
    slope_sums(scal, d, z_in, norm_in, keeps_in, dout, send)


def b10(
    scal, got, labels, dout_in, z, norm, keeps, w, grad_pre, slope, zc, zp, keeps_cp,
    dz, grad_pre_2, send, grad_norm, d,
):
    rows, chans = zc.shape[0], zc.shape[2]
    pixels = 1.0 * rows * (COLS - 4)
    mean, a, b, c = backward_norm(scal, got, labels, norm, keeps, pixels, grad_norm)
    keep = valid_cols(LANES)

    def put(i, carry):
        v = a * dout_in[i] + b * (z[i] - mean) + c
        dz[i] = jnp.where(keep, v, 0.0).astype(BF16)
        return carry

    lax.fori_loop(0, rows, put, 0, unroll=4)
    d[...] = mm_nt(flat(dz[...]), w[...]).reshape(d.shape)
    mean_c, rstd_c, mean_p, rstd_p = (keeps_cp[k : k + 1, :] for k in range(4))

    def sum_up(i, carry):
        sums, prod_c, prod_p = carry
        g = (grad_pre[i] + d[i]).astype(BF16).astype(F32) * slope[i]
        grad_pre_2[i] = g
        return (
            sums + fold(g),
            prod_c + fold(g * (zc[i] - mean_c)),
            prod_p + fold(g * (zp[i] - mean_p)),
        )

    start = zeros8(chans)
    sums, prod_c, prod_p = lax.fori_loop(0, rows, sum_up, (start, start, start), unroll=2)
    spread(send, [down(sums), down(prod_c) * rstd_c, down(prod_p) * rstd_p])


def b11(
    scal, got, labels, grad_pre_2, zc, zp, norm_c, norm_p, keeps_cp, w, z_in, norm_in, keeps_in,
    dz_c, dz_p, dout, send, grad_norm_c, grad_norm_p, d,
):
    rows, chans = zc.shape[0], zc.shape[2]
    pixels = 1.0 * rows * (COLS - 4)
    mean_c, a_c, b_c, c_c = backward_norm(
        scal, got, labels, norm_c, keeps_cp.at[0:2], pixels, grad_norm_c, (0, 1)
    )
    mean_p, a_p, b_p, c_p = backward_norm(
        scal, got, labels, norm_p, keeps_cp.at[2:4], pixels, grad_norm_p, (0, 2)
    )
    keep = valid_cols(chans)

    def put(i, carry):
        g = grad_pre_2[i]
        v = a_c * g + b_c * (zc[i] - mean_c) + c_c
        dz_c[i] = jnp.where(keep, v, 0.0).astype(BF16)
        v = a_p * g + b_p * (zp[i] - mean_p) + c_p
        dz_p[i] = jnp.where(keep, v, 0.0).astype(BF16)
        return carry

    lax.fori_loop(0, rows, put, 0, unroll=2)
    d[...] = mm_nt(flat(dz_c[...]), w[...]).reshape(d.shape)
    slope_sums(scal, d, z_in, norm_in, keeps_in, dout, send)


def b12(
    scal, got, labels, dout_in, z, norm, keeps, b_even, b_odd, z_own, z_oth, norm_in, keeps_in,
    dz, dn_own, dn_oth, send, grad_norm, d2, de, do, wide,
):
    rows = z.shape[0]
    pixels = 1.0 * rows * (COLS - 4)
    mean, a, b, c = backward_norm(scal, got, labels, norm, keeps, pixels, grad_norm)
    keep = valid_cols(LANES)
    n = LANES
    d2[rows] = jnp.zeros(d2.shape[1:], BF16)

    def put(i, carry):
        v = a * dout_in[i] + b * (z[i] - mean) + c
        v = jnp.where(keep, v, 0.0)
        low = v.astype(BF16)
        dz[i] = low
        d2[i, :, 0:n] = low
        d2[i, :, n : 2 * n] = pltpu.roll(v, COLS - 1, 0).astype(BF16)
        return carry

    lax.fori_loop(0, rows, put, 0, unroll=4)
    step = rows // 4
    for k in range(4):
        here = flat(d2[step * k : step * (k + 1)])
        below = flat(d2[step * k + 1 : step * (k + 1) + 1])
        de[step * k : step * (k + 1)] = mm_nt(here, b_even[...]).reshape(step, COLS, 2 * n)
        odd = mm_nt(here, b_odd[:, 0 : 2 * n]) + mm_nt(below, b_odd[:, 2 * n : 4 * n])
        do[step * k : step * (k + 1)] = odd.reshape(step, COLS, 2 * n)
    mean_1, rstd_1 = keeps_in[0:1, :], keeps_in[1:2, :]
    group = scal[OWN]
    scale = rstd_1 * gain_of(norm_in, group)
    bias = shift_of(norm_in, group) - mean_1 * scale
    keep = valid_cols(LANES) & chan_mask(scal[LIMIT], LANES)
    half = scal[HALF]
    totals = (zeros8(n), zeros8(n))
    for k, (zz, dn) in enumerate(((z_own, dn_own), (z_oth, dn_oth))):
        first = (rows // 2) * (half if k == 0 else 1 - half)

        def emit(i, carry, zz=zz, dn=dn, first=first):
            sums, products = carry
            for ra in (0, 1):
                planes = (de, do)[ra]
                for cb in (0, 1):
                    zv = zz[2 * i + ra, pl.ds(cb, COLS, stride=2), :]
                    v = zv * scale + bias
                    s = sigmoid(v)
                    g = planes[first + i, :, n * cb : n * (cb + 1)]
                    g = jnp.where(keep, g * (s * (1.0 + v * (1.0 - s))), 0.0)
                    sums = sums + fold(g)
                    products = products + fold(g * (zv - mean_1))
                    wide[ra, pl.ds(cb, COLS, stride=2), :] = g
                dn[2 * i + ra] = wide[ra].astype(BF16)
            return sums, products

        totals = lax.fori_loop(0, rows // 2, emit, totals, unroll=2)
    spread(send, [down(totals[0]), down(totals[1]) * rstd_1])


def b13(
    scal, got, labels, norm, keeps, images, w, z_own, dn_own, dn_oth, gs_own, gs_oth,
    grad, grad_norm, x_pad, z_oth, dz, wide,
):
    rows, cols = images.shape[1], images.shape[2]
    half = scal[HALF]
    pixels = 2.0 * rows * cols
    marks = labels[...]
    widen(images.at[1 - half], x_pad)
    for c in range(4):
        step = rows // 4
        values = mm(flat(x_pad[step * c : step * (c + 1)]), w[...])
        z_oth[step * c : step * (c + 1)] = values.reshape(step, x_pad.shape[1], LANES)
    totals = []
    for g in range(norm.shape[1]):
        total = group_sum(got, marks, float(g))
        totals.append((row(total, 0), row(total, 1)))
        grad_norm[0, g : g + 1, :] = totals[g][1]
        grad_norm[1, g : g + 1, :] = totals[g][0]
    keep = lax.broadcasted_iota(jnp.int32, (x_pad.shape[1], LANES), 0) < cols
    for k, (z, dn, gs) in enumerate(((z_own, dn_own, gs_own), (z_oth, dn_oth, gs_oth))):
        group = scal[OWN if k == 0 else OTHER]
        shift_sum, gain_sum = totals[0]
        for g in range(1, norm.shape[1]):
            shift_sum = jnp.where(group == g, totals[g][0], shift_sum)
            gain_sum = jnp.where(group == g, totals[g][1], gain_sum)
        count = group_count(marks, group.astype(F32)) * pixels
        mean, rstd = keeps[2 * k : 2 * k + 1, :], keeps[2 * k + 1 : 2 * k + 2, :]
        a = rstd * gain_of(norm, group)
        b = -(a * rstd) * gain_sum / count
        c = -a * shift_sum / count

        def put(i, carry, z=z, dn=dn, mean=mean, a=a, b=b, c=c):
            v = a * dn[i].astype(F32) + b * (z[i] - mean) + c
            dz[i] = jnp.where(keep, v, 0.0).astype(BF16)
            return carry

        lax.fori_loop(0, rows, put, 0, unroll=2)
        step = rows // 4
        for q in range(4):
            low = flat(dz[step * q : step * (q + 1)])
            for p in range(wide.shape[0]):
                values = mm_nt(low, w[LANES * p : LANES * (p + 1), :])
                wide[p, step * q : step * (q + 1)] = values.reshape(step, -1, LANES)
        place = half if k == 0 else 1 - half

        def emit(i, carry, gs=gs, place=place):
            even = pl.ds(0, COLS, stride=2)
            for p in range(wide.shape[0]):
                lanes = slice(LANES * p, LANES * (p + 1))
                wide[p, 2 * i, even, :] = wide[p, 2 * i, even, :] + gs[i, :, lanes].astype(F32)
                grad[place, 2 * i, :, lanes] = wide[p, 2 * i, 0:cols, :].astype(BF16)
                grad[place, 2 * i + 1, :, lanes] = wide[p, 2 * i + 1, 0:cols, :].astype(BF16)
            return carry

        lax.fori_loop(0, rows // 2, emit, 0, unroll=2)


def g_2c(act, dz, out):
    out[...] = mm_tn(flat(act[...]), flat(dz[...]))


def g_2b(x3, dz, out):
    rows = dz.shape[0]
    low = flat(dz[...])
    for y in range(3):
        got = mm_tn(flat(x3[y : y + rows]), low)
        out[y] = got.reshape(3, LANES, LANES)


def g_2a(joined, dz, out):
    out[...] = mm_tn(flat(joined[...]), flat(dz[...]))


def g_1(scal, act, dz_c, xee, dz_p, w_p, out_c, out_p, gs_own, gs_oth):
    out_c[...] = mm_tn(flat(act[...]), flat(dz_c[...]))
    out_p[...] = mm_tn(flat(xee[...]), flat(dz_p[...]))
    half = scal[HALF]
    rows = gs_own.shape[0]
    for k, gs in enumerate((gs_own, gs_oth)):
        first = rows * (half if k == 0 else 1 - half)
        got = mm_nt(flat(dz_p[pl.ds(first, rows)]), w_p[...])
        gs[...] = got.reshape(gs.shape).astype(BF16)


def g_1b(xs, dz, out):
    rows = dz.shape[0]
    low = flat(dz[...])
    n = LANES
    cur = mm_tn(flat(xs[1 : rows + 1]), low)
    for k, (y, x) in enumerate(((1, 1), (1, 2), (1, 0), (2, 1), (2, 2), (2, 0))):
        out[y, x] = cur[n * k : n * (k + 1)]
    up = mm_tn(flat(xs[0:rows, :, 3 * n : 6 * n]), low)
    for k, (y, x) in enumerate(((0, 1), (0, 2), (0, 0))):
        out[y, x] = up[n * k : n * (k + 1)]


def g_1a(scal, got, labels, norm, keeps, z_own, z_oth, dn_own, dn_oth, x_own, x_oth, out, dz):
    rows = z_own.shape[0]
    cols = 2 * (COLS - 4)
    pixels = 2.0 * rows * cols
    marks = labels[...]
    group = scal[OWN]
    total = group_sum(got, marks, group.astype(F32))
    count = group_count(marks, group.astype(F32)) * pixels
    mean, rstd = keeps[0:1, :], keeps[1:2, :]
    a = rstd * gain_of(norm, group)
    b = -(a * rstd) * row(total, 1) / count
    c = -a * row(total, 0) / count
    keep = lax.broadcasted_iota(jnp.int32, (z_own.shape[1], LANES), 0) < cols
    value = None
    for z, dn, x in ((z_own, dn_own, x_own), (z_oth, dn_oth, x_oth)):

        def put(i, carry, z=z, dn=dn):
            v = a * dn[i].astype(F32) + b * (z[i] - mean) + c
            dz[i] = jnp.where(keep, v, 0.0).astype(BF16)
            return carry

        lax.fori_loop(0, rows, put, 0, unroll=2)
        term = mm_tn(flat(x[...]), flat(dz[...]))
        value = term if value is None else value + term
    out[...] = value


def gather(send):
    return lax.all_to_all(send, AXES, 0, 0)


def reduce_weights(grads, devices):
    shapes = [g.shape for g in grads]
    sizes = [g.size for g in grads]
    total = sum(sizes)
    unit = devices * 16 * LANES
    padded = -(-total // unit) * unit
    one = jnp.concatenate(
        [g.astype(BF16).reshape(-1) for g in grads] + [jnp.zeros((padded - total,), BF16)]
    )
    parts = one.reshape(devices, padded // devices // LANES, LANES)
    mine = jnp.sum(lax.all_to_all(parts, AXES, 0, 0).astype(F32), axis=0).astype(BF16)
    everyone = lax.all_to_all(jnp.broadcast_to(mine[None], parts.shape), AXES, 0, 0)
    flat_sum = everyone.reshape(-1)
    outs, at = [], 0
    for shape, size in zip(shapes, sizes):
        outs.append(flat_sum[at : at + size].astype(F32).reshape(shape))
        at += size
    return outs


def swap(block):
    return lax.ppermute(block, "rows", [(0, 1), (1, 0)])


def body(
    images, w_1a, w_1b, w_1c, w_1p, w_2a, w_2b, w_2c,
    norm_1a, norm_1b, norm_1c, norm_1p, norm_2a, norm_2b, norm_2c,
    cotangent, group, width, gate,
):
    devices = lax.axis_size("rows") * lax.axis_size("batch")
    half = lax.axis_index("rows")
    own = jnp.take(group, half)
    other = jnp.take(group, 1 - half)
    inner, outer, inputs = w_1a.shape[1], w_1c.shape[1], w_1a.shape[0]
    scal = jnp.stack(
        [own, other, half.astype(jnp.int32), inner // 4 * jnp.take(width, own), jnp.take(gate, own)]
        + [jnp.int32(0)] * 3
    ).astype(jnp.int32)
    rows = cotangent.shape[1]
    cols_in = 2 * COLS
    n, m = LANES, devices

    def send(stats, channels=LANES):
        return ((m, channels // LANES, stats * LANES), F32)

    def maps(channels, dtype=F32):
        return ((rows, COLS, channels), dtype)

    def scratch(channels, dtype=F32):
        return pltpu.VMEM((rows, COLS, channels), dtype)

    def params(*arrays):
        return [((2, a.shape[1], a.shape[2]), F32) for a in arrays]

    def mean_scale(channels, count=1):
        return ((2 * count, channels), F32)

    received = swap(lax.dynamic_index_in_dim(images, 1 - half, 0, keepdims=False))
    w_cur, w_up, b_even, b_odd, b_same = stage(
        prepare,
        [((6 * n, n), BF16), ((3 * n, n), BF16), ((2 * n, 2 * n), BF16), ((2 * n, 4 * n), BF16),
         ((3, n, 3 * n), BF16)],
        smem=(),
    )(w_1b, w_2b)
    wide_in = ((rows, cols_in, inputs), BF16)
    wide_z = ((rows, cols_in, n), F32)
    x_own, z_own, part = stage(f1_own, [wide_in, wide_z, ((2, 8, n), F32)])(scal, images, w_1a)
    x_oth, z_oth, s1 = stage(f1_other, [wide_in, wide_z, send(3)])(scal, received, w_1a, part)
    g1 = gather(s1)
    xee, z_1p, stats_1p = stage(
        f1_strided,
        [maps(inputs, BF16), maps(outer), ((2, 1, outer), F32)],
        [pltpu.VMEM((inputs // n, cols_in, n), F32)],
    )(scal, x_own, x_oth, w_1p)
    xs, z_1b, s2, labels, k_1a = stage(
        f2,
        [((rows + 1, COLS, 6 * n), BF16), maps(n), send(2), ((m, 1, n), F32), mean_scale(n, 2)],
    )(scal, g1, z_own, z_oth, norm_1a, w_cur, w_up)
    g2 = gather(s2)
    act_1b, z_1c, s3, k_1b = stage(
        f3, [maps(n, BF16), maps(outer), send(4, outer), mean_scale(n)]
    )(scal, g2, labels, z_1b, norm_1b, w_1c, stats_1p)
    g3 = gather(s3)
    joined, slope, z_2a, s4, k_cp = stage(
        f4, [maps(outer, BF16), maps(outer), maps(n), send(2), mean_scale(outer, 2)]
    )(scal, g3, labels, z_1c, z_1p, norm_1c, norm_1p, w_2a)
    g4 = gather(s4)
    x3, z_2b, s5, k_2a = stage(
        f5, [((rows + 2, COLS, 3 * n), BF16), maps(n), send(2), mean_scale(n)]
    )(scal, g4, labels, z_2a, norm_2a, w_2b.reshape(3, 3 * n, n))
    g5 = gather(s5)
    act_2b, z_2c, s6, k_2b = stage(
        f6, [maps(n, BF16), maps(outer), send(2, outer), mean_scale(n)]
    )(scal, g5, labels, z_2b, norm_2b, w_2c)
    g6 = gather(s6)
    result, grad_pre, s7, k_2c = stage(
        b7, [(cotangent.shape[1:], BF16), maps(outer), send(2, outer), mean_scale(outer)]
    )(scal, g6, labels, joined, z_2c, norm_2c, cotangent[0])
    g7 = gather(s7)
    dz_2c, dout_2b, s8, grad_norm_2c = stage(
        b8, [maps(outer, BF16), maps(n), send(2), *params(norm_2c)], [scratch(n)]
    )(scal, g7, labels, grad_pre, z_2c, norm_2c, k_2c, w_2c, z_2b, norm_2b, k_2b)
    g8 = gather(s8)
    (grad_w_2c,) = stage(g_2c, [(w_2c.shape, F32)], smem=())(act_2b, dz_2c)
    dz_2b, dout_2a, s9, grad_norm_2b = stage(
        b9, [maps(n, BF16), maps(n), send(2), *params(norm_2b)],
        [pltpu.VMEM((rows + 2, COLS, 3 * n), BF16), scratch(n)],
    )(scal, g8, labels, dout_2b, z_2b, norm_2b, k_2b, b_same, z_2a, norm_2a, k_2a)
    g9 = gather(s9)
    (grad_w_2b,) = stage(g_2b, [(w_2b.shape, F32)], smem=())(x3, dz_2b)
    dz_2a, grad_pre_2, s10, grad_norm_2a = stage(
        b10, [maps(n, BF16), maps(outer), send(3, outer), *params(norm_2a)], [scratch(outer)]
    )(scal, g9, labels, dout_2a, z_2a, norm_2a, k_2a, w_2a, grad_pre, slope, z_1c, z_1p, k_cp)
    g10 = gather(s10)
    (grad_w_2a,) = stage(g_2a, [(w_2a.shape, F32)], smem=())(joined, dz_2a)
    dz_1c, dz_1p, dout_1b, s11, grad_norm_1c, grad_norm_1p = stage(
        b11, [maps(outer, BF16), maps(outer, BF16), maps(n), send(2), *params(norm_1c, norm_1p)],
        [scratch(n)],
    )(scal, g10, labels, grad_pre_2, z_1c, z_1p, norm_1c, norm_1p, k_cp, w_1c, z_1b, norm_1b, k_1b)
    g11 = gather(s11)
    half_map = ((rows // 2, COLS, inputs), BF16)
    grad_w_1c, grad_w_1p, gs_own, gs_send = stage(
        g_1, [(w_1c.shape, F32), (w_1p.shape, F32), half_map, half_map]
    )(scal, act_1b, dz_1c, xee, dz_1p, w_1p)
    gs_oth = swap(gs_send)
    half_in = ((rows, cols_in, n), BF16)
    dz_1b, dn_own, dn_send, s12, grad_norm_1b = stage(
        b12, [maps(n, BF16), half_in, half_in, send(2), *params(norm_1b)],
        [pltpu.VMEM((rows + 1, COLS, 2 * n), BF16), scratch(2 * n), scratch(2 * n),
         pltpu.VMEM((2, cols_in, n), F32)],
    )(scal, g11, labels, dout_1b, z_1b, norm_1b, k_1b, b_even, b_odd, z_own, z_oth, norm_1a, k_1a)
    dn_oth = swap(dn_send)
    g12 = gather(s12)
    (grad_w_1b,) = stage(g_1b, [(w_1b.shape, F32)], smem=())(xs, dz_1b)
    grad_images, grad_norm_1a = stage(
        b13, [(images.shape, BF16), *params(norm_1a)],
        [pltpu.VMEM(wide_in[0], BF16), pltpu.VMEM(wide_z[0], F32), pltpu.VMEM(half_in[0], BF16),
         pltpu.VMEM((inputs // n, rows, cols_in, n), F32)],
    )(scal, g12, labels, norm_1a, k_1a, images, w_1a, z_own, dn_own, dn_oth, gs_own, gs_oth)
    (grad_w_1a,) = stage(g_1a, [(w_1a.shape, F32)], [pltpu.VMEM(half_in[0], BF16)])(
        scal, g12, labels, norm_1a, k_1a, z_own, z_oth, dn_own, dn_send, x_own, x_oth
    )
    totals = reduce_weights(
        (grad_w_1a, grad_w_1b, grad_w_1c, grad_w_1p, grad_w_2a, grad_w_2b, grad_w_2c), devices
    )
    return (
        result[None], grad_images, *totals,
        grad_norm_1a, grad_norm_1b, grad_norm_1c, grad_norm_1p,
        grad_norm_2a, grad_norm_2b, grad_norm_2c,
    )


def solution(mesh):
    return jax.shard_map(
        body,
        mesh=mesh,
        in_specs=(
            P("batch", "rows", None, None),
            *[P()] * 14,
            P(("batch", "rows"), None, None, None),
            P("batch"),
            P(),
            P(),
        ),
        out_specs=(
            P(("batch", "rows"), None, None, None),
            P("batch", "rows", None, None),
            *[P()] * 14,
        ),
        check_vma=False,
    )
```

```python
import jax
import jax.numpy as jnp
from jax import lax
from jax.experimental import pallas as pl
from jax.experimental.pallas import tpu as pltpu
from jax.sharding import PartitionSpec as P

EPSILON = 1e-05
F32 = jnp.float32
BF16 = jnp.bfloat16
AXES = ("rows", "batch")
VMEM_LIMIT = 14 * 1024 * 1024
LANES = 128
COLS = 32


def full(memory=pltpu.VMEM):
    return pl.BlockSpec(memory_space=memory)


def stage(kernel, outs, scratch=(), flops=0, smem=(0,), smem_out=()):
    def call(*args):
        return pl.pallas_call(
            kernel,
            out_shape=tuple(jax.ShapeDtypeStruct(s, d) for s, d in outs),
            in_specs=[full(pltpu.SMEM if i in smem else pltpu.VMEM) for i in range(len(args))],
            out_specs=tuple(
                full(pltpu.SMEM if i in smem_out else pltpu.VMEM) for i in range(len(outs))
            ),
            scratch_shapes=list(scratch),
            compiler_params=pltpu.CompilerParams(vmem_limit_bytes=VMEM_LIMIT),
            cost_estimate=pl.CostEstimate(
                flops=flops, bytes_accessed=4 * 1024 * 1024, transcendentals=0
            ),
            name=kernel.__name__,
        )(*args)

    return call


def sigmoid(v):
    return 0.5 * jnp.tanh(0.5 * v) + 0.5


def fold(x):
    return (x[0:8] + x[8:16]) + (x[16:24] + x[24:32])


def row(total, stat):
    blocks = total.shape[0]
    pieces = [total[j : j + 1, LANES * stat : LANES * (stat + 1)] for j in range(blocks)]
    return pieces[0] if blocks == 1 else jnp.concatenate(pieces, axis=1)


def spread(out_ref, rows):
    blocks = out_ref.shape[1]
    for stat, values in enumerate(rows):
        for j in range(blocks):
            piece = values[:, LANES * j : LANES * (j + 1)]
            out_ref[:, j : j + 1, LANES * stat : LANES * (stat + 1)] = jnp.broadcast_to(
                piece[None], (out_ref.shape[0], 1, LANES)
            )


def group_sum(got_ref, labels, label):
    same = (labels == label).astype(F32)
    stats = got_ref.shape[2] // LANES
    parts = [
        jnp.sum(got_ref[:, :, LANES * s : LANES * (s + 1)] * same, axis=0) for s in range(stats)
    ]
    return jnp.concatenate(parts, axis=1) if stats > 1 else parts[0]


def group_count(labels, label):
    return jnp.sum((labels == label).astype(F32), axis=0)


def tiled(values, channels):
    return jnp.concatenate([values] * (channels // LANES), axis=1) if channels > LANES else values


def moments(first, second, pixels):
    mean = first / pixels
    return mean, lax.rsqrt(second / pixels - mean * mean + EPSILON)


def gain_of(norm_ref, group):
    return norm_ref[group, 0:1, :]


def shift_of(norm_ref, group):
    return norm_ref[group, 1:2, :]


def valid_cols(channels):
    return lax.broadcasted_iota(jnp.int32, (COLS, channels), 0) < COLS - 4


def chan_mask(limit, channels):
    return lax.broadcasted_iota(jnp.int32, (1, channels), 1) < limit


def flat(x):
    return x.reshape(x.shape[0] * x.shape[1], x.shape[2])


def mm(a, b):
    return jnp.dot(a, b, preferred_element_type=F32)


def mm_nt(a, b):
    return lax.dot_general(a, b, (((1,), (1,)), ((), ())), preferred_element_type=F32)


def mm_tn(a, b):
    return lax.dot_general(a, b, (((0,), (0,)), ((), ())), preferred_element_type=F32)


def zeros8(channels):
    return jnp.zeros((8, channels), F32)


def down(x):
    return jnp.sum(x, axis=0, keepdims=True)


OWN, OTHER, HALF, LIMIT, GATE = range(5)


def prepare(w1b, w2b, w_cur, w_up, b_even, b_odd, b_same):
    n = LANES
    for k, (y, x) in enumerate(((1, 1), (1, 2), (1, 0), (2, 1), (2, 2), (2, 0))):
        w_cur[n * k : n * (k + 1), :] = w1b[y, x]
    for k, (y, x) in enumerate(((0, 1), (0, 2), (0, 0))):
        w_up[n * k : n * (k + 1), :] = w1b[y, x]
    nothing = jnp.zeros((n, n), BF16)
    b_even[0:n, 0:n] = w1b[1, 1]
    b_even[0:n, n : 2 * n] = nothing
    b_even[n : 2 * n, 0:n] = w1b[1, 2]
    b_even[n : 2 * n, n : 2 * n] = w1b[1, 0]
    for k, top in ((0, 2), (1, 0)):
        b_odd[0:n, 2 * n * k : 2 * n * k + n] = w1b[top, 1]
        b_odd[0:n, 2 * n * k + n : 2 * n * (k + 1)] = nothing
        b_odd[n : 2 * n, 2 * n * k : 2 * n * k + n] = w1b[top, 2]
        b_odd[n : 2 * n, 2 * n * k + n : 2 * n * (k + 1)] = w1b[top, 0]
    for y in range(3):
        for x in range(3):
            b_same[y, :, n * x : n * (x + 1)] = w2b[y, x]


def widen(source, x_pad):
    rows, cols, chans = source.shape
    gap = x_pad.shape[1] - cols

    def put(i, carry):
        x_pad[i, 0:cols, :] = source[i]
        x_pad[i, cols : cols + gap, :] = jnp.zeros((gap, chans), BF16)
        return carry

    lax.fori_loop(0, rows, put, 0, unroll=4)


def first_project(x_pad, w, z, stats=True):
    rows = x_pad.shape[0]
    step = rows // 4
    sums, squares = zeros8(LANES), zeros8(LANES)
    for c in range(4):
        values = mm(flat(x_pad[step * c : step * (c + 1)]), w[...])
        z[step * c : step * (c + 1)] = values.reshape(step, x_pad.shape[1], LANES)
        if stats:
            parts = values.reshape(-1, 8, LANES)
            sums = sums + jnp.sum(parts, axis=0)
            squares = squares + jnp.sum(parts * parts, axis=0)
    return sums, squares


def f1(half_ref, group, width, gate, images, w, scal, x_own, x_for, z_own, z_for, send):
    half = half_ref[0]
    own, other = group[half], group[1 - half]
    scal[OWN] = own
    scal[OTHER] = other
    scal[HALF] = half
    scal[LIMIT] = w.shape[1] // 4 * width[own]
    scal[GATE] = gate[own]
    for k in range(GATE + 1, scal.shape[0]):
        scal[k] = 0
    widen(images.at[half], x_own)
    widen(images.at[1 - half], x_for)
    rows = []
    for x_pad, z in ((x_own, z_own), (x_for, z_for)):
        sums, squares = first_project(x_pad, w, z)
        rows += [down(sums), down(squares)]
    spread(send, [*rows, jnp.full((1, LANES), (own + 4 * other).astype(F32))])


def f1_strided(scal, x_own, x_oth, w, xee, z, stats, wide):
    half = scal[HALF]
    rows = x_own.shape[0] // 2
    for k, x_pad in enumerate((x_own, x_oth)):
        first = rows * (half if k == 0 else 1 - half)

        def put(i, carry, x_pad=x_pad, first=first):
            for b in range(wide.shape[0]):
                lanes = slice(LANES * b, LANES * (b + 1))
                wide[b] = x_pad[2 * i, :, lanes].astype(F32)
                xee[first + i, :, lanes] = wide[b, pl.ds(0, COLS, stride=2), :].astype(BF16)
            return carry

        lax.fori_loop(0, rows, put, 0, unroll=2)
    total = 2 * rows
    step = total // 7
    chans = z.shape[2]
    sums, squares = zeros8(chans), zeros8(chans)
    for c in range(7):
        values = mm(flat(xee[step * c : step * (c + 1)]), w[...])
        z[step * c : step * (c + 1)] = values.reshape(step, COLS, chans)
        parts = values.reshape(-1, 8, chans)
        sums = sums + jnp.sum(parts, axis=0)
        squares = squares + jnp.sum(parts * parts, axis=0)
    stats[0] = down(sums)
    stats[1] = down(squares)


def scale_shift(got, labels, scal, norm, pixels, slot=0):
    label = scal[OWN].astype(F32)
    total = group_sum(got, labels, label)
    chans = norm.shape[2]
    count = tiled(group_count(labels, label), chans) * pixels
    mean, rstd = moments(row(total, 2 * slot), row(total, 2 * slot + 1), count)
    gain, shift = gain_of(norm, scal[OWN]), shift_of(norm, scal[OWN])
    return mean, rstd, gain, shift, count


def conv_stats(z, pieces, send):
    keep = valid_cols(LANES)[None]
    rows = z.shape[0]
    step = rows // 4
    sums, squares = zeros8(LANES), zeros8(LANES)
    for c in range(4):
        values = None
        for source, first, lane, weight in pieces:
            term = mm(flat(source[first + step * c : first + step * (c + 1), :, lane:]), weight)
            values = term if values is None else values + term
        values = jnp.where(keep, values.reshape(step, COLS, LANES), 0.0)
        z[step * c : step * (c + 1)] = values
        parts = values.reshape(-1, 8, LANES)
        sums = sums + jnp.sum(parts, axis=0)
        squares = squares + jnp.sum(parts * parts, axis=0)
    spread(send, [down(sums), down(squares)])


def f2(scal, got, z_own, x_oth, w, norm, w_cur, w_up, xs, z, send, labels, keeps, z_oth):
    codes = got[:, :, 4 * LANES : 5 * LANES]
    others = jnp.floor(0.25 * codes)
    marks = codes - 4.0 * others
    labels[...] = marks
    rows = xs.shape[0] - 1
    pixels = 4.0 * rows * (COLS - 4)
    first_project(x_oth, w, z_oth, False)
    for k, slot in enumerate((OWN, OTHER)):
        label = scal[slot].astype(F32)
        mine, theirs = (marks == label).astype(F32), (others == label).astype(F32)
        totals = [
            jnp.sum(
                got[:, :, LANES * s : LANES * (s + 1)] * mine
                + got[:, :, LANES * (s + 2) : LANES * (s + 3)] * theirs,
                axis=0,
            )
            for s in (0, 1)
        ]
        mean, rstd = moments(*totals, group_count(marks, label) * pixels)
        keeps[2 * k : 2 * k + 1, :] = mean
        keeps[2 * k + 1 : 2 * k + 2, :] = rstd
    mean, rstd = keeps[0:1, :], keeps[1:2, :]
    gain, shift = gain_of(norm, scal[OWN]), shift_of(norm, scal[OWN])
    scale = rstd * gain
    bias = shift - mean * scale
    keep = valid_cols(LANES) & chan_mask(scal[LIMIT], LANES)
    half = scal[HALF]
    xs[0] = jnp.zeros(xs.shape[1:], BF16)
    n = LANES
    for k, zz in enumerate((z_own, z_oth)):
        first = 1 + (rows // 2) * (half if k == 0 else 1 - half)

        def put(i, carry, zz=zz, first=first):
            lane = 0
            for a in (0, 1):
                for b in (0, 1):
                    v = zz[2 * i + a, pl.ds(b, COLS, stride=2), :] * scale + bias
                    act = jnp.where(keep, v * sigmoid(v), 0.0)
                    xs[first + i, :, lane : lane + n] = act.astype(BF16)
                    lane += n
                    if b == 1:
                        moved = pltpu.roll(act, 1, 0)
                        xs[first + i, :, lane : lane + n] = moved.astype(BF16)
                        lane += n
            return carry

        lax.fori_loop(0, rows // 2, put, 0, unroll=2)
    conv_stats(z, ((xs, 1, 0, w_cur[...]), (xs, 0, 3 * n, w_up[...])), send)


def expand(act, w, z, send, extra=()):
    rows, chans = z.shape[0], z.shape[2]
    step = rows // 7
    sums, squares = zeros8(chans), zeros8(chans)
    for c in range(7):
        values = mm(flat(act[step * c : step * (c + 1)]), w[...])
        z[step * c : step * (c + 1)] = values.reshape(step, COLS, chans)
        parts = values.reshape(-1, 8, chans)
        sums = sums + jnp.sum(parts, axis=0)
        squares = squares + jnp.sum(parts * parts, axis=0)
    spread(send, [down(sums), down(squares), *extra])


def activate(scal, got, labels, z_in, norm, act, keeps):
    rows = z_in.shape[0]
    pixels = 1.0 * rows * (COLS - 4)
    mean, rstd, gain, shift, _ = scale_shift(got, labels[...], scal, norm, pixels)
    keeps[0:1, :] = mean
    keeps[1:2, :] = rstd
    scale = rstd * gain
    bias = shift - mean * scale
    keep = valid_cols(LANES) & chan_mask(scal[LIMIT], LANES)

    def put(i, carry):
        v = z_in[i] * scale + bias
        act[i] = jnp.where(keep, v * sigmoid(v), 0.0).astype(BF16)
        return carry

    lax.fori_loop(0, rows, put, 0, unroll=4)


def f3(scal, got, labels, z_in, norm, w, stats_p, act, z, send, keeps):
    activate(scal, got, labels, z_in, norm, act, keeps)
    expand(act, w, z, send, (stats_p[0], stats_p[1]))


def f4(scal, got, labels, zc, zp, norm_c, norm_p, w, joined, slope, z, send, keeps):
    rows, chans = zc.shape[0], zc.shape[2]
    pixels = 1.0 * rows * (COLS - 4)
    label = scal[OWN].astype(F32)
    marks = labels[...]
    total = group_sum(got, marks, label)
    count = tiled(group_count(marks, label), chans) * pixels
    mean_c, rstd_c = moments(row(total, 0), row(total, 1), count)
    mean_p, rstd_p = moments(row(total, 2), row(total, 3), count)
    for k, v in enumerate((mean_c, rstd_c, mean_p, rstd_p)):
        keeps[k : k + 1, :] = v
    group = scal[OWN]
    scale_c = rstd_c * gain_of(norm_c, group)
    scale_p = rstd_p * gain_of(norm_p, group)
    bias = (shift_of(norm_c, group) - mean_c * scale_c) + (
        shift_of(norm_p, group) - mean_p * scale_p
    )
    keep = valid_cols(chans)

    def put(i, carry):
        v = zc[i] * scale_c + zp[i] * scale_p + bias
        s = sigmoid(v)
        joined[i] = jnp.where(keep, v * s, 0.0).astype(BF16)
        slope[i] = s * (1.0 + v * (1.0 - s))
        return carry

    lax.fori_loop(0, rows, put, 0, unroll=2)
    step = rows // 4
    sums, squares = zeros8(LANES), zeros8(LANES)
    for c in range(4):
        values = mm(flat(joined[step * c : step * (c + 1)]), w[...])
        z[step * c : step * (c + 1)] = values.reshape(step, COLS, LANES)
        parts = values.reshape(-1, 8, LANES)
        sums = sums + jnp.sum(parts, axis=0)
        squares = squares + jnp.sum(parts * parts, axis=0)
    spread(send, [down(sums), down(squares)])


def f5(scal, got, labels, z_in, norm, w, x3, z, send, keeps):
    rows = z_in.shape[0]
    pixels = 1.0 * rows * (COLS - 4)
    mean, rstd, gain, shift, _ = scale_shift(got, labels[...], scal, norm, pixels)
    keeps[0:1, :] = mean
    keeps[1:2, :] = rstd
    scale = rstd * gain
    bias = shift - mean * scale
    keep = valid_cols(LANES) & chan_mask(scal[LIMIT], LANES)
    x3[0] = jnp.zeros(x3.shape[1:], BF16)
    x3[rows + 1] = jnp.zeros(x3.shape[1:], BF16)
    n = LANES

    def put(i, carry):
        v = z_in[i] * scale + bias
        act = jnp.where(keep, v * sigmoid(v), 0.0)
        x3[i + 1, :, 0:n] = pltpu.roll(act, 1, 0).astype(BF16)
        x3[i + 1, :, n : 2 * n] = act.astype(BF16)
        x3[i + 1, :, 2 * n : 3 * n] = pltpu.roll(act, COLS - 1, 0).astype(BF16)
        return carry

    lax.fori_loop(0, rows, put, 0, unroll=2)
    conv_stats(z, tuple((x3, y, 0, w[y]) for y in range(3)), send)


def f6(scal, got, labels, z_in, norm, w, act, z, send, keeps):
    activate(scal, got, labels, z_in, norm, act, keeps)
    expand(act, w, z, send)


def b7(scal, got, labels, joined, z, norm, cot, result, grad_pre, send, keeps):
    rows, chans = z.shape[0], z.shape[2]
    cols = COLS - 4
    pixels = 1.0 * rows * cols
    mean, rstd, gain, shift, _ = scale_shift(got, labels[...], scal, norm, pixels)
    keeps[0:1, :] = mean
    keeps[1:2, :] = rstd
    gate = 0.25 * scal[GATE].astype(F32)
    scale = rstd * gain * gate
    bias = (shift - mean * rstd * gain) * gate

    def put(i, carry):
        sums, products = carry
        zz = z[i, 0:cols, :]
        v = joined[i, 0:cols, :].astype(F32) + zz * scale + bias
        s = sigmoid(v)
        result[i] = (v * s).astype(BF16)
        g = cot[i].astype(F32) * (s * (1.0 + v * (1.0 - s)))
        grad_pre[i, 0:cols, :] = g
        grad_pre[i, cols:COLS, :] = jnp.zeros((COLS - cols, chans), F32)
        return sums + down(g), products + down(g * (zz - mean))

    start = jnp.zeros((1, chans), F32)
    sums, products = lax.fori_loop(0, rows, put, (start, start), unroll=2)
    spread(send, [sums * gate, products * rstd * gate])


def backward_norm(scal, got, labels, norm, keeps, pixels, grad_norm, slots=(0, 1)):
    marks = labels[...]
    chans = norm.shape[2]
    own_shift = jnp.zeros((1, chans), F32)
    own_gain = jnp.zeros((1, chans), F32)
    group = scal[OWN]
    for g in range(norm.shape[0]):
        total = group_sum(got, marks, float(g))
        shift_sum, gain_sum = row(total, slots[0]), row(total, slots[1])
        grad_norm[g, 0:1, :] = gain_sum
        grad_norm[g, 1:2, :] = shift_sum
        mine = group == g
        own_shift = jnp.where(mine, shift_sum, own_shift)
        own_gain = jnp.where(mine, gain_sum, own_gain)
    count = tiled(group_count(marks, group.astype(F32)), chans) * pixels
    mean, rstd = keeps[0:1, :], keeps[1:2, :]
    a = rstd * gain_of(norm, group)
    return mean, a, -(a * rstd) * own_gain / count, -a * own_shift / count


def slope_sums(scal, d, z_in, norm, keeps, dout, send):
    rows = z_in.shape[0]
    mean, rstd = keeps[0:1, :], keeps[1:2, :]
    group = scal[OWN]
    scale = rstd * gain_of(norm, group)
    bias = shift_of(norm, group) - mean * scale
    keep = valid_cols(LANES) & chan_mask(scal[LIMIT], LANES)

    def put(i, carry):
        sums, products = carry
        zz = z_in[i]
        v = zz * scale + bias
        s = sigmoid(v)
        g = jnp.where(keep, d[i] * (s * (1.0 + v * (1.0 - s))), 0.0)
        dout[i] = g
        return sums + fold(g), products + fold(g * (zz - mean))

    sums, products = lax.fori_loop(
        0, rows, put, (zeros8(LANES), zeros8(LANES)), unroll=4
    )
    spread(send, [down(sums), down(products) * rstd])


def b8(
    scal, got, labels, grad_pre, z, norm, keeps, w, z_in, norm_in, keeps_in,
    dz, dout, send, grad_norm, d,
):
    rows, chans = z.shape[0], z.shape[2]
    pixels = 1.0 * rows * (COLS - 4)
    mean, a, b, c = backward_norm(scal, got, labels, norm, keeps, pixels, grad_norm)
    a = a * (0.25 * scal[GATE].astype(F32))
    keep = valid_cols(chans)

    def put(i, carry):
        v = a * grad_pre[i] + b * (z[i] - mean) + c
        dz[i] = jnp.where(keep, v, 0.0).astype(BF16)
        return carry

    lax.fori_loop(0, rows, put, 0, unroll=2)
    d[...] = mm_nt(flat(dz[...]), w[...]).reshape(d.shape)
    slope_sums(scal, d, z_in, norm_in, keeps_in, dout, send)


def b9(
    scal, got, labels, dout_in, z, norm, keeps, b_same, z_in, norm_in, keeps_in,
    dz, dout, send, grad_norm, d3, d,
):
    rows = z.shape[0]
    pixels = 1.0 * rows * (COLS - 4)
    mean, a, b, c = backward_norm(scal, got, labels, norm, keeps, pixels, grad_norm)
    keep = valid_cols(LANES)
    n = LANES
    d3[0] = jnp.zeros(d3.shape[1:], BF16)
    d3[rows + 1] = jnp.zeros(d3.shape[1:], BF16)

    def put(i, carry):
        v = a * dout_in[i] + b * (z[i] - mean) + c
        v = jnp.where(keep, v, 0.0)
        d3[i + 1, :, 0:n] = pltpu.roll(v, COLS - 1, 0).astype(BF16)
        low = v.astype(BF16)
        d3[i + 1, :, n : 2 * n] = low
        dz[i] = low
        d3[i + 1, :, 2 * n : 3 * n] = pltpu.roll(v, 1, 0).astype(BF16)
        return carry

    lax.fori_loop(0, rows, put, 0, unroll=2)
    step = rows // 4
    for k in range(4):
        value = None
        for y in range(3):
            first = 2 - y + step * k
            term = mm_nt(flat(d3[first : first + step]), b_same[y])
            value = term if value is None else value + term
        d[step * k : step * (k + 1)] = value.reshape(step, COLS, LANES)
    slope_sums(scal, d, z_in, norm_in, keeps_in, dout, send)


def b10(
    scal, got, labels, dout_in, z, norm, keeps, w, grad_pre, slope, zc, zp, keeps_cp,
    dz, grad_pre_2, send, grad_norm, d,
):
    rows, chans = zc.shape[0], zc.shape[2]
    pixels = 1.0 * rows * (COLS - 4)
    mean, a, b, c = backward_norm(scal, got, labels, norm, keeps, pixels, grad_norm)
    keep = valid_cols(LANES)

    def put(i, carry):
        v = a * dout_in[i] + b * (z[i] - mean) + c
        dz[i] = jnp.where(keep, v, 0.0).astype(BF16)
        return carry

    lax.fori_loop(0, rows, put, 0, unroll=4)
    d[...] = mm_nt(flat(dz[...]), w[...]).reshape(d.shape)
    mean_c, rstd_c, mean_p, rstd_p = (keeps_cp[k : k + 1, :] for k in range(4))

    def sum_up(i, carry):
        sums, prod_c, prod_p = carry
        g = (grad_pre[i] + d[i]).astype(BF16).astype(F32) * slope[i]
        grad_pre_2[i] = g
        return (
            sums + fold(g),
            prod_c + fold(g * (zc[i] - mean_c)),
            prod_p + fold(g * (zp[i] - mean_p)),
        )

    start = zeros8(chans)
    sums, prod_c, prod_p = lax.fori_loop(0, rows, sum_up, (start, start, start), unroll=2)
    spread(send, [down(sums), down(prod_c) * rstd_c, down(prod_p) * rstd_p])


def b11(
    scal, got, labels, grad_pre_2, zc, zp, norm_c, norm_p, keeps_cp, w, z_in, norm_in, keeps_in,
    dz_c, dz_p, dout, send, grad_norm_c, grad_norm_p, d,
):
    rows, chans = zc.shape[0], zc.shape[2]
    pixels = 1.0 * rows * (COLS - 4)
    mean_c, a_c, b_c, c_c = backward_norm(
        scal, got, labels, norm_c, keeps_cp.at[0:2], pixels, grad_norm_c, (0, 1)
    )
    mean_p, a_p, b_p, c_p = backward_norm(
        scal, got, labels, norm_p, keeps_cp.at[2:4], pixels, grad_norm_p, (0, 2)
    )
    keep = valid_cols(chans)

    def put(i, carry):
        g = grad_pre_2[i]
        v = a_c * g + b_c * (zc[i] - mean_c) + c_c
        dz_c[i] = jnp.where(keep, v, 0.0).astype(BF16)
        v = a_p * g + b_p * (zp[i] - mean_p) + c_p
        dz_p[i] = jnp.where(keep, v, 0.0).astype(BF16)
        return carry

    lax.fori_loop(0, rows, put, 0, unroll=2)
    d[...] = mm_nt(flat(dz_c[...]), w[...]).reshape(d.shape)
    slope_sums(scal, d, z_in, norm_in, keeps_in, dout, send)


def b12(
    scal, got, labels, dout_in, z, norm, keeps, b_even, b_odd, z_own, z_oth, norm_in, keeps_in,
    dz, dn_own, dn_oth, send, grad_norm, d2, de, do, wide,
):
    rows = z.shape[0]
    pixels = 1.0 * rows * (COLS - 4)
    mean, a, b, c = backward_norm(scal, got, labels, norm, keeps, pixels, grad_norm)
    keep = valid_cols(LANES)
    n = LANES
    d2[rows] = jnp.zeros(d2.shape[1:], BF16)

    def put(i, carry):
        v = a * dout_in[i] + b * (z[i] - mean) + c
        v = jnp.where(keep, v, 0.0)
        low = v.astype(BF16)
        dz[i] = low
        d2[i, :, 0:n] = low
        d2[i, :, n : 2 * n] = pltpu.roll(v, COLS - 1, 0).astype(BF16)
        return carry

    lax.fori_loop(0, rows, put, 0, unroll=4)
    step = rows // 4
    for k in range(4):
        here = flat(d2[step * k : step * (k + 1)])
        below = flat(d2[step * k + 1 : step * (k + 1) + 1])
        de[step * k : step * (k + 1)] = mm_nt(here, b_even[...]).reshape(step, COLS, 2 * n)
        odd = mm_nt(here, b_odd[:, 0 : 2 * n]) + mm_nt(below, b_odd[:, 2 * n : 4 * n])
        do[step * k : step * (k + 1)] = odd.reshape(step, COLS, 2 * n)
    mean_1, rstd_1 = keeps_in[0:1, :], keeps_in[1:2, :]
    group = scal[OWN]
    scale = rstd_1 * gain_of(norm_in, group)
    bias = shift_of(norm_in, group) - mean_1 * scale
    keep = valid_cols(LANES) & chan_mask(scal[LIMIT], LANES)
    half = scal[HALF]
    totals = (zeros8(n), zeros8(n))
    for k, (zz, dn) in enumerate(((z_own, dn_own), (z_oth, dn_oth))):
        first = (rows // 2) * (half if k == 0 else 1 - half)

        def emit(i, carry, zz=zz, dn=dn, first=first):
            sums, products = carry
            for ra in (0, 1):
                planes = (de, do)[ra]
                for cb in (0, 1):
                    zv = zz[2 * i + ra, pl.ds(cb, COLS, stride=2), :]
                    v = zv * scale + bias
                    s = sigmoid(v)
                    g = planes[first + i, :, n * cb : n * (cb + 1)]
                    g = jnp.where(keep, g * (s * (1.0 + v * (1.0 - s))), 0.0)
                    sums = sums + fold(g)
                    products = products + fold(g * (zv - mean_1))
                    wide[ra, pl.ds(cb, COLS, stride=2), :] = g
                dn[2 * i + ra] = wide[ra].astype(BF16)
            return sums, products

        totals = lax.fori_loop(0, rows // 2, emit, totals, unroll=2)
    spread(send, [down(totals[0]), down(totals[1]) * rstd_1])


def b13(
    scal, got, labels, norm, keeps, w, z_own, z_for, dn_own, dn_for, gs_own, gs_for,
    grad, grad_norm, dz, wide,
):
    rows, cols = grad.shape[1], grad.shape[2]
    half = scal[HALF]
    pixels = 2.0 * rows * cols
    marks = labels[...]
    totals = []
    for g in range(norm.shape[0]):
        total = group_sum(got, marks, float(g))
        totals.append((row(total, 0), row(total, 1)))
        grad_norm[g, 0:1, :] = totals[g][1]
        grad_norm[g, 1:2, :] = totals[g][0]
    keep = lax.broadcasted_iota(jnp.int32, (z_own.shape[1], LANES), 0) < cols
    for k, (z, dn, gs) in enumerate(((z_own, dn_own, gs_own), (z_for, dn_for, gs_for))):
        group = scal[OWN if k == 0 else OTHER]
        shift_sum, gain_sum = totals[0]
        for g in range(1, norm.shape[0]):
            shift_sum = jnp.where(group == g, totals[g][0], shift_sum)
            gain_sum = jnp.where(group == g, totals[g][1], gain_sum)
        count = group_count(marks, group.astype(F32)) * pixels
        mean, rstd = keeps[2 * k : 2 * k + 1, :], keeps[2 * k + 1 : 2 * k + 2, :]
        a = rstd * gain_of(norm, group)
        b = -(a * rstd) * gain_sum / count
        c = -a * shift_sum / count

        def put(i, carry, z=z, dn=dn, mean=mean, a=a, b=b, c=c):
            v = a * dn[i].astype(F32) + b * (z[i] - mean) + c
            dz[i] = jnp.where(keep, v, 0.0).astype(BF16)
            return carry

        lax.fori_loop(0, rows, put, 0, unroll=2)
        step = rows // 4
        for q in range(4):
            low = flat(dz[step * q : step * (q + 1)])
            for p in range(wide.shape[0]):
                values = mm_nt(low, w[LANES * p : LANES * (p + 1), :])
                wide[p, step * q : step * (q + 1)] = values.reshape(step, -1, LANES)
        place = half if k == 0 else 1 - half

        def emit(i, carry, gs=gs, place=place):
            even = pl.ds(0, COLS, stride=2)
            for p in range(wide.shape[0]):
                lanes = slice(LANES * p, LANES * (p + 1))
                wide[p, 2 * i, even, :] = wide[p, 2 * i, even, :] + gs[i, :, lanes].astype(F32)
                grad[place, 2 * i, :, lanes] = wide[p, 2 * i, 0:cols, :].astype(BF16)
                grad[place, 2 * i + 1, :, lanes] = wide[p, 2 * i + 1, 0:cols, :].astype(BF16)
            return carry

        lax.fori_loop(0, rows // 2, emit, 0, unroll=2)


def put_rows(out, at, value):
    for j in range(value.shape[1] // LANES):
        out[at : at + value.shape[0], :] = value[:, LANES * j : LANES * (j + 1)].astype(BF16)
        at += value.shape[0]
    return at


def take_rows(source, at, out):
    rows = out.shape[0]
    for j in range(out.shape[1] // LANES):
        out[:, LANES * j : LANES * (j + 1)] = source(at, rows)
        at += rows
    return at


def g_most(
    scal, act_2b, dz_2c, x3, dz_2b, joined, dz_2a, act_1b, dz_1c, xee, dz_1p, w_1p,
    out, gs_own, gs_oth,
):
    rows = dz_2b.shape[0]
    at = put_rows(out, 0, mm_tn(flat(act_2b[...]), flat(dz_2c[...])))
    low = flat(dz_2b[...])
    for y in range(3):
        at = put_rows(out, at, mm_tn(flat(x3[y : y + rows]), low))
    at = put_rows(out, at, mm_tn(flat(joined[...]), flat(dz_2a[...])))
    at = put_rows(out, at, mm_tn(flat(act_1b[...]), flat(dz_1c[...])))
    put_rows(out, at, mm_tn(flat(xee[...]), flat(dz_1p[...])))
    half = scal[HALF]
    count = gs_own.shape[0]
    for k, gs in enumerate((gs_own, gs_oth)):
        first = count * (half if k == 0 else 1 - half)
        got = mm_nt(flat(dz_1p[pl.ds(first, count)]), w_1p[...])
        gs[...] = got.reshape(gs.shape).astype(BF16)


def g_1b(xs, dz, out):
    rows = dz.shape[0]
    low = flat(dz[...])
    n = LANES
    cur = mm_tn(flat(xs[1 : rows + 1]), low)
    for k, (y, x) in enumerate(((1, 1), (1, 2), (1, 0), (2, 1), (2, 2), (2, 0))):
        put_rows(out, n * (3 * y + x), cur[n * k : n * (k + 1)])
    up = mm_tn(flat(xs[0:rows, :, 3 * n : 6 * n]), low)
    for k, (y, x) in enumerate(((0, 1), (0, 2), (0, 0))):
        put_rows(out, n * (3 * y + x), up[n * k : n * (k + 1)])


def g_1a(
    scal, got, labels, norm, keeps, z_own, z_oth, dn_own, dn_oth, x_own, x_oth, most, grad_1b,
    kept, sent, dz, packed,
):
    rows = z_own.shape[0]
    cols = 2 * (COLS - 4)
    pixels = 2.0 * rows * cols
    marks = labels[...]
    group = scal[OWN]
    total = group_sum(got, marks, group.astype(F32))
    count = group_count(marks, group.astype(F32)) * pixels
    mean, rstd = keeps[0:1, :], keeps[1:2, :]
    a = rstd * gain_of(norm, group)
    b = -(a * rstd) * row(total, 1) / count
    c = -a * row(total, 0) / count
    keep = lax.broadcasted_iota(jnp.int32, (z_own.shape[1], LANES), 0) < cols
    value = None
    for z, dn, x in ((z_own, dn_own, x_own), (z_oth, dn_oth, x_oth)):

        def put(i, carry, z=z, dn=dn):
            v = a * dn[i].astype(F32) + b * (z[i] - mean) + c
            dz[i] = jnp.where(keep, v, 0.0).astype(BF16)
            return carry

        lax.fori_loop(0, rows, put, 0, unroll=2)
        term = mm_tn(flat(x[...]), flat(dz[...]))
        value = term if value is None else value + term
    at = put_rows(packed, 0, value)
    packed[at : at + grad_1b.shape[0], :] = grad_1b[...]
    at += grad_1b.shape[0]
    packed[at : at + most.shape[0], :] = most[...]
    at += most.shape[0]
    if at < packed.shape[0]:
        packed[at:, :] = jnp.zeros((packed.shape[0] - at, LANES), BF16)
    half = scal[HALF]
    size = kept.shape[0] * kept.shape[1]
    for out, place in ((kept, half), (sent, 1 - half)):
        out[...] = packed[pl.ds(pl.multiple_of(size * place, 16), size), :].reshape(out.shape)


def add_pair(kept, received, out):
    out[...] = (kept[...].astype(F32) + received[...].astype(F32)).astype(BF16)


def add_all(parts, out):
    half = parts.shape[0] // 2
    for k in (0, 1):
        total = jnp.sum(parts[half * k : half * (k + 1)].astype(F32), axis=0).astype(BF16)
        out[half * k : half * (k + 1)] = jnp.broadcast_to(total[None], (half, *total.shape))


def unpack(scal, own, other, w_1a, w_1b, w_2c, w_2b, w_2a, w_1c, w_1p, packed):
    half = scal[HALF]
    size = own.shape[0]
    for part, place in ((own, half), (other, 1 - half)):
        packed[pl.ds(pl.multiple_of(size * place, 16), size), :] = part[...]

    def source(at, rows):
        return packed[at : at + rows, :].astype(F32)

    at = 0
    for out in (w_1a, w_1b, w_2c, w_2b, w_2a, w_1c, w_1p):
        at = take_rows(source, at, out)


def gather(send):
    return lax.all_to_all(send, AXES, 0, 0)


def tie(*values):
    return lax.optimization_barrier(values)


def swap(block):
    return lax.ppermute(block, "rows", [(0, 1), (1, 0)])


def body(
    images, w_1a, w_1b, w_1c, w_1p, w_2a, w_2b, w_2c,
    norm_1a, norm_1b, norm_1c, norm_1p, norm_2a, norm_2b, norm_2c,
    cotangent, group, width, gate,
):
    devices = lax.axis_size("rows") * lax.axis_size("batch")
    half = lax.axis_index("rows").astype(jnp.int32).reshape(1)
    norms = (norm_1a, norm_1b, norm_1c, norm_1p, norm_2a, norm_2b, norm_2c)
    norm_1a, norm_1b, norm_1c, norm_1p, norm_2a, norm_2b, norm_2c = (
        v.transpose(1, 0, 2) for v in norms
    )
    outer, inputs = w_1c.shape[1], w_1a.shape[0]
    rows = cotangent.shape[1]
    cols_in = 2 * COLS
    n, m = LANES, devices

    def send(stats, channels=LANES):
        return ((m, channels // LANES, stats * LANES), F32)

    def maps(channels, dtype=F32):
        return ((rows, COLS, channels), dtype)

    def scratch(channels, dtype=F32):
        return pltpu.VMEM((rows, COLS, channels), dtype)

    def params(*arrays):
        return [(a.shape, F32) for a in arrays]

    def mean_scale(channels, count=1):
        return ((2 * count, channels), F32)

    wide_in = ((rows, cols_in, inputs), BF16)
    wide_z = ((rows, cols_in, n), F32)
    scal, x_own, x_for, z_own, z_for, s1 = stage(
        f1, [((8,), jnp.int32), wide_in, wide_in, wide_z, wide_z, send(5)],
        smem=(0, 1, 2, 3), smem_out=(0,),
    )(half, group, width, gate, images, w_1a)
    x_oth = swap(x_for)
    g1 = gather(s1)
    w_cur, w_up, b_even, b_odd, b_same = stage(
        prepare,
        [((6 * n, n), BF16), ((3 * n, n), BF16), ((2 * n, 2 * n), BF16), ((2 * n, 4 * n), BF16),
         ((3, n, 3 * n), BF16)],
        smem=(),
    )(w_1b, w_2b)
    g1, w_cur, w_up = tie(g1, w_cur, w_up)
    xs, z_1b, s2, labels, k_1a, z_oth = stage(
        f2,
        [((rows + 1, COLS, 6 * n), BF16), maps(n), send(2), ((m, 1, n), F32), mean_scale(n, 2),
         wide_z],
    )(scal, g1, z_own, x_oth, w_1a, norm_1a, w_cur, w_up)
    xee, z_1p, stats_1p = stage(
        f1_strided,
        [maps(inputs, BF16), maps(outer), ((2, 1, outer), F32)],
        [pltpu.VMEM((inputs // n, cols_in, n), F32)],
    )(scal, x_own, x_oth, w_1p)
    s2, xee, z_1p, stats_1p = tie(s2, xee, z_1p, stats_1p)
    g2 = gather(s2)
    act_1b, z_1c, s3, k_1b = stage(
        f3, [maps(n, BF16), maps(outer), send(4, outer), mean_scale(n)]
    )(scal, g2, labels, z_1b, norm_1b, w_1c, stats_1p)
    g3 = gather(s3)
    joined, slope, z_2a, s4, k_cp = stage(
        f4, [maps(outer, BF16), maps(outer), maps(n), send(2), mean_scale(outer, 2)]
    )(scal, g3, labels, z_1c, z_1p, norm_1c, norm_1p, w_2a)
    g4 = gather(s4)
    x3, z_2b, s5, k_2a = stage(
        f5, [((rows + 2, COLS, 3 * n), BF16), maps(n), send(2), mean_scale(n)]
    )(scal, g4, labels, z_2a, norm_2a, w_2b.reshape(3, 3 * n, n))
    g5 = gather(s5)
    act_2b, z_2c, s6, k_2b = stage(
        f6, [maps(n, BF16), maps(outer), send(2, outer), mean_scale(n)]
    )(scal, g5, labels, z_2b, norm_2b, w_2c)
    g6 = gather(s6)
    result, grad_pre, s7, k_2c = stage(
        b7, [(cotangent.shape[1:], BF16), maps(outer), send(2, outer), mean_scale(outer)]
    )(scal, g6, labels, joined, z_2c, norm_2c, cotangent[0])
    g7 = gather(s7)
    dz_2c, dout_2b, s8, grad_norm_2c = stage(
        b8, [maps(outer, BF16), maps(n), send(2), *params(norm_2c)], [scratch(n)]
    )(scal, g7, labels, grad_pre, z_2c, norm_2c, k_2c, w_2c, z_2b, norm_2b, k_2b)
    g8 = gather(s8)
    dz_2b, dout_2a, s9, grad_norm_2b = stage(
        b9, [maps(n, BF16), maps(n), send(2), *params(norm_2b)],
        [pltpu.VMEM((rows + 2, COLS, 3 * n), BF16), scratch(n)],
    )(scal, g8, labels, dout_2b, z_2b, norm_2b, k_2b, b_same, z_2a, norm_2a, k_2a)
    g9 = gather(s9)
    dz_2a, grad_pre_2, s10, grad_norm_2a = stage(
        b10, [maps(n, BF16), maps(outer), send(3, outer), *params(norm_2a)], [scratch(outer)]
    )(scal, g9, labels, dout_2a, z_2a, norm_2a, k_2a, w_2a, grad_pre, slope, z_1c, z_1p, k_cp)
    g10 = gather(s10)
    dz_1c, dz_1p, dout_1b, s11, grad_norm_1c, grad_norm_1p = stage(
        b11, [maps(outer, BF16), maps(outer, BF16), maps(n), send(2), *params(norm_1c, norm_1p)],
        [scratch(n)],
    )(scal, g10, labels, grad_pre_2, z_1c, z_1p, norm_1c, norm_1p, k_cp, w_1c, z_1b, norm_1b, k_1b)
    half_map = ((rows // 2, COLS, inputs), BF16)
    most_rows = sum(v.size for v in (w_2c, w_2b, w_2a, w_1c, w_1p)) // n
    most, gs_own, gs_send = stage(g_most, [((most_rows, n), BF16), half_map, half_map])(
        scal, act_2b, dz_2c, x3, dz_2b, joined, dz_2a, act_1b, dz_1c, xee, dz_1p, w_1p
    )
    s11, most, gs_own, gs_send = tie(s11, most, gs_own, gs_send)
    gs_for = swap(gs_send)
    g11 = gather(s11)
    half_in = ((rows, cols_in, n), BF16)
    dz_1b, dn_own, dn_send, s12, grad_norm_1b = stage(
        b12, [maps(n, BF16), half_in, half_in, send(2), *params(norm_1b)],
        [pltpu.VMEM((rows + 1, COLS, 2 * n), BF16), scratch(2 * n), scratch(2 * n),
         pltpu.VMEM((2, cols_in, n), F32)],
    )(scal, g11, labels, dout_1b, z_1b, norm_1b, k_1b, b_even, b_odd, z_own, z_oth, norm_1a, k_1a)
    (grad_1b,) = stage(g_1b, [((w_1b.size // n, n), BF16)], smem=())(xs, dz_1b)
    s12, grad_1b, dn_own, dn_send = tie(s12, grad_1b, dn_own, dn_send)
    dn_for = swap(dn_send)
    g12 = gather(s12)
    all_rows = most_rows + (w_1b.size + w_1a.size) // n
    unit = 2 * devices * 16
    piece = -(-all_rows // unit) * 16
    share = ((devices, piece, n), BF16)
    kept, sent = stage(
        g_1a, [share, share],
        [pltpu.VMEM(half_in[0], BF16), pltpu.VMEM((2 * devices * piece, n), BF16)],
    )(scal, g12, labels, norm_1a, k_1a, z_own, z_oth, dn_own, dn_send, x_own, x_oth, most, grad_1b)
    (pair,) = stage(add_pair, [share], smem=())(kept, swap(sent))
    (mine,) = stage(add_all, [share], smem=())(gather(pair))
    grad_images, grad_norm_1a = stage(
        b13, [(images.shape, BF16), *params(norm_1a)],
        [pltpu.VMEM(half_in[0], BF16), pltpu.VMEM((inputs // n, rows, cols_in, n), F32)],
    )(scal, g12, labels, norm_1a, k_1a, w_1a, z_own, z_for, dn_own, dn_for, gs_own, gs_for)
    part = gather(mine).reshape(devices * piece, n)
    totals = stage(
        unpack,
        [(v.shape, F32) for v in (w_1a, w_1b.reshape(-1, n), w_2c, w_2b.reshape(-1, n), w_2a, w_1c, w_1p)],
        [pltpu.VMEM((2 * devices * piece, n), BF16)],
    )(scal, part, swap(part))
    t_1a, t_1b, t_2c, t_2b, t_2a, t_1c, t_1p = totals
    grads = (
        grad_norm_1a, grad_norm_1b, grad_norm_1c, grad_norm_1p,
        grad_norm_2a, grad_norm_2b, grad_norm_2c,
    )
    return (
        result[None], grad_images, t_1a, t_1b.reshape(w_1b.shape), t_1c, t_1p, t_2a,
        t_2b.reshape(w_2b.shape), t_2c, *[v.transpose(1, 0, 2) for v in grads],
    )


def solution(mesh):
    return jax.shard_map(
        body,
        mesh=mesh,
        in_specs=(
            P("batch", "rows", None, None),
            *[P()] * 14,
            P(("batch", "rows"), None, None, None),
            P("batch"),
            P(),
            P(),
        ),
        out_specs=(
            P(("batch", "rows"), None, None, None),
            P("batch", "rows", None, None),
            *[P()] * 14,
        ),
        check_vma=False,
    )
```

```python
import functools

import jax
import jax.numpy as jnp
from jax import lax
from jax.experimental import pallas as pl
from jax.experimental.pallas import tpu as pltpu
from jax.sharding import PartitionSpec as P

EPSILON = 1e-05
F32 = jnp.float32
BF16 = jnp.bfloat16
AXES = ("rows", "batch")
VMEM_LIMIT = 14 * 1024 * 1024
LANES = 128
COLS = 32


def full(memory=pltpu.VMEM):
    return pl.BlockSpec(memory_space=memory)


def stage(kernel, outs, scratch=(), smem=(0,), smem_out=(), hbm=()):
    def place(i):
        return pltpu.SMEM if i in smem else pltpu.HBM if i in hbm else pltpu.VMEM

    def call(*args):
        args = [
            pltpu.with_memory_space_constraint(a, pltpu.HBM) if i in hbm else a
            for i, a in enumerate(args)
        ]
        return pl.pallas_call(
            kernel,
            out_shape=tuple(jax.ShapeDtypeStruct(s, d) for s, d in outs),
            in_specs=[full(place(i)) for i in range(len(args))],
            out_specs=tuple(
                full(pltpu.SMEM if i in smem_out else pltpu.VMEM) for i in range(len(outs))
            ),
            scratch_shapes=list(scratch),
            compiler_params=pltpu.CompilerParams(vmem_limit_bytes=VMEM_LIMIT),
            name=(kernel.func if isinstance(kernel, functools.partial) else kernel).__name__,
        )(*args)

    return call


def sigmoid(v):
    return 0.5 * jnp.tanh(0.5 * v) + 0.5


def fold(x):
    return (x[0:8] + x[8:16]) + (x[16:24] + x[24:32])


def row(total, stat):
    blocks = total.shape[0]
    pieces = [total[j : j + 1, LANES * stat : LANES * (stat + 1)] for j in range(blocks)]
    return pieces[0] if blocks == 1 else jnp.concatenate(pieces, axis=1)


def spread(out_ref, rows):
    blocks = out_ref.shape[1]
    for stat, values in enumerate(rows):
        for j in range(blocks):
            piece = values[:, LANES * j : LANES * (j + 1)]
            out_ref[:, j : j + 1, LANES * stat : LANES * (stat + 1)] = jnp.broadcast_to(
                piece[None], (out_ref.shape[0], 1, LANES)
            )


def group_sum(got_ref, labels, label):
    same = (labels == label).astype(F32)
    stats = got_ref.shape[2] // LANES
    parts = [
        jnp.sum(got_ref[:, :, LANES * s : LANES * (s + 1)] * same, axis=0) for s in range(stats)
    ]
    return jnp.concatenate(parts, axis=1) if stats > 1 else parts[0]


def group_count(labels, label):
    return jnp.sum((labels == label).astype(F32), axis=0)


def tiled(values, channels):
    return jnp.concatenate([values] * (channels // LANES), axis=1) if channels > LANES else values


def moments(first, second, pixels):
    mean = first / pixels
    return mean, lax.rsqrt(second / pixels - mean * mean + EPSILON)


def gain_of(norm_ref, group):
    return norm_ref[group, 0:1, :]


def shift_of(norm_ref, group):
    return norm_ref[group, 1:2, :]


def valid_cols(channels):
    return lax.broadcasted_iota(jnp.int32, (COLS, channels), 0) < COLS - 4


def chan_mask(limit, channels):
    return lax.broadcasted_iota(jnp.int32, (1, channels), 1) < limit


def flat(x):
    return x.reshape(x.shape[0] * x.shape[1], x.shape[2])


def mm(a, b):
    return jnp.dot(a, b, preferred_element_type=F32)


def mm_nt(a, b):
    return lax.dot_general(a, b, (((1,), (1,)), ((), ())), preferred_element_type=F32)


def mm_tn(a, b):
    return lax.dot_general(a, b, (((0,), (0,)), ((), ())), preferred_element_type=F32)


def zeros8(channels):
    return jnp.zeros((8, channels), F32)


def down(x):
    return jnp.sum(x, axis=0, keepdims=True)


OWN, OTHER, HALF, LIMIT, GATE = range(5)


def prepare(w1b, w2b, w_cur, w_up, b_even, b_odd, b_same):
    n = LANES
    for k, (y, x) in enumerate(((1, 1), (1, 2), (1, 0), (2, 1), (2, 2), (2, 0))):
        w_cur[n * k : n * (k + 1), :] = w1b[y, x]
    for k, (y, x) in enumerate(((0, 1), (0, 2), (0, 0))):
        w_up[n * k : n * (k + 1), :] = w1b[y, x]
    nothing = jnp.zeros((n, n), BF16)
    b_even[0:n, 0:n] = w1b[1, 1]
    b_even[0:n, n : 2 * n] = nothing
    b_even[n : 2 * n, 0:n] = w1b[1, 2]
    b_even[n : 2 * n, n : 2 * n] = w1b[1, 0]
    for k, top in ((0, 2), (1, 0)):
        b_odd[0:n, 2 * n * k : 2 * n * k + n] = w1b[top, 1]
        b_odd[0:n, 2 * n * k + n : 2 * n * (k + 1)] = nothing
        b_odd[n : 2 * n, 2 * n * k : 2 * n * k + n] = w1b[top, 2]
        b_odd[n : 2 * n, 2 * n * k + n : 2 * n * (k + 1)] = w1b[top, 0]
    for y in range(3):
        for x in range(3):
            b_same[y, :, n * x : n * (x + 1)] = w2b[y, x]


def widen(source, x_pad):
    rows, cols, chans = source.shape
    gap = x_pad.shape[1] - cols

    def put(i, carry):
        x_pad[i, 0:cols, :] = source[i]
        x_pad[i, cols : cols + gap, :] = jnp.zeros((gap, chans), BF16)
        return carry

    lax.fori_loop(0, rows, put, 0, unroll=4)


def first_project(x_pad, w, z, stats=True):
    rows = x_pad.shape[0]
    step = rows // 4
    sums, squares = zeros8(LANES), zeros8(LANES)
    for c in range(4):
        values = mm(flat(x_pad[step * c : step * (c + 1)]), w[...])
        z[step * c : step * (c + 1)] = values.reshape(step, x_pad.shape[1], LANES)
        if stats:
            parts = values.reshape(-1, 8, LANES)
            sums = sums + jnp.sum(parts, axis=0)
            squares = squares + jnp.sum(parts * parts, axis=0)
    return sums, squares


def f1(
    half_ref, group_at, width_at, gate_at, images, w_at, scal, x_own, x_for, z_own, z_for, send,
    group, width, gate, raw, w, sems,
):
    half = half_ref[0]
    small = [
        pltpu.make_async_copy(a, b, sems.at[k])
        for k, (a, b) in enumerate(((group_at, group), (width_at, width), (gate_at, gate)))
    ]
    large = [
        pltpu.make_async_copy(images.at[place], raw.at[k], sems.at[3 + k])
        for k, place in enumerate((half, 1 - half))
    ]
    weight = pltpu.make_async_copy(w_at, w, sems.at[5])
    for copy in (weight, *large, *small):
        copy.start()
    weight.wait()
    rows = []
    for k, (x_pad, z) in enumerate(((x_own, z_own), (x_for, z_for))):
        large[k].wait()
        widen(raw.at[k], x_pad)
        sums, squares = first_project(x_pad, w, z)
        rows += [down(sums), down(squares)]
    for copy in small:
        copy.wait()
    own, other = group[half], group[1 - half]
    scal[OWN] = own
    scal[OTHER] = other
    scal[HALF] = half
    scal[LIMIT] = w.shape[1] // 4 * width[own]
    scal[GATE] = gate[own]
    for k in range(GATE + 1, scal.shape[0]):
        scal[k] = 0
    spread(send, [*rows, jnp.full((1, LANES), (own + 4 * other).astype(F32))])


def f1_strided(scal, x_own, x_oth, w, xee, z, stats, wide):
    half = scal[HALF]
    rows = x_own.shape[0] // 2
    for k, x_pad in enumerate((x_own, x_oth)):
        first = rows * (half if k == 0 else 1 - half)

        def put(i, carry, x_pad=x_pad, first=first):
            for b in range(wide.shape[0]):
                lanes = slice(LANES * b, LANES * (b + 1))
                wide[b] = x_pad[2 * i, :, lanes].astype(F32)
                xee[first + i, :, lanes] = wide[b, pl.ds(0, COLS, stride=2), :].astype(BF16)
            return carry

        lax.fori_loop(0, rows, put, 0, unroll=2)
    total = 2 * rows
    step = total // 7
    chans = z.shape[2]
    sums, squares = zeros8(chans), zeros8(chans)
    for c in range(7):
        values = mm(flat(xee[step * c : step * (c + 1)]), w[...])
        z[step * c : step * (c + 1)] = values.reshape(step, COLS, chans)
        parts = values.reshape(-1, 8, chans)
        sums = sums + jnp.sum(parts, axis=0)
        squares = squares + jnp.sum(parts * parts, axis=0)
    stats[0] = down(sums)
    stats[1] = down(squares)


def scale_shift(got, labels, scal, norm, pixels, slot=0):
    label = scal[OWN].astype(F32)
    total = group_sum(got, labels, label)
    chans = norm.shape[2]
    count = tiled(group_count(labels, label), chans) * pixels
    mean, rstd = moments(row(total, 2 * slot), row(total, 2 * slot + 1), count)
    gain, shift = gain_of(norm, scal[OWN]), shift_of(norm, scal[OWN])
    return mean, rstd, gain, shift, count


def conv_stats(z, pieces, send, extra=()):
    keep = valid_cols(LANES)[None]
    rows = z.shape[0]
    step = rows // 4
    sums, squares = zeros8(LANES), zeros8(LANES)
    for c in range(4):
        values = None
        for source, first, lane, weight in pieces:
            term = mm(flat(source[first + step * c : first + step * (c + 1), :, lane:]), weight)
            values = term if values is None else values + term
        values = jnp.where(keep, values.reshape(step, COLS, LANES), 0.0)
        z[step * c : step * (c + 1)] = values
        parts = values.reshape(-1, 8, LANES)
        sums = sums + jnp.sum(parts, axis=0)
        squares = squares + jnp.sum(parts * parts, axis=0)
    spread(send, [down(sums), down(squares), *extra])


def f2(
    scal, got, z_own, x_own, x_oth, w, norm, w_cur, w_up, stats_p,
    xs, z, send, labels, keeps, keeps_all, z_oth, x_sum,
):
    codes = got[:, :, 4 * LANES : 5 * LANES]
    others = jnp.floor(0.25 * codes)
    marks = codes - 4.0 * others
    labels[...] = marks
    rows = xs.shape[0] - 1
    pixels = 4.0 * rows * (COLS - 4)
    first_project(x_oth, w, z_oth, False)
    for g in range(norm.shape[0]):
        mine, theirs = (marks == float(g)).astype(F32), (others == float(g)).astype(F32)
        totals = [
            jnp.sum(
                got[:, :, LANES * s : LANES * (s + 1)] * mine
                + got[:, :, LANES * (s + 2) : LANES * (s + 3)] * theirs,
                axis=0,
            )
            for s in (0, 1)
        ]
        mean, rstd = moments(*totals, group_count(marks, float(g)) * pixels)
        keeps_all[2 * g : 2 * g + 1, :] = mean
        keeps_all[2 * g + 1 : 2 * g + 2, :] = rstd
    for k, slot in enumerate((OWN, OTHER)):
        at = 2 * scal[slot]
        keeps[2 * k : 2 * k + 1, :] = keeps_all[pl.ds(at, 1), :]
        keeps[2 * k + 1 : 2 * k + 2, :] = keeps_all[pl.ds(at + 1, 1), :]
    mean, rstd = keeps[0:1, :], keeps[1:2, :]
    gain, shift = gain_of(norm, scal[OWN]), shift_of(norm, scal[OWN])
    ones = jnp.ones((8, x_own.shape[0] * x_own.shape[1]), BF16)
    x_sum[...] = mm(ones, flat(x_own[...])) + mm(ones, flat(x_oth[...]))
    scale = rstd * gain
    bias = shift - mean * scale
    keep = valid_cols(LANES) & chan_mask(scal[LIMIT], LANES)
    half = scal[HALF]
    xs[0] = jnp.zeros(xs.shape[1:], BF16)
    n = LANES
    for k, zz in enumerate((z_own, z_oth)):
        first = 1 + (rows // 2) * (half if k == 0 else 1 - half)

        def put(i, carry, zz=zz, first=first):
            lane = 0
            for a in (0, 1):
                for b in (0, 1):
                    v = zz[2 * i + a, pl.ds(b, COLS, stride=2), :] * scale + bias
                    act = jnp.where(keep, v * sigmoid(v), 0.0)
                    xs[first + i, :, lane : lane + n] = act.astype(BF16)
                    lane += n
                    if b == 1:
                        moved = pltpu.roll(act, 1, 0)
                        xs[first + i, :, lane : lane + n] = moved.astype(BF16)
                        lane += n
            return carry

        lax.fori_loop(0, rows // 2, put, 0, unroll=2)
    extra = [x_sum[0:1, n * b : n * (b + 1)] for b in range(x_sum.shape[1] // n)]
    for k in (0, 1):
        extra += [stats_p[k, :, n * b : n * (b + 1)] for b in range(stats_p.shape[2] // n)]
    conv_stats(z, ((xs, 1, 0, w_cur[...]), (xs, 0, 3 * n, w_up[...])), send, extra)


def expand(act, w, z, send, extra=()):
    rows, chans = z.shape[0], z.shape[2]
    step = rows // 7
    sums, squares = zeros8(chans), zeros8(chans)
    for c in range(7):
        values = mm(flat(act[step * c : step * (c + 1)]), w[...])
        z[step * c : step * (c + 1)] = values.reshape(step, COLS, chans)
        parts = values.reshape(-1, 8, chans)
        sums = sums + jnp.sum(parts, axis=0)
        squares = squares + jnp.sum(parts * parts, axis=0)
    spread(send, [down(sums), down(squares), *extra])


def activate(scal, got, labels, z_in, norm, act, keeps):
    got = got.at[:, :, 0 : 2 * LANES]
    rows = z_in.shape[0]
    pixels = 1.0 * rows * (COLS - 4)
    mean, rstd, gain, shift, _ = scale_shift(got, labels[...], scal, norm, pixels)
    keeps[0:1, :] = mean
    keeps[1:2, :] = rstd
    scale = rstd * gain
    bias = shift - mean * scale
    keep = valid_cols(LANES) & chan_mask(scal[LIMIT], LANES)

    def put(i, carry):
        v = z_in[i] * scale + bias
        act[i] = jnp.where(keep, v * sigmoid(v), 0.0).astype(BF16)
        return carry

    lax.fori_loop(0, rows, put, 0, unroll=4)


def f3(scal, got, labels, z_in, norm, w, x_sum, act, z, send, keeps, keeps_p, x_dev):
    activate(scal, got, labels, z_in, norm, act, keeps)
    expand(act, w, z, send)
    marks = labels[...]
    label = scal[OWN].astype(F32)
    inputs, outer = x_sum.shape[1] // LANES, z.shape[2] // LANES
    total = group_sum(got, marks, label)
    images = group_count(marks, label)
    for b in range(inputs):
        lanes = slice(LANES * b, LANES * (b + 1))
        x_dev[:, lanes] = x_sum[0:1, lanes] - row(total, 2 + b) / images
    pixels = images * (1.0 * z.shape[0] * (COLS - 4))
    for b in range(outer):
        lanes = slice(LANES * b, LANES * (b + 1))
        first = 2 + inputs + b
        mean, rstd = moments(row(total, first), row(total, first + outer), pixels)
        keeps_p[0:1, lanes] = mean
        keeps_p[1:2, lanes] = rstd


def f4(scal, got, labels, zc, zp, norm_c, norm_p, keeps_p, w, joined, slope, z, send, keeps):
    rows, chans = zc.shape[0], zc.shape[2]
    pixels = 1.0 * rows * (COLS - 4)
    label = scal[OWN].astype(F32)
    marks = labels[...]
    total = group_sum(got, marks, label)
    count = tiled(group_count(marks, label), chans) * pixels
    mean_c, rstd_c = moments(row(total, 0), row(total, 1), count)
    mean_p, rstd_p = keeps_p[0:1, :], keeps_p[1:2, :]
    for k, v in enumerate((mean_c, rstd_c, mean_p, rstd_p)):
        keeps[k : k + 1, :] = v
    group = scal[OWN]
    scale_c = rstd_c * gain_of(norm_c, group)
    scale_p = rstd_p * gain_of(norm_p, group)
    bias = (shift_of(norm_c, group) - mean_c * scale_c) + (
        shift_of(norm_p, group) - mean_p * scale_p
    )
    keep = valid_cols(chans)

    def put(i, carry):
        v = zc[i] * scale_c + zp[i] * scale_p + bias
        s = sigmoid(v)
        joined[i] = jnp.where(keep, v * s, 0.0).astype(BF16)
        slope[i] = s * (1.0 + v * (1.0 - s))
        return carry

    lax.fori_loop(0, rows, put, 0, unroll=2)
    step = rows // 4
    sums, squares = zeros8(LANES), zeros8(LANES)
    for c in range(4):
        values = mm(flat(joined[step * c : step * (c + 1)]), w[...])
        z[step * c : step * (c + 1)] = values.reshape(step, COLS, LANES)
        parts = values.reshape(-1, 8, LANES)
        sums = sums + jnp.sum(parts, axis=0)
        squares = squares + jnp.sum(parts * parts, axis=0)
    spread(send, [down(sums), down(squares)])


def f5(scal, got, labels, z_in, norm, w, xz, x3, z, send, keeps):
    rows = z_in.shape[0]
    pixels = 1.0 * rows * (COLS - 4)
    mean, rstd, gain, shift, _ = scale_shift(got, labels[...], scal, norm, pixels)
    keeps[0:1, :] = mean
    keeps[1:2, :] = rstd
    scale = rstd * gain
    bias = shift - mean * scale
    keep = valid_cols(LANES) & chan_mask(scal[LIMIT], LANES)
    x3[0] = jnp.zeros(x3.shape[1:], BF16)
    x3[rows + 1] = jnp.zeros(x3.shape[1:], BF16)
    n = LANES

    def put(i, carry):
        v = z_in[i] * scale + bias
        act = jnp.where(keep, v * sigmoid(v), 0.0)
        x3[i + 1, :, 0:n] = pltpu.roll(act, 1, 0).astype(BF16)
        x3[i + 1, :, n : 2 * n] = act.astype(BF16)
        x3[i + 1, :, 2 * n : 3 * n] = pltpu.roll(act, COLS - 1, 0).astype(BF16)
        return carry

    lax.fori_loop(0, rows, put, 0, unroll=2)
    conv_stats(z, tuple((x3, y, 0, w[y]) for y in range(3)), send.at[:, :, 0 : 2 * n])
    devices = send.shape[0]
    share = xz.shape[0] // devices
    pieces = xz[...].reshape(devices, share, n)
    for q in range(share):
        send[:, :, n * (2 + q) : n * (3 + q)] = pieces[:, q : q + 1, :]


def f6(scal, got, labels, z_in, norm, w, act, z, send, keeps):
    activate(scal, got, labels, z_in, norm, act, keeps)
    expand(act, w, z, send)


def b7(scal, got, labels, joined, z, norm, cot, result, grad_pre, send, keeps, wide):
    rows, chans = z.shape[0], z.shape[2]
    cols = COLS - 4
    pixels = 1.0 * rows * cols
    mean, rstd, gain, shift, _ = scale_shift(got, labels[...], scal, norm, pixels)
    keeps[0:1, :] = mean
    keeps[1:2, :] = rstd
    gate = 0.25 * scal[GATE].astype(F32)
    scale = rstd * gain * gate
    bias = (shift - mean * rstd * gain) * gate

    wide[...] = jnp.zeros(wide.shape, F32)

    def put(i, carry):
        sums, products = carry
        wide[0:cols, :] = cot[i].astype(F32)
        zz = z[i]
        v = joined[i].astype(F32) + zz * scale + bias
        s = sigmoid(v)
        result[i] = (v * s)[0:cols].astype(BF16)
        g = wide[...] * (s * (1.0 + v * (1.0 - s)))
        grad_pre[i] = g
        return sums + fold(g), products + fold(g * (zz - mean))

    start = zeros8(chans)
    sums, products = lax.fori_loop(0, rows, put, (start, start), unroll=2)
    sums, products = down(sums), down(products)
    spread(send, [sums * gate, products * rstd * gate])


def backward_norm(scal, got, labels, norm, keeps, pixels, grad_norm, slots=(0, 1)):
    marks = labels[...]
    chans = norm.shape[2]
    own_shift = jnp.zeros((1, chans), F32)
    own_gain = jnp.zeros((1, chans), F32)
    group = scal[OWN]
    for g in range(norm.shape[0]):
        total = group_sum(got, marks, float(g))
        shift_sum, gain_sum = row(total, slots[0]), row(total, slots[1])
        grad_norm[g, 0:1, :] = gain_sum
        grad_norm[g, 1:2, :] = shift_sum
        mine = group == g
        own_shift = jnp.where(mine, shift_sum, own_shift)
        own_gain = jnp.where(mine, gain_sum, own_gain)
    count = tiled(group_count(marks, group.astype(F32)), chans) * pixels
    mean, rstd = keeps[0:1, :], keeps[1:2, :]
    a = rstd * gain_of(norm, group)
    return mean, a, -(a * rstd) * own_gain / count, -a * own_shift / count


def slope_sums(scal, d, z_in, norm, keeps, dout, send):
    rows = z_in.shape[0]
    mean, rstd = keeps[0:1, :], keeps[1:2, :]
    group = scal[OWN]
    scale = rstd * gain_of(norm, group)
    bias = shift_of(norm, group) - mean * scale
    keep = valid_cols(LANES) & chan_mask(scal[LIMIT], LANES)

    def put(i, carry):
        sums, products = carry
        zz = z_in[i]
        v = zz * scale + bias
        s = sigmoid(v)
        g = jnp.where(keep, d[i] * (s * (1.0 + v * (1.0 - s))), 0.0)
        dout[i] = g
        return sums + fold(g), products + fold(g * (zz - mean))

    sums, products = lax.fori_loop(
        0, rows, put, (zeros8(LANES), zeros8(LANES)), unroll=4
    )
    spread(send, [down(sums), down(products) * rstd])


def b8(
    scal, got, labels, grad_pre, z, norm, keeps, w, z_in, norm_in, keeps_in,
    dz, dout, send, grad_norm, d,
):
    rows, chans = z.shape[0], z.shape[2]
    pixels = 1.0 * rows * (COLS - 4)
    mean, a, b, c = backward_norm(scal, got, labels, norm, keeps, pixels, grad_norm)
    a = a * (0.25 * scal[GATE].astype(F32))
    keep = valid_cols(chans)

    def put(i, carry):
        v = a * grad_pre[i] + b * (z[i] - mean) + c
        dz[i] = jnp.where(keep, v, 0.0).astype(BF16)
        return carry

    lax.fori_loop(0, rows, put, 0, unroll=2)
    d[...] = mm_nt(flat(dz[...]), w[...]).reshape(d.shape)
    slope_sums(scal, d, z_in, norm_in, keeps_in, dout, send)


def b9(
    scal, got, labels, dout_in, z, norm, keeps, b_same, z_in, norm_in, keeps_in,
    dz, dout, send, grad_norm, d3, d,
):
    rows = z.shape[0]
    pixels = 1.0 * rows * (COLS - 4)
    mean, a, b, c = backward_norm(scal, got, labels, norm, keeps, pixels, grad_norm)
    keep = valid_cols(LANES)
    n = LANES
    d3[0] = jnp.zeros(d3.shape[1:], BF16)
    d3[rows + 1] = jnp.zeros(d3.shape[1:], BF16)

    def put(i, carry):
        v = a * dout_in[i] + b * (z[i] - mean) + c
        v = jnp.where(keep, v, 0.0)
        d3[i + 1, :, 0:n] = pltpu.roll(v, COLS - 1, 0).astype(BF16)
        low = v.astype(BF16)
        d3[i + 1, :, n : 2 * n] = low
        dz[i] = low
        d3[i + 1, :, 2 * n : 3 * n] = pltpu.roll(v, 1, 0).astype(BF16)
        return carry

    lax.fori_loop(0, rows, put, 0, unroll=2)
    step = rows // 4
    for k in range(4):
        value = None
        for y in range(3):
            first = 2 - y + step * k
            term = mm_nt(flat(d3[first : first + step]), b_same[y])
            value = term if value is None else value + term
        d[step * k : step * (k + 1)] = value.reshape(step, COLS, LANES)
    slope_sums(scal, d, z_in, norm_in, keeps_in, dout, send)


def b10(
    scal, got, labels, dout_in, z, norm, keeps, w, grad_pre, slope, zc, zp, keeps_cp,
    dz, grad_pre_2, send, grad_norm, d,
):
    rows, chans = zc.shape[0], zc.shape[2]
    pixels = 1.0 * rows * (COLS - 4)
    mean, a, b, c = backward_norm(scal, got, labels, norm, keeps, pixels, grad_norm)
    keep = valid_cols(LANES)

    def put(i, carry):
        v = a * dout_in[i] + b * (z[i] - mean) + c
        dz[i] = jnp.where(keep, v, 0.0).astype(BF16)
        return carry

    lax.fori_loop(0, rows, put, 0, unroll=4)
    d[...] = mm_nt(flat(dz[...]), w[...]).reshape(d.shape)
    mean_c, rstd_c, mean_p, rstd_p = (keeps_cp[k : k + 1, :] for k in range(4))

    def sum_up(i, carry):
        sums, prod_c, prod_p = carry
        g = (grad_pre[i] + d[i]).astype(BF16).astype(F32) * slope[i]
        grad_pre_2[i] = g
        return (
            sums + fold(g),
            prod_c + fold(g * (zc[i] - mean_c)),
            prod_p + fold(g * (zp[i] - mean_p)),
        )

    start = zeros8(chans)
    sums, prod_c, prod_p = lax.fori_loop(0, rows, sum_up, (start, start, start), unroll=2)
    spread(send, [down(sums), down(prod_c) * rstd_c, down(prod_p) * rstd_p])


def b11(
    scal, got, labels, grad_pre_2, zc, zp, norm_c, norm_p, keeps_cp, w, z_in, norm_in, keeps_in,
    dz_c, dz_p, dout, send, grad_norm_c, grad_norm_p, d,
):
    rows, chans = zc.shape[0], zc.shape[2]
    pixels = 1.0 * rows * (COLS - 4)
    mean_c, a_c, b_c, c_c = backward_norm(
        scal, got, labels, norm_c, keeps_cp.at[0:2], pixels, grad_norm_c, (0, 1)
    )
    mean_p, a_p, b_p, c_p = backward_norm(
        scal, got, labels, norm_p, keeps_cp.at[2:4], pixels, grad_norm_p, (0, 2)
    )
    keep = valid_cols(chans)

    def put(i, carry):
        g = grad_pre_2[i]
        v = a_c * g + b_c * (zc[i] - mean_c) + c_c
        dz_c[i] = jnp.where(keep, v, 0.0).astype(BF16)
        v = a_p * g + b_p * (zp[i] - mean_p) + c_p
        dz_p[i] = jnp.where(keep, v, 0.0).astype(BF16)
        return carry

    lax.fori_loop(0, rows, put, 0, unroll=2)
    d[...] = mm_nt(flat(dz_c[...]), w[...]).reshape(d.shape)
    slope_sums(scal, d, z_in, norm_in, keeps_in, dout, send)


def b12(scal, got, labels, dout_in, z, norm, keeps, xs, d2, kept, sent, grad_norm, dz, packed):
    rows = z.shape[0]
    pixels = 1.0 * rows * (COLS - 4)
    mean, a, b, c = backward_norm(scal, got, labels, norm, keeps, pixels, grad_norm)
    keep = valid_cols(LANES)
    n = LANES
    d2[rows] = jnp.zeros(d2.shape[1:], BF16)

    def put(i, carry):
        v = a * dout_in[i] + b * (z[i] - mean) + c
        v = jnp.where(keep, v, 0.0)
        low = v.astype(BF16)
        dz[i] = low
        d2[i, :, 0:n] = low
        d2[i, :, n : 2 * n] = pltpu.roll(v, COLS - 1, 0).astype(BF16)
        return carry

    lax.fori_loop(0, rows, put, 0, unroll=4)
    low = flat(dz[...])
    cur = mm_tn(flat(xs[1 : rows + 1]), low)
    for k, (y, x) in enumerate(((1, 1), (1, 2), (1, 0), (2, 1), (2, 2), (2, 0))):
        put_rows(packed, n * (3 * y + x), cur[n * k : n * (k + 1)])
    up = mm_tn(flat(xs[0:rows, :, 3 * n : 6 * n]), low)
    for k, (y, x) in enumerate(((0, 1), (0, 2), (0, 0))):
        put_rows(packed, n * (3 * y + x), up[n * k : n * (k + 1)])
    share_out(scal, packed, 9 * n, kept, sent)


def b12_images(
    scal, d2, b_even, b_odd, zz, norm_in, keeps_in, dn, sums_out, de, do, wide, *, own
):
    rows = de.shape[0]
    n = LANES
    half = scal[HALF]
    first = rows * (half if own else 1 - half)
    step = rows // 2
    for k in range(2):
        here = flat(d2[pl.ds(first + step * k, step)])
        below = flat(d2[pl.ds(first + step * k + 1, step)])
        de[step * k : step * (k + 1)] = mm_nt(here, b_even[...]).reshape(step, COLS, 2 * n)
        odd = mm_nt(here, b_odd[:, 0 : 2 * n]) + mm_nt(below, b_odd[:, 2 * n : 4 * n])
        do[step * k : step * (k + 1)] = odd.reshape(step, COLS, 2 * n)
    mean_1, rstd_1 = keeps_in[0:1, :], keeps_in[1:2, :]
    group = scal[OWN]
    scale = rstd_1 * gain_of(norm_in, group)
    bias = shift_of(norm_in, group) - mean_1 * scale
    keep = valid_cols(LANES) & chan_mask(scal[LIMIT], LANES)

    def emit(i, carry):
        sums, products = carry
        for ra in (0, 1):
            planes = (de, do)[ra]
            for cb in (0, 1):
                zv = zz[2 * i + ra, pl.ds(cb, COLS, stride=2), :]
                v = zv * scale + bias
                s = sigmoid(v)
                g = planes[i, :, n * cb : n * (cb + 1)]
                g = jnp.where(keep, g * (s * (1.0 + v * (1.0 - s))), 0.0)
                sums = sums + fold(g)
                products = products + fold(g * (zv - mean_1))
                wide[ra, pl.ds(cb, COLS, stride=2), :] = g
            dn[2 * i + ra] = wide[ra].astype(BF16)
        return sums, products

    totals = lax.fori_loop(0, rows, emit, (zeros8(n), zeros8(n)), unroll=2)
    sums_out[0:1, :] = down(totals[0])
    sums_out[1:2, :] = down(totals[1]) * rstd_1


def b13(
    scal, got, labels, norm, keeps, w, z_own, z_for, dn_own, dn_for, gs_own, gs_for,
    grad, grad_norm, dz, wide, *, at,
):
    rows, cols = grad.shape[1], grad.shape[2]
    half = scal[HALF]
    pixels = 2.0 * rows * cols
    marks = labels[...]
    totals = last_sums(got.at[:, at : at + 4, :], marks, norm.shape[0])
    for g in range(norm.shape[0]):
        grad_norm[g, 0:1, :] = totals[g][1]
        grad_norm[g, 1:2, :] = totals[g][0]
    keep = lax.broadcasted_iota(jnp.int32, (z_own.shape[1], LANES), 0) < cols
    for k, (z, dn, gs) in enumerate(((z_own, dn_own, gs_own), (z_for, dn_for, gs_for))):
        group = scal[OWN if k == 0 else OTHER]
        shift_sum, gain_sum = totals[0]
        for g in range(1, norm.shape[0]):
            shift_sum = jnp.where(group == g, totals[g][0], shift_sum)
            gain_sum = jnp.where(group == g, totals[g][1], gain_sum)
        count = group_count(marks, group.astype(F32)) * pixels
        mean, rstd = keeps[2 * k : 2 * k + 1, :], keeps[2 * k + 1 : 2 * k + 2, :]
        a = rstd * gain_of(norm, group)
        b = -(a * rstd) * gain_sum / count
        c = -a * shift_sum / count

        def put(i, carry, z=z, dn=dn, mean=mean, a=a, b=b, c=c):
            v = a * dn[i].astype(F32) + b * (z[i] - mean) + c
            dz[i] = jnp.where(keep, v, 0.0).astype(BF16)
            return carry

        lax.fori_loop(0, rows, put, 0, unroll=2)
        step = rows // 4
        for q in range(4):
            low = flat(dz[step * q : step * (q + 1)])
            for p in range(wide.shape[0]):
                values = mm_nt(low, w[LANES * p : LANES * (p + 1), :])
                wide[p, step * q : step * (q + 1)] = values.reshape(step, -1, LANES)
        place = half if k == 0 else 1 - half

        def emit(i, carry, gs=gs, place=place):
            even = pl.ds(0, COLS, stride=2)
            for p in range(wide.shape[0]):
                lanes = slice(LANES * p, LANES * (p + 1))
                wide[p, 2 * i, even, :] = wide[p, 2 * i, even, :] + gs[i, :, lanes].astype(F32)
                grad[place, 2 * i, :, lanes] = wide[p, 2 * i, 0:cols, :].astype(BF16)
                grad[place, 2 * i + 1, :, lanes] = wide[p, 2 * i + 1, 0:cols, :].astype(BF16)
            return carry

        lax.fori_loop(0, rows // 2, emit, 0, unroll=2)


def put_rows(out, at, value):
    for j in range(value.shape[1] // LANES):
        out[at : at + value.shape[0], :] = value[:, LANES * j : LANES * (j + 1)].astype(BF16)
        at += value.shape[0]
    return at


def take_rows(source, at, out):
    rows = out.shape[0]
    for j in range(out.shape[1] // LANES):
        out[:, LANES * j : LANES * (j + 1)] = source(at, rows)
        at += rows
    return at


def share_out(scal, packed, used, kept, sent):
    if used < packed.shape[0]:
        packed[used:, :] = jnp.zeros((packed.shape[0] - used, LANES), BF16)
    half = scal[HALF]
    size = kept.shape[0] * kept.shape[1]
    for out, place in ((kept, half), (sent, 1 - half)):
        out[...] = packed[pl.ds(pl.multiple_of(size * place, 16), size), :].reshape(out.shape)


def g_most(
    scal, act_2b, dz_2c, x3, dz_2b, joined, dz_2a, act_1b, dz_1c, xee, dz_1p, w_1p,
    kept, sent, gs_own, gs_oth, packed,
):
    rows = dz_2b.shape[0]
    at = put_rows(packed, 0, mm_tn(flat(act_2b[...]), flat(dz_2c[...])))
    low = flat(dz_2b[...])
    for y in range(3):
        at = put_rows(packed, at, mm_tn(flat(x3[y : y + rows]), low))
    at = put_rows(packed, at, mm_tn(flat(joined[...]), flat(dz_2a[...])))
    at = put_rows(packed, at, mm_tn(flat(act_1b[...]), flat(dz_1c[...])))
    at = put_rows(packed, at, mm_tn(flat(xee[...]), flat(dz_1p[...])))
    share_out(scal, packed, at, kept, sent)
    half = scal[HALF]
    count = gs_own.shape[0]
    for k, gs in enumerate((gs_own, gs_oth)):
        first = count * (half if k == 0 else 1 - half)
        got = mm_nt(flat(dz_1p[pl.ds(first, count)]), w_1p[...])
        gs[...] = got.reshape(gs.shape).astype(BF16)


def g_xz(keeps, x_own, x_oth, z_own, z_oth, out, low):
    rows = z_own.shape[0]
    mean = keeps[0:1, :]
    value = None
    for x, z in ((x_own, z_own), (x_oth, z_oth)):

        def put(i, carry, z=z):
            low[i] = (z[i] - mean).astype(BF16)
            return carry

        lax.fori_loop(0, rows, put, 0, unroll=4)
        term = mm_tn(flat(x[...]), flat(low[...]))
        value = term if value is None else value + term
    at = value.shape[0]
    out[0:at, :] = value
    if at < out.shape[0]:
        out[at:, :] = jnp.zeros((out.shape[0] - at, LANES), F32)


def g_xd(scal, sums_own, sums_oth, norm, keeps, x_dev, x_own, x_oth, dn_own, dn_oth, out, sums, low):
    rows = dn_own.shape[0]
    n = LANES
    pixels = 1.0 * (2 * rows) * (2 * (COLS - 4))
    sums[...] = sums_own[...] + sums_oth[...]
    a = keeps[1:2, :] * gain_of(norm, scal[OWN])
    local = sums[0:1, :] / pixels
    value = None
    for x, dn in ((x_own, dn_own), (x_oth, dn_oth)):

        def put(i, carry, dn=dn):
            low[i] = (a * (dn[i].astype(F32) - local)).astype(BF16)
            return carry

        lax.fori_loop(0, rows, put, 0, unroll=4)
        term = mm_tn(flat(x[...]), flat(low[...]))
        value = term if value is None else value + term
    spread_dev = jnp.broadcast_to(x_dev[...], (8, x_dev.shape[1]))
    column = jnp.transpose(spread_dev)[:, 0:1]
    value = value + column * (a * local)
    at = value.shape[0]
    out[0:at, :] = value.astype(BF16)
    if at < out.shape[0]:
        out[at:, :] = jnp.zeros((out.shape[0] - at, n), BF16)


def pack_last(tall, sums, kept, got, kept_1b, got_1b, send, *, stats_at):
    n = LANES
    devices = send.shape[0]
    piece, share = kept.shape[1], tall.shape[0] // devices
    first = kept.shape[0]
    second = first + kept_1b.shape[0]
    send[0:first, 0:piece, :] = (kept[...].astype(F32) + got[...].astype(F32)).astype(BF16)
    send[first:second, 0:piece, :] = (kept_1b[...].astype(F32) + got_1b[...].astype(F32)).astype(BF16)
    if second < devices:
        send[second:, 0:piece, :] = jnp.zeros((devices - second, piece, n), BF16)
    send[:, piece : piece + share, :] = tall[...].reshape(devices, share, n)
    high = sums[...].astype(BF16)
    rest = (sums[...] - high.astype(F32)).astype(BF16)
    for k, v in enumerate((high, rest)):
        send[:, stats_at + 2 * k : stats_at + 2 * k + 2, :] = jnp.broadcast_to(v[None], (devices, 2, n))


def last_sums(stats, marks, groups):
    values = stats[:, 0:2, :].astype(F32) + stats[:, 2:4, :].astype(F32)
    out = []
    for g in range(groups):
        total = jnp.sum(values * (marks == float(g)).astype(F32), axis=0)
        out.append((total[0:1], total[1:2]))
    return out


def add_all(got, labels, norm, keeps_all, xz_got, out, *, at, pixels):
    devices, n = got.shape[0], LANES
    half = devices // 2
    share = xz_got.shape[2] // n - 2
    piece = out.shape[1] - share
    marks = labels[...]
    value = jnp.sum(got[:, piece : piece + share, :].astype(F32), axis=0)
    sums = last_sums(got.at[:, at : at + 4, :], marks, norm.shape[0])
    for g in range(norm.shape[0]):
        rstd = keeps_all[2 * g + 1 : 2 * g + 2, :]
        count = group_count(marks, float(g)) * pixels
        b = -(rstd * rstd * gain_of(norm, g)) * sums[g][1] / count
        same = (marks == float(g)).astype(F32)
        rows = [
            jnp.sum(xz_got[:, :, n * (2 + q) : n * (3 + q)] * same, axis=0) for q in range(share)
        ]
        value = value + jnp.concatenate(rows, axis=0) * b
    for k in (0, 1):
        total = jnp.sum(got[half * k : half * (k + 1), 0:piece, :].astype(F32), axis=0).astype(BF16)
        out[half * k : half * (k + 1), 0:piece, :] = jnp.broadcast_to(total[None], (half, piece, n))
    out[:, piece:, :] = jnp.broadcast_to(value.astype(BF16)[None], (devices, share, n))


def unpack(scal, own, other, w_1a, w_1b, w_2c, w_2b, w_2a, w_1c, w_1p, tall, packed, packed_1b):
    half = scal[HALF]
    devices = own.shape[0]
    piece = packed.shape[1]
    first, second = packed.shape[0] // 2, packed_1b.shape[0] // 2
    for part, place in ((own, half), (other, 1 - half)):
        packed[pl.ds(first * place, first)] = part[0:first, 0:piece, :]
        packed_1b[pl.ds(second * place, second)] = part[first : first + second, 0:piece, :]
    share = own.shape[1] - piece
    tall[...] = own[:, piece:, :].astype(F32).reshape(tall.shape)
    w_1a[...] = tall[0 : w_1a.shape[0], :]
    flat_1b, rest = flat(packed_1b[...]), flat(packed[...])
    w_1b[...] = flat_1b[0 : w_1b.shape[0]].astype(F32)

    def source(at, rows):
        return rest[at : at + rows].astype(F32)

    at = 0
    for out in (w_2c, w_2b, w_2a, w_1c, w_1p):
        at = take_rows(source, at, out)


def gather(send):
    return lax.all_to_all(send, AXES, 0, 0)


def tie(*values):
    return lax.optimization_barrier(values)


def swap(block):
    return lax.ppermute(block, "rows", [(0, 1), (1, 0)])


def body(
    images, w_1a, w_1b, w_1c, w_1p, w_2a, w_2b, w_2c,
    norm_1a, norm_1b, norm_1c, norm_1p, norm_2a, norm_2b, norm_2c,
    cotangent, group, width, gate,
):
    devices = lax.axis_size("rows") * lax.axis_size("batch")
    half = lax.axis_index("rows").astype(jnp.int32).reshape(1)
    norms = (norm_1a, norm_1b, norm_1c, norm_1p, norm_2a, norm_2b, norm_2c)
    norm_1a, norm_1b, norm_1c, norm_1p, norm_2a, norm_2b, norm_2c = (
        v.transpose(1, 0, 2) for v in norms
    )
    outer, inputs = w_1c.shape[1], w_1a.shape[0]
    rows = cotangent.shape[1]
    cols_in = 2 * COLS
    n, m = LANES, devices

    def send(stats, channels=LANES):
        return ((m, channels // LANES, stats * LANES), F32)

    def maps(channels, dtype=F32):
        return ((rows, COLS, channels), dtype)

    def scratch(channels, dtype=F32):
        return pltpu.VMEM((rows, COLS, channels), dtype)

    def params(*arrays):
        return [(a.shape, F32) for a in arrays]

    def mean_scale(channels, count=1):
        return ((2 * count, channels), F32)

    wide_in = ((rows, cols_in, inputs), BF16)
    wide_z = ((rows, cols_in, n), F32)
    raw = images.shape
    scal, x_own, x_for, z_own, z_for, s1 = stage(
        f1, [((8,), jnp.int32), wide_in, wide_in, wide_z, wide_z, send(5)],
        [*(pltpu.SMEM(v.shape, jnp.int32) for v in (group, width, gate)),
         pltpu.VMEM(raw, BF16), pltpu.VMEM(w_1a.shape, BF16), pltpu.SemaphoreType.DMA((6,))],
        smem=(0,), smem_out=(0,), hbm=(1, 2, 3, 4, 5),
    )(half, group, width, gate, images, w_1a)
    s1, v_1b, v_2b = tie(s1, w_1b, w_2b)
    w_cur, w_up, b_even, b_odd, b_same = stage(
        prepare,
        [((6 * n, n), BF16), ((3 * n, n), BF16), ((2 * n, 2 * n), BF16), ((2 * n, 4 * n), BF16),
         ((3, n, 3 * n), BF16)],
        smem=(),
    )(v_1b, v_2b)
    s1, x_for, w_cur, w_up, b_even, b_odd, b_same = tie(
        s1, x_for, w_cur, w_up, b_even, b_odd, b_same
    )
    x_oth = swap(x_for)
    g1 = gather(s1)
    g1, x_oth = tie(g1, x_oth)
    xee, z_1p, stats_1p = stage(
        f1_strided,
        [maps(inputs, BF16), maps(outer), ((2, 1, outer), F32)],
        [pltpu.VMEM((inputs // n, cols_in, n), F32)],
    )(scal, x_own, x_oth, w_1p)
    xs, z_1b, s2, labels, k_1a, k_all, z_oth, x_sum = stage(
        f2,
        [((rows + 1, COLS, 6 * n), BF16), maps(n), send(2 + (inputs + 2 * outer) // n),
         ((m, 1, n), F32), mean_scale(n, 2), mean_scale(n, norm_1a.shape[0]), wide_z,
         ((8, inputs), F32)],
    )(scal, g1, z_own, x_own, x_oth, w_1a, norm_1a, w_cur, w_up, stats_1p)
    g2 = gather(s2)
    act_1b, z_1c, s3, k_1b, k_p, x_dev = stage(
        f3, [maps(n, BF16), maps(outer), send(2, outer), mean_scale(n), mean_scale(outer),
             ((1, inputs), F32)],
    )(scal, g2, labels, z_1b, norm_1b, w_1c, x_sum)
    g3 = gather(s3)
    joined, slope, z_2a, s4, k_cp = stage(
        f4, [maps(outer, BF16), maps(outer), maps(n), send(2), mean_scale(outer, 2)]
    )(scal, g3, labels, z_1c, z_1p, norm_1c, norm_1p, k_p, w_2a)
    share = -(-inputs // devices)
    half_in = ((rows, cols_in, n), BF16)
    s4, k_1a = tie(s4, k_1a)
    (xz,) = stage(g_xz, [((devices * share, n), F32)], [pltpu.VMEM(half_in[0], BF16)], smem=())(
        k_1a, x_own, x_oth, z_own, z_oth
    )
    s4, xz = tie(s4, xz)
    g4 = gather(s4)
    x3, z_2b, s5, k_2a = stage(
        f5, [((rows + 2, COLS, 3 * n), BF16), maps(n), send(2 + share), mean_scale(n)]
    )(scal, g4, labels, z_2a, norm_2a, w_2b.reshape(3, 3 * n, n), xz)
    g5 = gather(s5)
    act_2b, z_2c, s6, k_2b = stage(
        f6, [maps(n, BF16), maps(outer), send(2, outer), mean_scale(n)]
    )(scal, g5, labels, z_2b, norm_2b, w_2c)
    g6 = gather(s6)
    result, grad_pre, s7, k_2c = stage(
        b7, [(cotangent.shape[1:], BF16), maps(outer), send(2, outer), mean_scale(outer)],
        [pltpu.VMEM((COLS, outer), F32)],
    )(scal, g6, labels, joined, z_2c, norm_2c, cotangent[0])
    g7 = gather(s7)
    dz_2c, dout_2b, s8, grad_norm_2c = stage(
        b8, [maps(outer, BF16), maps(n), send(2), *params(norm_2c)], [scratch(n)]
    )(scal, g7, labels, grad_pre, z_2c, norm_2c, k_2c, w_2c, z_2b, norm_2b, k_2b)
    g8 = gather(s8)
    dz_2b, dout_2a, s9, grad_norm_2b = stage(
        b9, [maps(n, BF16), maps(n), send(2), *params(norm_2b)],
        [pltpu.VMEM((rows + 2, COLS, 3 * n), BF16), scratch(n)],
    )(scal, g8, labels, dout_2b, z_2b, norm_2b, k_2b, b_same, z_2a, norm_2a, k_2a)
    g9 = gather(s9)
    dz_2a, grad_pre_2, s10, grad_norm_2a = stage(
        b10, [maps(n, BF16), maps(outer), send(3, outer), *params(norm_2a)], [scratch(outer)]
    )(scal, g9, labels, dout_2a, z_2a, norm_2a, k_2a, w_2a, grad_pre, slope, z_1c, z_1p, k_cp)
    g10 = gather(s10)
    dz_1c, dz_1p, dout_1b, s11, grad_norm_1c, grad_norm_1p = stage(
        b11, [maps(outer, BF16), maps(outer, BF16), maps(n), send(2), *params(norm_1c, norm_1p)],
        [scratch(n)],
    )(scal, g10, labels, grad_pre_2, z_1c, z_1p, norm_1c, norm_1p, k_cp, w_1c, z_1b, norm_1b, k_1b)
    half_map = ((rows // 2, COLS, inputs), BF16)
    most_rows = sum(v.size for v in (w_2c, w_2b, w_2a, w_1c, w_1p)) // n
    rows_1b = w_1b.size // n
    piece = 16
    while -(-most_rows // (2 * piece)) - (-rows_1b // (2 * piece)) > devices:
        piece += 16
    first, second = -(-most_rows // (2 * piece)), -(-rows_1b // (2 * piece))
    part, part_1b = ((first, piece, n), BF16), ((second, piece, n), BF16)
    kept, sent, gs_own, gs_send = stage(
        g_most, [part, part, half_map, half_map], [pltpu.VMEM((2 * first * piece, n), BF16)]
    )(scal, act_2b, dz_2c, x3, dz_2b, joined, dz_2a, act_1b, dz_1c, xee, dz_1p, w_1p)
    s11, sent, gs_send = tie(s11, sent, gs_send)
    g11, sent, gs_send = tie(gather(s11), sent, gs_send)
    got, gs_for = swap(sent), swap(gs_send)
    d2, kept_1b, sent_1b, grad_norm_1b = stage(
        b12, [((rows + 1, COLS, 2 * n), BF16), part_1b, part_1b, *params(norm_1b)],
        [scratch(n, BF16), pltpu.VMEM((2 * second * piece, n), BF16)],
    )(scal, g11, labels, dout_1b, z_1b, norm_1b, k_1b, xs)
    got_1b = swap(sent_1b)
    sides = []
    for own, z in ((False, z_oth), (True, z_own)):
        sides.append(
            stage(
                functools.partial(b12_images, own=own), [half_in, ((2, n), F32)],
                [pltpu.VMEM((rows // 2, COLS, 2 * n), F32), pltpu.VMEM((rows // 2, COLS, 2 * n), F32),
                 pltpu.VMEM((2, cols_in, n), F32)],
            )(scal, d2, b_even, b_odd, z, norm_1a, k_1a)
        )
        if not own:
            dn_for = swap(sides[0][0])
            d2, _ = tie(d2, sides[0][0])
    (dn_send, sums_send), (dn_own, sums_own) = sides
    stats_at = piece + -(-share // 8) * 8
    high = -(-(stats_at + 4) // 16) * 16
    tall, sums_1a = stage(
        g_xd, [((devices * share, n), BF16), ((2, n), F32)], [pltpu.VMEM(half_in[0], BF16)]
    )(scal, sums_own, sums_send, norm_1a, k_1a, x_dev, x_own, x_oth, dn_own, dn_send)
    tall, gs_for, dn_for = tie(tall, gs_for, dn_for)
    (s12,) = stage(
        functools.partial(pack_last, stats_at=stats_at), [((devices, high, n), BF16)], smem=()
    )(tall, sums_1a, kept, got, kept_1b, got_1b)
    g12 = gather(s12)
    pixels = 4.0 * images.shape[1] * images.shape[1]
    (mine,) = stage(
        functools.partial(add_all, at=stats_at, pixels=pixels),
        [((devices, piece + share, n), BF16)], smem=(),
    )(g12, labels, norm_1a, k_all, g5)
    grad_images, grad_norm_1a = stage(
        functools.partial(b13, at=stats_at), [(images.shape, BF16), *params(norm_1a)],
        [pltpu.VMEM(half_in[0], BF16), pltpu.VMEM((inputs // n, rows, cols_in, n), F32)],
    )(scal, g12, labels, norm_1a, k_1a, w_1a, z_own, z_for, dn_own, dn_for, gs_own, gs_for)
    whole = gather(mine)
    totals = stage(
        unpack,
        [(v.shape, F32) for v in (w_1a, w_1b.reshape(-1, n), w_2c, w_2b.reshape(-1, n), w_2a, w_1c, w_1p)],
        [pltpu.VMEM((devices * share, n), F32), pltpu.VMEM((2 * first, piece, n), BF16),
         pltpu.VMEM((2 * second, piece, n), BF16)],
    )(scal, whole, swap(whole))
    t_1a, t_1b, t_2c, t_2b, t_2a, t_1c, t_1p = totals
    grads = (
        grad_norm_1a, grad_norm_1b, grad_norm_1c, grad_norm_1p,
        grad_norm_2a, grad_norm_2b, grad_norm_2c,
    )
    return (
        result[None], grad_images, t_1a, t_1b.reshape(w_1b.shape), t_1c, t_1p, t_2a,
        t_2b.reshape(w_2b.shape), t_2c, *[v.transpose(1, 0, 2) for v in grads],
    )


def solution(mesh):
    return jax.shard_map(
        body,
        mesh=mesh,
        in_specs=(
            P("batch", "rows", None, None),
            *[P()] * 14,
            P(("batch", "rows"), None, None, None),
            P("batch"),
            P(),
            P(),
        ),
        out_specs=(
            P(("batch", "rows"), None, None, None),
            P("batch", "rows", None, None),
            *[P()] * 14,
        ),
        check_vma=False,
    )
```

```python
import functools

import jax
import jax.numpy as jnp
from jax import lax
from jax.experimental import pallas as pl
from jax.experimental.pallas import tpu as pltpu
from jax.sharding import PartitionSpec as P

EPSILON = 1e-05
F32 = jnp.float32
BF16 = jnp.bfloat16
AXES = ("rows", "batch")
VMEM_LIMIT = 14 * 1024 * 1024
LANES = 128
COLS = 32


def full(memory=pltpu.VMEM):
    return pl.BlockSpec(memory_space=memory)


def stage(kernel, outs, scratch=(), hbm=(), hbm_out=()):
    def place(i, outside):
        return pltpu.HBM if i in outside else pltpu.VMEM

    def call(*args):
        args = [
            pltpu.with_memory_space_constraint(a, pltpu.HBM) if i in hbm else a
            for i, a in enumerate(args)
        ]
        return pl.pallas_call(
            kernel,
            out_shape=tuple(jax.ShapeDtypeStruct(s, d) for s, d in outs),
            in_specs=[full(place(i, hbm)) for i in range(len(args))],
            out_specs=tuple(
                full(place(i, hbm_out)) for i in range(len(outs))
            ),
            scratch_shapes=list(scratch),
            compiler_params=pltpu.CompilerParams(vmem_limit_bytes=VMEM_LIMIT),
            name=(kernel.func if isinstance(kernel, functools.partial) else kernel).__name__,
        )(*args)

    return call


def silu_of_half(u):
    return u + u * jnp.tanh(u)


def slope_of_half(u):
    t = jnp.tanh(u)
    return (0.5 + 0.5 * t) * (1.0 + u - u * t)


def fold(x):
    return (x[0:8] + x[8:16]) + (x[16:24] + x[24:32])


def row(total, stat):
    blocks = total.shape[0]
    pieces = [total[j : j + 1, LANES * stat : LANES * (stat + 1)] for j in range(blocks)]
    return pieces[0] if blocks == 1 else jnp.concatenate(pieces, axis=1)


def spread(out_ref, rows):
    blocks = out_ref.shape[1]
    for stat, values in enumerate(rows):
        for j in range(blocks):
            piece = values[:, LANES * j : LANES * (j + 1)]
            out_ref[:, j : j + 1, LANES * stat : LANES * (stat + 1)] = jnp.broadcast_to(
                piece[None], (out_ref.shape[0], 1, LANES)
            )


def group_sum(got_ref, labels, label):
    same = (labels == label).astype(F32)
    stats = got_ref.shape[2] // LANES
    parts = [
        jnp.sum(got_ref[:, :, LANES * s : LANES * (s + 1)] * same, axis=0) for s in range(stats)
    ]
    return jnp.concatenate(parts, axis=1) if stats > 1 else parts[0]


def group_count(labels, label):
    return jnp.sum((labels == label).astype(F32), axis=0)


def tiled(values, channels):
    return jnp.concatenate([values] * (channels // LANES), axis=1) if channels > LANES else values


def moments(first, second, pixels):
    mean = first / pixels
    return mean, lax.rsqrt(second / pixels - mean * mean + EPSILON)


def own_of(values, label):
    out = values[0]
    label = tiled(label, out.shape[1])
    for g in range(1, len(values)):
        out = jnp.where(label == float(g), values[g], out)
    return out


def gain_of(norm_ref, label):
    return own_of([norm_ref[g, 0:1, :] for g in range(norm_ref.shape[0])], label)


def shift_of(norm_ref, label):
    return own_of([norm_ref[g, 1:2, :] for g in range(norm_ref.shape[0])], label)


def valid_cols(channels):
    return lax.broadcasted_iota(jnp.int32, (COLS, channels), 0) < COLS - 4


def chan_mask(tab):
    return lax.broadcasted_iota(jnp.int32, (1, LANES), 1).astype(F32) < entry(tab, LIMIT)


def flat(x):
    return x.reshape(x.shape[0] * x.shape[1], x.shape[2])


def mm(a, b):
    return jnp.dot(a, b, preferred_element_type=F32)


def mm_nt(a, b):
    return lax.dot_general(a, b, (((1,), (1,)), ((), ())), preferred_element_type=F32)


def mm_tn(a, b):
    return lax.dot_general(a, b, (((0,), (0,)), ((), ())), preferred_element_type=F32)


def mm_side(a, b):
    turned = mm_tn(b, a)
    blocks = [
        jnp.transpose(turned[:, LANES * j : LANES * (j + 1)]) for j in range(a.shape[1] // LANES)
    ]
    return blocks[0] if len(blocks) == 1 else jnp.concatenate(blocks, axis=0)


def zeros8(channels):
    return jnp.zeros((8, channels), F32)


def down(x):
    return jnp.sum(x, axis=0, keepdims=True)


OWN, OTHER, HALF, LIMIT, GATE = range(5)


def entry(tab, k):
    return tab[k : k + 1, :]


def half_of(tab):
    return (jnp.sum(entry(tab, HALF)) * (1.0 / LANES)).astype(jnp.int32)


def prepare(w1b, w2b, w_even, w_odd, w_two, w_last, b_even, b_odd, b_two, b_last):
    n = LANES
    for k, (y, x) in enumerate(((1, 1), (1, 2), (1, 0))):
        w_even[n * k : n * (k + 1), :] = w1b[y, x]
    for k, (low, high) in enumerate((((2, 1), (0, 1)), ((2, 2), (0, 2)), ((2, 0), (0, 0)))):
        w_odd[n * k : n * (k + 1), 0:n] = w1b[low]
        w_odd[n * k : n * (k + 1), n : 2 * n] = w1b[high]
    for x in range(3):
        w_two[n * x : n * (x + 1), 0:n] = w2b[0, x]
        w_two[n * x : n * (x + 1), n : 2 * n] = w2b[1, x]
        w_last[n * x : n * (x + 1), :] = w2b[2, x]
        b_two[0:n, n * x : n * (x + 1)] = w2b[1, x]
        b_two[n : 2 * n, n * x : n * (x + 1)] = w2b[2, x]
        b_last[:, n * x : n * (x + 1)] = w2b[0, x]
    nothing = jnp.zeros((n, n), BF16)
    b_even[0:n, 0:n] = w1b[1, 1]
    b_even[0:n, n : 2 * n] = nothing
    b_even[n : 2 * n, 0:n] = w1b[1, 2]
    b_even[n : 2 * n, n : 2 * n] = w1b[1, 0]
    for k, top in ((0, 2), (1, 0)):
        b_odd[0:n, 2 * n * k : 2 * n * k + n] = w1b[top, 1]
        b_odd[0:n, 2 * n * k + n : 2 * n * (k + 1)] = nothing
        b_odd[n : 2 * n, 2 * n * k : 2 * n * k + n] = w1b[top, 2]
        b_odd[n : 2 * n, 2 * n * k + n : 2 * n * (k + 1)] = w1b[top, 0]


def widen(source, x_pad):
    rows, cols, chans = source.shape
    gap = x_pad.shape[1] - cols

    def put(i, carry):
        x_pad[i, 0:cols, :] = source[i]
        x_pad[i, cols : cols + gap, :] = jnp.zeros((gap, chans), BF16)
        return carry

    lax.fori_loop(0, rows, put, 0, unroll=4)


def first_project(x_pad, w, z, stats=True):
    rows = x_pad.shape[0]
    step = rows // 4
    sums, squares = zeros8(LANES), zeros8(LANES)
    for c in range(4):
        values = mm(flat(x_pad[step * c : step * (c + 1)]), w[...])
        z[step * c : step * (c + 1)] = values.reshape(step, x_pad.shape[1], LANES)
        if stats:
            parts = values.reshape(-1, 8, LANES)
            sums = sums + jnp.sum(parts, axis=0)
            squares = squares + jnp.sum(parts * parts, axis=0)
    return sums, squares


def f1(
    half_at, group_at, width_at, gate_at, images, w_at, tab, x_own, x_for, z_own, z_for, send,
    half_ref, group, width, gate, raw, w, sems,
):
    pairs = (
        (half_at, half_ref), (group_at, group), (width_at, width), (gate_at, gate), (w_at, w),
        (images.at[0], raw.at[0]), (images.at[1], raw.at[1]),
    )
    copies = [pltpu.make_async_copy(a, b, sems.at[k]) for k, (a, b) in enumerate(pairs)]
    for k in (0, 4, 5, 6, 1, 2, 3):
        copies[k].start()
    for copy in copies:
        copy.wait()
    half = half_ref[0]
    rows = []
    for place, x_pad, z in ((half, x_own, z_own), (1 - half, x_for, z_for)):
        widen(raw.at[place], x_pad)
        sums, squares = first_project(x_pad, w, z)
        rows += [down(sums), down(squares)]
    own, other = group[half], group[1 - half]
    values = {
        OWN: own, OTHER: other, HALF: half, LIMIT: w.shape[1] // 4 * width[own], GATE: gate[own]
    }
    tab[...] = jnp.zeros(tab.shape, F32)
    for k, v in values.items():
        tab[k : k + 1, :] = jnp.full((1, LANES), v.astype(F32))
    spread(send, [*rows, jnp.full((1, LANES), (own + 4 * other).astype(F32))])


def f1_strided(tab, x_own, x_oth, w, xee, z, stats, wide):
    half = half_of(tab)
    rows = x_own.shape[0] // 2
    for k, x_pad in enumerate((x_own, x_oth)):
        first = rows * (half if k == 0 else 1 - half)

        def put(i, carry, x_pad=x_pad, first=first):
            for b in range(wide.shape[0]):
                lanes = slice(LANES * b, LANES * (b + 1))
                wide[b] = x_pad[2 * i, :, lanes].astype(F32)
                xee[first + i, :, lanes] = wide[b, pl.ds(0, COLS, stride=2), :].astype(BF16)
            return carry

        lax.fori_loop(0, rows, put, 0, unroll=2)
    total = 2 * rows
    step = total // 7
    chans = z.shape[2]
    squares = zeros8(chans)
    for c in range(7):
        values = mm(flat(xee[step * c : step * (c + 1)]), w[...])
        z[step * c : step * (c + 1)] = values.reshape(step, COLS, chans)
        parts = values.reshape(-1, 8, chans)
        squares = squares + jnp.sum(parts * parts, axis=0)
    ones = jnp.ones((8, total * COLS), BF16)
    stats[:, 0 : w.shape[0]] = mm(ones, flat(xee[...]))[0:1]
    stats[:, w.shape[0] :] = down(squares)


def scale_shift(got, labels, tab, norm, pixels, slot=0):
    label = entry(tab, OWN)
    total = group_sum(got, labels, label)
    chans = norm.shape[2]
    count = tiled(group_count(labels, label), chans) * pixels
    mean, rstd = moments(row(total, 2 * slot), row(total, 2 * slot + 1), count)
    gain, shift = gain_of(norm, entry(tab, OWN)), shift_of(norm, entry(tab, OWN))
    return mean, rstd, gain, shift, count


def conv_stats(z, source, pair, single, send, extra=()):
    keep = valid_cols(LANES)[None]
    rows = z.shape[0]
    step = rows // 4
    (lanes_2, w_2, offsets), (lanes_1, w_1, offset) = pair, single
    sums, squares = zeros8(LANES), zeros8(LANES)
    base = min(offsets)
    for c in range(4):
        at = step * c
        both = mm(flat(source[at + base : at + base + step + 1, :, lanes_2]), w_2)
        values = mm(flat(source[at + offset : at + offset + step, :, lanes_1]), w_1)
        for k, own in enumerate(offsets):
            skip = COLS * (own - base)
            values = values + both[skip : skip + step * COLS, LANES * k : LANES * (k + 1)]
        values = jnp.where(keep, values.reshape(step, COLS, LANES), 0.0)
        z[at : at + step] = values
        parts = values.reshape(-1, 8, LANES)
        sums = sums + jnp.sum(parts, axis=0)
        squares = squares + jnp.sum(parts * parts, axis=0)
    spread(send, [down(sums), down(squares), *extra])


def f2(
    tab, got, z_own, x_own, x_oth, w, norm, w_even, w_odd, stats_p,
    xs, z, send, labels, keeps, keeps_all, z_oth, x_sum,
):
    codes = got[:, :, 4 * LANES : 5 * LANES]
    others = jnp.floor(0.25 * codes)
    marks = codes - 4.0 * others
    labels[...] = marks
    rows = xs.shape[0] - 1
    pixels = 4.0 * rows * (COLS - 4)
    first_project(x_oth, w, z_oth, False)
    for g in range(norm.shape[0]):
        mine, theirs = (marks == float(g)).astype(F32), (others == float(g)).astype(F32)
        totals = [
            jnp.sum(
                got[:, :, LANES * s : LANES * (s + 1)] * mine
                + got[:, :, LANES * (s + 2) : LANES * (s + 3)] * theirs,
                axis=0,
            )
            for s in (0, 1)
        ]
        mean, rstd = moments(*totals, group_count(marks, float(g)) * pixels)
        keeps_all[2 * g : 2 * g + 1, :] = mean
        keeps_all[2 * g + 1 : 2 * g + 2, :] = rstd
    for k, slot in enumerate((OWN, OTHER)):
        for q in (0, 1):
            choices = [keeps_all[2 * g + q : 2 * g + q + 1, :] for g in range(norm.shape[0])]
            keeps[2 * k + q : 2 * k + q + 1, :] = own_of(choices, entry(tab, slot))
    mean, rstd = keeps[0:1, :], keeps[1:2, :]
    gain, shift = gain_of(norm, entry(tab, OWN)), shift_of(norm, entry(tab, OWN))
    ones = jnp.ones((8, x_own.shape[0] * x_own.shape[1]), BF16)
    x_sum[...] = mm(ones, flat(x_own[...])) + mm(ones, flat(x_oth[...]))
    scale = rstd * gain
    bias = 0.5 * (shift - mean * scale)
    scale = 0.5 * scale
    keep = valid_cols(LANES) & chan_mask(tab)
    half = half_of(tab)
    xs[0] = jnp.zeros(xs.shape[1:], BF16)
    n = LANES
    for k, zz in enumerate((z_own, z_oth)):
        first = 1 + (rows // 2) * (half if k == 0 else 1 - half)

        def put(i, carry, zz=zz, first=first):
            lane = 0
            for a in (0, 1):
                for b in (0, 1):
                    u = zz[2 * i + a, pl.ds(b, COLS, stride=2), :] * scale + bias
                    act = jnp.where(keep, silu_of_half(u), 0.0)
                    xs[first + i, :, lane : lane + n] = act.astype(BF16)
                    lane += n
                    if b == 1:
                        moved = pltpu.roll(act, 1, 0)
                        xs[first + i, :, lane : lane + n] = moved.astype(BF16)
                        lane += n
            return carry

        lax.fori_loop(0, rows // 2, put, 0, unroll=2)
    extra = [x_sum[0:1, n * b : n * (b + 1)] for b in range(x_sum.shape[1] // n)]
    extra += [stats_p[:, lanes] for lanes in columns(stats_p.shape[1])]
    pair = (slice(3 * n, 6 * n), w_odd[...], (1, 0))
    conv_stats(z, xs, pair, (slice(0, 3 * n), w_even[...], 1), send, extra)


def expand(act, w, z, send, act_sum):
    rows, chans = z.shape[0], z.shape[2]
    step = rows // 7
    squares = zeros8(chans)
    for c in range(7):
        values = mm(flat(act[step * c : step * (c + 1)]), w[...])
        z[step * c : step * (c + 1)] = values.reshape(step, COLS, chans)
        parts = values.reshape(-1, 8, chans)
        squares = squares + jnp.sum(parts * parts, axis=0)
    squares = down(squares)
    spread(send, [act_sum, *(squares[:, lanes] for lanes in columns(chans))])


def columns(channels):
    return [slice(LANES * j, LANES * (j + 1)) for j in range(channels // LANES)]


def through(sums, w):
    high = sums.astype(BF16)
    rest = sums - high.astype(F32)
    mid = rest.astype(BF16)
    low = (rest - mid.astype(F32)).astype(BF16)
    lines = [v.astype(F32) for v in (high, mid, low)]
    lines.append(jnp.zeros((5, sums.shape[1]), F32))
    return down(mm(jnp.concatenate(lines, axis=0).astype(BF16), w))


def expanded_moments(got, labels, tab, w, pixels):
    label = entry(tab, OWN)
    total = group_sum(got, labels, label)
    chans = w.shape[1]
    count = tiled(group_count(labels, label), chans) * pixels
    return moments(through(total[:, 0:LANES], w[...]), total[:, LANES:], count)


def activate(tab, got, labels, z_in, norm, act, keeps):
    got = got.at[:, :, 0 : 2 * LANES]
    rows = z_in.shape[0]
    pixels = 1.0 * rows * (COLS - 4)
    mean, rstd, gain, shift, _ = scale_shift(got, labels[...], tab, norm, pixels)
    keeps[0:1, :] = mean
    keeps[1:2, :] = rstd
    scale = rstd * gain
    bias = 0.5 * (shift - mean * scale)
    scale = 0.5 * scale
    keep = valid_cols(LANES) & chan_mask(tab)

    def put(i, sums):
        low = jnp.where(keep, silu_of_half(z_in[i] * scale + bias), 0.0).astype(BF16)
        act[i] = low
        return sums + fold(low.astype(F32))

    return down(lax.fori_loop(0, rows, put, zeros8(LANES), unroll=7))


def f3(tab, got, labels, z_in, norm, w, w_p, x_sum, act, z, send, keeps, keeps_p, x_dev):
    sums = activate(tab, got, labels, z_in, norm, act, keeps)
    expand(act, w, z, send, sums)
    marks = labels[...]
    label = entry(tab, OWN)
    inputs, outer = x_sum.shape[1] // LANES, z.shape[2] // LANES
    total = group_sum(got, marks, label)
    images = group_count(marks, label)
    for b in range(inputs):
        lanes = slice(LANES * b, LANES * (b + 1))
        x_dev[:, lanes] = x_sum[0:1, lanes] - row(total, 2 + b) / images
    count = tiled(images, outer * LANES) * (1.0 * z.shape[0] * (COLS - 4))
    first, second = LANES * (2 + inputs), LANES * (2 + 2 * inputs)
    mean, rstd = moments(through(total[:, first:second], w_p[...]), total[:, second:], count)
    keeps_p[0:1, :] = mean
    keeps_p[1:2, :] = rstd


def f4(tab, got, labels, zc, zp, norm_c, norm_p, keeps_p, w_c, w, joined, slope, z, send, keeps):
    rows, chans = zc.shape[0], zc.shape[2]
    pixels = 1.0 * rows * (COLS - 4)
    mean_c, rstd_c = expanded_moments(got, labels[...], tab, w_c, pixels)
    mean_p, rstd_p = keeps_p[0:1, :], keeps_p[1:2, :]
    for k, v in enumerate((mean_c, rstd_c, mean_p, rstd_p)):
        keeps[k : k + 1, :] = v
    group = entry(tab, OWN)
    scale_c = rstd_c * gain_of(norm_c, group)
    scale_p = rstd_p * gain_of(norm_p, group)
    bias = (shift_of(norm_c, group) - mean_c * scale_c) + (
        shift_of(norm_p, group) - mean_p * scale_p
    )
    keep = valid_cols(chans)
    scale_c, scale_p, bias = 0.5 * scale_c, 0.5 * scale_p, 0.5 * bias

    def put(i, carry):
        u = zc[i] * scale_c + zp[i] * scale_p + bias
        t = jnp.tanh(u)
        p = u * t
        joined[i] = jnp.where(keep, u + p, 0.0).astype(BF16)
        slope[i] = (0.5 + 0.5 * t) * (1.0 + u - p)
        return carry

    lax.fori_loop(0, rows, put, 0, unroll=4)
    step = rows // 4
    sums, squares = zeros8(LANES), zeros8(LANES)
    for c in range(4):
        values = mm(flat(joined[step * c : step * (c + 1)]), w[...])
        z[step * c : step * (c + 1)] = values.reshape(step, COLS, LANES)
        parts = values.reshape(-1, 8, LANES)
        sums = sums + jnp.sum(parts, axis=0)
        squares = squares + jnp.sum(parts * parts, axis=0)
    spread(send, [down(sums), down(squares)])


def f5(tab, got, labels, z_in, norm, w_two, w_last, xz, x3, z, send, keeps):
    rows = z_in.shape[0]
    pixels = 1.0 * rows * (COLS - 4)
    mean, rstd, gain, shift, _ = scale_shift(got, labels[...], tab, norm, pixels)
    keeps[0:1, :] = mean
    keeps[1:2, :] = rstd
    scale = rstd * gain
    bias = 0.5 * (shift - mean * scale)
    scale = 0.5 * scale
    keep = valid_cols(LANES) & chan_mask(tab)
    x3[0] = jnp.zeros(x3.shape[1:], BF16)
    x3[rows + 1] = jnp.zeros(x3.shape[1:], BF16)
    n = LANES

    def put(i, carry):
        act = jnp.where(keep, silu_of_half(z_in[i] * scale + bias), 0.0)
        x3[i + 1, :, 0:n] = pltpu.roll(act, 1, 0).astype(BF16)
        x3[i + 1, :, n : 2 * n] = act.astype(BF16)
        x3[i + 1, :, 2 * n : 3 * n] = pltpu.roll(act, COLS - 1, 0).astype(BF16)
        return carry

    lax.fori_loop(0, rows, put, 0, unroll=2)
    lanes = slice(0, 3 * n)
    conv_stats(
        z, x3, (lanes, w_two[...], (0, 1)), (lanes, w_last[...], 2), send.at[:, :, 0 : 2 * n]
    )
    devices = send.shape[0]
    share = xz.shape[0] // devices
    pieces = xz[...].reshape(devices, share, n)
    for q in range(share):
        send[:, :, n * (2 + q) : n * (3 + q)] = pieces[:, q : q + 1, :]


def f6(tab, got, labels, z_in, norm, w, act, z, send, keeps):
    sums = activate(tab, got, labels, z_in, norm, act, keeps)
    expand(act, w, z, send, sums)


def b7(tab, got, labels, joined, z, norm, w, cot, result, grad_pre, send, keeps, wide):
    rows, chans = z.shape[0], z.shape[2]
    cols = COLS - 4
    pixels = 1.0 * rows * cols
    mean, rstd = expanded_moments(got, labels[...], tab, w, pixels)
    gain, shift = gain_of(norm, entry(tab, OWN)), shift_of(norm, entry(tab, OWN))
    keeps[0:1, :] = mean
    keeps[1:2, :] = rstd
    gate = 0.25 * tiled(entry(tab, GATE), chans)
    scale = 0.5 * rstd * gain * gate
    bias = 0.5 * (shift - mean * rstd * gain) * gate
    wide[...] = jnp.zeros(wide.shape, F32)

    def put(i, carry):
        sums, products = carry
        wide[0:cols, :] = cot[i].astype(F32)
        zz = z[i]
        u = 0.5 * joined[i].astype(F32) + zz * scale + bias
        t = jnp.tanh(u)
        p = u * t
        result[i] = (u + p)[0:cols].astype(BF16)
        g = wide[...] * ((0.5 + 0.5 * t) * (1.0 + u - p))
        grad_pre[i] = g
        return sums + fold(g), products + fold(g * (zz - mean))

    start = zeros8(chans)
    sums, products = lax.fori_loop(0, rows, put, (start, start), unroll=2)
    spread(send, [down(sums) * gate, down(products) * rstd * gate])


def backward_norm(tab, got, labels, norm, keeps, pixels, grad_norm, slots=(0, 1)):
    marks = labels[...]
    chans = norm.shape[2]
    own_shift = jnp.zeros((1, chans), F32)
    own_gain = jnp.zeros((1, chans), F32)
    group = entry(tab, OWN)
    for g in range(norm.shape[0]):
        total = group_sum(got, marks, float(g))
        shift_sum, gain_sum = row(total, slots[0]), row(total, slots[1])
        grad_norm[g, 0:1, :] = gain_sum
        grad_norm[g, 1:2, :] = shift_sum
        mine = tiled(group, chans) == float(g)
        own_shift = jnp.where(mine, shift_sum, own_shift)
        own_gain = jnp.where(mine, gain_sum, own_gain)
    count = tiled(group_count(marks, group), chans) * pixels
    mean, rstd = keeps[0:1, :], keeps[1:2, :]
    a = rstd * gain_of(norm, group)
    return mean, a, -(a * rstd) * own_gain / count, -a * own_shift / count


def slope_sums(tab, d, z_in, norm, keeps, dout, send):
    rows = z_in.shape[0]
    mean, rstd = keeps[0:1, :], keeps[1:2, :]
    group = entry(tab, OWN)
    scale = rstd * gain_of(norm, group)
    bias = 0.5 * (shift_of(norm, group) - mean * scale)
    scale = 0.5 * scale
    keep = valid_cols(LANES) & chan_mask(tab)

    def put(i, carry):
        sums, products = carry
        zz = z_in[i]
        g = jnp.where(keep, d[i] * slope_of_half(zz * scale + bias), 0.0)
        dout[i] = g
        return sums + fold(g), products + fold(g * (zz - mean))

    sums, products = lax.fori_loop(
        0, rows, put, (zeros8(LANES), zeros8(LANES)), unroll=4
    )
    spread(send, [down(sums), down(products) * rstd])


def b8(
    tab, got, labels, grad_pre, z, norm, keeps, w, z_in, norm_in, keeps_in,
    dz, dout, send, grad_norm, d,
):
    rows, chans = z.shape[0], z.shape[2]
    pixels = 1.0 * rows * (COLS - 4)
    mean, a, b, c = backward_norm(tab, got, labels, norm, keeps, pixels, grad_norm)
    a = a * (0.25 * tiled(entry(tab, GATE), norm.shape[2]))
    keep = valid_cols(chans)

    def put(i, carry):
        v = a * grad_pre[i] + b * (z[i] - mean) + c
        dz[i] = jnp.where(keep, v, 0.0).astype(BF16)
        return carry

    lax.fori_loop(0, rows, put, 0, unroll=2)
    d[...] = mm_nt(flat(dz[...]), w[...]).reshape(d.shape)
    slope_sums(tab, d, z_in, norm_in, keeps_in, dout, send)


def b9(
    tab, got, labels, dout_in, z, norm, keeps, b_two, b_last, z_in, norm_in, keeps_in,
    dz, dout, send, grad_norm, d3, d,
):
    rows = z.shape[0]
    pixels = 1.0 * rows * (COLS - 4)
    mean, a, b, c = backward_norm(tab, got, labels, norm, keeps, pixels, grad_norm)
    keep = valid_cols(LANES)
    n = LANES
    d3[0] = jnp.zeros(d3.shape[1:], BF16)
    d3[rows + 1] = jnp.zeros(d3.shape[1:], BF16)

    def put(i, carry):
        v = a * dout_in[i] + b * (z[i] - mean) + c
        v = jnp.where(keep, v, 0.0)
        d3[i + 1, :, 0:n] = pltpu.roll(v, COLS - 1, 0).astype(BF16)
        low = v.astype(BF16)
        d3[i + 1, :, n : 2 * n] = low
        dz[i] = low
        d3[i + 1, :, 2 * n : 3 * n] = pltpu.roll(v, 1, 0).astype(BF16)
        return carry

    lax.fori_loop(0, rows, put, 0, unroll=2)
    step = rows // 4
    for k in range(4):
        both = mm_nt(flat(d3[step * k : step * (k + 1) + 1]), b_two[...])
        value = mm_nt(flat(d3[step * k + 2 : step * (k + 1) + 2]), b_last[...])
        value = value + both[COLS:, 0:n] + both[0 : step * COLS, n : 2 * n]
        d[step * k : step * (k + 1)] = value.reshape(step, COLS, LANES)
    slope_sums(tab, d, z_in, norm_in, keeps_in, dout, send)


def b10(
    tab, got, labels, dout_in, z, norm, keeps, w, grad_pre, slope, zc, zp, keeps_cp,
    dz, grad_pre_2, send, grad_norm, d,
):
    rows, chans = zc.shape[0], zc.shape[2]
    pixels = 1.0 * rows * (COLS - 4)
    mean, a, b, c = backward_norm(tab, got, labels, norm, keeps, pixels, grad_norm)
    keep = valid_cols(LANES)

    def put(i, carry):
        v = a * dout_in[i] + b * (z[i] - mean) + c
        dz[i] = jnp.where(keep, v, 0.0).astype(BF16)
        return carry

    lax.fori_loop(0, rows, put, 0, unroll=4)
    d[...] = mm_nt(flat(dz[...]), w[...]).reshape(d.shape)
    mean_c, rstd_c, mean_p, rstd_p = (keeps_cp[k : k + 1, :] for k in range(4))

    def sum_up(i, carry):
        sums, prod_c, prod_p = carry
        g = (grad_pre[i] + d[i]).astype(BF16).astype(F32) * slope[i]
        grad_pre_2[i] = g
        return (
            sums + fold(g),
            prod_c + fold(g * (zc[i] - mean_c)),
            prod_p + fold(g * (zp[i] - mean_p)),
        )

    start = zeros8(chans)
    sums, prod_c, prod_p = lax.fori_loop(0, rows, sum_up, (start, start, start), unroll=2)
    spread(send, [down(sums), down(prod_c) * rstd_c, down(prod_p) * rstd_p])


def b11(
    tab, got, labels, grad_pre_2, zc, zp, norm_c, norm_p, keeps_cp, w, z_in, norm_in, keeps_in,
    dz_c, dz_p, dout, send, grad_norm_c, grad_norm_p, d,
):
    rows, chans = zc.shape[0], zc.shape[2]
    pixels = 1.0 * rows * (COLS - 4)
    mean_c, a_c, b_c, c_c = backward_norm(
        tab, got, labels, norm_c, keeps_cp.at[0:2], pixels, grad_norm_c, (0, 1)
    )
    mean_p, a_p, b_p, c_p = backward_norm(
        tab, got, labels, norm_p, keeps_cp.at[2:4], pixels, grad_norm_p, (0, 2)
    )
    keep = valid_cols(chans)

    def put(i, carry):
        g = grad_pre_2[i]
        v = a_c * g + b_c * (zc[i] - mean_c) + c_c
        dz_c[i] = jnp.where(keep, v, 0.0).astype(BF16)
        v = a_p * g + b_p * (zp[i] - mean_p) + c_p
        dz_p[i] = jnp.where(keep, v, 0.0).astype(BF16)
        return carry

    lax.fori_loop(0, rows, put, 0, unroll=2)
    d[...] = mm_nt(flat(dz_c[...]), w[...]).reshape(d.shape)
    slope_sums(tab, d, z_in, norm_in, keeps_in, dout, send)


def b12(tab, got, labels, dout_in, z, norm, keeps, xs, d2, kept, sent, grad_norm, dz, packed):
    rows = z.shape[0]
    pixels = 1.0 * rows * (COLS - 4)
    mean, a, b, c = backward_norm(tab, got, labels, norm, keeps, pixels, grad_norm)
    keep = valid_cols(LANES)
    n = LANES
    d2[rows] = jnp.zeros(d2.shape[1:], BF16)

    def put(i, carry):
        v = a * dout_in[i] + b * (z[i] - mean) + c
        v = jnp.where(keep, v, 0.0)
        low = v.astype(BF16)
        dz[i] = low
        d2[i, :, 0:n] = low
        d2[i, :, n : 2 * n] = pltpu.roll(v, COLS - 1, 0).astype(BF16)
        return carry

    lax.fori_loop(0, rows, put, 0, unroll=4)
    low = flat(dz[...])
    cur = mm_side(flat(xs[1 : rows + 1]), low)
    for k, (y, x) in enumerate(((1, 1), (1, 2), (1, 0), (2, 1), (2, 2), (2, 0))):
        put_rows(packed, n * (3 * y + x), cur[n * k : n * (k + 1)])
    up = mm_side(flat(xs[0:rows, :, 3 * n : 6 * n]), low)
    for k, (y, x) in enumerate(((0, 1), (0, 2), (0, 0))):
        put_rows(packed, n * (3 * y + x), up[n * k : n * (k + 1)])
    share_out(tab, packed, 9 * n, kept, sent)


def b12_images(
    tab, d2, b_even, b_odd, zz, norm_in, keeps_in, dn, sums_out, de, do, wide, *, own
):
    rows = de.shape[0]
    n = LANES
    half = half_of(tab)
    first = rows * (half if own else 1 - half)
    step = rows // 2
    for k in range(2):
        here = flat(d2[pl.ds(first + step * k, step)])
        below = flat(d2[pl.ds(first + step * k + 1, step)])
        de[step * k : step * (k + 1)] = mm_nt(here, b_even[...]).reshape(step, COLS, 2 * n)
        odd = mm_nt(here, b_odd[:, 0 : 2 * n]) + mm_nt(below, b_odd[:, 2 * n : 4 * n])
        do[step * k : step * (k + 1)] = odd.reshape(step, COLS, 2 * n)
    mean_1, rstd_1 = keeps_in[0:1, :], keeps_in[1:2, :]
    group = entry(tab, OWN)
    scale = rstd_1 * gain_of(norm_in, group)
    bias = 0.5 * (shift_of(norm_in, group) - mean_1 * scale)
    scale = 0.5 * scale
    keep = valid_cols(LANES) & chan_mask(tab)

    def emit(i, carry):
        sums, products = carry
        for ra in (0, 1):
            planes = (de, do)[ra]
            for cb in (0, 1):
                zv = zz[2 * i + ra, pl.ds(cb, COLS, stride=2), :]
                g = planes[i, :, n * cb : n * (cb + 1)] * slope_of_half(zv * scale + bias)
                g = jnp.where(keep, g, 0.0)
                sums = sums + fold(g)
                products = products + fold(g * (zv - mean_1))
                wide[ra, pl.ds(cb, COLS, stride=2), :] = g
            dn[2 * i + ra] = wide[ra].astype(BF16)
        return sums, products

    totals = lax.fori_loop(0, rows, emit, (zeros8(n), zeros8(n)), unroll=2)
    sums_out[0:1, :] = down(totals[0])
    sums_out[1:2, :] = down(totals[1]) * rstd_1


def b13(
    tab, got, labels, norm, keeps, w, z_own, z_for, dn_own, dn_for, gs_own, gs_for, *rest, at, held
):
    finished, outs = rest[:held], rest[held : 2 * held]
    grad, grad_norm, dz, wide, grad_v, norm_v, sems = rest[2 * held :]
    copies = [
        pltpu.make_async_copy(a, b, sems.at[k]) for k, (a, b) in enumerate(zip(finished, outs))
    ]
    for copy in copies:
        copy.start()
    rows, cols = grad.shape[1], grad.shape[2]
    half = half_of(tab)
    pixels = 2.0 * rows * cols
    marks = labels[...]
    totals = last_sums(got.at[:, at : at + 4, :], marks, norm.shape[0])
    for g in range(norm.shape[0]):
        norm_v[g, 0:1, :] = totals[g][1]
        norm_v[g, 1:2, :] = totals[g][0]
    copies.append(pltpu.make_async_copy(norm_v, grad_norm, sems.at[held]))
    copies[-1].start()
    keep = lax.broadcasted_iota(jnp.int32, (z_own.shape[1], LANES), 0) < cols
    for k, (z, dn, gs) in enumerate(((z_own, dn_own, gs_own), (z_for, dn_for, gs_for))):
        group = entry(tab, OWN if k == 0 else OTHER)
        shift_sum = own_of([t[0] for t in totals], group)
        gain_sum = own_of([t[1] for t in totals], group)
        count = group_count(marks, group) * pixels
        mean, rstd = keeps[2 * k : 2 * k + 1, :], keeps[2 * k + 1 : 2 * k + 2, :]
        a = rstd * gain_of(norm, group)
        b = -(a * rstd) * gain_sum / count
        c = -a * shift_sum / count

        def put(i, carry, z=z, dn=dn, mean=mean, a=a, b=b, c=c):
            v = a * dn[i].astype(F32) + b * (z[i] - mean) + c
            dz[i] = jnp.where(keep, v, 0.0).astype(BF16)
            return carry

        lax.fori_loop(0, rows, put, 0, unroll=4)
        place = half if k == 0 else 1 - half
        step = rows // 2
        for q in range(2):
            low = flat(dz[step * q : step * (q + 1)])
            for p in range(wide.shape[0]):
                values = mm_nt(low, w[LANES * p : LANES * (p + 1), :])
                wide[p, step * q : step * (q + 1)] = values.reshape(step, -1, LANES)

            def emit(i, carry, gs=gs, place=place):
                even = pl.ds(0, COLS, stride=2)
                for p in range(wide.shape[0]):
                    lanes = slice(LANES * p, LANES * (p + 1))
                    wide[p, 2 * i, even, :] = wide[p, 2 * i, even, :] + gs[i, :, lanes].astype(F32)
                    grad_v[place, 2 * i, :, lanes] = wide[p, 2 * i, 0:cols, :].astype(BF16)
                    grad_v[place, 2 * i + 1, :, lanes] = wide[p, 2 * i + 1, 0:cols, :].astype(BF16)
                return carry

            lax.fori_loop(step // 2 * q, step // 2 * (q + 1), emit, 0, unroll=True)
            part = pl.ds(step * q, step)
            copies.append(
                pltpu.make_async_copy(
                    grad_v.at[place, part], grad.at[place, part], sems.at[held + 1 + 2 * k + q]
                )
            )
            copies[-1].start()
    for copy in copies:
        copy.wait()


def put_rows(out, at, value):
    for j in range(value.shape[1] // LANES):
        out[at : at + value.shape[0], :] = value[:, LANES * j : LANES * (j + 1)].astype(BF16)
        at += value.shape[0]
    return at


def take_rows(source, at, out):
    rows = out.shape[0]
    for j in range(out.shape[1] // LANES):
        out[:, LANES * j : LANES * (j + 1)] = source(at, rows)
        at += rows
    return at


def share_out(tab, packed, used, kept, sent):
    if used < packed.shape[0]:
        packed[used:, :] = jnp.zeros((packed.shape[0] - used, LANES), BF16)
    half = half_of(tab)
    size = kept.shape[0] * kept.shape[1]
    for out, place in ((kept, half), (sent, 1 - half)):
        out[...] = packed[pl.ds(pl.multiple_of(size * place, 16), size), :].reshape(out.shape)


def g_most(
    tab, act_2b, dz_2c, x3, dz_2b, joined, dz_2a, act_1b, dz_1c, xee, dz_1p, w_1p,
    kept, sent, gs_own, gs_oth, packed,
):
    rows = dz_2b.shape[0]
    at = put_rows(packed, 0, mm_tn(flat(act_2b[...]), flat(dz_2c[...])))
    low = flat(dz_2b[...])
    for y in range(3):
        at = put_rows(packed, at, mm_side(flat(x3[y : y + rows]), low))
    at = put_rows(packed, at, mm_side(flat(joined[...]), flat(dz_2a[...])))
    at = put_rows(packed, at, mm_tn(flat(act_1b[...]), flat(dz_1c[...])))
    at = put_rows(packed, at, mm_tn(flat(xee[...]), flat(dz_1p[...])))
    share_out(tab, packed, at, kept, sent)
    half = half_of(tab)
    count = gs_own.shape[0]
    for k, gs in enumerate((gs_own, gs_oth)):
        first = count * (half if k == 0 else 1 - half)
        got = mm_nt(flat(dz_1p[pl.ds(first, count)]), w_1p[...])
        gs[...] = got.reshape(gs.shape).astype(BF16)


def g_xz(keeps, x_own, x_oth, z_own, z_oth, out, low):
    rows = z_own.shape[0]
    mean = keeps[0:1, :]
    value = None
    for x, z in ((x_own, z_own), (x_oth, z_oth)):

        def put(i, carry, z=z):
            low[i] = (z[i] - mean).astype(BF16)
            return carry

        lax.fori_loop(0, rows, put, 0, unroll=4)
        term = mm_tn(flat(x[...]), flat(low[...]))
        value = term if value is None else value + term
    at = value.shape[0]
    out[0:at, :] = value
    if at < out.shape[0]:
        out[at:, :] = jnp.zeros((out.shape[0] - at, LANES), F32)


def g_xd(tab, sums_own, sums_oth, norm, keeps, x_dev, x_own, x_oth, dn_own, dn_oth, out, sums, low):
    rows = dn_own.shape[0]
    n = LANES
    pixels = 1.0 * (2 * rows) * (2 * (COLS - 4))
    sums[...] = sums_own[...] + sums_oth[...]
    a = keeps[1:2, :] * gain_of(norm, entry(tab, OWN))
    local = sums[0:1, :] / pixels
    value = None
    for x, dn in ((x_own, dn_own), (x_oth, dn_oth)):

        def put(i, carry, dn=dn):
            low[i] = (a * (dn[i].astype(F32) - local)).astype(BF16)
            return carry

        lax.fori_loop(0, rows, put, 0, unroll=4)
        term = mm_tn(flat(x[...]), flat(low[...]))
        value = term if value is None else value + term
    spread_dev = jnp.broadcast_to(x_dev[...], (8, x_dev.shape[1]))
    column = jnp.transpose(spread_dev)[:, 0:1]
    value = value + column * (a * local)
    at = value.shape[0]
    out[0:at, :] = value.astype(BF16)
    if at < out.shape[0]:
        out[at:, :] = jnp.zeros((out.shape[0] - at, n), BF16)


def pack_last(tall, sums, kept, got, kept_1b, got_1b, send, *, stats_at):
    n = LANES
    devices = send.shape[0]
    piece, share = kept.shape[1], tall.shape[0] // devices
    first = kept.shape[0]
    second = first + kept_1b.shape[0]
    send[0:first, 0:piece, :] = (kept[...].astype(F32) + got[...].astype(F32)).astype(BF16)
    send[first:second, 0:piece, :] = (kept_1b[...].astype(F32) + got_1b[...].astype(F32)).astype(BF16)
    if second < devices:
        send[second:, 0:piece, :] = jnp.zeros((devices - second, piece, n), BF16)
    send[:, piece : piece + share, :] = tall[...].reshape(devices, share, n)
    high = sums[...].astype(BF16)
    rest = (sums[...] - high.astype(F32)).astype(BF16)
    for k, v in enumerate((high, rest)):
        send[:, stats_at + 2 * k : stats_at + 2 * k + 2, :] = jnp.broadcast_to(v[None], (devices, 2, n))


def last_sums(stats, marks, groups):
    values = stats[:, 0:2, :].astype(F32) + stats[:, 2:4, :].astype(F32)
    out = []
    for g in range(groups):
        total = jnp.sum(values * (marks == float(g)).astype(F32), axis=0)
        out.append((total[0:1], total[1:2]))
    return out


def add_all(got, labels, norm, keeps_all, xz_got, out, *, at, pixels):
    devices, n = got.shape[0], LANES
    half = devices // 2
    share = xz_got.shape[2] // n - 2
    piece = out.shape[1] - share
    marks = labels[...]
    value = jnp.sum(got[:, piece : piece + share, :].astype(F32), axis=0)
    sums = last_sums(got.at[:, at : at + 4, :], marks, norm.shape[0])
    for g in range(norm.shape[0]):
        rstd = keeps_all[2 * g + 1 : 2 * g + 2, :]
        count = group_count(marks, float(g)) * pixels
        b = -(rstd * rstd * norm[g, 0:1, :]) * sums[g][1] / count
        same = (marks == float(g)).astype(F32)
        rows = [
            jnp.sum(xz_got[:, :, n * (2 + q) : n * (3 + q)] * same, axis=0) for q in range(share)
        ]
        value = value + jnp.concatenate(rows, axis=0) * b
    for k in (0, 1):
        total = jnp.sum(got[half * k : half * (k + 1), 0:piece, :].astype(F32), axis=0).astype(BF16)
        out[half * k : half * (k + 1), 0:piece, :] = jnp.broadcast_to(total[None], (half, piece, n))
    out[:, piece:, :] = jnp.broadcast_to(value.astype(BF16)[None], (devices, share, n))


def unpack(
    tab, own, other, o_1a, o_1b, o_2c, o_2b, o_2a, o_1c, o_1p,
    w_1a, w_1b, w_2c, w_2b, w_2a, w_1c, w_1p, tall, packed, packed_1b, sems,
):
    half = half_of(tab)
    piece = packed.shape[1]
    first, second = packed.shape[0] // 2, packed_1b.shape[0] // 2
    for part, place in ((own, half), (other, 1 - half)):
        packed[pl.ds(first * place, first)] = part[0:first, 0:piece, :]
        packed_1b[pl.ds(second * place, second)] = part[first : first + second, 0:piece, :]
    flat_1b, rest = flat(packed_1b[...]), flat(packed[...])
    copies = []

    def leave(value, out):
        copies.append(pltpu.make_async_copy(value, out, sems.at[len(copies)]))
        copies[-1].start()

    def source(at, rows):
        return rest[at : at + rows].astype(F32)

    at = 0
    for value, out in ((w_2c, o_2c), (w_2b, o_2b), (w_2a, o_2a), (w_1c, o_1c), (w_1p, o_1p)):
        at = take_rows(source, at, value)
        leave(value, out)
    w_1b[...] = flat_1b[0 : w_1b.shape[0]].astype(F32)
    leave(w_1b, o_1b)
    tall[...] = own[:, piece:, :].astype(F32).reshape(tall.shape)
    w_1a[...] = tall[0 : w_1a.shape[0], :]
    leave(w_1a, o_1a)
    for copy in copies:
        copy.wait()


def gather(send):
    return lax.all_to_all(send, AXES, 0, 0)


def tie(*values):
    return lax.optimization_barrier(values)


def swap(block):
    return lax.ppermute(block, "rows", [(0, 1), (1, 0)])


def body(
    images, w_1a, w_1b, w_1c, w_1p, w_2a, w_2b, w_2c,
    norm_1a, norm_1b, norm_1c, norm_1p, norm_2a, norm_2b, norm_2c,
    cotangent, group, width, gate,
):
    devices = lax.axis_size("rows") * lax.axis_size("batch")
    half = lax.axis_index("rows").astype(jnp.int32).reshape(1)
    norms = (norm_1a, norm_1b, norm_1c, norm_1p, norm_2a, norm_2b, norm_2c)
    norm_1a, norm_1b, norm_1c, norm_1p, norm_2a, norm_2b, norm_2c = (
        v.transpose(1, 0, 2) for v in norms
    )
    outer, inputs = w_1c.shape[1], w_1a.shape[0]
    rows = cotangent.shape[1]
    cols_in = 2 * COLS
    n, m = LANES, devices

    def send(stats, channels=LANES):
        return ((m, channels // LANES, stats * LANES), F32)

    def maps(channels, dtype=F32):
        return ((rows, COLS, channels), dtype)

    def scratch(channels, dtype=F32):
        return pltpu.VMEM((rows, COLS, channels), dtype)

    def params(*arrays):
        return [(a.shape, F32) for a in arrays]

    def mean_scale(channels, count=1):
        return ((2 * count, channels), F32)

    wide_in = ((rows, cols_in, inputs), BF16)
    wide_z = ((rows, cols_in, n), F32)
    raw = images.shape
    tab, x_own, x_for, z_own, z_for, s1 = stage(
        f1, [((8, n), F32), wide_in, wide_in, wide_z, wide_z, send(5)],
        [*(pltpu.SMEM(v.shape, jnp.int32) for v in (half, group, width, gate)),
         pltpu.VMEM(raw, BF16), pltpu.VMEM(w_1a.shape, BF16), pltpu.SemaphoreType.DMA((7,))],
        hbm=(0, 1, 2, 3, 4, 5),
    )(half, group, width, gate, images, w_1a)
    s1, v_1b, v_2b = tie(s1, w_1b, w_2b)
    built = stage(
        prepare,
        [(v, BF16) for v in (
            (3 * n, n), (3 * n, 2 * n), (3 * n, 2 * n), (3 * n, n),
            (2 * n, 2 * n), (2 * n, 4 * n), (2 * n, 3 * n), (n, 3 * n),
        )],
    )(v_1b, v_2b)
    s1, x_for, w_even, w_odd, w_two, w_last, b_even, b_odd, b_two, b_last = tie(s1, x_for, *built)
    x_oth = swap(x_for)
    g1 = gather(s1)
    g1, x_oth = tie(g1, x_oth)
    xee, z_1p, stats_1p = stage(
        f1_strided,
        [maps(inputs, BF16), maps(outer), ((1, inputs + outer), F32)],
        [pltpu.VMEM((inputs // n, cols_in, n), F32)],
    )(tab, x_own, x_oth, w_1p)
    xs, z_1b, s2, labels, k_1a, k_all, z_oth, x_sum = stage(
        f2,
        [((rows + 1, COLS, 6 * n), BF16), maps(n), send(2 + (2 * inputs + outer) // n),
         ((m, 1, n), F32), mean_scale(n, 2), mean_scale(n, norm_1a.shape[0]), wide_z,
         ((8, inputs), F32)],
    )(tab, g1, z_own, x_own, x_oth, w_1a, norm_1a, w_even, w_odd, stats_1p)
    g2 = gather(s2)
    act_1b, z_1c, s3, k_1b, k_p, x_dev = stage(
        f3, [maps(n, BF16), maps(outer), send(1 + outer // n), mean_scale(n), mean_scale(outer),
             ((1, inputs), F32)],
    )(tab, g2, labels, z_1b, norm_1b, w_1c, w_1p, x_sum)
    g3 = gather(s3)
    joined, slope, z_2a, s4, k_cp = stage(
        f4, [maps(outer, BF16), maps(outer), maps(n), send(2), mean_scale(outer, 2)]
    )(tab, g3, labels, z_1c, z_1p, norm_1c, norm_1p, k_p, w_1c, w_2a)
    share = -(-inputs // devices)
    half_in = ((rows, cols_in, n), BF16)
    s4, k_1a = tie(s4, k_1a)
    (xz,) = stage(g_xz, [((devices * share, n), F32)], [pltpu.VMEM(half_in[0], BF16)])(
        k_1a, x_own, x_oth, z_own, z_oth
    )
    s4, xz = tie(s4, xz)
    g4 = gather(s4)
    x3, z_2b, s5, k_2a = stage(
        f5, [((rows + 2, COLS, 3 * n), BF16), maps(n), send(2 + share), mean_scale(n)]
    )(tab, g4, labels, z_2a, norm_2a, w_two, w_last, xz)
    g5 = gather(s5)
    act_2b, z_2c, s6, k_2b = stage(
        f6, [maps(n, BF16), maps(outer), send(1 + outer // n), mean_scale(n)]
    )(tab, g5, labels, z_2b, norm_2b, w_2c)
    g6 = gather(s6)
    result, grad_pre, s7, k_2c = stage(
        b7, [(cotangent.shape[1:], BF16), maps(outer), send(2, outer), mean_scale(outer)],
        [pltpu.VMEM((COLS, outer), F32)],
    )(tab, g6, labels, joined, z_2c, norm_2c, w_2c, cotangent[0])
    g7 = gather(s7)
    dz_2c, dout_2b, s8, grad_norm_2c = stage(
        b8, [maps(outer, BF16), maps(n), send(2), *params(norm_2c)], [scratch(n)]
    )(tab, g7, labels, grad_pre, z_2c, norm_2c, k_2c, w_2c, z_2b, norm_2b, k_2b)
    g8 = gather(s8)
    dz_2b, dout_2a, s9, grad_norm_2b = stage(
        b9, [maps(n, BF16), maps(n), send(2), *params(norm_2b)],
        [pltpu.VMEM((rows + 2, COLS, 3 * n), BF16), scratch(n)],
    )(tab, g8, labels, dout_2b, z_2b, norm_2b, k_2b, b_two, b_last, z_2a, norm_2a, k_2a)
    g9 = gather(s9)
    dz_2a, grad_pre_2, s10, grad_norm_2a = stage(
        b10, [maps(n, BF16), maps(outer), send(3, outer), *params(norm_2a)], [scratch(outer)]
    )(tab, g9, labels, dout_2a, z_2a, norm_2a, k_2a, w_2a, grad_pre, slope, z_1c, z_1p, k_cp)
    g10 = gather(s10)
    dz_1c, dz_1p, dout_1b, s11, grad_norm_1c, grad_norm_1p = stage(
        b11, [maps(outer, BF16), maps(outer, BF16), maps(n), send(2), *params(norm_1c, norm_1p)],
        [scratch(n)],
    )(tab, g10, labels, grad_pre_2, z_1c, z_1p, norm_1c, norm_1p, k_cp, w_1c, z_1b, norm_1b, k_1b)
    half_map = ((rows // 2, COLS, inputs), BF16)
    most_rows = sum(v.size for v in (w_2c, w_2b, w_2a, w_1c, w_1p)) // n
    rows_1b = w_1b.size // n
    piece = 16
    while -(-most_rows // (2 * piece)) - (-rows_1b // (2 * piece)) > devices:
        piece += 16
    first, second = -(-most_rows // (2 * piece)), -(-rows_1b // (2 * piece))
    part, part_1b = ((first, piece, n), BF16), ((second, piece, n), BF16)
    kept, sent, gs_own, gs_send = stage(
        g_most, [part, part, half_map, half_map], [pltpu.VMEM((2 * first * piece, n), BF16)]
    )(tab, act_2b, dz_2c, x3, dz_2b, joined, dz_2a, act_1b, dz_1c, xee, dz_1p, w_1p)
    s11, sent, gs_send = tie(s11, sent, gs_send)
    g11, sent, gs_send = tie(gather(s11), sent, gs_send)
    got, gs_for = swap(sent), swap(gs_send)
    d2, kept_1b, sent_1b, grad_norm_1b = stage(
        b12, [((rows + 1, COLS, 2 * n), BF16), part_1b, part_1b, *params(norm_1b)],
        [scratch(n, BF16), pltpu.VMEM((2 * second * piece, n), BF16)],
    )(tab, g11, labels, dout_1b, z_1b, norm_1b, k_1b, xs)
    got_1b = swap(sent_1b)
    sides = []
    for own, z in ((False, z_oth), (True, z_own)):
        sides.append(
            stage(
                functools.partial(b12_images, own=own), [half_in, ((2, n), F32)],
                [pltpu.VMEM((rows // 2, COLS, 2 * n), F32), pltpu.VMEM((rows // 2, COLS, 2 * n), F32),
                 pltpu.VMEM((2, cols_in, n), F32)],
            )(tab, d2, b_even, b_odd, z, norm_1a, k_1a)
        )
        if not own:
            dn_for = swap(sides[0][0])
            d2, _ = tie(d2, sides[0][0])
    (dn_send, sums_send), (dn_own, sums_own) = sides
    stats_at = piece + -(-share // 8) * 8
    high = -(-(stats_at + 4) // 16) * 16
    tall, sums_1a = stage(
        g_xd, [((devices * share, n), BF16), ((2, n), F32)], [pltpu.VMEM(half_in[0], BF16)]
    )(tab, sums_own, sums_send, norm_1a, k_1a, x_dev, x_own, x_oth, dn_own, dn_send)
    tall, gs_for, dn_for = tie(tall, gs_for, dn_for)
    (s12,) = stage(
        functools.partial(pack_last, stats_at=stats_at), [((devices, high, n), BF16)]
    )(tall, sums_1a, kept, got, kept_1b, got_1b)
    g12 = gather(s12)
    pixels = 4.0 * images.shape[1] * images.shape[1]
    (mine,) = stage(
        functools.partial(add_all, at=stats_at, pixels=pixels),
        [((devices, piece + share, n), BF16)],
    )(g12, labels, norm_1a, k_all, g5)
    finished = (
        result, grad_norm_1b, grad_norm_1c, grad_norm_1p, grad_norm_2a, grad_norm_2b, grad_norm_2c
    )
    held = len(finished)
    *finished, grad_images, grad_norm_1a = stage(
        functools.partial(b13, at=stats_at, held=held),
        [*((v.shape, v.dtype) for v in finished), (images.shape, BF16), *params(norm_1a)],
        [pltpu.VMEM(half_in[0], BF16), pltpu.VMEM((inputs // n, rows, cols_in, n), F32),
         pltpu.VMEM(images.shape, BF16), pltpu.VMEM(norm_1a.shape, F32),
         pltpu.SemaphoreType.DMA((held + 5,))],
        hbm_out=range(held + 2),
    )(tab, g12, labels, norm_1a, k_1a, w_1a, z_own, z_for, dn_own, dn_for, gs_own, gs_for, *finished)
    result, grad_norm_1b, grad_norm_1c, grad_norm_1p, grad_norm_2a, grad_norm_2b, grad_norm_2c = finished
    whole = gather(mine)
    weights = (w_1a, w_1b.reshape(-1, n), w_2c, w_2b.reshape(-1, n), w_2a, w_1c, w_1p)
    totals = stage(
        unpack, [(v.shape, F32) for v in weights],
        [*(pltpu.VMEM(v.shape, F32) for v in weights),
         pltpu.VMEM((devices * share, n), F32), pltpu.VMEM((2 * first, piece, n), BF16),
         pltpu.VMEM((2 * second, piece, n), BF16), pltpu.SemaphoreType.DMA((7,))],
        hbm_out=range(7),
    )(tab, whole, swap(whole))
    t_1a, t_1b, t_2c, t_2b, t_2a, t_1c, t_1p = totals
    grads = (
        grad_norm_1a, grad_norm_1b, grad_norm_1c, grad_norm_1p,
        grad_norm_2a, grad_norm_2b, grad_norm_2c,
    )
    return (
        result[None], grad_images, t_1a, t_1b.reshape(w_1b.shape), t_1c, t_1p, t_2a,
        t_2b.reshape(w_2b.shape), t_2c, *[v.transpose(1, 0, 2) for v in grads],
    )


def solution(mesh):
    return jax.shard_map(
        body,
        mesh=mesh,
        in_specs=(
            P("batch", "rows", None, None),
            *[P()] * 14,
            P(("batch", "rows"), None, None, None),
            P("batch"),
            P(),
            P(),
        ),
        out_specs=(
            P(("batch", "rows"), None, None, None),
            P("batch", "rows", None, None),
            *[P()] * 14,
        ),
        check_vma=False,
    )
```

```python
import functools

import jax
import jax.numpy as jnp
from jax import lax
from jax.experimental import pallas as pl
from jax.experimental.pallas import tpu as pltpu
from jax.sharding import PartitionSpec as P

EPSILON = 1e-05
F32 = jnp.float32
BF16 = jnp.bfloat16
AXES = ("rows", "batch")
VMEM_LIMIT = 14 * 1024 * 1024
LANES = 128
COLS = 32


def full(memory=pltpu.VMEM):
    return pl.BlockSpec(memory_space=memory)


def stage(kernel, outs, scratch=(), hbm=(), hbm_out=()):
    def place(i, outside):
        return pltpu.HBM if i in outside else pltpu.VMEM

    def call(*args):
        args = [
            pltpu.with_memory_space_constraint(a, pltpu.HBM) if i in hbm else a
            for i, a in enumerate(args)
        ]
        return pl.pallas_call(
            kernel,
            out_shape=tuple(jax.ShapeDtypeStruct(s, d) for s, d in outs),
            in_specs=[full(place(i, hbm)) for i in range(len(args))],
            out_specs=tuple(
                full(place(i, hbm_out)) for i in range(len(outs))
            ),
            scratch_shapes=list(scratch),
            compiler_params=pltpu.CompilerParams(vmem_limit_bytes=VMEM_LIMIT),
            name=(kernel.func if isinstance(kernel, functools.partial) else kernel).__name__,
        )(*args)

    return call


def silu_of_half(u):
    return u + u * jnp.tanh(u)


def slope_of_half(u):
    t = jnp.tanh(u)
    return (0.5 + 0.5 * t) * (1.0 + u - u * t)


def fold(x):
    return (x[0:8] + x[8:16]) + (x[16:24] + x[24:32])


def row(total, stat):
    blocks = total.shape[0]
    pieces = [total[j : j + 1, LANES * stat : LANES * (stat + 1)] for j in range(blocks)]
    return pieces[0] if blocks == 1 else jnp.concatenate(pieces, axis=1)


def spread(out_ref, rows):
    blocks = out_ref.shape[1]
    for stat, values in enumerate(rows):
        for j in range(blocks):
            piece = values[:, LANES * j : LANES * (j + 1)]
            out_ref[:, j : j + 1, LANES * stat : LANES * (stat + 1)] = jnp.broadcast_to(
                piece[None], (out_ref.shape[0], 1, LANES)
            )


def group_sum(got_ref, labels, label):
    same = (labels == label).astype(F32)
    stats = got_ref.shape[2] // LANES
    parts = [
        jnp.sum(got_ref[:, :, LANES * s : LANES * (s + 1)] * same, axis=0) for s in range(stats)
    ]
    return jnp.concatenate(parts, axis=1) if stats > 1 else parts[0]


def group_count(labels, label):
    return jnp.sum((labels == label).astype(F32), axis=0)


def tiled(values, channels):
    return jnp.concatenate([values] * (channels // LANES), axis=1) if channels > LANES else values


def moments(first, second, pixels):
    mean = first / pixels
    return mean, lax.rsqrt(second / pixels - mean * mean + EPSILON)


def own_of(values, label):
    out = values[0]
    label = tiled(label, out.shape[1])
    for g in range(1, len(values)):
        out = jnp.where(label == float(g), values[g], out)
    return out


def gain_of(norm_ref, label):
    return own_of([norm_ref[g, 0:1, :] for g in range(norm_ref.shape[0])], label)


def shift_of(norm_ref, label):
    return own_of([norm_ref[g, 1:2, :] for g in range(norm_ref.shape[0])], label)


def valid_cols(channels):
    return lax.broadcasted_iota(jnp.int32, (COLS, channels), 0) < COLS - 4


def chan_mask(tab):
    return lax.broadcasted_iota(jnp.int32, (1, LANES), 1).astype(F32) < entry(tab, LIMIT)


def flat(x):
    return x.reshape(x.shape[0] * x.shape[1], x.shape[2])


def mm(a, b):
    return jnp.dot(a, b, preferred_element_type=F32)


def mm_nt(a, b):
    return lax.dot_general(a, b, (((1,), (1,)), ((), ())), preferred_element_type=F32)


def mm_tn(a, b):
    return lax.dot_general(a, b, (((0,), (0,)), ((), ())), preferred_element_type=F32)


def mm_side(a, b):
    turned = mm_tn(b, a)
    blocks = [
        jnp.transpose(turned[:, LANES * j : LANES * (j + 1)]) for j in range(a.shape[1] // LANES)
    ]
    return blocks[0] if len(blocks) == 1 else jnp.concatenate(blocks, axis=0)


def zeros8(channels):
    return jnp.zeros((8, channels), F32)


def down(x):
    return jnp.sum(x, axis=0, keepdims=True)


OWN, OTHER, HALF, LIMIT, GATE = range(5)


def entry(tab, k):
    return tab[k : k + 1, :]


def half_of(tab):
    return (jnp.sum(entry(tab, HALF)) * (1.0 / LANES)).astype(jnp.int32)


def prepare(w1b, w2b, w_even, w_odd, w_two, w_last, b_even, b_odd, b_two, b_last):
    n = LANES
    for k, (y, x) in enumerate(((1, 1), (1, 2), (1, 0))):
        w_even[n * k : n * (k + 1), :] = w1b[y, x]
    for k, (low, high) in enumerate((((2, 1), (0, 1)), ((2, 2), (0, 2)), ((2, 0), (0, 0)))):
        w_odd[n * k : n * (k + 1), 0:n] = w1b[low]
        w_odd[n * k : n * (k + 1), n : 2 * n] = w1b[high]
    for x in range(3):
        w_two[n * x : n * (x + 1), 0:n] = w2b[0, x]
        w_two[n * x : n * (x + 1), n : 2 * n] = w2b[1, x]
        w_last[n * x : n * (x + 1), :] = w2b[2, x]
        b_two[0:n, n * x : n * (x + 1)] = w2b[1, x]
        b_two[n : 2 * n, n * x : n * (x + 1)] = w2b[2, x]
        b_last[:, n * x : n * (x + 1)] = w2b[0, x]
    nothing = jnp.zeros((n, n), BF16)
    b_even[0:n, 0:n] = w1b[1, 1]
    b_even[0:n, n : 2 * n] = nothing
    b_even[n : 2 * n, 0:n] = w1b[1, 2]
    b_even[n : 2 * n, n : 2 * n] = w1b[1, 0]
    for k, top in ((0, 2), (1, 0)):
        b_odd[0:n, 2 * n * k : 2 * n * k + n] = w1b[top, 1]
        b_odd[0:n, 2 * n * k + n : 2 * n * (k + 1)] = nothing
        b_odd[n : 2 * n, 2 * n * k : 2 * n * k + n] = w1b[top, 2]
        b_odd[n : 2 * n, 2 * n * k + n : 2 * n * (k + 1)] = w1b[top, 0]


def widen(source, x_pad):
    rows, cols, chans = source.shape
    gap = x_pad.shape[1] - cols

    def put(i, carry):
        x_pad[i, 0:cols, :] = source[i]
        x_pad[i, cols : cols + gap, :] = jnp.zeros((gap, chans), BF16)
        return carry

    lax.fori_loop(0, rows, put, 0, unroll=4)


def first_project(x_pad, w, z, stats=True):
    rows = x_pad.shape[0]
    step = rows // 4
    sums, squares = zeros8(LANES), zeros8(LANES)
    for c in range(4):
        values = mm(flat(x_pad[step * c : step * (c + 1)]), w[...])
        z[step * c : step * (c + 1)] = values.reshape(step, x_pad.shape[1], LANES)
        if stats:
            parts = values.reshape(-1, 8, LANES)
            sums = sums + jnp.sum(parts, axis=0)
            squares = squares + jnp.sum(parts * parts, axis=0)
    return sums, squares


def f1(
    half_at, group_at, width_at, gate_at, images, w_at, tab, x_own, x_for, z_own, z_for, send,
    half_ref, group, width, gate, raw, w, found, sems,
):
    pairs = (
        (half_at, half_ref), (group_at, group), (width_at, width), (gate_at, gate), (w_at, w),
        (images.at[0], raw.at[0]), (images.at[1], raw.at[1]),
    )
    copies = [pltpu.make_async_copy(a, b, sems.at[k]) for k, (a, b) in enumerate(pairs)]
    for k in (0, 4, 5, 6, 1, 2, 3):
        copies[k].start()
    for k in (0, 4, 5):
        copies[k].wait()
    half = half_ref[0]
    sides = ((x_own, z_own), (x_for, z_for))

    def one(k):
        for place in (0, 1):

            @pl.when(half == place)
            def _():
                x_pad, z = sides[k] if place == 0 else sides[1 - k]
                widen(raw.at[k], x_pad)
                sums, squares = first_project(x_pad, w, z)
                at = 2 * (k if place == 0 else 1 - k)
                found[at : at + 1, :] = down(sums)
                found[at + 1 : at + 2, :] = down(squares)

    one(0)
    copies[6].wait()
    one(1)
    for k in (1, 2, 3):
        copies[k].wait()
    rows = [found[k : k + 1, :] for k in range(4)]
    own, other = group[half], group[1 - half]
    values = {
        OWN: own, OTHER: other, HALF: half, LIMIT: w.shape[1] // 4 * width[own], GATE: gate[own]
    }
    tab[...] = jnp.zeros(tab.shape, F32)
    for k, v in values.items():
        tab[k : k + 1, :] = jnp.full((1, LANES), v.astype(F32))
    spread(send, [*rows, jnp.full((1, LANES), (own + 4 * other).astype(F32))])


def f1_strided(tab, x_own, x_oth, w, xee, z, stats, wide):
    half = half_of(tab)
    rows = x_own.shape[0] // 2
    for k, x_pad in enumerate((x_own, x_oth)):
        first = rows * (half if k == 0 else 1 - half)

        def put(i, carry, x_pad=x_pad, first=first):
            for b in range(wide.shape[0]):
                lanes = slice(LANES * b, LANES * (b + 1))
                wide[b] = x_pad[2 * i, :, lanes].astype(F32)
                xee[first + i, :, lanes] = wide[b, pl.ds(0, COLS, stride=2), :].astype(BF16)
            return carry

        lax.fori_loop(0, rows, put, 0, unroll=2)
    total = 2 * rows
    step = total // 7
    chans = z.shape[2]
    squares = zeros8(chans)
    for c in range(7):
        values = mm(flat(xee[step * c : step * (c + 1)]), w[...])
        z[step * c : step * (c + 1)] = values.reshape(step, COLS, chans)
        parts = values.reshape(-1, 8, chans)
        squares = squares + jnp.sum(parts * parts, axis=0)
    ones = jnp.ones((8, total * COLS), BF16)
    stats[:, 0 : w.shape[0]] = mm(ones, flat(xee[...]))[0:1]
    stats[:, w.shape[0] :] = down(squares)


def scale_shift(got, labels, tab, norm, pixels, slot=0):
    label = entry(tab, OWN)
    total = group_sum(got, labels, label)
    chans = norm.shape[2]
    count = tiled(group_count(labels, label), chans) * pixels
    mean, rstd = moments(row(total, 2 * slot), row(total, 2 * slot + 1), count)
    gain, shift = gain_of(norm, entry(tab, OWN)), shift_of(norm, entry(tab, OWN))
    return mean, rstd, gain, shift, count


def conv_stats(z, source, pair, single, send, extra=()):
    keep = valid_cols(LANES)[None]
    rows = z.shape[0]
    step = rows // 4
    (lanes_2, w_2, offsets), (lanes_1, w_1, offset) = pair, single
    sums, squares = zeros8(LANES), zeros8(LANES)
    base = min(offsets)
    for c in range(4):
        at = step * c
        both = mm(flat(source[at + base : at + base + step + 1, :, lanes_2]), w_2)
        values = mm(flat(source[at + offset : at + offset + step, :, lanes_1]), w_1)
        for k, own in enumerate(offsets):
            skip = COLS * (own - base)
            values = values + both[skip : skip + step * COLS, LANES * k : LANES * (k + 1)]
        values = jnp.where(keep, values.reshape(step, COLS, LANES), 0.0)
        z[at : at + step] = values
        parts = values.reshape(-1, 8, LANES)
        sums = sums + jnp.sum(parts, axis=0)
        squares = squares + jnp.sum(parts * parts, axis=0)
    spread(send, [down(sums), down(squares), *extra])


def f2(
    tab, got, z_own, x_oth, w, norm, w_even, w_odd, stats_p,
    xs, z, send, labels, keeps, keeps_all, z_oth,
):
    codes = got[:, :, 4 * LANES : 5 * LANES]
    others = jnp.floor(0.25 * codes)
    marks = codes - 4.0 * others
    labels[...] = marks
    rows = xs.shape[0] - 1
    pixels = 4.0 * rows * (COLS - 4)
    first_project(x_oth, w, z_oth, False)
    for g in range(norm.shape[0]):
        mine, theirs = (marks == float(g)).astype(F32), (others == float(g)).astype(F32)
        totals = [
            jnp.sum(
                got[:, :, LANES * s : LANES * (s + 1)] * mine
                + got[:, :, LANES * (s + 2) : LANES * (s + 3)] * theirs,
                axis=0,
            )
            for s in (0, 1)
        ]
        mean, rstd = moments(*totals, group_count(marks, float(g)) * pixels)
        keeps_all[2 * g : 2 * g + 1, :] = mean
        keeps_all[2 * g + 1 : 2 * g + 2, :] = rstd
    for k, slot in enumerate((OWN, OTHER)):
        for q in (0, 1):
            choices = [keeps_all[2 * g + q : 2 * g + q + 1, :] for g in range(norm.shape[0])]
            keeps[2 * k + q : 2 * k + q + 1, :] = own_of(choices, entry(tab, slot))
    mean, rstd = keeps[0:1, :], keeps[1:2, :]
    gain, shift = gain_of(norm, entry(tab, OWN)), shift_of(norm, entry(tab, OWN))
    scale = rstd * gain
    bias = 0.5 * (shift - mean * scale)
    scale = 0.5 * scale
    keep = valid_cols(LANES) & chan_mask(tab)
    half = half_of(tab)
    xs[0] = jnp.zeros(xs.shape[1:], BF16)
    n = LANES
    for k, zz in enumerate((z_own, z_oth)):
        first = 1 + (rows // 2) * (half if k == 0 else 1 - half)

        def put(i, carry, zz=zz, first=first):
            lane = 0
            for a in (0, 1):
                for b in (0, 1):
                    u = zz[2 * i + a, pl.ds(b, COLS, stride=2), :] * scale + bias
                    act = jnp.where(keep, silu_of_half(u), 0.0)
                    xs[first + i, :, lane : lane + n] = act.astype(BF16)
                    lane += n
                    if b == 1:
                        moved = pltpu.roll(act, 1, 0)
                        xs[first + i, :, lane : lane + n] = moved.astype(BF16)
                        lane += n
            return carry

        lax.fori_loop(0, rows // 2, put, 0, unroll=2)
    extra = [stats_p[:, lanes] for lanes in columns(stats_p.shape[1])]
    pair = (slice(3 * n, 6 * n), w_odd[...], (1, 0))
    conv_stats(z, xs, pair, (slice(0, 3 * n), w_even[...], 1), send, extra)


def expand(act, w, z, send, act_sum):
    rows, chans = z.shape[0], z.shape[2]
    step = rows // 7
    squares = zeros8(chans)
    for c in range(7):
        values = mm(flat(act[step * c : step * (c + 1)]), w[...])
        z[step * c : step * (c + 1)] = values.reshape(step, COLS, chans)
        parts = values.reshape(-1, 8, chans)
        squares = squares + jnp.sum(parts * parts, axis=0)
    squares = down(squares)
    spread(send, [act_sum, *(squares[:, lanes] for lanes in columns(chans))])


def join(pieces):
    return pieces[0] if len(pieces) == 1 else jnp.concatenate(pieces, axis=1)


def columns(channels):
    return [slice(LANES * j, LANES * (j + 1)) for j in range(channels // LANES)]


def through(sums, w):
    high = sums.astype(BF16)
    rest = sums - high.astype(F32)
    mid = rest.astype(BF16)
    low = (rest - mid.astype(F32)).astype(BF16)
    lines = [v.astype(F32) for v in (high, mid, low)]
    lines.append(jnp.zeros((5, sums.shape[1]), F32))
    return down(mm(jnp.concatenate(lines, axis=0).astype(BF16), w))


def expanded_moments(got, labels, tab, w, pixels):
    label = entry(tab, OWN)
    total = group_sum(got, labels, label)
    chans = w.shape[1]
    count = tiled(group_count(labels, label), chans) * pixels
    return moments(through(total[:, 0:LANES], w[...]), total[:, LANES:], count)


def activate(tab, got, labels, z_in, norm, act, keeps):
    got = got.at[:, :, 0 : 2 * LANES]
    rows = z_in.shape[0]
    pixels = 1.0 * rows * (COLS - 4)
    mean, rstd, gain, shift, _ = scale_shift(got, labels[...], tab, norm, pixels)
    keeps[0:1, :] = mean
    keeps[1:2, :] = rstd
    scale = rstd * gain
    bias = 0.5 * (shift - mean * scale)
    scale = 0.5 * scale
    keep = valid_cols(LANES) & chan_mask(tab)

    def put(i, sums):
        low = jnp.where(keep, silu_of_half(z_in[i] * scale + bias), 0.0).astype(BF16)
        act[i] = low
        return sums + fold(low.astype(F32))

    return down(lax.fori_loop(0, rows, put, zeros8(LANES), unroll=7))


def f3(tab, got, labels, z_in, norm, w, w_p, act, z, send, keeps, keeps_p):
    sums = activate(tab, got, labels, z_in, norm, act, keeps)
    expand(act, w, z, send, sums)
    marks, label = labels[...], entry(tab, OWN)
    total = group_sum(got, marks, label)
    outer, first = z.shape[2], 2 * LANES
    second = first + w_p.shape[0]
    count = tiled(group_count(marks, label), outer) * (1.0 * z.shape[0] * (COLS - 4))
    mean, rstd = moments(through(total[:, first:second], w_p[...]), total[:, second:], count)
    keeps_p[0:1, :] = mean
    keeps_p[1:2, :] = rstd


def f4(tab, got, labels, zc, zp, norm_c, norm_p, keeps_p, w_c, w, joined, slope, z, send, keeps):
    rows, chans = zc.shape[0], zc.shape[2]
    pixels = 1.0 * rows * (COLS - 4)
    mean_c, rstd_c = expanded_moments(got, labels[...], tab, w_c, pixels)
    mean_p, rstd_p = keeps_p[0:1, :], keeps_p[1:2, :]
    for k, v in enumerate((mean_c, rstd_c, mean_p, rstd_p)):
        keeps[k : k + 1, :] = v
    group = entry(tab, OWN)
    scale_c = rstd_c * gain_of(norm_c, group)
    scale_p = rstd_p * gain_of(norm_p, group)
    bias = (shift_of(norm_c, group) - mean_c * scale_c) + (
        shift_of(norm_p, group) - mean_p * scale_p
    )
    keep = valid_cols(chans)
    scale_c, scale_p, bias = 0.5 * scale_c, 0.5 * scale_p, 0.5 * bias

    def put(i, carry):
        u = zc[i] * scale_c + zp[i] * scale_p + bias
        t = jnp.tanh(u)
        p = u * t
        joined[i] = jnp.where(keep, u + p, 0.0).astype(BF16)
        slope[i] = (0.5 + 0.5 * t) * (1.0 + u - p)
        return carry

    lax.fori_loop(0, rows, put, 0, unroll=4)
    step = rows // 4
    sums, squares = zeros8(LANES), zeros8(LANES)
    for c in range(4):
        values = mm(flat(joined[step * c : step * (c + 1)]), w[...])
        z[step * c : step * (c + 1)] = values.reshape(step, COLS, LANES)
        parts = values.reshape(-1, 8, LANES)
        sums = sums + jnp.sum(parts, axis=0)
        squares = squares + jnp.sum(parts * parts, axis=0)
    spread(send, [down(sums), down(squares)])


def put_shares(xz, send, part):
    n, devices = LANES, send.shape[0]
    share = xz.shape[0] // devices
    pieces = xz[...].reshape(devices, share, n)
    first = (share + 1) // 2 * part
    for q in range(first, (share + 1) // 2 if part == 0 else share):
        at = n * (2 + q - first)
        send[:, :, at : at + n] = pieces[:, q : q + 1, :]


def f5(tab, got, labels, z_in, norm, w_two, w_last, xz, x3, z, send, keeps):
    rows = z_in.shape[0]
    pixels = 1.0 * rows * (COLS - 4)
    mean, rstd, gain, shift, _ = scale_shift(got, labels[...], tab, norm, pixels)
    keeps[0:1, :] = mean
    keeps[1:2, :] = rstd
    scale = rstd * gain
    bias = 0.5 * (shift - mean * scale)
    scale = 0.5 * scale
    keep = valid_cols(LANES) & chan_mask(tab)
    x3[0] = jnp.zeros(x3.shape[1:], BF16)
    x3[rows + 1] = jnp.zeros(x3.shape[1:], BF16)
    n = LANES

    def put(i, carry):
        act = jnp.where(keep, silu_of_half(z_in[i] * scale + bias), 0.0)
        x3[i + 1, :, 0:n] = pltpu.roll(act, 1, 0).astype(BF16)
        x3[i + 1, :, n : 2 * n] = act.astype(BF16)
        x3[i + 1, :, 2 * n : 3 * n] = pltpu.roll(act, COLS - 1, 0).astype(BF16)
        return carry

    lax.fori_loop(0, rows, put, 0, unroll=2)
    lanes = slice(0, 3 * n)
    conv_stats(
        z, x3, (lanes, w_two[...], (0, 1)), (lanes, w_last[...], 2), send.at[:, :, 0 : 2 * n]
    )
    put_shares(xz, send, 0)


def f6(tab, got, labels, z_in, norm, w, act, z, send, keeps):
    sums = activate(tab, got, labels, z_in, norm, act, keeps)
    expand(act, w, z, send, sums)


def b7(tab, got, labels, joined, z, norm, w, cot, result, grad_pre, send, keeps, wide):
    rows, chans = z.shape[0], z.shape[2]
    cols = COLS - 4
    pixels = 1.0 * rows * cols
    mean, rstd = expanded_moments(got, labels[...], tab, w, pixels)
    gain, shift = gain_of(norm, entry(tab, OWN)), shift_of(norm, entry(tab, OWN))
    keeps[0:1, :] = mean
    keeps[1:2, :] = rstd
    gate = 0.25 * tiled(entry(tab, GATE), chans)
    scale = 0.5 * rstd * gain * gate
    bias = 0.5 * (shift - mean * rstd * gain) * gate
    wide[...] = jnp.zeros(wide.shape, F32)

    def put(i, carry):
        sums, products = carry
        wide[0:cols, :] = cot[i].astype(F32)
        zz = z[i]
        u = 0.5 * joined[i].astype(F32) + zz * scale + bias
        t = jnp.tanh(u)
        p = u * t
        result[i] = (u + p)[0:cols].astype(BF16)
        g = wide[...] * ((0.5 + 0.5 * t) * (1.0 + u - p))
        grad_pre[i] = g
        return sums + fold(g), products + fold(g * (zz - mean))

    start = zeros8(chans)
    sums, products = lax.fori_loop(0, rows, put, (start, start), unroll=2)
    spread(send, [down(sums) * gate, down(products) * rstd * gate])


def backward_norm(tab, got, labels, norm, keeps, pixels, grad_norm):
    marks = labels[...]
    chans = norm.shape[2]
    own_shift = jnp.zeros((1, chans), F32)
    own_gain = jnp.zeros((1, chans), F32)
    group = entry(tab, OWN)
    for g in range(norm.shape[0]):
        total = group_sum(got.at[:, :, 0 : 2 * LANES], marks, float(g))
        shift_sum, gain_sum = row(total, 0), row(total, 1)
        grad_norm[g, 0:1, :] = gain_sum
        grad_norm[g, 1:2, :] = shift_sum
        mine = tiled(group, chans) == float(g)
        own_shift = jnp.where(mine, shift_sum, own_shift)
        own_gain = jnp.where(mine, gain_sum, own_gain)
    count = tiled(group_count(marks, group), chans) * pixels
    mean, rstd = keeps[0:1, :], keeps[1:2, :]
    a = rstd * gain_of(norm, group)
    return mean, a, -(a * rstd) * own_gain / count, -a * own_shift / count


def slope_sums(tab, d, z_in, norm, keeps, dout, send):
    rows = z_in.shape[0]
    mean, rstd = keeps[0:1, :], keeps[1:2, :]
    group = entry(tab, OWN)
    scale = rstd * gain_of(norm, group)
    bias = 0.5 * (shift_of(norm, group) - mean * scale)
    scale = 0.5 * scale
    keep = valid_cols(LANES) & chan_mask(tab)

    def put(i, carry):
        sums, products = carry
        zz = z_in[i]
        g = jnp.where(keep, d[i] * slope_of_half(zz * scale + bias), 0.0)
        dout[i] = g
        return sums + fold(g), products + fold(g * (zz - mean))

    sums, products = lax.fori_loop(
        0, rows, put, (zeros8(LANES), zeros8(LANES)), unroll=4
    )
    spread(send, [down(sums), down(products) * rstd])


def b8(
    tab, got, labels, grad_pre, z, norm, keeps, w, z_in, norm_in, keeps_in, xz,
    dz, dout, send, grad_norm, d,
):
    rows, chans = z.shape[0], z.shape[2]
    pixels = 1.0 * rows * (COLS - 4)
    mean, a, b, c = backward_norm(tab, got, labels, norm, keeps, pixels, grad_norm)
    a = a * (0.25 * tiled(entry(tab, GATE), norm.shape[2]))
    keep = valid_cols(chans)

    def put(i, carry):
        v = a * grad_pre[i] + b * (z[i] - mean) + c
        dz[i] = jnp.where(keep, v, 0.0).astype(BF16)
        return carry

    lax.fori_loop(0, rows, put, 0, unroll=2)
    d[...] = mm_nt(flat(dz[...]), w[...]).reshape(d.shape)
    slope_sums(tab, d, z_in, norm_in, keeps_in, dout, send.at[:, :, 0 : 2 * LANES])
    put_shares(xz, send, 1)


def b9(
    tab, got, labels, dout_in, z, norm, keeps, b_two, b_last, z_in, norm_in, keeps_in, x_sum,
    dz, dout, send, grad_norm, d3, d,
):
    rows = z.shape[0]
    pixels = 1.0 * rows * (COLS - 4)
    mean, a, b, c = backward_norm(tab, got, labels, norm, keeps, pixels, grad_norm)
    keep = valid_cols(LANES)
    n = LANES
    d3[0] = jnp.zeros(d3.shape[1:], BF16)
    d3[rows + 1] = jnp.zeros(d3.shape[1:], BF16)

    def put(i, carry):
        v = a * dout_in[i] + b * (z[i] - mean) + c
        v = jnp.where(keep, v, 0.0)
        d3[i + 1, :, 0:n] = pltpu.roll(v, COLS - 1, 0).astype(BF16)
        low = v.astype(BF16)
        d3[i + 1, :, n : 2 * n] = low
        dz[i] = low
        d3[i + 1, :, 2 * n : 3 * n] = pltpu.roll(v, 1, 0).astype(BF16)
        return carry

    lax.fori_loop(0, rows, put, 0, unroll=2)
    step = rows // 4
    for k in range(4):
        both = mm_nt(flat(d3[step * k : step * (k + 1) + 1]), b_two[...])
        value = mm_nt(flat(d3[step * k + 2 : step * (k + 1) + 2]), b_last[...])
        value = value + both[COLS:, 0:n] + both[0 : step * COLS, n : 2 * n]
        d[step * k : step * (k + 1)] = value.reshape(step, COLS, LANES)
    slope_sums(tab, d, z_in, norm_in, keeps_in, dout, send.at[:, :, 0 : 2 * n])
    turned = join([jnp.transpose(x_sum[lanes, :])[0:1] for lanes in columns(x_sum.shape[0])])
    spread(send.at[:, :, 2 * n :], [turned[:, lanes] for lanes in columns(x_sum.shape[0])])


def b10(
    tab, got, labels, dout_in, z, norm, keeps, w, grad_pre, slope, zc, zp, keeps_cp,
    dz, grad_pre_2, send, grad_norm, sums_p, d,
):
    rows, chans = zc.shape[0], zc.shape[2]
    pixels = 1.0 * rows * (COLS - 4)
    mean, a, b, c = backward_norm(tab, got, labels, norm, keeps, pixels, grad_norm)
    keep = valid_cols(LANES)

    def put(i, carry):
        v = a * dout_in[i] + b * (z[i] - mean) + c
        dz[i] = jnp.where(keep, v, 0.0).astype(BF16)
        return carry

    lax.fori_loop(0, rows, put, 0, unroll=4)
    d[...] = mm_nt(flat(dz[...]), w[...]).reshape(d.shape)
    mean_c, rstd_c, mean_p, rstd_p = (keeps_cp[k : k + 1, :] for k in range(4))

    def sum_up(i, carry):
        sums, prod_c, prod_p = carry
        g = (grad_pre[i] + d[i]).astype(BF16).astype(F32) * slope[i]
        grad_pre_2[i] = g
        return (
            sums + fold(g),
            prod_c + fold(g * (zc[i] - mean_c)),
            prod_p + fold(g * (zp[i] - mean_p)),
        )

    start = zeros8(chans)
    sums, prod_c, prod_p = lax.fori_loop(0, rows, sum_up, (start, start, start), unroll=2)
    spread(send, [down(sums), down(prod_c) * rstd_c])
    sums_p[0:1, :] = down(sums)
    sums_p[1:2, :] = down(prod_p) * rstd_p


def b11(
    tab, got, labels, grad_pre_2, zc, norm, keeps, w, z_in, norm_in, keeps_in, sums_p,
    dz, dout, send, grad_norm, d,
):
    pixels = 1.0 * zc.shape[0] * (COLS - 4)
    mean, a, b, c = backward_norm(tab, got, labels, norm, keeps.at[0:2], pixels, grad_norm)
    normed_grad(dz, grad_pre_2, zc, mean, a, b, c)
    d[...] = mm_nt(flat(dz[...]), w[...]).reshape(d.shape)
    slope_sums(tab, d, z_in, norm_in, keeps_in, dout, send.at[:, :, 0 : 2 * LANES])
    products = sums_p[1:2, :]
    spread(send.at[:, :, 2 * LANES :], [products[:, lanes] for lanes in columns(zc.shape[2])])


def normed_grad(dz, dout, z, mean, a, b, c):
    keep = valid_cols(z.shape[2])

    def put(i, carry):
        v = a * dout[i] + b * (z[i] - mean) + c
        dz[i] = jnp.where(keep, v, 0.0).astype(BF16)
        return carry

    lax.fori_loop(0, z.shape[0], put, 0, unroll=2)


def joined_norm(tab, got_c, got_p, labels, norm, keeps, pixels, grad_norm):
    marks, group, chans = labels[...], entry(tab, OWN), norm.shape[2]
    sums = []
    for g in range(norm.shape[0]):
        shift_sum = row(group_sum(got_c.at[:, :, 0:LANES], marks, float(g)), 0)
        gain_sum = group_sum(got_p.at[:, :, 2 * LANES :], marks, float(g))
        grad_norm[g, 0:1, :] = gain_sum
        grad_norm[g, 1:2, :] = shift_sum
        sums.append((gain_sum, shift_sum))
    count = tiled(group_count(marks, group), chans) * pixels
    own_gain, own_shift = (own_of([v[k] for v in sums], group) for k in (0, 1))
    mean, rstd = keeps[0:1, :], keeps[1:2, :]
    a = rstd * gain_of(norm, group)
    return mean, a, -(a * rstd) * own_gain / count, -a * own_shift / count


def b12(tab, got, labels, dout_in, z, norm, keeps, xs, d2, kept, sent, grad_norm, dz, packed):
    rows = z.shape[0]
    pixels = 1.0 * rows * (COLS - 4)
    mean, a, b, c = backward_norm(tab, got, labels, norm, keeps, pixels, grad_norm)
    keep = valid_cols(LANES)
    n = LANES
    d2[rows] = jnp.zeros(d2.shape[1:], BF16)

    def put(i, carry):
        v = a * dout_in[i] + b * (z[i] - mean) + c
        v = jnp.where(keep, v, 0.0)
        low = v.astype(BF16)
        dz[i] = low
        d2[i, :, 0:n] = low
        d2[i, :, n : 2 * n] = pltpu.roll(v, COLS - 1, 0).astype(BF16)
        return carry

    lax.fori_loop(0, rows, put, 0, unroll=4)
    low = flat(dz[...])
    cur = mm_side(flat(xs[1 : rows + 1]), low)
    for k, (y, x) in enumerate(((1, 1), (1, 2), (1, 0), (2, 1), (2, 2), (2, 0))):
        put_rows(packed, n * (3 * y + x), cur[n * k : n * (k + 1)])
    up = mm_side(flat(xs[0:rows, :, 3 * n : 6 * n]), low)
    for k, (y, x) in enumerate(((0, 1), (0, 2), (0, 0))):
        put_rows(packed, n * (3 * y + x), up[n * k : n * (k + 1)])
    share_out(tab, packed, 9 * n, kept, sent)


def b12_images(
    tab, d2, b_even, b_odd, zz, norm_in, keeps_in, dn, sums_out, de, do, wide, *, own
):
    rows = de.shape[0]
    n = LANES
    half = half_of(tab)
    first = rows * (half if own else 1 - half)
    step = rows // 2
    for k in range(2):
        here = flat(d2[pl.ds(first + step * k, step)])
        below = flat(d2[pl.ds(first + step * k + 1, step)])
        de[step * k : step * (k + 1)] = mm_nt(here, b_even[...]).reshape(step, COLS, 2 * n)
        odd = mm_nt(here, b_odd[:, 0 : 2 * n]) + mm_nt(below, b_odd[:, 2 * n : 4 * n])
        do[step * k : step * (k + 1)] = odd.reshape(step, COLS, 2 * n)
    mean_1, rstd_1 = keeps_in[0:1, :], keeps_in[1:2, :]
    group = entry(tab, OWN)
    scale = rstd_1 * gain_of(norm_in, group)
    bias = 0.5 * (shift_of(norm_in, group) - mean_1 * scale)
    scale = 0.5 * scale
    keep = valid_cols(LANES) & chan_mask(tab)

    def emit(i, carry):
        sums, products = carry
        for ra in (0, 1):
            planes = (de, do)[ra]
            for cb in (0, 1):
                zv = zz[2 * i + ra, pl.ds(cb, COLS, stride=2), :]
                g = planes[i, :, n * cb : n * (cb + 1)] * slope_of_half(zv * scale + bias)
                g = jnp.where(keep, g, 0.0)
                sums = sums + fold(g)
                products = products + fold(g * (zv - mean_1))
                wide[ra, pl.ds(cb, COLS, stride=2), :] = g
            dn[2 * i + ra] = wide[ra].astype(BF16)
        return sums, products

    totals = lax.fori_loop(0, rows, emit, (zeros8(n), zeros8(n)), unroll=2)
    sums_out[0:1, :] = down(totals[0])
    sums_out[1:2, :] = down(totals[1]) * rstd_1


def b13(
    tab, got, labels, norm, keeps, w, z_own, z_for, dn_own, dn_for, gs_own, gs_for, *rest, at, held
):
    finished, outs = rest[:held], rest[held : 2 * held]
    grad, grad_norm, dz, wide, grad_v, norm_v, sems = rest[2 * held :]
    copies = [
        pltpu.make_async_copy(a, b, sems.at[k]) for k, (a, b) in enumerate(zip(finished, outs))
    ]
    for copy in copies:
        copy.start()
    rows, cols = grad.shape[1], grad.shape[2]
    half = half_of(tab)
    pixels = 2.0 * rows * cols
    marks = labels[...]
    totals = last_sums(got.at[:, at : at + 4, :], marks, norm.shape[0])
    for g in range(norm.shape[0]):
        norm_v[g, 0:1, :] = totals[g][1]
        norm_v[g, 1:2, :] = totals[g][0]
    copies.append(pltpu.make_async_copy(norm_v, grad_norm, sems.at[held]))
    copies[-1].start()
    keep = lax.broadcasted_iota(jnp.int32, (z_own.shape[1], LANES), 0) < cols
    for k, (z, dn, gs) in enumerate(((z_own, dn_own, gs_own), (z_for, dn_for, gs_for))):
        group = entry(tab, OWN if k == 0 else OTHER)
        shift_sum = own_of([t[0] for t in totals], group)
        gain_sum = own_of([t[1] for t in totals], group)
        count = group_count(marks, group) * pixels
        mean, rstd = keeps[2 * k : 2 * k + 1, :], keeps[2 * k + 1 : 2 * k + 2, :]
        a = rstd * gain_of(norm, group)
        b = -(a * rstd) * gain_sum / count
        c = -a * shift_sum / count

        def put(i, carry, z=z, dn=dn, mean=mean, a=a, b=b, c=c):
            v = a * dn[i].astype(F32) + b * (z[i] - mean) + c
            dz[i] = jnp.where(keep, v, 0.0).astype(BF16)
            return carry

        lax.fori_loop(0, rows, put, 0, unroll=4)
        place = half if k == 0 else 1 - half
        step = rows // 2
        for q in range(2):
            low = flat(dz[step * q : step * (q + 1)])
            for p in range(wide.shape[0]):
                values = mm_nt(low, w[LANES * p : LANES * (p + 1), :])
                wide[p, step * q : step * (q + 1)] = values.reshape(step, -1, LANES)

            def emit(i, carry, gs=gs, place=place):
                even = pl.ds(0, COLS, stride=2)
                for p in range(wide.shape[0]):
                    lanes = slice(LANES * p, LANES * (p + 1))
                    wide[p, 2 * i, even, :] = wide[p, 2 * i, even, :] + gs[i, :, lanes].astype(F32)
                    grad_v[place, 2 * i, :, lanes] = wide[p, 2 * i, 0:cols, :].astype(BF16)
                    grad_v[place, 2 * i + 1, :, lanes] = wide[p, 2 * i + 1, 0:cols, :].astype(BF16)
                return carry

            lax.fori_loop(step // 2 * q, step // 2 * (q + 1), emit, 0, unroll=True)
            part = pl.ds(step * q, step)
            copies.append(
                pltpu.make_async_copy(
                    grad_v.at[place, part], grad.at[place, part], sems.at[held + 1 + 2 * k + q]
                )
            )
            copies[-1].start()
    for copy in copies:
        copy.wait()


def put_rows(out, at, value):
    for j in range(value.shape[1] // LANES):
        out[at : at + value.shape[0], :] = value[:, LANES * j : LANES * (j + 1)].astype(BF16)
        at += value.shape[0]
    return at


def take_rows(source, at, out):
    rows = out.shape[0]
    for j in range(out.shape[1] // LANES):
        out[:, LANES * j : LANES * (j + 1)] = source(at, rows)
        at += rows
    return at


def share_out(tab, packed, used, kept, sent):
    if used < packed.shape[0]:
        packed[used:, :] = jnp.zeros((packed.shape[0] - used, LANES), BF16)
    half = half_of(tab)
    size = kept.shape[0] * kept.shape[1]
    for out, place in ((kept, half), (sent, 1 - half)):
        out[...] = packed[pl.ds(pl.multiple_of(size * place, 16), size), :].reshape(out.shape)


def g_most(
    tab, act_2b, dz_2c, x3, dz_2b, joined, dz_2a, act_1b, dz_1c, xee, w_p,
    got_c, got_p, labels, norm, keeps, grad_pre_2, zp,
    kept, sent, gs_own, gs_oth, grad_norm, packed, dz_p,
):
    rows = dz_2b.shape[0]
    pixels = 1.0 * rows * (COLS - 4)
    coefs = joined_norm(tab, got_c, got_p, labels, norm, keeps.at[2:4], pixels, grad_norm)
    normed_grad(dz_p, grad_pre_2, zp, *coefs)
    at = put_rows(packed, 0, mm_tn(flat(act_2b[...]), flat(dz_2c[...])))
    low = flat(dz_2b[...])
    for y in range(3):
        at = put_rows(packed, at, mm_side(flat(x3[y : y + rows]), low))
    at = put_rows(packed, at, mm_side(flat(joined[...]), flat(dz_2a[...])))
    at = put_rows(packed, at, mm_tn(flat(act_1b[...]), flat(dz_1c[...])))
    at = put_rows(packed, at, mm_tn(flat(xee[...]), flat(dz_p[...])))
    share_out(tab, packed, at, kept, sent)
    half = half_of(tab)
    count = gs_own.shape[0]
    for k, gs in enumerate((gs_own, gs_oth)):
        first = count * (half if k == 0 else 1 - half)
        got = mm_nt(flat(dz_p[pl.ds(first, count)]), w_p[...])
        gs[...] = got.reshape(gs.shape).astype(BF16)


def g_xz(keeps, x_own, x_oth, z_own, z_oth, out, x_sum, low):
    rows, n = z_own.shape[0], LANES
    mean = keeps[0:1, :]
    low[:, :, n : 2 * n] = jnp.ones((rows, z_own.shape[1], n), BF16)
    value = None
    for x, z in ((x_own, z_own), (x_oth, z_oth)):

        def put(i, carry, z=z):
            low[i, :, 0:n] = (z[i] - mean).astype(BF16)
            return carry

        lax.fori_loop(0, rows, put, 0, unroll=4)
        term = mm_tn(flat(x[...]), flat(low[...]))
        value = term if value is None else value + term
    at = value.shape[0]
    out[0:at, :] = value[:, 0:n]
    if at < out.shape[0]:
        out[at:, :] = jnp.zeros((out.shape[0] - at, n), F32)
    x_sum[...] = value[:, n : 2 * n]


def g_xd(
    tab, sums_own, sums_oth, norm, keeps, x_sum, got_x, labels, x_own, x_oth, dn_own, dn_oth,
    out, sums, low,
):
    rows = dn_own.shape[0]
    n = LANES
    pixels = 1.0 * (2 * rows) * (2 * (COLS - 4))
    sums[...] = sums_own[...] + sums_oth[...]
    a = keeps[1:2, :] * gain_of(norm, entry(tab, OWN))
    local = sums[0:1, :] / pixels
    value = None
    for x, dn in ((x_own, dn_own), (x_oth, dn_oth)):

        def put(i, carry, dn=dn):
            low[i] = (a * (dn[i].astype(F32) - local)).astype(BF16)
            return carry

        lax.fori_loop(0, rows, put, 0, unroll=4)
        term = mm_tn(flat(x[...]), flat(low[...]))
        value = term if value is None else value + term
    marks, label = labels[...], entry(tab, OWN)
    total = group_sum(got_x.at[:, :, 2 * n :], marks, label)
    total = total / tiled(group_count(marks, label), total.shape[1])
    total = jnp.broadcast_to(total, (8, total.shape[1]))
    means = jnp.concatenate(
        [jnp.transpose(total[:, lanes])[:, 0:1] for lanes in columns(total.shape[1])], axis=0
    )
    value = value + (x_sum[...] - means) * (a * local)
    at = value.shape[0]
    out[0:at, :] = value.astype(BF16)
    if at < out.shape[0]:
        out[at:, :] = jnp.zeros((out.shape[0] - at, n), BF16)


def pack_last(tall, sums, kept, got, kept_1b, got_1b, send, *, stats_at):
    n = LANES
    devices = send.shape[0]
    piece, share = kept.shape[1], tall.shape[0] // devices
    first = kept.shape[0]
    second = first + kept_1b.shape[0]
    send[0:first, 0:piece, :] = (kept[...].astype(F32) + got[...].astype(F32)).astype(BF16)
    send[first:second, 0:piece, :] = (kept_1b[...].astype(F32) + got_1b[...].astype(F32)).astype(BF16)
    if second < devices:
        send[second:, 0:piece, :] = jnp.zeros((devices - second, piece, n), BF16)
    send[:, piece : piece + share, :] = tall[...].reshape(devices, share, n)
    high = sums[...].astype(BF16)
    rest = (sums[...] - high.astype(F32)).astype(BF16)
    for k, v in enumerate((high, rest)):
        send[:, stats_at + 2 * k : stats_at + 2 * k + 2, :] = jnp.broadcast_to(v[None], (devices, 2, n))


def last_sums(stats, marks, groups):
    values = stats[:, 0:2, :].astype(F32) + stats[:, 2:4, :].astype(F32)
    out = []
    for g in range(groups):
        total = jnp.sum(values * (marks == float(g)).astype(F32), axis=0)
        out.append((total[0:1], total[1:2]))
    return out


def add_all(got, labels, norm, keeps_all, got_a, got_b, out, *, at, pixels):
    devices, n = got.shape[0], LANES
    half = devices // 2
    split = got_a.shape[2] // n - 2
    share = split + got_b.shape[2] // n - 2
    piece = out.shape[1] - share
    marks = labels[...]
    value = jnp.sum(got[:, piece : piece + share, :].astype(F32), axis=0)
    sums = last_sums(got.at[:, at : at + 4, :], marks, norm.shape[0])
    for g in range(norm.shape[0]):
        rstd = keeps_all[2 * g + 1 : 2 * g + 2, :]
        count = group_count(marks, float(g)) * pixels
        b = -(rstd * rstd * norm[g, 0:1, :]) * sums[g][1] / count
        same = (marks == float(g)).astype(F32)
        rows = [
            jnp.sum(source[:, :, n * (2 + q) : n * (3 + q)] * same, axis=0)
            for source, count_q in ((got_a, split), (got_b, share - split))
            for q in range(count_q)
        ]
        value = value + jnp.concatenate(rows, axis=0) * b
    for k in (0, 1):
        total = jnp.sum(got[half * k : half * (k + 1), 0:piece, :].astype(F32), axis=0).astype(BF16)
        out[half * k : half * (k + 1), 0:piece, :] = jnp.broadcast_to(total[None], (half, piece, n))
    out[:, piece:, :] = jnp.broadcast_to(value.astype(BF16)[None], (devices, share, n))


def unpack(
    tab, own, other, o_1a, o_1b, o_2c, o_2b, o_2a, o_1c, o_1p,
    w_1a, w_1b, w_2c, w_2b, w_2a, w_1c, w_1p, tall, sems, *, first, second, piece,
):
    half = half_of(tab)
    copies = []

    def leave(value, out):
        copies.append(pltpu.make_async_copy(value, out, sems.at[len(copies)]))
        return copies[-1]

    weights = ((w_2c, o_2c), (w_2b, o_2b), (w_2a, o_2a), (w_1c, o_1c), (w_1p, o_1p))
    leaving = [leave(*v) for v in (*weights, (w_1b, o_1b), (w_1a, o_1a))]
    for place in (0, 1):

        @pl.when(half == place)
        def _():
            halves = (own, other) if place == 0 else (other, own)
            most = [flat(v[0:first, 0:piece, :]) for v in halves]
            last = [flat(v[first : first + second, 0:piece, :]) for v in halves]
            size = first * piece

            def source(at, rows):
                pieces = []
                if at < size:
                    pieces.append(most[0][at : min(at + rows, size)])
                if at + rows > size:
                    pieces.append(most[1][max(at - size, 0) : at + rows - size])
                pieces = [v.astype(F32) for v in pieces]
                return pieces[0] if len(pieces) == 1 else jnp.concatenate(pieces, axis=0)

            at = 0
            for k, (value, _) in enumerate(weights):
                at = take_rows(source, at, value)
                leaving[k].start()
            size = second * piece
            w_1b[0:size] = last[0].astype(F32)
            w_1b[size:] = last[1][0 : w_1b.shape[0] - size].astype(F32)
            leaving[5].start()

    tall[...] = own[:, piece:, :].astype(F32).reshape(tall.shape)
    w_1a[...] = tall[0 : w_1a.shape[0], :]
    leaving[6].start()
    for copy in copies:
        copy.wait()


def gather(send):
    return lax.all_to_all(send, AXES, 0, 0)


def tie(*values):
    return lax.optimization_barrier(values)


def swap(block):
    return lax.ppermute(block, "rows", [(0, 1), (1, 0)])


def body(
    images, w_1a, w_1b, w_1c, w_1p, w_2a, w_2b, w_2c,
    norm_1a, norm_1b, norm_1c, norm_1p, norm_2a, norm_2b, norm_2c,
    cotangent, group, width, gate,
):
    devices = lax.axis_size("rows") * lax.axis_size("batch")
    half = lax.axis_index("rows").astype(jnp.int32).reshape(1)
    norms = (norm_1a, norm_1b, norm_1c, norm_1p, norm_2a, norm_2b, norm_2c)
    norm_1a, norm_1b, norm_1c, norm_1p, norm_2a, norm_2b, norm_2c = (
        v.transpose(1, 0, 2) for v in norms
    )
    outer, inputs = w_1c.shape[1], w_1a.shape[0]
    rows = cotangent.shape[1]
    cols_in = 2 * COLS
    n, m = LANES, devices

    def send(stats, channels=LANES):
        return ((m, channels // LANES, stats * LANES), F32)

    def maps(channels, dtype=F32):
        return ((rows, COLS, channels), dtype)

    def scratch(channels, dtype=F32):
        return pltpu.VMEM((rows, COLS, channels), dtype)

    def params(*arrays):
        return [(a.shape, F32) for a in arrays]

    def mean_scale(channels, count=1):
        return ((2 * count, channels), F32)

    wide_in = ((rows, cols_in, inputs), BF16)
    wide_z = ((rows, cols_in, n), F32)
    raw = images.shape
    tab, x_own, x_for, z_own, z_for, s1 = stage(
        f1, [((8, n), F32), wide_in, wide_in, wide_z, wide_z, send(5)],
        [*(pltpu.SMEM(v.shape, jnp.int32) for v in (half, group, width, gate)),
         pltpu.VMEM(raw, BF16), pltpu.VMEM(w_1a.shape, BF16), pltpu.VMEM((8, n), F32),
         pltpu.SemaphoreType.DMA((7,))],
        hbm=(0, 1, 2, 3, 4, 5),
    )(half, group, width, gate, images, w_1a)
    s1, v_1b, v_2b = tie(s1, w_1b, w_2b)
    built = stage(
        prepare,
        [(v, BF16) for v in (
            (3 * n, n), (3 * n, 2 * n), (3 * n, 2 * n), (3 * n, n),
            (2 * n, 2 * n), (2 * n, 4 * n), (2 * n, 3 * n), (n, 3 * n),
        )],
    )(v_1b, v_2b)
    s1, x_for, w_even, w_odd, w_two, w_last, b_even, b_odd, b_two, b_last = tie(s1, x_for, *built)
    x_oth = swap(x_for)
    g1 = gather(s1)
    g1, x_oth = tie(g1, x_oth)
    xee, z_1p, stats_1p = stage(
        f1_strided,
        [maps(inputs, BF16), maps(outer), ((1, inputs + outer), F32)],
        [pltpu.VMEM((inputs // n, cols_in, n), F32)],
    )(tab, x_own, x_oth, w_1p)
    xs, z_1b, s2, labels, k_1a, k_all, z_oth = stage(
        f2,
        [((rows + 1, COLS, 6 * n), BF16), maps(n), send(2 + (inputs + outer) // n),
         ((m, 1, n), F32), mean_scale(n, 2), mean_scale(n, norm_1a.shape[0]), wide_z],
    )(tab, g1, z_own, x_oth, w_1a, norm_1a, w_even, w_odd, stats_1p)
    g2 = gather(s2)
    act_1b, z_1c, s3, k_1b, k_p = stage(
        f3, [maps(n, BF16), maps(outer), send(1 + outer // n), mean_scale(n), mean_scale(outer)]
    )(tab, g2, labels, z_1b, norm_1b, w_1c, w_1p)
    g3 = gather(s3)
    joined, slope, z_2a, s4, k_cp = stage(
        f4, [maps(outer, BF16), maps(outer), maps(n), send(2), mean_scale(outer, 2)]
    )(tab, g3, labels, z_1c, z_1p, norm_1c, norm_1p, k_p, w_1c, w_2a)
    share = -(-inputs // devices)
    half_in = ((rows, cols_in, n), BF16)
    s4, k_1a = tie(s4, k_1a)
    xz, x_sum = stage(
        g_xz, [((devices * share, n), F32), ((inputs, n), F32)],
        [pltpu.VMEM((rows, cols_in, 2 * n), BF16)],
    )(k_1a, x_own, x_oth, z_own, z_oth)
    s4, xz, x_sum = tie(s4, xz, x_sum)
    g4 = gather(s4)
    x3, z_2b, s5, k_2a = stage(
        f5, [((rows + 2, COLS, 3 * n), BF16), maps(n), send(2 + (share + 1) // 2), mean_scale(n)]
    )(tab, g4, labels, z_2a, norm_2a, w_two, w_last, xz)
    g5 = gather(s5)
    act_2b, z_2c, s6, k_2b = stage(
        f6, [maps(n, BF16), maps(outer), send(1 + outer // n), mean_scale(n)]
    )(tab, g5, labels, z_2b, norm_2b, w_2c)
    g6 = gather(s6)
    result, grad_pre, s7, k_2c = stage(
        b7, [(cotangent.shape[1:], BF16), maps(outer), send(2, outer), mean_scale(outer)],
        [pltpu.VMEM((COLS, outer), F32)],
    )(tab, g6, labels, joined, z_2c, norm_2c, w_2c, cotangent[0])
    g7 = gather(s7)
    dz_2c, dout_2b, s8, grad_norm_2c = stage(
        b8, [maps(outer, BF16), maps(n), send(2 + share // 2), *params(norm_2c)], [scratch(n)]
    )(tab, g7, labels, grad_pre, z_2c, norm_2c, k_2c, w_2c, z_2b, norm_2b, k_2b, xz)
    g8 = gather(s8)
    dz_2b, dout_2a, s9, grad_norm_2b = stage(
        b9, [maps(n, BF16), maps(n), send(2 + inputs // n), *params(norm_2b)],
        [pltpu.VMEM((rows + 2, COLS, 3 * n), BF16), scratch(n)],
    )(tab, g8, labels, dout_2b, z_2b, norm_2b, k_2b, b_two, b_last, z_2a, norm_2a, k_2a, x_sum)
    g9 = gather(s9)
    dz_2a, grad_pre_2, s10, grad_norm_2a, sums_p = stage(
        b10,
        [maps(n, BF16), maps(outer), send(2, outer), *params(norm_2a), mean_scale(outer)],
        [scratch(outer)],
    )(tab, g9, labels, dout_2a, z_2a, norm_2a, k_2a, w_2a, grad_pre, slope, z_1c, z_1p, k_cp)
    g10 = gather(s10)
    dz_1c, dout_1b, s11, grad_norm_1c = stage(
        b11, [maps(outer, BF16), maps(n), send(2 + outer // n), *params(norm_1c)], [scratch(n)]
    )(tab, g10, labels, grad_pre_2, z_1c, norm_1c, k_cp, w_1c, z_1b, norm_1b, k_1b, sums_p)
    g11 = gather(s11)
    half_map = ((rows // 2, COLS, inputs), BF16)
    most_rows = sum(v.size for v in (w_2c, w_2b, w_2a, w_1c, w_1p)) // n
    rows_1b = w_1b.size // n
    piece = 16
    while -(-most_rows // (2 * piece)) - (-rows_1b // (2 * piece)) > devices:
        piece += 16
    first, second = -(-most_rows // (2 * piece)), -(-rows_1b // (2 * piece))
    part, part_1b = ((first, piece, n), BF16), ((second, piece, n), BF16)
    kept, sent, gs_own, gs_send, grad_norm_1p = stage(
        g_most, [part, part, half_map, half_map, *params(norm_1p)],
        [pltpu.VMEM((2 * first * piece, n), BF16), scratch(outer, BF16)],
    )(tab, act_2b, dz_2c, x3, dz_2b, joined, dz_2a, act_1b, dz_1c, xee, w_1p,
      g10, g11, labels, norm_1p, k_cp, grad_pre_2, z_1p)
    got, gs_for = swap(sent), swap(gs_send)
    g11, _ = tie(g11, sent)
    d2, kept_1b, sent_1b, grad_norm_1b = stage(
        b12, [((rows + 1, COLS, 2 * n), BF16), part_1b, part_1b, *params(norm_1b)],
        [scratch(n, BF16), pltpu.VMEM((2 * second * piece, n), BF16)],
    )(tab, g11, labels, dout_1b, z_1b, norm_1b, k_1b, xs)
    got_1b = swap(sent_1b)
    sides = []
    for own, z in ((False, z_oth), (True, z_own)):
        sides.append(
            stage(
                functools.partial(b12_images, own=own), [half_in, ((2, n), F32)],
                [pltpu.VMEM((rows // 2, COLS, 2 * n), F32), pltpu.VMEM((rows // 2, COLS, 2 * n), F32),
                 pltpu.VMEM((2, cols_in, n), F32)],
            )(tab, d2, b_even, b_odd, z, norm_1a, k_1a)
        )
        if not own:
            dn_for = swap(sides[0][0])
            d2, _ = tie(d2, sides[0][0])
    (dn_send, sums_send), (dn_own, sums_own) = sides
    stats_at = piece + -(-share // 8) * 8
    high = -(-(stats_at + 4) // 16) * 16
    tall, sums_1a = stage(
        g_xd, [((devices * share, n), BF16), ((2, n), F32)], [pltpu.VMEM(half_in[0], BF16)]
    )(tab, sums_own, sums_send, norm_1a, k_1a, x_sum, g9, labels, x_own, x_oth, dn_own, dn_send)
    tall, gs_for, dn_for = tie(tall, gs_for, dn_for)
    (s12,) = stage(
        functools.partial(pack_last, stats_at=stats_at), [((devices, high, n), BF16)]
    )(tall, sums_1a, kept, got, kept_1b, got_1b)
    g12 = gather(s12)
    pixels = 4.0 * images.shape[1] * images.shape[1]
    (mine,) = stage(
        functools.partial(add_all, at=stats_at, pixels=pixels),
        [((devices, piece + share, n), BF16)],
    )(g12, labels, norm_1a, k_all, g5, g8)
    finished = (
        result, grad_norm_1b, grad_norm_1c, grad_norm_1p, grad_norm_2a, grad_norm_2b, grad_norm_2c
    )
    held = len(finished)
    *finished, grad_images, grad_norm_1a = stage(
        functools.partial(b13, at=stats_at, held=held),
        [*((v.shape, v.dtype) for v in finished), (images.shape, BF16), *params(norm_1a)],
        [pltpu.VMEM(half_in[0], BF16), pltpu.VMEM((inputs // n, rows, cols_in, n), F32),
         pltpu.VMEM(images.shape, BF16), pltpu.VMEM(norm_1a.shape, F32),
         pltpu.SemaphoreType.DMA((held + 5,))],
        hbm_out=range(held + 2),
    )(tab, g12, labels, norm_1a, k_1a, w_1a, z_own, z_for, dn_own, dn_for, gs_own, gs_for, *finished)
    result, grad_norm_1b, grad_norm_1c, grad_norm_1p, grad_norm_2a, grad_norm_2b, grad_norm_2c = finished
    whole = gather(mine)
    weights = (w_1a, w_1b.reshape(-1, n), w_2c, w_2b.reshape(-1, n), w_2a, w_1c, w_1p)
    totals = stage(
        functools.partial(unpack, first=first, second=second, piece=piece),
        [(v.shape, F32) for v in weights],
        [*(pltpu.VMEM(v.shape, F32) for v in weights),
         pltpu.VMEM((devices * share, n), F32), pltpu.SemaphoreType.DMA((7,))],
        hbm_out=range(7),
    )(tab, whole, swap(whole))
    t_1a, t_1b, t_2c, t_2b, t_2a, t_1c, t_1p = totals
    grads = (
        grad_norm_1a, grad_norm_1b, grad_norm_1c, grad_norm_1p,
        grad_norm_2a, grad_norm_2b, grad_norm_2c,
    )
    return (
        result[None], grad_images, t_1a, t_1b.reshape(w_1b.shape), t_1c, t_1p, t_2a,
        t_2b.reshape(w_2b.shape), t_2c, *[v.transpose(1, 0, 2) for v in grads],
    )


def solution(mesh):
    return jax.shard_map(
        body,
        mesh=mesh,
        in_specs=(
            P("batch", "rows", None, None),
            *[P()] * 14,
            P(("batch", "rows"), None, None, None),
            P("batch"),
            P(),
            P(),
        ),
        out_specs=(
            P(("batch", "rows"), None, None, None),
            P("batch", "rows", None, None),
            *[P()] * 14,
        ),
        check_vma=False,
    )
```

```python
import functools

import jax
import jax.numpy as jnp
from jax import lax
from jax.experimental import pallas as pl
from jax.experimental.pallas import tpu as pltpu
from jax.sharding import PartitionSpec as P

EPSILON = 1e-05
F32 = jnp.float32
BF16 = jnp.bfloat16
AXES = ("rows", "batch")
VMEM_LIMIT = 14 * 1024 * 1024
LANES = 128
COLS = 32


def full(memory=pltpu.VMEM):
    return pl.BlockSpec(memory_space=memory)


def stage(kernel, outs, scratch=(), hbm=(), hbm_out=()):
    def place(i, outside):
        return pltpu.HBM if i in outside else pltpu.VMEM

    def call(*args):
        args = [
            pltpu.with_memory_space_constraint(a, pltpu.HBM) if i in hbm else a
            for i, a in enumerate(args)
        ]
        return pl.pallas_call(
            kernel,
            out_shape=tuple(jax.ShapeDtypeStruct(s, d) for s, d in outs),
            in_specs=[full(place(i, hbm)) for i in range(len(args))],
            out_specs=tuple(
                full(place(i, hbm_out)) for i in range(len(outs))
            ),
            scratch_shapes=list(scratch),
            compiler_params=pltpu.CompilerParams(vmem_limit_bytes=VMEM_LIMIT),
            name=(kernel.func if isinstance(kernel, functools.partial) else kernel).__name__,
        )(*args)

    return call


def silu_of_half(u):
    return u + u * jnp.tanh(u)


def slope_of_half(u):
    t = jnp.tanh(u)
    return (0.5 + 0.5 * t) * (1.0 + u - u * t)


def fold(x):
    return (x[0:8] + x[8:16]) + (x[16:24] + x[24:32])


def row(total, stat):
    blocks = total.shape[0]
    pieces = [total[j : j + 1, LANES * stat : LANES * (stat + 1)] for j in range(blocks)]
    return pieces[0] if blocks == 1 else jnp.concatenate(pieces, axis=1)


def spread(out_ref, rows):
    blocks = out_ref.shape[1]
    for stat, values in enumerate(rows):
        for j in range(blocks):
            piece = values[:, LANES * j : LANES * (j + 1)]
            out_ref[:, j : j + 1, LANES * stat : LANES * (stat + 1)] = jnp.broadcast_to(
                piece[None], (out_ref.shape[0], 1, LANES)
            )


def group_sum(got_ref, labels, label):
    same = (labels == label).astype(F32)
    stats = got_ref.shape[2] // LANES
    parts = [
        jnp.sum(got_ref[:, :, LANES * s : LANES * (s + 1)] * same, axis=0) for s in range(stats)
    ]
    return jnp.concatenate(parts, axis=1) if stats > 1 else parts[0]


def group_count(labels, label):
    return jnp.sum((labels == label).astype(F32), axis=0)


def tiled(values, channels):
    return jnp.concatenate([values] * (channels // LANES), axis=1) if channels > LANES else values


def moments(first, second, pixels):
    mean = first / pixels
    return mean, lax.rsqrt(second / pixels - mean * mean + EPSILON)


def own_of(values, label):
    out = values[0]
    label = tiled(label, out.shape[1])
    for g in range(1, len(values)):
        out = jnp.where(label == float(g), values[g], out)
    return out


def gain_of(norm_ref, label):
    return own_of([norm_ref[g, 0:1, :] for g in range(norm_ref.shape[0])], label)


def shift_of(norm_ref, label):
    return own_of([norm_ref[g, 1:2, :] for g in range(norm_ref.shape[0])], label)


def valid_cols(channels):
    return lax.broadcasted_iota(jnp.int32, (COLS, channels), 0) < COLS - 4


def chan_mask(tab):
    return lax.broadcasted_iota(jnp.int32, (1, LANES), 1).astype(F32) < entry(tab, LIMIT)


def flat(x):
    return x.reshape(x.shape[0] * x.shape[1], x.shape[2])


def mm(a, b):
    return jnp.dot(a, b, preferred_element_type=F32)


def mm_nt(a, b):
    return lax.dot_general(a, b, (((1,), (1,)), ((), ())), preferred_element_type=F32)


def mm_tn(a, b):
    return lax.dot_general(a, b, (((0,), (0,)), ((), ())), preferred_element_type=F32)


def mm_side(a, b):
    turned = mm_tn(b, a)
    blocks = [
        jnp.transpose(turned[:, LANES * j : LANES * (j + 1)]) for j in range(a.shape[1] // LANES)
    ]
    return blocks[0] if len(blocks) == 1 else jnp.concatenate(blocks, axis=0)


def zeros8(channels):
    return jnp.zeros((8, channels), F32)


def down(x):
    return jnp.sum(x, axis=0, keepdims=True)


OWN, OTHER, HALF, LIMIT, GATE = range(5)


def entry(tab, k):
    return tab[k : k + 1, :]


def half_of(tab):
    return (jnp.sum(entry(tab, HALF)) * (1.0 / LANES)).astype(jnp.int32)


def prepare(w1b, w2b, w_even, w_odd, w_two, w_last, b_even, b_odd, b_two, b_last):
    n = LANES
    for k, (y, x) in enumerate(((1, 1), (1, 2), (1, 0))):
        w_even[n * k : n * (k + 1), :] = w1b[y, x]
    for k, (low, high) in enumerate((((2, 1), (0, 1)), ((2, 2), (0, 2)), ((2, 0), (0, 0)))):
        w_odd[n * k : n * (k + 1), 0:n] = w1b[low]
        w_odd[n * k : n * (k + 1), n : 2 * n] = w1b[high]
    for x in range(3):
        w_two[n * x : n * (x + 1), 0:n] = w2b[0, x]
        w_two[n * x : n * (x + 1), n : 2 * n] = w2b[1, x]
        w_last[n * x : n * (x + 1), :] = w2b[2, x]
        b_two[0:n, n * x : n * (x + 1)] = w2b[1, x]
        b_two[n : 2 * n, n * x : n * (x + 1)] = w2b[2, x]
        b_last[:, n * x : n * (x + 1)] = w2b[0, x]
    nothing = jnp.zeros((n, n), BF16)
    b_even[0:n, 0:n] = w1b[1, 1]
    b_even[0:n, n : 2 * n] = nothing
    b_even[n : 2 * n, 0:n] = w1b[1, 2]
    b_even[n : 2 * n, n : 2 * n] = w1b[1, 0]
    for k, top in ((0, 2), (1, 0)):
        b_odd[0:n, 2 * n * k : 2 * n * k + n] = w1b[top, 1]
        b_odd[0:n, 2 * n * k + n : 2 * n * (k + 1)] = nothing
        b_odd[n : 2 * n, 2 * n * k : 2 * n * k + n] = w1b[top, 2]
        b_odd[n : 2 * n, 2 * n * k + n : 2 * n * (k + 1)] = w1b[top, 0]


def widen(source, x_pad):
    rows, cols, chans = source.shape
    gap = x_pad.shape[1] - cols

    def put(i, carry):
        x_pad[i, 0:cols, :] = source[i]
        x_pad[i, cols : cols + gap, :] = jnp.zeros((gap, chans), BF16)
        return carry

    lax.fori_loop(0, rows, put, 0, unroll=4)


def first_project(x_pad, w, z, stats=True):
    rows = x_pad.shape[0]
    step = rows // 4
    sums, squares = zeros8(LANES), zeros8(LANES)
    for c in range(4):
        values = mm(flat(x_pad[step * c : step * (c + 1)]), w[...])
        z[step * c : step * (c + 1)] = values.reshape(step, x_pad.shape[1], LANES)
        if stats:
            parts = values.reshape(-1, 8, LANES)
            sums = sums + jnp.sum(parts, axis=0)
            squares = squares + jnp.sum(parts * parts, axis=0)
    return sums, squares


def f1(
    half_at, group_at, width_at, gate_at, images, w_at, tab, x_own, x_for, z_own, z_for, send,
    half_ref, group, width, gate, raw, w, found, sems,
):
    pairs = (
        (half_at, half_ref), (group_at, group), (width_at, width), (gate_at, gate), (w_at, w),
        (images.at[0], raw.at[0]), (images.at[1], raw.at[1]),
    )
    copies = [pltpu.make_async_copy(a, b, sems.at[k]) for k, (a, b) in enumerate(pairs)]
    for k in (0, 4, 5, 6, 1, 2, 3):
        copies[k].start()
    for k in (0, 4, 5):
        copies[k].wait()
    half = half_ref[0]
    sides = ((x_own, z_own), (x_for, z_for))

    def one(k):
        for place in (0, 1):

            @pl.when(half == place)
            def _():
                x_pad, z = sides[k] if place == 0 else sides[1 - k]
                widen(raw.at[k], x_pad)
                sums, squares = first_project(x_pad, w, z)
                at = 2 * (k if place == 0 else 1 - k)
                found[at : at + 1, :] = down(sums)
                found[at + 1 : at + 2, :] = down(squares)

    one(0)
    copies[6].wait()
    one(1)
    for k in (1, 2, 3):
        copies[k].wait()
    rows = [found[k : k + 1, :] for k in range(4)]
    own, other = group[half], group[1 - half]
    values = {
        OWN: own, OTHER: other, HALF: half, LIMIT: w.shape[1] // 4 * width[own], GATE: gate[own]
    }
    tab[...] = jnp.zeros(tab.shape, F32)
    for k, v in values.items():
        tab[k : k + 1, :] = jnp.full((1, LANES), v.astype(F32))
    spread(send, [*rows, jnp.full((1, LANES), (own + 4 * other).astype(F32))])


def f1_strided(tab, x_own, x_oth, w, xee, z, stats, wide):
    half = half_of(tab)
    rows = x_own.shape[0] // 2
    for k, x_pad in enumerate((x_own, x_oth)):
        first = rows * (half if k == 0 else 1 - half)

        def put(i, carry, x_pad=x_pad, first=first):
            for b in range(wide.shape[0]):
                lanes = slice(LANES * b, LANES * (b + 1))
                wide[b] = x_pad[2 * i, :, lanes].astype(F32)
                xee[first + i, :, lanes] = wide[b, pl.ds(0, COLS, stride=2), :].astype(BF16)
            return carry

        lax.fori_loop(0, rows, put, 0, unroll=2)
    total = 2 * rows
    step = total // 7
    chans = z.shape[2]
    squares = zeros8(chans)
    for c in range(7):
        values = mm(flat(xee[step * c : step * (c + 1)]), w[...])
        z[step * c : step * (c + 1)] = values.reshape(step, COLS, chans)
        parts = values.reshape(-1, 8, chans)
        squares = squares + jnp.sum(parts * parts, axis=0)
    ones = jnp.ones((8, total * COLS), BF16)
    stats[:, 0 : w.shape[0]] = mm(ones, flat(xee[...]))[0:1]
    stats[:, w.shape[0] :] = down(squares)


def scale_shift(got, labels, tab, norm, pixels, slot=0):
    label = entry(tab, OWN)
    total = group_sum(got, labels, label)
    chans = norm.shape[2]
    count = tiled(group_count(labels, label), chans) * pixels
    mean, rstd = moments(row(total, 2 * slot), row(total, 2 * slot + 1), count)
    gain, shift = gain_of(norm, entry(tab, OWN)), shift_of(norm, entry(tab, OWN))
    return mean, rstd, gain, shift, count


def conv_stats(z, source, pair, single, send, extra=()):
    keep = valid_cols(LANES)[None]
    rows = z.shape[0]
    step = rows // 4
    (lanes_2, w_2, offsets), (lanes_1, w_1, offset) = pair, single
    sums, squares = zeros8(LANES), zeros8(LANES)
    base = min(offsets)
    for c in range(4):
        at = step * c
        both = mm(flat(source[at + base : at + base + step + 1, :, lanes_2]), w_2)
        values = mm(flat(source[at + offset : at + offset + step, :, lanes_1]), w_1)
        for k, own in enumerate(offsets):
            skip = COLS * (own - base)
            values = values + both[skip : skip + step * COLS, LANES * k : LANES * (k + 1)]
        values = jnp.where(keep, values.reshape(step, COLS, LANES), 0.0)
        z[at : at + step] = values
        parts = values.reshape(-1, 8, LANES)
        sums = sums + jnp.sum(parts, axis=0)
        squares = squares + jnp.sum(parts * parts, axis=0)
    spread(send, [down(sums), down(squares), *extra])


def f2(
    tab, got, z_own, x_oth, w, norm, w_even, w_odd, stats_p,
    xs, z, send, labels, keeps, keeps_all, z_oth,
):
    codes = got[:, :, 4 * LANES : 5 * LANES]
    others = jnp.floor(0.25 * codes)
    marks = codes - 4.0 * others
    labels[...] = marks
    rows = xs.shape[0] - 1
    pixels = 4.0 * rows * (COLS - 4)
    first_project(x_oth, w, z_oth, False)
    for g in range(norm.shape[0]):
        mine, theirs = (marks == float(g)).astype(F32), (others == float(g)).astype(F32)
        totals = [
            jnp.sum(
                got[:, :, LANES * s : LANES * (s + 1)] * mine
                + got[:, :, LANES * (s + 2) : LANES * (s + 3)] * theirs,
                axis=0,
            )
            for s in (0, 1)
        ]
        mean, rstd = moments(*totals, group_count(marks, float(g)) * pixels)
        keeps_all[2 * g : 2 * g + 1, :] = mean
        keeps_all[2 * g + 1 : 2 * g + 2, :] = rstd
    for k, slot in enumerate((OWN, OTHER)):
        for q in (0, 1):
            choices = [keeps_all[2 * g + q : 2 * g + q + 1, :] for g in range(norm.shape[0])]
            keeps[2 * k + q : 2 * k + q + 1, :] = own_of(choices, entry(tab, slot))
    mean, rstd = keeps[0:1, :], keeps[1:2, :]
    gain, shift = gain_of(norm, entry(tab, OWN)), shift_of(norm, entry(tab, OWN))
    scale = rstd * gain
    bias = 0.5 * (shift - mean * scale)
    scale = 0.5 * scale
    keep = valid_cols(LANES) & chan_mask(tab)
    half = half_of(tab)
    xs[0] = jnp.zeros(xs.shape[1:], BF16)
    n = LANES
    for k, zz in enumerate((z_own, z_oth)):
        first = 1 + (rows // 2) * (half if k == 0 else 1 - half)

        def put(i, carry, zz=zz, first=first):
            lane = 0
            for a in (0, 1):
                for b in (0, 1):
                    u = zz[2 * i + a, pl.ds(b, COLS, stride=2), :] * scale + bias
                    act = jnp.where(keep, silu_of_half(u), 0.0)
                    xs[first + i, :, lane : lane + n] = act.astype(BF16)
                    lane += n
                    if b == 1:
                        moved = pltpu.roll(act, 1, 0)
                        xs[first + i, :, lane : lane + n] = moved.astype(BF16)
                        lane += n
            return carry

        lax.fori_loop(0, rows // 2, put, 0, unroll=2)
    extra = [stats_p[:, lanes] for lanes in columns(stats_p.shape[1])]
    pair = (slice(3 * n, 6 * n), w_odd[...], (1, 0))
    conv_stats(z, xs, pair, (slice(0, 3 * n), w_even[...], 1), send, extra)


def expand(act, w, z, send, act_sum):
    rows, chans = z.shape[0], z.shape[2]
    step = rows // 7
    squares = zeros8(chans)
    for c in range(7):
        values = mm(flat(act[step * c : step * (c + 1)]), w[...])
        z[step * c : step * (c + 1)] = values.reshape(step, COLS, chans)
        parts = values.reshape(-1, 8, chans)
        squares = squares + jnp.sum(parts * parts, axis=0)
    squares = down(squares)
    spread(send, [act_sum, *(squares[:, lanes] for lanes in columns(chans))])


def join(pieces):
    return pieces[0] if len(pieces) == 1 else jnp.concatenate(pieces, axis=1)


def columns(channels):
    return [slice(LANES * j, LANES * (j + 1)) for j in range(channels // LANES)]


def through(sums, w):
    high = sums.astype(BF16)
    rest = sums - high.astype(F32)
    mid = rest.astype(BF16)
    low = (rest - mid.astype(F32)).astype(BF16)
    lines = [v.astype(F32) for v in (high, mid, low)]
    lines.append(jnp.zeros((5, sums.shape[1]), F32))
    return down(mm(jnp.concatenate(lines, axis=0).astype(BF16), w))


def through_nt(sums, w):
    high = sums.astype(BF16)
    rest = sums - high.astype(F32)
    mid = rest.astype(BF16)
    low = (rest - mid.astype(F32)).astype(BF16)
    lines = [v.astype(F32) for v in (high, mid, low)]
    lines.append(jnp.zeros((5, sums.shape[1]), F32))
    return down(mm_nt(jnp.concatenate(lines, axis=0).astype(BF16), w))


def put_split(send, at, values):
    rows = values.shape[0]
    high = values.astype(BF16)
    rest = (values - high.astype(F32)).astype(BF16)
    for k, part in enumerate((high, rest)):
        send[:, at + rows * k : at + rows * (k + 1), :] = jnp.broadcast_to(
            part[None], (send.shape[0], rows, LANES)
        )


def get_split(got, at, rows):
    return got[:, at : at + rows, :].astype(F32) + got[:, at + rows : at + 2 * rows, :].astype(F32)


def over_group(values, marks, label):
    return jnp.sum(values * (marks == label).astype(F32), axis=0)


def stack(rows):
    return jnp.concatenate(rows, axis=0)


def pair_products(tab, z, norm, keeps, act, act_sum, slope, both, centred):
    rows = z.shape[0]
    label = entry(tab, OWN)
    mean, rstd = keeps[0:1, :], keeps[1:2, :]
    scale = rstd * gain_of(norm, label)
    bias = 0.5 * (shift_of(norm, label) - mean * scale)
    scale = 0.5 * scale
    keep = valid_cols(LANES) & chan_mask(tab)
    middle = act_sum * (1.0 / (rows * (COLS - 4)))

    def put(i, carry):
        zz = z[i]
        s = jnp.where(keep, slope_of_half(zz * scale + bias), 0.0)
        sx = s * ((zz - mean) * rstd)
        slope[i] = s
        both[i, :, 0:LANES] = s.astype(BF16)
        both[i, :, LANES:] = sx.astype(BF16)
        centred[i] = (act[i].astype(F32) - middle).astype(BF16)
        return carry[0] + fold(s), carry[1] + fold(sx)

    sums = lax.fori_loop(0, rows, put, (zeros8(LANES), zeros8(LANES)), unroll=4)
    return mm_tn(flat(centred[...]), flat(both[...])), stack([down(v) for v in sums])


def put_pair(send, at, share, product, sums):
    devices, n = send.shape[0], LANES
    missing = devices * share - n
    for h in (0, 1):
        values = product[:, n * h : n * (h + 1)]
        if missing:
            values = stack([values, jnp.zeros((missing, n), F32)])
        first = at + share * h
        send[:, first : first + share, :] = values.reshape(devices, share, n).astype(BF16)
    put_split(send, at + 2 * share, sums)


def pass_pair(send, at, got, got_at, share, marks, groups):
    rows = got[:, got_at : got_at + 2 * share, :].astype(F32)
    out = None
    for g in range(groups):
        same = (marks == float(g)).astype(F32)
        term = jnp.sum(rows * same, axis=0)[None] * same
        out = term if out is None else out + term
    send[:, at : at + 2 * share, :] = out.astype(BF16)


def pair_solve(tab, marks, outer, inner, sums, w, act_sums, q_rows, p_rows, pixels):
    label, n = entry(tab, OWN), LANES
    (norm_o, keeps_o), (norm_i, keeps_i) = outer, inner
    shift_o, gain_o, shift_i, gain_i = sums
    images = group_count(marks, label)
    count, count_o = images * pixels, tiled(images, norm_o.shape[2]) * pixels
    rstd_o = keeps_o[1:2, :]
    a_o = rstd_o * gain_of(norm_o, label)
    b_o, c_o = -(a_o * rstd_o) * gain_o / count_o, -a_o * shift_o / count_o
    m = mm_nt((w[...].astype(F32) * b_o).astype(BF16), w[...]).astype(BF16)
    e = through_nt(c_o, w[...])
    same = (marks == label).astype(F32)
    middle = jnp.sum(act_sums * same, axis=0) / count
    spread_out = ((act_sums * (1.0 / pixels) - middle[None]) * same).reshape(-1, n).astype(BF16)
    share = p_rows.shape[1] // 2
    found = []
    for h, start in enumerate((shift_i, gain_i)):
        q = q_rows[:, h : h + 1, :]
        p = p_rows[:, share * h : share * (h + 1), :].reshape(-1, n)[0:n]
        p = p + mm_tn(spread_out, q.reshape(-1, n).astype(BF16))
        found.append(start + down(m.astype(F32) * p) + e * jnp.sum(q * same, axis=0))
    rstd_i = keeps_i[1:2, :]
    a = rstd_i * gain_of(norm_i, label)
    coefs = a, -(a * rstd_i) * found[1] / count, -a * found[0] / count
    return m, e - through(middle, m), coefs, found


def expanded_moments(got, labels, tab, w, pixels):
    label = entry(tab, OWN)
    total = group_sum(got, labels, label)
    chans = w.shape[1]
    count = tiled(group_count(labels, label), chans) * pixels
    return moments(through(total[:, 0:LANES], w[...]), total[:, LANES:], count)


def activate(tab, got, labels, z_in, norm, act, keeps):
    got = got.at[:, :, 0 : 2 * LANES]
    rows = z_in.shape[0]
    pixels = 1.0 * rows * (COLS - 4)
    mean, rstd, gain, shift, _ = scale_shift(got, labels[...], tab, norm, pixels)
    keeps[0:1, :] = mean
    keeps[1:2, :] = rstd
    scale = rstd * gain
    bias = 0.5 * (shift - mean * scale)
    scale = 0.5 * scale
    keep = valid_cols(LANES) & chan_mask(tab)

    def put(i, sums):
        low = jnp.where(keep, silu_of_half(z_in[i] * scale + bias), 0.0).astype(BF16)
        act[i] = low
        return sums + fold(low.astype(F32))

    return down(lax.fori_loop(0, rows, put, zeros8(LANES), unroll=7))


def f3(tab, got, labels, z_in, norm, w, w_p, act, z, send, keeps, keeps_p, act_sum):
    sums = activate(tab, got, labels, z_in, norm, act, keeps)
    act_sum[...] = sums
    expand(act, w, z, send, sums)
    marks, label = labels[...], entry(tab, OWN)
    total = group_sum(got, marks, label)
    outer, first = z.shape[2], 2 * LANES
    second = first + w_p.shape[0]
    count = tiled(group_count(marks, label), outer) * (1.0 * z.shape[0] * (COLS - 4))
    mean, rstd = moments(through(total[:, first:second], w_p[...]), total[:, second:], count)
    keeps_p[0:1, :] = mean
    keeps_p[1:2, :] = rstd


def f4(tab, got, labels, zc, zp, norm_c, norm_p, keeps_p, w_c, w, joined, slope, z, stats, keeps):
    rows, chans = zc.shape[0], zc.shape[2]
    pixels = 1.0 * rows * (COLS - 4)
    mean_c, rstd_c = expanded_moments(got, labels[...], tab, w_c, pixels)
    mean_p, rstd_p = keeps_p[0:1, :], keeps_p[1:2, :]
    for k, v in enumerate((mean_c, rstd_c, mean_p, rstd_p)):
        keeps[k : k + 1, :] = v
    group = entry(tab, OWN)
    scale_c = rstd_c * gain_of(norm_c, group)
    scale_p = rstd_p * gain_of(norm_p, group)
    bias = (shift_of(norm_c, group) - mean_c * scale_c) + (
        shift_of(norm_p, group) - mean_p * scale_p
    )
    keep = valid_cols(chans)
    scale_c, scale_p, bias = 0.5 * scale_c, 0.5 * scale_p, 0.5 * bias

    def put(i, carry):
        u = zc[i] * scale_c + zp[i] * scale_p + bias
        t = jnp.tanh(u)
        p = u * t
        joined[i] = jnp.where(keep, u + p, 0.0).astype(BF16)
        slope[i] = (0.5 + 0.5 * t) * (1.0 + u - p)
        return carry

    lax.fori_loop(0, rows, put, 0, unroll=4)
    step = rows // 4
    sums, squares = zeros8(LANES), zeros8(LANES)
    for c in range(4):
        values = mm(flat(joined[step * c : step * (c + 1)]), w[...])
        z[step * c : step * (c + 1)] = values.reshape(step, COLS, LANES)
        parts = values.reshape(-1, 8, LANES)
        sums = sums + jnp.sum(parts, axis=0)
        squares = squares + jnp.sum(parts * parts, axis=0)
    stats[0:1, :] = down(sums)
    stats[1:2, :] = down(squares)


def pair_1(tab, stats, z, norm, keeps, act, act_sum, send, slope, both, centred, *, share):
    product, sums = pair_products(tab, z, norm, keeps, act, act_sum[...], slope, both, centred)
    put_split(send, 0, stats[...])
    put_pair(send, 4, share, product, sums)


def put_shares(xz, send, part):
    n, devices = LANES, send.shape[0]
    share = xz.shape[0] // devices
    pieces = xz[...].reshape(devices, share, n)
    first = (share + 1) // 2 * part
    for q in range(first, (share + 1) // 2 if part == 0 else share):
        at = n * (2 + q - first)
        send[:, :, at : at + n] = pieces[:, q : q + 1, :]


def f5(tab, got, labels, z_in, norm, w_two, w_last, xz, x3, z, send, keeps):
    rows = z_in.shape[0]
    pixels = 1.0 * rows * (COLS - 4)
    marks, label = labels[...], entry(tab, OWN)
    total = over_group(get_split(got, 0, 2), marks, label)
    mean, rstd = moments(total[0:1], total[1:2], group_count(marks, label) * pixels)
    gain, shift = gain_of(norm, label), shift_of(norm, label)
    keeps[0:1, :] = mean
    keeps[1:2, :] = rstd
    scale = rstd * gain
    bias = 0.5 * (shift - mean * scale)
    scale = 0.5 * scale
    keep = valid_cols(LANES) & chan_mask(tab)
    x3[0] = jnp.zeros(x3.shape[1:], BF16)
    x3[rows + 1] = jnp.zeros(x3.shape[1:], BF16)
    n = LANES

    def put(i, carry):
        act = jnp.where(keep, silu_of_half(z_in[i] * scale + bias), 0.0)
        x3[i + 1, :, 0:n] = pltpu.roll(act, 1, 0).astype(BF16)
        x3[i + 1, :, n : 2 * n] = act.astype(BF16)
        x3[i + 1, :, 2 * n : 3 * n] = pltpu.roll(act, COLS - 1, 0).astype(BF16)
        return carry

    lax.fori_loop(0, rows, put, 0, unroll=2)
    lanes = slice(0, 3 * n)
    conv_stats(
        z, x3, (lanes, w_two[...], (0, 1)), (lanes, w_last[...], 2), send.at[:, :, 0 : 2 * n]
    )
    put_shares(xz, send, 0)


def f6(tab, got, labels, z_in, norm, w, act, z, send, keeps):
    sums = activate(tab, got, labels, z_in, norm, act, keeps)
    expand(act, w, z, send, sums)


def b7(tab, got, labels, joined, z, norm, w, cot, result, grad_pre, send, keeps, wide):
    rows, chans = z.shape[0], z.shape[2]
    cols = COLS - 4
    pixels = 1.0 * rows * cols
    mean, rstd = expanded_moments(got, labels[...], tab, w, pixels)
    gain, shift = gain_of(norm, entry(tab, OWN)), shift_of(norm, entry(tab, OWN))
    keeps[0:1, :] = mean
    keeps[1:2, :] = rstd
    gate = 0.25 * tiled(entry(tab, GATE), chans)
    scale = 0.5 * rstd * gain * gate
    bias = 0.5 * (shift - mean * rstd * gain) * gate
    wide[...] = jnp.zeros(wide.shape, F32)

    def put(i, carry):
        sums, products = carry
        wide[0:cols, :] = cot[i].astype(F32)
        zz = z[i]
        u = 0.5 * joined[i].astype(F32) + zz * scale + bias
        t = jnp.tanh(u)
        p = u * t
        result[i] = (u + p)[0:cols].astype(BF16)
        g = wide[...] * ((0.5 + 0.5 * t) * (1.0 + u - p))
        grad_pre[i] = g
        return sums + fold(g), products + fold(g * (zz - mean))

    start = zeros8(chans)
    sums, products = lax.fori_loop(0, rows, put, (start, start), unroll=2)
    spread(send, [down(sums) * gate, down(products) * rstd * gate])


def lane_sums(got, marks, channels):
    def sums_of(g):
        total = group_sum(got, marks, float(g))
        return row(total, 0), row(total, 1)

    return sums_of


def row_sums(got, marks):
    def sums_of(g):
        total = over_group(get_split(got, 0, 2), marks, float(g))
        return total[0:1], total[1:2]

    return sums_of


def backward_norm(tab, sums_of, marks, norm, keeps, pixels, grad_norm):
    group, chans = entry(tab, OWN), norm.shape[2]
    sums = [sums_of(g) for g in range(norm.shape[0])]
    for g, (shift_sum, gain_sum) in enumerate(sums):
        grad_norm[g, 0:1, :] = gain_sum
        grad_norm[g, 1:2, :] = shift_sum
    count = tiled(group_count(marks, group), chans) * pixels
    own_shift, own_gain = (own_of([v[k] for v in sums], group) for k in (0, 1))
    mean, rstd = keeps[0:1, :], keeps[1:2, :]
    a = rstd * gain_of(norm, group)
    return mean, a, -(a * rstd) * own_gain / count, -a * own_shift / count


def slope_sums(tab, d, z_in, norm, keeps, dout):
    rows = z_in.shape[0]
    mean, rstd = keeps[0:1, :], keeps[1:2, :]
    group = entry(tab, OWN)
    scale = rstd * gain_of(norm, group)
    bias = 0.5 * (shift_of(norm, group) - mean * scale)
    scale = 0.5 * scale
    keep = valid_cols(LANES) & chan_mask(tab)

    def put(i, carry):
        sums, products = carry
        zz = z_in[i]
        g = jnp.where(keep, d[i] * slope_of_half(zz * scale + bias), 0.0)
        dout[i] = g
        return sums + fold(g), products + fold(g * (zz - mean))

    sums, products = lax.fori_loop(
        0, rows, put, (zeros8(LANES), zeros8(LANES)), unroll=4
    )
    return down(sums), down(products) * rstd


def b8(
    tab, got, labels, grad_pre, z, norm, keeps, w, z_in, norm_in, keeps_in, xz,
    dz, dout, send, grad_norm, d,
):
    rows, chans = z.shape[0], z.shape[2]
    pixels = 1.0 * rows * (COLS - 4)
    marks = labels[...]
    sums_of = lane_sums(got, marks, chans)
    mean, a, b, c = backward_norm(tab, sums_of, marks, norm, keeps, pixels, grad_norm)
    a = a * (0.25 * tiled(entry(tab, GATE), norm.shape[2]))
    keep = valid_cols(chans)

    def put(i, carry):
        v = a * grad_pre[i] + b * (z[i] - mean) + c
        dz[i] = jnp.where(keep, v, 0.0).astype(BF16)
        return carry

    lax.fori_loop(0, rows, put, 0, unroll=2)
    d[...] = mm_nt(flat(dz[...]), w[...]).reshape(d.shape)
    sums = slope_sums(tab, d, z_in, norm_in, keeps_in, dout)
    spread(send.at[:, :, 0 : 2 * LANES], sums)
    put_shares(xz, send, 1)


def b9(
    tab, got, labels, dout_in, z, norm, keeps, b_two, b_last, z_in, norm_in, keeps_in, x_sum, pair_got,
    dz, dout, send, grad_norm, d3, d, *, share,
):
    rows = z.shape[0]
    pixels = 1.0 * rows * (COLS - 4)
    marks = labels[...]
    sums_of = lane_sums(got.at[:, :, 0 : 2 * LANES], marks, LANES)
    mean, a, b, c = backward_norm(tab, sums_of, marks, norm, keeps, pixels, grad_norm)
    keep = valid_cols(LANES)
    n = LANES
    d3[0] = jnp.zeros(d3.shape[1:], BF16)
    d3[rows + 1] = jnp.zeros(d3.shape[1:], BF16)

    def put(i, carry):
        v = a * dout_in[i] + b * (z[i] - mean) + c
        v = jnp.where(keep, v, 0.0)
        d3[i + 1, :, 0:n] = pltpu.roll(v, COLS - 1, 0).astype(BF16)
        low = v.astype(BF16)
        d3[i + 1, :, n : 2 * n] = low
        dz[i] = low
        d3[i + 1, :, 2 * n : 3 * n] = pltpu.roll(v, 1, 0).astype(BF16)
        return carry

    lax.fori_loop(0, rows, put, 0, unroll=2)
    step = rows // 4
    for k in range(4):
        both = mm_nt(flat(d3[step * k : step * (k + 1) + 1]), b_two[...])
        value = mm_nt(flat(d3[step * k + 2 : step * (k + 1) + 2]), b_last[...])
        value = value + both[COLS:, 0:n] + both[0 : step * COLS, n : 2 * n]
        d[step * k : step * (k + 1)] = value.reshape(step, COLS, LANES)
    put_split(send, 0, stack(slope_sums(tab, d, z_in, norm_in, keeps_in, dout)))
    blocks = columns(x_sum.shape[0])
    put_split(send, 4, stack([jnp.transpose(x_sum[lanes, :])[0:1] for lanes in blocks]))
    pass_pair(send, 4 + 2 * len(blocks), pair_got, 4, share, marks, norm.shape[0])


def b10(
    tab, got, labels, dout_in, z, norm, keeps, w, grad_pre, slope, zc, zp, keeps_cp,
    norm_c, w_c, slope_in, z_in, keeps_in,
    dz, grad_pre_2, send, grad_norm, d_in, d, low,
):
    rows, chans = zc.shape[0], zc.shape[2]
    pixels = 1.0 * rows * (COLS - 4)
    marks = labels[...]
    coefs = backward_norm(tab, row_sums(got, marks), marks, norm, keeps, pixels, grad_norm)
    normed_grad(dz, dout_in, z, *coefs)
    d[...] = mm_nt(flat(dz[...]), w[...]).reshape(d.shape)
    mean_c, rstd_c, mean_p, rstd_p = (keeps_cp[k : k + 1, :] for k in range(4))
    a_c = rstd_c * gain_of(norm_c, entry(tab, OWN))

    def sum_up(i, carry):
        sums, prod_c, prod_p = carry
        g = (grad_pre[i] + d[i]).astype(BF16).astype(F32) * slope[i]
        grad_pre_2[i] = g
        low[i] = (a_c * g).astype(BF16)
        return (
            sums + fold(g),
            prod_c + fold(g * (zc[i] - mean_c)),
            prod_p + fold(g * (zp[i] - mean_p)),
        )

    start = zeros8(chans)
    sums, prod_c, prod_p = lax.fori_loop(0, rows, sum_up, (start, start, start), unroll=2)
    wide = [down(sums), down(prod_c) * rstd_c, down(prod_p) * rstd_p]
    inner = inner_sums(low, w_c, slope_in, z_in, keeps_in, d_in)
    parts = [stack([v[:, 0 : chans // 2], v[:, chans // 2 :]]) for v in wide]
    values = join([*parts, stack(inner)])
    send[...] = jnp.broadcast_to(values[None], send.shape)


def inner_sums(low, w, slope, z, keeps, d_in):
    d_in[...] = mm_nt(flat(low[...]), w[...]).reshape(d_in.shape)
    mean, rstd = keeps[0:1, :], keeps[1:2, :]

    def add(i, carry):
        g = slope[i] * d_in[i]
        return carry[0] + fold(g), carry[1] + fold(g * (z[i] - mean))

    sums = lax.fori_loop(0, z.shape[0], add, (zeros8(LANES), zeros8(LANES)), unroll=7)
    return down(sums[0]), down(sums[1]) * rstd


def inner_grad(act, m, line, slope, d_in, d):
    d[...] = mm(flat(act[...]), m).reshape(d.shape)

    def put(i, carry):
        d[i] = slope[i] * (d_in[i] + d[i] + line)
        return carry

    lax.fori_loop(0, d.shape[0], put, 0, unroll=7)


def normed_grad(dz, dout, z, mean, a, b, c):
    keep = valid_cols(z.shape[2])

    def put(i, carry):
        v = a * dout[i] + b * (z[i] - mean) + c
        dz[i] = jnp.where(keep, v, 0.0).astype(BF16)
        return carry

    lax.fori_loop(0, z.shape[0], put, 0, unroll=2)


def b12(
    tab, own10, labels, norm_c, keeps_c, w_c, got_act, got_q, got_p, act, slope, d_in,
    z, norm, keeps, xs, d2, kept, sent, own_sums, dz, packed, dout, *, share, q_at, p_at,
):
    rows = z.shape[0]
    pixels = 1.0 * rows * (COLS - 4)
    outer, n = norm_c.shape[2], LANES
    marks = labels[...]
    total = own10[...]
    cuts = (0, outer, 2 * outer, 2 * outer + n, 2 * outer + 2 * n)
    m, line, (a, b, c), found = pair_solve(
        tab, marks, (norm_c, keeps_c.at[0:2]), (norm, keeps),
        [total[:, u:v] for u, v in zip(cuts, cuts[1:])], w_c, got_act[:, :, 0:n],
        get_split(got_q, q_at, 2), got_p[:, p_at : p_at + 2 * share, :].astype(F32), pixels,
    )
    own_sums[0:1, :] = found[0]
    own_sums[1:2, :] = found[1]
    inner_grad(act, m, line, slope, d_in, dout)
    mean = keeps[0:1, :]
    keep = valid_cols(LANES)
    d2[rows] = jnp.zeros(d2.shape[1:], BF16)

    def put(i, carry):
        v = a * dout[i] + b * (z[i] - mean) + c
        v = jnp.where(keep, v, 0.0)
        low = v.astype(BF16)
        dz[i] = low
        d2[i, :, 0:n] = low
        d2[i, :, n : 2 * n] = pltpu.roll(v, COLS - 1, 0).astype(BF16)
        return carry

    lax.fori_loop(0, rows, put, 0, unroll=4)
    low = flat(dz[...])
    cur = mm_side(flat(xs[1 : rows + 1]), low)
    for k, (y, x) in enumerate(((1, 1), (1, 2), (1, 0), (2, 1), (2, 2), (2, 0))):
        put_rows(packed, n * (3 * y + x), cur[n * k : n * (k + 1)])
    up = mm_side(flat(xs[0:rows, :, 3 * n : 6 * n]), low)
    for k, (y, x) in enumerate(((0, 1), (0, 2), (0, 0))):
        put_rows(packed, n * (3 * y + x), up[n * k : n * (k + 1)])
    share_out(tab, packed, 9 * n, kept, sent)


def b12_images(
    tab, d2, b_even, b_odd, zz, norm_in, keeps_in, dn, sums_out, de, do, wide, *, own
):
    rows = de.shape[0]
    n = LANES
    half = half_of(tab)
    first = rows * (half if own else 1 - half)
    step = rows // 2
    for k in range(2):
        here = flat(d2[pl.ds(first + step * k, step)])
        below = flat(d2[pl.ds(first + step * k + 1, step)])
        de[step * k : step * (k + 1)] = mm_nt(here, b_even[...]).reshape(step, COLS, 2 * n)
        odd = mm_nt(here, b_odd[:, 0 : 2 * n]) + mm_nt(below, b_odd[:, 2 * n : 4 * n])
        do[step * k : step * (k + 1)] = odd.reshape(step, COLS, 2 * n)
    mean_1, rstd_1 = keeps_in[0:1, :], keeps_in[1:2, :]
    group = entry(tab, OWN)
    scale = rstd_1 * gain_of(norm_in, group)
    bias = 0.5 * (shift_of(norm_in, group) - mean_1 * scale)
    scale = 0.5 * scale
    keep = valid_cols(LANES) & chan_mask(tab)

    def emit(i, carry):
        sums, products = carry
        for ra in (0, 1):
            planes = (de, do)[ra]
            for cb in (0, 1):
                zv = zz[2 * i + ra, pl.ds(cb, COLS, stride=2), :]
                g = planes[i, :, n * cb : n * (cb + 1)] * slope_of_half(zv * scale + bias)
                g = jnp.where(keep, g, 0.0)
                sums = sums + fold(g)
                products = products + fold(g * (zv - mean_1))
                wide[ra, pl.ds(cb, COLS, stride=2), :] = g
            dn[2 * i + ra] = wide[ra].astype(BF16)
        return sums, products

    totals = lax.fori_loop(0, rows, emit, (zeros8(n), zeros8(n)), unroll=2)
    sums_out[0:1, :] = down(totals[0])
    sums_out[1:2, :] = down(totals[1]) * rstd_1


def b13(
    tab, got, labels, norm, keeps, w, z_own, z_for, dn_own, dn_for, gs_own, gs_for, *rest, at, held
):
    finished, outs = rest[:held], rest[held : 2 * held]
    grad, grad_norm, grad_inner, dz, wide, grad_v, norm_v, inner_v, sems = rest[2 * held :]
    copies = [
        pltpu.make_async_copy(a, b, sems.at[k]) for k, (a, b) in enumerate(zip(finished, outs))
    ]
    for copy in copies:
        copy.start()
    rows, cols = grad.shape[1], grad.shape[2]
    half = half_of(tab)
    pixels = 2.0 * rows * cols
    marks = labels[...]
    totals = last_sums(got.at[:, at : at + 4, :], marks, norm.shape[0])
    for g in range(norm.shape[0]):
        norm_v[g, 0:1, :] = totals[g][1]
        norm_v[g, 1:2, :] = totals[g][0]
    found = get_split(got, at + 4, 2)
    for g in range(norm.shape[0]):
        total = over_group(found, marks, float(g)) / group_count(marks, float(g))
        inner_v[g, 0:1, :] = total[1:2]
        inner_v[g, 1:2, :] = total[0:1]
    for k, (value, out) in enumerate(((norm_v, grad_norm), (inner_v, grad_inner))):
        copies.append(pltpu.make_async_copy(value, out, sems.at[held + k]))
        copies[-1].start()
    keep = lax.broadcasted_iota(jnp.int32, (z_own.shape[1], LANES), 0) < cols
    for k, (z, dn, gs) in enumerate(((z_own, dn_own, gs_own), (z_for, dn_for, gs_for))):
        group = entry(tab, OWN if k == 0 else OTHER)
        shift_sum = own_of([t[0] for t in totals], group)
        gain_sum = own_of([t[1] for t in totals], group)
        count = group_count(marks, group) * pixels
        mean, rstd = keeps[2 * k : 2 * k + 1, :], keeps[2 * k + 1 : 2 * k + 2, :]
        a = rstd * gain_of(norm, group)
        b = -(a * rstd) * gain_sum / count
        c = -a * shift_sum / count

        def put(i, carry, z=z, dn=dn, mean=mean, a=a, b=b, c=c):
            v = a * dn[i].astype(F32) + b * (z[i] - mean) + c
            dz[i] = jnp.where(keep, v, 0.0).astype(BF16)
            return carry

        lax.fori_loop(0, rows, put, 0, unroll=4)
        place = half if k == 0 else 1 - half
        step = rows // 2
        for q in range(2):
            low = flat(dz[step * q : step * (q + 1)])
            for p in range(wide.shape[0]):
                values = mm_nt(low, w[LANES * p : LANES * (p + 1), :])
                wide[p, step * q : step * (q + 1)] = values.reshape(step, -1, LANES)

            def emit(i, carry, gs=gs, place=place):
                even = pl.ds(0, COLS, stride=2)
                for p in range(wide.shape[0]):
                    lanes = slice(LANES * p, LANES * (p + 1))
                    wide[p, 2 * i, even, :] = wide[p, 2 * i, even, :] + gs[i, :, lanes].astype(F32)
                    grad_v[place, 2 * i, :, lanes] = wide[p, 2 * i, 0:cols, :].astype(BF16)
                    grad_v[place, 2 * i + 1, :, lanes] = wide[p, 2 * i + 1, 0:cols, :].astype(BF16)
                return carry

            lax.fori_loop(step // 2 * q, step // 2 * (q + 1), emit, 0, unroll=True)
            part = pl.ds(step * q, step)
            copies.append(
                pltpu.make_async_copy(
                    grad_v.at[place, part], grad.at[place, part], sems.at[held + 2 + 2 * k + q]
                )
            )
            copies[-1].start()
    for copy in copies:
        copy.wait()


def put_rows(out, at, value):
    for j in range(value.shape[1] // LANES):
        out[at : at + value.shape[0], :] = value[:, LANES * j : LANES * (j + 1)].astype(BF16)
        at += value.shape[0]
    return at


def take_rows(source, at, out):
    rows = out.shape[0]
    for j in range(out.shape[1] // LANES):
        out[:, LANES * j : LANES * (j + 1)] = source(at, rows)
        at += rows
    return at


def share_out(tab, packed, used, kept, sent):
    if used < packed.shape[0]:
        packed[used:, :] = jnp.zeros((packed.shape[0] - used, LANES), BF16)
    half = half_of(tab)
    size = kept.shape[0] * kept.shape[1]
    for out, place in ((kept, half), (sent, 1 - half)):
        out[...] = packed[pl.ds(pl.multiple_of(size * place, 16), size), :].reshape(out.shape)


def g_most(
    tab, act_2b, dz_2c, x3, dz_2b, joined, dz_2a, act_1b, xee, w_p,
    got, labels, norm_c, norm_p, keeps, grad_pre_2, zc, zp,
    kept, sent, gs_own, gs_oth, grad_norm_c, grad_norm_p, own10, packed, dz_1c, dz_p,
):
    rows, outer = dz_2b.shape[0], zc.shape[2]
    pixels = 1.0 * rows * (COLS - 4)
    marks = labels[...]

    totals = [group_sum(got, marks, float(g)) for g in range(norm_c.shape[0])]
    side = outer // 2

    def line(total, k):
        return join([total[h : h + 1, side * k : side * (k + 1)] for h in (0, 1)])

    lines = [[line(total, k) for k in range(3)] for total in totals]
    label = entry(tab, OWN)
    for k in range(2):
        own10[:, outer * k : outer * (k + 1)] = own_of([v[k] for v in lines], label)
        inner = [total[k : k + 1, 3 * side :] for total in totals]
        at = 2 * outer + LANES * k
        own10[:, at : at + LANES] = own_of(inner, label)
    coefs = backward_norm(
        tab, lambda g: (lines[g][0], lines[g][1]), marks, norm_c, keeps.at[0:2], pixels, grad_norm_c
    )
    normed_grad(dz_1c, grad_pre_2, zc, *coefs)
    coefs = backward_norm(
        tab, lambda g: (lines[g][0], lines[g][2]), marks, norm_p, keeps.at[2:4], pixels, grad_norm_p
    )
    normed_grad(dz_p, grad_pre_2, zp, *coefs)
    at = put_rows(packed, 0, mm_tn(flat(act_2b[...]), flat(dz_2c[...])))
    low = flat(dz_2b[...])
    for y in range(3):
        at = put_rows(packed, at, mm_side(flat(x3[y : y + rows]), low))
    at = put_rows(packed, at, mm_side(flat(joined[...]), flat(dz_2a[...])))
    at = put_rows(packed, at, mm_tn(flat(act_1b[...]), flat(dz_1c[...])))
    at = put_rows(packed, at, mm_tn(flat(xee[...]), flat(dz_p[...])))
    share_out(tab, packed, at, kept, sent)
    half = half_of(tab)
    count = gs_own.shape[0]
    for k, gs in enumerate((gs_own, gs_oth)):
        first = count * (half if k == 0 else 1 - half)
        got = mm_nt(flat(dz_p[pl.ds(first, count)]), w_p[...])
        gs[...] = got.reshape(gs.shape).astype(BF16)


def g_xz(keeps, x_own, x_oth, z_own, z_oth, out, x_sum, low):
    rows, n = z_own.shape[0], LANES
    mean = keeps[0:1, :]
    low[:, :, n : 2 * n] = jnp.ones((rows, z_own.shape[1], n), BF16)
    value = None
    for x, z in ((x_own, z_own), (x_oth, z_oth)):

        def put(i, carry, z=z):
            low[i, :, 0:n] = (z[i] - mean).astype(BF16)
            return carry

        lax.fori_loop(0, rows, put, 0, unroll=4)
        term = mm_tn(flat(x[...]), flat(low[...]))
        value = term if value is None else value + term
    at = value.shape[0]
    out[0:at, :] = value[:, 0:n]
    if at < out.shape[0]:
        out[at:, :] = jnp.zeros((out.shape[0] - at, n), F32)
    x_sum[...] = value[:, n : 2 * n]


def g_xd(
    tab, sums_own, sums_oth, norm, keeps, x_sum, got_x, labels, x_own, x_oth, dn_own, dn_oth,
    out, sums, low,
):
    rows = dn_own.shape[0]
    n = LANES
    pixels = 1.0 * (2 * rows) * (2 * (COLS - 4))
    sums[...] = sums_own[...] + sums_oth[...]
    a = keeps[1:2, :] * gain_of(norm, entry(tab, OWN))
    local = sums[0:1, :] / pixels
    value = None
    for x, dn in ((x_own, dn_own), (x_oth, dn_oth)):

        def put(i, carry, dn=dn):
            low[i] = (a * (dn[i].astype(F32) - local)).astype(BF16)
            return carry

        lax.fori_loop(0, rows, put, 0, unroll=4)
        term = mm_tn(flat(x[...]), flat(low[...]))
        value = term if value is None else value + term
    marks, label = labels[...], entry(tab, OWN)
    total = over_group(get_split(got_x, 4, x_sum.shape[0] // n), marks, label)
    total = join([total[k : k + 1] for k in range(total.shape[0])])
    total = total / tiled(group_count(marks, label), total.shape[1])
    total = jnp.broadcast_to(total, (8, total.shape[1]))
    means = jnp.concatenate(
        [jnp.transpose(total[:, lanes])[:, 0:1] for lanes in columns(total.shape[1])], axis=0
    )
    value = value + (x_sum[...] - means) * (a * local)
    at = value.shape[0]
    out[0:at, :] = value.astype(BF16)
    if at < out.shape[0]:
        out[at:, :] = jnp.zeros((out.shape[0] - at, n), BF16)


def pack_last(tall, sums, found, kept, got, kept_1b, got_1b, send, *, stats_at):
    n = LANES
    devices = send.shape[0]
    piece, share = kept.shape[1], tall.shape[0] // devices
    first = kept.shape[0]
    second = first + kept_1b.shape[0]
    send[0:first, 0:piece, :] = (kept[...].astype(F32) + got[...].astype(F32)).astype(BF16)
    send[first:second, 0:piece, :] = (kept_1b[...].astype(F32) + got_1b[...].astype(F32)).astype(BF16)
    if second < devices:
        send[second:, 0:piece, :] = jnp.zeros((devices - second, piece, n), BF16)
    send[:, piece : piece + share, :] = tall[...].reshape(devices, share, n)
    put_split(send, stats_at, sums[...])
    put_split(send, stats_at + 4, found[...])


def last_sums(stats, marks, groups):
    values = stats[:, 0:2, :].astype(F32) + stats[:, 2:4, :].astype(F32)
    out = []
    for g in range(groups):
        total = jnp.sum(values * (marks == float(g)).astype(F32), axis=0)
        out.append((total[0:1], total[1:2]))
    return out


def add_all(got, labels, norm, keeps_all, got_a, got_b, out, *, at, pixels):
    devices, n = got.shape[0], LANES
    half = devices // 2
    split = got_a.shape[2] // n - 2
    share = split + got_b.shape[2] // n - 2
    piece = out.shape[1] - share
    marks = labels[...]
    value = jnp.sum(got[:, piece : piece + share, :].astype(F32), axis=0)
    sums = last_sums(got.at[:, at : at + 4, :], marks, norm.shape[0])
    for g in range(norm.shape[0]):
        rstd = keeps_all[2 * g + 1 : 2 * g + 2, :]
        count = group_count(marks, float(g)) * pixels
        b = -(rstd * rstd * norm[g, 0:1, :]) * sums[g][1] / count
        same = (marks == float(g)).astype(F32)
        rows = [
            jnp.sum(source[:, :, n * (2 + q) : n * (3 + q)] * same, axis=0)
            for source, count_q in ((got_a, split), (got_b, share - split))
            for q in range(count_q)
        ]
        value = value + jnp.concatenate(rows, axis=0) * b
    for k in (0, 1):
        total = jnp.sum(got[half * k : half * (k + 1), 0:piece, :].astype(F32), axis=0).astype(BF16)
        out[half * k : half * (k + 1), 0:piece, :] = jnp.broadcast_to(total[None], (half, piece, n))
    out[:, piece:, :] = jnp.broadcast_to(value.astype(BF16)[None], (devices, share, n))


def unpack(
    tab, own, other, o_1a, o_1b, o_2c, o_2b, o_2a, o_1c, o_1p,
    w_1a, w_1b, w_2c, w_2b, w_2a, w_1c, w_1p, tall, sems, *, first, second, piece,
):
    half = half_of(tab)
    copies = []

    def leave(value, out):
        copies.append(pltpu.make_async_copy(value, out, sems.at[len(copies)]))
        return copies[-1]

    weights = ((w_2c, o_2c), (w_2b, o_2b), (w_2a, o_2a), (w_1c, o_1c), (w_1p, o_1p))
    leaving = [leave(*v) for v in (*weights, (w_1b, o_1b), (w_1a, o_1a))]
    for place in (0, 1):

        @pl.when(half == place)
        def _():
            halves = (own, other) if place == 0 else (other, own)
            most = [flat(v[0:first, 0:piece, :]) for v in halves]
            last = [flat(v[first : first + second, 0:piece, :]) for v in halves]
            size = first * piece

            def source(at, rows):
                pieces = []
                if at < size:
                    pieces.append(most[0][at : min(at + rows, size)])
                if at + rows > size:
                    pieces.append(most[1][max(at - size, 0) : at + rows - size])
                pieces = [v.astype(F32) for v in pieces]
                return pieces[0] if len(pieces) == 1 else jnp.concatenate(pieces, axis=0)

            at = 0
            for k, (value, _) in enumerate(weights):
                at = take_rows(source, at, value)
                leaving[k].start()
            size = second * piece
            w_1b[0:size] = last[0].astype(F32)
            w_1b[size:] = last[1][0 : w_1b.shape[0] - size].astype(F32)
            leaving[5].start()

    tall[...] = own[:, piece:, :].astype(F32).reshape(tall.shape)
    w_1a[...] = tall[0 : w_1a.shape[0], :]
    leaving[6].start()
    for copy in copies:
        copy.wait()


def gather(send):
    return lax.all_to_all(send, AXES, 0, 0)


def tie(*values):
    return lax.optimization_barrier(values)


def swap(block):
    return lax.ppermute(block, "rows", [(0, 1), (1, 0)])


def body(
    images, w_1a, w_1b, w_1c, w_1p, w_2a, w_2b, w_2c,
    norm_1a, norm_1b, norm_1c, norm_1p, norm_2a, norm_2b, norm_2c,
    cotangent, group, width, gate,
):
    devices = lax.axis_size("rows") * lax.axis_size("batch")
    half = lax.axis_index("rows").astype(jnp.int32).reshape(1)
    norms = (norm_1a, norm_1b, norm_1c, norm_1p, norm_2a, norm_2b, norm_2c)
    norm_1a, norm_1b, norm_1c, norm_1p, norm_2a, norm_2b, norm_2c = (
        v.transpose(1, 0, 2) for v in norms
    )
    outer, inputs = w_1c.shape[1], w_1a.shape[0]
    rows = cotangent.shape[1]
    cols_in = 2 * COLS
    n, m = LANES, devices

    def send(stats, channels=LANES):
        return ((m, channels // LANES, stats * LANES), F32)

    def maps(channels, dtype=F32):
        return ((rows, COLS, channels), dtype)

    def scratch(channels, dtype=F32):
        return pltpu.VMEM((rows, COLS, channels), dtype)

    def params(*arrays):
        return [(a.shape, F32) for a in arrays]

    def mean_scale(channels, count=1):
        return ((2 * count, channels), F32)

    wide_in = ((rows, cols_in, inputs), BF16)
    wide_z = ((rows, cols_in, n), F32)
    raw = images.shape
    tab, x_own, x_for, z_own, z_for, s1 = stage(
        f1, [((8, n), F32), wide_in, wide_in, wide_z, wide_z, send(5)],
        [*(pltpu.SMEM(v.shape, jnp.int32) for v in (half, group, width, gate)),
         pltpu.VMEM(raw, BF16), pltpu.VMEM(w_1a.shape, BF16), pltpu.VMEM((8, n), F32),
         pltpu.SemaphoreType.DMA((7,))],
        hbm=(0, 1, 2, 3, 4, 5),
    )(half, group, width, gate, images, w_1a)
    s1, v_1b, v_2b = tie(s1, w_1b, w_2b)
    built = stage(
        prepare,
        [(v, BF16) for v in (
            (3 * n, n), (3 * n, 2 * n), (3 * n, 2 * n), (3 * n, n),
            (2 * n, 2 * n), (2 * n, 4 * n), (2 * n, 3 * n), (n, 3 * n),
        )],
    )(v_1b, v_2b)
    s1, x_for, w_even, w_odd, w_two, w_last, b_even, b_odd, b_two, b_last = tie(s1, x_for, *built)
    x_oth = swap(x_for)
    g1 = gather(s1)
    g1, x_oth = tie(g1, x_oth)
    xee, z_1p, stats_1p = stage(
        f1_strided,
        [maps(inputs, BF16), maps(outer), ((1, inputs + outer), F32)],
        [pltpu.VMEM((inputs // n, cols_in, n), F32)],
    )(tab, x_own, x_oth, w_1p)
    xs, z_1b, s2, labels, k_1a, k_all, z_oth = stage(
        f2,
        [((rows + 1, COLS, 6 * n), BF16), maps(n), send(2 + (inputs + outer) // n),
         ((m, 1, n), F32), mean_scale(n, 2), mean_scale(n, norm_1a.shape[0]), wide_z],
    )(tab, g1, z_own, x_oth, w_1a, norm_1a, w_even, w_odd, stats_1p)
    g2 = gather(s2)
    act_1b, z_1c, s3, k_1b, k_p, sum_1b = stage(
        f3,
        [maps(n, BF16), maps(outer), send(1 + outer // n), mean_scale(n), mean_scale(outer),
         ((1, n), F32)],
    )(tab, g2, labels, z_1b, norm_1b, w_1c, w_1p)
    g3 = gather(s3)
    joined, slope, z_2a, stats_2a, k_cp = stage(
        f4, [maps(outer, BF16), maps(outer), maps(n), ((2, n), F32), mean_scale(outer, 2)]
    )(tab, g3, labels, z_1c, z_1p, norm_1c, norm_1p, k_p, w_1c, w_2a)
    share = -(-inputs // devices)
    half_in = ((rows, cols_in, n), BF16)
    share_1 = -(-n // devices)
    high = -(-(8 + 2 * share_1) // 16) * 16
    s4, slope_1b = stage(
        functools.partial(pair_1, share=share_1), [((devices, high, n), BF16), maps(n)],
        [scratch(2 * n, BF16), scratch(n, BF16)],
    )(tab, stats_2a, z_1b, norm_1b, k_1b, act_1b, sum_1b)
    s4, k_1a = tie(s4, k_1a)
    xz, x_sum = stage(
        g_xz, [((devices * share, n), F32), ((inputs, n), F32)],
        [pltpu.VMEM((rows, cols_in, 2 * n), BF16)],
    )(k_1a, x_own, x_oth, z_own, z_oth)
    s4, xz, x_sum = tie(s4, xz, x_sum)
    g4 = gather(s4)
    x3, z_2b, s5, k_2a = stage(
        f5, [((rows + 2, COLS, 3 * n), BF16), maps(n), send(2 + (share + 1) // 2), mean_scale(n)]
    )(tab, g4, labels, z_2a, norm_2a, w_two, w_last, xz)
    g5 = gather(s5)
    act_2b, z_2c, s6, k_2b = stage(
        f6, [maps(n, BF16), maps(outer), send(1 + outer // n), mean_scale(n)]
    )(tab, g5, labels, z_2b, norm_2b, w_2c)
    g6 = gather(s6)
    result, grad_pre, s7, k_2c = stage(
        b7, [(cotangent.shape[1:], BF16), maps(outer), send(2, outer), mean_scale(outer)],
        [pltpu.VMEM((COLS, outer), F32)],
    )(tab, g6, labels, joined, z_2c, norm_2c, w_2c, cotangent[0])
    g7 = gather(s7)
    dz_2c, dout_2b, s8, grad_norm_2c = stage(
        b8, [maps(outer, BF16), maps(n), send(2 + share // 2), *params(norm_2c)], [scratch(n)]
    )(tab, g7, labels, grad_pre, z_2c, norm_2c, k_2c, w_2c, z_2b, norm_2b, k_2b, xz)
    g8 = gather(s8)
    dz_2b, dout_2a, s9, grad_norm_2b = stage(
        functools.partial(b9, share=share_1),
        [maps(n, BF16), maps(n), ((devices, high, n), BF16), *params(norm_2b)],
        [pltpu.VMEM((rows + 2, COLS, 3 * n), BF16), scratch(n)],
    )(tab, g8, labels, dout_2b, z_2b, norm_2b, k_2b, b_two, b_last, z_2a, norm_2a, k_2a, x_sum, g4)
    g9 = gather(s9)
    dz_2a, grad_pre_2, s10, grad_norm_2a, d_1b = stage(
        b10,
        [maps(n, BF16), maps(outer), ((devices, 2, 3 * outer // 2 + n), F32), *params(norm_2a), maps(n)],
        [scratch(outer), scratch(outer, BF16)],
    )(tab, g9, labels, dout_2a, z_2a, norm_2a, k_2a, w_2a, grad_pre, slope, z_1c, z_1p, k_cp,
      norm_1c, w_1c, slope_1b, z_1b, k_1b)
    g10 = gather(s10)
    half_map = ((rows // 2, COLS, inputs), BF16)
    most_rows = sum(v.size for v in (w_2c, w_2b, w_2a, w_1c, w_1p)) // n
    rows_1b = w_1b.size // n
    piece = 16
    while -(-most_rows // (2 * piece)) - (-rows_1b // (2 * piece)) > devices:
        piece += 16
    first, second = -(-most_rows // (2 * piece)), -(-rows_1b // (2 * piece))
    part, part_1b = ((first, piece, n), BF16), ((second, piece, n), BF16)
    kept, sent, gs_own, gs_send, grad_norm_1c, grad_norm_1p, own10 = stage(
        g_most,
        [part, part, half_map, half_map, *params(norm_1c, norm_1p), ((1, 2 * outer + 2 * n), F32)],
        [pltpu.VMEM((2 * first * piece, n), BF16), scratch(outer, BF16), scratch(outer, BF16)],
    )(tab, act_2b, dz_2c, x3, dz_2b, joined, dz_2a, act_1b, xee, w_1p,
      g10, labels, norm_1c, norm_1p, k_cp, grad_pre_2, z_1c, z_1p)
    got, gs_for = swap(sent), swap(gs_send)
    half_in = ((rows, cols_in, n), BF16)
    d2, kept_1b, sent_1b, found_1b = stage(
        functools.partial(b12, share=share_1, q_at=4 + 2 * share_1, p_at=4 + 2 * (inputs // n)),
        [((rows + 1, COLS, 2 * n), BF16), part_1b, part_1b, ((2, n), F32)],
        [scratch(n, BF16), pltpu.VMEM((2 * second * piece, n), BF16), scratch(n)],
    )(tab, own10, labels, norm_1c, k_cp, w_1c, g3, g4, g9, act_1b, slope_1b, d_1b,
      z_1b, norm_1b, k_1b, xs)
    got_1b = swap(sent_1b)
    sides = []
    for own, z in ((False, z_oth), (True, z_own)):
        sides.append(
            stage(
                functools.partial(b12_images, own=own), [half_in, ((2, n), F32)],
                [pltpu.VMEM((rows // 2, COLS, 2 * n), F32), pltpu.VMEM((rows // 2, COLS, 2 * n), F32),
                 pltpu.VMEM((2, cols_in, n), F32)],
            )(tab, d2, b_even, b_odd, z, norm_1a, k_1a)
        )
        if not own:
            dn_for = swap(sides[0][0])
            d2, _ = tie(d2, sides[0][0])
    (dn_send, sums_send), (dn_own, sums_own) = sides
    stats_at = piece + -(-share // 8) * 8
    high = -(-(stats_at + 8) // 16) * 16
    tall, sums_1a = stage(
        g_xd, [((devices * share, n), BF16), ((2, n), F32)], [pltpu.VMEM(half_in[0], BF16)]
    )(tab, sums_own, sums_send, norm_1a, k_1a, x_sum, g9, labels, x_own, x_oth, dn_own, dn_send)
    tall, gs_for, dn_for = tie(tall, gs_for, dn_for)
    (s12,) = stage(
        functools.partial(pack_last, stats_at=stats_at), [((devices, high, n), BF16)]
    )(tall, sums_1a, found_1b, kept, got, kept_1b, got_1b)
    g12 = gather(s12)
    pixels = 4.0 * images.shape[1] * images.shape[1]
    (mine,) = stage(
        functools.partial(add_all, at=stats_at, pixels=pixels),
        [((devices, piece + share, n), BF16)],
    )(g12, labels, norm_1a, k_all, g5, g8)
    finished = (
        result, grad_norm_1c, grad_norm_1p, grad_norm_2a, grad_norm_2b, grad_norm_2c
    )
    held = len(finished)
    *finished, grad_images, grad_norm_1a, grad_norm_1b = stage(
        functools.partial(b13, at=stats_at, held=held),
        [*((v.shape, v.dtype) for v in finished), (images.shape, BF16), *params(norm_1a, norm_1b)],
        [pltpu.VMEM(half_in[0], BF16), pltpu.VMEM((inputs // n, rows, cols_in, n), F32),
         pltpu.VMEM(images.shape, BF16), *(pltpu.VMEM(norm_1a.shape, F32) for _ in range(2)),
         pltpu.SemaphoreType.DMA((held + 6,))],
        hbm_out=range(held + 3),
    )(tab, g12, labels, norm_1a, k_1a, w_1a, z_own, z_for, dn_own, dn_for, gs_own, gs_for, *finished)
    result, grad_norm_1c, grad_norm_1p, grad_norm_2a, grad_norm_2b, grad_norm_2c = finished
    whole = gather(mine)
    weights = (w_1a, w_1b.reshape(-1, n), w_2c, w_2b.reshape(-1, n), w_2a, w_1c, w_1p)
    totals = stage(
        functools.partial(unpack, first=first, second=second, piece=piece),
        [(v.shape, F32) for v in weights],
        [*(pltpu.VMEM(v.shape, F32) for v in weights),
         pltpu.VMEM((devices * share, n), F32), pltpu.SemaphoreType.DMA((7,))],
        hbm_out=range(7),
    )(tab, whole, swap(whole))
    t_1a, t_1b, t_2c, t_2b, t_2a, t_1c, t_1p = totals
    grads = (
        grad_norm_1a, grad_norm_1b, grad_norm_1c, grad_norm_1p,
        grad_norm_2a, grad_norm_2b, grad_norm_2c,
    )
    return (
        result[None], grad_images, t_1a, t_1b.reshape(w_1b.shape), t_1c, t_1p, t_2a,
        t_2b.reshape(w_2b.shape), t_2c, *[v.transpose(1, 0, 2) for v in grads],
    )


def solution(mesh):
    return jax.shard_map(
        body,
        mesh=mesh,
        in_specs=(
            P("batch", "rows", None, None),
            *[P()] * 14,
            P(("batch", "rows"), None, None, None),
            P("batch"),
            P(),
            P(),
        ),
        out_specs=(
            P(("batch", "rows"), None, None, None),
            P("batch", "rows", None, None),
            *[P()] * 14,
        ),
        check_vma=False,
    )
```

```python
import functools

import jax
import jax.numpy as jnp
from jax import lax
from jax.experimental import pallas as pl
from jax.experimental.pallas import tpu as pltpu
from jax.sharding import PartitionSpec as P

EPSILON = 1e-05
F32 = jnp.float32
BF16 = jnp.bfloat16
AXES = ("rows", "batch")
VMEM_LIMIT = 14 * 1024 * 1024
LANES = 128
COLS = 32
NEAR = 4


def full(memory=pltpu.VMEM):
    return pl.BlockSpec(memory_space=memory)


def stage(kernel, outs, scratch=(), hbm=(), hbm_out=()):
    def place(i, outside):
        return pltpu.HBM if i in outside else pltpu.VMEM

    def call(*args):
        args = [
            pltpu.with_memory_space_constraint(a, pltpu.HBM) if i in hbm else a
            for i, a in enumerate(args)
        ]
        return pl.pallas_call(
            kernel,
            out_shape=tuple(jax.ShapeDtypeStruct(s, d) for s, d in outs),
            in_specs=[full(place(i, hbm)) for i in range(len(args))],
            out_specs=tuple(
                full(place(i, hbm_out)) for i in range(len(outs))
            ),
            scratch_shapes=list(scratch),
            compiler_params=pltpu.CompilerParams(vmem_limit_bytes=VMEM_LIMIT),
            name=(kernel.func if isinstance(kernel, functools.partial) else kernel).__name__,
        )(*args)

    return call


def silu_of_half(u):
    return u + u * jnp.tanh(u)


def slope_of_half(u):
    t = jnp.tanh(u)
    return (0.5 + 0.5 * t) * (1.0 + u - u * t)


def fold(x):
    return (x[0:8] + x[8:16]) + (x[16:24] + x[24:32])


def row(total, stat):
    blocks = total.shape[0]
    pieces = [total[j : j + 1, LANES * stat : LANES * (stat + 1)] for j in range(blocks)]
    return pieces[0] if blocks == 1 else jnp.concatenate(pieces, axis=1)


def spread(out_ref, rows):
    blocks = out_ref.shape[1]
    for stat, values in enumerate(rows):
        for j in range(blocks):
            piece = values[:, LANES * j : LANES * (j + 1)]
            out_ref[:, j : j + 1, LANES * stat : LANES * (stat + 1)] = jnp.broadcast_to(
                piece[None], (out_ref.shape[0], 1, LANES)
            )


def group_sum(got_ref, labels, label):
    same = (labels == label).astype(F32)
    stats = got_ref.shape[2] // LANES
    parts = [
        jnp.sum(got_ref[:, :, LANES * s : LANES * (s + 1)] * same, axis=0) for s in range(stats)
    ]
    return jnp.concatenate(parts, axis=1) if stats > 1 else parts[0]


def group_count(labels, label):
    return jnp.sum((labels == label).astype(F32), axis=0)


def tiled(values, channels):
    return jnp.concatenate([values] * (channels // LANES), axis=1) if channels > LANES else values


def moments(first, second, pixels):
    mean = first / pixels
    return mean, lax.rsqrt(second / pixels - mean * mean + EPSILON)


def own_of(values, label):
    out = values[0]
    label = tiled(label, out.shape[1])
    for g in range(1, len(values)):
        out = jnp.where(label == float(g), values[g], out)
    return out


def gain_of(norm_ref, label):
    return own_of([norm_ref[g, 0:1, :] for g in range(norm_ref.shape[0])], label)


def shift_of(norm_ref, label):
    return own_of([norm_ref[g, 1:2, :] for g in range(norm_ref.shape[0])], label)


def valid_cols(channels):
    return lax.broadcasted_iota(jnp.int32, (COLS, channels), 0) < COLS - 4


def chan_mask(tab):
    return lax.broadcasted_iota(jnp.int32, (1, LANES), 1).astype(F32) < entry(tab, LIMIT)


def flat(x):
    return x.reshape(x.shape[0] * x.shape[1], x.shape[2])


def mm(a, b):
    return jnp.dot(a, b, preferred_element_type=F32)


def mm_nt(a, b):
    return lax.dot_general(a, b, (((1,), (1,)), ((), ())), preferred_element_type=F32)


def mm_tn(a, b):
    return lax.dot_general(a, b, (((0,), (0,)), ((), ())), preferred_element_type=F32)


def mm_side(a, b):
    turned = mm_tn(b, a)
    blocks = [
        jnp.transpose(turned[:, LANES * j : LANES * (j + 1)]) for j in range(a.shape[1] // LANES)
    ]
    return blocks[0] if len(blocks) == 1 else jnp.concatenate(blocks, axis=0)


def zeros8(channels):
    return jnp.zeros((8, channels), F32)


def down(x):
    return jnp.sum(x, axis=0, keepdims=True)


OWN, OTHER, HALF, LIMIT, GATE, MINOR = range(6)


def entry(tab, k):
    return tab[k : k + 1, :]


def half_of(tab, k=HALF):
    return (jnp.sum(entry(tab, k)) * (1.0 / LANES)).astype(jnp.int32)


def prepare(w1b, w2b, w_even, w_odd, w_two, w_last, b_even, b_odd, b_two, b_last):
    n = LANES
    for k, (y, x) in enumerate(((1, 1), (1, 2), (1, 0))):
        w_even[n * k : n * (k + 1), :] = w1b[y, x]
    for k, (low, high) in enumerate((((2, 1), (0, 1)), ((2, 2), (0, 2)), ((2, 0), (0, 0)))):
        w_odd[n * k : n * (k + 1), 0:n] = w1b[low]
        w_odd[n * k : n * (k + 1), n : 2 * n] = w1b[high]
    for x in range(3):
        w_two[n * x : n * (x + 1), 0:n] = w2b[0, x]
        w_two[n * x : n * (x + 1), n : 2 * n] = w2b[1, x]
        w_last[n * x : n * (x + 1), :] = w2b[2, x]
        b_two[0:n, n * x : n * (x + 1)] = w2b[1, x]
        b_two[n : 2 * n, n * x : n * (x + 1)] = w2b[2, x]
        b_last[:, n * x : n * (x + 1)] = w2b[0, x]
    nothing = jnp.zeros((n, n), BF16)
    b_even[0:n, 0:n] = w1b[1, 1]
    b_even[0:n, n : 2 * n] = nothing
    b_even[n : 2 * n, 0:n] = w1b[1, 2]
    b_even[n : 2 * n, n : 2 * n] = w1b[1, 0]
    for k, top in ((0, 2), (1, 0)):
        b_odd[0:n, 2 * n * k : 2 * n * k + n] = w1b[top, 1]
        b_odd[0:n, 2 * n * k + n : 2 * n * (k + 1)] = nothing
        b_odd[n : 2 * n, 2 * n * k : 2 * n * k + n] = w1b[top, 2]
        b_odd[n : 2 * n, 2 * n * k + n : 2 * n * (k + 1)] = w1b[top, 0]


def widen(source, x_pad):
    rows, cols, chans = source.shape
    gap = x_pad.shape[1] - cols

    def put(i, carry):
        x_pad[i, 0:cols, :] = source[i]
        x_pad[i, cols : cols + gap, :] = jnp.zeros((gap, chans), BF16)
        return carry

    lax.fori_loop(0, rows, put, 0, unroll=4)


def first_project(x_pad, w, z, stats=True):
    rows = x_pad.shape[0]
    step = rows // 4
    sums, squares = zeros8(LANES), zeros8(LANES)
    for c in range(4):
        values = mm(flat(x_pad[step * c : step * (c + 1)]), w[...])
        z[step * c : step * (c + 1)] = values.reshape(step, x_pad.shape[1], LANES)
        if stats:
            parts = values.reshape(-1, 8, LANES)
            sums = sums + jnp.sum(parts, axis=0)
            squares = squares + jnp.sum(parts * parts, axis=0)
    return sums, squares


def f1(
    place_at, group_at, width_at, gate_at, images, w_at, tab, x_own, x_for, z_own, z_for, send,
    place_ref, group, width, gate, raw, w, found, sems, *, batch,
):
    pairs = (
        (place_at, place_ref), (group_at, group), (width_at, width), (gate_at, gate), (w_at, w),
        (images.at[0], raw.at[0]), (images.at[1], raw.at[1]),
    )
    copies = [pltpu.make_async_copy(a, b, sems.at[k]) for k, (a, b) in enumerate(pairs)]
    for k in (0, 4, 5, 6, 1, 2, 3):
        copies[k].start()
    for k in (0, 4, 5):
        copies[k].wait()
    half = lax.div(place_ref[0], batch)
    sides = ((x_own, z_own), (x_for, z_for))

    def one(k):
        for place in (0, 1):

            @pl.when(half == place)
            def _():
                x_pad, z = sides[k] if place == 0 else sides[1 - k]
                widen(raw.at[k], x_pad)
                sums, squares = first_project(x_pad, w, z)
                at = 2 * (k if place == 0 else 1 - k)
                found[at : at + 1, :] = down(sums)
                found[at + 1 : at + 2, :] = down(squares)

    one(0)
    copies[6].wait()
    one(1)
    for k in (1, 2, 3):
        copies[k].wait()
    rows = [found[k : k + 1, :] for k in range(4)]
    own, other = group[half], group[1 - half]
    values = {
        OWN: own, OTHER: other, HALF: half, LIMIT: w.shape[1] // 4 * width[own], GATE: gate[own],
        MINOR: lax.rem(lax.rem(place_ref[0], batch), NEAR),
    }
    tab[...] = jnp.zeros(tab.shape, F32)
    for k, v in values.items():
        tab[k : k + 1, :] = jnp.full((1, LANES), v.astype(F32))
    spread(send, [*rows, jnp.full((1, LANES), (own + 4 * other).astype(F32))])


def f1_strided(tab, x_own, x_oth, w, xee, z, stats, wide):
    half = half_of(tab)
    rows = x_own.shape[0] // 2
    for k, x_pad in enumerate((x_own, x_oth)):
        first = rows * (half if k == 0 else 1 - half)

        def put(i, carry, x_pad=x_pad, first=first):
            for b in range(wide.shape[0]):
                lanes = slice(LANES * b, LANES * (b + 1))
                wide[b] = x_pad[2 * i, :, lanes].astype(F32)
                xee[first + i, :, lanes] = wide[b, pl.ds(0, COLS, stride=2), :].astype(BF16)
            return carry

        lax.fori_loop(0, rows, put, 0, unroll=2)
    total = 2 * rows
    step = total // 7
    chans = z.shape[2]
    squares = zeros8(chans)
    for c in range(7):
        values = mm(flat(xee[step * c : step * (c + 1)]), w[...])
        z[step * c : step * (c + 1)] = values.reshape(step, COLS, chans)
        parts = values.reshape(-1, 8, chans)
        squares = squares + jnp.sum(parts * parts, axis=0)
    ones = jnp.ones((8, total * COLS), BF16)
    stats[:, 0 : w.shape[0]] = mm(ones, flat(xee[...]))[0:1]
    stats[:, w.shape[0] :] = down(squares)


def scale_shift(got, labels, tab, norm, pixels, slot=0):
    label = entry(tab, OWN)
    total = group_sum(got, labels, label)
    chans = norm.shape[2]
    count = tiled(group_count(labels, label), chans) * pixels
    mean, rstd = moments(row(total, 2 * slot), row(total, 2 * slot + 1), count)
    gain, shift = gain_of(norm, entry(tab, OWN)), shift_of(norm, entry(tab, OWN))
    return mean, rstd, gain, shift, count


def conv_stats(z, source, pair, single, send, extra=()):
    keep = valid_cols(LANES)[None]
    rows = z.shape[0]
    step = rows // 4
    (lanes_2, w_2, offsets), (lanes_1, w_1, offset) = pair, single
    sums, squares = zeros8(LANES), zeros8(LANES)
    base = min(offsets)
    for c in range(4):
        at = step * c
        both = mm(flat(source[at + base : at + base + step + 1, :, lanes_2]), w_2)
        values = mm(flat(source[at + offset : at + offset + step, :, lanes_1]), w_1)
        for k, own in enumerate(offsets):
            skip = COLS * (own - base)
            values = values + both[skip : skip + step * COLS, LANES * k : LANES * (k + 1)]
        values = jnp.where(keep, values.reshape(step, COLS, LANES), 0.0)
        z[at : at + step] = values
        parts = values.reshape(-1, 8, LANES)
        sums = sums + jnp.sum(parts, axis=0)
        squares = squares + jnp.sum(parts * parts, axis=0)
    spread(send, [down(sums), down(squares), *extra])


def f2(
    tab, got, z_own, x_oth, w, norm, w_even, w_odd, stats_p,
    xs, z, send, labels, keeps, keeps_all, z_oth,
):
    codes = got[:, :, 4 * LANES : 5 * LANES]
    others = jnp.floor(0.25 * codes)
    marks = codes - 4.0 * others
    labels[...] = marks
    rows = xs.shape[0] - 1
    pixels = 4.0 * rows * (COLS - 4)
    first_project(x_oth, w, z_oth, False)
    for g in range(norm.shape[0]):
        mine, theirs = (marks == float(g)).astype(F32), (others == float(g)).astype(F32)
        totals = [
            jnp.sum(
                got[:, :, LANES * s : LANES * (s + 1)] * mine
                + got[:, :, LANES * (s + 2) : LANES * (s + 3)] * theirs,
                axis=0,
            )
            for s in (0, 1)
        ]
        mean, rstd = moments(*totals, group_count(marks, float(g)) * pixels)
        keeps_all[2 * g : 2 * g + 1, :] = mean
        keeps_all[2 * g + 1 : 2 * g + 2, :] = rstd
    for k, slot in enumerate((OWN, OTHER)):
        for q in (0, 1):
            choices = [keeps_all[2 * g + q : 2 * g + q + 1, :] for g in range(norm.shape[0])]
            keeps[2 * k + q : 2 * k + q + 1, :] = own_of(choices, entry(tab, slot))
    mean, rstd = keeps[0:1, :], keeps[1:2, :]
    gain, shift = gain_of(norm, entry(tab, OWN)), shift_of(norm, entry(tab, OWN))
    scale = rstd * gain
    bias = 0.5 * (shift - mean * scale)
    scale = 0.5 * scale
    keep = valid_cols(LANES) & chan_mask(tab)
    half = half_of(tab)
    xs[0] = jnp.zeros(xs.shape[1:], BF16)
    n = LANES
    for k, zz in enumerate((z_own, z_oth)):
        first = 1 + (rows // 2) * (half if k == 0 else 1 - half)

        def put(i, carry, zz=zz, first=first):
            lane = 0
            for a in (0, 1):
                for b in (0, 1):
                    u = zz[2 * i + a, pl.ds(b, COLS, stride=2), :] * scale + bias
                    act = jnp.where(keep, silu_of_half(u), 0.0)
                    xs[first + i, :, lane : lane + n] = act.astype(BF16)
                    lane += n
                    if b == 1:
                        moved = pltpu.roll(act, 1, 0)
                        xs[first + i, :, lane : lane + n] = moved.astype(BF16)
                        lane += n
            return carry

        lax.fori_loop(0, rows // 2, put, 0, unroll=2)
    extra = [stats_p[:, lanes] for lanes in columns(stats_p.shape[1])]
    pair = (slice(3 * n, 6 * n), w_odd[...], (1, 0))
    conv_stats(z, xs, pair, (slice(0, 3 * n), w_even[...], 1), send, extra)


def expand(act, w, z, send, act_sum):
    rows, chans = z.shape[0], z.shape[2]
    step = rows // 7
    squares = zeros8(chans)
    for c in range(7):
        values = mm(flat(act[step * c : step * (c + 1)]), w[...])
        z[step * c : step * (c + 1)] = values.reshape(step, COLS, chans)
        parts = values.reshape(-1, 8, chans)
        squares = squares + jnp.sum(parts * parts, axis=0)
    squares = down(squares)
    spread(send, [act_sum, *(squares[:, lanes] for lanes in columns(chans))])


def join(pieces):
    return pieces[0] if len(pieces) == 1 else jnp.concatenate(pieces, axis=1)


def columns(channels):
    return [slice(LANES * j, LANES * (j + 1)) for j in range(channels // LANES)]


def through(sums, w):
    high = sums.astype(BF16)
    rest = sums - high.astype(F32)
    mid = rest.astype(BF16)
    low = (rest - mid.astype(F32)).astype(BF16)
    lines = [v.astype(F32) for v in (high, mid, low)]
    lines.append(jnp.zeros((5, sums.shape[1]), F32))
    return down(mm(jnp.concatenate(lines, axis=0).astype(BF16), w))


def through_nt(sums, w):
    high = sums.astype(BF16)
    rest = sums - high.astype(F32)
    mid = rest.astype(BF16)
    low = (rest - mid.astype(F32)).astype(BF16)
    lines = [v.astype(F32) for v in (high, mid, low)]
    lines.append(jnp.zeros((5, sums.shape[1]), F32))
    return down(mm_nt(jnp.concatenate(lines, axis=0).astype(BF16), w))


def put_split(send, at, values):
    rows = values.shape[0]
    high = values.astype(BF16)
    rest = (values - high.astype(F32)).astype(BF16)
    for k, part in enumerate((high, rest)):
        send[:, at + rows * k : at + rows * (k + 1), :] = jnp.broadcast_to(
            part[None], (send.shape[0], rows, LANES)
        )


def get_split(got, at, rows):
    return got[:, at : at + rows, :].astype(F32) + got[:, at + rows : at + 2 * rows, :].astype(F32)


def over_group(values, marks, label):
    return jnp.sum(values * (marks == label).astype(F32), axis=0)


def stack(rows):
    return jnp.concatenate(rows, axis=0)


def pair_products(tab, z, norm, keeps, act, act_sum, slope, both, centred):
    rows = z.shape[0]
    label = entry(tab, OWN)
    mean, rstd = keeps[0:1, :], keeps[1:2, :]
    scale = rstd * gain_of(norm, label)
    bias = 0.5 * (shift_of(norm, label) - mean * scale)
    scale = 0.5 * scale
    keep = valid_cols(LANES) & chan_mask(tab)
    middle = act_sum * (1.0 / (rows * (COLS - 4)))

    def put(i, carry):
        zz = z[i]
        s = jnp.where(keep, slope_of_half(zz * scale + bias), 0.0)
        sx = s * ((zz - mean) * rstd)
        slope[i] = s
        both[i, :, 0:LANES] = s.astype(BF16)
        both[i, :, LANES:] = sx.astype(BF16)
        centred[i] = (act[i].astype(F32) - middle).astype(BF16)
        return carry[0] + fold(s), carry[1] + fold(sx)

    sums = lax.fori_loop(0, rows, put, (zeros8(LANES), zeros8(LANES)), unroll=4)
    return mm_tn(flat(centred[...]), flat(both[...])), stack([down(v) for v in sums])


def put_pair(send, at, share, product, sums):
    devices, n = send.shape[0], LANES
    missing = devices * share - n
    for h in (0, 1):
        values = product[:, n * h : n * (h + 1)]
        if missing:
            values = stack([values, jnp.zeros((missing, n), F32)])
        first = at + share * h
        send[:, first : first + share, :] = values.reshape(devices, share, n).astype(BF16)
    put_split(send, at + 2 * share, sums)


def pass_pair(send, at, got, got_at, share, marks, groups):
    rows = got[:, got_at : got_at + 2 * share, :].astype(F32)
    out = None
    for g in range(groups):
        same = (marks == float(g)).astype(F32)
        term = jnp.sum(rows * same, axis=0)[None] * same
        out = term if out is None else out + term
    send[:, at : at + 2 * share, :] = out.astype(BF16)


def pair_solve(tab, marks, outer, inner, sums, w, act_sums, q_rows, p_rows, pixels):
    label, n = entry(tab, OWN), LANES
    (norm_o, keeps_o), (norm_i, keeps_i) = outer, inner
    shift_o, gain_o, shift_i, gain_i = sums
    images = group_count(marks, label)
    count, count_o = images * pixels, tiled(images, norm_o.shape[2]) * pixels
    rstd_o = keeps_o[1:2, :]
    a_o = rstd_o * gain_of(norm_o, label)
    b_o, c_o = -(a_o * rstd_o) * gain_o / count_o, -a_o * shift_o / count_o
    m = mm_nt((w[...].astype(F32) * b_o).astype(BF16), w[...]).astype(BF16)
    e = through_nt(c_o, w[...])
    same = (marks == label).astype(F32)
    middle = jnp.sum(act_sums * same, axis=0) / count
    spread_out = ((act_sums * (1.0 / pixels) - middle[None]) * same).reshape(-1, n).astype(BF16)
    share = p_rows.shape[1] // 2
    found = []
    for h, start in enumerate((shift_i, gain_i)):
        q = q_rows[:, h : h + 1, :]
        p = p_rows[:, share * h : share * (h + 1), :].reshape(-1, n)[0:n]
        p = p + mm_tn(spread_out, q.reshape(-1, n).astype(BF16))
        found.append(start + down(m.astype(F32) * p) + e * jnp.sum(q * same, axis=0))
    rstd_i = keeps_i[1:2, :]
    a = rstd_i * gain_of(norm_i, label)
    coefs = a, -(a * rstd_i) * found[1] / count, -a * found[0] / count
    return m, e - through(middle, m), coefs, found


def expanded_moments(got, labels, tab, w, pixels):
    label = entry(tab, OWN)
    total = group_sum(got, labels, label)
    chans = w.shape[1]
    count = tiled(group_count(labels, label), chans) * pixels
    return moments(through(total[:, 0:LANES], w[...]), total[:, LANES:], count)


def activate(tab, got, labels, z_in, norm, act, keeps):
    got = got.at[:, :, 0 : 2 * LANES]
    rows = z_in.shape[0]
    pixels = 1.0 * rows * (COLS - 4)
    mean, rstd, gain, shift, _ = scale_shift(got, labels[...], tab, norm, pixels)
    keeps[0:1, :] = mean
    keeps[1:2, :] = rstd
    scale = rstd * gain
    bias = 0.5 * (shift - mean * scale)
    scale = 0.5 * scale
    keep = valid_cols(LANES) & chan_mask(tab)

    def put(i, sums):
        low = jnp.where(keep, silu_of_half(z_in[i] * scale + bias), 0.0).astype(BF16)
        act[i] = low
        return sums + fold(low.astype(F32))

    return down(lax.fori_loop(0, rows, put, zeros8(LANES), unroll=7))


def f3(tab, got, labels, z_in, norm, w, w_p, act, z, send, keeps, keeps_p, act_sum):
    sums = activate(tab, got, labels, z_in, norm, act, keeps)
    act_sum[...] = sums
    expand(act, w, z, send, sums)
    marks, label = labels[...], entry(tab, OWN)
    total = group_sum(got, marks, label)
    outer, first = z.shape[2], 2 * LANES
    second = first + w_p.shape[0]
    count = tiled(group_count(marks, label), outer) * (1.0 * z.shape[0] * (COLS - 4))
    mean, rstd = moments(through(total[:, first:second], w_p[...]), total[:, second:], count)
    keeps_p[0:1, :] = mean
    keeps_p[1:2, :] = rstd


def f4(tab, got, labels, zc, zp, norm_c, norm_p, keeps_p, w_c, w, joined, slope, z, stats, keeps):
    rows, chans = zc.shape[0], zc.shape[2]
    pixels = 1.0 * rows * (COLS - 4)
    mean_c, rstd_c = expanded_moments(got, labels[...], tab, w_c, pixels)
    mean_p, rstd_p = keeps_p[0:1, :], keeps_p[1:2, :]
    for k, v in enumerate((mean_c, rstd_c, mean_p, rstd_p)):
        keeps[k : k + 1, :] = v
    group = entry(tab, OWN)
    scale_c = rstd_c * gain_of(norm_c, group)
    scale_p = rstd_p * gain_of(norm_p, group)
    bias = (shift_of(norm_c, group) - mean_c * scale_c) + (
        shift_of(norm_p, group) - mean_p * scale_p
    )
    keep = valid_cols(chans)
    scale_c, scale_p, bias = 0.5 * scale_c, 0.5 * scale_p, 0.5 * bias

    def put(i, carry):
        u = zc[i] * scale_c + zp[i] * scale_p + bias
        t = jnp.tanh(u)
        p = u * t
        joined[i] = jnp.where(keep, u + p, 0.0).astype(BF16)
        slope[i] = (0.5 + 0.5 * t) * (1.0 + u - p)
        return carry

    lax.fori_loop(0, rows, put, 0, unroll=4)
    step = rows // 4
    sums, squares = zeros8(LANES), zeros8(LANES)
    for c in range(4):
        values = mm(flat(joined[step * c : step * (c + 1)]), w[...])
        z[step * c : step * (c + 1)] = values.reshape(step, COLS, LANES)
        parts = values.reshape(-1, 8, LANES)
        sums = sums + jnp.sum(parts, axis=0)
        squares = squares + jnp.sum(parts * parts, axis=0)
    stats[0:1, :] = down(sums)
    stats[1:2, :] = down(squares)


def pair_1(tab, stats, z, norm, keeps, act, act_sum, send, slope, both, centred, *, share):
    product, sums = pair_products(tab, z, norm, keeps, act, act_sum[...], slope, both, centred)
    put_split(send, 0, stats[...])
    put_pair(send, 4, share, product, sums)


def put_shares(xz, send, part):
    n, devices = LANES, send.shape[0]
    share = xz.shape[0] // devices
    pieces = xz[...].reshape(devices, share, n)
    first = (share + 1) // 2 * part
    for q in range(first, (share + 1) // 2 if part == 0 else share):
        at = n * (2 + q - first)
        send[:, :, at : at + n] = pieces[:, q : q + 1, :]


def f5(tab, got, labels, z_in, norm, w_two, w_last, xz, x3, z, send, keeps):
    rows = z_in.shape[0]
    pixels = 1.0 * rows * (COLS - 4)
    marks, label = labels[...], entry(tab, OWN)
    total = over_group(get_split(got, 0, 2), marks, label)
    mean, rstd = moments(total[0:1], total[1:2], group_count(marks, label) * pixels)
    gain, shift = gain_of(norm, label), shift_of(norm, label)
    keeps[0:1, :] = mean
    keeps[1:2, :] = rstd
    scale = rstd * gain
    bias = 0.5 * (shift - mean * scale)
    scale = 0.5 * scale
    keep = valid_cols(LANES) & chan_mask(tab)
    x3[0] = jnp.zeros(x3.shape[1:], BF16)
    x3[rows + 1] = jnp.zeros(x3.shape[1:], BF16)
    n = LANES

    def put(i, carry):
        act = jnp.where(keep, silu_of_half(z_in[i] * scale + bias), 0.0)
        x3[i + 1, :, 0:n] = pltpu.roll(act, 1, 0).astype(BF16)
        x3[i + 1, :, n : 2 * n] = act.astype(BF16)
        x3[i + 1, :, 2 * n : 3 * n] = pltpu.roll(act, COLS - 1, 0).astype(BF16)
        return carry

    lax.fori_loop(0, rows, put, 0, unroll=2)
    lanes = slice(0, 3 * n)
    conv_stats(
        z, x3, (lanes, w_two[...], (0, 1)), (lanes, w_last[...], 2), send.at[:, :, 0 : 2 * n]
    )
    put_shares(xz, send, 0)


def f6(tab, got, labels, z_in, norm, w, act, z, send, keeps):
    sums = activate(tab, got, labels, z_in, norm, act, keeps)
    expand(act, w, z, send, sums)


def b7(tab, got, labels, joined, z, norm, w, cot, result, grad_pre, send, keeps, wide):
    rows, chans = z.shape[0], z.shape[2]
    cols = COLS - 4
    pixels = 1.0 * rows * cols
    mean, rstd = expanded_moments(got, labels[...], tab, w, pixels)
    gain, shift = gain_of(norm, entry(tab, OWN)), shift_of(norm, entry(tab, OWN))
    keeps[0:1, :] = mean
    keeps[1:2, :] = rstd
    gate = 0.25 * tiled(entry(tab, GATE), chans)
    scale = 0.5 * rstd * gain * gate
    bias = 0.5 * (shift - mean * rstd * gain) * gate
    wide[...] = jnp.zeros(wide.shape, F32)

    def put(i, carry):
        sums, products = carry
        wide[0:cols, :] = cot[i].astype(F32)
        zz = z[i]
        u = 0.5 * joined[i].astype(F32) + zz * scale + bias
        t = jnp.tanh(u)
        p = u * t
        result[i] = (u + p)[0:cols].astype(BF16)
        g = wide[...] * ((0.5 + 0.5 * t) * (1.0 + u - p))
        grad_pre[i] = g
        return sums + fold(g), products + fold(g * (zz - mean))

    start = zeros8(chans)
    sums, products = lax.fori_loop(0, rows, put, (start, start), unroll=2)
    spread(send, [down(sums) * gate, down(products) * rstd * gate])


def lane_sums(got, marks, channels):
    def sums_of(g):
        total = group_sum(got, marks, float(g))
        return row(total, 0), row(total, 1)

    return sums_of


def row_sums(got, marks):
    def sums_of(g):
        total = over_group(get_split(got, 0, 2), marks, float(g))
        return total[0:1], total[1:2]

    return sums_of


def backward_norm(tab, sums_of, marks, norm, keeps, pixels, grad_norm):
    group, chans = entry(tab, OWN), norm.shape[2]
    sums = [sums_of(g) for g in range(norm.shape[0])]
    for g, (shift_sum, gain_sum) in enumerate(sums):
        grad_norm[g, 0:1, :] = gain_sum
        grad_norm[g, 1:2, :] = shift_sum
    count = tiled(group_count(marks, group), chans) * pixels
    own_shift, own_gain = (own_of([v[k] for v in sums], group) for k in (0, 1))
    mean, rstd = keeps[0:1, :], keeps[1:2, :]
    a = rstd * gain_of(norm, group)
    return mean, a, -(a * rstd) * own_gain / count, -a * own_shift / count


def slope_sums(tab, d, z_in, norm, keeps, dout):
    rows = z_in.shape[0]
    mean, rstd = keeps[0:1, :], keeps[1:2, :]
    group = entry(tab, OWN)
    scale = rstd * gain_of(norm, group)
    bias = 0.5 * (shift_of(norm, group) - mean * scale)
    scale = 0.5 * scale
    keep = valid_cols(LANES) & chan_mask(tab)

    def put(i, carry):
        sums, products = carry
        zz = z_in[i]
        g = jnp.where(keep, d[i] * slope_of_half(zz * scale + bias), 0.0)
        dout[i] = g
        return sums + fold(g), products + fold(g * (zz - mean))

    sums, products = lax.fori_loop(
        0, rows, put, (zeros8(LANES), zeros8(LANES)), unroll=4
    )
    return down(sums), down(products) * rstd


def b8(
    tab, got, labels, grad_pre, z, norm, keeps, w, z_in, norm_in, keeps_in, xz,
    dz, dout, send, grad_norm, d,
):
    rows, chans = z.shape[0], z.shape[2]
    pixels = 1.0 * rows * (COLS - 4)
    marks = labels[...]
    sums_of = lane_sums(got, marks, chans)
    mean, a, b, c = backward_norm(tab, sums_of, marks, norm, keeps, pixels, grad_norm)
    a = a * (0.25 * tiled(entry(tab, GATE), norm.shape[2]))
    keep = valid_cols(chans)

    def put(i, carry):
        v = a * grad_pre[i] + b * (z[i] - mean) + c
        dz[i] = jnp.where(keep, v, 0.0).astype(BF16)
        return carry

    lax.fori_loop(0, rows, put, 0, unroll=2)
    d[...] = mm_nt(flat(dz[...]), w[...]).reshape(d.shape)
    sums = slope_sums(tab, d, z_in, norm_in, keeps_in, dout)
    spread(send.at[:, :, 0 : 2 * LANES], sums)
    put_shares(xz, send, 1)


def b9(
    tab, got, labels, dout_in, z, norm, keeps, b_two, b_last, z_in, norm_in, keeps_in, x_sum, pair_got,
    dz, dout, send, grad_norm, d3, d, *, share,
):
    rows = z.shape[0]
    pixels = 1.0 * rows * (COLS - 4)
    marks = labels[...]
    sums_of = lane_sums(got.at[:, :, 0 : 2 * LANES], marks, LANES)
    mean, a, b, c = backward_norm(tab, sums_of, marks, norm, keeps, pixels, grad_norm)
    keep = valid_cols(LANES)
    n = LANES
    d3[0] = jnp.zeros(d3.shape[1:], BF16)
    d3[rows + 1] = jnp.zeros(d3.shape[1:], BF16)

    def put(i, carry):
        v = a * dout_in[i] + b * (z[i] - mean) + c
        v = jnp.where(keep, v, 0.0)
        d3[i + 1, :, 0:n] = pltpu.roll(v, COLS - 1, 0).astype(BF16)
        low = v.astype(BF16)
        d3[i + 1, :, n : 2 * n] = low
        dz[i] = low
        d3[i + 1, :, 2 * n : 3 * n] = pltpu.roll(v, 1, 0).astype(BF16)
        return carry

    lax.fori_loop(0, rows, put, 0, unroll=2)
    step = rows // 4
    for k in range(4):
        both = mm_nt(flat(d3[step * k : step * (k + 1) + 1]), b_two[...])
        value = mm_nt(flat(d3[step * k + 2 : step * (k + 1) + 2]), b_last[...])
        value = value + both[COLS:, 0:n] + both[0 : step * COLS, n : 2 * n]
        d[step * k : step * (k + 1)] = value.reshape(step, COLS, LANES)
    put_split(send, 0, stack(slope_sums(tab, d, z_in, norm_in, keeps_in, dout)))
    blocks = columns(x_sum.shape[0])
    put_split(send, 4, stack([jnp.transpose(x_sum[lanes, :])[0:1] for lanes in blocks]))
    pass_pair(send, 4 + 2 * len(blocks), pair_got, 4, share, marks, norm.shape[0])


def b10(
    tab, got, labels, dout_in, z, norm, keeps, w, grad_pre, slope, zc, zp, keeps_cp,
    norm_c, w_c, slope_in, z_in, keeps_in,
    dz, grad_pre_2, send, grad_norm, d_in, d, low,
):
    rows, chans = zc.shape[0], zc.shape[2]
    pixels = 1.0 * rows * (COLS - 4)
    marks = labels[...]
    coefs = backward_norm(tab, row_sums(got, marks), marks, norm, keeps, pixels, grad_norm)
    normed_grad(dz, dout_in, z, *coefs)
    d[...] = mm_nt(flat(dz[...]), w[...]).reshape(d.shape)
    mean_c, rstd_c, mean_p, rstd_p = (keeps_cp[k : k + 1, :] for k in range(4))
    a_c = rstd_c * gain_of(norm_c, entry(tab, OWN))

    def sum_up(i, carry):
        sums, prod_c, prod_p = carry
        g = (grad_pre[i] + d[i]).astype(BF16).astype(F32) * slope[i]
        grad_pre_2[i] = g
        low[i] = (a_c * g).astype(BF16)
        return (
            sums + fold(g),
            prod_c + fold(g * (zc[i] - mean_c)),
            prod_p + fold(g * (zp[i] - mean_p)),
        )

    start = zeros8(chans)
    sums, prod_c, prod_p = lax.fori_loop(0, rows, sum_up, (start, start, start), unroll=2)
    wide = [down(sums), down(prod_c) * rstd_c, down(prod_p) * rstd_p]
    inner = inner_sums(low, w_c, slope_in, z_in, keeps_in, d_in)
    parts = [stack([v[:, 0 : chans // 2], v[:, chans // 2 :]]) for v in wide]
    values = join([*parts, stack(inner)])
    send[...] = jnp.broadcast_to(values[None], send.shape)


def inner_sums(low, w, slope, z, keeps, d_in):
    d_in[...] = mm_nt(flat(low[...]), w[...]).reshape(d_in.shape)
    mean, rstd = keeps[0:1, :], keeps[1:2, :]

    def add(i, carry):
        g = slope[i] * d_in[i]
        return carry[0] + fold(g), carry[1] + fold(g * (z[i] - mean))

    sums = lax.fori_loop(0, z.shape[0], add, (zeros8(LANES), zeros8(LANES)), unroll=7)
    return down(sums[0]), down(sums[1]) * rstd


def inner_grad(act, m, line, slope, d_in, d):
    d[...] = mm(flat(act[...]), m).reshape(d.shape)

    def put(i, carry):
        d[i] = slope[i] * (d_in[i] + d[i] + line)
        return carry

    lax.fori_loop(0, d.shape[0], put, 0, unroll=7)


def normed_grad(dz, dout, z, mean, a, b, c):
    keep = valid_cols(z.shape[2])

    def put(i, carry):
        v = a * dout[i] + b * (z[i] - mean) + c
        dz[i] = jnp.where(keep, v, 0.0).astype(BF16)
        return carry

    lax.fori_loop(0, z.shape[0], put, 0, unroll=2)


def b12(
    tab, own10, labels, norm_c, keeps_c, w_c, got_act, got_q, got_p, act, slope, d_in,
    z, norm, keeps, xs, d2, kept, sent, own_sums, dz, packed, dout, *, share, q_at, p_at,
):
    rows = z.shape[0]
    pixels = 1.0 * rows * (COLS - 4)
    outer, n = norm_c.shape[2], LANES
    marks = labels[...]
    total = own10[...]
    cuts = (0, outer, 2 * outer, 2 * outer + n, 2 * outer + 2 * n)
    m, line, (a, b, c), found = pair_solve(
        tab, marks, (norm_c, keeps_c.at[0:2]), (norm, keeps),
        [total[:, u:v] for u, v in zip(cuts, cuts[1:])], w_c, got_act[:, :, 0:n],
        get_split(got_q, q_at, 2), got_p[:, p_at : p_at + 2 * share, :].astype(F32), pixels,
    )
    own_sums[0:1, :] = found[0]
    own_sums[1:2, :] = found[1]
    inner_grad(act, m, line, slope, d_in, dout)
    mean = keeps[0:1, :]
    keep = valid_cols(LANES)
    d2[rows] = jnp.zeros(d2.shape[1:], BF16)

    def put(i, carry):
        v = a * dout[i] + b * (z[i] - mean) + c
        v = jnp.where(keep, v, 0.0)
        low = v.astype(BF16)
        dz[i] = low
        d2[i, :, 0:n] = low
        d2[i, :, n : 2 * n] = pltpu.roll(v, COLS - 1, 0).astype(BF16)
        return carry

    lax.fori_loop(0, rows, put, 0, unroll=4)
    low = flat(dz[...])
    cur = mm_side(flat(xs[1 : rows + 1]), low)
    for k, (y, x) in enumerate(((1, 1), (1, 2), (1, 0), (2, 1), (2, 2), (2, 0))):
        put_rows(packed, n * (3 * y + x), cur[n * k : n * (k + 1)])
    up = mm_side(flat(xs[0:rows, :, 3 * n : 6 * n]), low)
    for k, (y, x) in enumerate(((0, 1), (0, 2), (0, 0))):
        put_rows(packed, n * (3 * y + x), up[n * k : n * (k + 1)])
    share_out(tab, packed, 9 * n, kept, sent)


def b12_images(
    tab, d2, b_even, b_odd, zz, norm_in, keeps_in, dn, sums_out, de, do, wide, *, own
):
    rows = de.shape[0]
    n = LANES
    half = half_of(tab)
    first = rows * (half if own else 1 - half)
    step = rows // 2
    for k in range(2):
        here = flat(d2[pl.ds(first + step * k, step)])
        below = flat(d2[pl.ds(first + step * k + 1, step)])
        de[step * k : step * (k + 1)] = mm_nt(here, b_even[...]).reshape(step, COLS, 2 * n)
        odd = mm_nt(here, b_odd[:, 0 : 2 * n]) + mm_nt(below, b_odd[:, 2 * n : 4 * n])
        do[step * k : step * (k + 1)] = odd.reshape(step, COLS, 2 * n)
    mean_1, rstd_1 = keeps_in[0:1, :], keeps_in[1:2, :]
    group = entry(tab, OWN)
    scale = rstd_1 * gain_of(norm_in, group)
    bias = 0.5 * (shift_of(norm_in, group) - mean_1 * scale)
    scale = 0.5 * scale
    keep = valid_cols(LANES) & chan_mask(tab)

    def emit(i, carry):
        sums, products = carry
        for ra in (0, 1):
            planes = (de, do)[ra]
            for cb in (0, 1):
                zv = zz[2 * i + ra, pl.ds(cb, COLS, stride=2), :]
                g = planes[i, :, n * cb : n * (cb + 1)] * slope_of_half(zv * scale + bias)
                g = jnp.where(keep, g, 0.0)
                sums = sums + fold(g)
                products = products + fold(g * (zv - mean_1))
                wide[ra, pl.ds(cb, COLS, stride=2), :] = g
            dn[2 * i + ra] = wide[ra].astype(BF16)
        return sums, products

    totals = lax.fori_loop(0, rows, emit, (zeros8(n), zeros8(n)), unroll=2)
    sums_out[0:1, :] = down(totals[0])
    sums_out[1:2, :] = down(totals[1]) * rstd_1


def b13(
    tab, got, labels, norm, keeps, w, z_own, z_for, dn_own, dn_for, gs_own, gs_for, *rest, at, held
):
    finished, outs = rest[:held], rest[held : 2 * held]
    grad, grad_norm, grad_inner, dz, wide, grad_v, norm_v, inner_v, sems = rest[2 * held :]
    copies = [
        pltpu.make_async_copy(a, b, sems.at[k]) for k, (a, b) in enumerate(zip(finished, outs))
    ]
    for copy in copies:
        copy.start()
    rows, cols = grad.shape[1], grad.shape[2]
    half = half_of(tab)
    pixels = 2.0 * rows * cols
    marks = labels[...]
    totals = last_sums(got.at[:, at : at + 4, :], marks, norm.shape[0])
    for g in range(norm.shape[0]):
        norm_v[g, 0:1, :] = totals[g][1]
        norm_v[g, 1:2, :] = totals[g][0]
    found = get_split(got, at + 4, 2)
    for g in range(norm.shape[0]):
        total = over_group(found, marks, float(g)) / group_count(marks, float(g))
        inner_v[g, 0:1, :] = total[1:2]
        inner_v[g, 1:2, :] = total[0:1]
    for k, (value, out) in enumerate(((norm_v, grad_norm), (inner_v, grad_inner))):
        copies.append(pltpu.make_async_copy(value, out, sems.at[held + k]))
        copies[-1].start()
    keep = lax.broadcasted_iota(jnp.int32, (z_own.shape[1], LANES), 0) < cols
    for k, (z, dn, gs) in enumerate(((z_own, dn_own, gs_own), (z_for, dn_for, gs_for))):
        group = entry(tab, OWN if k == 0 else OTHER)
        shift_sum = own_of([t[0] for t in totals], group)
        gain_sum = own_of([t[1] for t in totals], group)
        count = group_count(marks, group) * pixels
        mean, rstd = keeps[2 * k : 2 * k + 1, :], keeps[2 * k + 1 : 2 * k + 2, :]
        a = rstd * gain_of(norm, group)
        b = -(a * rstd) * gain_sum / count
        c = -a * shift_sum / count

        def put(i, carry, z=z, dn=dn, mean=mean, a=a, b=b, c=c):
            v = a * dn[i].astype(F32) + b * (z[i] - mean) + c
            dz[i] = jnp.where(keep, v, 0.0).astype(BF16)
            return carry

        lax.fori_loop(0, rows, put, 0, unroll=4)
        place = half if k == 0 else 1 - half
        step = rows // 2
        for q in range(2):
            low = flat(dz[step * q : step * (q + 1)])
            for p in range(wide.shape[0]):
                values = mm_nt(low, w[LANES * p : LANES * (p + 1), :])
                wide[p, step * q : step * (q + 1)] = values.reshape(step, -1, LANES)

            def emit(i, carry, gs=gs, place=place):
                even = pl.ds(0, COLS, stride=2)
                for p in range(wide.shape[0]):
                    lanes = slice(LANES * p, LANES * (p + 1))
                    wide[p, 2 * i, even, :] = wide[p, 2 * i, even, :] + gs[i, :, lanes].astype(F32)
                    grad_v[place, 2 * i, :, lanes] = wide[p, 2 * i, 0:cols, :].astype(BF16)
                    grad_v[place, 2 * i + 1, :, lanes] = wide[p, 2 * i + 1, 0:cols, :].astype(BF16)
                return carry

            lax.fori_loop(step // 2 * q, step // 2 * (q + 1), emit, 0, unroll=True)
            part = pl.ds(step * q, step)
            copies.append(
                pltpu.make_async_copy(
                    grad_v.at[place, part], grad.at[place, part], sems.at[held + 2 + 2 * k + q]
                )
            )
            copies[-1].start()
    for copy in copies:
        copy.wait()


def put_rows(out, at, value):
    for j in range(value.shape[1] // LANES):
        out[at : at + value.shape[0], :] = value[:, LANES * j : LANES * (j + 1)].astype(BF16)
        at += value.shape[0]
    return at


def take_rows(source, at, out):
    rows = out.shape[0]
    for j in range(out.shape[1] // LANES):
        out[:, LANES * j : LANES * (j + 1)] = source(at, rows)
        at += rows
    return at


def share_out(tab, packed, used, kept, sent):
    if used < packed.shape[0]:
        packed[used:, :] = jnp.zeros((packed.shape[0] - used, LANES), BF16)
    half = half_of(tab)
    size = kept.shape[0] * kept.shape[1]
    for out, place in ((kept, half), (sent, 1 - half)):
        out[...] = packed[pl.ds(pl.multiple_of(size * place, 16), size), :].reshape(out.shape)


def g_most(
    tab, act_2b, dz_2c, x3, dz_2b, joined, dz_2a, act_1b, xee, w_p,
    got, labels, norm_c, norm_p, keeps, grad_pre_2, zc, zp,
    kept, sent, gs_own, gs_oth, grad_norm_c, grad_norm_p, own10, packed, dz_1c, dz_p,
):
    rows, outer = dz_2b.shape[0], zc.shape[2]
    pixels = 1.0 * rows * (COLS - 4)
    marks = labels[...]

    totals = [group_sum(got, marks, float(g)) for g in range(norm_c.shape[0])]
    side = outer // 2

    def line(total, k):
        return join([total[h : h + 1, side * k : side * (k + 1)] for h in (0, 1)])

    lines = [[line(total, k) for k in range(3)] for total in totals]
    label = entry(tab, OWN)
    for k in range(2):
        own10[:, outer * k : outer * (k + 1)] = own_of([v[k] for v in lines], label)
        inner = [total[k : k + 1, 3 * side :] for total in totals]
        at = 2 * outer + LANES * k
        own10[:, at : at + LANES] = own_of(inner, label)
    coefs = backward_norm(
        tab, lambda g: (lines[g][0], lines[g][1]), marks, norm_c, keeps.at[0:2], pixels, grad_norm_c
    )
    normed_grad(dz_1c, grad_pre_2, zc, *coefs)
    coefs = backward_norm(
        tab, lambda g: (lines[g][0], lines[g][2]), marks, norm_p, keeps.at[2:4], pixels, grad_norm_p
    )
    normed_grad(dz_p, grad_pre_2, zp, *coefs)
    at = put_rows(packed, 0, mm_tn(flat(act_2b[...]), flat(dz_2c[...])))
    low = flat(dz_2b[...])
    for y in range(3):
        at = put_rows(packed, at, mm_side(flat(x3[y : y + rows]), low))
    at = put_rows(packed, at, mm_side(flat(joined[...]), flat(dz_2a[...])))
    at = put_rows(packed, at, mm_tn(flat(act_1b[...]), flat(dz_1c[...])))
    at = put_rows(packed, at, mm_tn(flat(xee[...]), flat(dz_p[...])))
    share_out(tab, packed, at, kept, sent)
    half = half_of(tab)
    count = gs_own.shape[0]
    for k, gs in enumerate((gs_own, gs_oth)):
        first = count * (half if k == 0 else 1 - half)
        got = mm_nt(flat(dz_p[pl.ds(first, count)]), w_p[...])
        gs[...] = got.reshape(gs.shape).astype(BF16)


def g_xz(keeps, x_own, x_oth, z_own, z_oth, out, x_sum, low):
    rows, n = z_own.shape[0], LANES
    mean = keeps[0:1, :]
    low[:, :, n : 2 * n] = jnp.ones((rows, z_own.shape[1], n), BF16)
    value = None
    for x, z in ((x_own, z_own), (x_oth, z_oth)):

        def put(i, carry, z=z):
            low[i, :, 0:n] = (z[i] - mean).astype(BF16)
            return carry

        lax.fori_loop(0, rows, put, 0, unroll=4)
        term = mm_tn(flat(x[...]), flat(low[...]))
        value = term if value is None else value + term
    at = value.shape[0]
    out[0:at, :] = value[:, 0:n]
    if at < out.shape[0]:
        out[at:, :] = jnp.zeros((out.shape[0] - at, n), F32)
    x_sum[...] = value[:, n : 2 * n]


def g_xd(
    tab, sums_own, sums_oth, norm, keeps, x_sum, got_x, labels, x_own, x_oth, dn_own, dn_oth,
    out, sums, low,
):
    rows = dn_own.shape[0]
    n = LANES
    pixels = 1.0 * (2 * rows) * (2 * (COLS - 4))
    sums[...] = sums_own[...] + sums_oth[...]
    a = keeps[1:2, :] * gain_of(norm, entry(tab, OWN))
    local = sums[0:1, :] / pixels
    value = None
    for x, dn in ((x_own, dn_own), (x_oth, dn_oth)):

        def put(i, carry, dn=dn):
            low[i] = (a * (dn[i].astype(F32) - local)).astype(BF16)
            return carry

        lax.fori_loop(0, rows, put, 0, unroll=4)
        term = mm_tn(flat(x[...]), flat(low[...]))
        value = term if value is None else value + term
    marks, label = labels[...], entry(tab, OWN)
    total = over_group(get_split(got_x, 4, x_sum.shape[0] // n), marks, label)
    total = join([total[k : k + 1] for k in range(total.shape[0])])
    total = total / tiled(group_count(marks, label), total.shape[1])
    total = jnp.broadcast_to(total, (8, total.shape[1]))
    means = jnp.concatenate(
        [jnp.transpose(total[:, lanes])[:, 0:1] for lanes in columns(total.shape[1])], axis=0
    )
    value = value + (x_sum[...] - means) * (a * local)
    at = value.shape[0]
    out[0:at, :] = value.astype(BF16)
    if at < out.shape[0]:
        out[at:, :] = jnp.zeros((out.shape[0] - at, n), BF16)


def pack_last(tall, sums, found, kept, got, kept_1b, got_1b, send, *, stats_at):
    n = LANES
    devices = send.shape[0]
    piece, share = kept.shape[1], tall.shape[0] // devices
    first = kept.shape[0]
    second = first + kept_1b.shape[0]
    send[0:first, 0:piece, :] = (kept[...].astype(F32) + got[...].astype(F32)).astype(BF16)
    send[first:second, 0:piece, :] = (kept_1b[...].astype(F32) + got_1b[...].astype(F32)).astype(BF16)
    if second < devices:
        send[second:, 0:piece, :] = jnp.zeros((devices - second, piece, n), BF16)
    send[:, piece : piece + share, :] = tall[...].reshape(devices, share, n)
    put_split(send, stats_at, sums[...])
    put_split(send, stats_at + 4, found[...])


def last_sums(stats, marks, groups):
    values = stats[:, 0:2, :].astype(F32) + stats[:, 2:4, :].astype(F32)
    out = []
    for g in range(groups):
        total = jnp.sum(values * (marks == float(g)).astype(F32), axis=0)
        out.append((total[0:1], total[1:2]))
    return out


def add_all(got, labels, norm, keeps_all, got_a, got_b, out, *, at, pixels):
    devices, n = got.shape[0], LANES
    half = devices // 2
    split = got_a.shape[2] // n - 2
    share = split + got_b.shape[2] // n - 2
    piece = (out.shape[1] - share) // 2
    marks = labels[...]
    value = jnp.sum(got[:, piece : piece + share, :].astype(F32), axis=0)
    sums = last_sums(got.at[:, at : at + 4, :], marks, norm.shape[0])
    for g in range(norm.shape[0]):
        rstd = keeps_all[2 * g + 1 : 2 * g + 2, :]
        count = group_count(marks, float(g)) * pixels
        b = -(rstd * rstd * norm[g, 0:1, :]) * sums[g][1] / count
        same = (marks == float(g)).astype(F32)
        rows = [
            jnp.sum(source[:, :, n * (2 + q) : n * (3 + q)] * same, axis=0)
            for source, count_q in ((got_a, split), (got_b, share - split))
            for q in range(count_q)
        ]
        value = value + jnp.concatenate(rows, axis=0) * b
    for k in (0, 1):
        total = jnp.sum(got[half * k : half * (k + 1), 0:piece, :].astype(F32), axis=0).astype(BF16)
        out[:, piece * k : piece * (k + 1), :] = jnp.broadcast_to(
            total[None], (out.shape[0], piece, n)
        )
    out[:, 2 * piece :, :] = jnp.broadcast_to(value.astype(BF16)[None], (out.shape[0], share, n))


def unpack(tab, *refs, first, second, piece):
    parts, outs, values = refs[: 2 * NEAR], refs[2 * NEAR : 2 * NEAR + 7], refs[2 * NEAR + 7 :]
    *values, tall, packed, sems = values
    half, minor = half_of(tab), half_of(tab, MINOR)
    far = parts[0].shape[0]
    for k, part in enumerate(parts):
        core = half if k < NEAR else 1 - half
        base = core * (far * NEAR) + lax.bitwise_xor(minor, jnp.int32(k % NEAR))

        def place(z, carry, part=part, base=base):
            owner = base + NEAR * z
            for h in (0, 1):
                packed[h, owner] = part[z, piece * h : piece * (h + 1), :]
            tall[owner] = part[z, 2 * piece :, :].astype(F32)
            return carry

        lax.fori_loop(0, far, place, 0, unroll=min(far, 4))
    copies = [
        pltpu.make_async_copy(value, out, sems.at[k]) for k, (value, out) in enumerate(zip(values, outs))
    ]
    most = [flat(packed[h, 0:first]) for h in (0, 1)]
    last = [flat(packed[h, first : first + second]) for h in (0, 1)]
    size = first * piece

    def source(at, rows):
        pieces = []
        if at < size:
            pieces.append(most[0][at : min(at + rows, size)])
        if at + rows > size:
            pieces.append(most[1][max(at - size, 0) : at + rows - size])
        pieces = [v.astype(F32) for v in pieces]
        return pieces[0] if len(pieces) == 1 else stack(pieces)

    at = 0
    for k, value in enumerate(values[0:5]):
        at = take_rows(source, at, value)
        copies[k].start()
    w_1b, w_1a = values[5:7]
    size = second * piece
    w_1b[0:size] = last[0].astype(F32)
    w_1b[size:] = last[1][0 : w_1b.shape[0] - size].astype(F32)
    copies[5].start()
    w_1a[...] = flat(tall[...])[0 : w_1a.shape[0]]
    copies[6].start()
    for copy in copies:
        copy.wait()


def gather(send):
    return lax.all_to_all(send, AXES, 0, 0)


def tie(*values):
    return lax.optimization_barrier(values)


def swap(block):
    return lax.ppermute(block, "rows", [(0, 1), (1, 0)])


def body(
    images, w_1a, w_1b, w_1c, w_1p, w_2a, w_2b, w_2c,
    norm_1a, norm_1b, norm_1c, norm_1p, norm_2a, norm_2b, norm_2c,
    cotangent, group, width, gate,
):
    devices = lax.axis_size("rows") * lax.axis_size("batch")
    place = lax.axis_index(AXES).astype(jnp.int32).reshape(1)
    norms = (norm_1a, norm_1b, norm_1c, norm_1p, norm_2a, norm_2b, norm_2c)
    norm_1a, norm_1b, norm_1c, norm_1p, norm_2a, norm_2b, norm_2c = (
        v.transpose(1, 0, 2) for v in norms
    )
    outer, inputs = w_1c.shape[1], w_1a.shape[0]
    rows = cotangent.shape[1]
    cols_in = 2 * COLS
    n, m = LANES, devices

    def send(stats, channels=LANES):
        return ((m, channels // LANES, stats * LANES), F32)

    def maps(channels, dtype=F32):
        return ((rows, COLS, channels), dtype)

    def scratch(channels, dtype=F32):
        return pltpu.VMEM((rows, COLS, channels), dtype)

    def params(*arrays):
        return [(a.shape, F32) for a in arrays]

    def mean_scale(channels, count=1):
        return ((2 * count, channels), F32)

    wide_in = ((rows, cols_in, inputs), BF16)
    wide_z = ((rows, cols_in, n), F32)
    raw = images.shape
    tab, x_own, x_for, z_own, z_for, s1 = stage(
        functools.partial(f1, batch=devices // 2), [((8, n), F32), wide_in, wide_in, wide_z, wide_z, send(5)],
        [*(pltpu.SMEM(v.shape, jnp.int32) for v in (place, group, width, gate)),
         pltpu.VMEM(raw, BF16), pltpu.VMEM(w_1a.shape, BF16), pltpu.VMEM((8, n), F32),
         pltpu.SemaphoreType.DMA((7,))],
        hbm=(0, 1, 2, 3, 4, 5),
    )(place, group, width, gate, images, w_1a)
    s1, v_1b, v_2b = tie(s1, w_1b, w_2b)
    built = stage(
        prepare,
        [(v, BF16) for v in (
            (3 * n, n), (3 * n, 2 * n), (3 * n, 2 * n), (3 * n, n),
            (2 * n, 2 * n), (2 * n, 4 * n), (2 * n, 3 * n), (n, 3 * n),
        )],
    )(v_1b, v_2b)
    s1, x_for, w_even, w_odd, w_two, w_last, b_even, b_odd, b_two, b_last = tie(s1, x_for, *built)
    x_oth = swap(x_for)
    g1 = gather(s1)
    g1, x_oth = tie(g1, x_oth)
    xee, z_1p, stats_1p = stage(
        f1_strided,
        [maps(inputs, BF16), maps(outer), ((1, inputs + outer), F32)],
        [pltpu.VMEM((inputs // n, cols_in, n), F32)],
    )(tab, x_own, x_oth, w_1p)
    xs, z_1b, s2, labels, k_1a, k_all, z_oth = stage(
        f2,
        [((rows + 1, COLS, 6 * n), BF16), maps(n), send(2 + (inputs + outer) // n),
         ((m, 1, n), F32), mean_scale(n, 2), mean_scale(n, norm_1a.shape[0]), wide_z],
    )(tab, g1, z_own, x_oth, w_1a, norm_1a, w_even, w_odd, stats_1p)
    g2 = gather(s2)
    act_1b, z_1c, s3, k_1b, k_p, sum_1b = stage(
        f3,
        [maps(n, BF16), maps(outer), send(1 + outer // n), mean_scale(n), mean_scale(outer),
         ((1, n), F32)],
    )(tab, g2, labels, z_1b, norm_1b, w_1c, w_1p)
    g3 = gather(s3)
    joined, slope, z_2a, stats_2a, k_cp = stage(
        f4, [maps(outer, BF16), maps(outer), maps(n), ((2, n), F32), mean_scale(outer, 2)]
    )(tab, g3, labels, z_1c, z_1p, norm_1c, norm_1p, k_p, w_1c, w_2a)
    share = -(-inputs // devices)
    half_in = ((rows, cols_in, n), BF16)
    share_1 = -(-n // devices)
    high = -(-(8 + 2 * share_1) // 16) * 16
    s4, slope_1b = stage(
        functools.partial(pair_1, share=share_1), [((devices, high, n), BF16), maps(n)],
        [scratch(2 * n, BF16), scratch(n, BF16)],
    )(tab, stats_2a, z_1b, norm_1b, k_1b, act_1b, sum_1b)
    s4, k_1a = tie(s4, k_1a)
    xz, x_sum = stage(
        g_xz, [((devices * share, n), F32), ((inputs, n), F32)],
        [pltpu.VMEM((rows, cols_in, 2 * n), BF16)],
    )(k_1a, x_own, x_oth, z_own, z_oth)
    s4, xz, x_sum = tie(s4, xz, x_sum)
    g4 = gather(s4)
    x3, z_2b, s5, k_2a = stage(
        f5, [((rows + 2, COLS, 3 * n), BF16), maps(n), send(2 + (share + 1) // 2), mean_scale(n)]
    )(tab, g4, labels, z_2a, norm_2a, w_two, w_last, xz)
    g5 = gather(s5)
    act_2b, z_2c, s6, k_2b = stage(
        f6, [maps(n, BF16), maps(outer), send(1 + outer // n), mean_scale(n)]
    )(tab, g5, labels, z_2b, norm_2b, w_2c)
    g6 = gather(s6)
    result, grad_pre, s7, k_2c = stage(
        b7, [(cotangent.shape[1:], BF16), maps(outer), send(2, outer), mean_scale(outer)],
        [pltpu.VMEM((COLS, outer), F32)],
    )(tab, g6, labels, joined, z_2c, norm_2c, w_2c, cotangent[0])
    g7 = gather(s7)
    dz_2c, dout_2b, s8, grad_norm_2c = stage(
        b8, [maps(outer, BF16), maps(n), send(2 + share // 2), *params(norm_2c)], [scratch(n)]
    )(tab, g7, labels, grad_pre, z_2c, norm_2c, k_2c, w_2c, z_2b, norm_2b, k_2b, xz)
    g8 = gather(s8)
    dz_2b, dout_2a, s9, grad_norm_2b = stage(
        functools.partial(b9, share=share_1),
        [maps(n, BF16), maps(n), ((devices, high, n), BF16), *params(norm_2b)],
        [pltpu.VMEM((rows + 2, COLS, 3 * n), BF16), scratch(n)],
    )(tab, g8, labels, dout_2b, z_2b, norm_2b, k_2b, b_two, b_last, z_2a, norm_2a, k_2a, x_sum, g4)
    g9 = gather(s9)
    dz_2a, grad_pre_2, s10, grad_norm_2a, d_1b = stage(
        b10,
        [maps(n, BF16), maps(outer), ((devices, 2, 3 * outer // 2 + n), F32), *params(norm_2a), maps(n)],
        [scratch(outer), scratch(outer, BF16)],
    )(tab, g9, labels, dout_2a, z_2a, norm_2a, k_2a, w_2a, grad_pre, slope, z_1c, z_1p, k_cp,
      norm_1c, w_1c, slope_1b, z_1b, k_1b)
    g10 = gather(s10)
    half_map = ((rows // 2, COLS, inputs), BF16)
    most_rows = sum(v.size for v in (w_2c, w_2b, w_2a, w_1c, w_1p)) // n
    rows_1b = w_1b.size // n
    piece = 16
    while -(-most_rows // (2 * piece)) - (-rows_1b // (2 * piece)) > devices:
        piece += 16
    first, second = -(-most_rows // (2 * piece)), -(-rows_1b // (2 * piece))
    part, part_1b = ((first, piece, n), BF16), ((second, piece, n), BF16)
    kept, sent, gs_own, gs_send, grad_norm_1c, grad_norm_1p, own10 = stage(
        g_most,
        [part, part, half_map, half_map, *params(norm_1c, norm_1p), ((1, 2 * outer + 2 * n), F32)],
        [pltpu.VMEM((2 * first * piece, n), BF16), scratch(outer, BF16), scratch(outer, BF16)],
    )(tab, act_2b, dz_2c, x3, dz_2b, joined, dz_2a, act_1b, xee, w_1p,
      g10, labels, norm_1c, norm_1p, k_cp, grad_pre_2, z_1c, z_1p)
    got, gs_for = swap(sent), swap(gs_send)
    half_in = ((rows, cols_in, n), BF16)
    d2, kept_1b, sent_1b, found_1b = stage(
        functools.partial(b12, share=share_1, q_at=4 + 2 * share_1, p_at=4 + 2 * (inputs // n)),
        [((rows + 1, COLS, 2 * n), BF16), part_1b, part_1b, ((2, n), F32)],
        [scratch(n, BF16), pltpu.VMEM((2 * second * piece, n), BF16), scratch(n)],
    )(tab, own10, labels, norm_1c, k_cp, w_1c, g3, g4, g9, act_1b, slope_1b, d_1b,
      z_1b, norm_1b, k_1b, xs)
    got_1b = swap(sent_1b)
    sides = []
    for own, z in ((False, z_oth), (True, z_own)):
        sides.append(
            stage(
                functools.partial(b12_images, own=own), [half_in, ((2, n), F32)],
                [pltpu.VMEM((rows // 2, COLS, 2 * n), F32), pltpu.VMEM((rows // 2, COLS, 2 * n), F32),
                 pltpu.VMEM((2, cols_in, n), F32)],
            )(tab, d2, b_even, b_odd, z, norm_1a, k_1a)
        )
        if not own:
            dn_for = swap(sides[0][0])
            d2, _ = tie(d2, sides[0][0])
    (dn_send, sums_send), (dn_own, sums_own) = sides
    stats_at = piece + -(-share // 8) * 8
    high = -(-(stats_at + 8) // 16) * 16
    tall, sums_1a = stage(
        g_xd, [((devices * share, n), BF16), ((2, n), F32)], [pltpu.VMEM(half_in[0], BF16)]
    )(tab, sums_own, sums_send, norm_1a, k_1a, x_sum, g9, labels, x_own, x_oth, dn_own, dn_send)
    tall, gs_for, dn_for = tie(tall, gs_for, dn_for)
    (s12,) = stage(
        functools.partial(pack_last, stats_at=stats_at), [((devices, high, n), BF16)]
    )(tall, sums_1a, found_1b, kept, got, kept_1b, got_1b)
    g12 = gather(s12)
    pixels = 4.0 * images.shape[1] * images.shape[1]
    batch = devices // 2
    far = batch // NEAR
    (mine,) = stage(
        functools.partial(add_all, at=stats_at, pixels=pixels),
        [((far, 2 * piece + share, n), BF16)],
    )(g12, labels, norm_1a, k_all, g5, g8)
    columns_of = [[k + NEAR * z for z in range(far)] for k in range(NEAR)]
    along = lax.all_to_all(mine, "batch", 0, 0, axis_index_groups=columns_of)
    near = [
        lax.ppermute(along, "batch", [(i, i ^ k) for i in range(batch)]) for k in range(1, NEAR)
    ]
    finished = (
        result, grad_norm_1c, grad_norm_1p, grad_norm_2a, grad_norm_2b, grad_norm_2c
    )
    held = len(finished)
    *finished, grad_images, grad_norm_1a, grad_norm_1b = stage(
        functools.partial(b13, at=stats_at, held=held),
        [*((v.shape, v.dtype) for v in finished), (images.shape, BF16), *params(norm_1a, norm_1b)],
        [pltpu.VMEM(half_in[0], BF16), pltpu.VMEM((inputs // n, rows, cols_in, n), F32),
         pltpu.VMEM(images.shape, BF16), *(pltpu.VMEM(norm_1a.shape, F32) for _ in range(2)),
         pltpu.SemaphoreType.DMA((held + 6,))],
        hbm_out=range(held + 3),
    )(tab, g12, labels, norm_1a, k_1a, w_1a, z_own, z_for, dn_own, dn_for, gs_own, gs_for, *finished)
    result, grad_norm_1c, grad_norm_1p, grad_norm_2a, grad_norm_2b, grad_norm_2c = finished
    *near, grad_images = tie(*near, grad_images)
    parts = [along, *near]
    weights = (w_2c, w_2b.reshape(-1, n), w_2a, w_1c, w_1p, w_1b.reshape(-1, n), w_1a)
    t_2c, t_2b, t_2a, t_1c, t_1p, t_1b, t_1a = stage(
        functools.partial(unpack, first=first, second=second, piece=piece),
        [(v.shape, F32) for v in weights],
        [*(pltpu.VMEM(v.shape, F32) for v in weights), pltpu.VMEM((devices, share, n), F32),
         pltpu.VMEM((2, devices, piece, n), BF16), pltpu.SemaphoreType.DMA((7,))],
        hbm_out=range(7),
    )(tab, *parts, *(swap(v) for v in parts))
    grads = (
        grad_norm_1a, grad_norm_1b, grad_norm_1c, grad_norm_1p,
        grad_norm_2a, grad_norm_2b, grad_norm_2c,
    )
    return (
        result[None], grad_images, t_1a, t_1b.reshape(w_1b.shape), t_1c, t_1p, t_2a,
        t_2b.reshape(w_2b.shape), t_2c, *[v.transpose(1, 0, 2) for v in grads],
    )


def solution(mesh):
    return jax.shard_map(
        body,
        mesh=mesh,
        in_specs=(
            P("batch", "rows", None, None),
            *[P()] * 14,
            P(("batch", "rows"), None, None, None),
            P("batch"),
            P(),
            P(),
        ),
        out_specs=(
            P(("batch", "rows"), None, None, None),
            P("batch", "rows", None, None),
            *[P()] * 14,
        ),
        check_vma=False,
    )
```

```python
import functools

import jax
import jax.numpy as jnp
from jax import lax
from jax.experimental import pallas as pl
from jax.experimental.pallas import tpu as pltpu
from jax.sharding import PartitionSpec as P

EPSILON = 1e-05
F32 = jnp.float32
BF16 = jnp.bfloat16
AXES = ("rows", "batch")
VMEM_LIMIT = 14 * 1024 * 1024
LANES = 128
COLS = 32
NEAR = 4


def full(memory=pltpu.VMEM):
    return pl.BlockSpec(memory_space=memory)


def stage(kernel, outs, scratch=(), hbm=(), hbm_out=()):
    def place(i, outside):
        return pltpu.HBM if i in outside else pltpu.VMEM

    def call(*args):
        args = [
            pltpu.with_memory_space_constraint(a, pltpu.HBM) if i in hbm else a
            for i, a in enumerate(args)
        ]
        return pl.pallas_call(
            kernel,
            out_shape=tuple(jax.ShapeDtypeStruct(s, d) for s, d in outs),
            in_specs=[full(place(i, hbm)) for i in range(len(args))],
            out_specs=tuple(
                full(place(i, hbm_out)) for i in range(len(outs))
            ),
            scratch_shapes=list(scratch),
            compiler_params=pltpu.CompilerParams(vmem_limit_bytes=VMEM_LIMIT),
            name=(kernel.func if isinstance(kernel, functools.partial) else kernel).__name__,
        )(*args)

    return call


def silu_of_half(u):
    return u + u * jnp.tanh(u)


def slope_of_half(u):
    t = jnp.tanh(u)
    return (0.5 + 0.5 * t) * (1.0 + u - u * t)


def fold(x):
    return (x[0:8] + x[8:16]) + (x[16:24] + x[24:32])


def row(total, stat):
    blocks = total.shape[0]
    pieces = [total[j : j + 1, LANES * stat : LANES * (stat + 1)] for j in range(blocks)]
    return pieces[0] if blocks == 1 else jnp.concatenate(pieces, axis=1)


def spread(out_ref, rows):
    blocks = out_ref.shape[1]
    for stat, values in enumerate(rows):
        for j in range(blocks):
            piece = values[:, LANES * j : LANES * (j + 1)]
            out_ref[:, j : j + 1, LANES * stat : LANES * (stat + 1)] = jnp.broadcast_to(
                piece[None], (out_ref.shape[0], 1, LANES)
            )


def group_sum(got_ref, labels, label):
    same = (labels == label).astype(F32)
    stats = got_ref.shape[2] // LANES
    parts = [
        jnp.sum(got_ref[:, :, LANES * s : LANES * (s + 1)] * same, axis=0) for s in range(stats)
    ]
    return jnp.concatenate(parts, axis=1) if stats > 1 else parts[0]


def group_count(labels, label):
    return jnp.sum((labels == label).astype(F32), axis=0)


def tiled(values, channels):
    return jnp.concatenate([values] * (channels // LANES), axis=1) if channels > LANES else values


def moments(first, second, pixels):
    mean = first / pixels
    return mean, lax.rsqrt(second / pixels - mean * mean + EPSILON)


def own_of(values, label):
    out = values[0]
    label = tiled(label, out.shape[1])
    for g in range(1, len(values)):
        out = jnp.where(label == float(g), values[g], out)
    return out


def gain_of(norm_ref, label):
    return own_of([norm_ref[g, 0:1, :] for g in range(norm_ref.shape[0])], label)


def shift_of(norm_ref, label):
    return own_of([norm_ref[g, 1:2, :] for g in range(norm_ref.shape[0])], label)


def valid_cols(channels):
    return lax.broadcasted_iota(jnp.int32, (COLS, channels), 0) < COLS - 4


def chan_mask(tab):
    return lax.broadcasted_iota(jnp.int32, (1, LANES), 1).astype(F32) < entry(tab, LIMIT)


def flat(x):
    return x.reshape(x.shape[0] * x.shape[1], x.shape[2])


def mm(a, b):
    return jnp.dot(a, b, preferred_element_type=F32)


def mm_nt(a, b):
    return lax.dot_general(a, b, (((1,), (1,)), ((), ())), preferred_element_type=F32)


def mm_tn(a, b):
    return lax.dot_general(a, b, (((0,), (0,)), ((), ())), preferred_element_type=F32)


def mm_side(a, b):
    turned = mm_tn(b, a)
    blocks = [
        jnp.transpose(turned[:, LANES * j : LANES * (j + 1)]) for j in range(a.shape[1] // LANES)
    ]
    return blocks[0] if len(blocks) == 1 else jnp.concatenate(blocks, axis=0)


def zeros8(channels):
    return jnp.zeros((8, channels), F32)


def down(x):
    return jnp.sum(x, axis=0, keepdims=True)


OWN, OTHER, HALF, LIMIT, GATE, MINOR = range(6)


def entry(tab, k):
    return tab[k : k + 1, :]


def half_of(tab, k=HALF):
    return (jnp.sum(entry(tab, k)) * (1.0 / LANES)).astype(jnp.int32)


def prepare(w1b, w2b, w_even, w_odd, w_two, w_last, b_even, b_odd, b_two, b_last):
    n = LANES
    for k, (y, x) in enumerate(((1, 1), (1, 2), (1, 0))):
        w_even[n * k : n * (k + 1), :] = w1b[y, x]
    for k, (low, high) in enumerate((((2, 1), (0, 1)), ((2, 2), (0, 2)), ((2, 0), (0, 0)))):
        w_odd[n * k : n * (k + 1), 0:n] = w1b[low]
        w_odd[n * k : n * (k + 1), n : 2 * n] = w1b[high]
    for x in range(3):
        w_two[n * x : n * (x + 1), 0:n] = w2b[0, x]
        w_two[n * x : n * (x + 1), n : 2 * n] = w2b[1, x]
        w_last[n * x : n * (x + 1), :] = w2b[2, x]
        b_two[0:n, n * x : n * (x + 1)] = w2b[1, x]
        b_two[n : 2 * n, n * x : n * (x + 1)] = w2b[2, x]
        b_last[:, n * x : n * (x + 1)] = w2b[0, x]
    nothing = jnp.zeros((n, n), BF16)
    b_even[0:n, 0:n] = w1b[1, 1]
    b_even[0:n, n : 2 * n] = nothing
    b_even[n : 2 * n, 0:n] = w1b[1, 2]
    b_even[n : 2 * n, n : 2 * n] = w1b[1, 0]
    for k, top in ((0, 2), (1, 0)):
        b_odd[0:n, 2 * n * k : 2 * n * k + n] = w1b[top, 1]
        b_odd[0:n, 2 * n * k + n : 2 * n * (k + 1)] = nothing
        b_odd[n : 2 * n, 2 * n * k : 2 * n * k + n] = w1b[top, 2]
        b_odd[n : 2 * n, 2 * n * k + n : 2 * n * (k + 1)] = w1b[top, 0]


def widen(source, x_pad):
    rows, cols, chans = source.shape
    gap = x_pad.shape[1] - cols

    def put(i, carry):
        x_pad[i, 0:cols, :] = source[i]
        x_pad[i, cols : cols + gap, :] = jnp.zeros((gap, chans), BF16)
        return carry

    lax.fori_loop(0, rows, put, 0, unroll=4)


def first_project(x_pad, w, z, stats=True):
    rows = x_pad.shape[0]
    step = rows // 4
    sums, squares = zeros8(LANES), zeros8(LANES)
    for c in range(4):
        values = mm(flat(x_pad[step * c : step * (c + 1)]), w[...])
        z[step * c : step * (c + 1)] = values.reshape(step, x_pad.shape[1], LANES)
        if stats:
            parts = values.reshape(-1, 8, LANES)
            sums = sums + jnp.sum(parts, axis=0)
            squares = squares + jnp.sum(parts * parts, axis=0)
    return sums, squares


def f1(
    place_at, group_at, width_at, gate_at, images, w_at, tab, x_own, x_for, z_own, z_for, send,
    place_ref, group, width, gate, raw, w, found, sems, *, batch,
):
    pairs = (
        (place_at, place_ref), (group_at, group), (width_at, width), (gate_at, gate), (w_at, w),
        (images.at[0], raw.at[0]), (images.at[1], raw.at[1]),
    )
    copies = [pltpu.make_async_copy(a, b, sems.at[k]) for k, (a, b) in enumerate(pairs)]
    for k in (0, 4, 5, 6, 1, 2, 3):
        copies[k].start()
    for k in (0, 4, 5):
        copies[k].wait()
    half = lax.div(place_ref[0], batch)
    sides = ((x_own, z_own), (x_for, z_for))

    def one(k):
        for place in (0, 1):

            @pl.when(half == place)
            def _():
                x_pad, z = sides[k] if place == 0 else sides[1 - k]
                widen(raw.at[k], x_pad)
                sums, squares = first_project(x_pad, w, z)
                at = 2 * (k if place == 0 else 1 - k)
                found[at : at + 1, :] = down(sums)
                found[at + 1 : at + 2, :] = down(squares)

    one(0)
    copies[6].wait()
    one(1)
    for k in (1, 2, 3):
        copies[k].wait()
    rows = [found[k : k + 1, :] for k in range(4)]
    own, other = group[half], group[1 - half]
    values = {
        OWN: own, OTHER: other, HALF: half, LIMIT: w.shape[1] // 4 * width[own], GATE: gate[own],
        MINOR: lax.rem(lax.rem(place_ref[0], batch), NEAR),
    }
    tab[...] = jnp.zeros(tab.shape, F32)
    for k, v in values.items():
        tab[k : k + 1, :] = jnp.full((1, LANES), v.astype(F32))
    spread(send, [*rows, jnp.full((1, LANES), (own + 4 * other).astype(F32))])


def f1_strided(tab, x_own, x_oth, w, xee, z, stats, wide):
    half = half_of(tab)
    rows = x_own.shape[0] // 2
    for k, x_pad in enumerate((x_own, x_oth)):
        first = rows * (half if k == 0 else 1 - half)

        def put(i, carry, x_pad=x_pad, first=first):
            for b in range(wide.shape[0]):
                lanes = slice(LANES * b, LANES * (b + 1))
                wide[b] = x_pad[2 * i, :, lanes].astype(F32)
                xee[first + i, :, lanes] = wide[b, pl.ds(0, COLS, stride=2), :].astype(BF16)
            return carry

        lax.fori_loop(0, rows, put, 0, unroll=2)
    total = 2 * rows
    step = total // 7
    chans = z.shape[2]
    squares = zeros8(chans)
    for c in range(7):
        values = mm(flat(xee[step * c : step * (c + 1)]), w[...])
        z[step * c : step * (c + 1)] = values.reshape(step, COLS, chans)
        parts = values.reshape(-1, 8, chans)
        squares = squares + jnp.sum(parts * parts, axis=0)
    ones = jnp.ones((8, total * COLS), BF16)
    stats[:, 0 : w.shape[0]] = mm(ones, flat(xee[...]))[0:1]
    stats[:, w.shape[0] :] = down(squares)


def scale_shift(got, labels, tab, norm, pixels, slot=0):
    label = entry(tab, OWN)
    total = group_sum(got, labels, label)
    chans = norm.shape[2]
    count = tiled(group_count(labels, label), chans) * pixels
    mean, rstd = moments(row(total, 2 * slot), row(total, 2 * slot + 1), count)
    gain, shift = gain_of(norm, entry(tab, OWN)), shift_of(norm, entry(tab, OWN))
    return mean, rstd, gain, shift, count


def conv_stats(z, source, pair, single, send, extra=()):
    keep = valid_cols(LANES)[None]
    rows = z.shape[0]
    step = rows // 4
    (lanes_2, w_2, offsets), (lanes_1, w_1, offset) = pair, single
    sums, squares = zeros8(LANES), zeros8(LANES)
    base = min(offsets)
    for c in range(4):
        at = step * c
        both = mm(flat(source[at + base : at + base + step + 1, :, lanes_2]), w_2)
        values = mm(flat(source[at + offset : at + offset + step, :, lanes_1]), w_1)
        for k, own in enumerate(offsets):
            skip = COLS * (own - base)
            values = values + both[skip : skip + step * COLS, LANES * k : LANES * (k + 1)]
        values = jnp.where(keep, values.reshape(step, COLS, LANES), 0.0)
        z[at : at + step] = values
        parts = values.reshape(-1, 8, LANES)
        sums = sums + jnp.sum(parts, axis=0)
        squares = squares + jnp.sum(parts * parts, axis=0)
    spread(send, [down(sums), down(squares), *extra])


def f2(
    tab, got, z_own, x_oth, w, norm, w_even, w_odd, stats_p,
    xs, z, send, labels, keeps, keeps_all, z_oth,
):
    codes = got[:, :, 4 * LANES : 5 * LANES]
    others = jnp.floor(0.25 * codes)
    marks = codes - 4.0 * others
    labels[...] = marks
    rows = xs.shape[0] - 1
    pixels = 4.0 * rows * (COLS - 4)
    first_project(x_oth, w, z_oth, False)
    for g in range(norm.shape[0]):
        mine, theirs = (marks == float(g)).astype(F32), (others == float(g)).astype(F32)
        totals = [
            jnp.sum(
                got[:, :, LANES * s : LANES * (s + 1)] * mine
                + got[:, :, LANES * (s + 2) : LANES * (s + 3)] * theirs,
                axis=0,
            )
            for s in (0, 1)
        ]
        mean, rstd = moments(*totals, group_count(marks, float(g)) * pixels)
        keeps_all[2 * g : 2 * g + 1, :] = mean
        keeps_all[2 * g + 1 : 2 * g + 2, :] = rstd
    for k, slot in enumerate((OWN, OTHER)):
        for q in (0, 1):
            choices = [keeps_all[2 * g + q : 2 * g + q + 1, :] for g in range(norm.shape[0])]
            keeps[2 * k + q : 2 * k + q + 1, :] = own_of(choices, entry(tab, slot))
    mean, rstd = keeps[0:1, :], keeps[1:2, :]
    gain, shift = gain_of(norm, entry(tab, OWN)), shift_of(norm, entry(tab, OWN))
    scale = rstd * gain
    bias = 0.5 * (shift - mean * scale)
    scale = 0.5 * scale
    keep = valid_cols(LANES) & chan_mask(tab)
    half = half_of(tab)
    xs[0] = jnp.zeros(xs.shape[1:], BF16)
    n = LANES
    for k, zz in enumerate((z_own, z_oth)):
        first = 1 + (rows // 2) * (half if k == 0 else 1 - half)

        def put(i, carry, zz=zz, first=first):
            lane = 0
            for a in (0, 1):
                for b in (0, 1):
                    u = zz[2 * i + a, pl.ds(b, COLS, stride=2), :] * scale + bias
                    act = jnp.where(keep, silu_of_half(u), 0.0)
                    xs[first + i, :, lane : lane + n] = act.astype(BF16)
                    lane += n
                    if b == 1:
                        moved = pltpu.roll(act, 1, 0)
                        xs[first + i, :, lane : lane + n] = moved.astype(BF16)
                        lane += n
            return carry

        lax.fori_loop(0, rows // 2, put, 0, unroll=2)
    extra = [stats_p[:, lanes] for lanes in columns(stats_p.shape[1])]
    pair = (slice(3 * n, 6 * n), w_odd[...], (1, 0))
    conv_stats(z, xs, pair, (slice(0, 3 * n), w_even[...], 1), send, extra)


def project(act, w, z):
    rows, chans = z.shape[0], z.shape[2]
    step = rows // 7
    squares = zeros8(chans)
    for c in range(7):
        values = mm(flat(act[step * c : step * (c + 1)]), w[...])
        z[step * c : step * (c + 1)] = values.reshape(step, COLS, chans)
        parts = values.reshape(-1, 8, chans)
        squares = squares + jnp.sum(parts * parts, axis=0)
    return down(squares)


def expand(act, w, z, send, act_sum):
    squares = project(act, w, z)
    spread(send, [act_sum, *(squares[:, lanes] for lanes in columns(z.shape[2]))])


def join(pieces):
    return pieces[0] if len(pieces) == 1 else jnp.concatenate(pieces, axis=1)


def columns(channels):
    return [slice(LANES * j, LANES * (j + 1)) for j in range(channels // LANES)]


def through(sums, w):
    high = sums.astype(BF16)
    rest = sums - high.astype(F32)
    mid = rest.astype(BF16)
    low = (rest - mid.astype(F32)).astype(BF16)
    lines = [v.astype(F32) for v in (high, mid, low)]
    lines.append(jnp.zeros((5, sums.shape[1]), F32))
    return down(mm(jnp.concatenate(lines, axis=0).astype(BF16), w))


def through_nt(sums, w):
    high = sums.astype(BF16)
    rest = sums - high.astype(F32)
    mid = rest.astype(BF16)
    low = (rest - mid.astype(F32)).astype(BF16)
    lines = [v.astype(F32) for v in (high, mid, low)]
    lines.append(jnp.zeros((5, sums.shape[1]), F32))
    return down(mm_nt(jnp.concatenate(lines, axis=0).astype(BF16), w))


def put_split(send, at, values):
    rows = values.shape[0]
    high = values.astype(BF16)
    rest = (values - high.astype(F32)).astype(BF16)
    for k, part in enumerate((high, rest)):
        send[:, at + rows * k : at + rows * (k + 1), :] = jnp.broadcast_to(
            part[None], (send.shape[0], rows, LANES)
        )


def get_split(got, at, rows):
    return got[:, at : at + rows, :].astype(F32) + got[:, at + rows : at + 2 * rows, :].astype(F32)


def over_group(values, marks, label):
    return jnp.sum(values * (marks == label).astype(F32), axis=0)


def stack(rows):
    return jnp.concatenate(rows, axis=0)


def pair_products(tab, z, norm, keeps, act, act_sum, slope, both, centred):
    rows = z.shape[0]
    label = entry(tab, OWN)
    mean, rstd = keeps[0:1, :], keeps[1:2, :]
    scale = rstd * gain_of(norm, label)
    bias = 0.5 * (shift_of(norm, label) - mean * scale)
    scale = 0.5 * scale
    keep = valid_cols(LANES) & chan_mask(tab)
    middle = act_sum * (1.0 / (rows * (COLS - 4)))

    def put(i, carry):
        zz = z[i]
        s = jnp.where(keep, slope_of_half(zz * scale + bias), 0.0)
        sx = s * ((zz - mean) * rstd)
        slope[i] = s
        both[i, :, 0:LANES] = s.astype(BF16)
        both[i, :, LANES:] = sx.astype(BF16)
        centred[i] = (act[i].astype(F32) - middle).astype(BF16)
        return carry[0] + fold(s), carry[1] + fold(sx)

    sums = lax.fori_loop(0, rows, put, (zeros8(LANES), zeros8(LANES)), unroll=4)
    return mm_tn(flat(centred[...]), flat(both[...])), stack([down(v) for v in sums])


def rows_of(line):
    return stack([line[:, lanes] for lanes in columns(line.shape[1])])


def line_of(rows):
    return join([rows[k : k + 1, :] for k in range(rows.shape[0])])


def put_pair(send, at, share, product):
    devices, n = send.shape[0], LANES
    missing = devices * share - n
    for h in (0, 1):
        values = product[:, n * h : n * (h + 1)]
        if missing:
            values = stack([values, jnp.zeros((missing, n), F32)])
        first = at + share * h
        send[:, first : first + share, :] = values.reshape(devices, share, n).astype(BF16)


def pass_pair(send, at, got, got_at, share, marks, groups):
    rows = got[:, got_at : got_at + 2 * share, :].astype(F32)
    out = None
    for g in range(groups):
        same = (marks == float(g)).astype(F32)
        term = jnp.sum(rows * same, axis=0)[None] * same
        out = term if out is None else out + term
    send[:, at : at + 2 * share, :] = out.astype(BF16)


def pair_solve(tab, marks, outer, inner, sums, w, act_sums, q_rows, p_rows, pixels):
    label, n = entry(tab, OWN), LANES
    (norm_o, keeps_o), (norm_i, keeps_i) = outer, inner
    shift_o, gain_o, shift_i, gain_i = sums
    images = group_count(marks, label)
    count, count_o = images * pixels, tiled(images, norm_o.shape[2]) * pixels
    rstd_o = keeps_o[1:2, :]
    a_o = rstd_o * gain_of(norm_o, label)
    b_o, c_o = -(a_o * rstd_o) * gain_o / count_o, -a_o * shift_o / count_o
    m = mm_nt((w[...].astype(F32) * b_o).astype(BF16), w[...]).astype(BF16)
    e = through_nt(c_o, w[...])
    same = (marks == label).astype(F32)
    middle = jnp.sum(act_sums * same, axis=0) / count
    spread_out = ((act_sums * (1.0 / pixels) - middle[None]) * same).reshape(-1, n).astype(BF16)
    share = p_rows.shape[1] // 2
    found = []
    for h, start in enumerate((shift_i, gain_i)):
        q = q_rows[:, h : h + 1, :]
        p = p_rows[:, share * h : share * (h + 1), :].reshape(-1, n)[0:n]
        p = p + mm_tn(spread_out, q.reshape(-1, n).astype(BF16))
        found.append(start + down(m.astype(F32) * p) + e * jnp.sum(q * same, axis=0))
    rstd_i = keeps_i[1:2, :]
    a = rstd_i * gain_of(norm_i, label)
    coefs = a, -(a * rstd_i) * found[1] / count, -a * found[0] / count
    return m, e - through(middle, m), coefs, found


def expanded_moments(got, labels, tab, w, pixels):
    label = entry(tab, OWN)
    total = group_sum(got, labels, label)
    chans = w.shape[1]
    count = tiled(group_count(labels, label), chans) * pixels
    return moments(through(total[:, 0:LANES], w[...]), total[:, LANES:], count)


def activate(tab, got, labels, z_in, norm, act, keeps):
    got = got.at[:, :, 0 : 2 * LANES]
    rows = z_in.shape[0]
    pixels = 1.0 * rows * (COLS - 4)
    mean, rstd, gain, shift, _ = scale_shift(got, labels[...], tab, norm, pixels)
    keeps[0:1, :] = mean
    keeps[1:2, :] = rstd
    scale = rstd * gain
    bias = 0.5 * (shift - mean * scale)
    scale = 0.5 * scale
    keep = valid_cols(LANES) & chan_mask(tab)

    def put(i, sums):
        low = jnp.where(keep, silu_of_half(z_in[i] * scale + bias), 0.0).astype(BF16)
        act[i] = low
        return sums + fold(low.astype(F32))

    return down(lax.fori_loop(0, rows, put, zeros8(LANES), unroll=7))


def f3(tab, got, labels, z_in, norm, w, w_p, act, z, send, keeps, keeps_p, act_sum):
    sums = activate(tab, got, labels, z_in, norm, act, keeps)
    act_sum[...] = sums
    expand(act, w, z, send, sums)
    marks, label = labels[...], entry(tab, OWN)
    total = group_sum(got, marks, label)
    outer, first = z.shape[2], 2 * LANES
    second = first + w_p.shape[0]
    count = tiled(group_count(marks, label), outer) * (1.0 * z.shape[0] * (COLS - 4))
    mean, rstd = moments(through(total[:, first:second], w_p[...]), total[:, second:], count)
    keeps_p[0:1, :] = mean
    keeps_p[1:2, :] = rstd


def f4(tab, got, labels, zc, zp, norm_c, norm_p, keeps_p, w_c, w, joined, slope, z, stats, keeps):
    rows, chans = zc.shape[0], zc.shape[2]
    pixels = 1.0 * rows * (COLS - 4)
    mean_c, rstd_c = expanded_moments(got, labels[...], tab, w_c, pixels)
    mean_p, rstd_p = keeps_p[0:1, :], keeps_p[1:2, :]
    for k, v in enumerate((mean_c, rstd_c, mean_p, rstd_p)):
        keeps[k : k + 1, :] = v
    group = entry(tab, OWN)
    scale_c = rstd_c * gain_of(norm_c, group)
    scale_p = rstd_p * gain_of(norm_p, group)
    bias = (shift_of(norm_c, group) - mean_c * scale_c) + (
        shift_of(norm_p, group) - mean_p * scale_p
    )
    keep = valid_cols(chans)
    scale_c, scale_p, bias = 0.5 * scale_c, 0.5 * scale_p, 0.5 * bias

    def put(i, carry):
        u = zc[i] * scale_c + zp[i] * scale_p + bias
        t = jnp.tanh(u)
        p = u * t
        joined[i] = jnp.where(keep, u + p, 0.0).astype(BF16)
        slope[i] = (0.5 + 0.5 * t) * (1.0 + u - p)
        return carry

    lax.fori_loop(0, rows, put, 0, unroll=4)
    step = rows // 4
    sums, squares = zeros8(LANES), zeros8(LANES)
    for c in range(4):
        values = mm(flat(joined[step * c : step * (c + 1)]), w[...])
        z[step * c : step * (c + 1)] = values.reshape(step, COLS, LANES)
        parts = values.reshape(-1, 8, LANES)
        sums = sums + jnp.sum(parts, axis=0)
        squares = squares + jnp.sum(parts * parts, axis=0)
    stats[0:1, :] = down(sums)
    stats[1:2, :] = down(squares)


def pair_1(tab, stats, z, norm, keeps, act, act_sum, send, slope, both, centred, *, share):
    product, sums = pair_products(tab, z, norm, keeps, act, act_sum[...], slope, both, centred)
    put_split(send, 0, stats[...])
    put_pair(send, 4, share, product)
    put_split(send, 4 + 2 * share, sums)


def put_shares(xz, send):
    n, devices = LANES, send.shape[0]
    share = xz.shape[0] // devices
    pieces = xz[...].reshape(devices, share, n)
    for q in range(share):
        send[:, :, n * (2 + q) : n * (3 + q)] = pieces[:, q : q + 1, :]


def f5(tab, got, labels, z_in, norm, w_two, w_last, xz, x3, z, send, keeps):
    rows = z_in.shape[0]
    pixels = 1.0 * rows * (COLS - 4)
    marks, label = labels[...], entry(tab, OWN)
    total = over_group(get_split(got, 0, 2), marks, label)
    mean, rstd = moments(total[0:1], total[1:2], group_count(marks, label) * pixels)
    gain, shift = gain_of(norm, label), shift_of(norm, label)
    keeps[0:1, :] = mean
    keeps[1:2, :] = rstd
    scale = rstd * gain
    bias = 0.5 * (shift - mean * scale)
    scale = 0.5 * scale
    keep = valid_cols(LANES) & chan_mask(tab)
    x3[0] = jnp.zeros(x3.shape[1:], BF16)
    x3[rows + 1] = jnp.zeros(x3.shape[1:], BF16)
    n = LANES

    def put(i, carry):
        act = jnp.where(keep, silu_of_half(z_in[i] * scale + bias), 0.0)
        x3[i + 1, :, 0:n] = pltpu.roll(act, 1, 0).astype(BF16)
        x3[i + 1, :, n : 2 * n] = act.astype(BF16)
        x3[i + 1, :, 2 * n : 3 * n] = pltpu.roll(act, COLS - 1, 0).astype(BF16)
        return carry

    lax.fori_loop(0, rows, put, 0, unroll=2)
    lanes = slice(0, 3 * n)
    conv_stats(
        z, x3, (lanes, w_two[...], (0, 1)), (lanes, w_last[...], 2), send.at[:, :, 0 : 2 * n]
    )
    put_shares(xz, send)


def f6(tab, got, labels, z_in, norm, w, act, z, send, keeps, slope, q, both, centred, *, share):
    sums = activate(tab, got, labels, z_in, norm, act, keeps)
    pixels = 1.0 * z.shape[0] * (COLS - 4)
    squares = project(act, w, z)
    first = through(sums, w[...])
    second = squares - first * first / pixels
    product, q[...] = pair_products(tab, z_in, norm, keeps, act, sums, slope, both, centred)
    put_split(send, 0, sums)
    low = rows_of(second).astype(BF16)
    send[:, 2 : 2 + low.shape[0], :] = jnp.broadcast_to(low[None], (send.shape[0], *low.shape))
    put_pair(send, 2 + low.shape[0], share, product)


def gathered_moments(got, marks, label, w, pixels):
    devices, chans = got.shape[0], w.shape[1]
    low = (got[:, k : k + 1, :].astype(F32).reshape(devices, LANES).astype(BF16) for k in (0, 1))
    means = sum(mm(v, w[...]) for v in low) * (1.0 / pixels)
    blocks = chans // LANES
    moments_2 = join(
        [got[:, 2 + k : 3 + k, :].astype(F32).reshape(devices, LANES) for k in range(blocks)]
    )
    same = join([(marks == label).astype(F32).reshape(devices, LANES)] * blocks)
    images = tiled(group_count(marks, label), chans)
    mean = down(means * same) / images
    away = means - mean
    variance = down((moments_2 + pixels * (away * away)) * same) / (images * pixels)
    return mean, lax.rsqrt(variance + EPSILON)


def b7(
    tab, got, labels, joined, z, norm, w, cot, slope_in, z_in, keeps_in, q,
    result, grad_pre, send, keeps, d_in, wide, low, *, share, p_at,
):
    rows, chans = z.shape[0], z.shape[2]
    cols = COLS - 4
    pixels = 1.0 * rows * cols
    marks, label = labels[...], entry(tab, OWN)
    mean, rstd = gathered_moments(got, marks, label, w, pixels)
    gain, shift = gain_of(norm, label), shift_of(norm, label)
    keeps[0:1, :] = mean
    keeps[1:2, :] = rstd
    gate = 0.25 * tiled(entry(tab, GATE), chans)
    scale = 0.5 * rstd * gain * gate
    bias = 0.5 * (shift - mean * rstd * gain) * gate
    wide[...] = jnp.zeros(wide.shape, F32)
    a_gate = rstd * gain * gate

    def put(i, carry):
        sums, products = carry
        wide[0:cols, :] = cot[i].astype(F32)
        zz = z[i]
        u = 0.5 * joined[i].astype(F32) + zz * scale + bias
        t = jnp.tanh(u)
        p = u * t
        result[i] = (u + p)[0:cols].astype(BF16)
        g = wide[...] * ((0.5 + 0.5 * t) * (1.0 + u - p))
        grad_pre[i] = g
        low[i] = (a_gate * g).astype(BF16)
        return sums + fold(g), products + fold(g * (zz - mean))

    start = zeros8(chans)
    sums, products = lax.fori_loop(0, rows, put, (start, start), unroll=2)
    inner = inner_sums(low, w, slope_in, z_in, keeps_in, d_in)
    blocks = chans // LANES
    put_split(send, 0, rows_of(down(sums) * gate))
    put_split(send, 2 * blocks, rows_of(down(products) * rstd * gate))
    put_split(send, 4 * blocks, stack(inner))
    put_split(send, 4 * blocks + 4, q[...])
    pass_pair(send, 4 * blocks + 8, got, p_at, share, marks, norm.shape[0])


def lane_sums(got, marks, channels):
    def sums_of(g):
        total = group_sum(got, marks, float(g))
        return row(total, 0), row(total, 1)

    return sums_of


def row_sums(got, marks):
    def sums_of(g):
        total = over_group(get_split(got, 0, 2), marks, float(g))
        return total[0:1], total[1:2]

    return sums_of


def backward_norm(tab, sums_of, marks, norm, keeps, pixels, grad_norm):
    group, chans = entry(tab, OWN), norm.shape[2]
    sums = [sums_of(g) for g in range(norm.shape[0])]
    for g, (shift_sum, gain_sum) in enumerate(sums):
        grad_norm[g, 0:1, :] = gain_sum
        grad_norm[g, 1:2, :] = shift_sum
    count = tiled(group_count(marks, group), chans) * pixels
    own_shift, own_gain = (own_of([v[k] for v in sums], group) for k in (0, 1))
    mean, rstd = keeps[0:1, :], keeps[1:2, :]
    a = rstd * gain_of(norm, group)
    return mean, a, -(a * rstd) * own_gain / count, -a * own_shift / count


def slope_sums(tab, d, z_in, norm, keeps, dout):
    rows = z_in.shape[0]
    mean, rstd = keeps[0:1, :], keeps[1:2, :]
    group = entry(tab, OWN)
    scale = rstd * gain_of(norm, group)
    bias = 0.5 * (shift_of(norm, group) - mean * scale)
    scale = 0.5 * scale
    keep = valid_cols(LANES) & chan_mask(tab)

    def put(i, carry):
        sums, products = carry
        zz = z_in[i]
        g = jnp.where(keep, d[i] * slope_of_half(zz * scale + bias), 0.0)
        dout[i] = g
        return sums + fold(g), products + fold(g * (zz - mean))

    sums, products = lax.fori_loop(
        0, rows, put, (zeros8(LANES), zeros8(LANES)), unroll=4
    )
    return down(sums), down(products) * rstd


def b9(
    tab, got, labels, norm_c, keeps_c, w_c, got_act, act, slope, d_in, z, norm, keeps,
    b_two, b_last, z_in, norm_in, keeps_in, x_sum, pair_got,
    dz, dout, send, own_sums, d3, d, *, share,
):
    rows = z.shape[0]
    pixels = 1.0 * rows * (COLS - 4)
    marks, label = labels[...], entry(tab, OWN)
    blocks = norm_c.shape[2] // LANES
    at = 4 * blocks
    wide = [
        line_of(over_group(get_split(got, 2 * blocks * k, blocks), marks, label)) for k in (0, 1)
    ]
    inner = over_group(get_split(got, at, 2), marks, label)
    m, line, (a, b, c), found = pair_solve(
        tab, marks, (norm_c, keeps_c), (norm, keeps), [*wide, inner[0:1], inner[1:2]], w_c,
        get_split(got_act, 0, 1), get_split(got, at + 4, 2),
        got[:, at + 8 : at + 8 + 2 * share, :].astype(F32), pixels,
    )
    own_sums[0:1, :] = found[0]
    own_sums[1:2, :] = found[1]
    inner_grad(act, m, line, slope, d_in, d)
    mean = keeps[0:1, :]
    keep = valid_cols(LANES)
    n = LANES
    d3[0] = jnp.zeros(d3.shape[1:], BF16)
    d3[rows + 1] = jnp.zeros(d3.shape[1:], BF16)

    def put(i, carry):
        v = a * d[i] + b * (z[i] - mean) + c
        v = jnp.where(keep, v, 0.0)
        d3[i + 1, :, 0:n] = pltpu.roll(v, COLS - 1, 0).astype(BF16)
        low = v.astype(BF16)
        d3[i + 1, :, n : 2 * n] = low
        dz[i] = low
        d3[i + 1, :, 2 * n : 3 * n] = pltpu.roll(v, 1, 0).astype(BF16)
        return carry

    lax.fori_loop(0, rows, put, 0, unroll=2)
    step = rows // 4
    for k in range(4):
        both = mm_nt(flat(d3[step * k : step * (k + 1) + 1]), b_two[...])
        value = mm_nt(flat(d3[step * k + 2 : step * (k + 1) + 2]), b_last[...])
        value = value + both[COLS:, 0:n] + both[0 : step * COLS, n : 2 * n]
        d[step * k : step * (k + 1)] = value.reshape(step, COLS, LANES)
    put_split(send, 0, stack(slope_sums(tab, d, z_in, norm_in, keeps_in, dout)))
    blocks = columns(x_sum.shape[0])
    put_split(send, 4, stack([jnp.transpose(x_sum[lanes, :])[0:1] for lanes in blocks]))
    pass_pair(send, 4 + 2 * len(blocks), pair_got, 4, share, marks, norm.shape[0])


def b10(
    tab, got, labels, dout_in, z, norm, keeps, w, grad_pre, slope, zc, zp, keeps_cp,
    norm_c, w_c, slope_in, z_in, keeps_in,
    dz, grad_pre_2, send, grad_norm, d_in, d, low,
):
    rows, chans = zc.shape[0], zc.shape[2]
    pixels = 1.0 * rows * (COLS - 4)
    marks = labels[...]
    coefs = backward_norm(tab, row_sums(got, marks), marks, norm, keeps, pixels, grad_norm)
    normed_grad(dz, dout_in, z, *coefs)
    d[...] = mm_nt(flat(dz[...]), w[...]).reshape(d.shape)
    mean_c, rstd_c, mean_p, rstd_p = (keeps_cp[k : k + 1, :] for k in range(4))
    a_c = rstd_c * gain_of(norm_c, entry(tab, OWN))

    def sum_up(i, carry):
        sums, prod_c, prod_p = carry
        g = (grad_pre[i] + d[i]) * slope[i]
        grad_pre_2[i] = g
        low[i] = (a_c * g).astype(BF16)
        return (
            sums + fold(g),
            prod_c + fold(g * (zc[i] - mean_c)),
            prod_p + fold(g * (zp[i] - mean_p)),
        )

    start = zeros8(chans)
    sums, prod_c, prod_p = lax.fori_loop(0, rows, sum_up, (start, start, start), unroll=2)
    wide = [down(sums), down(prod_c) * rstd_c, down(prod_p) * rstd_p]
    inner = inner_sums(low, w_c, slope_in, z_in, keeps_in, d_in)
    blocks = chans // LANES
    put_split(send, 0, rows_of(wide[0]))
    put_split(send, 2 * blocks, rows_of(wide[1]))
    put_split(send, 4 * blocks, stack(inner))
    last = rows_of(wide[2]).astype(BF16)
    send[:, 4 * blocks + 4 : 5 * blocks + 4, :] = jnp.broadcast_to(
        last[None], (send.shape[0], *last.shape)
    )


def inner_sums(low, w, slope, z, keeps, d_in):
    d_in[...] = mm_nt(flat(low[...]), w[...]).reshape(d_in.shape)
    mean, rstd = keeps[0:1, :], keeps[1:2, :]

    def add(i, carry):
        g = slope[i] * d_in[i]
        return carry[0] + fold(g), carry[1] + fold(g * (z[i] - mean))

    sums = lax.fori_loop(0, z.shape[0], add, (zeros8(LANES), zeros8(LANES)), unroll=7)
    return down(sums[0]), down(sums[1]) * rstd


def inner_grad(act, m, line, slope, d_in, d):
    d[...] = mm(flat(act[...]), m).reshape(d.shape)

    def put(i, carry):
        d[i] = slope[i] * (d_in[i] + d[i] + line)
        return carry

    lax.fori_loop(0, d.shape[0], put, 0, unroll=7)


def normed_grad(dz, dout, z, mean, a, b, c):
    keep = valid_cols(z.shape[2])

    def put(i, carry):
        v = a * dout[i] + b * (z[i] - mean) + c
        dz[i] = jnp.where(keep, v, 0.0).astype(BF16)
        return carry

    lax.fori_loop(0, z.shape[0], put, 0, unroll=2)


def b12(
    tab, own10, labels, norm_c, keeps_c, w_c, got_act, got_q, got_p, act, slope, d_in,
    z, norm, keeps, xs, d2, kept, sent, own_sums, dz, packed, dout, *, share, q_at, p_at,
):
    rows = z.shape[0]
    pixels = 1.0 * rows * (COLS - 4)
    outer, n = norm_c.shape[2], LANES
    marks = labels[...]
    total = own10[...]
    cuts = (0, outer, 2 * outer, 2 * outer + n, 2 * outer + 2 * n)
    m, line, (a, b, c), found = pair_solve(
        tab, marks, (norm_c, keeps_c.at[0:2]), (norm, keeps),
        [total[:, u:v] for u, v in zip(cuts, cuts[1:])], w_c, got_act[:, :, 0:n],
        get_split(got_q, q_at, 2), got_p[:, p_at : p_at + 2 * share, :].astype(F32), pixels,
    )
    own_sums[0:1, :] = found[0]
    own_sums[1:2, :] = found[1]
    inner_grad(act, m, line, slope, d_in, dout)
    mean = keeps[0:1, :]
    keep = valid_cols(LANES)
    d2[rows] = jnp.zeros(d2.shape[1:], BF16)

    def put(i, carry):
        v = a * dout[i] + b * (z[i] - mean) + c
        v = jnp.where(keep, v, 0.0)
        low = v.astype(BF16)
        dz[i] = low
        d2[i, :, 0:n] = low
        d2[i, :, n : 2 * n] = pltpu.roll(v, COLS - 1, 0).astype(BF16)
        return carry

    lax.fori_loop(0, rows, put, 0, unroll=4)
    low = flat(dz[...])
    cur = mm_side(flat(xs[1 : rows + 1]), low)
    for k, (y, x) in enumerate(((1, 1), (1, 2), (1, 0), (2, 1), (2, 2), (2, 0))):
        put_rows(packed, n * (3 * y + x), cur[n * k : n * (k + 1)])
    up = mm_side(flat(xs[0:rows, :, 3 * n : 6 * n]), low)
    for k, (y, x) in enumerate(((0, 1), (0, 2), (0, 0))):
        put_rows(packed, n * (3 * y + x), up[n * k : n * (k + 1)])
    share_out(tab, packed, 9 * n, kept, sent)


def b12_images(
    tab, d2, b_even, b_odd, zz, norm_in, keeps_in, dn, sums_out, de, do, wide, *, own
):
    rows = de.shape[0]
    n = LANES
    half = half_of(tab)
    first = rows * (half if own else 1 - half)
    step = rows // 2
    for k in range(2):
        here = flat(d2[pl.ds(first + step * k, step)])
        below = flat(d2[pl.ds(first + step * k + 1, step)])
        de[step * k : step * (k + 1)] = mm_nt(here, b_even[...]).reshape(step, COLS, 2 * n)
        odd = mm_nt(here, b_odd[:, 0 : 2 * n]) + mm_nt(below, b_odd[:, 2 * n : 4 * n])
        do[step * k : step * (k + 1)] = odd.reshape(step, COLS, 2 * n)
    mean_1, rstd_1 = keeps_in[0:1, :], keeps_in[1:2, :]
    group = entry(tab, OWN)
    scale = rstd_1 * gain_of(norm_in, group)
    bias = 0.5 * (shift_of(norm_in, group) - mean_1 * scale)
    scale = 0.5 * scale
    keep = valid_cols(LANES) & chan_mask(tab)

    def emit(i, carry):
        sums, products = carry
        for ra in (0, 1):
            planes = (de, do)[ra]
            for cb in (0, 1):
                zv = zz[2 * i + ra, pl.ds(cb, COLS, stride=2), :]
                g = planes[i, :, n * cb : n * (cb + 1)] * slope_of_half(zv * scale + bias)
                g = jnp.where(keep, g, 0.0)
                sums = sums + fold(g)
                products = products + fold(g * (zv - mean_1))
                wide[ra, pl.ds(cb, COLS, stride=2), :] = g
            dn[2 * i + ra] = wide[ra].astype(BF16)
        return sums, products

    totals = lax.fori_loop(0, rows, emit, (zeros8(n), zeros8(n)), unroll=2)
    sums_out[0:1, :] = down(totals[0])
    sums_out[1:2, :] = down(totals[1]) * rstd_1


def b13(
    tab, got, labels, norm, keeps, w, z_own, z_for, dn_own, dn_for, gs_own, gs_for, *rest, at, held
):
    finished, outs = rest[:held], rest[held : 2 * held]
    grad, grad_norm, grad_inner, dz, wide, grad_v, norm_v, inner_v, sems = rest[2 * held :]
    copies = [
        pltpu.make_async_copy(a, b, sems.at[k]) for k, (a, b) in enumerate(zip(finished, outs))
    ]
    for copy in copies:
        copy.start()
    rows, cols = grad.shape[1], grad.shape[2]
    half = half_of(tab)
    pixels = 2.0 * rows * cols
    marks = labels[...]
    totals = last_sums(got.at[:, at : at + 4, :], marks, norm.shape[0])
    for g in range(norm.shape[0]):
        norm_v[g, 0:1, :] = totals[g][1]
        norm_v[g, 1:2, :] = totals[g][0]
    norm_from_owners(get_split(got, at + 4, 2), marks, inner_v)
    for k, (value, out) in enumerate(((norm_v, grad_norm), (inner_v, grad_inner))):
        copies.append(pltpu.make_async_copy(value, out, sems.at[held + k]))
        copies[-1].start()
    keep = lax.broadcasted_iota(jnp.int32, (z_own.shape[1], LANES), 0) < cols
    for k, (z, dn, gs) in enumerate(((z_own, dn_own, gs_own), (z_for, dn_for, gs_for))):
        group = entry(tab, OWN if k == 0 else OTHER)
        shift_sum = own_of([t[0] for t in totals], group)
        gain_sum = own_of([t[1] for t in totals], group)
        count = group_count(marks, group) * pixels
        mean, rstd = keeps[2 * k : 2 * k + 1, :], keeps[2 * k + 1 : 2 * k + 2, :]
        a = rstd * gain_of(norm, group)
        b = -(a * rstd) * gain_sum / count
        c = -a * shift_sum / count

        def put(i, carry, z=z, dn=dn, mean=mean, a=a, b=b, c=c):
            v = a * dn[i].astype(F32) + b * (z[i] - mean) + c
            dz[i] = jnp.where(keep, v, 0.0).astype(BF16)
            return carry

        lax.fori_loop(0, rows, put, 0, unroll=4)
        place = half if k == 0 else 1 - half
        step = rows // 2
        for q in range(2):
            low = flat(dz[step * q : step * (q + 1)])
            for p in range(wide.shape[0]):
                values = mm_nt(low, w[LANES * p : LANES * (p + 1), :])
                wide[p, step * q : step * (q + 1)] = values.reshape(step, -1, LANES)

            def emit(i, carry, gs=gs, place=place):
                even = pl.ds(0, COLS, stride=2)
                for p in range(wide.shape[0]):
                    lanes = slice(LANES * p, LANES * (p + 1))
                    wide[p, 2 * i, even, :] = wide[p, 2 * i, even, :] + gs[i, :, lanes].astype(F32)
                    grad_v[place, 2 * i, :, lanes] = wide[p, 2 * i, 0:cols, :].astype(BF16)
                    grad_v[place, 2 * i + 1, :, lanes] = wide[p, 2 * i + 1, 0:cols, :].astype(BF16)
                return carry

            lax.fori_loop(step // 2 * q, step // 2 * (q + 1), emit, 0, unroll=True)
            part = pl.ds(step * q, step)
            copies.append(
                pltpu.make_async_copy(
                    grad_v.at[place, part], grad.at[place, part], sems.at[held + 2 + 2 * k + q]
                )
            )
            copies[-1].start()
    for copy in copies:
        copy.wait()


def put_rows(out, at, value):
    for j in range(value.shape[1] // LANES):
        out[at : at + value.shape[0], :] = value[:, LANES * j : LANES * (j + 1)].astype(BF16)
        at += value.shape[0]
    return at


def take_rows(source, at, out):
    rows = out.shape[0]
    for j in range(out.shape[1] // LANES):
        out[:, LANES * j : LANES * (j + 1)] = source(at, rows)
        at += rows
    return at


def share_out(tab, packed, used, kept, sent):
    if used < packed.shape[0]:
        packed[used:, :] = jnp.zeros((packed.shape[0] - used, LANES), BF16)
    half = half_of(tab)
    size = kept.shape[0] * kept.shape[1]
    for out, place in ((kept, half), (sent, 1 - half)):
        out[...] = packed[pl.ds(pl.multiple_of(size * place, 16), size), :].reshape(out.shape)


def g_most(
    tab, act_2b, x3, dz_2b, joined, dz_2a, act_1b, xee, w_p,
    got, labels, norm_c, norm_p, keeps, grad_pre_2, zc, zp,
    got_2c, norm_2c, keeps_2c, grad_pre, z_2c,
    kept, sent, gs_own, gs_oth, grad_norm_c, grad_norm_p, grad_norm_2c, own10, packed, dz_1c, dz_p, dz_2c,
):
    rows, outer = dz_2b.shape[0], zc.shape[2]
    pixels = 1.0 * rows * (COLS - 4)
    marks = labels[...]

    blocks = outer // LANES
    label = entry(tab, OWN)

    def wide_sums(source, count):
        values = [get_split(source, 2 * blocks * k, blocks) for k in range(count)]
        return [
            [line_of(over_group(v, marks, float(g))) for v in values]
            for g in range(norm_c.shape[0])
        ]

    lines = wide_sums(got, 2)
    last = got[:, 4 * blocks + 4 : 5 * blocks + 4, :].astype(F32)
    for g, line in enumerate(lines):
        line.append(line_of(over_group(last, marks, float(g))))
    for k in range(2):
        own10[:, outer * k : outer * (k + 1)] = own_of([v[k] for v in lines], label)
    inner = over_group(get_split(got, 4 * blocks, 2), marks, label)
    for k in range(2):
        at = 2 * outer + LANES * k
        own10[:, at : at + LANES] = inner[k : k + 1]
    lines_2c = wide_sums(got_2c, 2)
    mean, a, b, c = backward_norm(
        tab, lambda g: (lines_2c[g][0], lines_2c[g][1]), marks, norm_2c, keeps_2c, pixels,
        grad_norm_2c,
    )
    gate = 0.25 * tiled(entry(tab, GATE), outer)
    normed_grad(dz_2c, grad_pre, z_2c, mean, a * gate, b, c)
    coefs = backward_norm(
        tab, lambda g: (lines[g][0], lines[g][1]), marks, norm_c, keeps.at[0:2], pixels, grad_norm_c
    )
    normed_grad(dz_1c, grad_pre_2, zc, *coefs)
    coefs = backward_norm(
        tab, lambda g: (lines[g][0], lines[g][2]), marks, norm_p, keeps.at[2:4], pixels, grad_norm_p
    )
    normed_grad(dz_p, grad_pre_2, zp, *coefs)
    at = put_rows(packed, 0, mm_tn(flat(act_2b[...]), flat(dz_2c[...])))
    low = flat(dz_2b[...])
    for y in range(3):
        at = put_rows(packed, at, mm_side(flat(x3[y : y + rows]), low))
    at = put_rows(packed, at, mm_side(flat(joined[...]), flat(dz_2a[...])))
    at = put_rows(packed, at, mm_tn(flat(act_1b[...]), flat(dz_1c[...])))
    at = put_rows(packed, at, mm_tn(flat(xee[...]), flat(dz_p[...])))
    share_out(tab, packed, at, kept, sent)
    half = half_of(tab)
    count = gs_own.shape[0]
    for k, gs in enumerate((gs_own, gs_oth)):
        first = count * (half if k == 0 else 1 - half)
        got = mm_nt(flat(dz_p[pl.ds(first, count)]), w_p[...])
        gs[...] = got.reshape(gs.shape).astype(BF16)


def g_xz(keeps, x_own, x_oth, z_own, z_oth, out, x_sum, low):
    rows, n = z_own.shape[0], LANES
    mean = keeps[0:1, :]
    low[:, :, n : 2 * n] = jnp.ones((rows, z_own.shape[1], n), BF16)
    value = None
    for x, z in ((x_own, z_own), (x_oth, z_oth)):

        def put(i, carry, z=z):
            low[i, :, 0:n] = (z[i] - mean).astype(BF16)
            return carry

        lax.fori_loop(0, rows, put, 0, unroll=4)
        term = mm_tn(flat(x[...]), flat(low[...]))
        value = term if value is None else value + term
    at = value.shape[0]
    out[0:at, :] = value[:, 0:n]
    if at < out.shape[0]:
        out[at:, :] = jnp.zeros((out.shape[0] - at, n), F32)
    x_sum[...] = value[:, n : 2 * n]


def g_xd(
    tab, sums_own, sums_oth, norm, keeps, x_sum, got_x, labels, x_own, x_oth, dn_own, dn_oth,
    out, sums, low,
):
    rows = dn_own.shape[0]
    n = LANES
    pixels = 1.0 * (2 * rows) * (2 * (COLS - 4))
    sums[...] = sums_own[...] + sums_oth[...]
    a = keeps[1:2, :] * gain_of(norm, entry(tab, OWN))
    local = sums[0:1, :] / pixels
    value = None
    for x, dn in ((x_own, dn_own), (x_oth, dn_oth)):

        def put(i, carry, dn=dn):
            low[i] = (a * (dn[i].astype(F32) - local)).astype(BF16)
            return carry

        lax.fori_loop(0, rows, put, 0, unroll=4)
        term = mm_tn(flat(x[...]), flat(low[...]))
        value = term if value is None else value + term
    marks, label = labels[...], entry(tab, OWN)
    total = over_group(get_split(got_x, 4, x_sum.shape[0] // n), marks, label)
    total = join([total[k : k + 1] for k in range(total.shape[0])])
    total = total / tiled(group_count(marks, label), total.shape[1])
    total = jnp.broadcast_to(total, (8, total.shape[1]))
    means = jnp.concatenate(
        [jnp.transpose(total[:, lanes])[:, 0:1] for lanes in columns(total.shape[1])], axis=0
    )
    value = value + (x_sum[...] - means) * (a * local)
    at = value.shape[0]
    out[0:at, :] = value.astype(BF16)
    if at < out.shape[0]:
        out[at:, :] = jnp.zeros((out.shape[0] - at, n), BF16)


def pack_last(tall, sums, found, kept, got, kept_1b, got_1b, send, *, stats_at):
    n = LANES
    devices = send.shape[0]
    piece, share = kept.shape[1], tall.shape[0] // devices
    first = kept.shape[0]
    second = first + kept_1b.shape[0]
    send[0:first, 0:piece, :] = (kept[...].astype(F32) + got[...].astype(F32)).astype(BF16)
    send[first:second, 0:piece, :] = (kept_1b[...].astype(F32) + got_1b[...].astype(F32)).astype(BF16)
    if second < devices:
        send[second:, 0:piece, :] = jnp.zeros((devices - second, piece, n), BF16)
    send[:, piece : piece + share, :] = tall[...].reshape(devices, share, n)
    put_split(send, stats_at, sums[...])
    put_split(send, stats_at + 4, found[...])


def last_sums(stats, marks, groups):
    values = stats[:, 0:2, :].astype(F32) + stats[:, 2:4, :].astype(F32)
    out = []
    for g in range(groups):
        total = jnp.sum(values * (marks == float(g)).astype(F32), axis=0)
        out.append((total[0:1], total[1:2]))
    return out


def add_all(got, labels, norm, keeps_all, xz_got, found, out, *, at, pixels):
    devices, n = got.shape[0], LANES
    half = devices // 2
    share = xz_got.shape[2] // n - 2
    piece = (out.shape[1] - share - 4) // 2
    marks = labels[...]
    value = jnp.sum(got[:, piece : piece + share, :].astype(F32), axis=0)
    sums = last_sums(got.at[:, at : at + 4, :], marks, norm.shape[0])
    for g in range(norm.shape[0]):
        rstd = keeps_all[2 * g + 1 : 2 * g + 2, :]
        count = group_count(marks, float(g)) * pixels
        b = -(rstd * rstd * norm[g, 0:1, :]) * sums[g][1] / count
        same = (marks == float(g)).astype(F32)
        rows = [
            jnp.sum(xz_got[:, :, n * (2 + q) : n * (3 + q)] * same, axis=0) for q in range(share)
        ]
        value = value + jnp.concatenate(rows, axis=0) * b
    for k in (0, 1):
        total = jnp.sum(got[half * k : half * (k + 1), 0:piece, :].astype(F32), axis=0).astype(BF16)
        out[:, piece * k : piece * (k + 1), :] = jnp.broadcast_to(
            total[None], (out.shape[0], piece, n)
        )
    out[:, 2 * piece : 2 * piece + share, :] = jnp.broadcast_to(
        value.astype(BF16)[None], (out.shape[0], share, n)
    )
    put_split(out, 2 * piece + share, found[...])


def unpack(tab, labels, *refs, first, second, piece):
    parts, outs, values = refs[: 2 * NEAR], refs[2 * NEAR : 2 * NEAR + 8], refs[2 * NEAR + 8 :]
    *values, tall, packed, found, sems = values
    half, minor = half_of(tab), half_of(tab, MINOR)
    far, share = parts[0].shape[0], tall.shape[1]
    for k, part in enumerate(parts):
        core = half if k < NEAR else 1 - half
        base = core * (far * NEAR) + lax.bitwise_xor(minor, jnp.int32(k % NEAR))

        def place(z, carry, part=part, base=base):
            owner = base + NEAR * z
            for h in (0, 1):
                packed[h, owner] = part[z, piece * h : piece * (h + 1), :]
            tall[owner] = part[z, 2 * piece : 2 * piece + share, :].astype(F32)
            sums = part[z, 2 * piece + share :, :].astype(F32)
            found[owner] = sums[0:2] + sums[2:4]
            return carry

        lax.fori_loop(0, far, place, 0, unroll=min(far, 4))
    copies = [
        pltpu.make_async_copy(value, out, sems.at[k]) for k, (value, out) in enumerate(zip(values, outs))
    ]
    most = [flat(packed[h, 0:first]) for h in (0, 1)]
    last = [flat(packed[h, first : first + second]) for h in (0, 1)]
    size = first * piece

    def source(at, rows):
        pieces = []
        if at < size:
            pieces.append(most[0][at : min(at + rows, size)])
        if at + rows > size:
            pieces.append(most[1][max(at - size, 0) : at + rows - size])
        pieces = [v.astype(F32) for v in pieces]
        return pieces[0] if len(pieces) == 1 else stack(pieces)

    at = 0
    for k, value in enumerate(values[0:5]):
        at = take_rows(source, at, value)
        copies[k].start()
    w_1b, w_1a, grad_norm = values[5:8]
    size = second * piece
    w_1b[0:size] = last[0].astype(F32)
    w_1b[size:] = last[1][0 : w_1b.shape[0] - size].astype(F32)
    copies[5].start()
    w_1a[...] = flat(tall[...])[0 : w_1a.shape[0]]
    copies[6].start()
    norm_from_owners(found[...], labels[...], grad_norm)
    copies[7].start()
    for copy in copies:
        copy.wait()


def norm_from_owners(found, marks, grad_norm):
    for g in range(grad_norm.shape[0]):
        total = over_group(found, marks, float(g)) / group_count(marks, float(g))
        grad_norm[g, 0:1, :] = total[1:2]
        grad_norm[g, 1:2, :] = total[0:1]


def gather(send):
    return lax.all_to_all(send, AXES, 0, 0)


def tie(*values):
    return lax.optimization_barrier(values)


def swap(block):
    return lax.ppermute(block, "rows", [(0, 1), (1, 0)])


def body(
    images, w_1a, w_1b, w_1c, w_1p, w_2a, w_2b, w_2c,
    norm_1a, norm_1b, norm_1c, norm_1p, norm_2a, norm_2b, norm_2c,
    cotangent, group, width, gate,
):
    devices = lax.axis_size("rows") * lax.axis_size("batch")
    place = lax.axis_index(AXES).astype(jnp.int32).reshape(1)
    norms = (norm_1a, norm_1b, norm_1c, norm_1p, norm_2a, norm_2b, norm_2c)
    norm_1a, norm_1b, norm_1c, norm_1p, norm_2a, norm_2b, norm_2c = (
        v.transpose(1, 0, 2) for v in norms
    )
    outer, inputs = w_1c.shape[1], w_1a.shape[0]
    rows = cotangent.shape[1]
    cols_in = 2 * COLS
    n, m = LANES, devices

    def send(stats, channels=LANES):
        return ((m, channels // LANES, stats * LANES), F32)

    def maps(channels, dtype=F32):
        return ((rows, COLS, channels), dtype)

    def scratch(channels, dtype=F32):
        return pltpu.VMEM((rows, COLS, channels), dtype)

    def params(*arrays):
        return [(a.shape, F32) for a in arrays]

    def mean_scale(channels, count=1):
        return ((2 * count, channels), F32)

    wide_in = ((rows, cols_in, inputs), BF16)
    wide_z = ((rows, cols_in, n), F32)
    raw = images.shape
    tab, x_own, x_for, z_own, z_for, s1 = stage(
        functools.partial(f1, batch=devices // 2), [((8, n), F32), wide_in, wide_in, wide_z, wide_z, send(5)],
        [*(pltpu.SMEM(v.shape, jnp.int32) for v in (place, group, width, gate)),
         pltpu.VMEM(raw, BF16), pltpu.VMEM(w_1a.shape, BF16), pltpu.VMEM((8, n), F32),
         pltpu.SemaphoreType.DMA((7,))],
        hbm=(0, 1, 2, 3, 4, 5),
    )(place, group, width, gate, images, w_1a)
    s1, v_1b, v_2b = tie(s1, w_1b, w_2b)
    built = stage(
        prepare,
        [(v, BF16) for v in (
            (3 * n, n), (3 * n, 2 * n), (3 * n, 2 * n), (3 * n, n),
            (2 * n, 2 * n), (2 * n, 4 * n), (2 * n, 3 * n), (n, 3 * n),
        )],
    )(v_1b, v_2b)
    s1, x_for, w_even, w_odd, w_two, w_last, b_even, b_odd, b_two, b_last = tie(s1, x_for, *built)
    x_oth = swap(x_for)
    g1 = gather(s1)
    g1, x_oth = tie(g1, x_oth)
    xee, z_1p, stats_1p = stage(
        f1_strided,
        [maps(inputs, BF16), maps(outer), ((1, inputs + outer), F32)],
        [pltpu.VMEM((inputs // n, cols_in, n), F32)],
    )(tab, x_own, x_oth, w_1p)
    xs, z_1b, s2, labels, k_1a, k_all, z_oth = stage(
        f2,
        [((rows + 1, COLS, 6 * n), BF16), maps(n), send(2 + (inputs + outer) // n),
         ((m, 1, n), F32), mean_scale(n, 2), mean_scale(n, norm_1a.shape[0]), wide_z],
    )(tab, g1, z_own, x_oth, w_1a, norm_1a, w_even, w_odd, stats_1p)
    g2 = gather(s2)
    act_1b, z_1c, s3, k_1b, k_p, sum_1b = stage(
        f3,
        [maps(n, BF16), maps(outer), send(1 + outer // n), mean_scale(n), mean_scale(outer),
         ((1, n), F32)],
    )(tab, g2, labels, z_1b, norm_1b, w_1c, w_1p)
    g3 = gather(s3)
    joined, slope, z_2a, stats_2a, k_cp = stage(
        f4, [maps(outer, BF16), maps(outer), maps(n), ((2, n), F32), mean_scale(outer, 2)]
    )(tab, g3, labels, z_1c, z_1p, norm_1c, norm_1p, k_p, w_1c, w_2a)
    share = -(-inputs // devices)
    half_in = ((rows, cols_in, n), BF16)
    share_1 = -(-n // devices)
    high = -(-(8 + 2 * share_1) // 16) * 16
    s4, slope_1b = stage(
        functools.partial(pair_1, share=share_1), [((devices, high, n), BF16), maps(n)],
        [scratch(2 * n, BF16), scratch(n, BF16)],
    )(tab, stats_2a, z_1b, norm_1b, k_1b, act_1b, sum_1b)
    s4, k_1a = tie(s4, k_1a)
    xz, x_sum = stage(
        g_xz, [((devices * share, n), F32), ((inputs, n), F32)],
        [pltpu.VMEM((rows, cols_in, 2 * n), BF16)],
    )(k_1a, x_own, x_oth, z_own, z_oth)
    s4, xz, x_sum = tie(s4, xz, x_sum)
    g4 = gather(s4)
    x3, z_2b, s5, k_2a = stage(
        f5, [((rows + 2, COLS, 3 * n), BF16), maps(n), send(2 + share), mean_scale(n)]
    )(tab, g4, labels, z_2a, norm_2a, w_two, w_last, xz)
    g5 = gather(s5)
    wide_rows = outer // n
    p_6 = 2 + wide_rows
    high_6 = -(-(p_6 + 2 * share_1) // 16) * 16
    act_2b, z_2c, s6, k_2b, slope_2b, q_2b = stage(
        functools.partial(f6, share=share_1),
        [maps(n, BF16), maps(outer), ((devices, high_6, n), BF16), mean_scale(n), maps(n),
         ((2, n), F32)],
        [scratch(2 * n, BF16), scratch(n, BF16)],
    )(tab, g5, labels, z_2b, norm_2b, w_2c)
    g6 = gather(s6)
    high_7 = -(-(4 * wide_rows + 8 + 2 * share_1) // 16) * 16
    result, grad_pre, s7, k_2c, d_2b = stage(
        functools.partial(b7, share=share_1, p_at=p_6),
        [(cotangent.shape[1:], BF16), maps(outer), ((devices, high_7, n), BF16),
         mean_scale(outer), maps(n)],
        [pltpu.VMEM((COLS, outer), F32), scratch(outer, BF16)],
    )(tab, g6, labels, joined, z_2c, norm_2c, w_2c, cotangent[0], slope_2b, z_2b, k_2b, q_2b)
    g7 = gather(s7)
    dz_2b, dout_2a, s9, found_2b = stage(
        functools.partial(b9, share=share_1),
        [maps(n, BF16), maps(n), ((devices, high, n), BF16), ((2, n), F32)],
        [pltpu.VMEM((rows + 2, COLS, 3 * n), BF16), scratch(n)],
    )(tab, g7, labels, norm_2c, k_2c, w_2c, g6, act_2b, slope_2b, d_2b, z_2b, norm_2b, k_2b,
      b_two, b_last, z_2a, norm_2a, k_2a, x_sum, g4)
    g9 = gather(s9)
    dz_2a, grad_pre_2, s10, grad_norm_2a, d_1b = stage(
        b10,
        [maps(n, BF16), maps(outer), ((devices, 5 * wide_rows + 4, n), BF16), *params(norm_2a), maps(n)],
        [scratch(outer), scratch(outer, BF16)],
    )(tab, g9, labels, dout_2a, z_2a, norm_2a, k_2a, w_2a, grad_pre, slope, z_1c, z_1p, k_cp,
      norm_1c, w_1c, slope_1b, z_1b, k_1b)
    g10 = gather(s10)
    half_map = ((rows // 2, COLS, inputs), BF16)
    most_rows = sum(v.size for v in (w_2c, w_2b, w_2a, w_1c, w_1p)) // n
    rows_1b = w_1b.size // n
    piece = 16
    while -(-most_rows // (2 * piece)) - (-rows_1b // (2 * piece)) > devices:
        piece += 16
    first, second = -(-most_rows // (2 * piece)), -(-rows_1b // (2 * piece))
    part, part_1b = ((first, piece, n), BF16), ((second, piece, n), BF16)
    kept, sent, gs_own, gs_send, grad_norm_1c, grad_norm_1p, grad_norm_2c, own10 = stage(
        g_most,
        [part, part, half_map, half_map, *params(norm_1c, norm_1p, norm_2c),
         ((1, 2 * outer + 2 * n), F32)],
        [pltpu.VMEM((2 * first * piece, n), BF16), *(scratch(outer, BF16) for _ in range(3))],
    )(tab, act_2b, x3, dz_2b, joined, dz_2a, act_1b, xee, w_1p,
      g10, labels, norm_1c, norm_1p, k_cp, grad_pre_2, z_1c, z_1p,
      g7, norm_2c, k_2c, grad_pre, z_2c)
    got, gs_for = swap(sent), swap(gs_send)
    half_in = ((rows, cols_in, n), BF16)
    d2, kept_1b, sent_1b, found_1b = stage(
        functools.partial(b12, share=share_1, q_at=4 + 2 * share_1, p_at=4 + 2 * (inputs // n)),
        [((rows + 1, COLS, 2 * n), BF16), part_1b, part_1b, ((2, n), F32)],
        [scratch(n, BF16), pltpu.VMEM((2 * second * piece, n), BF16), scratch(n)],
    )(tab, own10, labels, norm_1c, k_cp, w_1c, g3, g4, g9, act_1b, slope_1b, d_1b,
      z_1b, norm_1b, k_1b, xs)
    got_1b = swap(sent_1b)
    sides = []
    for own, z in ((False, z_oth), (True, z_own)):
        sides.append(
            stage(
                functools.partial(b12_images, own=own), [half_in, ((2, n), F32)],
                [pltpu.VMEM((rows // 2, COLS, 2 * n), F32), pltpu.VMEM((rows // 2, COLS, 2 * n), F32),
                 pltpu.VMEM((2, cols_in, n), F32)],
            )(tab, d2, b_even, b_odd, z, norm_1a, k_1a)
        )
        if not own:
            dn_for = swap(sides[0][0])
            d2, _ = tie(d2, sides[0][0])
    (dn_send, sums_send), (dn_own, sums_own) = sides
    stats_at = piece + -(-share // 8) * 8
    high = -(-(stats_at + 8) // 16) * 16
    tall, sums_1a = stage(
        g_xd, [((devices * share, n), BF16), ((2, n), F32)], [pltpu.VMEM(half_in[0], BF16)]
    )(tab, sums_own, sums_send, norm_1a, k_1a, x_sum, g9, labels, x_own, x_oth, dn_own, dn_send)
    tall, gs_for, dn_for = tie(tall, gs_for, dn_for)
    (s12,) = stage(
        functools.partial(pack_last, stats_at=stats_at), [((devices, high, n), BF16)]
    )(tall, sums_1a, found_1b, kept, got, kept_1b, got_1b)
    g12 = gather(s12)
    pixels = 4.0 * images.shape[1] * images.shape[1]
    batch = devices // 2
    far = batch // NEAR
    (mine,) = stage(
        functools.partial(add_all, at=stats_at, pixels=pixels),
        [((far, 2 * piece + share + 4, n), BF16)],
    )(g12, labels, norm_1a, k_all, g5, found_2b)
    columns_of = [[k + NEAR * z for z in range(far)] for k in range(NEAR)]
    along = lax.all_to_all(mine, "batch", 0, 0, axis_index_groups=columns_of)
    near = [
        lax.ppermute(along, "batch", [(i, i ^ k) for i in range(batch)]) for k in range(1, NEAR)
    ]
    finished = (
        result, grad_norm_1c, grad_norm_1p, grad_norm_2a, grad_norm_2c
    )
    held = len(finished)
    *finished, grad_images, grad_norm_1a, grad_norm_1b = stage(
        functools.partial(b13, at=stats_at, held=held),
        [*((v.shape, v.dtype) for v in finished), (images.shape, BF16), *params(norm_1a, norm_1b)],
        [pltpu.VMEM(half_in[0], BF16), pltpu.VMEM((inputs // n, rows, cols_in, n), F32),
         pltpu.VMEM(images.shape, BF16), *(pltpu.VMEM(norm_1a.shape, F32) for _ in range(2)),
         pltpu.SemaphoreType.DMA((held + 6,))],
        hbm_out=range(held + 3),
    )(tab, g12, labels, norm_1a, k_1a, w_1a, z_own, z_for, dn_own, dn_for, gs_own, gs_for, *finished)
    result, grad_norm_1c, grad_norm_1p, grad_norm_2a, grad_norm_2c = finished
    *near, grad_images = tie(*near, grad_images)
    parts = [along, *near]
    weights = (w_2c, w_2b.reshape(-1, n), w_2a, w_1c, w_1p, w_1b.reshape(-1, n), w_1a)
    t_2c, t_2b, t_2a, t_1c, t_1p, t_1b, t_1a, grad_norm_2b = stage(
        functools.partial(unpack, first=first, second=second, piece=piece),
        [(v.shape, F32) for v in (*weights, norm_2b)],
        [*(pltpu.VMEM(v.shape, F32) for v in (*weights, norm_2b)),
         pltpu.VMEM((devices, share, n), F32), pltpu.VMEM((2, devices, piece, n), BF16),
         pltpu.VMEM((devices, 2, n), F32), pltpu.SemaphoreType.DMA((8,))],
        hbm_out=range(8),
    )(tab, labels, *parts, *(swap(v) for v in parts))
    grads = (
        grad_norm_1a, grad_norm_1b, grad_norm_1c, grad_norm_1p,
        grad_norm_2a, grad_norm_2b, grad_norm_2c,
    )
    return (
        result[None], grad_images, t_1a, t_1b.reshape(w_1b.shape), t_1c, t_1p, t_2a,
        t_2b.reshape(w_2b.shape), t_2c, *[v.transpose(1, 0, 2) for v in grads],
    )


def solution(mesh):
    return jax.shard_map(
        body,
        mesh=mesh,
        in_specs=(
            P("batch", "rows", None, None),
            *[P()] * 14,
            P(("batch", "rows"), None, None, None),
            P("batch"),
            P(),
            P(),
        ),
        out_specs=(
            P(("batch", "rows"), None, None, None),
            P("batch", "rows", None, None),
            *[P()] * 14,
        ),
        check_vma=False,
    )
```

```python
import functools

import jax
import jax.numpy as jnp
from jax import lax
from jax.experimental import pallas as pl
from jax.experimental.pallas import tpu as pltpu
from jax.sharding import PartitionSpec as P

EPSILON = 1e-05
F32 = jnp.float32
BF16 = jnp.bfloat16
AXES = ("rows", "batch")
VMEM_LIMIT = 14 * 1024 * 1024
LANES = 128
COLS = 32
NEAR = 4


def full(memory=pltpu.VMEM):
    return pl.BlockSpec(memory_space=memory)


def stage(kernel, outs, scratch=(), hbm=(), hbm_out=()):
    def place(i, outside):
        return pltpu.HBM if i in outside else pltpu.VMEM

    def call(*args):
        args = [
            pltpu.with_memory_space_constraint(a, pltpu.HBM) if i in hbm else a
            for i, a in enumerate(args)
        ]
        return pl.pallas_call(
            kernel,
            out_shape=tuple(jax.ShapeDtypeStruct(s, d) for s, d in outs),
            in_specs=[full(place(i, hbm)) for i in range(len(args))],
            out_specs=tuple(
                full(place(i, hbm_out)) for i in range(len(outs))
            ),
            scratch_shapes=list(scratch),
            compiler_params=pltpu.CompilerParams(vmem_limit_bytes=VMEM_LIMIT),
            name=(kernel.func if isinstance(kernel, functools.partial) else kernel).__name__,
        )(*args)

    return call


def silu_of_half(u):
    return u + u * jnp.tanh(u)


def slope_of_half(u):
    t = jnp.tanh(u)
    return (0.5 + 0.5 * t) * (1.0 + u - u * t)


def fold(x):
    return (x[0:8] + x[8:16]) + (x[16:24] + x[24:32])


def row(total, stat):
    blocks = total.shape[0]
    pieces = [total[j : j + 1, LANES * stat : LANES * (stat + 1)] for j in range(blocks)]
    return pieces[0] if blocks == 1 else jnp.concatenate(pieces, axis=1)


def spread(out_ref, rows):
    blocks = out_ref.shape[1]
    for stat, values in enumerate(rows):
        for j in range(blocks):
            piece = values[:, LANES * j : LANES * (j + 1)]
            out_ref[:, j : j + 1, LANES * stat : LANES * (stat + 1)] = jnp.broadcast_to(
                piece[None], (out_ref.shape[0], 1, LANES)
            )


def group_sum(got_ref, labels, label):
    same = (labels == label).astype(F32)
    stats = got_ref.shape[2] // LANES
    parts = [
        jnp.sum(got_ref[:, :, LANES * s : LANES * (s + 1)] * same, axis=0) for s in range(stats)
    ]
    return jnp.concatenate(parts, axis=1) if stats > 1 else parts[0]


def group_count(labels, label):
    return jnp.sum((labels == label).astype(F32), axis=0)


def tiled(values, channels):
    return jnp.concatenate([values] * (channels // LANES), axis=1) if channels > LANES else values


def moments(first, second, pixels):
    mean = first / pixels
    return mean, lax.rsqrt(second / pixels - mean * mean + EPSILON)


def own_of(values, label):
    out = values[0]
    label = tiled(label, out.shape[1])
    for g in range(1, len(values)):
        out = jnp.where(label == float(g), values[g], out)
    return out


def gain_of(norm_ref, label):
    return own_of([norm_ref[g, 0:1, :] for g in range(norm_ref.shape[0])], label)


def shift_of(norm_ref, label):
    return own_of([norm_ref[g, 1:2, :] for g in range(norm_ref.shape[0])], label)


def valid_cols(channels):
    return lax.broadcasted_iota(jnp.int32, (COLS, channels), 0) < COLS - 4


def chan_mask(tab):
    return lax.broadcasted_iota(jnp.int32, (1, LANES), 1).astype(F32) < entry(tab, LIMIT)


def flat(x):
    return x.reshape(x.shape[0] * x.shape[1], x.shape[2])


def mm(a, b):
    return jnp.dot(a, b, preferred_element_type=F32)


def mm_nt(a, b):
    return lax.dot_general(a, b, (((1,), (1,)), ((), ())), preferred_element_type=F32)


def mm_tn(a, b):
    return lax.dot_general(a, b, (((0,), (0,)), ((), ())), preferred_element_type=F32)


def mm_side(a, b):
    turned = mm_tn(b, a)
    blocks = [
        jnp.transpose(turned[:, LANES * j : LANES * (j + 1)]) for j in range(a.shape[1] // LANES)
    ]
    return blocks[0] if len(blocks) == 1 else jnp.concatenate(blocks, axis=0)


def zeros8(channels):
    return jnp.zeros((8, channels), F32)


def down(x):
    return jnp.sum(x, axis=0, keepdims=True)


OWN, OTHER, HALF, LIMIT, GATE, MINOR = range(6)


def entry(tab, k):
    return tab[k : k + 1, :]


def half_of(tab, k=HALF):
    return (jnp.sum(entry(tab, k)) * (1.0 / LANES)).astype(jnp.int32)


def prepare(w1b, w2b, w_even, w_odd, w_two, w_last, b_even, b_odd, b_two, b_last):
    n = LANES
    for k, (y, x) in enumerate(((1, 1), (1, 2), (1, 0))):
        w_even[n * k : n * (k + 1), :] = w1b[y, x]
    for k, (low, high) in enumerate((((2, 1), (0, 1)), ((2, 2), (0, 2)), ((2, 0), (0, 0)))):
        w_odd[n * k : n * (k + 1), 0:n] = w1b[low]
        w_odd[n * k : n * (k + 1), n : 2 * n] = w1b[high]
    for x in range(3):
        w_two[n * x : n * (x + 1), 0:n] = w2b[0, x]
        w_two[n * x : n * (x + 1), n : 2 * n] = w2b[1, x]
        w_last[n * x : n * (x + 1), :] = w2b[2, x]
        b_two[0:n, n * x : n * (x + 1)] = w2b[1, x]
        b_two[n : 2 * n, n * x : n * (x + 1)] = w2b[2, x]
        b_last[:, n * x : n * (x + 1)] = w2b[0, x]
    nothing = jnp.zeros((n, n), BF16)
    b_even[0:n, 0:n] = w1b[1, 1]
    b_even[0:n, n : 2 * n] = nothing
    b_even[n : 2 * n, 0:n] = w1b[1, 2]
    b_even[n : 2 * n, n : 2 * n] = w1b[1, 0]
    for k, top in ((0, 2), (1, 0)):
        b_odd[0:n, 2 * n * k : 2 * n * k + n] = w1b[top, 1]
        b_odd[0:n, 2 * n * k + n : 2 * n * (k + 1)] = nothing
        b_odd[n : 2 * n, 2 * n * k : 2 * n * k + n] = w1b[top, 2]
        b_odd[n : 2 * n, 2 * n * k + n : 2 * n * (k + 1)] = w1b[top, 0]


def widen(source, x_pad):
    rows, cols, chans = source.shape
    gap = x_pad.shape[1] - cols

    def put(i, carry):
        x_pad[i, 0:cols, :] = source[i]
        x_pad[i, cols : cols + gap, :] = jnp.zeros((gap, chans), BF16)
        return carry

    lax.fori_loop(0, rows, put, 0, unroll=4)


def first_project(x_pad, w, z, stats=True):
    rows = x_pad.shape[0]
    step = rows // 4
    sums, squares = zeros8(LANES), zeros8(LANES)
    for c in range(4):
        values = mm(flat(x_pad[step * c : step * (c + 1)]), w[...])
        z[step * c : step * (c + 1)] = values.reshape(step, x_pad.shape[1], LANES)
        if stats:
            parts = values.reshape(-1, 8, LANES)
            sums = sums + jnp.sum(parts, axis=0)
            squares = squares + jnp.sum(parts * parts, axis=0)
    return sums, squares


def f1(
    place_at, group_at, width_at, gate_at, images, w_at, tab, x_own, x_for, z_own, z_for, send,
    place_ref, group, width, gate, raw, w, found, sems, *, batch,
):
    pairs = (
        (place_at, place_ref), (group_at, group), (width_at, width), (gate_at, gate), (w_at, w),
        (images.at[0], raw.at[0]), (images.at[1], raw.at[1]),
    )
    copies = [pltpu.make_async_copy(a, b, sems.at[k]) for k, (a, b) in enumerate(pairs)]
    for k in (0, 4, 5, 6, 1, 2, 3):
        copies[k].start()
    for k in (0, 4, 5):
        copies[k].wait()
    half = lax.div(place_ref[0], batch)
    sides = ((x_own, z_own), (x_for, z_for))

    def one(k):
        for place in (0, 1):

            @pl.when(half == place)
            def _():
                x_pad, z = sides[k] if place == 0 else sides[1 - k]
                widen(raw.at[k], x_pad)
                sums, squares = first_project(x_pad, w, z)
                at = 2 * (k if place == 0 else 1 - k)
                found[at : at + 1, :] = down(sums)
                found[at + 1 : at + 2, :] = down(squares)

    one(0)
    copies[6].wait()
    one(1)
    for k in (1, 2, 3):
        copies[k].wait()
    rows = [found[k : k + 1, :] for k in range(4)]
    own, other = group[half], group[1 - half]
    values = {
        OWN: own, OTHER: other, HALF: half, LIMIT: w.shape[1] // 4 * width[own], GATE: gate[own],
        MINOR: lax.rem(lax.rem(place_ref[0], batch), NEAR),
    }
    tab[...] = jnp.zeros(tab.shape, F32)
    for k, v in values.items():
        tab[k : k + 1, :] = jnp.full((1, LANES), v.astype(F32))
    spread(send, [*rows, jnp.full((1, LANES), (own + 4 * other).astype(F32))])


def f1_strided(tab, x_own, x_oth, w, xee, z, stats, wide):
    half = half_of(tab)
    rows = x_own.shape[0] // 2
    for k, x_pad in enumerate((x_own, x_oth)):
        first = rows * (half if k == 0 else 1 - half)

        def put(i, carry, x_pad=x_pad, first=first):
            for b in range(wide.shape[0]):
                lanes = slice(LANES * b, LANES * (b + 1))
                wide[b] = x_pad[2 * i, :, lanes].astype(F32)
                xee[first + i, :, lanes] = wide[b, pl.ds(0, COLS, stride=2), :].astype(BF16)
            return carry

        lax.fori_loop(0, rows, put, 0, unroll=2)
    total = 2 * rows
    step = total // 7
    chans = z.shape[2]
    squares = zeros8(chans)
    for c in range(7):
        values = mm(flat(xee[step * c : step * (c + 1)]), w[...])
        z[step * c : step * (c + 1)] = values.reshape(step, COLS, chans)
        parts = values.reshape(-1, 8, chans)
        squares = squares + jnp.sum(parts * parts, axis=0)
    ones = jnp.ones((8, total * COLS), BF16)
    stats[:, 0 : w.shape[0]] = mm(ones, flat(xee[...]))[0:1]
    stats[:, w.shape[0] :] = down(squares)


def scale_shift(got, labels, tab, norm, pixels, slot=0):
    label = entry(tab, OWN)
    total = group_sum(got, labels, label)
    chans = norm.shape[2]
    count = tiled(group_count(labels, label), chans) * pixels
    mean, rstd = moments(row(total, 2 * slot), row(total, 2 * slot + 1), count)
    gain, shift = gain_of(norm, entry(tab, OWN)), shift_of(norm, entry(tab, OWN))
    return mean, rstd, gain, shift, count


def conv_stats(z, source, pair, single, send, extra=()):
    keep = valid_cols(LANES)[None]
    rows = z.shape[0]
    step = rows // 4
    (lanes_2, w_2, offsets), (lanes_1, w_1, offset) = pair, single
    sums, squares = zeros8(LANES), zeros8(LANES)
    base = min(offsets)
    for c in range(4):
        at = step * c
        both = mm(flat(source[at + base : at + base + step + 1, :, lanes_2]), w_2)
        values = mm(flat(source[at + offset : at + offset + step, :, lanes_1]), w_1)
        for k, own in enumerate(offsets):
            skip = COLS * (own - base)
            values = values + both[skip : skip + step * COLS, LANES * k : LANES * (k + 1)]
        values = jnp.where(keep, values.reshape(step, COLS, LANES), 0.0)
        z[at : at + step] = values
        parts = values.reshape(-1, 8, LANES)
        sums = sums + jnp.sum(parts, axis=0)
        squares = squares + jnp.sum(parts * parts, axis=0)
    spread(send, [down(sums), down(squares), *extra])


def f2(
    tab, got, z_own, x_oth, w, norm, w_even, w_odd, stats_p,
    xs, z, send, labels, keeps, keeps_all, z_oth,
):
    codes = got[:, :, 4 * LANES : 5 * LANES]
    others = jnp.floor(0.25 * codes)
    marks = codes - 4.0 * others
    labels[...] = marks
    rows = xs.shape[0] - 1
    pixels = 4.0 * rows * (COLS - 4)
    first_project(x_oth, w, z_oth, False)
    for g in range(norm.shape[0]):
        mine, theirs = (marks == float(g)).astype(F32), (others == float(g)).astype(F32)
        totals = [
            jnp.sum(
                got[:, :, LANES * s : LANES * (s + 1)] * mine
                + got[:, :, LANES * (s + 2) : LANES * (s + 3)] * theirs,
                axis=0,
            )
            for s in (0, 1)
        ]
        mean, rstd = moments(*totals, group_count(marks, float(g)) * pixels)
        keeps_all[2 * g : 2 * g + 1, :] = mean
        keeps_all[2 * g + 1 : 2 * g + 2, :] = rstd
    for k, slot in enumerate((OWN, OTHER)):
        for q in (0, 1):
            choices = [keeps_all[2 * g + q : 2 * g + q + 1, :] for g in range(norm.shape[0])]
            keeps[2 * k + q : 2 * k + q + 1, :] = own_of(choices, entry(tab, slot))
    mean, rstd = keeps[0:1, :], keeps[1:2, :]
    gain, shift = gain_of(norm, entry(tab, OWN)), shift_of(norm, entry(tab, OWN))
    scale = rstd * gain
    bias = 0.5 * (shift - mean * scale)
    scale = 0.5 * scale
    keep = valid_cols(LANES) & chan_mask(tab)
    half = half_of(tab)
    xs[0] = jnp.zeros(xs.shape[1:], BF16)
    n = LANES
    for k, zz in enumerate((z_own, z_oth)):
        first = 1 + (rows // 2) * (half if k == 0 else 1 - half)

        def put(i, carry, zz=zz, first=first):
            lane = 0
            for a in (0, 1):
                for b in (0, 1):
                    u = zz[2 * i + a, pl.ds(b, COLS, stride=2), :] * scale + bias
                    act = jnp.where(keep, silu_of_half(u), 0.0)
                    xs[first + i, :, lane : lane + n] = act.astype(BF16)
                    lane += n
                    if b == 1:
                        moved = pltpu.roll(act, 1, 0)
                        xs[first + i, :, lane : lane + n] = moved.astype(BF16)
                        lane += n
            return carry

        lax.fori_loop(0, rows // 2, put, 0, unroll=2)
    extra = [stats_p[:, lanes] for lanes in columns(stats_p.shape[1])]
    pair = (slice(3 * n, 6 * n), w_odd[...], (1, 0))
    conv_stats(z, xs, pair, (slice(0, 3 * n), w_even[...], 1), send, extra)


def project(act, w, z):
    rows, chans = z.shape[0], z.shape[2]
    step = rows // 7
    squares = zeros8(chans)
    for c in range(7):
        values = mm(flat(act[step * c : step * (c + 1)]), w[...])
        z[step * c : step * (c + 1)] = values.reshape(step, COLS, chans)
        parts = values.reshape(-1, 8, chans)
        squares = squares + jnp.sum(parts * parts, axis=0)
    return down(squares)


def join(pieces):
    return pieces[0] if len(pieces) == 1 else jnp.concatenate(pieces, axis=1)


def columns(channels):
    return [slice(LANES * j, LANES * (j + 1)) for j in range(channels // LANES)]


def through(sums, w):
    high = sums.astype(BF16)
    rest = sums - high.astype(F32)
    mid = rest.astype(BF16)
    low = (rest - mid.astype(F32)).astype(BF16)
    lines = [v.astype(F32) for v in (high, mid, low)]
    lines.append(jnp.zeros((5, sums.shape[1]), F32))
    return down(mm(jnp.concatenate(lines, axis=0).astype(BF16), w))


def through_nt(sums, w):
    high = sums.astype(BF16)
    rest = sums - high.astype(F32)
    mid = rest.astype(BF16)
    low = (rest - mid.astype(F32)).astype(BF16)
    lines = [v.astype(F32) for v in (high, mid, low)]
    lines.append(jnp.zeros((5, sums.shape[1]), F32))
    return down(mm_nt(jnp.concatenate(lines, axis=0).astype(BF16), w))


def put_split(send, at, values):
    rows = values.shape[0]
    high = values.astype(BF16)
    rest = (values - high.astype(F32)).astype(BF16)
    for k, part in enumerate((high, rest)):
        send[:, at + rows * k : at + rows * (k + 1), :] = jnp.broadcast_to(
            part[None], (send.shape[0], rows, LANES)
        )


def get_split(got, at, rows):
    return got[:, at : at + rows, :].astype(F32) + got[:, at + rows : at + 2 * rows, :].astype(F32)


def over_group(values, marks, label):
    return jnp.sum(values * (marks == label).astype(F32), axis=0)


def stack(rows):
    return jnp.concatenate(rows, axis=0)


def pair_products(tab, z, norm, keeps, act, act_sum, slope, both):
    rows = z.shape[0]
    label = entry(tab, OWN)
    mean, rstd = keeps[0:1, :], keeps[1:2, :]
    scale = rstd * gain_of(norm, label)
    bias = 0.5 * (shift_of(norm, label) - mean * scale)
    scale = 0.5 * scale
    keep = valid_cols(LANES) & chan_mask(tab)
    middle = act_sum * (1.0 / (rows * (COLS - 4)))

    def put(i, carry):
        zz = z[i]
        s = jnp.where(keep, slope_of_half(zz * scale + bias), 0.0)
        sx = s * ((zz - mean) * rstd)
        slope[i] = s
        for k, v in enumerate((s, sx)):
            high = v.astype(BF16)
            both[i, :, LANES * k : LANES * (k + 1)] = high
            both[i, :, LANES * (k + 2) : LANES * (k + 3)] = (v - high.astype(F32)).astype(BF16)
        return carry[0] + fold(s), carry[1] + fold(sx)

    sums = lax.fori_loop(0, rows, put, (zeros8(LANES), zeros8(LANES)), unroll=4)
    sums = [down(v) for v in sums]
    product = mm_tn(flat(act[...]), flat(both[...]))
    product = product[:, 0 : 2 * LANES] + product[:, 2 * LANES :]
    column = jnp.transpose(jnp.broadcast_to(middle, (8, LANES)))[:, 0:1]
    return product - column * join(sums), stack(sums)


def rows_of(line):
    return stack([line[:, lanes] for lanes in columns(line.shape[1])])


def line_of(rows):
    return join([rows[k : k + 1, :] for k in range(rows.shape[0])])


def pair_rows(product, devices, share, high, low, own):
    n = LANES
    missing = devices * share - n
    for h in (0, 1):
        values = product[:, n * h : n * (h + 1)]
        if missing:
            values = stack([values, jnp.zeros((missing, n), F32)])
        values = values.reshape(devices, share, n)
        first, last = share * h, share * (h + 1)
        top = values.astype(BF16)
        rest = (values - top.astype(F32)).astype(BF16)
        high[:, first:last, :] = top
        low[:, first:last, :] = rest
        own[:, first:last, :] = top.astype(F32) + rest.astype(F32)


def pass_pair(send, at, high, low, marks, groups):
    rows = high.astype(F32) + low.astype(F32)
    out = -rows
    for g in range(groups):
        same = (marks == float(g)).astype(F32)
        images = jnp.maximum(jnp.sum(same, axis=0), 1.0)
        out = out + (jnp.sum(rows * same, axis=0) / images)[None] * same
    send[:, at : at + rows.shape[1], :] = out.astype(BF16)


def pair_solve(tab, marks, outer, inner, sums, w, act_sums, q_rows, p_rows, pixels):
    label, n = entry(tab, OWN), LANES
    (norm_o, keeps_o), (norm_i, keeps_i) = outer, inner
    shift_o, gain_o, shift_i, gain_i = sums
    images = group_count(marks, label)
    count, count_o = images * pixels, tiled(images, norm_o.shape[2]) * pixels
    rstd_o = keeps_o[1:2, :]
    a_o = rstd_o * gain_of(norm_o, label)
    b_o, c_o = -(a_o * rstd_o) * gain_o / count_o, -a_o * shift_o / count_o
    scaled = w[...].astype(F32) * b_o
    high = scaled.astype(BF16)
    m = mm_nt(high, w[...]) + mm_nt((scaled - high.astype(F32)).astype(BF16), w[...])
    m_high = m.astype(BF16)
    m_low = (m - m_high.astype(F32)).astype(BF16)
    m = m_high.astype(F32) + m_low.astype(F32)
    e = through_nt(c_o, w[...])
    same = (marks == label).astype(F32)
    middle = jnp.sum(act_sums * same, axis=0) / count
    spread_out = ((act_sums * (1.0 / pixels) - middle[None]) * same).reshape(-1, n).astype(BF16)
    share = p_rows.shape[1] // 2
    p_rows = p_rows * images[None]
    found = []
    for h, start in enumerate((shift_i, gain_i)):
        q = q_rows[:, h : h + 1, :]
        p = p_rows[:, share * h : share * (h + 1), :].reshape(-1, n)[0:n]
        p = p + mm_tn(spread_out, q.reshape(-1, n).astype(BF16))
        found.append(start + down(m * p) + e * jnp.sum(q * same, axis=0))
    rstd_i = keeps_i[1:2, :]
    a = rstd_i * gain_of(norm_i, label)
    coefs = a, -(a * rstd_i) * found[1] / count, -a * found[0] / count
    line = e - through(middle, m_high) - through(middle, m_low)
    return join([m_high, m_low]), line, coefs, found


def activate(tab, got, labels, z_in, norm, act, keeps):
    got = got.at[:, :, 0 : 2 * LANES]
    rows = z_in.shape[0]
    pixels = 1.0 * rows * (COLS - 4)
    mean, rstd, gain, shift, _ = scale_shift(got, labels[...], tab, norm, pixels)
    keeps[0:1, :] = mean
    keeps[1:2, :] = rstd
    scale = rstd * gain
    bias = 0.5 * (shift - mean * scale)
    scale = 0.5 * scale
    keep = valid_cols(LANES) & chan_mask(tab)

    def put(i, sums):
        low = jnp.where(keep, silu_of_half(z_in[i] * scale + bias), 0.0).astype(BF16)
        act[i] = low
        return sums + fold(low.astype(F32))

    return down(lax.fori_loop(0, rows, put, zeros8(LANES), unroll=7))


def f3(
    tab, got, labels, z_in, norm, w, w_p,
    act, z, send, keeps, keeps_p, slope, q, high, own, both, low, *, share,
):
    sums = activate(tab, got, labels, z_in, norm, act, keeps)
    at = expand_pair(tab, z_in, norm, keeps, act, sums, w, z, send, slope, q, both, high, low, own, share)
    send[:, at : at + 2 * share, :] = low[...]
    marks, label = labels[...], entry(tab, OWN)
    total = group_sum(got, marks, label)
    outer, first = z.shape[2], 2 * LANES
    second = first + w_p.shape[0]
    count = tiled(group_count(marks, label), outer) * (1.0 * z.shape[0] * (COLS - 4))
    mean, rstd = moments(through(total[:, first:second], w_p[...]), total[:, second:], count)
    keeps_p[0:1, :] = mean
    keeps_p[1:2, :] = rstd


def expand_pair(tab, z_in, norm, keeps, act, sums, w, z, send, slope, q, both, high, low, own, share):
    pixels = 1.0 * z.shape[0] * (COLS - 4)
    squares = project(act, w, z)
    first = through(sums, w[...])
    second = squares - first * first / pixels
    product, q[...] = pair_products(tab, z_in, norm, keeps, act, sums, slope, both)
    pair_rows(product, send.shape[0], share, high, low, own)
    put_split(send, 0, sums)
    moved = rows_of(second).astype(BF16)
    send[:, 2 : 2 + moved.shape[0], :] = jnp.broadcast_to(moved[None], (send.shape[0], *moved.shape))
    return 2 + moved.shape[0]


def f4(
    tab, got, labels, zc, zp, norm_c, norm_p, keeps_p, w_c, w, high, q,
    joined, slope, z, send, keeps,
):
    rows, chans = zc.shape[0], zc.shape[2]
    pixels = 1.0 * rows * (COLS - 4)
    mean_c, rstd_c = gathered_moments(got, labels[...], entry(tab, OWN), w_c, pixels)
    mean_p, rstd_p = keeps_p[0:1, :], keeps_p[1:2, :]
    for k, v in enumerate((mean_c, rstd_c, mean_p, rstd_p)):
        keeps[k : k + 1, :] = v
    group = entry(tab, OWN)
    scale_c = rstd_c * gain_of(norm_c, group)
    scale_p = rstd_p * gain_of(norm_p, group)
    bias = (shift_of(norm_c, group) - mean_c * scale_c) + (
        shift_of(norm_p, group) - mean_p * scale_p
    )
    keep = valid_cols(chans)
    scale_c, scale_p, bias = 0.5 * scale_c, 0.5 * scale_p, 0.5 * bias

    def put(i, carry):
        u = zc[i] * scale_c + zp[i] * scale_p + bias
        t = jnp.tanh(u)
        p = u * t
        joined[i] = jnp.where(keep, u + p, 0.0).astype(BF16)
        slope[i] = (0.5 + 0.5 * t) * (1.0 + u - p)
        return carry

    lax.fori_loop(0, rows, put, 0, unroll=4)
    step = rows // 4
    sums, squares = zeros8(LANES), zeros8(LANES)
    for c in range(4):
        values = mm(flat(joined[step * c : step * (c + 1)]), w[...])
        z[step * c : step * (c + 1)] = values.reshape(step, COLS, LANES)
        parts = values.reshape(-1, 8, LANES)
        sums = sums + jnp.sum(parts, axis=0)
        squares = squares + jnp.sum(parts * parts, axis=0)
    put_split(send, 0, stack([down(sums), down(squares)]))
    send[:, 4 : 4 + high.shape[1], :] = high[...]
    put_split(send, 4 + high.shape[1], q[...])


def put_shares(xz, send):
    n, devices = LANES, send.shape[0]
    share = xz.shape[0] // devices
    pieces = xz[...].reshape(devices, share, n)
    for q in range(share):
        send[:, :, n * (2 + q) : n * (3 + q)] = pieces[:, q : q + 1, :]


def f5(tab, got, labels, z_in, norm, w_two, w_last, xz, x3, z, send, keeps):
    rows = z_in.shape[0]
    pixels = 1.0 * rows * (COLS - 4)
    marks, label = labels[...], entry(tab, OWN)
    total = over_group(get_split(got, 0, 2), marks, label)
    mean, rstd = moments(total[0:1], total[1:2], group_count(marks, label) * pixels)
    gain, shift = gain_of(norm, label), shift_of(norm, label)
    keeps[0:1, :] = mean
    keeps[1:2, :] = rstd
    scale = rstd * gain
    bias = 0.5 * (shift - mean * scale)
    scale = 0.5 * scale
    keep = valid_cols(LANES) & chan_mask(tab)
    x3[0] = jnp.zeros(x3.shape[1:], BF16)
    x3[rows + 1] = jnp.zeros(x3.shape[1:], BF16)
    n = LANES

    def put(i, carry):
        act = jnp.where(keep, silu_of_half(z_in[i] * scale + bias), 0.0)
        x3[i + 1, :, 0:n] = pltpu.roll(act, 1, 0).astype(BF16)
        x3[i + 1, :, n : 2 * n] = act.astype(BF16)
        x3[i + 1, :, 2 * n : 3 * n] = pltpu.roll(act, COLS - 1, 0).astype(BF16)
        return carry

    lax.fori_loop(0, rows, put, 0, unroll=2)
    lanes = slice(0, 3 * n)
    conv_stats(
        z, x3, (lanes, w_two[...], (0, 1)), (lanes, w_last[...], 2), send.at[:, :, 0 : 2 * n]
    )
    put_shares(xz, send)


def f6(
    tab, got, labels, z_in, norm, w,
    act, z, send, keeps, slope, q, own, both, high, low, *, share,
):
    sums = activate(tab, got, labels, z_in, norm, act, keeps)
    at = expand_pair(tab, z_in, norm, keeps, act, sums, w, z, send, slope, q, both, high, low, own, share)
    send[:, at : at + 2 * share, :] = high[...]
    send[:, at + 2 * share : at + 4 * share, :] = low[...]


def gathered_moments(got, marks, label, w, pixels):
    devices, chans = got.shape[0], w.shape[1]
    low = (got[:, k : k + 1, :].astype(F32).reshape(devices, LANES).astype(BF16) for k in (0, 1))
    means = sum(mm(v, w[...]) for v in low) * (1.0 / pixels)
    blocks = chans // LANES
    moments_2 = join(
        [got[:, 2 + k : 3 + k, :].astype(F32).reshape(devices, LANES) for k in range(blocks)]
    )
    same = join([(marks == label).astype(F32).reshape(devices, LANES)] * blocks)
    images = tiled(group_count(marks, label), chans)
    mean = down(means * same) / images
    away = means - mean
    variance = down((moments_2 + pixels * (away * away)) * same) / (images * pixels)
    return mean, lax.rsqrt(variance + EPSILON)


def b7(
    tab, got, labels, joined, z, norm, w, cot, slope_in, z_in, keeps_in, q,
    result, grad_pre, send, keeps, d_in, wide, low, *, share, p_at,
):
    rows, chans = z.shape[0], z.shape[2]
    cols = COLS - 4
    pixels = 1.0 * rows * cols
    marks, label = labels[...], entry(tab, OWN)
    mean, rstd = gathered_moments(got, marks, label, w, pixels)
    gain, shift = gain_of(norm, label), shift_of(norm, label)
    keeps[0:1, :] = mean
    keeps[1:2, :] = rstd
    gate = 0.25 * tiled(entry(tab, GATE), chans)
    scale = 0.5 * rstd * gain * gate
    bias = 0.5 * (shift - mean * rstd * gain) * gate
    wide[...] = jnp.zeros(wide.shape, F32)
    a_gate = rstd * gain * gate

    def put(i, carry):
        sums, products = carry
        wide[0:cols, :] = cot[i].astype(F32)
        zz = z[i]
        u = 0.5 * joined[i].astype(F32) + zz * scale + bias
        t = jnp.tanh(u)
        p = u * t
        result[i] = (u + p)[0:cols].astype(BF16)
        g = wide[...] * ((0.5 + 0.5 * t) * (1.0 + u - p))
        grad_pre[i] = g
        low[i] = (a_gate * g).astype(BF16)
        return sums + fold(g), products + fold(g * (zz - mean))

    start = zeros8(chans)
    sums, products = lax.fori_loop(0, rows, put, (start, start), unroll=2)
    inner = inner_sums(low, w, slope_in, z_in, keeps_in, d_in)
    blocks = chans // LANES
    put_split(send, 0, rows_of(down(sums) * gate))
    put_split(send, 2 * blocks, rows_of(down(products) * rstd * gate))
    put_split(send, 4 * blocks, stack(inner))
    put_split(send, 4 * blocks + 4, q[...])
    high = got[:, p_at : p_at + 2 * share, :]
    low_p = got[:, p_at + 2 * share : p_at + 4 * share, :]
    pass_pair(send, 4 * blocks + 8, high, low_p, marks, norm.shape[0])


def lane_sums(got, marks, channels):
    def sums_of(g):
        total = group_sum(got, marks, float(g))
        return row(total, 0), row(total, 1)

    return sums_of


def row_sums(got, marks):
    def sums_of(g):
        total = over_group(get_split(got, 0, 2), marks, float(g))
        return total[0:1], total[1:2]

    return sums_of


def backward_norm(tab, sums_of, marks, norm, keeps, pixels, grad_norm):
    group, chans = entry(tab, OWN), norm.shape[2]
    sums = [sums_of(g) for g in range(norm.shape[0])]
    for g, (shift_sum, gain_sum) in enumerate(sums):
        grad_norm[g, 0:1, :] = gain_sum
        grad_norm[g, 1:2, :] = shift_sum
    count = tiled(group_count(marks, group), chans) * pixels
    own_shift, own_gain = (own_of([v[k] for v in sums], group) for k in (0, 1))
    mean, rstd = keeps[0:1, :], keeps[1:2, :]
    a = rstd * gain_of(norm, group)
    return mean, a, -(a * rstd) * own_gain / count, -a * own_shift / count


def slope_sums(tab, d, z_in, norm, keeps, dout):
    rows = z_in.shape[0]
    mean, rstd = keeps[0:1, :], keeps[1:2, :]
    group = entry(tab, OWN)
    scale = rstd * gain_of(norm, group)
    bias = 0.5 * (shift_of(norm, group) - mean * scale)
    scale = 0.5 * scale
    keep = valid_cols(LANES) & chan_mask(tab)

    def put(i, carry):
        sums, products = carry
        zz = z_in[i]
        g = jnp.where(keep, d[i] * slope_of_half(zz * scale + bias), 0.0)
        dout[i] = g
        return sums + fold(g), products + fold(g * (zz - mean))

    sums, products = lax.fori_loop(
        0, rows, put, (zeros8(LANES), zeros8(LANES)), unroll=4
    )
    return down(sums), down(products) * rstd


def b9(
    tab, got, labels, norm_c, keeps_c, w_c, got_act, act, slope, d_in, z, norm, keeps,
    b_two, b_last, z_in, norm_in, keeps_in, x_sum, pair_high, pair_low, own_p,
    dz, dout, send, own_sums, d3, d, *, share, p_at,
):
    rows = z.shape[0]
    pixels = 1.0 * rows * (COLS - 4)
    marks, label = labels[...], entry(tab, OWN)
    blocks = norm_c.shape[2] // LANES
    at = 4 * blocks
    wide = [
        line_of(over_group(get_split(got, 2 * blocks * k, blocks), marks, label)) for k in (0, 1)
    ]
    inner = over_group(get_split(got, at, 2), marks, label)
    m, line, (a, b, c), found = pair_solve(
        tab, marks, (norm_c, keeps_c), (norm, keeps), [*wide, inner[0:1], inner[1:2]], w_c,
        get_split(got_act, 0, 1), get_split(got, at + 4, 2),
        got[:, at + 8 : at + 8 + 2 * share, :].astype(F32) + own_p[...], pixels,
    )
    own_sums[0:1, :] = found[0]
    own_sums[1:2, :] = found[1]
    inner_grad(act, m, line, slope, d_in, d)
    mean = keeps[0:1, :]
    keep = valid_cols(LANES)
    n = LANES
    d3[0] = jnp.zeros(d3.shape[1:], BF16)
    d3[rows + 1] = jnp.zeros(d3.shape[1:], BF16)

    def put(i, carry):
        v = a * d[i] + b * (z[i] - mean) + c
        v = jnp.where(keep, v, 0.0)
        d3[i + 1, :, 0:n] = pltpu.roll(v, COLS - 1, 0).astype(BF16)
        low = v.astype(BF16)
        d3[i + 1, :, n : 2 * n] = low
        dz[i] = low
        d3[i + 1, :, 2 * n : 3 * n] = pltpu.roll(v, 1, 0).astype(BF16)
        return carry

    lax.fori_loop(0, rows, put, 0, unroll=2)
    step = rows // 4
    for k in range(4):
        both = mm_nt(flat(d3[step * k : step * (k + 1) + 1]), b_two[...])
        value = mm_nt(flat(d3[step * k + 2 : step * (k + 1) + 2]), b_last[...])
        value = value + both[COLS:, 0:n] + both[0 : step * COLS, n : 2 * n]
        d[step * k : step * (k + 1)] = value.reshape(step, COLS, LANES)
    put_split(send, 0, stack(slope_sums(tab, d, z_in, norm_in, keeps_in, dout)))
    blocks = columns(x_sum.shape[0])
    put_split(send, 4, stack([jnp.transpose(x_sum[lanes, :])[0:1] for lanes in blocks]))
    high, low = pair_high[:, 4 : 4 + 2 * share, :], pair_low[:, p_at : p_at + 2 * share, :]
    pass_pair(send, 4 + 2 * len(blocks), high, low, marks, norm.shape[0])


def b10(
    tab, got, labels, dout_in, z, norm, keeps, w, grad_pre, slope, zc, zp, keeps_cp,
    norm_c, w_c, slope_in, z_in, keeps_in,
    dz, grad_pre_2, send, grad_norm, d_in, d, low,
):
    rows, chans = zc.shape[0], zc.shape[2]
    pixels = 1.0 * rows * (COLS - 4)
    marks = labels[...]
    coefs = backward_norm(tab, row_sums(got, marks), marks, norm, keeps, pixels, grad_norm)
    normed_grad(dz, dout_in, z, *coefs)
    d[...] = mm_nt(flat(dz[...]), w[...]).reshape(d.shape)
    mean_c, rstd_c, mean_p, rstd_p = (keeps_cp[k : k + 1, :] for k in range(4))
    a_c = rstd_c * gain_of(norm_c, entry(tab, OWN))

    def sum_up(i, carry):
        sums, prod_c, prod_p = carry
        g = (grad_pre[i] + d[i]) * slope[i]
        grad_pre_2[i] = g
        low[i] = (a_c * g).astype(BF16)
        return (
            sums + fold(g),
            prod_c + fold(g * (zc[i] - mean_c)),
            prod_p + fold(g * (zp[i] - mean_p)),
        )

    start = zeros8(chans)
    sums, prod_c, prod_p = lax.fori_loop(0, rows, sum_up, (start, start, start), unroll=2)
    wide = [down(sums), down(prod_c) * rstd_c, down(prod_p) * rstd_p]
    inner = inner_sums(low, w_c, slope_in, z_in, keeps_in, d_in)
    parts = [stack([v[:, 0 : chans // 2], v[:, chans // 2 :]]) for v in wide]
    values = join([*parts, stack(inner)])
    send[...] = jnp.broadcast_to(values[None], send.shape)


def inner_sums(low, w, slope, z, keeps, d_in):
    d_in[...] = mm_nt(flat(low[...]), w[...]).reshape(d_in.shape)
    mean, rstd = keeps[0:1, :], keeps[1:2, :]

    def add(i, carry):
        g = slope[i] * d_in[i]
        return carry[0] + fold(g), carry[1] + fold(g * (z[i] - mean))

    sums = lax.fori_loop(0, z.shape[0], add, (zeros8(LANES), zeros8(LANES)), unroll=7)
    return down(sums[0]), down(sums[1]) * rstd


def inner_grad(act, m, line, slope, d_in, d):
    both = mm(flat(act[...]), m)
    d[...] = (both[:, 0:LANES] + both[:, LANES:]).reshape(d.shape)

    def put(i, carry):
        d[i] = slope[i] * (d_in[i] + d[i] + line)
        return carry

    lax.fori_loop(0, d.shape[0], put, 0, unroll=7)


def normed_grad(dz, dout, z, mean, a, b, c):
    keep = valid_cols(z.shape[2])

    def put(i, carry):
        v = a * dout[i] + b * (z[i] - mean) + c
        dz[i] = jnp.where(keep, v, 0.0).astype(BF16)
        return carry

    lax.fori_loop(0, z.shape[0], put, 0, unroll=2)


def b12(
    tab, own10, labels, norm_c, keeps_c, w_c, got_act, got_q, got_p, own_p, act, slope, d_in,
    z, norm, keeps, xs, d2, kept, sent, own_sums, dz, packed, dout, *, share, q_at, p_at,
):
    rows = z.shape[0]
    pixels = 1.0 * rows * (COLS - 4)
    outer, n = norm_c.shape[2], LANES
    marks = labels[...]
    total = own10[...]
    cuts = (0, outer, 2 * outer, 2 * outer + n, 2 * outer + 2 * n)
    m, line, (a, b, c), found = pair_solve(
        tab, marks, (norm_c, keeps_c.at[0:2]), (norm, keeps),
        [total[:, u:v] for u, v in zip(cuts, cuts[1:])], w_c, get_split(got_act, 0, 1),
        get_split(got_q, q_at, 2),
        got_p[:, p_at : p_at + 2 * share, :].astype(F32) + own_p[...], pixels,
    )
    own_sums[0:1, :] = found[0]
    own_sums[1:2, :] = found[1]
    inner_grad(act, m, line, slope, d_in, dout)
    mean = keeps[0:1, :]
    keep = valid_cols(LANES)
    d2[rows] = jnp.zeros(d2.shape[1:], BF16)

    def put(i, carry):
        v = a * dout[i] + b * (z[i] - mean) + c
        v = jnp.where(keep, v, 0.0)
        low = v.astype(BF16)
        dz[i] = low
        d2[i, :, 0:n] = low
        d2[i, :, n : 2 * n] = pltpu.roll(v, COLS - 1, 0).astype(BF16)
        return carry

    lax.fori_loop(0, rows, put, 0, unroll=4)
    low = flat(dz[...])
    cur = mm_side(flat(xs[1 : rows + 1]), low)
    for k, (y, x) in enumerate(((1, 1), (1, 2), (1, 0), (2, 1), (2, 2), (2, 0))):
        put_rows(packed, n * (3 * y + x), cur[n * k : n * (k + 1)])
    up = mm_side(flat(xs[0:rows, :, 3 * n : 6 * n]), low)
    for k, (y, x) in enumerate(((0, 1), (0, 2), (0, 0))):
        put_rows(packed, n * (3 * y + x), up[n * k : n * (k + 1)])
    share_out(tab, packed, 9 * n, kept, sent)


def b12_images(
    tab, d2, b_even, b_odd, zz, norm_in, keeps_in, dn, sums_out, de, do, wide, *, own
):
    rows = de.shape[0]
    n = LANES
    half = half_of(tab)
    first = rows * (half if own else 1 - half)
    step = rows // 2
    for k in range(2):
        here = flat(d2[pl.ds(first + step * k, step)])
        below = flat(d2[pl.ds(first + step * k + 1, step)])
        de[step * k : step * (k + 1)] = mm_nt(here, b_even[...]).reshape(step, COLS, 2 * n)
        odd = mm_nt(here, b_odd[:, 0 : 2 * n]) + mm_nt(below, b_odd[:, 2 * n : 4 * n])
        do[step * k : step * (k + 1)] = odd.reshape(step, COLS, 2 * n)
    mean_1, rstd_1 = keeps_in[0:1, :], keeps_in[1:2, :]
    group = entry(tab, OWN)
    scale = rstd_1 * gain_of(norm_in, group)
    bias = 0.5 * (shift_of(norm_in, group) - mean_1 * scale)
    scale = 0.5 * scale
    keep = valid_cols(LANES) & chan_mask(tab)

    def emit(i, carry):
        sums, products = carry
        for ra in (0, 1):
            planes = (de, do)[ra]
            for cb in (0, 1):
                zv = zz[2 * i + ra, pl.ds(cb, COLS, stride=2), :]
                g = planes[i, :, n * cb : n * (cb + 1)] * slope_of_half(zv * scale + bias)
                g = jnp.where(keep, g, 0.0)
                sums = sums + fold(g)
                products = products + fold(g * (zv - mean_1))
                wide[ra, pl.ds(cb, COLS, stride=2), :] = g
            dn[2 * i + ra] = wide[ra].astype(BF16)
        return sums, products

    totals = lax.fori_loop(0, rows, emit, (zeros8(n), zeros8(n)), unroll=2)
    sums_out[0:1, :] = down(totals[0])
    sums_out[1:2, :] = down(totals[1]) * rstd_1


def b13(
    tab, got, labels, norm, keeps, w, z_own, z_for, dn_own, dn_for, gs_own, gs_for, *rest, at, held
):
    finished, outs = rest[:held], rest[held : 2 * held]
    grad, grad_norm, grad_inner, dz, wide, grad_v, norm_v, inner_v, sems = rest[2 * held :]
    copies = [
        pltpu.make_async_copy(a, b, sems.at[k]) for k, (a, b) in enumerate(zip(finished, outs))
    ]
    for copy in copies:
        copy.start()
    rows, cols = grad.shape[1], grad.shape[2]
    half = half_of(tab)
    pixels = 2.0 * rows * cols
    marks = labels[...]
    totals = last_sums(got.at[:, at : at + 4, :], marks, norm.shape[0])
    for g in range(norm.shape[0]):
        norm_v[g, 0:1, :] = totals[g][1]
        norm_v[g, 1:2, :] = totals[g][0]
    norm_from_owners(get_split(got, at + 4, 2), marks, inner_v)
    for k, (value, out) in enumerate(((norm_v, grad_norm), (inner_v, grad_inner))):
        copies.append(pltpu.make_async_copy(value, out, sems.at[held + k]))
        copies[-1].start()
    keep = lax.broadcasted_iota(jnp.int32, (z_own.shape[1], LANES), 0) < cols
    for k, (z, dn, gs) in enumerate(((z_own, dn_own, gs_own), (z_for, dn_for, gs_for))):
        group = entry(tab, OWN if k == 0 else OTHER)
        shift_sum = own_of([t[0] for t in totals], group)
        gain_sum = own_of([t[1] for t in totals], group)
        count = group_count(marks, group) * pixels
        mean, rstd = keeps[2 * k : 2 * k + 1, :], keeps[2 * k + 1 : 2 * k + 2, :]
        a = rstd * gain_of(norm, group)
        b = -(a * rstd) * gain_sum / count
        c = -a * shift_sum / count

        def put(i, carry, z=z, dn=dn, mean=mean, a=a, b=b, c=c):
            v = a * dn[i].astype(F32) + b * (z[i] - mean) + c
            dz[i] = jnp.where(keep, v, 0.0).astype(BF16)
            return carry

        lax.fori_loop(0, rows, put, 0, unroll=4)
        place = half if k == 0 else 1 - half
        step = rows // 2
        for q in range(2):
            low = flat(dz[step * q : step * (q + 1)])
            for p in range(wide.shape[0]):
                values = mm_nt(low, w[LANES * p : LANES * (p + 1), :])
                wide[p, step * q : step * (q + 1)] = values.reshape(step, -1, LANES)

            def emit(i, carry, gs=gs, place=place):
                even = pl.ds(0, COLS, stride=2)
                for p in range(wide.shape[0]):
                    lanes = slice(LANES * p, LANES * (p + 1))
                    wide[p, 2 * i, even, :] = wide[p, 2 * i, even, :] + gs[i, :, lanes].astype(F32)
                    grad_v[place, 2 * i, :, lanes] = wide[p, 2 * i, 0:cols, :].astype(BF16)
                    grad_v[place, 2 * i + 1, :, lanes] = wide[p, 2 * i + 1, 0:cols, :].astype(BF16)
                return carry

            lax.fori_loop(step // 2 * q, step // 2 * (q + 1), emit, 0, unroll=True)
            part = pl.ds(step * q, step)
            copies.append(
                pltpu.make_async_copy(
                    grad_v.at[place, part], grad.at[place, part], sems.at[held + 2 + 2 * k + q]
                )
            )
            copies[-1].start()
    for copy in copies:
        copy.wait()


def put_rows(out, at, value):
    for j in range(value.shape[1] // LANES):
        out[at : at + value.shape[0], :] = value[:, LANES * j : LANES * (j + 1)].astype(BF16)
        at += value.shape[0]
    return at


def take_rows(source, at, out):
    rows = out.shape[0]
    for j in range(out.shape[1] // LANES):
        out[:, LANES * j : LANES * (j + 1)] = source(at, rows)
        at += rows
    return at


def share_out(tab, packed, used, kept, sent):
    if used < packed.shape[0]:
        packed[used:, :] = jnp.zeros((packed.shape[0] - used, LANES), BF16)
    half = half_of(tab)
    size = kept.shape[0] * kept.shape[1]
    for out, place in ((kept, half), (sent, 1 - half)):
        out[...] = packed[pl.ds(pl.multiple_of(size * place, 16), size), :].reshape(out.shape)


def g_most(
    tab, act_2b, x3, dz_2b, joined, dz_2a, act_1b, xee, w_p,
    got, labels, norm_c, norm_p, keeps, grad_pre_2, zc, zp,
    got_2c, norm_2c, keeps_2c, grad_pre, z_2c,
    kept, sent, gs_own, gs_oth, grad_norm_c, grad_norm_p, grad_norm_2c, own10, packed, dz_1c, dz_p, dz_2c,
):
    rows, outer = dz_2b.shape[0], zc.shape[2]
    pixels = 1.0 * rows * (COLS - 4)
    marks = labels[...]

    blocks = outer // LANES
    label = entry(tab, OWN)

    def wide_sums(source, count):
        values = [get_split(source, 2 * blocks * k, blocks) for k in range(count)]
        return [
            [line_of(over_group(v, marks, float(g))) for v in values]
            for g in range(norm_c.shape[0])
        ]

    totals = [group_sum(got, marks, float(g)) for g in range(norm_c.shape[0])]
    side = outer // 2
    lines = [
        [join([total[h : h + 1, side * k : side * (k + 1)] for h in (0, 1)]) for k in range(3)]
        for total in totals
    ]
    for k in range(2):
        own10[:, outer * k : outer * (k + 1)] = own_of([v[k] for v in lines], label)
        at = 2 * outer + LANES * k
        own10[:, at : at + LANES] = own_of([v[k : k + 1, 3 * side :] for v in totals], label)
    lines_2c = wide_sums(got_2c, 2)
    mean, a, b, c = backward_norm(
        tab, lambda g: (lines_2c[g][0], lines_2c[g][1]), marks, norm_2c, keeps_2c, pixels,
        grad_norm_2c,
    )
    gate = 0.25 * tiled(entry(tab, GATE), outer)
    normed_grad(dz_2c, grad_pre, z_2c, mean, a * gate, b, c)
    coefs = backward_norm(
        tab, lambda g: (lines[g][0], lines[g][1]), marks, norm_c, keeps.at[0:2], pixels, grad_norm_c
    )
    normed_grad(dz_1c, grad_pre_2, zc, *coefs)
    coefs = backward_norm(
        tab, lambda g: (lines[g][0], lines[g][2]), marks, norm_p, keeps.at[2:4], pixels, grad_norm_p
    )
    normed_grad(dz_p, grad_pre_2, zp, *coefs)
    at = put_rows(packed, 0, mm_tn(flat(act_2b[...]), flat(dz_2c[...])))
    low = flat(dz_2b[...])
    for y in range(3):
        at = put_rows(packed, at, mm_side(flat(x3[y : y + rows]), low))
    at = put_rows(packed, at, mm_side(flat(joined[...]), flat(dz_2a[...])))
    at = put_rows(packed, at, mm_tn(flat(act_1b[...]), flat(dz_1c[...])))
    at = put_rows(packed, at, mm_tn(flat(xee[...]), flat(dz_p[...])))
    share_out(tab, packed, at, kept, sent)
    half = half_of(tab)
    count = gs_own.shape[0]
    for k, gs in enumerate((gs_own, gs_oth)):
        first = count * (half if k == 0 else 1 - half)
        got = mm_nt(flat(dz_p[pl.ds(first, count)]), w_p[...])
        gs[...] = got.reshape(gs.shape).astype(BF16)


def g_xz(keeps, x_own, x_oth, z_own, z_oth, out, x_sum, low):
    rows, n = z_own.shape[0], LANES
    mean = keeps[0:1, :]
    low[:, :, n : 2 * n] = jnp.ones((rows, z_own.shape[1], n), BF16)
    value = None
    for x, z in ((x_own, z_own), (x_oth, z_oth)):

        def put(i, carry, z=z):
            low[i, :, 0:n] = (z[i] - mean).astype(BF16)
            return carry

        lax.fori_loop(0, rows, put, 0, unroll=4)
        term = mm_tn(flat(x[...]), flat(low[...]))
        value = term if value is None else value + term
    at = value.shape[0]
    out[0:at, :] = value[:, 0:n]
    if at < out.shape[0]:
        out[at:, :] = jnp.zeros((out.shape[0] - at, n), F32)
    x_sum[...] = value[:, n : 2 * n]


def g_xd(
    tab, sums_own, sums_oth, norm, keeps, x_sum, got_x, labels, x_own, x_oth, dn_own, dn_oth,
    z_own, z_oth, out, sums, low,
):
    rows = dn_own.shape[0]
    n = LANES
    pixels = 1.0 * (2 * rows) * (2 * (COLS - 4))
    sums[...] = sums_own[...] + sums_oth[...]
    a = keeps[1:2, :] * gain_of(norm, entry(tab, OWN))
    local = sums[0:1, :] / pixels
    mean = keeps[0:1, :]
    b = -(a * keeps[1:2, :]) * sums[1:2, :] / pixels
    value = None
    for x, dn, z in ((x_own, dn_own, z_own), (x_oth, dn_oth, z_oth)):

        def put(i, carry, dn=dn, z=z):
            low[i] = (a * (dn[i].astype(F32) - local) + b * (z[i] - mean)).astype(BF16)
            return carry

        lax.fori_loop(0, rows, put, 0, unroll=4)
        term = mm_tn(flat(x[...]), flat(low[...]))
        value = term if value is None else value + term
    marks, label = labels[...], entry(tab, OWN)
    total = over_group(get_split(got_x, 4, x_sum.shape[0] // n), marks, label)
    total = join([total[k : k + 1] for k in range(total.shape[0])])
    total = total / tiled(group_count(marks, label), total.shape[1])
    total = jnp.broadcast_to(total, (8, total.shape[1]))
    means = jnp.concatenate(
        [jnp.transpose(total[:, lanes])[:, 0:1] for lanes in columns(total.shape[1])], axis=0
    )
    value = value + (x_sum[...] - means) * (a * local)
    at = value.shape[0]
    out[0:at, :] = value.astype(BF16)
    if at < out.shape[0]:
        out[at:, :] = jnp.zeros((out.shape[0] - at, n), BF16)


def pack_last(tall, sums, found, kept, got, kept_1b, got_1b, send, *, stats_at):
    n = LANES
    devices = send.shape[0]
    piece, share = kept.shape[1], tall.shape[0] // devices
    first = kept.shape[0]
    second = first + kept_1b.shape[0]
    send[0:first, 0:piece, :] = (kept[...].astype(F32) + got[...].astype(F32)).astype(BF16)
    send[first:second, 0:piece, :] = (kept_1b[...].astype(F32) + got_1b[...].astype(F32)).astype(BF16)
    if second < devices:
        send[second:, 0:piece, :] = jnp.zeros((devices - second, piece, n), BF16)
    send[:, piece : piece + share, :] = tall[...].reshape(devices, share, n)
    put_split(send, stats_at, sums[...])
    put_split(send, stats_at + 4, found[...])


def last_sums(stats, marks, groups):
    values = stats[:, 0:2, :].astype(F32) + stats[:, 2:4, :].astype(F32)
    out = []
    for g in range(groups):
        total = jnp.sum(values * (marks == float(g)).astype(F32), axis=0)
        out.append((total[0:1], total[1:2]))
    return out


def add_all(got, labels, norm, keeps_all, xz_got, found, out, *, at, pixels):
    devices, n = got.shape[0], LANES
    half = devices // 2
    share = xz_got.shape[2] // n - 2
    piece = (out.shape[1] - share - 4) // 2
    marks = labels[...]
    value = jnp.sum(got[:, piece : piece + share, :].astype(F32), axis=0)
    products = get_split(got, at, 2)[:, 1:2, :]
    lack = jnp.zeros(products.shape, F32)
    for g in range(norm.shape[0]):
        rstd = keeps_all[2 * g + 1 : 2 * g + 2, :]
        factor = -(rstd * rstd * norm[g, 0:1, :]) / pixels
        same = (marks == float(g)).astype(F32)
        middle = jnp.sum(products * same, axis=0) / jnp.sum(same, axis=0)
        lack = lack + (middle[None] - products) * (factor[None] * same)
    rows = [
        jnp.sum(xz_got[:, :, n * (2 + q) : n * (3 + q)] * lack, axis=0) for q in range(share)
    ]
    value = value + jnp.concatenate(rows, axis=0)
    for k in (0, 1):
        total = jnp.sum(got[half * k : half * (k + 1), 0:piece, :].astype(F32), axis=0).astype(BF16)
        out[:, piece * k : piece * (k + 1), :] = jnp.broadcast_to(
            total[None], (out.shape[0], piece, n)
        )
    out[:, 2 * piece : 2 * piece + share, :] = jnp.broadcast_to(
        value.astype(BF16)[None], (out.shape[0], share, n)
    )
    put_split(out, 2 * piece + share, found[...])


def unpack(tab, labels, *refs, first, second, piece):
    parts, outs, values = refs[: 2 * NEAR], refs[2 * NEAR : 2 * NEAR + 8], refs[2 * NEAR + 8 :]
    *values, tall, packed, found, sems = values
    half, minor = half_of(tab), half_of(tab, MINOR)
    far, share = parts[0].shape[0], tall.shape[1]
    for k, part in enumerate(parts):
        core = half if k < NEAR else 1 - half
        base = core * (far * NEAR) + lax.bitwise_xor(minor, jnp.int32(k % NEAR))

        def place(z, carry, part=part, base=base):
            owner = base + NEAR * z
            for h in (0, 1):
                packed[h, owner] = part[z, piece * h : piece * (h + 1), :]
            tall[owner] = part[z, 2 * piece : 2 * piece + share, :].astype(F32)
            sums = part[z, 2 * piece + share :, :].astype(F32)
            found[owner] = sums[0:2] + sums[2:4]
            return carry

        lax.fori_loop(0, far, place, 0, unroll=min(far, 4))
    copies = [
        pltpu.make_async_copy(value, out, sems.at[k]) for k, (value, out) in enumerate(zip(values, outs))
    ]
    most = [flat(packed[h, 0:first]) for h in (0, 1)]
    last = [flat(packed[h, first : first + second]) for h in (0, 1)]
    size = first * piece

    def source(at, rows):
        pieces = []
        if at < size:
            pieces.append(most[0][at : min(at + rows, size)])
        if at + rows > size:
            pieces.append(most[1][max(at - size, 0) : at + rows - size])
        pieces = [v.astype(F32) for v in pieces]
        return pieces[0] if len(pieces) == 1 else stack(pieces)

    at = 0
    for k, value in enumerate(values[0:5]):
        at = take_rows(source, at, value)
        copies[k].start()
    w_1b, w_1a, grad_norm = values[5:8]
    size = second * piece
    w_1b[0:size] = last[0].astype(F32)
    w_1b[size:] = last[1][0 : w_1b.shape[0] - size].astype(F32)
    copies[5].start()
    w_1a[...] = flat(tall[...])[0 : w_1a.shape[0]]
    copies[6].start()
    norm_from_owners(found[...], labels[...], grad_norm)
    copies[7].start()
    for copy in copies:
        copy.wait()


def norm_from_owners(found, marks, grad_norm):
    for g in range(grad_norm.shape[0]):
        total = over_group(found, marks, float(g)) / group_count(marks, float(g))
        grad_norm[g, 0:1, :] = total[1:2]
        grad_norm[g, 1:2, :] = total[0:1]


def gather(send):
    return lax.all_to_all(send, AXES, 0, 0)


def tie(*values):
    return lax.optimization_barrier(values)


def swap(block):
    return lax.ppermute(block, "rows", [(0, 1), (1, 0)])


def body(
    images, w_1a, w_1b, w_1c, w_1p, w_2a, w_2b, w_2c,
    norm_1a, norm_1b, norm_1c, norm_1p, norm_2a, norm_2b, norm_2c,
    cotangent, group, width, gate,
):
    devices = lax.axis_size("rows") * lax.axis_size("batch")
    place = lax.axis_index(AXES).astype(jnp.int32).reshape(1)
    norms = (norm_1a, norm_1b, norm_1c, norm_1p, norm_2a, norm_2b, norm_2c)
    norm_1a, norm_1b, norm_1c, norm_1p, norm_2a, norm_2b, norm_2c = (
        v.transpose(1, 0, 2) for v in norms
    )
    outer, inputs = w_1c.shape[1], w_1a.shape[0]
    rows = cotangent.shape[1]
    cols_in = 2 * COLS
    n, m = LANES, devices

    def send(stats, channels=LANES):
        return ((m, channels // LANES, stats * LANES), F32)

    def maps(channels, dtype=F32):
        return ((rows, COLS, channels), dtype)

    def scratch(channels, dtype=F32):
        return pltpu.VMEM((rows, COLS, channels), dtype)

    def params(*arrays):
        return [(a.shape, F32) for a in arrays]

    def mean_scale(channels, count=1):
        return ((2 * count, channels), F32)

    wide_in = ((rows, cols_in, inputs), BF16)
    wide_z = ((rows, cols_in, n), F32)
    raw = images.shape
    tab, x_own, x_for, z_own, z_for, s1 = stage(
        functools.partial(f1, batch=devices // 2), [((8, n), F32), wide_in, wide_in, wide_z, wide_z, send(5)],
        [*(pltpu.SMEM(v.shape, jnp.int32) for v in (place, group, width, gate)),
         pltpu.VMEM(raw, BF16), pltpu.VMEM(w_1a.shape, BF16), pltpu.VMEM((8, n), F32),
         pltpu.SemaphoreType.DMA((7,))],
        hbm=(0, 1, 2, 3, 4, 5),
    )(place, group, width, gate, images, w_1a)
    s1, v_1b, v_2b = tie(s1, w_1b, w_2b)
    built = stage(
        prepare,
        [(v, BF16) for v in (
            (3 * n, n), (3 * n, 2 * n), (3 * n, 2 * n), (3 * n, n),
            (2 * n, 2 * n), (2 * n, 4 * n), (2 * n, 3 * n), (n, 3 * n),
        )],
    )(v_1b, v_2b)
    s1, x_for, w_even, w_odd, w_two, w_last, b_even, b_odd, b_two, b_last = tie(s1, x_for, *built)
    x_oth = swap(x_for)
    g1 = gather(s1)
    g1, x_oth = tie(g1, x_oth)
    xee, z_1p, stats_1p = stage(
        f1_strided,
        [maps(inputs, BF16), maps(outer), ((1, inputs + outer), F32)],
        [pltpu.VMEM((inputs // n, cols_in, n), F32)],
    )(tab, x_own, x_oth, w_1p)
    xs, z_1b, s2, labels, k_1a, k_all, z_oth = stage(
        f2,
        [((rows + 1, COLS, 6 * n), BF16), maps(n), send(2 + (inputs + outer) // n),
         ((m, 1, n), F32), mean_scale(n, 2), mean_scale(n, norm_1a.shape[0]), wide_z],
    )(tab, g1, z_own, x_oth, w_1a, norm_1a, w_even, w_odd, stats_1p)
    g2 = gather(s2)
    share_1 = -(-n // devices)
    p_rows = ((devices, 2 * share_1, n), BF16)
    own_rows = ((devices, 2 * share_1, n), F32)
    wide_rows = outer // n
    p_at = 2 + wide_rows
    high_3 = -(-(p_at + 2 * share_1) // 16) * 16
    act_1b, z_1c, s3, k_1b, k_p, slope_1b, q_1b, p_1b, own_1b = stage(
        functools.partial(f3, share=share_1),
        [maps(n, BF16), maps(outer), ((devices, high_3, n), BF16), mean_scale(n),
         mean_scale(outer), maps(n), ((2, n), F32), p_rows, own_rows],
        [scratch(4 * n, BF16), pltpu.VMEM(p_rows[0], BF16)],
    )(tab, g2, labels, z_1b, norm_1b, w_1c, w_1p)
    g3 = gather(s3)
    high = -(-(8 + 2 * share_1) // 16) * 16
    joined, slope, z_2a, s4, k_cp = stage(
        f4,
        [maps(outer, BF16), maps(outer), maps(n), ((devices, high, n), BF16),
         mean_scale(outer, 2)],
    )(tab, g3, labels, z_1c, z_1p, norm_1c, norm_1p, k_p, w_1c, w_2a, p_1b, q_1b)
    share = -(-inputs // devices)
    half_in = ((rows, cols_in, n), BF16)
    s4, k_1a = tie(s4, k_1a)
    xz, x_sum = stage(
        g_xz, [((devices * share, n), F32), ((inputs, n), F32)],
        [pltpu.VMEM((rows, cols_in, 2 * n), BF16)],
    )(k_1a, x_own, x_oth, z_own, z_oth)
    s4, xz, x_sum = tie(s4, xz, x_sum)
    g4 = gather(s4)
    x3, z_2b, s5, k_2a = stage(
        f5, [((rows + 2, COLS, 3 * n), BF16), maps(n), send(2 + share), mean_scale(n)]
    )(tab, g4, labels, z_2a, norm_2a, w_two, w_last, xz)
    g5 = gather(s5)
    high_6 = -(-(p_at + 4 * share_1) // 8) * 8
    act_2b, z_2c, s6, k_2b, slope_2b, q_2b, own_2b = stage(
        functools.partial(f6, share=share_1),
        [maps(n, BF16), maps(outer), ((devices, high_6, n), BF16), mean_scale(n), maps(n),
         ((2, n), F32), own_rows],
        [scratch(4 * n, BF16), *(pltpu.VMEM(p_rows[0], BF16) for _ in range(2))],
    )(tab, g5, labels, z_2b, norm_2b, w_2c)
    g6 = gather(s6)
    high_7 = -(-(4 * wide_rows + 8 + 2 * share_1) // 16) * 16
    result, grad_pre, s7, k_2c, d_2b = stage(
        functools.partial(b7, share=share_1, p_at=p_at),
        [(cotangent.shape[1:], BF16), maps(outer), ((devices, high_7, n), BF16),
         mean_scale(outer), maps(n)],
        [pltpu.VMEM((COLS, outer), F32), scratch(outer, BF16)],
    )(tab, g6, labels, joined, z_2c, norm_2c, w_2c, cotangent[0], slope_2b, z_2b, k_2b, q_2b)
    g7 = gather(s7)
    dz_2b, dout_2a, s9, found_2b = stage(
        functools.partial(b9, share=share_1, p_at=p_at),
        [maps(n, BF16), maps(n), ((devices, high, n), BF16), ((2, n), F32)],
        [pltpu.VMEM((rows + 2, COLS, 3 * n), BF16), scratch(n)],
    )(tab, g7, labels, norm_2c, k_2c, w_2c, g6, act_2b, slope_2b, d_2b, z_2b, norm_2b, k_2b,
      b_two, b_last, z_2a, norm_2a, k_2a, x_sum, g4, g3, own_2b)
    g9 = gather(s9)
    dz_2a, grad_pre_2, s10, grad_norm_2a, d_1b = stage(
        b10,
        [maps(n, BF16), maps(outer), ((devices, 2, 3 * outer // 2 + n), F32), *params(norm_2a), maps(n)],
        [scratch(outer), scratch(outer, BF16)],
    )(tab, g9, labels, dout_2a, z_2a, norm_2a, k_2a, w_2a, grad_pre, slope, z_1c, z_1p, k_cp,
      norm_1c, w_1c, slope_1b, z_1b, k_1b)
    g10 = gather(s10)
    half_map = ((rows // 2, COLS, inputs), BF16)
    most_rows = sum(v.size for v in (w_2c, w_2b, w_2a, w_1c, w_1p)) // n
    rows_1b = w_1b.size // n
    piece = 16
    while -(-most_rows // (2 * piece)) - (-rows_1b // (2 * piece)) > devices:
        piece += 16
    first, second = -(-most_rows // (2 * piece)), -(-rows_1b // (2 * piece))
    part, part_1b = ((first, piece, n), BF16), ((second, piece, n), BF16)
    kept, sent, gs_own, gs_send, grad_norm_1c, grad_norm_1p, grad_norm_2c, own10 = stage(
        g_most,
        [part, part, half_map, half_map, *params(norm_1c, norm_1p, norm_2c),
         ((1, 2 * outer + 2 * n), F32)],
        [pltpu.VMEM((2 * first * piece, n), BF16), *(scratch(outer, BF16) for _ in range(3))],
    )(tab, act_2b, x3, dz_2b, joined, dz_2a, act_1b, xee, w_1p,
      g10, labels, norm_1c, norm_1p, k_cp, grad_pre_2, z_1c, z_1p,
      g7, norm_2c, k_2c, grad_pre, z_2c)
    got, gs_for = swap(sent), swap(gs_send)
    half_in = ((rows, cols_in, n), BF16)
    d2, kept_1b, sent_1b, found_1b = stage(
        functools.partial(b12, share=share_1, q_at=4 + 2 * share_1, p_at=4 + 2 * (inputs // n)),
        [((rows + 1, COLS, 2 * n), BF16), part_1b, part_1b, ((2, n), F32)],
        [scratch(n, BF16), pltpu.VMEM((2 * second * piece, n), BF16), scratch(n)],
    )(tab, own10, labels, norm_1c, k_cp, w_1c, g3, g4, g9, own_1b, act_1b, slope_1b, d_1b,
      z_1b, norm_1b, k_1b, xs)
    got_1b = swap(sent_1b)
    sides = []
    for own, z in ((False, z_oth), (True, z_own)):
        sides.append(
            stage(
                functools.partial(b12_images, own=own), [half_in, ((2, n), F32)],
                [pltpu.VMEM((rows // 2, COLS, 2 * n), F32), pltpu.VMEM((rows // 2, COLS, 2 * n), F32),
                 pltpu.VMEM((2, cols_in, n), F32)],
            )(tab, d2, b_even, b_odd, z, norm_1a, k_1a)
        )
        if not own:
            dn_for = swap(sides[0][0])
            d2, _ = tie(d2, sides[0][0])
    (dn_send, sums_send), (dn_own, sums_own) = sides
    stats_at = piece + -(-share // 8) * 8
    high = -(-(stats_at + 8) // 16) * 16
    tall, sums_1a = stage(
        g_xd, [((devices * share, n), BF16), ((2, n), F32)], [pltpu.VMEM(half_in[0], BF16)]
    )(tab, sums_own, sums_send, norm_1a, k_1a, x_sum, g9, labels, x_own, x_oth, dn_own, dn_send,
      z_own, z_oth)
    tall, gs_for, dn_for = tie(tall, gs_for, dn_for)
    (s12,) = stage(
        functools.partial(pack_last, stats_at=stats_at), [((devices, high, n), BF16)]
    )(tall, sums_1a, found_1b, kept, got, kept_1b, got_1b)
    g12 = gather(s12)
    pixels = 4.0 * images.shape[1] * images.shape[1]
    batch = devices // 2
    far = batch // NEAR
    (mine,) = stage(
        functools.partial(add_all, at=stats_at, pixels=pixels),
        [((far, 2 * piece + share + 4, n), BF16)],
    )(g12, labels, norm_1a, k_all, g5, found_2b)
    columns_of = [[k + NEAR * z for z in range(far)] for k in range(NEAR)]
    along = lax.all_to_all(mine, "batch", 0, 0, axis_index_groups=columns_of)
    near = [
        lax.ppermute(along, "batch", [(i, i ^ k) for i in range(batch)]) for k in range(1, NEAR)
    ]
    finished = (
        result, grad_norm_1c, grad_norm_1p, grad_norm_2a, grad_norm_2c
    )
    held = len(finished)
    *finished, grad_images, grad_norm_1a, grad_norm_1b = stage(
        functools.partial(b13, at=stats_at, held=held),
        [*((v.shape, v.dtype) for v in finished), (images.shape, BF16), *params(norm_1a, norm_1b)],
        [pltpu.VMEM(half_in[0], BF16), pltpu.VMEM((inputs // n, rows, cols_in, n), F32),
         pltpu.VMEM(images.shape, BF16), *(pltpu.VMEM(norm_1a.shape, F32) for _ in range(2)),
         pltpu.SemaphoreType.DMA((held + 6,))],
        hbm_out=range(held + 3),
    )(tab, g12, labels, norm_1a, k_1a, w_1a, z_own, z_for, dn_own, dn_for, gs_own, gs_for, *finished)
    result, grad_norm_1c, grad_norm_1p, grad_norm_2a, grad_norm_2c = finished
    *near, grad_images = tie(*near, grad_images)
    parts = [along, *near]
    weights = (w_2c, w_2b.reshape(-1, n), w_2a, w_1c, w_1p, w_1b.reshape(-1, n), w_1a)
    t_2c, t_2b, t_2a, t_1c, t_1p, t_1b, t_1a, grad_norm_2b = stage(
        functools.partial(unpack, first=first, second=second, piece=piece),
        [(v.shape, F32) for v in (*weights, norm_2b)],
        [*(pltpu.VMEM(v.shape, F32) for v in (*weights, norm_2b)),
         pltpu.VMEM((devices, share, n), F32), pltpu.VMEM((2, devices, piece, n), BF16),
         pltpu.VMEM((devices, 2, n), F32), pltpu.SemaphoreType.DMA((8,))],
        hbm_out=range(8),
    )(tab, labels, *parts, *(swap(v) for v in parts))
    grads = (
        grad_norm_1a, grad_norm_1b, grad_norm_1c, grad_norm_1p,
        grad_norm_2a, grad_norm_2b, grad_norm_2c,
    )
    return (
        result[None], grad_images, t_1a, t_1b.reshape(w_1b.shape), t_1c, t_1p, t_2a,
        t_2b.reshape(w_2b.shape), t_2c, *[v.transpose(1, 0, 2) for v in grads],
    )


def solution(mesh):
    return jax.shard_map(
        body,
        mesh=mesh,
        in_specs=(
            P("batch", "rows", None, None),
            *[P()] * 14,
            P(("batch", "rows"), None, None, None),
            P("batch"),
            P(),
            P(),
        ),
        out_specs=(
            P(("batch", "rows"), None, None, None),
            P("batch", "rows", None, None),
            *[P()] * 14,
        ),
        check_vma=False,
    )
```

```python
import functools

import jax
import jax.numpy as jnp
from jax import lax
from jax.experimental import pallas as pl
from jax.experimental.pallas import tpu as pltpu
from jax.sharding import PartitionSpec as P

EPSILON = 1e-05
F32 = jnp.float32
BF16 = jnp.bfloat16
AXES = ("rows", "batch")
VMEM_LIMIT = 14 * 1024 * 1024
LANES = 128
COLS = 32
NEAR = 4


def full(memory=pltpu.VMEM):
    return pl.BlockSpec(memory_space=memory)


def stage(kernel, outs, scratch=(), hbm=(), hbm_out=()):
    def place(i, outside):
        return pltpu.HBM if i in outside else pltpu.VMEM

    def call(*args):
        args = [
            pltpu.with_memory_space_constraint(a, pltpu.HBM) if i in hbm else a
            for i, a in enumerate(args)
        ]
        return pl.pallas_call(
            kernel,
            out_shape=tuple(jax.ShapeDtypeStruct(s, d) for s, d in outs),
            in_specs=[full(place(i, hbm)) for i in range(len(args))],
            out_specs=tuple(
                full(place(i, hbm_out)) for i in range(len(outs))
            ),
            scratch_shapes=list(scratch),
            compiler_params=pltpu.CompilerParams(vmem_limit_bytes=VMEM_LIMIT),
            name=(kernel.func if isinstance(kernel, functools.partial) else kernel).__name__,
        )(*args)

    return call


def silu_of_half(u):
    return u + u * jnp.tanh(u)


def slope_of_half(u):
    t = jnp.tanh(u)
    return (0.5 + 0.5 * t) * (1.0 + u - u * t)


def fold(x):
    return (x[0:8] + x[8:16]) + (x[16:24] + x[24:32])


def row(total, stat):
    blocks = total.shape[0]
    pieces = [total[j : j + 1, LANES * stat : LANES * (stat + 1)] for j in range(blocks)]
    return pieces[0] if blocks == 1 else jnp.concatenate(pieces, axis=1)


def spread(out_ref, rows):
    blocks = out_ref.shape[1]
    for stat, values in enumerate(rows):
        for j in range(blocks):
            piece = values[:, LANES * j : LANES * (j + 1)]
            out_ref[:, j : j + 1, LANES * stat : LANES * (stat + 1)] = jnp.broadcast_to(
                piece[None], (out_ref.shape[0], 1, LANES)
            )


def group_sum(got_ref, labels, label):
    same = (labels == label).astype(F32)
    stats = got_ref.shape[2] // LANES
    parts = [
        jnp.sum(got_ref[:, :, LANES * s : LANES * (s + 1)] * same, axis=0) for s in range(stats)
    ]
    return jnp.concatenate(parts, axis=1) if stats > 1 else parts[0]


def group_count(labels, label):
    return jnp.sum((labels == label).astype(F32), axis=0)


def tiled(values, channels):
    return jnp.concatenate([values] * (channels // LANES), axis=1) if channels > LANES else values


def moments(first, second, pixels):
    mean = first / pixels
    return mean, lax.rsqrt(second / pixels - mean * mean + EPSILON)


def own_of(values, label):
    out = values[0]
    label = tiled(label, out.shape[1])
    for g in range(1, len(values)):
        out = jnp.where(label == float(g), values[g], out)
    return out


def gain_of(norm_ref, label):
    return own_of([norm_ref[g, 0:1, :] for g in range(norm_ref.shape[0])], label)


def shift_of(norm_ref, label):
    return own_of([norm_ref[g, 1:2, :] for g in range(norm_ref.shape[0])], label)


def valid_cols(channels):
    return lax.broadcasted_iota(jnp.int32, (COLS, channels), 0) < COLS - 4


def chan_mask(tab):
    return lax.broadcasted_iota(jnp.int32, (1, LANES), 1).astype(F32) < entry(tab, LIMIT)


def flat(x):
    return x.reshape(x.shape[0] * x.shape[1], x.shape[2])


def mm(a, b):
    return jnp.dot(a, b, preferred_element_type=F32)


def mm_nt(a, b):
    return lax.dot_general(a, b, (((1,), (1,)), ((), ())), preferred_element_type=F32)


def mm_tn(a, b):
    return lax.dot_general(a, b, (((0,), (0,)), ((), ())), preferred_element_type=F32)


def mm_side(a, b):
    turned = mm_tn(b, a)
    blocks = [
        jnp.transpose(turned[:, LANES * j : LANES * (j + 1)]) for j in range(a.shape[1] // LANES)
    ]
    return blocks[0] if len(blocks) == 1 else jnp.concatenate(blocks, axis=0)


def zeros8(channels):
    return jnp.zeros((8, channels), F32)


def down(x):
    return jnp.sum(x, axis=0, keepdims=True)


OWN, OTHER, HALF, LIMIT, GATE, MINOR = range(6)


def entry(tab, k):
    return tab[k : k + 1, :]


def half_of(tab, k=HALF):
    return (jnp.sum(entry(tab, k)) * (1.0 / LANES)).astype(jnp.int32)


def prepare(w1b, w2b, w_even, w_odd, w_two, w_last, b_even, b_odd, b_two, b_last):
    n = LANES
    for k, (y, x) in enumerate(((1, 1), (1, 2), (1, 0))):
        w_even[n * k : n * (k + 1), :] = w1b[y, x]
    for k, (low, high) in enumerate((((2, 1), (0, 1)), ((2, 2), (0, 2)), ((2, 0), (0, 0)))):
        w_odd[n * k : n * (k + 1), 0:n] = w1b[low]
        w_odd[n * k : n * (k + 1), n : 2 * n] = w1b[high]
    for x in range(3):
        w_two[n * x : n * (x + 1), 0:n] = w2b[0, x]
        w_two[n * x : n * (x + 1), n : 2 * n] = w2b[1, x]
        w_last[n * x : n * (x + 1), :] = w2b[2, x]
        b_two[0:n, n * x : n * (x + 1)] = w2b[1, x]
        b_two[n : 2 * n, n * x : n * (x + 1)] = w2b[2, x]
        b_last[:, n * x : n * (x + 1)] = w2b[0, x]
    nothing = jnp.zeros((n, n), BF16)
    b_even[0:n, 0:n] = w1b[1, 1]
    b_even[0:n, n : 2 * n] = nothing
    b_even[n : 2 * n, 0:n] = w1b[1, 2]
    b_even[n : 2 * n, n : 2 * n] = w1b[1, 0]
    for k, top in ((0, 2), (1, 0)):
        b_odd[0:n, 2 * n * k : 2 * n * k + n] = w1b[top, 1]
        b_odd[0:n, 2 * n * k + n : 2 * n * (k + 1)] = nothing
        b_odd[n : 2 * n, 2 * n * k : 2 * n * k + n] = w1b[top, 2]
        b_odd[n : 2 * n, 2 * n * k + n : 2 * n * (k + 1)] = w1b[top, 0]


def widen(source, x_pad):
    rows, cols, chans = source.shape
    gap = x_pad.shape[1] - cols

    def put(i, carry):
        x_pad[i, 0:cols, :] = source[i]
        x_pad[i, cols : cols + gap, :] = jnp.zeros((gap, chans), BF16)
        return carry

    lax.fori_loop(0, rows, put, 0, unroll=4)


def first_project(x_pad, w, z, stats=True):
    rows = x_pad.shape[0]
    step = rows // 4
    sums, squares = zeros8(LANES), zeros8(LANES)
    for c in range(4):
        values = mm(flat(x_pad[step * c : step * (c + 1)]), w[...])
        z[step * c : step * (c + 1)] = values.reshape(step, x_pad.shape[1], LANES)
        if stats:
            parts = values.reshape(-1, 8, LANES)
            sums = sums + jnp.sum(parts, axis=0)
            squares = squares + jnp.sum(parts * parts, axis=0)
    return sums, squares


def f1(
    place_at, group_at, width_at, gate_at, images, w_at, tab, x_own, x_for, z_own, z_for, send,
    place_ref, group, width, gate, raw, w, found, sems, *, batch,
):
    pairs = (
        (place_at, place_ref), (group_at, group), (width_at, width), (gate_at, gate), (w_at, w),
        (images.at[0], raw.at[0]), (images.at[1], raw.at[1]),
    )
    copies = [pltpu.make_async_copy(a, b, sems.at[k]) for k, (a, b) in enumerate(pairs)]
    for k in (0, 4, 5, 6, 1, 2, 3):
        copies[k].start()
    for k in (0, 4, 5):
        copies[k].wait()
    half = lax.div(place_ref[0], batch)
    sides = ((x_own, z_own), (x_for, z_for))

    def one(k):
        for place in (0, 1):

            @pl.when(half == place)
            def _():
                x_pad, z = sides[k] if place == 0 else sides[1 - k]
                widen(raw.at[k], x_pad)
                sums, squares = first_project(x_pad, w, z)
                at = 2 * (k if place == 0 else 1 - k)
                found[at : at + 1, :] = down(sums)
                found[at + 1 : at + 2, :] = down(squares)

    one(0)
    copies[6].wait()
    one(1)
    for k in (1, 2, 3):
        copies[k].wait()
    rows = [found[k : k + 1, :] for k in range(4)]
    own, other = group[half], group[1 - half]
    values = {
        OWN: own, OTHER: other, HALF: half, LIMIT: w.shape[1] // 4 * width[own], GATE: gate[own],
        MINOR: lax.rem(lax.rem(place_ref[0], batch), NEAR),
    }
    tab[...] = jnp.zeros(tab.shape, F32)
    for k, v in values.items():
        tab[k : k + 1, :] = jnp.full((1, LANES), v.astype(F32))
    spread(send, [*rows, jnp.full((1, LANES), (own + 4 * other).astype(F32))])


def f1_strided(tab, x_own, x_oth, w, xee, z, stats, wide):
    half = half_of(tab)
    rows = x_own.shape[0] // 2
    for k, x_pad in enumerate((x_own, x_oth)):
        first = rows * (half if k == 0 else 1 - half)

        def put(i, carry, x_pad=x_pad, first=first):
            for b in range(wide.shape[0]):
                lanes = slice(LANES * b, LANES * (b + 1))
                wide[b] = x_pad[2 * i, :, lanes].astype(F32)
                xee[first + i, :, lanes] = wide[b, pl.ds(0, COLS, stride=2), :].astype(BF16)
            return carry

        lax.fori_loop(0, rows, put, 0, unroll=2)
    total = 2 * rows
    step = total // 7
    chans = z.shape[2]
    squares = zeros8(chans)
    for c in range(7):
        values = mm(flat(xee[step * c : step * (c + 1)]), w[...])
        z[step * c : step * (c + 1)] = values.reshape(step, COLS, chans)
        parts = values.reshape(-1, 8, chans)
        squares = squares + jnp.sum(parts * parts, axis=0)
    ones = jnp.ones((8, total * COLS), BF16)
    stats[:, 0 : w.shape[0]] = mm(ones, flat(xee[...]))[0:1]
    stats[:, w.shape[0] :] = down(squares)


def scale_shift(got, labels, tab, norm, pixels, slot=0):
    label = entry(tab, OWN)
    total = group_sum(got, labels, label)
    chans = norm.shape[2]
    count = tiled(group_count(labels, label), chans) * pixels
    mean, rstd = moments(row(total, 2 * slot), row(total, 2 * slot + 1), count)
    gain, shift = gain_of(norm, entry(tab, OWN)), shift_of(norm, entry(tab, OWN))
    return mean, rstd, gain, shift, count


def conv_stats(z, source, pair, single, send, extra=()):
    keep = valid_cols(LANES)[None]
    rows = z.shape[0]
    step = rows // 4
    (lanes_2, w_2, offsets), (lanes_1, w_1, offset) = pair, single
    sums, squares = zeros8(LANES), zeros8(LANES)
    base = min(offsets)
    for c in range(4):
        at = step * c
        both = mm(flat(source[at + base : at + base + step + 1, :, lanes_2]), w_2)
        values = mm(flat(source[at + offset : at + offset + step, :, lanes_1]), w_1)
        for k, own in enumerate(offsets):
            skip = COLS * (own - base)
            values = values + both[skip : skip + step * COLS, LANES * k : LANES * (k + 1)]
        values = jnp.where(keep, values.reshape(step, COLS, LANES), 0.0)
        z[at : at + step] = values
        parts = values.reshape(-1, 8, LANES)
        sums = sums + jnp.sum(parts, axis=0)
        squares = squares + jnp.sum(parts * parts, axis=0)
    spread(send, [down(sums), down(squares), *extra])


def f2(
    tab, got, z_own, x_oth, w, norm, w_even, w_odd, stats_p,
    xs, z, send, labels, keeps, keeps_all, z_oth,
):
    codes = got[:, :, 4 * LANES : 5 * LANES]
    others = jnp.floor(0.25 * codes)
    marks = codes - 4.0 * others
    labels[...] = marks
    rows = xs.shape[0] - 1
    pixels = 4.0 * rows * (COLS - 4)
    first_project(x_oth, w, z_oth, False)
    for g in range(norm.shape[0]):
        mine, theirs = (marks == float(g)).astype(F32), (others == float(g)).astype(F32)
        totals = [
            jnp.sum(
                got[:, :, LANES * s : LANES * (s + 1)] * mine
                + got[:, :, LANES * (s + 2) : LANES * (s + 3)] * theirs,
                axis=0,
            )
            for s in (0, 1)
        ]
        mean, rstd = moments(*totals, group_count(marks, float(g)) * pixels)
        keeps_all[2 * g : 2 * g + 1, :] = mean
        keeps_all[2 * g + 1 : 2 * g + 2, :] = rstd
    for k, slot in enumerate((OWN, OTHER)):
        for q in (0, 1):
            choices = [keeps_all[2 * g + q : 2 * g + q + 1, :] for g in range(norm.shape[0])]
            keeps[2 * k + q : 2 * k + q + 1, :] = own_of(choices, entry(tab, slot))
    mean, rstd = keeps[0:1, :], keeps[1:2, :]
    gain, shift = gain_of(norm, entry(tab, OWN)), shift_of(norm, entry(tab, OWN))
    scale = rstd * gain
    bias = 0.5 * (shift - mean * scale)
    scale = 0.5 * scale
    keep = valid_cols(LANES) & chan_mask(tab)
    half = half_of(tab)
    xs[0] = jnp.zeros(xs.shape[1:], BF16)
    n = LANES
    for k, zz in enumerate((z_own, z_oth)):
        first = 1 + (rows // 2) * (half if k == 0 else 1 - half)

        def put(i, carry, zz=zz, first=first):
            lane = 0
            for a in (0, 1):
                for b in (0, 1):
                    u = zz[2 * i + a, pl.ds(b, COLS, stride=2), :] * scale + bias
                    act = jnp.where(keep, silu_of_half(u), 0.0)
                    xs[first + i, :, lane : lane + n] = act.astype(BF16)
                    lane += n
                    if b == 1:
                        moved = pltpu.roll(act, 1, 0)
                        xs[first + i, :, lane : lane + n] = moved.astype(BF16)
                        lane += n
            return carry

        lax.fori_loop(0, rows // 2, put, 0, unroll=2)
    extra = [stats_p[:, lanes] for lanes in columns(stats_p.shape[1])]
    pair = (slice(3 * n, 6 * n), w_odd[...], (1, 0))
    conv_stats(z, xs, pair, (slice(0, 3 * n), w_even[...], 1), send, extra)


def project(act, w, z):
    rows, chans = z.shape[0], z.shape[2]
    step = rows // 7
    squares = zeros8(chans)
    for c in range(7):
        values = mm(flat(act[step * c : step * (c + 1)]), w[...])
        z[step * c : step * (c + 1)] = values.reshape(step, COLS, chans)
        parts = values.reshape(-1, 8, chans)
        squares = squares + jnp.sum(parts * parts, axis=0)
    return down(squares)


def join(pieces):
    return pieces[0] if len(pieces) == 1 else jnp.concatenate(pieces, axis=1)


def columns(channels):
    return [slice(LANES * j, LANES * (j + 1)) for j in range(channels // LANES)]


def three_parts(sums):
    high = sums.astype(BF16)
    rest = sums - high.astype(F32)
    mid = rest.astype(BF16)
    low = (rest - mid.astype(F32)).astype(BF16)
    lines = [v.astype(F32) for v in (high, mid, low)]
    lines.append(jnp.zeros((13, sums.shape[1]), F32))
    return jnp.concatenate(lines, axis=0).astype(BF16)


def through(sums, w):
    return down(mm(three_parts(sums), w))


def put_split(send, at, values):
    rows = values.shape[0]
    high = values.astype(BF16)
    rest = (values - high.astype(F32)).astype(BF16)
    for k, part in enumerate((high, rest)):
        send[:, at + rows * k : at + rows * (k + 1), :] = jnp.broadcast_to(
            part[None], (send.shape[0], rows, LANES)
        )


def get_split(got, at, rows):
    return got[:, at : at + rows, :].astype(F32) + got[:, at + rows : at + 2 * rows, :].astype(F32)


def over_group(values, marks, label):
    return jnp.sum(values * (marks == label).astype(F32), axis=0)


def stack(rows):
    return jnp.concatenate(rows, axis=0)


def pair_products(tab, z, norm, keeps, act, act_sum, slope, both):
    rows = z.shape[0]
    label = entry(tab, OWN)
    mean, rstd = keeps[0:1, :], keeps[1:2, :]
    scale = rstd * gain_of(norm, label)
    bias = 0.5 * (shift_of(norm, label) - mean * scale)
    scale = 0.5 * scale
    keep = valid_cols(LANES) & chan_mask(tab)
    middle = act_sum * (1.0 / (rows * (COLS - 4)))

    def put(i, carry):
        zz = z[i]
        s = jnp.where(keep, slope_of_half(zz * scale + bias), 0.0)
        sx = s * ((zz - mean) * rstd)
        slope[i] = s
        for k, v in enumerate((s, sx)):
            high = v.astype(BF16)
            both[i, :, LANES * k : LANES * (k + 1)] = high
            both[i, :, LANES * (k + 2) : LANES * (k + 3)] = (v - high.astype(F32)).astype(BF16)
        return carry[0] + fold(s), carry[1] + fold(sx)

    sums = lax.fori_loop(0, rows, put, (zeros8(LANES), zeros8(LANES)), unroll=4)
    sums = [down(v) for v in sums]
    product = mm_tn(flat(act[...]), flat(both[...]))
    product = product[:, 0 : 2 * LANES] + product[:, 2 * LANES :]
    column = jnp.transpose(jnp.broadcast_to(middle, (8, LANES)))[:, 0:1]
    return product - column * join(sums), stack(sums)


def rows_of(line):
    return stack([line[:, lanes] for lanes in columns(line.shape[1])])


def line_of(rows):
    return join([rows[k : k + 1, :] for k in range(rows.shape[0])])


def put_part(send, at, rows, part):
    first, last = part
    if last > first:
        send[:, at : at + last - first, :] = rows[:, first:last, :]


def pair_rows(product, devices, share, high, low, own):
    n = LANES
    missing = devices * share - n
    for h in (0, 1):
        values = product[:, n * h : n * (h + 1)]
        if missing:
            values = stack([values, jnp.zeros((missing, n), F32)])
        values = values.reshape(devices, share, n)
        first, last = share * h, share * (h + 1)
        top = values.astype(BF16)
        rest = (values - top.astype(F32)).astype(BF16)
        high[:, first:last, :] = top
        low[:, first:last, :] = rest
        own[:, first:last, :] = top.astype(F32) + rest.astype(F32)


def pass_pair(send, at, high, low, marks, groups):
    rows = high.astype(F32) + low.astype(F32)
    out = -rows
    for g in range(groups):
        same = (marks == float(g)).astype(F32)
        images = jnp.maximum(jnp.sum(same, axis=0), 1.0)
        out = out + (jnp.sum(rows * same, axis=0) / images)[None] * same
    send[:, at : at + rows.shape[1], :] = out.astype(BF16)


def pair_solve(tab, marks, outer, inner, sums, w, act_sums, q_rows, p_rows, pixels):
    label, n = entry(tab, OWN), LANES
    (norm_o, keeps_o), (norm_i, keeps_i) = outer, inner
    shift_o, gain_o, shift_i, gain_i = sums
    images = group_count(marks, label)
    count, count_o = images * pixels, tiled(images, norm_o.shape[2]) * pixels
    rstd_o = keeps_o[1:2, :]
    a_o = rstd_o * gain_of(norm_o, label)
    b_o, c_o = -(a_o * rstd_o) * gain_o / count_o, -a_o * shift_o / count_o
    scaled = w[...].astype(F32) * b_o
    high = scaled.astype(BF16)
    low = (scaled - high.astype(F32)).astype(BF16)
    got = mm_nt(jnp.concatenate([high, low, three_parts(c_o)], axis=0), w[...])
    m, e = got[0:n] + got[n : 2 * n], down(got[2 * n :])
    m_high = m.astype(BF16)
    m_low = (m - m_high.astype(F32)).astype(BF16)
    m = m_high.astype(F32) + m_low.astype(F32)
    same = (marks == label).astype(F32)
    middle = jnp.sum(act_sums * same, axis=0) / count
    spread_out = ((act_sums * (1.0 / pixels) - middle[None]) * same).reshape(-1, n).astype(BF16)
    share = p_rows.shape[1] // 2
    p_rows = p_rows * images[None]
    found = []
    q = join([q_rows[:, h : h + 1, :].reshape(-1, n) for h in (0, 1)])
    away = mm_tn(spread_out, q.astype(BF16))
    q = down(q * join([same.reshape(-1, n)] * 2))
    for h, start in enumerate((shift_i, gain_i)):
        lanes = slice(n * h, n * (h + 1))
        p = p_rows[:, share * h : share * (h + 1), :].reshape(-1, n)[0:n] + away[:, lanes]
        found.append(start + down(m * p) + e * q[:, lanes])
    rstd_i = keeps_i[1:2, :]
    a = rstd_i * gain_of(norm_i, label)
    coefs = a, -(a * rstd_i) * found[1] / count, -a * found[0] / count
    both = join([m_high, m_low])
    line = through(middle, both)
    return both, e - line[:, 0:n] - line[:, n:], coefs, found


def activate(tab, got, labels, z_in, norm, act, keeps):
    got = got.at[:, :, 0 : 2 * LANES]
    rows = z_in.shape[0]
    pixels = 1.0 * rows * (COLS - 4)
    mean, rstd, gain, shift, _ = scale_shift(got, labels[...], tab, norm, pixels)
    keeps[0:1, :] = mean
    keeps[1:2, :] = rstd
    scale = rstd * gain
    bias = 0.5 * (shift - mean * scale)
    scale = 0.5 * scale
    keep = valid_cols(LANES) & chan_mask(tab)

    def put(i, sums):
        low = jnp.where(keep, silu_of_half(z_in[i] * scale + bias), 0.0).astype(BF16)
        act[i] = low
        return sums + fold(low.astype(F32))

    return down(lax.fori_loop(0, rows, put, zeros8(LANES), unroll=7))


def f3(
    tab, got, labels, z_in, norm, w, w_p, xz,
    act, z, send, keeps, keeps_p, slope, q, high, own, both, low, *, share, part,
):
    sums = activate(tab, got, labels, z_in, norm, act, keeps)
    at = expand_pair(tab, z_in, norm, keeps, act, sums, w, z, send, slope, q, both, high, low, own, share)
    send[:, at : at + 2 * share, :] = low[...]
    put_part(send, at + 2 * share, xz, part)
    marks, label = labels[...], entry(tab, OWN)
    total = group_sum(got, marks, label)
    outer, first = z.shape[2], 2 * LANES
    second = first + w_p.shape[0]
    count = tiled(group_count(marks, label), outer) * (1.0 * z.shape[0] * (COLS - 4))
    mean, rstd = moments(through(total[:, first:second], w_p[...]), total[:, second:], count)
    keeps_p[0:1, :] = mean
    keeps_p[1:2, :] = rstd


def expand_pair(tab, z_in, norm, keeps, act, sums, w, z, send, slope, q, both, high, low, own, share):
    pixels = 1.0 * z.shape[0] * (COLS - 4)
    squares = project(act, w, z)
    first = through(sums, w[...])
    second = squares - first * first / pixels
    product, q[...] = pair_products(tab, z_in, norm, keeps, act, sums, slope, both)
    pair_rows(product, send.shape[0], share, high, low, own)
    put_split(send, 0, sums)
    moved = rows_of(second).astype(BF16)
    send[:, 2 : 2 + moved.shape[0], :] = jnp.broadcast_to(moved[None], (send.shape[0], *moved.shape))
    return 2 + moved.shape[0]


def f4(
    tab, got, labels, zc, zp, norm_c, norm_p, keeps_p, w_c, w, high, q,
    joined, slope, z, send, keeps,
):
    rows, chans = zc.shape[0], zc.shape[2]
    pixels = 1.0 * rows * (COLS - 4)
    mean_c, rstd_c = gathered_moments(got, labels[...], entry(tab, OWN), w_c, pixels)
    mean_p, rstd_p = keeps_p[0:1, :], keeps_p[1:2, :]
    for k, v in enumerate((mean_c, rstd_c, mean_p, rstd_p)):
        keeps[k : k + 1, :] = v
    group = entry(tab, OWN)
    scale_c = rstd_c * gain_of(norm_c, group)
    scale_p = rstd_p * gain_of(norm_p, group)
    bias = (shift_of(norm_c, group) - mean_c * scale_c) + (
        shift_of(norm_p, group) - mean_p * scale_p
    )
    keep = valid_cols(chans)
    scale_c, scale_p, bias = 0.5 * scale_c, 0.5 * scale_p, 0.5 * bias

    def put(i, carry):
        u = zc[i] * scale_c + zp[i] * scale_p + bias
        t = jnp.tanh(u)
        p = u * t
        joined[i] = jnp.where(keep, u + p, 0.0).astype(BF16)
        slope[i] = (0.5 + 0.5 * t) * (1.0 + u - p)
        return carry

    lax.fori_loop(0, rows, put, 0, unroll=4)
    step = rows // 4
    sums, squares = zeros8(LANES), zeros8(LANES)
    for c in range(4):
        values = mm(flat(joined[step * c : step * (c + 1)]), w[...])
        z[step * c : step * (c + 1)] = values.reshape(step, COLS, LANES)
        parts = values.reshape(-1, 8, LANES)
        sums = sums + jnp.sum(parts, axis=0)
        squares = squares + jnp.sum(parts * parts, axis=0)
    put_split(send, 0, stack([down(sums), down(squares)]))
    send[:, 4 : 4 + high.shape[1], :] = high[...]
    put_split(send, 4 + high.shape[1], q[...])


def f5(tab, got, labels, z_in, norm, w_two, w_last, x3, z, send, keeps):
    rows = z_in.shape[0]
    pixels = 1.0 * rows * (COLS - 4)
    marks, label = labels[...], entry(tab, OWN)
    total = over_group(get_split(got, 0, 2), marks, label)
    mean, rstd = moments(total[0:1], total[1:2], group_count(marks, label) * pixels)
    gain, shift = gain_of(norm, label), shift_of(norm, label)
    keeps[0:1, :] = mean
    keeps[1:2, :] = rstd
    scale = rstd * gain
    bias = 0.5 * (shift - mean * scale)
    scale = 0.5 * scale
    keep = valid_cols(LANES) & chan_mask(tab)
    x3[0] = jnp.zeros(x3.shape[1:], BF16)
    x3[rows + 1] = jnp.zeros(x3.shape[1:], BF16)
    n = LANES

    def put(i, carry):
        act = jnp.where(keep, silu_of_half(z_in[i] * scale + bias), 0.0)
        x3[i + 1, :, 0:n] = pltpu.roll(act, 1, 0).astype(BF16)
        x3[i + 1, :, n : 2 * n] = act.astype(BF16)
        x3[i + 1, :, 2 * n : 3 * n] = pltpu.roll(act, COLS - 1, 0).astype(BF16)
        return carry

    lax.fori_loop(0, rows, put, 0, unroll=2)
    lanes = slice(0, 3 * n)
    conv_stats(
        z, x3, (lanes, w_two[...], (0, 1)), (lanes, w_last[...], 2), send
    )


def f6(
    tab, got, labels, z_in, norm, w, xz,
    act, z, send, keeps, slope, q, own, both, high, low, *, share, part,
):
    sums = activate(tab, got, labels, z_in, norm, act, keeps)
    at = expand_pair(tab, z_in, norm, keeps, act, sums, w, z, send, slope, q, both, high, low, own, share)
    send[:, at : at + 2 * share, :] = high[...]
    send[:, at + 2 * share : at + 4 * share, :] = low[...]
    put_part(send, at + 4 * share, xz, part)


def gathered_moments(got, marks, label, w, pixels):
    devices, chans = got.shape[0], w.shape[1]
    low = stack([got[:, k : k + 1, :].astype(F32).reshape(devices, LANES) for k in (0, 1)])
    means = mm(low.astype(BF16), w[...]) * (1.0 / pixels)
    means = means[0:devices] + means[devices:]
    blocks = chans // LANES
    moments_2 = join(
        [got[:, 2 + k : 3 + k, :].astype(F32).reshape(devices, LANES) for k in range(blocks)]
    )
    same = join([(marks == label).astype(F32).reshape(devices, LANES)] * blocks)
    images = tiled(group_count(marks, label), chans)
    mean = down(means * same) / images
    away = means - mean
    variance = down((moments_2 + pixels * (away * away)) * same) / (images * pixels)
    return mean, lax.rsqrt(variance + EPSILON)


def b7(
    tab, got, labels, joined, z, norm, w, cot, slope_in, z_in, keeps_in, q,
    result, grad_pre, send, keeps, d_in, wide, low, *, share, p_at,
):
    rows, chans = z.shape[0], z.shape[2]
    cols = COLS - 4
    pixels = 1.0 * rows * cols
    marks, label = labels[...], entry(tab, OWN)
    mean, rstd = gathered_moments(got, marks, label, w, pixels)
    gain, shift = gain_of(norm, label), shift_of(norm, label)
    keeps[0:1, :] = mean
    keeps[1:2, :] = rstd
    gate = 0.25 * tiled(entry(tab, GATE), chans)
    scale = 0.5 * rstd * gain * gate
    bias = 0.5 * (shift - mean * rstd * gain) * gate
    wide[...] = jnp.zeros(wide.shape, F32)
    a_gate = rstd * gain * gate

    def put(i, carry):
        sums, products = carry
        wide[0:cols, :] = cot[i].astype(F32)
        zz = z[i]
        u = 0.5 * joined[i].astype(F32) + zz * scale + bias
        t = jnp.tanh(u)
        p = u * t
        result[i] = (u + p)[0:cols].astype(BF16)
        g = wide[...] * ((0.5 + 0.5 * t) * (1.0 + u - p))
        grad_pre[i] = g
        low[i] = (a_gate * g).astype(BF16)
        return sums + fold(g), products + fold(g * (zz - mean))

    start = zeros8(chans)
    sums, products = lax.fori_loop(0, rows, put, (start, start), unroll=2)
    inner = inner_sums(low, w, slope_in, z_in, keeps_in, d_in)
    blocks = chans // LANES
    put_split(send, 0, rows_of(down(sums) * gate))
    put_split(send, 2 * blocks, rows_of(down(products) * rstd * gate))
    put_split(send, 4 * blocks, stack(inner))
    put_split(send, 4 * blocks + 4, q[...])
    high = got[:, p_at : p_at + 2 * share, :]
    low_p = got[:, p_at + 2 * share : p_at + 4 * share, :]
    pass_pair(send, 4 * blocks + 8, high, low_p, marks, norm.shape[0])


def lane_sums(got, marks, channels):
    def sums_of(g):
        total = group_sum(got, marks, float(g))
        return row(total, 0), row(total, 1)

    return sums_of


def row_sums(got, marks):
    def sums_of(g):
        total = over_group(get_split(got, 0, 2), marks, float(g))
        return total[0:1], total[1:2]

    return sums_of


def backward_norm(tab, sums_of, marks, norm, keeps, pixels, grad_norm):
    group, chans = entry(tab, OWN), norm.shape[2]
    sums = [sums_of(g) for g in range(norm.shape[0])]
    for g, (shift_sum, gain_sum) in enumerate(sums):
        grad_norm[g, 0:1, :] = gain_sum
        grad_norm[g, 1:2, :] = shift_sum
    count = tiled(group_count(marks, group), chans) * pixels
    own_shift, own_gain = (own_of([v[k] for v in sums], group) for k in (0, 1))
    mean, rstd = keeps[0:1, :], keeps[1:2, :]
    a = rstd * gain_of(norm, group)
    return mean, a, -(a * rstd) * own_gain / count, -a * own_shift / count


def slope_sums(tab, d, z_in, norm, keeps, dout):
    rows = z_in.shape[0]
    mean, rstd = keeps[0:1, :], keeps[1:2, :]
    group = entry(tab, OWN)
    scale = rstd * gain_of(norm, group)
    bias = 0.5 * (shift_of(norm, group) - mean * scale)
    scale = 0.5 * scale
    keep = valid_cols(LANES) & chan_mask(tab)

    def put(i, carry):
        sums, products = carry
        zz = z_in[i]
        g = jnp.where(keep, d[i] * slope_of_half(zz * scale + bias), 0.0)
        dout[i] = g
        return sums + fold(g), products + fold(g * (zz - mean))

    sums, products = lax.fori_loop(
        0, rows, put, (zeros8(LANES), zeros8(LANES)), unroll=4
    )
    return down(sums), down(products) * rstd


def b9(
    tab, got, labels, norm_c, keeps_c, w_c, got_act, act, slope, d_in, z, norm, keeps,
    b_two, b_last, z_in, norm_in, keeps_in, x_sum, pair_high, pair_low, own_p,
    dz, dout, send, own_sums, d3, d, *, share, p_at,
):
    rows = z.shape[0]
    pixels = 1.0 * rows * (COLS - 4)
    marks, label = labels[...], entry(tab, OWN)
    blocks = norm_c.shape[2] // LANES
    at = 4 * blocks
    wide = [
        line_of(over_group(get_split(got, 2 * blocks * k, blocks), marks, label)) for k in (0, 1)
    ]
    inner = over_group(get_split(got, at, 2), marks, label)
    m, line, (a, b, c), found = pair_solve(
        tab, marks, (norm_c, keeps_c), (norm, keeps), [*wide, inner[0:1], inner[1:2]], w_c,
        get_split(got_act, 0, 1), get_split(got, at + 4, 2),
        got[:, at + 8 : at + 8 + 2 * share, :].astype(F32) + own_p[...], pixels,
    )
    own_sums[0:1, :] = found[0]
    own_sums[1:2, :] = found[1]
    inner_grad(act, m, line, slope, d_in, d)
    mean = keeps[0:1, :]
    keep = valid_cols(LANES)
    n = LANES
    d3[0] = jnp.zeros(d3.shape[1:], BF16)
    d3[rows + 1] = jnp.zeros(d3.shape[1:], BF16)

    def put(i, carry):
        v = a * d[i] + b * (z[i] - mean) + c
        v = jnp.where(keep, v, 0.0)
        d3[i + 1, :, 0:n] = pltpu.roll(v, COLS - 1, 0).astype(BF16)
        low = v.astype(BF16)
        d3[i + 1, :, n : 2 * n] = low
        dz[i] = low
        d3[i + 1, :, 2 * n : 3 * n] = pltpu.roll(v, 1, 0).astype(BF16)
        return carry

    lax.fori_loop(0, rows, put, 0, unroll=2)
    step = rows // 4
    for k in range(4):
        both = mm_nt(flat(d3[step * k : step * (k + 1) + 1]), b_two[...])
        value = mm_nt(flat(d3[step * k + 2 : step * (k + 1) + 2]), b_last[...])
        value = value + both[COLS:, 0:n] + both[0 : step * COLS, n : 2 * n]
        d[step * k : step * (k + 1)] = value.reshape(step, COLS, LANES)
    put_split(send, 0, stack(slope_sums(tab, d, z_in, norm_in, keeps_in, dout)))
    blocks = columns(x_sum.shape[0])
    put_split(send, 4, stack([jnp.transpose(x_sum[lanes, :])[0:1] for lanes in blocks]))
    high, low = pair_high[:, 4 : 4 + 2 * share, :], pair_low[:, p_at : p_at + 2 * share, :]
    pass_pair(send, 4 + 2 * len(blocks), high, low, marks, norm.shape[0])


def b10(
    tab, got, labels, dout_in, z, norm, keeps, w, grad_pre, slope, zc, zp, keeps_cp,
    norm_c, w_c, slope_in, z_in, keeps_in,
    dz, grad_pre_2, send, grad_norm, d_in, d, low,
):
    rows, chans = zc.shape[0], zc.shape[2]
    pixels = 1.0 * rows * (COLS - 4)
    marks = labels[...]
    coefs = backward_norm(tab, row_sums(got, marks), marks, norm, keeps, pixels, grad_norm)
    normed_grad(dz, dout_in, z, *coefs)
    d[...] = mm_nt(flat(dz[...]), w[...]).reshape(d.shape)
    mean_c, rstd_c, mean_p, rstd_p = (keeps_cp[k : k + 1, :] for k in range(4))
    a_c = rstd_c * gain_of(norm_c, entry(tab, OWN))

    def sum_up(i, carry):
        sums, prod_c, prod_p = carry
        g = (grad_pre[i] + d[i]) * slope[i]
        grad_pre_2[i] = g
        low[i] = (a_c * g).astype(BF16)
        return (
            sums + fold(g),
            prod_c + fold(g * (zc[i] - mean_c)),
            prod_p + fold(g * (zp[i] - mean_p)),
        )

    start = zeros8(chans)
    sums, prod_c, prod_p = lax.fori_loop(0, rows, sum_up, (start, start, start), unroll=2)
    wide = [down(sums), down(prod_c) * rstd_c, down(prod_p) * rstd_p]
    inner = inner_sums(low, w_c, slope_in, z_in, keeps_in, d_in)
    parts = [stack([v[:, 0 : chans // 2], v[:, chans // 2 :]]) for v in wide]
    values = join([*parts, stack(inner)])
    send[...] = jnp.broadcast_to(values[None], send.shape)


def inner_sums(low, w, slope, z, keeps, d_in):
    d_in[...] = mm_nt(flat(low[...]), w[...]).reshape(d_in.shape)
    mean, rstd = keeps[0:1, :], keeps[1:2, :]

    def add(i, carry):
        g = slope[i] * d_in[i]
        return carry[0] + fold(g), carry[1] + fold(g * (z[i] - mean))

    sums = lax.fori_loop(0, z.shape[0], add, (zeros8(LANES), zeros8(LANES)), unroll=7)
    return down(sums[0]), down(sums[1]) * rstd


def inner_grad(act, m, line, slope, d_in, d):
    both = mm(flat(act[...]), m)
    d[...] = (both[:, 0:LANES] + both[:, LANES:]).reshape(d.shape)

    def put(i, carry):
        d[i] = slope[i] * (d_in[i] + d[i] + line)
        return carry

    lax.fori_loop(0, d.shape[0], put, 0, unroll=7)


def normed_grad(dz, dout, z, mean, a, b, c):
    keep = valid_cols(z.shape[2])

    def put(i, carry):
        v = a * dout[i] + b * (z[i] - mean) + c
        dz[i] = jnp.where(keep, v, 0.0).astype(BF16)
        return carry

    lax.fori_loop(0, z.shape[0], put, 0, unroll=2)


def b12(
    tab, own10, labels, norm_c, keeps_c, w_c, got_act, got_q, got_p, own_p, act, slope, d_in,
    z, norm, keeps, xs, d2, kept, sent, own_sums, dz, packed, dout, *, share, q_at, p_at,
):
    rows = z.shape[0]
    pixels = 1.0 * rows * (COLS - 4)
    outer, n = norm_c.shape[2], LANES
    marks = labels[...]
    total = own10[...]
    cuts = (0, outer, 2 * outer, 2 * outer + n, 2 * outer + 2 * n)
    m, line, (a, b, c), found = pair_solve(
        tab, marks, (norm_c, keeps_c.at[0:2]), (norm, keeps),
        [total[:, u:v] for u, v in zip(cuts, cuts[1:])], w_c, get_split(got_act, 0, 1),
        get_split(got_q, q_at, 2),
        got_p[:, p_at : p_at + 2 * share, :].astype(F32) + own_p[...], pixels,
    )
    own_sums[0:1, :] = found[0]
    own_sums[1:2, :] = found[1]
    inner_grad(act, m, line, slope, d_in, dout)
    mean = keeps[0:1, :]
    keep = valid_cols(LANES)
    d2[rows] = jnp.zeros(d2.shape[1:], BF16)

    def put(i, carry):
        v = a * dout[i] + b * (z[i] - mean) + c
        v = jnp.where(keep, v, 0.0)
        low = v.astype(BF16)
        dz[i] = low
        d2[i, :, 0:n] = low
        d2[i, :, n : 2 * n] = pltpu.roll(v, COLS - 1, 0).astype(BF16)
        return carry

    lax.fori_loop(0, rows, put, 0, unroll=4)
    low = flat(dz[...])
    cur = mm_side(flat(xs[1 : rows + 1]), low)
    for k, (y, x) in enumerate(((1, 1), (1, 2), (1, 0), (2, 1), (2, 2), (2, 0))):
        put_rows(packed, n * (3 * y + x), cur[n * k : n * (k + 1)])
    up = mm_side(flat(xs[0:rows, :, 3 * n : 6 * n]), low)
    for k, (y, x) in enumerate(((0, 1), (0, 2), (0, 0))):
        put_rows(packed, n * (3 * y + x), up[n * k : n * (k + 1)])
    share_out(tab, packed, 9 * n, kept, sent)


def b12_images(
    tab, d2, b_even, b_odd, zz, norm_in, keeps_in, dn, sums_out, de, do, wide, *, own
):
    rows = de.shape[0]
    n = LANES
    half = half_of(tab)
    first = rows * (half if own else 1 - half)
    step = rows // 2
    for k in range(2):
        here = flat(d2[pl.ds(first + step * k, step)])
        below = flat(d2[pl.ds(first + step * k + 1, step)])
        de[step * k : step * (k + 1)] = mm_nt(here, b_even[...]).reshape(step, COLS, 2 * n)
        odd = mm_nt(here, b_odd[:, 0 : 2 * n]) + mm_nt(below, b_odd[:, 2 * n : 4 * n])
        do[step * k : step * (k + 1)] = odd.reshape(step, COLS, 2 * n)
    mean_1, rstd_1 = keeps_in[0:1, :], keeps_in[1:2, :]
    group = entry(tab, OWN)
    scale = rstd_1 * gain_of(norm_in, group)
    bias = 0.5 * (shift_of(norm_in, group) - mean_1 * scale)
    scale = 0.5 * scale
    keep = valid_cols(LANES) & chan_mask(tab)

    def emit(i, carry):
        sums, products = carry
        for ra in (0, 1):
            planes = (de, do)[ra]
            for cb in (0, 1):
                zv = zz[2 * i + ra, pl.ds(cb, COLS, stride=2), :]
                g = planes[i, :, n * cb : n * (cb + 1)] * slope_of_half(zv * scale + bias)
                g = jnp.where(keep, g, 0.0)
                sums = sums + fold(g)
                products = products + fold(g * (zv - mean_1))
                wide[ra, pl.ds(cb, COLS, stride=2), :] = g
            dn[2 * i + ra] = wide[ra].astype(BF16)
        return sums, products

    totals = lax.fori_loop(0, rows, emit, (zeros8(n), zeros8(n)), unroll=2)
    sums_out[0:1, :] = down(totals[0])
    sums_out[1:2, :] = down(totals[1]) * rstd_1


def b13(
    tab, got, labels, norm, keeps, w, z_own, z_for, dn_own, dn_for, gs_own, gs_for, *rest, at, held
):
    finished, outs = rest[:held], rest[held : 2 * held]
    grad, grad_norm, dz, wide, grad_v, norm_v, sems = rest[2 * held :]
    copies = [
        pltpu.make_async_copy(a, b, sems.at[k]) for k, (a, b) in enumerate(zip(finished, outs))
    ]
    for copy in copies:
        copy.start()
    rows, cols = grad.shape[1], grad.shape[2]
    half = half_of(tab)
    pixels = 2.0 * rows * cols
    marks = labels[...]
    totals = last_sums(got.at[:, at : at + 4, :], marks, norm.shape[0])
    for g in range(norm.shape[0]):
        norm_v[g, 0:1, :] = totals[g][1]
        norm_v[g, 1:2, :] = totals[g][0]
    copies.append(pltpu.make_async_copy(norm_v, grad_norm, sems.at[held]))
    copies[-1].start()
    keep = lax.broadcasted_iota(jnp.int32, (z_own.shape[1], LANES), 0) < cols
    for k, (z, dn, gs) in enumerate(((z_own, dn_own, gs_own), (z_for, dn_for, gs_for))):
        group = entry(tab, OWN if k == 0 else OTHER)
        shift_sum = own_of([t[0] for t in totals], group)
        gain_sum = own_of([t[1] for t in totals], group)
        count = group_count(marks, group) * pixels
        mean, rstd = keeps[2 * k : 2 * k + 1, :], keeps[2 * k + 1 : 2 * k + 2, :]
        a = rstd * gain_of(norm, group)
        b = -(a * rstd) * gain_sum / count
        c = -a * shift_sum / count

        def put(i, carry, z=z, dn=dn, mean=mean, a=a, b=b, c=c):
            v = a * dn[i].astype(F32) + b * (z[i] - mean) + c
            dz[i] = jnp.where(keep, v, 0.0).astype(BF16)
            return carry

        lax.fori_loop(0, rows, put, 0, unroll=4)
        place = half if k == 0 else 1 - half
        step = rows // 2
        for q in range(2):
            low = flat(dz[step * q : step * (q + 1)])
            for p in range(wide.shape[0]):
                values = mm_nt(low, w[LANES * p : LANES * (p + 1), :])
                wide[p, step * q : step * (q + 1)] = values.reshape(step, -1, LANES)

            def emit(i, carry, gs=gs, place=place):
                even = pl.ds(0, COLS, stride=2)
                for p in range(wide.shape[0]):
                    lanes = slice(LANES * p, LANES * (p + 1))
                    wide[p, 2 * i, even, :] = wide[p, 2 * i, even, :] + gs[i, :, lanes].astype(F32)
                    grad_v[place, 2 * i, :, lanes] = wide[p, 2 * i, 0:cols, :].astype(BF16)
                    grad_v[place, 2 * i + 1, :, lanes] = wide[p, 2 * i + 1, 0:cols, :].astype(BF16)
                return carry

            lax.fori_loop(step // 2 * q, step // 2 * (q + 1), emit, 0, unroll=True)
            part = pl.ds(step * q, step)
            copies.append(
                pltpu.make_async_copy(
                    grad_v.at[place, part], grad.at[place, part], sems.at[held + 1 + 2 * k + q]
                )
            )
            copies[-1].start()
    for copy in copies:
        copy.wait()


def put_rows(out, at, value):
    for j in range(value.shape[1] // LANES):
        out[at : at + value.shape[0], :] = value[:, LANES * j : LANES * (j + 1)].astype(BF16)
        at += value.shape[0]
    return at


def take_rows(source, at, out):
    rows = out.shape[0]
    for j in range(out.shape[1] // LANES):
        out[:, LANES * j : LANES * (j + 1)] = source(at, rows)
        at += rows
    return at


def share_out(tab, packed, used, kept, sent):
    if used < packed.shape[0]:
        packed[used:, :] = jnp.zeros((packed.shape[0] - used, LANES), BF16)
    half = half_of(tab)
    size = kept.shape[0] * kept.shape[1]
    for out, place in ((kept, half), (sent, 1 - half)):
        out[...] = packed[pl.ds(pl.multiple_of(size * place, 16), size), :].reshape(out.shape)


def g_most(
    tab, act_2b, x3, dz_2b, joined, dz_2a, act_1b, xee, w_p,
    got, labels, norm_c, norm_p, keeps, grad_pre_2, zc, zp,
    got_2c, norm_2c, keeps_2c, grad_pre, z_2c,
    kept, sent, gs_own, gs_oth, grad_norm_c, grad_norm_p, grad_norm_2c, own10, packed, dz_1c, dz_p, dz_2c,
):
    rows, outer = dz_2b.shape[0], zc.shape[2]
    pixels = 1.0 * rows * (COLS - 4)
    marks = labels[...]

    blocks = outer // LANES
    label = entry(tab, OWN)

    def wide_sums(source, count):
        values = [get_split(source, 2 * blocks * k, blocks) for k in range(count)]
        return [
            [line_of(over_group(v, marks, float(g))) for v in values]
            for g in range(norm_c.shape[0])
        ]

    totals = [group_sum(got, marks, float(g)) for g in range(norm_c.shape[0])]
    side = outer // 2
    lines = [
        [join([total[h : h + 1, side * k : side * (k + 1)] for h in (0, 1)]) for k in range(3)]
        for total in totals
    ]
    for k in range(2):
        own10[:, outer * k : outer * (k + 1)] = own_of([v[k] for v in lines], label)
        at = 2 * outer + LANES * k
        own10[:, at : at + LANES] = own_of([v[k : k + 1, 3 * side :] for v in totals], label)
    lines_2c = wide_sums(got_2c, 2)
    mean, a, b, c = backward_norm(
        tab, lambda g: (lines_2c[g][0], lines_2c[g][1]), marks, norm_2c, keeps_2c, pixels,
        grad_norm_2c,
    )
    gate = 0.25 * tiled(entry(tab, GATE), outer)
    normed_grad(dz_2c, grad_pre, z_2c, mean, a * gate, b, c)
    coefs = backward_norm(
        tab, lambda g: (lines[g][0], lines[g][1]), marks, norm_c, keeps.at[0:2], pixels, grad_norm_c
    )
    normed_grad(dz_1c, grad_pre_2, zc, *coefs)
    coefs = backward_norm(
        tab, lambda g: (lines[g][0], lines[g][2]), marks, norm_p, keeps.at[2:4], pixels, grad_norm_p
    )
    normed_grad(dz_p, grad_pre_2, zp, *coefs)
    at = put_rows(packed, 0, mm_tn(flat(act_2b[...]), flat(dz_2c[...])))
    low = flat(dz_2b[...])
    for y in range(3):
        at = put_rows(packed, at, mm_side(flat(x3[y : y + rows]), low))
    at = put_rows(packed, at, mm_side(flat(joined[...]), flat(dz_2a[...])))
    at = put_rows(packed, at, mm_tn(flat(act_1b[...]), flat(dz_1c[...])))
    at = put_rows(packed, at, mm_tn(flat(xee[...]), flat(dz_p[...])))
    share_out(tab, packed, at, kept, sent)
    half = half_of(tab)
    count = gs_own.shape[0]
    for k, gs in enumerate((gs_own, gs_oth)):
        first = count * (half if k == 0 else 1 - half)
        got = mm_nt(flat(dz_p[pl.ds(first, count)]), w_p[...])
        gs[...] = got.reshape(gs.shape).astype(BF16)


def g_xz(keeps, x_own, x_oth, z_own, z_oth, out, x_sum, low, tall):
    rows, n = z_own.shape[0], LANES
    mean = keeps[0:1, :]
    low[:, :, n : 2 * n] = jnp.ones((rows, z_own.shape[1], n), BF16)
    value = None
    for x, z in ((x_own, z_own), (x_oth, z_oth)):

        def put(i, carry, z=z):
            low[i, :, 0:n] = (z[i] - mean).astype(BF16)
            return carry

        lax.fori_loop(0, rows, put, 0, unroll=4)
        term = mm_tn(flat(x[...]), flat(low[...]))
        value = term if value is None else value + term
    at = value.shape[0]
    tall[0:at, :] = value[:, 0:n]
    if at < tall.shape[0]:
        tall[at:, :] = jnp.zeros((tall.shape[0] - at, n), F32)
    out[...] = tall[...].reshape(out.shape).astype(BF16)
    x_sum[...] = value[:, n : 2 * n]


def g_xd(
    tab, sums_own, sums_oth, norm, keeps, x_sum, got_x, labels, x_own, x_oth, dn_own, dn_oth,
    z_own, z_oth, out, sums, low,
):
    rows = dn_own.shape[0]
    n = LANES
    pixels = 1.0 * (2 * rows) * (2 * (COLS - 4))
    sums[...] = sums_own[...] + sums_oth[...]
    a = keeps[1:2, :] * gain_of(norm, entry(tab, OWN))
    local = sums[0:1, :] / pixels
    mean = keeps[0:1, :]
    b = -(a * keeps[1:2, :]) * sums[1:2, :] / pixels
    value = None
    for x, dn, z in ((x_own, dn_own, z_own), (x_oth, dn_oth, z_oth)):

        def put(i, carry, dn=dn, z=z):
            low[i] = (a * (dn[i].astype(F32) - local) + b * (z[i] - mean)).astype(BF16)
            return carry

        lax.fori_loop(0, rows, put, 0, unroll=4)
        term = mm_tn(flat(x[...]), flat(low[...]))
        value = term if value is None else value + term
    marks, label = labels[...], entry(tab, OWN)
    total = over_group(get_split(got_x, 4, x_sum.shape[0] // n), marks, label)
    total = join([total[k : k + 1] for k in range(total.shape[0])])
    total = total / tiled(group_count(marks, label), total.shape[1])
    total = jnp.broadcast_to(total, (8, total.shape[1]))
    means = jnp.concatenate(
        [jnp.transpose(total[:, lanes])[:, 0:1] for lanes in columns(total.shape[1])], axis=0
    )
    value = value + (x_sum[...] - means) * (a * local)
    at = value.shape[0]
    out[0:at, :] = value.astype(BF16)
    if at < out.shape[0]:
        out[at:, :] = jnp.zeros((out.shape[0] - at, n), BF16)


def pack_last(tall, sums, kept, got, kept_1b, got_1b, xz, send, *, stats_at, part):
    n = LANES
    devices = send.shape[0]
    piece, share = kept.shape[1], tall.shape[0] // devices
    first = kept.shape[0]
    second = first + kept_1b.shape[0]
    send[0:first, 0:piece, :] = (kept[...].astype(F32) + got[...].astype(F32)).astype(BF16)
    send[first:second, 0:piece, :] = (kept_1b[...].astype(F32) + got_1b[...].astype(F32)).astype(BF16)
    if second < devices:
        send[second:, 0:piece, :] = jnp.zeros((devices - second, piece, n), BF16)
    send[:, piece : piece + share, :] = tall[...].reshape(devices, share, n)
    put_split(send, stats_at, sums[...])
    put_part(send, stats_at + 4, xz, part)


def last_sums(stats, marks, groups):
    values = stats[:, 0:2, :].astype(F32) + stats[:, 2:4, :].astype(F32)
    out = []
    for g in range(groups):
        total = jnp.sum(values * (marks == float(g)).astype(F32), axis=0)
        out.append((total[0:1], total[1:2]))
    return out


def add_all(
    got, labels, norm, keeps_all, got_a, got_b, found_2b, found_1b, out, *, at, pixels, parts
):
    devices, n = got.shape[0], LANES
    half = devices // 2
    share = parts[-1][2]
    piece = (out.shape[1] - share - 8) // 2
    marks = labels[...]
    value = jnp.sum(got[:, piece : piece + share, :].astype(F32), axis=0)
    products = get_split(got, at, 2)[:, 1:2, :]
    lack = jnp.zeros(products.shape, F32)
    for g in range(norm.shape[0]):
        rstd = keeps_all[2 * g + 1 : 2 * g + 2, :]
        factor = -(rstd * rstd * norm[g, 0:1, :]) / pixels
        same = (marks == float(g)).astype(F32)
        middle = jnp.sum(products * same, axis=0) / jnp.sum(same, axis=0)
        lack = lack + (middle[None] - products) * (factor[None] * same)
    rows = [
        jnp.sum(source[:, start : start + last - first, :].astype(F32) * lack, axis=0)
        for source, (start, first, last) in zip((got_a, got_b, got), parts)
        if last > first
    ]
    value = value + jnp.concatenate(rows, axis=0)
    for k in (0, 1):
        total = jnp.sum(got[half * k : half * (k + 1), 0:piece, :].astype(F32), axis=0).astype(BF16)
        out[:, piece * k : piece * (k + 1), :] = jnp.broadcast_to(
            total[None], (out.shape[0], piece, n)
        )
    out[:, 2 * piece : 2 * piece + share, :] = jnp.broadcast_to(
        value.astype(BF16)[None], (out.shape[0], share, n)
    )
    put_split(out, 2 * piece + share, stack([found_2b[...], found_1b[...]]))


def place_parts(minor, parts, packed, tall, found, piece):
    far, share = parts[0].shape[0], tall.shape[1]
    for k, part in enumerate(parts):
        base = lax.bitwise_xor(minor, jnp.int32(k))

        def place(z, carry, part=part, base=base):
            owner = base + NEAR * z
            for h in (0, 1):
                packed[h, owner] = part[z, piece * h : piece * (h + 1), :]
            tall[owner] = part[z, 2 * piece : 2 * piece + share, :].astype(F32)
            sums = part[z, 2 * piece + share :, :].astype(F32)
            found[owner] = sums[0:4] + sums[4:8]
            return carry

        lax.fori_loop(0, far, place, 0, unroll=min(far, 4))


def unpack_own(tab, *refs, piece):
    place_parts(half_of(tab, MINOR), refs[:NEAR], *refs[NEAR:], piece)


def unpack(tab, labels, packed_own, tall_own, found_own, *refs, first, second, piece):
    parts, outs, values = refs[:NEAR], refs[NEAR : NEAR + 9], refs[NEAR + 9 :]
    *values, packed_oth, tall_oth, found_oth, sems = values
    place_parts(half_of(tab, MINOR), parts, packed_oth, tall_oth, found_oth, piece)
    half = half_of(tab)
    copies = [
        pltpu.make_async_copy(value, out, sems.at[k]) for k, (value, out) in enumerate(zip(values, outs))
    ]
    w_1b, w_1a, *grad_norms = values[5:9]
    own, oth = (packed_own, tall_own, found_own), (packed_oth, tall_oth, found_oth)
    for core in (0, 1):

        @pl.when(half == core)
        def _():
            packed, tall, found = zip(*((own, oth) if core == 0 else (oth, own)))
            most, last = [], []
            for h in (0, 1):
                pieces = [flat(v[h]) for v in packed]
                middle = pieces[0].shape[0]
                cut = first * piece
                most.append((pieces, middle))
                last.append((cut, pieces, middle))

            def span(pieces, middle, at, rows):
                found_rows = []
                if at < middle:
                    found_rows.append(pieces[0][at : min(at + rows, middle)])
                if at + rows > middle:
                    found_rows.append(pieces[1][max(at - middle, 0) : at + rows - middle])
                return [v.astype(F32) for v in found_rows]

            size = first * piece

            def source(at, rows):
                out = []
                if at < size:
                    out += span(*most[0], at, min(rows, size - at))
                if at + rows > size:
                    start = max(at - size, 0)
                    out += span(*most[1], start, at + rows - size - start)
                return out[0] if len(out) == 1 else stack(out)

            at = 0
            for k, value in enumerate(values[0:5]):
                at = take_rows(source, at, value)
                copies[k].start()
            left = w_1b.shape[0]
            for k, (cut, pieces, middle) in enumerate(last):
                rows = min(second * piece, left)
                lines = span(pieces, middle, cut, rows)
                start = second * piece * k
                w_1b[start : start + rows, :] = lines[0] if len(lines) == 1 else stack(lines)
                left -= rows
            copies[5].start()
            lines = stack([flat(v[...]) for v in tall])
            w_1a[...] = lines[0 : w_1a.shape[0]]
            copies[6].start()
            sums = jnp.concatenate([v[...] for v in found], axis=0)
            for k, grad_norm in enumerate(grad_norms):
                norm_from_owners(sums[:, 2 * k : 2 * k + 2, :], labels[...], grad_norm)
                copies[7 + k].start()

    for copy in copies:
        copy.wait()


def norm_from_owners(found, marks, grad_norm):
    for g in range(grad_norm.shape[0]):
        total = over_group(found, marks, float(g)) / group_count(marks, float(g))
        grad_norm[g, 0:1, :] = total[1:2]
        grad_norm[g, 1:2, :] = total[0:1]


def gather(send):
    return lax.all_to_all(send, AXES, 0, 0)


def tie(*values):
    return lax.optimization_barrier(values)


def swap(block):
    return lax.ppermute(block, "rows", [(0, 1), (1, 0)])


def body(
    images, w_1a, w_1b, w_1c, w_1p, w_2a, w_2b, w_2c,
    norm_1a, norm_1b, norm_1c, norm_1p, norm_2a, norm_2b, norm_2c,
    cotangent, group, width, gate,
):
    devices = lax.axis_size("rows") * lax.axis_size("batch")
    place = lax.axis_index(AXES).astype(jnp.int32).reshape(1)
    norms = (norm_1a, norm_1b, norm_1c, norm_1p, norm_2a, norm_2b, norm_2c)
    norm_1a, norm_1b, norm_1c, norm_1p, norm_2a, norm_2b, norm_2c = (
        v.transpose(1, 0, 2) for v in norms
    )
    outer, inputs = w_1c.shape[1], w_1a.shape[0]
    rows = cotangent.shape[1]
    cols_in = 2 * COLS
    n, m = LANES, devices

    def send(stats, channels=LANES):
        return ((m, channels // LANES, stats * LANES), F32)

    def maps(channels, dtype=F32):
        return ((rows, COLS, channels), dtype)

    def scratch(channels, dtype=F32):
        return pltpu.VMEM((rows, COLS, channels), dtype)

    def params(*arrays):
        return [(a.shape, F32) for a in arrays]

    def mean_scale(channels, count=1):
        return ((2 * count, channels), F32)

    wide_in = ((rows, cols_in, inputs), BF16)
    wide_z = ((rows, cols_in, n), F32)
    raw = images.shape
    tab, x_own, x_for, z_own, z_for, s1 = stage(
        functools.partial(f1, batch=devices // 2), [((8, n), F32), wide_in, wide_in, wide_z, wide_z, send(5)],
        [*(pltpu.SMEM(v.shape, jnp.int32) for v in (place, group, width, gate)),
         pltpu.VMEM(raw, BF16), pltpu.VMEM(w_1a.shape, BF16), pltpu.VMEM((8, n), F32),
         pltpu.SemaphoreType.DMA((7,))],
        hbm=(0, 1, 2, 3, 4, 5),
    )(place, group, width, gate, images, w_1a)
    s1, v_1b, v_2b = tie(s1, w_1b, w_2b)
    built = stage(
        prepare,
        [(v, BF16) for v in (
            (3 * n, n), (3 * n, 2 * n), (3 * n, 2 * n), (3 * n, n),
            (2 * n, 2 * n), (2 * n, 4 * n), (2 * n, 3 * n), (n, 3 * n),
        )],
    )(v_1b, v_2b)
    s1, x_for, w_even, w_odd, w_two, w_last, b_even, b_odd, b_two, b_last = tie(s1, x_for, *built)
    x_oth = swap(x_for)
    g1 = gather(s1)
    g1, x_oth = tie(g1, x_oth)
    xee, z_1p, stats_1p = stage(
        f1_strided,
        [maps(inputs, BF16), maps(outer), ((1, inputs + outer), F32)],
        [pltpu.VMEM((inputs // n, cols_in, n), F32)],
    )(tab, x_own, x_oth, w_1p)
    xs, z_1b, s2, labels, k_1a, k_all, z_oth = stage(
        f2,
        [((rows + 1, COLS, 6 * n), BF16), maps(n), send(2 + (inputs + outer) // n),
         ((m, 1, n), F32), mean_scale(n, 2), mean_scale(n, norm_1a.shape[0]), wide_z],
    )(tab, g1, z_own, x_oth, w_1a, norm_1a, w_even, w_odd, stats_1p)
    share = -(-inputs // devices)
    half_in = ((rows, cols_in, n), BF16)
    xz, x_sum = stage(
        g_xz, [((devices, share, n), BF16), ((inputs, n), F32)],
        [pltpu.VMEM((rows, cols_in, 2 * n), BF16), pltpu.VMEM((devices * share, n), F32)],
    )(k_1a, x_own, x_oth, z_own, z_oth)
    s2, xz, x_sum = tie(s2, xz, x_sum)
    g2 = gather(s2)
    share_1 = -(-n // devices)
    p_rows = ((devices, 2 * share_1, n), BF16)
    own_rows = ((devices, 2 * share_1, n), F32)
    wide_rows = outer // n
    p_at = 2 + wide_rows
    xz_3 = p_at + 2 * share_1
    high_3 = -(-xz_3 // 16) * 16
    xz_6 = p_at + 4 * share_1
    high_6 = -(-xz_6 // 8) * 8
    cut_3 = min(share, high_3 - xz_3)
    cut_6 = min(share, cut_3 + high_6 - xz_6)
    act_1b, z_1c, s3, k_1b, k_p, slope_1b, q_1b, p_1b, own_1b = stage(
        functools.partial(f3, share=share_1, part=(0, cut_3)),
        [maps(n, BF16), maps(outer), ((devices, high_3, n), BF16), mean_scale(n),
         mean_scale(outer), maps(n), ((2, n), F32), p_rows, own_rows],
        [scratch(4 * n, BF16), pltpu.VMEM(p_rows[0], BF16)],
    )(tab, g2, labels, z_1b, norm_1b, w_1c, w_1p, xz)
    g3 = gather(s3)
    high = -(-(8 + 2 * share_1) // 16) * 16
    joined, slope, z_2a, s4, k_cp = stage(
        f4,
        [maps(outer, BF16), maps(outer), maps(n), ((devices, high, n), BF16),
         mean_scale(outer, 2)],
    )(tab, g3, labels, z_1c, z_1p, norm_1c, norm_1p, k_p, w_1c, w_2a, p_1b, q_1b)
    g4 = gather(s4)
    x3, z_2b, s5, k_2a = stage(
        f5, [((rows + 2, COLS, 3 * n), BF16), maps(n), send(2), mean_scale(n)]
    )(tab, g4, labels, z_2a, norm_2a, w_two, w_last)
    g5 = gather(s5)
    act_2b, z_2c, s6, k_2b, slope_2b, q_2b, own_2b = stage(
        functools.partial(f6, share=share_1, part=(cut_3, cut_6)),
        [maps(n, BF16), maps(outer), ((devices, high_6, n), BF16), mean_scale(n), maps(n),
         ((2, n), F32), own_rows],
        [scratch(4 * n, BF16), *(pltpu.VMEM(p_rows[0], BF16) for _ in range(2))],
    )(tab, g5, labels, z_2b, norm_2b, w_2c, xz)
    g6 = gather(s6)
    high_7 = -(-(4 * wide_rows + 8 + 2 * share_1) // 16) * 16
    result, grad_pre, s7, k_2c, d_2b = stage(
        functools.partial(b7, share=share_1, p_at=p_at),
        [(cotangent.shape[1:], BF16), maps(outer), ((devices, high_7, n), BF16),
         mean_scale(outer), maps(n)],
        [pltpu.VMEM((COLS, outer), F32), scratch(outer, BF16)],
    )(tab, g6, labels, joined, z_2c, norm_2c, w_2c, cotangent[0], slope_2b, z_2b, k_2b, q_2b)
    g7 = gather(s7)
    dz_2b, dout_2a, s9, found_2b = stage(
        functools.partial(b9, share=share_1, p_at=p_at),
        [maps(n, BF16), maps(n), ((devices, high, n), BF16), ((2, n), F32)],
        [pltpu.VMEM((rows + 2, COLS, 3 * n), BF16), scratch(n)],
    )(tab, g7, labels, norm_2c, k_2c, w_2c, g6, act_2b, slope_2b, d_2b, z_2b, norm_2b, k_2b,
      b_two, b_last, z_2a, norm_2a, k_2a, x_sum, g4, g3, own_2b)
    g9 = gather(s9)
    dz_2a, grad_pre_2, s10, grad_norm_2a, d_1b = stage(
        b10,
        [maps(n, BF16), maps(outer), ((devices, 2, 3 * outer // 2 + n), F32), *params(norm_2a), maps(n)],
        [scratch(outer), scratch(outer, BF16)],
    )(tab, g9, labels, dout_2a, z_2a, norm_2a, k_2a, w_2a, grad_pre, slope, z_1c, z_1p, k_cp,
      norm_1c, w_1c, slope_1b, z_1b, k_1b)
    g10 = gather(s10)
    half_map = ((rows // 2, COLS, inputs), BF16)
    most_rows = sum(v.size for v in (w_2c, w_2b, w_2a, w_1c, w_1p)) // n
    rows_1b = w_1b.size // n
    piece = 16
    while -(-most_rows // (2 * piece)) - (-rows_1b // (2 * piece)) > devices:
        piece += 16
    first, second = -(-most_rows // (2 * piece)), -(-rows_1b // (2 * piece))
    part, part_1b = ((first, piece, n), BF16), ((second, piece, n), BF16)
    kept, sent, gs_own, gs_send, grad_norm_1c, grad_norm_1p, grad_norm_2c, own10 = stage(
        g_most,
        [part, part, half_map, half_map, *params(norm_1c, norm_1p, norm_2c),
         ((1, 2 * outer + 2 * n), F32)],
        [pltpu.VMEM((2 * first * piece, n), BF16), *(scratch(outer, BF16) for _ in range(3))],
    )(tab, act_2b, x3, dz_2b, joined, dz_2a, act_1b, xee, w_1p,
      g10, labels, norm_1c, norm_1p, k_cp, grad_pre_2, z_1c, z_1p,
      g7, norm_2c, k_2c, grad_pre, z_2c)
    got, gs_for = swap(sent), swap(gs_send)
    half_in = ((rows, cols_in, n), BF16)
    d2, kept_1b, sent_1b, found_1b = stage(
        functools.partial(b12, share=share_1, q_at=4 + 2 * share_1, p_at=4 + 2 * (inputs // n)),
        [((rows + 1, COLS, 2 * n), BF16), part_1b, part_1b, ((2, n), F32)],
        [scratch(n, BF16), pltpu.VMEM((2 * second * piece, n), BF16), scratch(n)],
    )(tab, own10, labels, norm_1c, k_cp, w_1c, g3, g4, g9, own_1b, act_1b, slope_1b, d_1b,
      z_1b, norm_1b, k_1b, xs)
    got_1b = swap(sent_1b)
    sides = []
    for own, z in ((False, z_oth), (True, z_own)):
        sides.append(
            stage(
                functools.partial(b12_images, own=own), [half_in, ((2, n), F32)],
                [pltpu.VMEM((rows // 2, COLS, 2 * n), F32), pltpu.VMEM((rows // 2, COLS, 2 * n), F32),
                 pltpu.VMEM((2, cols_in, n), F32)],
            )(tab, d2, b_even, b_odd, z, norm_1a, k_1a)
        )
        if not own:
            dn_for = swap(sides[0][0])
            d2, _ = tie(d2, sides[0][0])
    (dn_send, sums_send), (dn_own, sums_own) = sides
    stats_at = piece + -(-share // 8) * 8
    high = -(-(stats_at + 4 + share - cut_6) // 16) * 16
    tall, sums_1a = stage(
        g_xd, [((devices * share, n), BF16), ((2, n), F32)], [pltpu.VMEM(half_in[0], BF16)]
    )(tab, sums_own, sums_send, norm_1a, k_1a, x_sum, g9, labels, x_own, x_oth, dn_own, dn_send,
      z_own, z_oth)
    tall, gs_for, dn_for = tie(tall, gs_for, dn_for)
    (s12,) = stage(
        functools.partial(pack_last, stats_at=stats_at, part=(cut_6, share)),
        [((devices, high, n), BF16)]
    )(tall, sums_1a, kept, got, kept_1b, got_1b, xz)
    g12 = gather(s12)
    pixels = 4.0 * images.shape[1] * images.shape[1]
    batch = devices // 2
    far = batch // NEAR
    (mine,) = stage(
        functools.partial(
            add_all, at=stats_at, pixels=pixels,
            parts=((xz_3, 0, cut_3), (xz_6, cut_3, cut_6), (stats_at + 4, cut_6, share)),
        ),
        [((far, 2 * piece + share + 8, n), BF16)],
    )(g12, labels, norm_1a, k_all, g3, g6, found_2b, found_1b)
    columns_of = [[k + NEAR * z for z in range(far)] for k in range(NEAR)]
    along = lax.all_to_all(mine, "batch", 0, 0, axis_index_groups=columns_of)
    near = [
        lax.ppermute(along, "batch", [(i, i ^ k) for i in range(batch)]) for k in range(1, NEAR)
    ]
    finished = (
        result, grad_norm_1c, grad_norm_1p, grad_norm_2a, grad_norm_2c
    )
    held = len(finished)
    *finished, grad_images, grad_norm_1a = stage(
        functools.partial(b13, at=stats_at, held=held),
        [*((v.shape, v.dtype) for v in finished), (images.shape, BF16), *params(norm_1a)],
        [pltpu.VMEM(half_in[0], BF16), pltpu.VMEM((inputs // n, rows, cols_in, n), F32),
         pltpu.VMEM(images.shape, BF16), pltpu.VMEM(norm_1a.shape, F32),
         pltpu.SemaphoreType.DMA((held + 5,))],
        hbm_out=range(held + 2),
    )(tab, g12, labels, norm_1a, k_1a, w_1a, z_own, z_for, dn_own, dn_for, gs_own, gs_for, *finished)
    result, grad_norm_1c, grad_norm_1p, grad_norm_2a, grad_norm_2c = finished
    *near, grad_images = tie(*near, grad_images)
    parts = [along, *near]
    weights = (w_2c, w_2b.reshape(-1, n), w_2a, w_1c, w_1p, w_1b.reshape(-1, n), w_1a)
    side = [
        ((2, batch, piece, n), BF16), ((batch, share, n), F32), ((batch, 4, n), F32)
    ]
    crossed = [swap(v) for v in parts]
    placed = stage(functools.partial(unpack_own, piece=piece), side)(tab, *parts)
    t_2c, t_2b, t_2a, t_1c, t_1p, t_1b, t_1a, grad_norm_2b, grad_norm_1b = stage(
        functools.partial(unpack, first=first, second=second, piece=piece),
        [(v.shape, F32) for v in (*weights, norm_2b, norm_1b)],
        [*(pltpu.VMEM(v.shape, F32) for v in (*weights, norm_2b, norm_1b)),
         *(pltpu.VMEM(*v) for v in side), pltpu.SemaphoreType.DMA((9,))],
        hbm_out=range(9),
    )(tab, labels, *placed, *crossed)
    grads = (
        grad_norm_1a, grad_norm_1b, grad_norm_1c, grad_norm_1p,
        grad_norm_2a, grad_norm_2b, grad_norm_2c,
    )
    return (
        result[None], grad_images, t_1a, t_1b.reshape(w_1b.shape), t_1c, t_1p, t_2a,
        t_2b.reshape(w_2b.shape), t_2c, *[v.transpose(1, 0, 2) for v in grads],
    )


def solution(mesh):
    return jax.shard_map(
        body,
        mesh=mesh,
        in_specs=(
            P("batch", "rows", None, None),
            *[P()] * 14,
            P(("batch", "rows"), None, None, None),
            P("batch"),
            P(),
            P(),
        ),
        out_specs=(
            P(("batch", "rows"), None, None, None),
            P("batch", "rows", None, None),
            *[P()] * 14,
        ),
        check_vma=False,
    )
```

```python
import functools

import jax
import jax.numpy as jnp
from jax import lax
from jax.experimental import pallas as pl
from jax.experimental.pallas import tpu as pltpu
from jax.sharding import PartitionSpec as P

EPSILON = 1e-05
F32 = jnp.float32
BF16 = jnp.bfloat16
AXES = ("rows", "batch")
VMEM_LIMIT = 14 * 1024 * 1024
LANES = 128
COLS = 32
NEAR = 4


def full(memory=pltpu.VMEM):
    return pl.BlockSpec(memory_space=memory)


def stage(kernel, outs, scratch=(), hbm=(), hbm_out=()):
    def place(i, outside):
        return pltpu.HBM if i in outside else pltpu.VMEM

    def call(*args):
        args = [
            pltpu.with_memory_space_constraint(a, pltpu.HBM) if i in hbm else a
            for i, a in enumerate(args)
        ]
        return pl.pallas_call(
            kernel,
            out_shape=tuple(jax.ShapeDtypeStruct(s, d) for s, d in outs),
            in_specs=[full(place(i, hbm)) for i in range(len(args))],
            out_specs=tuple(
                full(place(i, hbm_out)) for i in range(len(outs))
            ),
            scratch_shapes=list(scratch),
            compiler_params=pltpu.CompilerParams(vmem_limit_bytes=VMEM_LIMIT),
            name=(kernel.func if isinstance(kernel, functools.partial) else kernel).__name__,
        )(*args)

    return call


def silu_of_half(u):
    return u + u * jnp.tanh(u)


def slope_of_half(u):
    t = jnp.tanh(u)
    return (0.5 + 0.5 * t) * (1.0 + u - u * t)


def fold(x):
    return (x[0:8] + x[8:16]) + (x[16:24] + x[24:32])


def row(total, stat):
    blocks = total.shape[0]
    pieces = [total[j : j + 1, LANES * stat : LANES * (stat + 1)] for j in range(blocks)]
    return pieces[0] if blocks == 1 else jnp.concatenate(pieces, axis=1)


def spread(out_ref, rows):
    blocks = out_ref.shape[1]
    for stat, values in enumerate(rows):
        for j in range(blocks):
            piece = values[:, LANES * j : LANES * (j + 1)]
            out_ref[:, j : j + 1, LANES * stat : LANES * (stat + 1)] = jnp.broadcast_to(
                piece[None], (out_ref.shape[0], 1, LANES)
            )


def group_sum(got_ref, labels, label):
    same = (labels == label).astype(F32)
    stats = got_ref.shape[2] // LANES
    parts = [
        jnp.sum(got_ref[:, :, LANES * s : LANES * (s + 1)] * same, axis=0) for s in range(stats)
    ]
    return jnp.concatenate(parts, axis=1) if stats > 1 else parts[0]


def group_count(labels, label):
    return jnp.sum((labels == label).astype(F32), axis=0)


def tiled(values, channels):
    return jnp.concatenate([values] * (channels // LANES), axis=1) if channels > LANES else values


def moments(first, second, pixels):
    mean = first / pixels
    return mean, lax.rsqrt(second / pixels - mean * mean + EPSILON)


def own_of(values, label):
    out = values[0]
    label = tiled(label, out.shape[1])
    for g in range(1, len(values)):
        out = jnp.where(label == float(g), values[g], out)
    return out


def gain_of(norm_ref, label):
    return own_of([norm_ref[g, 0:1, :] for g in range(norm_ref.shape[0])], label)


def shift_of(norm_ref, label):
    return own_of([norm_ref[g, 1:2, :] for g in range(norm_ref.shape[0])], label)


def valid_cols(channels):
    return lax.broadcasted_iota(jnp.int32, (COLS, channels), 0) < COLS - 4


def chan_mask(tab):
    return lax.broadcasted_iota(jnp.int32, (1, LANES), 1).astype(F32) < entry(tab, LIMIT)


def flat(x):
    return x.reshape(x.shape[0] * x.shape[1], x.shape[2])


def mm(a, b):
    return jnp.dot(a, b, preferred_element_type=F32)


def mm_nt(a, b):
    return lax.dot_general(a, b, (((1,), (1,)), ((), ())), preferred_element_type=F32)


def mm_tn(a, b):
    return lax.dot_general(a, b, (((0,), (0,)), ((), ())), preferred_element_type=F32)


def mm_side(a, b):
    turned = mm_tn(b, a)
    blocks = [
        jnp.transpose(turned[:, LANES * j : LANES * (j + 1)]) for j in range(a.shape[1] // LANES)
    ]
    return blocks[0] if len(blocks) == 1 else jnp.concatenate(blocks, axis=0)


def zeros8(channels):
    return jnp.zeros((8, channels), F32)


def down(x):
    return jnp.sum(x, axis=0, keepdims=True)


OWN, OTHER, HALF, LIMIT, GATE, MINOR = range(6)


def entry(tab, k):
    return tab[k : k + 1, :]


def half_of(tab, k=HALF):
    return (jnp.sum(entry(tab, k)) * (1.0 / LANES)).astype(jnp.int32)


def prepare(w1b, w2b, w_even, w_odd, w_two, w_last, b_even, b_odd, b_two, b_last):
    n = LANES
    for k, (y, x) in enumerate(((1, 1), (1, 2), (1, 0))):
        w_even[n * k : n * (k + 1), :] = w1b[y, x]
    for k, (low, high) in enumerate((((2, 1), (0, 1)), ((2, 2), (0, 2)), ((2, 0), (0, 0)))):
        w_odd[n * k : n * (k + 1), 0:n] = w1b[low]
        w_odd[n * k : n * (k + 1), n : 2 * n] = w1b[high]
    for x in range(3):
        w_two[n * x : n * (x + 1), 0:n] = w2b[0, x]
        w_two[n * x : n * (x + 1), n : 2 * n] = w2b[1, x]
        w_last[n * x : n * (x + 1), :] = w2b[2, x]
        b_two[0:n, n * x : n * (x + 1)] = w2b[1, x]
        b_two[n : 2 * n, n * x : n * (x + 1)] = w2b[2, x]
        b_last[:, n * x : n * (x + 1)] = w2b[0, x]
    nothing = jnp.zeros((n, n), BF16)
    b_even[0:n, 0:n] = w1b[1, 1]
    b_even[0:n, n : 2 * n] = nothing
    b_even[n : 2 * n, 0:n] = w1b[1, 2]
    b_even[n : 2 * n, n : 2 * n] = w1b[1, 0]
    for k, top in ((0, 2), (1, 0)):
        b_odd[0:n, 2 * n * k : 2 * n * k + n] = w1b[top, 1]
        b_odd[0:n, 2 * n * k + n : 2 * n * (k + 1)] = nothing
        b_odd[n : 2 * n, 2 * n * k : 2 * n * k + n] = w1b[top, 2]
        b_odd[n : 2 * n, 2 * n * k + n : 2 * n * (k + 1)] = w1b[top, 0]


def widen(source, x_pad):
    rows, cols, chans = source.shape
    gap = x_pad.shape[1] - cols

    def put(i, carry):
        x_pad[i, 0:cols, :] = source[i]
        x_pad[i, cols : cols + gap, :] = jnp.zeros((gap, chans), BF16)
        return carry

    lax.fori_loop(0, rows, put, 0, unroll=4)


def first_project(x_pad, w, z, stats=True):
    rows = x_pad.shape[0]
    step = rows // 4
    sums, squares = zeros8(LANES), zeros8(LANES)
    for c in range(4):
        values = mm(flat(x_pad[step * c : step * (c + 1)]), w[...])
        z[step * c : step * (c + 1)] = values.reshape(step, x_pad.shape[1], LANES)
        if stats:
            parts = values.reshape(-1, 8, LANES)
            sums = sums + jnp.sum(parts, axis=0)
            squares = squares + jnp.sum(parts * parts, axis=0)
    return sums, squares


def f1(
    place_at, group_at, width_at, gate_at, images, w_at, tab, x_own, x_for, z_own, z_for, send,
    place_ref, group, width, gate, raw, w, found, sems, *, batch,
):
    pairs = (
        (place_at, place_ref), (group_at, group), (width_at, width), (gate_at, gate), (w_at, w),
        (images.at[0], raw.at[0]), (images.at[1], raw.at[1]),
    )
    copies = [pltpu.make_async_copy(a, b, sems.at[k]) for k, (a, b) in enumerate(pairs)]
    for k in (0, 4, 5, 6, 1, 2, 3):
        copies[k].start()
    for k in (0, 4, 5):
        copies[k].wait()
    half = lax.div(place_ref[0], batch)
    sides = ((x_own, z_own), (x_for, z_for))

    def one(k):
        for place in (0, 1):

            @pl.when(half == place)
            def _():
                x_pad, z = sides[k] if place == 0 else sides[1 - k]
                widen(raw.at[k], x_pad)
                sums, squares = first_project(x_pad, w, z)
                at = 2 * (k if place == 0 else 1 - k)
                found[at : at + 1, :] = down(sums)
                found[at + 1 : at + 2, :] = down(squares)

    one(0)
    copies[6].wait()
    one(1)
    for k in (1, 2, 3):
        copies[k].wait()
    rows = [found[k : k + 1, :] for k in range(4)]
    own, other = group[half], group[1 - half]
    values = {
        OWN: own, OTHER: other, HALF: half, LIMIT: w.shape[1] // 4 * width[own], GATE: gate[own],
        MINOR: lax.rem(lax.rem(place_ref[0], batch), NEAR),
    }
    tab[...] = jnp.zeros(tab.shape, F32)
    for k, v in values.items():
        tab[k : k + 1, :] = jnp.full((1, LANES), v.astype(F32))
    spread(send, [*rows, jnp.full((1, LANES), (own + 4 * other).astype(F32))])


def f1_strided(tab, x_own, x_oth, w, xee, z, stats, wide):
    half = half_of(tab)
    rows = x_own.shape[0] // 2
    for k, x_pad in enumerate((x_own, x_oth)):
        first = rows * (half if k == 0 else 1 - half)

        def put(i, carry, x_pad=x_pad, first=first):
            for b in range(wide.shape[0]):
                lanes = slice(LANES * b, LANES * (b + 1))
                wide[b] = x_pad[2 * i, :, lanes].astype(F32)
                xee[first + i, :, lanes] = wide[b, pl.ds(0, COLS, stride=2), :].astype(BF16)
            return carry

        lax.fori_loop(0, rows, put, 0, unroll=4)
    total = 2 * rows
    step = total // 7
    chans = z.shape[2]
    squares = zeros8(chans)
    for c in range(7):
        values = mm(flat(xee[step * c : step * (c + 1)]), w[...])
        z[step * c : step * (c + 1)] = values.reshape(step, COLS, chans)
        parts = values.reshape(-1, 8, chans)
        squares = squares + jnp.sum(parts * parts, axis=0)
    ones = jnp.ones((8, total * COLS), BF16)
    stats[:, 0 : w.shape[0]] = mm(ones, flat(xee[...]))[0:1]
    stats[:, w.shape[0] :] = down(squares)


def scale_shift(got, labels, tab, norm, pixels, slot=0):
    label = entry(tab, OWN)
    total = group_sum(got, labels, label)
    chans = norm.shape[2]
    count = tiled(group_count(labels, label), chans) * pixels
    mean, rstd = moments(row(total, 2 * slot), row(total, 2 * slot + 1), count)
    gain, shift = gain_of(norm, entry(tab, OWN)), shift_of(norm, entry(tab, OWN))
    return mean, rstd, gain, shift, count


def conv_stats(z, source, pair, single, send, extra=()):
    keep = valid_cols(LANES)[None]
    rows = z.shape[0]
    step = rows // 4
    (lanes_2, w_2, offsets), (lanes_1, w_1, offset) = pair, single
    sums, squares = zeros8(LANES), zeros8(LANES)
    base = min(offsets)
    for c in range(4):
        at = step * c
        both = mm(flat(source[at + base : at + base + step + 1, :, lanes_2]), w_2)
        values = mm(flat(source[at + offset : at + offset + step, :, lanes_1]), w_1)
        for k, own in enumerate(offsets):
            skip = COLS * (own - base)
            values = values + both[skip : skip + step * COLS, LANES * k : LANES * (k + 1)]
        values = jnp.where(keep, values.reshape(step, COLS, LANES), 0.0)
        z[at : at + step] = values
        parts = values.reshape(-1, 8, LANES)
        sums = sums + jnp.sum(parts, axis=0)
        squares = squares + jnp.sum(parts * parts, axis=0)
    spread(send, [down(sums), down(squares), *extra])


def f2(
    tab, got, z_own, x_oth, w, norm, w_even, w_odd, stats_p,
    xs, z, send, labels, keeps, keeps_all, z_oth,
):
    codes = got[:, :, 4 * LANES : 5 * LANES]
    others = jnp.floor(0.25 * codes)
    marks = codes - 4.0 * others
    labels[...] = marks
    rows = xs.shape[0] - 1
    pixels = 4.0 * rows * (COLS - 4)
    first_project(x_oth, w, z_oth, False)
    for g in range(norm.shape[0]):
        mine, theirs = (marks == float(g)).astype(F32), (others == float(g)).astype(F32)
        totals = [
            jnp.sum(
                got[:, :, LANES * s : LANES * (s + 1)] * mine
                + got[:, :, LANES * (s + 2) : LANES * (s + 3)] * theirs,
                axis=0,
            )
            for s in (0, 1)
        ]
        mean, rstd = moments(*totals, group_count(marks, float(g)) * pixels)
        keeps_all[2 * g : 2 * g + 1, :] = mean
        keeps_all[2 * g + 1 : 2 * g + 2, :] = rstd
    for k, slot in enumerate((OWN, OTHER)):
        for q in (0, 1):
            choices = [keeps_all[2 * g + q : 2 * g + q + 1, :] for g in range(norm.shape[0])]
            keeps[2 * k + q : 2 * k + q + 1, :] = own_of(choices, entry(tab, slot))
    mean, rstd = keeps[0:1, :], keeps[1:2, :]
    gain, shift = gain_of(norm, entry(tab, OWN)), shift_of(norm, entry(tab, OWN))
    scale = rstd * gain
    bias = 0.5 * (shift - mean * scale)
    scale = 0.5 * scale
    keep = valid_cols(LANES) & chan_mask(tab)
    half = half_of(tab)
    xs[0] = jnp.zeros(xs.shape[1:], BF16)
    n = LANES
    for k, zz in enumerate((z_own, z_oth)):
        first = 1 + (rows // 2) * (half if k == 0 else 1 - half)

        def put(i, carry, zz=zz, first=first):
            lane = 0
            for a in (0, 1):
                for b in (0, 1):
                    u = zz[2 * i + a, pl.ds(b, COLS, stride=2), :] * scale + bias
                    act = jnp.where(keep, silu_of_half(u), 0.0)
                    xs[first + i, :, lane : lane + n] = act.astype(BF16)
                    lane += n
                    if b == 1:
                        moved = pltpu.roll(act, 1, 0)
                        xs[first + i, :, lane : lane + n] = moved.astype(BF16)
                        lane += n
            return carry

        lax.fori_loop(0, rows // 2, put, 0, unroll=4)
    extra = [stats_p[:, lanes] for lanes in columns(stats_p.shape[1])]
    pair = (slice(3 * n, 6 * n), w_odd[...], (1, 0))
    conv_stats(z, xs, pair, (slice(0, 3 * n), w_even[...], 1), send, extra)


def project(act, w, z):
    rows, chans = z.shape[0], z.shape[2]
    step = rows // 7
    squares = zeros8(chans)
    for c in range(7):
        values = mm(flat(act[step * c : step * (c + 1)]), w[...])
        z[step * c : step * (c + 1)] = values.reshape(step, COLS, chans)
        parts = values.reshape(-1, 8, chans)
        squares = squares + jnp.sum(parts * parts, axis=0)
    return down(squares)


def join(pieces):
    return pieces[0] if len(pieces) == 1 else jnp.concatenate(pieces, axis=1)


def columns(channels):
    return [slice(LANES * j, LANES * (j + 1)) for j in range(channels // LANES)]


def three_parts(sums):
    high = sums.astype(BF16)
    rest = sums - high.astype(F32)
    mid = rest.astype(BF16)
    low = (rest - mid.astype(F32)).astype(BF16)
    lines = [v.astype(F32) for v in (high, mid, low)]
    lines.append(jnp.zeros((13, sums.shape[1]), F32))
    return jnp.concatenate(lines, axis=0).astype(BF16)


def through(sums, w):
    return down(mm(three_parts(sums), w))


def put_split(send, at, values):
    rows = values.shape[0]
    high = values.astype(BF16)
    rest = (values - high.astype(F32)).astype(BF16)
    for k, part in enumerate((high, rest)):
        send[:, at + rows * k : at + rows * (k + 1), :] = jnp.broadcast_to(
            part[None], (send.shape[0], rows, LANES)
        )


def get_split(got, at, rows):
    return got[:, at : at + rows, :].astype(F32) + got[:, at + rows : at + 2 * rows, :].astype(F32)


def over_group(values, marks, label):
    return jnp.sum(values * (marks == label).astype(F32), axis=0)


def stack(rows):
    return jnp.concatenate(rows, axis=0)


def activate_pair(tab, got, labels, z, norm, act, keeps, slope, both):
    rows = z.shape[0]
    pixels = 1.0 * rows * (COLS - 4)
    mean, rstd, gain, shift, _ = scale_shift(got, labels[...], tab, norm, pixels)
    keeps[0:1, :] = mean
    keeps[1:2, :] = rstd
    scale = rstd * gain
    bias = 0.5 * (shift - mean * scale)
    scale = 0.5 * scale
    keep = valid_cols(LANES) & chan_mask(tab)

    def put(i, carry):
        zz = z[i]
        u = zz * scale + bias
        t = jnp.tanh(u)
        p = u * t
        low = jnp.where(keep, u + p, 0.0).astype(BF16)
        act[i] = low
        s = jnp.where(keep, (0.5 + 0.5 * t) * (1.0 + u - p), 0.0)
        sx = s * ((zz - mean) * rstd)
        slope[i] = s
        for k, v in enumerate((s, sx)):
            high = v.astype(BF16)
            both[i, :, LANES * k : LANES * (k + 1)] = high
            both[i, :, LANES * (k + 2) : LANES * (k + 3)] = (v - high.astype(F32)).astype(BF16)
        return carry[0] + fold(low.astype(F32)), carry[1] + fold(s), carry[2] + fold(sx)

    start = zeros8(LANES)
    sums = lax.fori_loop(0, rows, put, (start, start, start), unroll=4)
    act_sum, *sums = [down(v) for v in sums]
    product = mm_tn(flat(act[...]), flat(both[...]))
    product = product[:, 0 : 2 * LANES] + product[:, 2 * LANES :]
    middle = jnp.broadcast_to(act_sum * (1.0 / pixels), (8, LANES))
    return act_sum, product - jnp.transpose(middle)[:, 0:1] * join(sums), stack(sums)


def rows_of(line):
    return stack([line[:, lanes] for lanes in columns(line.shape[1])])


def line_of(rows):
    return join([rows[k : k + 1, :] for k in range(rows.shape[0])])


def put_part(send, at, rows, part):
    first, last = part
    if last > first:
        send[:, at : at + last - first, :] = rows[:, first:last, :]


def pair_rows(product, devices, share, high, low, own):
    n = LANES
    missing = devices * share - n
    for h in (0, 1):
        values = product[:, n * h : n * (h + 1)]
        if missing:
            values = stack([values, jnp.zeros((missing, n), F32)])
        values = values.reshape(devices, share, n)
        first, last = share * h, share * (h + 1)
        top = values.astype(BF16)
        rest = (values - top.astype(F32)).astype(BF16)
        high[:, first:last, :] = top
        low[:, first:last, :] = rest
        own[:, first:last, :] = top.astype(F32) + rest.astype(F32)


def pass_pair(send, at, high, low, marks, groups):
    rows = high.astype(F32) + low.astype(F32)
    out = -rows
    for g in range(groups):
        same = (marks == float(g)).astype(F32)
        images = jnp.maximum(jnp.sum(same, axis=0), 1.0)
        out = out + (jnp.sum(rows * same, axis=0) / images)[None] * same
    send[:, at : at + rows.shape[1], :] = out.astype(BF16)


def pair_solve(tab, marks, outer, inner, sums, w, act_sums, q_rows, p_rows, pixels):
    label, n = entry(tab, OWN), LANES
    (norm_o, keeps_o), (norm_i, keeps_i) = outer, inner
    shift_o, gain_o, shift_i, gain_i = sums
    images = group_count(marks, label)
    count, count_o = images * pixels, tiled(images, norm_o.shape[2]) * pixels
    rstd_o = keeps_o[1:2, :]
    a_o = rstd_o * gain_of(norm_o, label)
    b_o, c_o = -(a_o * rstd_o) * gain_o / count_o, -a_o * shift_o / count_o
    scaled = w[...].astype(F32) * b_o
    high = scaled.astype(BF16)
    low = (scaled - high.astype(F32)).astype(BF16)
    got = mm_nt(jnp.concatenate([high, low, three_parts(c_o)], axis=0), w[...])
    m, e = got[0:n] + got[n : 2 * n], down(got[2 * n :])
    m_high = m.astype(BF16)
    m_low = (m - m_high.astype(F32)).astype(BF16)
    m = m_high.astype(F32) + m_low.astype(F32)
    same = (marks == label).astype(F32)
    middle = jnp.sum(act_sums * same, axis=0) / count
    spread_out = ((act_sums * (1.0 / pixels) - middle[None]) * same).reshape(-1, n).astype(BF16)
    share = p_rows.shape[1] // 2
    p_rows = p_rows * images[None]
    found = []
    q = join([q_rows[:, h : h + 1, :].reshape(-1, n) for h in (0, 1)])
    away = mm_tn(spread_out, q.astype(BF16))
    q = down(q * join([same.reshape(-1, n)] * 2))
    for h, start in enumerate((shift_i, gain_i)):
        lanes = slice(n * h, n * (h + 1))
        p = p_rows[:, share * h : share * (h + 1), :].reshape(-1, n)[0:n] + away[:, lanes]
        found.append(start + down(m * p) + e * q[:, lanes])
    rstd_i = keeps_i[1:2, :]
    a = rstd_i * gain_of(norm_i, label)
    coefs = a, -(a * rstd_i) * found[1] / count, -a * found[0] / count
    both = join([m_high, m_low])
    line = through(middle, both)
    return both, e - line[:, 0:n] - line[:, n:], coefs, found


def f3(
    tab, got, labels, z_in, norm, w, w_p, xz,
    act, z, send, keeps, keeps_p, slope, q, high, own, both, low, *, share, part,
):
    got_1 = got.at[:, :, 0 : 2 * LANES]
    found = activate_pair(tab, got_1, labels, z_in, norm, act, keeps, slope, both)
    at = expand_pair(found, act, w, z, send, q, high, low, own, share)
    send[:, at : at + 2 * share, :] = low[...]
    put_part(send, at + 2 * share, xz, part)
    marks, label = labels[...], entry(tab, OWN)
    total = group_sum(got, marks, label)
    outer, first = z.shape[2], 2 * LANES
    second = first + w_p.shape[0]
    count = tiled(group_count(marks, label), outer) * (1.0 * z.shape[0] * (COLS - 4))
    mean, rstd = moments(through(total[:, first:second], w_p[...]), total[:, second:], count)
    keeps_p[0:1, :] = mean
    keeps_p[1:2, :] = rstd


def expand_pair(found, act, w, z, send, q, high, low, own, share):
    sums, product, q[...] = found
    pixels = 1.0 * z.shape[0] * (COLS - 4)
    squares = project(act, w, z)
    first = through(sums, w[...])
    second = squares - first * first / pixels
    pair_rows(product, send.shape[0], share, high, low, own)
    put_split(send, 0, sums)
    moved = rows_of(second).astype(BF16)
    send[:, 2 : 2 + moved.shape[0], :] = jnp.broadcast_to(moved[None], (send.shape[0], *moved.shape))
    return 2 + moved.shape[0]


def f4(
    tab, got, labels, zc, zp, norm_c, norm_p, keeps_p, w_c, w, high, q,
    joined, slope, z, send, keeps,
):
    rows, chans = zc.shape[0], zc.shape[2]
    pixels = 1.0 * rows * (COLS - 4)
    mean_c, rstd_c = gathered_moments(got, labels[...], entry(tab, OWN), w_c, pixels)
    mean_p, rstd_p = keeps_p[0:1, :], keeps_p[1:2, :]
    for k, v in enumerate((mean_c, rstd_c, mean_p, rstd_p)):
        keeps[k : k + 1, :] = v
    group = entry(tab, OWN)
    scale_c = rstd_c * gain_of(norm_c, group)
    scale_p = rstd_p * gain_of(norm_p, group)
    bias = (shift_of(norm_c, group) - mean_c * scale_c) + (
        shift_of(norm_p, group) - mean_p * scale_p
    )
    keep = valid_cols(chans)
    scale_c, scale_p, bias = 0.5 * scale_c, 0.5 * scale_p, 0.5 * bias

    def put(i, carry):
        u = zc[i] * scale_c + zp[i] * scale_p + bias
        t = jnp.tanh(u)
        p = u * t
        joined[i] = jnp.where(keep, u + p, 0.0).astype(BF16)
        slope[i] = (0.5 + 0.5 * t) * (1.0 + u - p)
        return carry

    lax.fori_loop(0, rows, put, 0, unroll=4)
    step = rows // 4
    sums, squares = zeros8(LANES), zeros8(LANES)
    for c in range(4):
        values = mm(flat(joined[step * c : step * (c + 1)]), w[...])
        z[step * c : step * (c + 1)] = values.reshape(step, COLS, LANES)
        parts = values.reshape(-1, 8, LANES)
        sums = sums + jnp.sum(parts, axis=0)
        squares = squares + jnp.sum(parts * parts, axis=0)
    put_split(send, 0, stack([down(sums), down(squares)]))
    send[:, 4 : 4 + high.shape[1], :] = high[...]
    put_split(send, 4 + high.shape[1], q[...])


def f5(tab, got, labels, z_in, norm, w_two, w_last, x3, z, send, keeps):
    rows = z_in.shape[0]
    pixels = 1.0 * rows * (COLS - 4)
    marks, label = labels[...], entry(tab, OWN)
    total = over_group(get_split(got, 0, 2), marks, label)
    mean, rstd = moments(total[0:1], total[1:2], group_count(marks, label) * pixels)
    gain, shift = gain_of(norm, label), shift_of(norm, label)
    keeps[0:1, :] = mean
    keeps[1:2, :] = rstd
    scale = rstd * gain
    bias = 0.5 * (shift - mean * scale)
    scale = 0.5 * scale
    keep = valid_cols(LANES) & chan_mask(tab)
    x3[0] = jnp.zeros(x3.shape[1:], BF16)
    x3[rows + 1] = jnp.zeros(x3.shape[1:], BF16)
    n = LANES

    def put(i, carry):
        act = jnp.where(keep, silu_of_half(z_in[i] * scale + bias), 0.0)
        x3[i + 1, :, 0:n] = pltpu.roll(act, 1, 0).astype(BF16)
        x3[i + 1, :, n : 2 * n] = act.astype(BF16)
        x3[i + 1, :, 2 * n : 3 * n] = pltpu.roll(act, COLS - 1, 0).astype(BF16)
        return carry

    lax.fori_loop(0, rows, put, 0, unroll=4)
    lanes = slice(0, 3 * n)
    conv_stats(
        z, x3, (lanes, w_two[...], (0, 1)), (lanes, w_last[...], 2), send
    )


def f6(
    tab, got, labels, z_in, norm, w, xz,
    act, z, send, keeps, slope, q, own, both, high, low, *, share, part,
):
    got_1 = got.at[:, :, 0 : 2 * LANES]
    found = activate_pair(tab, got_1, labels, z_in, norm, act, keeps, slope, both)
    at = expand_pair(found, act, w, z, send, q, high, low, own, share)
    send[:, at : at + 2 * share, :] = high[...]
    send[:, at + 2 * share : at + 4 * share, :] = low[...]
    put_part(send, at + 4 * share, xz, part)


def gathered_moments(got, marks, label, w, pixels):
    devices, chans = got.shape[0], w.shape[1]
    low = stack([got[:, k : k + 1, :].astype(F32).reshape(devices, LANES) for k in (0, 1)])
    means = mm(low.astype(BF16), w[...]) * (1.0 / pixels)
    means = means[0:devices] + means[devices:]
    blocks = chans // LANES
    moments_2 = join(
        [got[:, 2 + k : 3 + k, :].astype(F32).reshape(devices, LANES) for k in range(blocks)]
    )
    same = join([(marks == label).astype(F32).reshape(devices, LANES)] * blocks)
    images = tiled(group_count(marks, label), chans)
    mean = down(means * same) / images
    away = means - mean
    variance = down((moments_2 + pixels * (away * away)) * same) / (images * pixels)
    return mean, lax.rsqrt(variance + EPSILON)


def b7(
    tab, got, labels, joined, z, norm, w, cot, slope_in, z_in, keeps_in, q,
    result, grad_pre, send, keeps, d_in, wide, low, *, share, p_at,
):
    rows, chans = z.shape[0], z.shape[2]
    cols = COLS - 4
    pixels = 1.0 * rows * cols
    marks, label = labels[...], entry(tab, OWN)
    mean, rstd = gathered_moments(got, marks, label, w, pixels)
    gain, shift = gain_of(norm, label), shift_of(norm, label)
    keeps[0:1, :] = mean
    keeps[1:2, :] = rstd
    gate = 0.25 * tiled(entry(tab, GATE), chans)
    scale = 0.5 * rstd * gain * gate
    bias = 0.5 * (shift - mean * rstd * gain) * gate
    wide[...] = jnp.zeros(wide.shape, F32)
    a_gate = rstd * gain * gate

    def put(i, carry):
        sums, products = carry
        wide[0:cols, :] = cot[i].astype(F32)
        zz = z[i]
        u = 0.5 * joined[i].astype(F32) + zz * scale + bias
        t = jnp.tanh(u)
        p = u * t
        result[i] = (u + p)[0:cols].astype(BF16)
        g = wide[...] * ((0.5 + 0.5 * t) * (1.0 + u - p))
        grad_pre[i] = g
        low[i] = (a_gate * g).astype(BF16)
        return sums + fold(g), products + fold(g * (zz - mean))

    start = zeros8(chans)
    sums, products = lax.fori_loop(0, rows, put, (start, start), unroll=4)
    inner = inner_sums(low, w, slope_in, z_in, keeps_in, d_in)
    blocks = chans // LANES
    put_split(send, 0, rows_of(down(sums) * gate))
    put_split(send, 2 * blocks, rows_of(down(products) * rstd * gate))
    put_split(send, 4 * blocks, stack(inner))
    put_split(send, 4 * blocks + 4, q[...])
    high = got[:, p_at : p_at + 2 * share, :]
    low_p = got[:, p_at + 2 * share : p_at + 4 * share, :]
    pass_pair(send, 4 * blocks + 8, high, low_p, marks, norm.shape[0])


def own_coefs(tab, marks, norm, keeps, pixels, shift_sum, gain_sum):
    group = entry(tab, OWN)
    count = tiled(group_count(marks, group), norm.shape[2]) * pixels
    mean, rstd = keeps[0:1, :], keeps[1:2, :]
    a = rstd * gain_of(norm, group)
    return mean, a, -(a * rstd) * gain_sum / count, -a * shift_sum / count


def wide_lines(total, outer):
    side = outer // 2
    return [join([total[h : h + 1, side * k : side * (k + 1)] for h in (0, 1)]) for k in range(3)]


def norm_tail(labels, got_2c, got_2a, got_1, grad_2c, grad_2a, grad_1c, grad_1p):
    marks = labels[...]
    outer = grad_2c.shape[2]
    blocks = outer // LANES
    for g in range(grad_2c.shape[0]):
        label = float(g)
        rows = [
            line_of(over_group(get_split(got_2c, 2 * blocks * k, blocks), marks, label))
            for k in (0, 1)
        ]
        pair = over_group(get_split(got_2a, 0, 2), marks, label)
        lines = wide_lines(group_sum(got_1, marks, label), outer)
        for out, shift_sum, gain_sum in (
            (grad_2c, rows[0], rows[1]),
            (grad_2a, pair[0:1], pair[1:2]),
            (grad_1c, lines[0], lines[1]),
            (grad_1p, lines[0], lines[2]),
        ):
            out[g, 0:1, :] = gain_sum
            out[g, 1:2, :] = shift_sum


def slope_sums(tab, d, z_in, norm, keeps, dout):
    rows = z_in.shape[0]
    mean, rstd = keeps[0:1, :], keeps[1:2, :]
    group = entry(tab, OWN)
    scale = rstd * gain_of(norm, group)
    bias = 0.5 * (shift_of(norm, group) - mean * scale)
    scale = 0.5 * scale
    keep = valid_cols(LANES) & chan_mask(tab)

    def put(i, carry):
        sums, products = carry
        zz = z_in[i]
        g = jnp.where(keep, d[i] * slope_of_half(zz * scale + bias), 0.0)
        dout[i] = g
        return sums + fold(g), products + fold(g * (zz - mean))

    sums, products = lax.fori_loop(
        0, rows, put, (zeros8(LANES), zeros8(LANES)), unroll=4
    )
    return down(sums), down(products) * rstd


def b9(
    tab, got, labels, norm_c, keeps_c, w_c, got_act, act, slope, d_in, z, norm, keeps,
    b_two, b_last, z_in, norm_in, keeps_in, x_sum, pair_high, pair_low, own_p,
    dz, dout, send, own_sums, d3, d, *, share, p_at,
):
    rows = z.shape[0]
    pixels = 1.0 * rows * (COLS - 4)
    marks, label = labels[...], entry(tab, OWN)
    blocks = norm_c.shape[2] // LANES
    at = 4 * blocks
    wide = [
        line_of(over_group(get_split(got, 2 * blocks * k, blocks), marks, label)) for k in (0, 1)
    ]
    inner = over_group(get_split(got, at, 2), marks, label)
    m, line, (a, b, c), found = pair_solve(
        tab, marks, (norm_c, keeps_c), (norm, keeps), [*wide, inner[0:1], inner[1:2]], w_c,
        get_split(got_act, 0, 1), get_split(got, at + 4, 2),
        got[:, at + 8 : at + 8 + 2 * share, :].astype(F32) + own_p[...], pixels,
    )
    own_sums[0:1, :] = found[0]
    own_sums[1:2, :] = found[1]
    inner_grad(act, m, line, slope, d_in, d)
    mean = keeps[0:1, :]
    keep = valid_cols(LANES)
    n = LANES
    d3[0] = jnp.zeros(d3.shape[1:], BF16)
    d3[rows + 1] = jnp.zeros(d3.shape[1:], BF16)

    def put(i, carry):
        v = a * d[i] + b * (z[i] - mean) + c
        v = jnp.where(keep, v, 0.0)
        d3[i + 1, :, 0:n] = pltpu.roll(v, COLS - 1, 0).astype(BF16)
        low = v.astype(BF16)
        d3[i + 1, :, n : 2 * n] = low
        dz[i] = low
        d3[i + 1, :, 2 * n : 3 * n] = pltpu.roll(v, 1, 0).astype(BF16)
        return carry

    lax.fori_loop(0, rows, put, 0, unroll=4)
    step = rows // 4
    for k in range(4):
        both = mm_nt(flat(d3[step * k : step * (k + 1) + 1]), b_two[...])
        value = mm_nt(flat(d3[step * k + 2 : step * (k + 1) + 2]), b_last[...])
        value = value + both[COLS:, 0:n] + both[0 : step * COLS, n : 2 * n]
        d[step * k : step * (k + 1)] = value.reshape(step, COLS, LANES)
    put_split(send, 0, stack(slope_sums(tab, d, z_in, norm_in, keeps_in, dout)))
    blocks = columns(x_sum.shape[0])
    put_split(send, 4, stack([jnp.transpose(x_sum[lanes, :])[0:1] for lanes in blocks]))
    high, low = pair_high[:, 4 : 4 + 2 * share, :], pair_low[:, p_at : p_at + 2 * share, :]
    pass_pair(send, 4 + 2 * len(blocks), high, low, marks, norm.shape[0])


def b10(
    tab, got, labels, dout_in, z, norm, keeps, w, grad_pre, slope, zc, zp, keeps_cp,
    norm_c, w_c, slope_in, z_in, keeps_in,
    dz, grad_pre_2, send, d_in, d, low,
):
    rows, chans = zc.shape[0], zc.shape[2]
    pixels = 1.0 * rows * (COLS - 4)
    marks = labels[...]
    total = over_group(get_split(got, 0, 2), marks, entry(tab, OWN))
    coefs = own_coefs(tab, marks, norm, keeps, pixels, total[0:1], total[1:2])
    normed_grad(dz, dout_in, z, *coefs)
    d[...] = mm_nt(flat(dz[...]), w[...]).reshape(d.shape)
    mean_c, rstd_c, mean_p, rstd_p = (keeps_cp[k : k + 1, :] for k in range(4))
    a_c = rstd_c * gain_of(norm_c, entry(tab, OWN))

    def sum_up(i, carry):
        sums, prod_c, prod_p = carry
        g = (grad_pre[i] + d[i]) * slope[i]
        grad_pre_2[i] = g
        low[i] = (a_c * g).astype(BF16)
        return (
            sums + fold(g),
            prod_c + fold(g * (zc[i] - mean_c)),
            prod_p + fold(g * (zp[i] - mean_p)),
        )

    start = zeros8(chans)
    sums, prod_c, prod_p = lax.fori_loop(0, rows, sum_up, (start, start, start), unroll=4)
    wide = [down(sums), down(prod_c) * rstd_c, down(prod_p) * rstd_p]
    inner = inner_sums(low, w_c, slope_in, z_in, keeps_in, d_in)
    parts = [stack([v[:, 0 : chans // 2], v[:, chans // 2 :]]) for v in wide]
    values = join([*parts, stack(inner)])
    send[...] = jnp.broadcast_to(values[None], send.shape)


def inner_sums(low, w, slope, z, keeps, d_in):
    d_in[...] = mm_nt(flat(low[...]), w[...]).reshape(d_in.shape)
    mean, rstd = keeps[0:1, :], keeps[1:2, :]

    def add(i, carry):
        g = slope[i] * d_in[i]
        return carry[0] + fold(g), carry[1] + fold(g * (z[i] - mean))

    sums = lax.fori_loop(0, z.shape[0], add, (zeros8(LANES), zeros8(LANES)), unroll=7)
    return down(sums[0]), down(sums[1]) * rstd


def inner_grad(act, m, line, slope, d_in, d):
    both = mm(flat(act[...]), m)
    d[...] = (both[:, 0:LANES] + both[:, LANES:]).reshape(d.shape)

    def put(i, carry):
        d[i] = slope[i] * (d_in[i] + d[i] + line)
        return carry

    lax.fori_loop(0, d.shape[0], put, 0, unroll=7)


def normed_grad(dz, dout, z, mean, a, b, c):
    keep = valid_cols(z.shape[2])

    def put(i, carry):
        v = a * dout[i] + b * (z[i] - mean) + c
        dz[i] = jnp.where(keep, v, 0.0).astype(BF16)
        return carry

    lax.fori_loop(0, z.shape[0], put, 0, unroll=4)


def b12(
    tab, own10, labels, norm_c, keeps_c, w_c, got_act, got_q, got_p, own_p, act, slope, d_in,
    z, norm, keeps, xs, d2, kept, sent, own_sums, dz, packed, dout, *, share, q_at, p_at,
):
    rows = z.shape[0]
    pixels = 1.0 * rows * (COLS - 4)
    outer, n = norm_c.shape[2], LANES
    marks = labels[...]
    total = own10[...]
    cuts = (0, outer, 2 * outer, 2 * outer + n, 2 * outer + 2 * n)
    m, line, (a, b, c), found = pair_solve(
        tab, marks, (norm_c, keeps_c.at[0:2]), (norm, keeps),
        [total[:, u:v] for u, v in zip(cuts, cuts[1:])], w_c, get_split(got_act, 0, 1),
        get_split(got_q, q_at, 2),
        got_p[:, p_at : p_at + 2 * share, :].astype(F32) + own_p[...], pixels,
    )
    own_sums[0:1, :] = found[0]
    own_sums[1:2, :] = found[1]
    inner_grad(act, m, line, slope, d_in, dout)
    mean = keeps[0:1, :]
    keep = valid_cols(LANES)
    d2[rows] = jnp.zeros(d2.shape[1:], BF16)

    def put(i, carry):
        v = a * dout[i] + b * (z[i] - mean) + c
        v = jnp.where(keep, v, 0.0)
        low = v.astype(BF16)
        dz[i] = low
        d2[i, :, 0:n] = low
        d2[i, :, n : 2 * n] = pltpu.roll(v, COLS - 1, 0).astype(BF16)
        return carry

    lax.fori_loop(0, rows, put, 0, unroll=4)
    low = flat(dz[...])
    cur = mm_side(flat(xs[1 : rows + 1]), low)
    for k, (y, x) in enumerate(((1, 1), (1, 2), (1, 0), (2, 1), (2, 2), (2, 0))):
        put_rows(packed, n * (3 * y + x), cur[n * k : n * (k + 1)])
    up = mm_side(flat(xs[0:rows, :, 3 * n : 6 * n]), low)
    for k, (y, x) in enumerate(((0, 1), (0, 2), (0, 0))):
        put_rows(packed, n * (3 * y + x), up[n * k : n * (k + 1)])
    share_out(tab, packed, 9 * n, kept, sent)


def b12_images(
    tab, d2, b_even, b_odd, zz, norm_in, keeps_in, dn, sums_out, de, do, wide, *, own
):
    rows = de.shape[0]
    n = LANES
    half = half_of(tab)
    first = rows * (half if own else 1 - half)
    step = rows // 2
    for k in range(2):
        here = flat(d2[pl.ds(first + step * k, step)])
        below = flat(d2[pl.ds(first + step * k + 1, step)])
        de[step * k : step * (k + 1)] = mm_nt(here, b_even[...]).reshape(step, COLS, 2 * n)
        odd = mm_nt(here, b_odd[:, 0 : 2 * n]) + mm_nt(below, b_odd[:, 2 * n : 4 * n])
        do[step * k : step * (k + 1)] = odd.reshape(step, COLS, 2 * n)
    mean_1, rstd_1 = keeps_in[0:1, :], keeps_in[1:2, :]
    group = entry(tab, OWN)
    scale = rstd_1 * gain_of(norm_in, group)
    bias = 0.5 * (shift_of(norm_in, group) - mean_1 * scale)
    scale = 0.5 * scale
    keep = valid_cols(LANES) & chan_mask(tab)

    def emit(i, carry):
        sums, products = carry
        for ra in (0, 1):
            planes = (de, do)[ra]
            for cb in (0, 1):
                zv = zz[2 * i + ra, pl.ds(cb, COLS, stride=2), :]
                g = planes[i, :, n * cb : n * (cb + 1)] * slope_of_half(zv * scale + bias)
                g = jnp.where(keep, g, 0.0)
                sums = sums + fold(g)
                products = products + fold(g * (zv - mean_1))
                wide[ra, pl.ds(cb, COLS, stride=2), :] = g
            dn[2 * i + ra] = wide[ra].astype(BF16)
        return sums, products

    totals = lax.fori_loop(0, rows, emit, (zeros8(n), zeros8(n)), unroll=4)
    sums_out[0:1, :] = down(totals[0])
    sums_out[1:2, :] = down(totals[1]) * rstd_1


def b13(
    tab, got, labels, norm, keeps, w, z_own, z_for, dn_own, dn_for, gs_own, gs_for, *rest, at, held
):
    finished, outs = rest[:held], rest[held : 2 * held]
    grad, grad_norm, dz, wide, grad_v, norm_v, sems = rest[2 * held :]
    copies = [
        pltpu.make_async_copy(a, b, sems.at[k]) for k, (a, b) in enumerate(zip(finished, outs))
    ]
    for copy in copies:
        copy.start()
    rows, cols = grad.shape[1], grad.shape[2]
    half = half_of(tab)
    pixels = 2.0 * rows * cols
    marks = labels[...]
    totals = last_sums(got.at[:, at : at + 4, :], marks, norm.shape[0])
    for g in range(norm.shape[0]):
        norm_v[g, 0:1, :] = totals[g][1]
        norm_v[g, 1:2, :] = totals[g][0]
    copies.append(pltpu.make_async_copy(norm_v, grad_norm, sems.at[held]))
    copies[-1].start()
    keep = lax.broadcasted_iota(jnp.int32, (z_own.shape[1], LANES), 0) < cols
    for k, (z, dn, gs) in enumerate(((z_own, dn_own, gs_own), (z_for, dn_for, gs_for))):
        group = entry(tab, OWN if k == 0 else OTHER)
        shift_sum = own_of([t[0] for t in totals], group)
        gain_sum = own_of([t[1] for t in totals], group)
        count = group_count(marks, group) * pixels
        mean, rstd = keeps[2 * k : 2 * k + 1, :], keeps[2 * k + 1 : 2 * k + 2, :]
        a = rstd * gain_of(norm, group)
        b = -(a * rstd) * gain_sum / count
        c = -a * shift_sum / count

        def put(i, carry, z=z, dn=dn, mean=mean, a=a, b=b, c=c):
            v = a * dn[i].astype(F32) + b * (z[i] - mean) + c
            dz[i] = jnp.where(keep, v, 0.0).astype(BF16)
            return carry

        lax.fori_loop(0, rows, put, 0, unroll=4)
        place = half if k == 0 else 1 - half
        step = rows // 2
        for q in range(2):
            low = flat(dz[step * q : step * (q + 1)])
            for p in range(wide.shape[0]):
                values = mm_nt(low, w[LANES * p : LANES * (p + 1), :])
                wide[p, step * q : step * (q + 1)] = values.reshape(step, -1, LANES)

            def emit(i, carry, gs=gs, place=place):
                even = pl.ds(0, COLS, stride=2)
                for p in range(wide.shape[0]):
                    lanes = slice(LANES * p, LANES * (p + 1))
                    wide[p, 2 * i, even, :] = wide[p, 2 * i, even, :] + gs[i, :, lanes].astype(F32)
                    grad_v[place, 2 * i, :, lanes] = wide[p, 2 * i, 0:cols, :].astype(BF16)
                    grad_v[place, 2 * i + 1, :, lanes] = wide[p, 2 * i + 1, 0:cols, :].astype(BF16)
                return carry

            lax.fori_loop(step // 2 * q, step // 2 * (q + 1), emit, 0, unroll=True)
            part = pl.ds(step * q, step)
            copies.append(
                pltpu.make_async_copy(
                    grad_v.at[place, part], grad.at[place, part], sems.at[held + 1 + 2 * k + q]
                )
            )
            copies[-1].start()
    for copy in copies:
        copy.wait()


def put_rows(out, at, value):
    for j in range(value.shape[1] // LANES):
        out[at : at + value.shape[0], :] = value[:, LANES * j : LANES * (j + 1)].astype(BF16)
        at += value.shape[0]
    return at


def take_rows(source, at, out):
    rows = out.shape[0]
    for j in range(out.shape[1] // LANES):
        out[:, LANES * j : LANES * (j + 1)] = source(at, rows)
        at += rows
    return at


def share_out(tab, packed, used, kept, sent):
    if used < packed.shape[0]:
        packed[used:, :] = jnp.zeros((packed.shape[0] - used, LANES), BF16)
    half = half_of(tab)
    size = kept.shape[0] * kept.shape[1]
    for out, place in ((kept, half), (sent, 1 - half)):
        out[...] = packed[pl.ds(pl.multiple_of(size * place, 16), size), :].reshape(out.shape)


def g_most(
    tab, act_2b, x3, dz_2b, joined, dz_2a, act_1b, xee,
    got, labels, norm_c, norm_p, keeps, grad_pre_2, zc, zp,
    got_2c, norm_2c, keeps_2c, grad_pre, z_2c,
    kept, sent, dz_p, own10, packed, dz_1c, dz_2c,
):
    rows, outer = dz_2b.shape[0], zc.shape[2]
    pixels = 1.0 * rows * (COLS - 4)
    marks, label = labels[...], entry(tab, OWN)
    blocks = outer // LANES
    total = group_sum(got, marks, label)
    lines = wide_lines(total, outer)
    for k in range(2):
        own10[:, outer * k : outer * (k + 1)] = lines[k]
        at = 2 * outer + LANES * k
        own10[:, at : at + LANES] = total[k : k + 1, 3 * outer // 2 :]
    wide = [
        line_of(over_group(get_split(got_2c, 2 * blocks * k, blocks), marks, label)) for k in (0, 1)
    ]
    mean, a, b, c = own_coefs(tab, marks, norm_2c, keeps_2c, pixels, *wide)
    gate = 0.25 * tiled(entry(tab, GATE), outer)
    normed_grad(dz_2c, grad_pre, z_2c, mean, a * gate, b, c)
    coefs = own_coefs(tab, marks, norm_c, keeps.at[0:2], pixels, lines[0], lines[1])
    normed_grad(dz_1c, grad_pre_2, zc, *coefs)
    coefs = own_coefs(tab, marks, norm_p, keeps.at[2:4], pixels, lines[0], lines[2])
    normed_grad(dz_p, grad_pre_2, zp, *coefs)
    at = put_rows(packed, 0, mm_tn(flat(act_2b[...]), flat(dz_2c[...])))
    low = flat(dz_2b[...])
    for y in range(3):
        at = put_rows(packed, at, mm_side(flat(x3[y : y + rows]), low))
    at = put_rows(packed, at, mm_side(flat(joined[...]), flat(dz_2a[...])))
    at = put_rows(packed, at, mm_tn(flat(act_1b[...]), flat(dz_1c[...])))
    at = put_rows(packed, at, mm_tn(flat(xee[...]), flat(dz_p[...])))
    share_out(tab, packed, at, kept, sent)


def strided_grad(tab, dz_p, w_p, gs_own, gs_oth):
    half = half_of(tab)
    count = gs_own.shape[0]
    for k, gs in enumerate((gs_own, gs_oth)):
        first = count * (half if k == 0 else 1 - half)
        got = mm_nt(flat(dz_p[pl.ds(first, count)]), w_p[...])
        gs[...] = got.reshape(gs.shape).astype(BF16)


def g_xz(keeps, x_own, x_oth, z_own, z_oth, out, x_sum, low, tall):
    rows, n = z_own.shape[0], LANES
    mean = keeps[0:1, :]
    low[:, :, n : 2 * n] = jnp.ones((rows, z_own.shape[1], n), BF16)
    value = None
    for x, z in ((x_own, z_own), (x_oth, z_oth)):

        def put(i, carry, z=z):
            low[i, :, 0:n] = (z[i] - mean).astype(BF16)
            return carry

        lax.fori_loop(0, rows, put, 0, unroll=4)
        term = mm_tn(flat(x[...]), flat(low[...]))
        value = term if value is None else value + term
    at = value.shape[0]
    tall[0:at, :] = value[:, 0:n]
    if at < tall.shape[0]:
        tall[at:, :] = jnp.zeros((tall.shape[0] - at, n), F32)
    out[...] = tall[...].reshape(out.shape).astype(BF16)
    x_sum[...] = value[:, n : 2 * n]


def g_xd(
    tab, sums_own, sums_oth, norm, keeps, x_sum, got_x, labels, x_own, x_oth, dn_own, dn_oth,
    z_own, z_oth, out, sums, low,
):
    rows = dn_own.shape[0]
    n = LANES
    pixels = 1.0 * (2 * rows) * (2 * (COLS - 4))
    sums[...] = sums_own[...] + sums_oth[...]
    a = keeps[1:2, :] * gain_of(norm, entry(tab, OWN))
    local = sums[0:1, :] / pixels
    mean = keeps[0:1, :]
    b = -(a * keeps[1:2, :]) * sums[1:2, :] / pixels
    value = None
    for x, dn, z in ((x_own, dn_own, z_own), (x_oth, dn_oth, z_oth)):

        def put(i, carry, dn=dn, z=z):
            low[i] = (a * (dn[i].astype(F32) - local) + b * (z[i] - mean)).astype(BF16)
            return carry

        lax.fori_loop(0, rows, put, 0, unroll=4)
        term = mm_tn(flat(low[...]), flat(x[...]))
        value = term if value is None else value + term
    value = stack([jnp.transpose(value[:, lanes]) for lanes in columns(value.shape[1])])
    marks, label = labels[...], entry(tab, OWN)
    total = over_group(get_split(got_x, 4, x_sum.shape[0] // n), marks, label)
    total = join([total[k : k + 1] for k in range(total.shape[0])])
    total = total / tiled(group_count(marks, label), total.shape[1])
    total = jnp.broadcast_to(total, (8, total.shape[1]))
    means = jnp.concatenate(
        [jnp.transpose(total[:, lanes])[:, 0:1] for lanes in columns(total.shape[1])], axis=0
    )
    value = value + (x_sum[...] - means) * (a * local)
    at = value.shape[0]
    out[0:at, :] = value.astype(BF16)
    if at < out.shape[0]:
        out[at:, :] = jnp.zeros((out.shape[0] - at, n), BF16)


def pack_last(tall, sums, kept, got, kept_1b, got_1b, xz, send, *, stats_at, part):
    n = LANES
    devices = send.shape[0]
    piece, share = kept.shape[1], tall.shape[0] // devices
    first = kept.shape[0]
    second = first + kept_1b.shape[0]
    send[0:first, 0:piece, :] = (kept[...].astype(F32) + got[...].astype(F32)).astype(BF16)
    send[first:second, 0:piece, :] = (kept_1b[...].astype(F32) + got_1b[...].astype(F32)).astype(BF16)
    if second < devices:
        send[second:, 0:piece, :] = jnp.zeros((devices - second, piece, n), BF16)
    send[:, piece : piece + share, :] = tall[...].reshape(devices, share, n)
    put_split(send, stats_at, sums[...])
    put_part(send, stats_at + 4, xz, part)


def last_sums(stats, marks, groups):
    values = stats[:, 0:2, :].astype(F32) + stats[:, 2:4, :].astype(F32)
    out = []
    for g in range(groups):
        total = jnp.sum(values * (marks == float(g)).astype(F32), axis=0)
        out.append((total[0:1], total[1:2]))
    return out


def add_all(
    got, labels, norm, keeps_all, got_a, got_b, found_2b, found_1b, out, *, at, pixels, parts
):
    devices, n = got.shape[0], LANES
    half = devices // 2
    share = parts[-1][2]
    piece = (out.shape[1] - share - 8) // 2
    marks = labels[...]
    value = jnp.sum(got[:, piece : piece + share, :].astype(F32), axis=0)
    products = get_split(got, at, 2)[:, 1:2, :]
    lack = jnp.zeros(products.shape, F32)
    for g in range(norm.shape[0]):
        rstd = keeps_all[2 * g + 1 : 2 * g + 2, :]
        factor = -(rstd * rstd * norm[g, 0:1, :]) / pixels
        same = (marks == float(g)).astype(F32)
        middle = jnp.sum(products * same, axis=0) / jnp.sum(same, axis=0)
        lack = lack + (middle[None] - products) * (factor[None] * same)
    rows = [
        jnp.sum(source[:, start : start + last - first, :].astype(F32) * lack, axis=0)
        for source, (start, first, last) in zip((got_a, got_b, got), parts)
        if last > first
    ]
    value = value + jnp.concatenate(rows, axis=0)
    for k in (0, 1):
        total = jnp.sum(got[half * k : half * (k + 1), 0:piece, :].astype(F32), axis=0).astype(BF16)
        out[:, piece * k : piece * (k + 1), :] = jnp.broadcast_to(
            total[None], (out.shape[0], piece, n)
        )
    out[:, 2 * piece : 2 * piece + share, :] = jnp.broadcast_to(
        value.astype(BF16)[None], (out.shape[0], share, n)
    )
    put_split(out, 2 * piece + share, stack([found_2b[...], found_1b[...]]))


def place_parts(minor, parts, packed, tall, found, piece):
    far, share = parts[0].shape[0], tall.shape[1]
    for k, part in enumerate(parts):
        base = lax.bitwise_xor(minor, jnp.int32(k))

        def place(z, carry, part=part, base=base):
            owner = base + NEAR * z
            for h in (0, 1):
                packed[h, owner] = part[z, piece * h : piece * (h + 1), :]
            tall[owner] = part[z, 2 * piece : 2 * piece + share, :].astype(F32)
            sums = part[z, 2 * piece + share :, :].astype(F32)
            found[owner] = sums[0:4] + sums[4:8]
            return carry

        lax.fori_loop(0, far, place, 0, unroll=min(far, 4))


def unpack_own(tab, *refs, piece):
    place_parts(half_of(tab, MINOR), refs[:NEAR], *refs[NEAR:], piece)


def unpack(tab, labels, packed_own, tall_own, found_own, *refs, first, second, piece):
    parts, outs, values = refs[:NEAR], refs[NEAR : NEAR + 9], refs[NEAR + 9 :]
    *values, packed_oth, tall_oth, found_oth, sems = values
    place_parts(half_of(tab, MINOR), parts, packed_oth, tall_oth, found_oth, piece)
    half = half_of(tab)
    copies = [
        pltpu.make_async_copy(value, out, sems.at[k]) for k, (value, out) in enumerate(zip(values, outs))
    ]
    w_1b, w_1a, *grad_norms = values[5:9]
    own, oth = (packed_own, tall_own, found_own), (packed_oth, tall_oth, found_oth)
    for core in (0, 1):

        @pl.when(half == core)
        def _():
            packed, tall, found = zip(*((own, oth) if core == 0 else (oth, own)))
            most, last = [], []
            for h in (0, 1):
                pieces = [flat(v[h]) for v in packed]
                middle = pieces[0].shape[0]
                cut = first * piece
                most.append((pieces, middle))
                last.append((cut, pieces, middle))

            def span(pieces, middle, at, rows):
                found_rows = []
                if at < middle:
                    found_rows.append(pieces[0][at : min(at + rows, middle)])
                if at + rows > middle:
                    found_rows.append(pieces[1][max(at - middle, 0) : at + rows - middle])
                return [v.astype(F32) for v in found_rows]

            size = first * piece

            def source(at, rows):
                out = []
                if at < size:
                    out += span(*most[0], at, min(rows, size - at))
                if at + rows > size:
                    start = max(at - size, 0)
                    out += span(*most[1], start, at + rows - size - start)
                return out[0] if len(out) == 1 else stack(out)

            starts = [0]
            for value in values[0:4]:
                starts.append(starts[-1] + value.shape[0] * value.shape[1] // LANES)
            for k in (1, 4):
                take_rows(source, starts[k], values[k])
                copies[k].start()
            left = w_1b.shape[0]
            for k, (cut, pieces, middle) in enumerate(last):
                rows = min(second * piece, left)
                lines = span(pieces, middle, cut, rows)
                start = second * piece * k
                w_1b[start : start + rows, :] = lines[0] if len(lines) == 1 else stack(lines)
                left -= rows
            copies[5].start()
            for k in (0, 2, 3):
                take_rows(source, starts[k], values[k])
                copies[k].start()
            lines = stack([flat(v[...]) for v in tall])
            w_1a[...] = lines[0 : w_1a.shape[0]]
            copies[6].start()
            sums = jnp.concatenate([v[...] for v in found], axis=0)
            for k, grad_norm in enumerate(grad_norms):
                norm_from_owners(sums[:, 2 * k : 2 * k + 2, :], labels[...], grad_norm)
                copies[7 + k].start()

    for copy in copies:
        copy.wait()


def norm_from_owners(found, marks, grad_norm):
    for g in range(grad_norm.shape[0]):
        total = over_group(found, marks, float(g)) / group_count(marks, float(g))
        grad_norm[g, 0:1, :] = total[1:2]
        grad_norm[g, 1:2, :] = total[0:1]


def gather(send):
    return lax.all_to_all(send, AXES, 0, 0)


def tie(*values):
    return lax.optimization_barrier(values)


def swap(block):
    return lax.ppermute(block, "rows", [(0, 1), (1, 0)])


def body(
    images, w_1a, w_1b, w_1c, w_1p, w_2a, w_2b, w_2c,
    norm_1a, norm_1b, norm_1c, norm_1p, norm_2a, norm_2b, norm_2c,
    cotangent, group, width, gate,
):
    devices = lax.axis_size("rows") * lax.axis_size("batch")
    place = lax.axis_index(AXES).astype(jnp.int32).reshape(1)
    norms = (norm_1a, norm_1b, norm_1c, norm_1p, norm_2a, norm_2b, norm_2c)
    norm_1a, norm_1b, norm_1c, norm_1p, norm_2a, norm_2b, norm_2c = (
        v.transpose(1, 0, 2) for v in norms
    )
    outer, inputs = w_1c.shape[1], w_1a.shape[0]
    rows = cotangent.shape[1]
    cols_in = 2 * COLS
    n, m = LANES, devices

    def send(stats, channels=LANES):
        return ((m, channels // LANES, stats * LANES), F32)

    def maps(channels, dtype=F32):
        return ((rows, COLS, channels), dtype)

    def scratch(channels, dtype=F32):
        return pltpu.VMEM((rows, COLS, channels), dtype)

    def params(*arrays):
        return [(a.shape, F32) for a in arrays]

    def mean_scale(channels, count=1):
        return ((2 * count, channels), F32)

    wide_in = ((rows, cols_in, inputs), BF16)
    wide_z = ((rows, cols_in, n), F32)
    raw = images.shape
    tab, x_own, x_for, z_own, z_for, s1 = stage(
        functools.partial(f1, batch=devices // 2), [((8, n), F32), wide_in, wide_in, wide_z, wide_z, send(5)],
        [*(pltpu.SMEM(v.shape, jnp.int32) for v in (place, group, width, gate)),
         pltpu.VMEM(raw, BF16), pltpu.VMEM(w_1a.shape, BF16), pltpu.VMEM((8, n), F32),
         pltpu.SemaphoreType.DMA((7,))],
        hbm=(0, 1, 2, 3, 4, 5),
    )(place, group, width, gate, images, w_1a)
    s1, v_1b, v_2b = tie(s1, w_1b, w_2b)
    built = stage(
        prepare,
        [(v, BF16) for v in (
            (3 * n, n), (3 * n, 2 * n), (3 * n, 2 * n), (3 * n, n),
            (2 * n, 2 * n), (2 * n, 4 * n), (2 * n, 3 * n), (n, 3 * n),
        )],
    )(v_1b, v_2b)
    s1, x_for, w_even, w_odd, w_two, w_last, b_even, b_odd, b_two, b_last = tie(s1, x_for, *built)
    x_oth = swap(x_for)
    g1 = gather(s1)
    g1, x_oth = tie(g1, x_oth)
    xee, z_1p, stats_1p = stage(
        f1_strided,
        [maps(inputs, BF16), maps(outer), ((1, inputs + outer), F32)],
        [pltpu.VMEM((inputs // n, cols_in, n), F32)],
    )(tab, x_own, x_oth, w_1p)
    xs, z_1b, s2, labels, k_1a, k_all, z_oth = stage(
        f2,
        [((rows + 1, COLS, 6 * n), BF16), maps(n), send(2 + (inputs + outer) // n),
         ((m, 1, n), F32), mean_scale(n, 2), mean_scale(n, norm_1a.shape[0]), wide_z],
    )(tab, g1, z_own, x_oth, w_1a, norm_1a, w_even, w_odd, stats_1p)
    share = -(-inputs // devices)
    half_in = ((rows, cols_in, n), BF16)
    xz, x_sum = stage(
        g_xz, [((devices, share, n), BF16), ((inputs, n), F32)],
        [pltpu.VMEM((rows, cols_in, 2 * n), BF16), pltpu.VMEM((devices * share, n), F32)],
    )(k_1a, x_own, x_oth, z_own, z_oth)
    s2, xz, x_sum = tie(s2, xz, x_sum)
    g2 = gather(s2)
    share_1 = -(-n // devices)
    p_rows = ((devices, 2 * share_1, n), BF16)
    own_rows = ((devices, 2 * share_1, n), F32)
    wide_rows = outer // n
    p_at = 2 + wide_rows
    xz_3 = p_at + 2 * share_1
    high_3 = -(-xz_3 // 16) * 16
    xz_6 = p_at + 4 * share_1
    high_6 = -(-xz_6 // 8) * 8
    cut_3 = min(share, high_3 - xz_3)
    cut_6 = min(share, cut_3 + high_6 - xz_6)
    act_1b, z_1c, s3, k_1b, k_p, slope_1b, q_1b, p_1b, own_1b = stage(
        functools.partial(f3, share=share_1, part=(0, cut_3)),
        [maps(n, BF16), maps(outer), ((devices, high_3, n), BF16), mean_scale(n),
         mean_scale(outer), maps(n), ((2, n), F32), p_rows, own_rows],
        [scratch(4 * n, BF16), pltpu.VMEM(p_rows[0], BF16)],
    )(tab, g2, labels, z_1b, norm_1b, w_1c, w_1p, xz)
    g3 = gather(s3)
    high = -(-(8 + 2 * share_1) // 16) * 16
    joined, slope, z_2a, s4, k_cp = stage(
        f4,
        [maps(outer, BF16), maps(outer), maps(n), ((devices, high, n), BF16),
         mean_scale(outer, 2)],
    )(tab, g3, labels, z_1c, z_1p, norm_1c, norm_1p, k_p, w_1c, w_2a, p_1b, q_1b)
    g4 = gather(s4)
    x3, z_2b, s5, k_2a = stage(
        f5, [((rows + 2, COLS, 3 * n), BF16), maps(n), send(2), mean_scale(n)]
    )(tab, g4, labels, z_2a, norm_2a, w_two, w_last)
    g5 = gather(s5)
    act_2b, z_2c, s6, k_2b, slope_2b, q_2b, own_2b = stage(
        functools.partial(f6, share=share_1, part=(cut_3, cut_6)),
        [maps(n, BF16), maps(outer), ((devices, high_6, n), BF16), mean_scale(n), maps(n),
         ((2, n), F32), own_rows],
        [scratch(4 * n, BF16), *(pltpu.VMEM(p_rows[0], BF16) for _ in range(2))],
    )(tab, g5, labels, z_2b, norm_2b, w_2c, xz)
    g6 = gather(s6)
    high_7 = -(-(4 * wide_rows + 8 + 2 * share_1) // 16) * 16
    result, grad_pre, s7, k_2c, d_2b = stage(
        functools.partial(b7, share=share_1, p_at=p_at),
        [(cotangent.shape[1:], BF16), maps(outer), ((devices, high_7, n), BF16),
         mean_scale(outer), maps(n)],
        [pltpu.VMEM((COLS, outer), F32), scratch(outer, BF16)],
    )(tab, g6, labels, joined, z_2c, norm_2c, w_2c, cotangent[0], slope_2b, z_2b, k_2b, q_2b)
    g7 = gather(s7)
    dz_2b, dout_2a, s9, found_2b = stage(
        functools.partial(b9, share=share_1, p_at=p_at),
        [maps(n, BF16), maps(n), ((devices, high, n), BF16), ((2, n), F32)],
        [pltpu.VMEM((rows + 2, COLS, 3 * n), BF16), scratch(n)],
    )(tab, g7, labels, norm_2c, k_2c, w_2c, g6, act_2b, slope_2b, d_2b, z_2b, norm_2b, k_2b,
      b_two, b_last, z_2a, norm_2a, k_2a, x_sum, g4, g3, own_2b)
    g9 = gather(s9)
    dz_2a, grad_pre_2, s10, d_1b = stage(
        b10,
        [maps(n, BF16), maps(outer), ((devices, 2, 3 * outer // 2 + n), F32), maps(n)],
        [scratch(outer), scratch(outer, BF16)],
    )(tab, g9, labels, dout_2a, z_2a, norm_2a, k_2a, w_2a, grad_pre, slope, z_1c, z_1p, k_cp,
      norm_1c, w_1c, slope_1b, z_1b, k_1b)
    g10 = gather(s10)
    half_map = ((rows // 2, COLS, inputs), BF16)
    most_rows = sum(v.size for v in (w_2c, w_2b, w_2a, w_1c, w_1p)) // n
    rows_1b = w_1b.size // n
    piece = 16
    while -(-most_rows // (2 * piece)) - (-rows_1b // (2 * piece)) > devices:
        piece += 16
    first, second = -(-most_rows // (2 * piece)), -(-rows_1b // (2 * piece))
    part, part_1b = ((first, piece, n), BF16), ((second, piece, n), BF16)
    kept, sent, dz_1p, own10 = stage(
        g_most,
        [part, part, maps(outer, BF16), ((1, 2 * outer + 2 * n), F32)],
        [pltpu.VMEM((2 * first * piece, n), BF16), *(scratch(outer, BF16) for _ in range(2))],
    )(tab, act_2b, x3, dz_2b, joined, dz_2a, act_1b, xee,
      g10, labels, norm_1c, norm_1p, k_cp, grad_pre_2, z_1c, z_1p,
      g7, norm_2c, k_2c, grad_pre, z_2c)
    gs_own, gs_send = stage(strided_grad, [half_map, half_map])(tab, dz_1p, w_1p)
    got, gs_for = swap(sent), swap(gs_send)
    half_in = ((rows, cols_in, n), BF16)
    d2, kept_1b, sent_1b, found_1b = stage(
        functools.partial(b12, share=share_1, q_at=4 + 2 * share_1, p_at=4 + 2 * (inputs // n)),
        [((rows + 1, COLS, 2 * n), BF16), part_1b, part_1b, ((2, n), F32)],
        [scratch(n, BF16), pltpu.VMEM((2 * second * piece, n), BF16), scratch(n)],
    )(tab, own10, labels, norm_1c, k_cp, w_1c, g3, g4, g9, own_1b, act_1b, slope_1b, d_1b,
      z_1b, norm_1b, k_1b, xs)
    got_1b = swap(sent_1b)
    sides = []
    for own, z in ((False, z_oth), (True, z_own)):
        sides.append(
            stage(
                functools.partial(b12_images, own=own), [half_in, ((2, n), F32)],
                [pltpu.VMEM((rows // 2, COLS, 2 * n), F32), pltpu.VMEM((rows // 2, COLS, 2 * n), F32),
                 pltpu.VMEM((2, cols_in, n), F32)],
            )(tab, d2, b_even, b_odd, z, norm_1a, k_1a)
        )
        if not own:
            dn_for = swap(sides[0][0])
            d2, _ = tie(d2, sides[0][0])
    (dn_send, sums_send), (dn_own, sums_own) = sides
    stats_at = piece + -(-share // 8) * 8
    high = -(-(stats_at + 4 + share - cut_6) // 16) * 16
    tall, sums_1a = stage(
        g_xd, [((devices * share, n), BF16), ((2, n), F32)], [pltpu.VMEM(half_in[0], BF16)]
    )(tab, sums_own, sums_send, norm_1a, k_1a, x_sum, g9, labels, x_own, x_oth, dn_own, dn_send,
      z_own, z_oth)
    tall, gs_for, dn_for = tie(tall, gs_for, dn_for)
    (s12,) = stage(
        functools.partial(pack_last, stats_at=stats_at, part=(cut_6, share)),
        [((devices, high, n), BF16)]
    )(tall, sums_1a, kept, got, kept_1b, got_1b, xz)
    g12 = gather(s12)
    pixels = 4.0 * images.shape[1] * images.shape[1]
    batch = devices // 2
    far = batch // NEAR
    (mine,) = stage(
        functools.partial(
            add_all, at=stats_at, pixels=pixels,
            parts=((xz_3, 0, cut_3), (xz_6, cut_3, cut_6), (stats_at + 4, cut_6, share)),
        ),
        [((far, 2 * piece + share + 8, n), BF16)],
    )(g12, labels, norm_1a, k_all, g3, g6, found_2b, found_1b)
    columns_of = [[k + NEAR * z for z in range(far)] for k in range(NEAR)]
    along = lax.all_to_all(mine, "batch", 0, 0, axis_index_groups=columns_of)
    near = [
        lax.ppermute(along, "batch", [(i, i ^ k) for i in range(batch)]) for k in range(1, NEAR)
    ]
    late, _ = tie(labels, along)
    grad_norms = stage(norm_tail, params(norm_2c, norm_2a, norm_1c, norm_1p))(late, g7, g9, g10)
    finished = (result, *grad_norms)
    held = len(finished)
    *finished, grad_images, grad_norm_1a = stage(
        functools.partial(b13, at=stats_at, held=held),
        [*((v.shape, v.dtype) for v in finished), (images.shape, BF16), *params(norm_1a)],
        [pltpu.VMEM(half_in[0], BF16), pltpu.VMEM((inputs // n, rows, cols_in, n), F32),
         pltpu.VMEM(images.shape, BF16), pltpu.VMEM(norm_1a.shape, F32),
         pltpu.SemaphoreType.DMA((held + 5,))],
        hbm_out=range(held + 2),
    )(tab, g12, labels, norm_1a, k_1a, w_1a, z_own, z_for, dn_own, dn_for, gs_own, gs_for, *finished)
    result, grad_norm_2c, grad_norm_2a, grad_norm_1c, grad_norm_1p = finished
    *near, grad_images = tie(*near, grad_images)
    parts = [along, *near]
    weights = (w_2c, w_2b.reshape(-1, n), w_2a, w_1c, w_1p, w_1b.reshape(-1, n), w_1a)
    side = [
        ((2, batch, piece, n), BF16), ((batch, share, n), F32), ((batch, 4, n), F32)
    ]
    crossed = [swap(v) for v in parts]
    placed = stage(functools.partial(unpack_own, piece=piece), side)(tab, *parts)
    t_2c, t_2b, t_2a, t_1c, t_1p, t_1b, t_1a, grad_norm_2b, grad_norm_1b = stage(
        functools.partial(unpack, first=first, second=second, piece=piece),
        [(v.shape, F32) for v in (*weights, norm_2b, norm_1b)],
        [*(pltpu.VMEM(v.shape, F32) for v in (*weights, norm_2b, norm_1b)),
         *(pltpu.VMEM(*v) for v in side), pltpu.SemaphoreType.DMA((9,))],
        hbm_out=range(9),
    )(tab, labels, *placed, *crossed)
    grads = (
        grad_norm_1a, grad_norm_1b, grad_norm_1c, grad_norm_1p,
        grad_norm_2a, grad_norm_2b, grad_norm_2c,
    )
    return (
        result[None], grad_images, t_1a, t_1b.reshape(w_1b.shape), t_1c, t_1p, t_2a,
        t_2b.reshape(w_2b.shape), t_2c, *[v.transpose(1, 0, 2) for v in grads],
    )


def solution(mesh):
    return jax.shard_map(
        body,
        mesh=mesh,
        in_specs=(
            P("batch", "rows", None, None),
            *[P()] * 14,
            P(("batch", "rows"), None, None, None),
            P("batch"),
            P(),
            P(),
        ),
        out_specs=(
            P(("batch", "rows"), None, None, None),
            P("batch", "rows", None, None),
            *[P()] * 14,
        ),
        check_vma=False,
    )
```

```python
import functools

import jax
import jax.numpy as jnp
from jax import lax
from jax.experimental import pallas as pl
from jax.experimental.pallas import tpu as pltpu
from jax.sharding import PartitionSpec as P

EPSILON = 1e-05
F32 = jnp.float32
BF16 = jnp.bfloat16
AXES = ("rows", "batch")
VMEM_LIMIT = 14 * 1024 * 1024
LANES = 128
COLS = 32
NEAR = 4


def full(memory=pltpu.VMEM):
    return pl.BlockSpec(memory_space=memory)


def stage(kernel, outs, scratch=(), hbm=(), hbm_out=()):
    def place(i, outside):
        return pltpu.HBM if i in outside else pltpu.VMEM

    def call(*args):
        args = [
            pltpu.with_memory_space_constraint(a, pltpu.HBM) if i in hbm else a
            for i, a in enumerate(args)
        ]
        return pl.pallas_call(
            kernel,
            out_shape=tuple(jax.ShapeDtypeStruct(s, d) for s, d in outs),
            in_specs=[full(place(i, hbm)) for i in range(len(args))],
            out_specs=tuple(
                full(place(i, hbm_out)) for i in range(len(outs))
            ),
            scratch_shapes=list(scratch),
            compiler_params=pltpu.CompilerParams(vmem_limit_bytes=VMEM_LIMIT),
            name=(kernel.func if isinstance(kernel, functools.partial) else kernel).__name__,
        )(*args)

    return call


def silu_of_half(u):
    return u + u * jnp.tanh(u)


def slope_of_half(u):
    t = jnp.tanh(u)
    return (0.5 + 0.5 * t) * (1.0 + u - u * t)


def fold(x):
    return (x[0:8] + x[8:16]) + (x[16:24] + x[24:32])


def row(total, stat):
    blocks = total.shape[0]
    pieces = [total[j : j + 1, LANES * stat : LANES * (stat + 1)] for j in range(blocks)]
    return pieces[0] if blocks == 1 else jnp.concatenate(pieces, axis=1)


def spread(out_ref, rows):
    blocks = out_ref.shape[1]
    for stat, values in enumerate(rows):
        for j in range(blocks):
            piece = values[:, LANES * j : LANES * (j + 1)]
            out_ref[:, j : j + 1, LANES * stat : LANES * (stat + 1)] = jnp.broadcast_to(
                piece[None], (out_ref.shape[0], 1, LANES)
            )


def group_sum(got_ref, labels, label):
    same = (labels == label).astype(F32)
    stats = got_ref.shape[2] // LANES
    parts = [
        jnp.sum(got_ref[:, :, LANES * s : LANES * (s + 1)] * same, axis=0) for s in range(stats)
    ]
    return jnp.concatenate(parts, axis=1) if stats > 1 else parts[0]


def group_count(labels, label):
    return jnp.sum((labels == label).astype(F32), axis=0)


def tiled(values, channels):
    return jnp.concatenate([values] * (channels // LANES), axis=1) if channels > LANES else values


def moments(first, second, pixels):
    mean = first / pixels
    return mean, lax.rsqrt(second / pixels - mean * mean + EPSILON)


def own_of(values, label):
    out = values[0]
    label = tiled(label, out.shape[1])
    for g in range(1, len(values)):
        out = jnp.where(label == float(g), values[g], out)
    return out


def gain_of(norm_ref, label):
    return own_of([norm_ref[g, 0:1, :] for g in range(norm_ref.shape[0])], label)


def shift_of(norm_ref, label):
    return own_of([norm_ref[g, 1:2, :] for g in range(norm_ref.shape[0])], label)


def valid_cols(channels):
    return lax.broadcasted_iota(jnp.int32, (COLS, channels), 0) < COLS - 4


def chan_mask(tab):
    return lax.broadcasted_iota(jnp.int32, (1, LANES), 1).astype(F32) < entry(tab, LIMIT)


def flat(x):
    return x.reshape(x.shape[0] * x.shape[1], x.shape[2])


def mm(a, b):
    return jnp.dot(a, b, preferred_element_type=F32)


def mm_nt(a, b):
    return lax.dot_general(a, b, (((1,), (1,)), ((), ())), preferred_element_type=F32)


def mm_tn(a, b):
    return lax.dot_general(a, b, (((0,), (0,)), ((), ())), preferred_element_type=F32)


def mm_side(a, b):
    turned = mm_tn(b, a)
    blocks = [
        jnp.transpose(turned[:, LANES * j : LANES * (j + 1)]) for j in range(a.shape[1] // LANES)
    ]
    return blocks[0] if len(blocks) == 1 else jnp.concatenate(blocks, axis=0)


def zeros8(channels):
    return jnp.zeros((8, channels), F32)


def down(x):
    return jnp.sum(x, axis=0, keepdims=True)


OWN, OTHER, HALF, LIMIT, GATE, MINOR = range(6)


def entry(tab, k):
    return tab[k : k + 1, :]


def half_of(tab, k=HALF):
    return (jnp.sum(entry(tab, k)) * (1.0 / LANES)).astype(jnp.int32)


def prepare(w1b, w2b, w_even, w_odd, w_two, w_last, b_even, b_odd, b_two, b_last):
    n = LANES
    for k, (y, x) in enumerate(((1, 1), (1, 2), (1, 0))):
        w_even[n * k : n * (k + 1), :] = w1b[y, x]
    for k, (low, high) in enumerate((((2, 1), (0, 1)), ((2, 2), (0, 2)), ((2, 0), (0, 0)))):
        w_odd[n * k : n * (k + 1), 0:n] = w1b[low]
        w_odd[n * k : n * (k + 1), n : 2 * n] = w1b[high]
    for x in range(3):
        w_two[n * x : n * (x + 1), 0:n] = w2b[0, x]
        w_two[n * x : n * (x + 1), n : 2 * n] = w2b[1, x]
        w_last[n * x : n * (x + 1), :] = w2b[2, x]
        b_two[0:n, n * x : n * (x + 1)] = w2b[1, x]
        b_two[n : 2 * n, n * x : n * (x + 1)] = w2b[2, x]
        b_last[:, n * x : n * (x + 1)] = w2b[0, x]
    nothing = jnp.zeros((n, n), BF16)
    b_even[0:n, 0:n] = w1b[1, 1]
    b_even[0:n, n : 2 * n] = nothing
    b_even[n : 2 * n, 0:n] = w1b[1, 2]
    b_even[n : 2 * n, n : 2 * n] = w1b[1, 0]
    for k, top in ((0, 2), (1, 0)):
        b_odd[0:n, 2 * n * k : 2 * n * k + n] = w1b[top, 1]
        b_odd[0:n, 2 * n * k + n : 2 * n * (k + 1)] = nothing
        b_odd[n : 2 * n, 2 * n * k : 2 * n * k + n] = w1b[top, 2]
        b_odd[n : 2 * n, 2 * n * k + n : 2 * n * (k + 1)] = w1b[top, 0]


def widen(source, x_pad):
    rows, cols, chans = source.shape
    gap = x_pad.shape[1] - cols

    def put(i, carry):
        x_pad[i, 0:cols, :] = source[i]
        x_pad[i, cols : cols + gap, :] = jnp.zeros((gap, chans), BF16)
        return carry

    lax.fori_loop(0, rows, put, 0, unroll=4)


def first_project(x_pad, w, z, stats=True):
    rows = x_pad.shape[0]
    step = rows // 4
    sums, squares = zeros8(LANES), zeros8(LANES)
    for c in range(4):
        values = mm(flat(x_pad[step * c : step * (c + 1)]), w[...])
        z[step * c : step * (c + 1)] = values.reshape(step, x_pad.shape[1], LANES)
        if stats:
            parts = values.reshape(-1, 8, LANES)
            sums = sums + jnp.sum(parts, axis=0)
            squares = squares + jnp.sum(parts * parts, axis=0)
    return sums, squares


def f1(
    place_at, group_at, width_at, gate_at, images, w_at, tab, x_own, x_for, z_own, z_for, send,
    place_ref, group, width, gate, raw, w, found, sems, *, batch,
):
    rows = images.shape[1] // 2
    parts = [pl.ds(rows * p, rows) for p in (0, 1)]
    pairs = (
        (place_at, place_ref), (group_at, group), (width_at, width), (gate_at, gate), (w_at, w),
        *((images.at[k, part], raw.at[k, part]) for k in (0, 1) for part in parts),
    )
    copies = [pltpu.make_async_copy(a, b, sems.at[k]) for k, (a, b) in enumerate(pairs)]
    for k in (0, 5, 4, 6, 7, 8, 1, 2, 3):
        copies[k].start()
    for k in (0, 4):
        copies[k].wait()
    half = lax.div(place_ref[0], batch)
    sides = ((x_own, z_own), (x_for, z_for))

    def one(k):
        for p, part in enumerate(parts):
            copies[5 + 2 * k + p].wait()
            for place in (0, 1):

                @pl.when(half == place)
                def _():
                    x_pad, _ = sides[k] if place == 0 else sides[1 - k]
                    widen(raw.at[k, part], x_pad.at[part])

        for place in (0, 1):

            @pl.when(half == place)
            def _():
                x_pad, z = sides[k] if place == 0 else sides[1 - k]
                sums, squares = first_project(x_pad, w, z)
                at = 2 * (k if place == 0 else 1 - k)
                found[at : at + 1, :] = down(sums)
                found[at + 1 : at + 2, :] = down(squares)

    one(0)
    one(1)
    for k in (1, 2, 3):
        copies[k].wait()
    rows = [found[k : k + 1, :] for k in range(4)]
    own, other = group[half], group[1 - half]
    values = {
        OWN: own, OTHER: other, HALF: half, LIMIT: w.shape[1] // 4 * width[own], GATE: gate[own],
        MINOR: lax.rem(lax.rem(place_ref[0], batch), NEAR),
    }
    tab[...] = jnp.zeros(tab.shape, F32)
    for k, v in values.items():
        tab[k : k + 1, :] = jnp.full((1, LANES), v.astype(F32))
    spread(send, [*rows, jnp.full((1, LANES), (own + 4 * other).astype(F32))])


def f1_strided(tab, x_own, x_oth, w, xee, z, stats, wide):
    half = half_of(tab)
    rows = x_own.shape[0] // 2
    for k, x_pad in enumerate((x_own, x_oth)):
        first = rows * (half if k == 0 else 1 - half)

        def put(i, carry, x_pad=x_pad, first=first):
            for b in range(wide.shape[0]):
                lanes = slice(LANES * b, LANES * (b + 1))
                wide[b] = x_pad[2 * i, :, lanes].astype(F32)
                xee[first + i, :, lanes] = wide[b, pl.ds(0, COLS, stride=2), :].astype(BF16)
            return carry

        lax.fori_loop(0, rows, put, 0, unroll=4)
    total = 2 * rows
    step = total // 7
    chans = z.shape[2]
    squares = zeros8(chans)
    for c in range(7):
        values = mm(flat(xee[step * c : step * (c + 1)]), w[...])
        z[step * c : step * (c + 1)] = values.reshape(step, COLS, chans)
        parts = values.reshape(-1, 8, chans)
        squares = squares + jnp.sum(parts * parts, axis=0)
    ones = jnp.ones((8, total * COLS), BF16)
    stats[:, 0 : w.shape[0]] = mm(ones, flat(xee[...]))[0:1]
    stats[:, w.shape[0] :] = down(squares)


def scale_shift(got, labels, tab, norm, pixels, slot=0):
    label = entry(tab, OWN)
    total = group_sum(got, labels, label)
    chans = norm.shape[2]
    count = tiled(group_count(labels, label), chans) * pixels
    mean, rstd = moments(row(total, 2 * slot), row(total, 2 * slot + 1), count)
    gain, shift = gain_of(norm, entry(tab, OWN)), shift_of(norm, entry(tab, OWN))
    return mean, rstd, gain, shift, count


def conv_stats(z, source, pair, single, send, extra=()):
    keep = valid_cols(LANES)[None]
    rows = z.shape[0]
    step = rows // 4
    (lanes_2, w_2, offsets), (lanes_1, w_1, offset) = pair, single
    sums, squares = zeros8(LANES), zeros8(LANES)
    base = min(offsets)
    for c in range(4):
        at = step * c
        both = mm(flat(source[at + base : at + base + step + 1, :, lanes_2]), w_2)
        values = mm(flat(source[at + offset : at + offset + step, :, lanes_1]), w_1)
        for k, own in enumerate(offsets):
            skip = COLS * (own - base)
            values = values + both[skip : skip + step * COLS, LANES * k : LANES * (k + 1)]
        values = jnp.where(keep, values.reshape(step, COLS, LANES), 0.0)
        z[at : at + step] = values
        parts = values.reshape(-1, 8, LANES)
        sums = sums + jnp.sum(parts, axis=0)
        squares = squares + jnp.sum(parts * parts, axis=0)
    spread(send, [down(sums), down(squares), *extra])


def f2(
    tab, got, z_own, x_oth, w, norm, w_even, w_odd, stats_p,
    xs, z, send, labels, keeps, keeps_all, z_oth,
):
    codes = got[:, :, 4 * LANES : 5 * LANES]
    others = jnp.floor(0.25 * codes)
    marks = codes - 4.0 * others
    labels[...] = marks
    rows = xs.shape[0] - 1
    pixels = 4.0 * rows * (COLS - 4)
    first_project(x_oth, w, z_oth, False)
    for g in range(norm.shape[0]):
        mine, theirs = (marks == float(g)).astype(F32), (others == float(g)).astype(F32)
        totals = [
            jnp.sum(
                got[:, :, LANES * s : LANES * (s + 1)] * mine
                + got[:, :, LANES * (s + 2) : LANES * (s + 3)] * theirs,
                axis=0,
            )
            for s in (0, 1)
        ]
        mean, rstd = moments(*totals, group_count(marks, float(g)) * pixels)
        keeps_all[2 * g : 2 * g + 1, :] = mean
        keeps_all[2 * g + 1 : 2 * g + 2, :] = rstd
    for k, slot in enumerate((OWN, OTHER)):
        for q in (0, 1):
            choices = [keeps_all[2 * g + q : 2 * g + q + 1, :] for g in range(norm.shape[0])]
            keeps[2 * k + q : 2 * k + q + 1, :] = own_of(choices, entry(tab, slot))
    mean, rstd = keeps[0:1, :], keeps[1:2, :]
    gain, shift = gain_of(norm, entry(tab, OWN)), shift_of(norm, entry(tab, OWN))
    scale = rstd * gain
    bias = 0.5 * (shift - mean * scale)
    scale = 0.5 * scale
    keep = valid_cols(LANES) & chan_mask(tab)
    half = half_of(tab)
    xs[0] = jnp.zeros(xs.shape[1:], BF16)
    n = LANES
    for k, zz in enumerate((z_own, z_oth)):
        first = 1 + (rows // 2) * (half if k == 0 else 1 - half)

        def put(i, carry, zz=zz, first=first):
            lane = 0
            for a in (0, 1):
                for b in (0, 1):
                    u = zz[2 * i + a, pl.ds(b, COLS, stride=2), :] * scale + bias
                    act = jnp.where(keep, silu_of_half(u), 0.0)
                    xs[first + i, :, lane : lane + n] = act.astype(BF16)
                    lane += n
                    if b == 1:
                        moved = pltpu.roll(act, 1, 0)
                        xs[first + i, :, lane : lane + n] = moved.astype(BF16)
                        lane += n
            return carry

        lax.fori_loop(0, rows // 2, put, 0, unroll=4)
    extra = [stats_p[:, lanes] for lanes in columns(stats_p.shape[1])]
    pair = (slice(3 * n, 6 * n), w_odd[...], (1, 0))
    conv_stats(z, xs, pair, (slice(0, 3 * n), w_even[...], 1), send, extra)


def project(act, w, z):
    rows, chans = z.shape[0], z.shape[2]
    step = rows // 7
    squares = zeros8(chans)
    for c in range(7):
        values = mm(flat(act[step * c : step * (c + 1)]), w[...])
        z[step * c : step * (c + 1)] = values.reshape(step, COLS, chans)
        parts = values.reshape(-1, 8, chans)
        squares = squares + jnp.sum(parts * parts, axis=0)
    return down(squares)


def join(pieces):
    return pieces[0] if len(pieces) == 1 else jnp.concatenate(pieces, axis=1)


def columns(channels):
    return [slice(LANES * j, LANES * (j + 1)) for j in range(channels // LANES)]


def three_parts(sums):
    high = sums.astype(BF16)
    rest = sums - high.astype(F32)
    mid = rest.astype(BF16)
    low = (rest - mid.astype(F32)).astype(BF16)
    lines = [v.astype(F32) for v in (high, mid, low)]
    lines.append(jnp.zeros((13, sums.shape[1]), F32))
    return jnp.concatenate(lines, axis=0).astype(BF16)


def through(sums, w):
    return down(mm(three_parts(sums), w))


def put_split(send, at, values):
    rows = values.shape[0]
    high = values.astype(BF16)
    rest = (values - high.astype(F32)).astype(BF16)
    for k, part in enumerate((high, rest)):
        send[:, at + rows * k : at + rows * (k + 1), :] = jnp.broadcast_to(
            part[None], (send.shape[0], rows, LANES)
        )


def get_split(got, at, rows):
    return got[:, at : at + rows, :].astype(F32) + got[:, at + rows : at + 2 * rows, :].astype(F32)


def over_group(values, marks, label):
    return jnp.sum(values * (marks == label).astype(F32), axis=0)


def stack(rows):
    return jnp.concatenate(rows, axis=0)


def activate_pair(tab, got, labels, z, norm, act, keeps, slope, both):
    rows = z.shape[0]
    pixels = 1.0 * rows * (COLS - 4)
    mean, rstd, gain, shift, _ = scale_shift(got, labels[...], tab, norm, pixels)
    keeps[0:1, :] = mean
    keeps[1:2, :] = rstd
    scale = rstd * gain
    bias = 0.5 * (shift - mean * scale)
    scale = 0.5 * scale
    keep = valid_cols(LANES) & chan_mask(tab)

    def put(i, carry):
        zz = z[i]
        u = zz * scale + bias
        t = jnp.tanh(u)
        p = u * t
        low = jnp.where(keep, u + p, 0.0).astype(BF16)
        act[i] = low
        s = jnp.where(keep, (0.5 + 0.5 * t) * (1.0 + u - p), 0.0)
        sx = s * ((zz - mean) * rstd)
        slope[i] = s
        for k, v in enumerate((s, sx)):
            high = v.astype(BF16)
            both[i, :, LANES * k : LANES * (k + 1)] = high
            both[i, :, LANES * (k + 2) : LANES * (k + 3)] = (v - high.astype(F32)).astype(BF16)
        return carry[0] + fold(low.astype(F32)), carry[1] + fold(s), carry[2] + fold(sx)

    start = zeros8(LANES)
    sums = lax.fori_loop(0, rows, put, (start, start, start), unroll=4)
    act_sum, *sums = [down(v) for v in sums]
    product = mm_tn(flat(act[...]), flat(both[...]))
    product = product[:, 0 : 2 * LANES] + product[:, 2 * LANES :]
    middle = jnp.broadcast_to(act_sum * (1.0 / pixels), (8, LANES))
    return act_sum, product - jnp.transpose(middle)[:, 0:1] * join(sums), stack(sums)


def rows_of(line):
    return stack([line[:, lanes] for lanes in columns(line.shape[1])])


def line_of(rows):
    return join([rows[k : k + 1, :] for k in range(rows.shape[0])])


def put_part(send, at, rows, part):
    first, last = part
    if last > first:
        send[:, at : at + last - first, :] = rows[:, first:last, :]


def pair_rows(product, devices, share, high, low, own):
    n = LANES
    missing = devices * share - n
    for h in (0, 1):
        values = product[:, n * h : n * (h + 1)]
        if missing:
            values = stack([values, jnp.zeros((missing, n), F32)])
        values = values.reshape(devices, share, n)
        first, last = share * h, share * (h + 1)
        top = values.astype(BF16)
        rest = (values - top.astype(F32)).astype(BF16)
        high[:, first:last, :] = top
        low[:, first:last, :] = rest
        own[:, first:last, :] = top.astype(F32) + rest.astype(F32)


def pass_pair(send, at, high, low, marks, groups):
    rows = high.astype(F32) + low.astype(F32)
    out = -rows
    for g in range(groups):
        same = (marks == float(g)).astype(F32)
        images = jnp.maximum(jnp.sum(same, axis=0), 1.0)
        out = out + (jnp.sum(rows * same, axis=0) / images)[None] * same
    send[:, at : at + rows.shape[1], :] = out.astype(BF16)


def pair_solve(tab, marks, outer, inner, sums, w, act_sums, q_rows, p_rows, pixels):
    label, n = entry(tab, OWN), LANES
    (norm_o, keeps_o), (norm_i, keeps_i) = outer, inner
    shift_o, gain_o, shift_i, gain_i = sums
    images = group_count(marks, label)
    count, count_o = images * pixels, tiled(images, norm_o.shape[2]) * pixels
    rstd_o = keeps_o[1:2, :]
    a_o = rstd_o * gain_of(norm_o, label)
    b_o, c_o = -(a_o * rstd_o) * gain_o / count_o, -a_o * shift_o / count_o
    scaled = w[...].astype(F32) * b_o
    high = scaled.astype(BF16)
    low = (scaled - high.astype(F32)).astype(BF16)
    got = mm_nt(jnp.concatenate([high, low, three_parts(c_o)], axis=0), w[...])
    m, e = got[0:n] + got[n : 2 * n], down(got[2 * n :])
    m_high = m.astype(BF16)
    m_low = (m - m_high.astype(F32)).astype(BF16)
    m = m_high.astype(F32) + m_low.astype(F32)
    same = (marks == label).astype(F32)
    middle = jnp.sum(act_sums * same, axis=0) / count
    spread_out = ((act_sums * (1.0 / pixels) - middle[None]) * same).reshape(-1, n).astype(BF16)
    share = p_rows.shape[1] // 2
    p_rows = p_rows * images[None]
    found = []
    q = join([q_rows[:, h : h + 1, :].reshape(-1, n) for h in (0, 1)])
    away = mm_tn(spread_out, q.astype(BF16))
    q = down(q * join([same.reshape(-1, n)] * 2))
    for h, start in enumerate((shift_i, gain_i)):
        lanes = slice(n * h, n * (h + 1))
        p = p_rows[:, share * h : share * (h + 1), :].reshape(-1, n)[0:n] + away[:, lanes]
        found.append(start + down(m * p) + e * q[:, lanes])
    rstd_i = keeps_i[1:2, :]
    a = rstd_i * gain_of(norm_i, label)
    coefs = a, -(a * rstd_i) * found[1] / count, -a * found[0] / count
    both = join([m_high, m_low])
    line = through(middle, both)
    return both, e - line[:, 0:n] - line[:, n:], coefs, found


def f3(
    tab, got, labels, z_in, norm, w, w_p, xz,
    act, z, send, keeps, keeps_p, slope, q, high, own, both, low, *, share, part,
):
    got_1 = got.at[:, :, 0 : 2 * LANES]
    found = activate_pair(tab, got_1, labels, z_in, norm, act, keeps, slope, both)
    at = expand_pair(found, act, w, z, send, q, high, low, own, share)
    send[:, at : at + 2 * share, :] = low[...]
    put_part(send, at + 2 * share, xz, part)
    marks, label = labels[...], entry(tab, OWN)
    total = group_sum(got, marks, label)
    outer, first = z.shape[2], 2 * LANES
    second = first + w_p.shape[0]
    count = tiled(group_count(marks, label), outer) * (1.0 * z.shape[0] * (COLS - 4))
    mean, rstd = moments(through(total[:, first:second], w_p[...]), total[:, second:], count)
    keeps_p[0:1, :] = mean
    keeps_p[1:2, :] = rstd


def expand_pair(found, act, w, z, send, q, high, low, own, share):
    sums, product, q[...] = found
    pixels = 1.0 * z.shape[0] * (COLS - 4)
    squares = project(act, w, z)
    first = through(sums, w[...])
    second = squares - first * first / pixels
    pair_rows(product, send.shape[0], share, high, low, own)
    put_split(send, 0, sums)
    moved = rows_of(second).astype(BF16)
    send[:, 2 : 2 + moved.shape[0], :] = jnp.broadcast_to(moved[None], (send.shape[0], *moved.shape))
    return 2 + moved.shape[0]


def f4(
    tab, got, labels, zc, zp, norm_c, norm_p, keeps_p, w_c, w, high, q,
    joined, slope, z, send, keeps,
):
    rows, chans = zc.shape[0], zc.shape[2]
    pixels = 1.0 * rows * (COLS - 4)
    mean_c, rstd_c = gathered_moments(got, labels[...], entry(tab, OWN), w_c, pixels)
    mean_p, rstd_p = keeps_p[0:1, :], keeps_p[1:2, :]
    for k, v in enumerate((mean_c, rstd_c, mean_p, rstd_p)):
        keeps[k : k + 1, :] = v
    group = entry(tab, OWN)
    scale_c = rstd_c * gain_of(norm_c, group)
    scale_p = rstd_p * gain_of(norm_p, group)
    bias = (shift_of(norm_c, group) - mean_c * scale_c) + (
        shift_of(norm_p, group) - mean_p * scale_p
    )
    keep = valid_cols(chans)
    scale_c, scale_p, bias = 0.5 * scale_c, 0.5 * scale_p, 0.5 * bias

    def put(i, carry):
        u = zc[i] * scale_c + zp[i] * scale_p + bias
        t = jnp.tanh(u)
        p = u * t
        joined[i] = jnp.where(keep, u + p, 0.0).astype(BF16)
        slope[i] = (0.5 + 0.5 * t) * (1.0 + u - p)
        return carry

    lax.fori_loop(0, rows, put, 0, unroll=4)
    step = rows // 4
    sums, squares = zeros8(LANES), zeros8(LANES)
    for c in range(4):
        values = mm(flat(joined[step * c : step * (c + 1)]), w[...])
        z[step * c : step * (c + 1)] = values.reshape(step, COLS, LANES)
        parts = values.reshape(-1, 8, LANES)
        sums = sums + jnp.sum(parts, axis=0)
        squares = squares + jnp.sum(parts * parts, axis=0)
    put_split(send, 0, stack([down(sums), down(squares)]))
    send[:, 4 : 4 + high.shape[1], :] = high[...]
    put_split(send, 4 + high.shape[1], q[...])


def f5(tab, got, labels, z_in, norm, w_two, w_last, x3, z, send, keeps):
    rows = z_in.shape[0]
    pixels = 1.0 * rows * (COLS - 4)
    marks, label = labels[...], entry(tab, OWN)
    total = over_group(get_split(got, 0, 2), marks, label)
    mean, rstd = moments(total[0:1], total[1:2], group_count(marks, label) * pixels)
    gain, shift = gain_of(norm, label), shift_of(norm, label)
    keeps[0:1, :] = mean
    keeps[1:2, :] = rstd
    scale = rstd * gain
    bias = 0.5 * (shift - mean * scale)
    scale = 0.5 * scale
    keep = valid_cols(LANES) & chan_mask(tab)
    x3[0] = jnp.zeros(x3.shape[1:], BF16)
    x3[rows + 1] = jnp.zeros(x3.shape[1:], BF16)
    n = LANES

    def put(i, carry):
        act = jnp.where(keep, silu_of_half(z_in[i] * scale + bias), 0.0)
        x3[i + 1, :, 0:n] = pltpu.roll(act, 1, 0).astype(BF16)
        x3[i + 1, :, n : 2 * n] = act.astype(BF16)
        x3[i + 1, :, 2 * n : 3 * n] = pltpu.roll(act, COLS - 1, 0).astype(BF16)
        return carry

    lax.fori_loop(0, rows, put, 0, unroll=4)
    lanes = slice(0, 3 * n)
    conv_stats(
        z, x3, (lanes, w_two[...], (0, 1)), (lanes, w_last[...], 2), send
    )


def f6(
    tab, got, labels, z_in, norm, w, xz,
    act, z, send, keeps, slope, q, own, both, high, low, *, share, part,
):
    got_1 = got.at[:, :, 0 : 2 * LANES]
    found = activate_pair(tab, got_1, labels, z_in, norm, act, keeps, slope, both)
    at = expand_pair(found, act, w, z, send, q, high, low, own, share)
    send[:, at : at + 2 * share, :] = high[...]
    send[:, at + 2 * share : at + 4 * share, :] = low[...]
    put_part(send, at + 4 * share, xz, part)


def gathered_moments(got, marks, label, w, pixels):
    devices, chans = got.shape[0], w.shape[1]
    low = stack([got[:, k : k + 1, :].astype(F32).reshape(devices, LANES) for k in (0, 1)])
    means = mm(low.astype(BF16), w[...]) * (1.0 / pixels)
    means = means[0:devices] + means[devices:]
    blocks = chans // LANES
    moments_2 = join(
        [got[:, 2 + k : 3 + k, :].astype(F32).reshape(devices, LANES) for k in range(blocks)]
    )
    same = join([(marks == label).astype(F32).reshape(devices, LANES)] * blocks)
    images = tiled(group_count(marks, label), chans)
    mean = down(means * same) / images
    away = means - mean
    variance = down((moments_2 + pixels * (away * away)) * same) / (images * pixels)
    return mean, lax.rsqrt(variance + EPSILON)


def b7(
    tab, got, labels, joined, z, norm, w, cot, slope_in, z_in, keeps_in, q,
    result, grad_pre, send, keeps, d_in, wide, low, *, share, p_at,
):
    rows, chans = z.shape[0], z.shape[2]
    cols = COLS - 4
    pixels = 1.0 * rows * cols
    marks, label = labels[...], entry(tab, OWN)
    mean, rstd = gathered_moments(got, marks, label, w, pixels)
    gain, shift = gain_of(norm, label), shift_of(norm, label)
    keeps[0:1, :] = mean
    keeps[1:2, :] = rstd
    gate = 0.25 * tiled(entry(tab, GATE), chans)
    scale = 0.5 * rstd * gain * gate
    bias = 0.5 * (shift - mean * rstd * gain) * gate
    wide[...] = jnp.zeros(wide.shape, F32)
    a_gate = rstd * gain * gate

    def put(i, carry):
        sums, products = carry
        wide[0:cols, :] = cot[i].astype(F32)
        zz = z[i]
        u = 0.5 * joined[i].astype(F32) + zz * scale + bias
        t = jnp.tanh(u)
        p = u * t
        result[i] = (u + p)[0:cols].astype(BF16)
        g = wide[...] * ((0.5 + 0.5 * t) * (1.0 + u - p))
        grad_pre[i] = g
        low[i] = (a_gate * g).astype(BF16)
        return sums + fold(g), products + fold(g * (zz - mean))

    start = zeros8(chans)
    sums, products = lax.fori_loop(0, rows, put, (start, start), unroll=4)
    inner = inner_sums(low, w, slope_in, z_in, keeps_in, d_in)
    blocks = chans // LANES
    put_split(send, 0, rows_of(down(sums) * gate))
    put_split(send, 2 * blocks, rows_of(down(products) * rstd * gate))
    put_split(send, 4 * blocks, stack(inner))
    put_split(send, 4 * blocks + 4, q[...])
    high = got[:, p_at : p_at + 2 * share, :]
    low_p = got[:, p_at + 2 * share : p_at + 4 * share, :]
    pass_pair(send, 4 * blocks + 8, high, low_p, marks, norm.shape[0])


def own_coefs(tab, marks, norm, keeps, pixels, shift_sum, gain_sum):
    group = entry(tab, OWN)
    count = tiled(group_count(marks, group), norm.shape[2]) * pixels
    mean, rstd = keeps[0:1, :], keeps[1:2, :]
    a = rstd * gain_of(norm, group)
    return mean, a, -(a * rstd) * gain_sum / count, -a * shift_sum / count


def wide_lines(total, outer):
    side = outer // 2
    return [join([total[h : h + 1, side * k : side * (k + 1)] for h in (0, 1)]) for k in range(3)]


def norm_tail(labels, got_2c, got_2a, got_1, grad_2c, grad_2a, grad_1c, grad_1p):
    marks = labels[...]
    outer = grad_2c.shape[2]
    blocks = outer // LANES
    for g in range(grad_2c.shape[0]):
        label = float(g)
        rows = [
            line_of(over_group(get_split(got_2c, 2 * blocks * k, blocks), marks, label))
            for k in (0, 1)
        ]
        pair = over_group(get_split(got_2a, 0, 2), marks, label)
        lines = wide_lines(group_sum(got_1, marks, label), outer)
        for out, shift_sum, gain_sum in (
            (grad_2c, rows[0], rows[1]),
            (grad_2a, pair[0:1], pair[1:2]),
            (grad_1c, lines[0], lines[1]),
            (grad_1p, lines[0], lines[2]),
        ):
            out[g, 0:1, :] = gain_sum
            out[g, 1:2, :] = shift_sum


def slope_sums(tab, d, z_in, norm, keeps, dout):
    rows = z_in.shape[0]
    mean, rstd = keeps[0:1, :], keeps[1:2, :]
    group = entry(tab, OWN)
    scale = rstd * gain_of(norm, group)
    bias = 0.5 * (shift_of(norm, group) - mean * scale)
    scale = 0.5 * scale
    keep = valid_cols(LANES) & chan_mask(tab)

    def put(i, carry):
        sums, products = carry
        zz = z_in[i]
        g = jnp.where(keep, d[i] * slope_of_half(zz * scale + bias), 0.0)
        dout[i] = g
        return sums + fold(g), products + fold(g * (zz - mean))

    sums, products = lax.fori_loop(
        0, rows, put, (zeros8(LANES), zeros8(LANES)), unroll=4
    )
    return down(sums), down(products) * rstd


def b9(
    tab, got, labels, norm_c, keeps_c, w_c, got_act, act, slope, d_in, z, norm, keeps,
    b_two, b_last, z_in, norm_in, keeps_in, x_sum, pair_high, pair_low, own_p,
    dz, dout, send, own_sums, d3, d, *, share, p_at,
):
    rows = z.shape[0]
    pixels = 1.0 * rows * (COLS - 4)
    marks, label = labels[...], entry(tab, OWN)
    blocks = norm_c.shape[2] // LANES
    at = 4 * blocks
    wide = [
        line_of(over_group(get_split(got, 2 * blocks * k, blocks), marks, label)) for k in (0, 1)
    ]
    inner = over_group(get_split(got, at, 2), marks, label)
    m, line, (a, b, c), found = pair_solve(
        tab, marks, (norm_c, keeps_c), (norm, keeps), [*wide, inner[0:1], inner[1:2]], w_c,
        get_split(got_act, 0, 1), get_split(got, at + 4, 2),
        got[:, at + 8 : at + 8 + 2 * share, :].astype(F32) + own_p[...], pixels,
    )
    own_sums[0:1, :] = found[0]
    own_sums[1:2, :] = found[1]
    inner_part(act, m, d_in, d)
    mean = keeps[0:1, :]
    keep = valid_cols(LANES)
    n = LANES
    d3[0] = jnp.zeros(d3.shape[1:], BF16)
    d3[rows + 1] = jnp.zeros(d3.shape[1:], BF16)

    def put(i, carry):
        v = a * (slope[i] * (d[i] + line)) + b * (z[i] - mean) + c
        v = jnp.where(keep, v, 0.0)
        d3[i + 1, :, 0:n] = pltpu.roll(v, COLS - 1, 0).astype(BF16)
        low = v.astype(BF16)
        d3[i + 1, :, n : 2 * n] = low
        dz[i] = low
        d3[i + 1, :, 2 * n : 3 * n] = pltpu.roll(v, 1, 0).astype(BF16)
        return carry

    lax.fori_loop(0, rows, put, 0, unroll=4)
    step = rows // 4
    for k in range(4):
        both = mm_nt(flat(d3[step * k : step * (k + 1) + 1]), b_two[...])
        value = mm_nt(flat(d3[step * k + 2 : step * (k + 1) + 2]), b_last[...])
        value = value + both[COLS:, 0:n] + both[0 : step * COLS, n : 2 * n]
        d[step * k : step * (k + 1)] = value.reshape(step, COLS, LANES)
    put_split(send, 0, stack(slope_sums(tab, d, z_in, norm_in, keeps_in, dout)))
    blocks = columns(x_sum.shape[0])
    put_split(send, 4, stack([jnp.transpose(x_sum[lanes, :])[0:1] for lanes in blocks]))
    high, low = pair_high[:, 4 : 4 + 2 * share, :], pair_low[:, p_at : p_at + 2 * share, :]
    pass_pair(send, 4 + 2 * len(blocks), high, low, marks, norm.shape[0])


def b10(
    tab, got, labels, dout_in, z, norm, keeps, w, grad_pre, slope, zc, zp, keeps_cp,
    norm_c, w_c, slope_in, z_in, keeps_in,
    dz, grad_pre_2, send, d_in, d, low,
):
    rows, chans = zc.shape[0], zc.shape[2]
    pixels = 1.0 * rows * (COLS - 4)
    marks = labels[...]
    total = over_group(get_split(got, 0, 2), marks, entry(tab, OWN))
    coefs = own_coefs(tab, marks, norm, keeps, pixels, total[0:1], total[1:2])
    normed_grad(dz, dout_in, z, *coefs)
    d[...] = mm_nt(flat(dz[...]), w[...]).reshape(d.shape)
    mean_c, rstd_c, mean_p, rstd_p = (keeps_cp[k : k + 1, :] for k in range(4))
    a_c = rstd_c * gain_of(norm_c, entry(tab, OWN))

    def sum_up(i, carry):
        sums, prod_c, prod_p = carry
        g = (grad_pre[i] + d[i]) * slope[i]
        grad_pre_2[i] = g
        low[i] = (a_c * g).astype(BF16)
        return (
            sums + fold(g),
            prod_c + fold(g * (zc[i] - mean_c)),
            prod_p + fold(g * (zp[i] - mean_p)),
        )

    start = zeros8(chans)
    sums, prod_c, prod_p = lax.fori_loop(0, rows, sum_up, (start, start, start), unroll=4)
    wide = [down(sums), down(prod_c) * rstd_c, down(prod_p) * rstd_p]
    inner = inner_sums(low, w_c, slope_in, z_in, keeps_in, d_in)
    parts = [stack([v[:, 0 : chans // 2], v[:, chans // 2 :]]) for v in wide]
    values = join([*parts, stack(inner)])
    send[...] = jnp.broadcast_to(values[None], send.shape)


def inner_sums(low, w, slope, z, keeps, d_in):
    d_in[...] = mm_nt(flat(low[...]), w[...]).reshape(d_in.shape)
    mean, rstd = keeps[0:1, :], keeps[1:2, :]

    def add(i, carry):
        g = slope[i] * d_in[i]
        return carry[0] + fold(g), carry[1] + fold(g * (z[i] - mean))

    sums = lax.fori_loop(0, z.shape[0], add, (zeros8(LANES), zeros8(LANES)), unroll=7)
    return down(sums[0]), down(sums[1]) * rstd


def inner_part(act, m, d_in, d):
    both = mm(flat(act[...]), m)
    d[...] = d_in[...] + (both[:, 0:LANES] + both[:, LANES:]).reshape(d.shape)


def normed_grad(dz, dout, z, mean, a, b, c):
    keep = valid_cols(z.shape[2])

    def put(i, carry):
        v = a * dout[i] + b * (z[i] - mean) + c
        dz[i] = jnp.where(keep, v, 0.0).astype(BF16)
        return carry

    lax.fori_loop(0, z.shape[0], put, 0, unroll=4)


def b12(
    tab, own10, labels, norm_c, keeps_c, w_c, got_act, got_q, got_p, own_p, act, slope, d_in,
    z, norm, keeps, xs, d2, kept, sent, own_sums, dz, packed, dout, *, share, q_at, p_at,
):
    rows = z.shape[0]
    pixels = 1.0 * rows * (COLS - 4)
    outer, n = norm_c.shape[2], LANES
    marks = labels[...]
    total = own10[...]
    cuts = (0, outer, 2 * outer, 2 * outer + n, 2 * outer + 2 * n)
    m, line, (a, b, c), found = pair_solve(
        tab, marks, (norm_c, keeps_c.at[0:2]), (norm, keeps),
        [total[:, u:v] for u, v in zip(cuts, cuts[1:])], w_c, get_split(got_act, 0, 1),
        get_split(got_q, q_at, 2),
        got_p[:, p_at : p_at + 2 * share, :].astype(F32) + own_p[...], pixels,
    )
    own_sums[0:1, :] = found[0]
    own_sums[1:2, :] = found[1]
    inner_part(act, m, d_in, dout)
    mean = keeps[0:1, :]
    keep = valid_cols(LANES)
    d2[rows] = jnp.zeros(d2.shape[1:], BF16)

    def put(i, carry):
        v = a * (slope[i] * (dout[i] + line)) + b * (z[i] - mean) + c
        v = jnp.where(keep, v, 0.0)
        low = v.astype(BF16)
        dz[i] = low
        d2[i, :, 0:n] = low
        d2[i, :, n : 2 * n] = pltpu.roll(v, COLS - 1, 0).astype(BF16)
        return carry

    lax.fori_loop(0, rows, put, 0, unroll=4)
    low = flat(dz[...])
    cur = mm_side(flat(xs[1 : rows + 1]), low)
    for k, (y, x) in enumerate(((1, 1), (1, 2), (1, 0), (2, 1), (2, 2), (2, 0))):
        put_rows(packed, n * (3 * y + x), cur[n * k : n * (k + 1)])
    up = mm_side(flat(xs[0:rows, :, 3 * n : 6 * n]), low)
    for k, (y, x) in enumerate(((0, 1), (0, 2), (0, 0))):
        put_rows(packed, n * (3 * y + x), up[n * k : n * (k + 1)])
    share_out(tab, packed, 9 * n, kept, sent)


def b12_images(
    tab, d2, b_even, b_odd, zz, norm_in, keeps_in, dn, sums_out, de, do, wide, *, own
):
    rows = de.shape[0]
    n = LANES
    half = half_of(tab)
    first = rows * (half if own else 1 - half)
    step = rows // 2
    for k in range(2):
        here = flat(d2[pl.ds(first + step * k, step)])
        below = flat(d2[pl.ds(first + step * k + 1, step)])
        de[step * k : step * (k + 1)] = mm_nt(here, b_even[...]).reshape(step, COLS, 2 * n)
        odd = mm_nt(here, b_odd[:, 0 : 2 * n]) + mm_nt(below, b_odd[:, 2 * n : 4 * n])
        do[step * k : step * (k + 1)] = odd.reshape(step, COLS, 2 * n)
    mean_1, rstd_1 = keeps_in[0:1, :], keeps_in[1:2, :]
    group = entry(tab, OWN)
    scale = rstd_1 * gain_of(norm_in, group)
    bias = 0.5 * (shift_of(norm_in, group) - mean_1 * scale)
    scale = 0.5 * scale
    keep = valid_cols(LANES) & chan_mask(tab)

    def emit(i, carry):
        sums, products = carry
        for ra in (0, 1):
            planes = (de, do)[ra]
            for cb in (0, 1):
                zv = zz[2 * i + ra, pl.ds(cb, COLS, stride=2), :]
                g = planes[i, :, n * cb : n * (cb + 1)] * slope_of_half(zv * scale + bias)
                g = jnp.where(keep, g, 0.0)
                sums = sums + fold(g)
                products = products + fold(g * (zv - mean_1))
                wide[ra, pl.ds(cb, COLS, stride=2), :] = g
            dn[2 * i + ra] = wide[ra].astype(BF16)
        return sums, products

    totals = lax.fori_loop(0, rows, emit, (zeros8(n), zeros8(n)), unroll=4)
    sums_out[0:1, :] = down(totals[0])
    sums_out[1:2, :] = down(totals[1]) * rstd_1


def b13(
    tab, got, labels, norm, keeps, w, z_own, z_for, dn_own, dn_for, gs_own, gs_for, *rest, at, held
):
    finished, outs = rest[:held], rest[held : 2 * held]
    grad, grad_norm, dz, wide, grad_v, norm_v, sems = rest[2 * held :]
    copies = [
        pltpu.make_async_copy(a, b, sems.at[k]) for k, (a, b) in enumerate(zip(finished, outs))
    ]
    for copy in copies:
        copy.start()
    rows, cols = grad.shape[1], grad.shape[2]
    half = half_of(tab)
    pixels = 2.0 * rows * cols
    marks = labels[...]
    totals = last_sums(got.at[:, at : at + 4, :], marks, norm.shape[0])
    for g in range(norm.shape[0]):
        norm_v[g, 0:1, :] = totals[g][1]
        norm_v[g, 1:2, :] = totals[g][0]
    copies.append(pltpu.make_async_copy(norm_v, grad_norm, sems.at[held]))
    copies[-1].start()
    keep = lax.broadcasted_iota(jnp.int32, (z_own.shape[1], LANES), 0) < cols
    for k, (z, dn, gs) in enumerate(((z_own, dn_own, gs_own), (z_for, dn_for, gs_for))):
        group = entry(tab, OWN if k == 0 else OTHER)
        shift_sum = own_of([t[0] for t in totals], group)
        gain_sum = own_of([t[1] for t in totals], group)
        count = group_count(marks, group) * pixels
        mean, rstd = keeps[2 * k : 2 * k + 1, :], keeps[2 * k + 1 : 2 * k + 2, :]
        a = rstd * gain_of(norm, group)
        b = -(a * rstd) * gain_sum / count
        c = -a * shift_sum / count

        def put(i, carry, z=z, dn=dn, mean=mean, a=a, b=b, c=c):
            v = a * dn[i].astype(F32) + b * (z[i] - mean) + c
            dz[i] = jnp.where(keep, v, 0.0).astype(BF16)
            return carry

        lax.fori_loop(0, rows, put, 0, unroll=4)
        place = half if k == 0 else 1 - half
        step = rows // 2
        for q in range(2):
            low = flat(dz[step * q : step * (q + 1)])
            for p in range(wide.shape[0]):
                values = mm_nt(low, w[LANES * p : LANES * (p + 1), :])
                wide[p, step * q : step * (q + 1)] = values.reshape(step, -1, LANES)

            def emit(i, carry, gs=gs, place=place):
                even = pl.ds(0, COLS, stride=2)
                for p in range(wide.shape[0]):
                    lanes = slice(LANES * p, LANES * (p + 1))
                    wide[p, 2 * i, even, :] = wide[p, 2 * i, even, :] + gs[i, :, lanes].astype(F32)
                    grad_v[place, 2 * i, :, lanes] = wide[p, 2 * i, 0:cols, :].astype(BF16)
                    grad_v[place, 2 * i + 1, :, lanes] = wide[p, 2 * i + 1, 0:cols, :].astype(BF16)
                return carry

            lax.fori_loop(step // 2 * q, step // 2 * (q + 1), emit, 0, unroll=True)
            part = pl.ds(step * q, step)
            copies.append(
                pltpu.make_async_copy(
                    grad_v.at[place, part], grad.at[place, part], sems.at[held + 1 + 2 * k + q]
                )
            )
            copies[-1].start()
    for copy in copies:
        copy.wait()


def put_rows(out, at, value):
    for j in range(value.shape[1] // LANES):
        out[at : at + value.shape[0], :] = value[:, LANES * j : LANES * (j + 1)].astype(BF16)
        at += value.shape[0]
    return at


def take_rows(source, at, out):
    rows = out.shape[0]
    for j in range(out.shape[1] // LANES):
        out[:, LANES * j : LANES * (j + 1)] = source(at, rows)
        at += rows
    return at


def share_out(tab, packed, used, kept, sent):
    if used < packed.shape[0]:
        packed[used:, :] = jnp.zeros((packed.shape[0] - used, LANES), BF16)
    half = half_of(tab)
    size = kept.shape[0] * kept.shape[1]
    for out, place in ((kept, half), (sent, 1 - half)):
        out[...] = packed[pl.ds(pl.multiple_of(size * place, 16), size), :].reshape(out.shape)


def g_most(
    tab, act_2b, x3, dz_2b, joined, dz_2a, act_1b, xee,
    got, labels, norm_c, norm_p, keeps, grad_pre_2, zc, zp,
    got_2c, norm_2c, keeps_2c, grad_pre, z_2c,
    kept, sent, dz_p, own10, packed, dz_1c, dz_2c,
):
    rows, outer = dz_2b.shape[0], zc.shape[2]
    pixels = 1.0 * rows * (COLS - 4)
    marks, label = labels[...], entry(tab, OWN)
    blocks = outer // LANES
    total = group_sum(got, marks, label)
    lines = wide_lines(total, outer)
    for k in range(2):
        own10[:, outer * k : outer * (k + 1)] = lines[k]
        at = 2 * outer + LANES * k
        own10[:, at : at + LANES] = total[k : k + 1, 3 * outer // 2 :]
    wide = [
        line_of(over_group(get_split(got_2c, 2 * blocks * k, blocks), marks, label)) for k in (0, 1)
    ]
    mean, a, b, c = own_coefs(tab, marks, norm_2c, keeps_2c, pixels, *wide)
    gate = 0.25 * tiled(entry(tab, GATE), outer)
    normed_grad(dz_2c, grad_pre, z_2c, mean, a * gate, b, c)
    coefs = own_coefs(tab, marks, norm_c, keeps.at[0:2], pixels, lines[0], lines[1])
    normed_grad(dz_1c, grad_pre_2, zc, *coefs)
    coefs = own_coefs(tab, marks, norm_p, keeps.at[2:4], pixels, lines[0], lines[2])
    normed_grad(dz_p, grad_pre_2, zp, *coefs)
    at = put_rows(packed, 0, mm_tn(flat(act_2b[...]), flat(dz_2c[...])))
    low = flat(dz_2b[...])
    for y in range(3):
        at = put_rows(packed, at, mm_side(flat(x3[y : y + rows]), low))
    at = put_rows(packed, at, mm_side(flat(joined[...]), flat(dz_2a[...])))
    at = put_rows(packed, at, mm_tn(flat(act_1b[...]), flat(dz_1c[...])))
    at = put_rows(packed, at, mm_tn(flat(xee[...]), flat(dz_p[...])))
    share_out(tab, packed, at, kept, sent)


def strided_grad(tab, dz_p, w_p, gs_own, gs_oth):
    half = half_of(tab)
    count = gs_own.shape[0]
    for k, gs in enumerate((gs_own, gs_oth)):
        first = count * (half if k == 0 else 1 - half)
        got = mm_nt(flat(dz_p[pl.ds(first, count)]), w_p[...])
        gs[...] = got.reshape(gs.shape).astype(BF16)


def g_xz(keeps, x_own, x_oth, z_own, z_oth, out, x_sum, low, tall):
    rows, n = z_own.shape[0], LANES
    mean = keeps[0:1, :]
    low[:, :, n : 2 * n] = jnp.ones((rows, z_own.shape[1], n), BF16)
    value = None
    for x, z in ((x_own, z_own), (x_oth, z_oth)):

        def put(i, carry, z=z):
            low[i, :, 0:n] = (z[i] - mean).astype(BF16)
            return carry

        lax.fori_loop(0, rows, put, 0, unroll=4)
        term = mm_tn(flat(x[...]), flat(low[...]))
        value = term if value is None else value + term
    at = value.shape[0]
    tall[0:at, :] = value[:, 0:n]
    if at < tall.shape[0]:
        tall[at:, :] = jnp.zeros((tall.shape[0] - at, n), F32)
    out[...] = tall[...].reshape(out.shape).astype(BF16)
    x_sum[...] = value[:, n : 2 * n]


def g_xd(
    tab, sums_own, sums_oth, norm, keeps, x_sum, got_x, labels, x_own, x_oth, dn_own, dn_oth,
    z_own, z_oth, out, sums, low,
):
    rows = dn_own.shape[0]
    n = LANES
    pixels = 1.0 * (2 * rows) * (2 * (COLS - 4))
    sums[...] = sums_own[...] + sums_oth[...]
    a = keeps[1:2, :] * gain_of(norm, entry(tab, OWN))
    local = sums[0:1, :] / pixels
    mean = keeps[0:1, :]
    b = -(a * keeps[1:2, :]) * sums[1:2, :] / pixels
    value = None
    for x, dn, z in ((x_own, dn_own, z_own), (x_oth, dn_oth, z_oth)):

        def put(i, carry, dn=dn, z=z):
            low[i] = (a * (dn[i].astype(F32) - local) + b * (z[i] - mean)).astype(BF16)
            return carry

        lax.fori_loop(0, rows, put, 0, unroll=4)
        term = mm_tn(flat(low[...]), flat(x[...]))
        value = term if value is None else value + term
    value = stack([jnp.transpose(value[:, lanes]) for lanes in columns(value.shape[1])])
    marks, label = labels[...], entry(tab, OWN)
    total = over_group(get_split(got_x, 4, x_sum.shape[0] // n), marks, label)
    total = join([total[k : k + 1] for k in range(total.shape[0])])
    total = total / tiled(group_count(marks, label), total.shape[1])
    total = jnp.broadcast_to(total, (8, total.shape[1]))
    means = jnp.concatenate(
        [jnp.transpose(total[:, lanes])[:, 0:1] for lanes in columns(total.shape[1])], axis=0
    )
    value = value + (x_sum[...] - means) * (a * local)
    at = value.shape[0]
    out[0:at, :] = value.astype(BF16)
    if at < out.shape[0]:
        out[at:, :] = jnp.zeros((out.shape[0] - at, n), BF16)


def pack_last(tall, sums, kept, got, kept_1b, got_1b, xz, send, *, stats_at, part):
    n = LANES
    devices = send.shape[0]
    piece, share = kept.shape[1], tall.shape[0] // devices
    first = kept.shape[0]
    second = first + kept_1b.shape[0]
    send[0:first, 0:piece, :] = (kept[...].astype(F32) + got[...].astype(F32)).astype(BF16)
    send[first:second, 0:piece, :] = (kept_1b[...].astype(F32) + got_1b[...].astype(F32)).astype(BF16)
    if second < devices:
        send[second:, 0:piece, :] = jnp.zeros((devices - second, piece, n), BF16)
    send[:, piece : piece + share, :] = tall[...].reshape(devices, share, n)
    put_split(send, stats_at, sums[...])
    put_part(send, stats_at + 4, xz, part)


def last_sums(stats, marks, groups):
    values = stats[:, 0:2, :].astype(F32) + stats[:, 2:4, :].astype(F32)
    out = []
    for g in range(groups):
        total = jnp.sum(values * (marks == float(g)).astype(F32), axis=0)
        out.append((total[0:1], total[1:2]))
    return out


def add_all(
    got, labels, norm, keeps_all, got_a, got_b, found_2b, found_1b, out, *, at, pixels, parts
):
    devices, n = got.shape[0], LANES
    half = devices // 2
    share = parts[-1][2]
    piece = (out.shape[1] - share - 8) // 2
    marks = labels[...]
    value = jnp.sum(got[:, piece : piece + share, :].astype(F32), axis=0)
    products = get_split(got, at, 2)[:, 1:2, :]
    lack = jnp.zeros(products.shape, F32)
    for g in range(norm.shape[0]):
        rstd = keeps_all[2 * g + 1 : 2 * g + 2, :]
        factor = -(rstd * rstd * norm[g, 0:1, :]) / pixels
        same = (marks == float(g)).astype(F32)
        middle = jnp.sum(products * same, axis=0) / jnp.sum(same, axis=0)
        lack = lack + (middle[None] - products) * (factor[None] * same)
    rows = [
        jnp.sum(source[:, start : start + last - first, :].astype(F32) * lack, axis=0)
        for source, (start, first, last) in zip((got_a, got_b, got), parts)
        if last > first
    ]
    value = value + jnp.concatenate(rows, axis=0)
    for k in (0, 1):
        total = jnp.sum(got[half * k : half * (k + 1), 0:piece, :].astype(F32), axis=0).astype(BF16)
        out[:, piece * k : piece * (k + 1), :] = jnp.broadcast_to(
            total[None], (out.shape[0], piece, n)
        )
    out[:, 2 * piece : 2 * piece + share, :] = jnp.broadcast_to(
        value.astype(BF16)[None], (out.shape[0], share, n)
    )
    put_split(out, 2 * piece + share, stack([found_2b[...], found_1b[...]]))


def place_parts(minor, parts, packed, tall, found, piece):
    far, share = parts[0].shape[0], tall.shape[1]
    for k, part in enumerate(parts):
        base = lax.bitwise_xor(minor, jnp.int32(k))

        def place(z, carry, part=part, base=base):
            owner = base + NEAR * z
            for h in (0, 1):
                packed[h, owner] = part[z, piece * h : piece * (h + 1), :]
            tall[owner] = part[z, 2 * piece : 2 * piece + share, :].astype(F32)
            sums = part[z, 2 * piece + share :, :].astype(F32)
            found[owner] = sums[0:4] + sums[4:8]
            return carry

        lax.fori_loop(0, far, place, 0, unroll=min(far, 4))


def unpack_own(tab, *refs, piece):
    place_parts(half_of(tab, MINOR), refs[:NEAR], *refs[NEAR:], piece)


def unpack(tab, labels, packed_own, tall_own, found_own, *refs, first, second, piece):
    parts, outs, values = refs[:NEAR], refs[NEAR : NEAR + 9], refs[NEAR + 9 :]
    *values, packed_oth, tall_oth, found_oth, sems = values
    place_parts(half_of(tab, MINOR), parts, packed_oth, tall_oth, found_oth, piece)
    half = half_of(tab)
    copies = [
        pltpu.make_async_copy(value, out, sems.at[k]) for k, (value, out) in enumerate(zip(values, outs))
    ]
    w_1b, w_1a, *grad_norms = values[5:9]
    own, oth = (packed_own, tall_own, found_own), (packed_oth, tall_oth, found_oth)
    for core in (0, 1):

        @pl.when(half == core)
        def _():
            packed, tall, found = zip(*((own, oth) if core == 0 else (oth, own)))
            most, last = [], []
            for h in (0, 1):
                pieces = [flat(v[h]) for v in packed]
                middle = pieces[0].shape[0]
                cut = first * piece
                most.append((pieces, middle))
                last.append((cut, pieces, middle))

            def span(pieces, middle, at, rows):
                found_rows = []
                if at < middle:
                    found_rows.append(pieces[0][at : min(at + rows, middle)])
                if at + rows > middle:
                    found_rows.append(pieces[1][max(at - middle, 0) : at + rows - middle])
                return [v.astype(F32) for v in found_rows]

            size = first * piece

            def source(at, rows):
                out = []
                if at < size:
                    out += span(*most[0], at, min(rows, size - at))
                if at + rows > size:
                    start = max(at - size, 0)
                    out += span(*most[1], start, at + rows - size - start)
                return out[0] if len(out) == 1 else stack(out)

            starts = [0]
            for value in values[0:4]:
                starts.append(starts[-1] + value.shape[0] * value.shape[1] // LANES)
            for k in (1, 4):
                take_rows(source, starts[k], values[k])
                copies[k].start()
            left = w_1b.shape[0]
            for k, (cut, pieces, middle) in enumerate(last):
                rows = min(second * piece, left)
                lines = span(pieces, middle, cut, rows)
                start = second * piece * k
                w_1b[start : start + rows, :] = lines[0] if len(lines) == 1 else stack(lines)
                left -= rows
            copies[5].start()
            for k in (0, 2, 3):
                take_rows(source, starts[k], values[k])
                copies[k].start()
            lines = stack([flat(v[...]) for v in tall])
            w_1a[...] = lines[0 : w_1a.shape[0]]
            copies[6].start()
            sums = jnp.concatenate([v[...] for v in found], axis=0)
            for k, grad_norm in enumerate(grad_norms):
                norm_from_owners(sums[:, 2 * k : 2 * k + 2, :], labels[...], grad_norm)
                copies[7 + k].start()

    for copy in copies:
        copy.wait()


def norm_from_owners(found, marks, grad_norm):
    for g in range(grad_norm.shape[0]):
        total = over_group(found, marks, float(g)) / group_count(marks, float(g))
        grad_norm[g, 0:1, :] = total[1:2]
        grad_norm[g, 1:2, :] = total[0:1]


def gather(send):
    return lax.all_to_all(send, AXES, 0, 0)


def tie(*values):
    return lax.optimization_barrier(values)


def swap(block):
    return lax.ppermute(block, "rows", [(0, 1), (1, 0)])


def body(
    images, w_1a, w_1b, w_1c, w_1p, w_2a, w_2b, w_2c,
    norm_1a, norm_1b, norm_1c, norm_1p, norm_2a, norm_2b, norm_2c,
    cotangent, group, width, gate,
):
    devices = lax.axis_size("rows") * lax.axis_size("batch")
    place = lax.axis_index(AXES).astype(jnp.int32).reshape(1)
    norms = (norm_1a, norm_1b, norm_1c, norm_1p, norm_2a, norm_2b, norm_2c)
    norm_1a, norm_1b, norm_1c, norm_1p, norm_2a, norm_2b, norm_2c = (
        v.transpose(1, 0, 2) for v in norms
    )
    outer, inputs = w_1c.shape[1], w_1a.shape[0]
    rows = cotangent.shape[1]
    cols_in = 2 * COLS
    n, m = LANES, devices

    def send(stats, channels=LANES):
        return ((m, channels // LANES, stats * LANES), F32)

    def maps(channels, dtype=F32):
        return ((rows, COLS, channels), dtype)

    def scratch(channels, dtype=F32):
        return pltpu.VMEM((rows, COLS, channels), dtype)

    def params(*arrays):
        return [(a.shape, F32) for a in arrays]

    def mean_scale(channels, count=1):
        return ((2 * count, channels), F32)

    wide_in = ((rows, cols_in, inputs), BF16)
    wide_z = ((rows, cols_in, n), F32)
    raw = images.shape
    tab, x_own, x_for, z_own, z_for, s1 = stage(
        functools.partial(f1, batch=devices // 2), [((8, n), F32), wide_in, wide_in, wide_z, wide_z, send(5)],
        [*(pltpu.SMEM(v.shape, jnp.int32) for v in (place, group, width, gate)),
         pltpu.VMEM(raw, BF16), pltpu.VMEM(w_1a.shape, BF16), pltpu.VMEM((8, n), F32),
         pltpu.SemaphoreType.DMA((9,))],
        hbm=(0, 1, 2, 3, 4, 5),
    )(place, group, width, gate, images, w_1a)
    s1, v_1b, v_2b = tie(s1, w_1b, w_2b)
    built = stage(
        prepare,
        [(v, BF16) for v in (
            (3 * n, n), (3 * n, 2 * n), (3 * n, 2 * n), (3 * n, n),
            (2 * n, 2 * n), (2 * n, 4 * n), (2 * n, 3 * n), (n, 3 * n),
        )],
    )(v_1b, v_2b)
    s1, x_for, w_even, w_odd, w_two, w_last, b_even, b_odd, b_two, b_last = tie(s1, x_for, *built)
    x_oth = swap(x_for)
    g1 = gather(s1)
    g1, x_oth = tie(g1, x_oth)
    xee, z_1p, stats_1p = stage(
        f1_strided,
        [maps(inputs, BF16), maps(outer), ((1, inputs + outer), F32)],
        [pltpu.VMEM((inputs // n, cols_in, n), F32)],
    )(tab, x_own, x_oth, w_1p)
    xs, z_1b, s2, labels, k_1a, k_all, z_oth = stage(
        f2,
        [((rows + 1, COLS, 6 * n), BF16), maps(n), send(2 + (inputs + outer) // n),
         ((m, 1, n), F32), mean_scale(n, 2), mean_scale(n, norm_1a.shape[0]), wide_z],
    )(tab, g1, z_own, x_oth, w_1a, norm_1a, w_even, w_odd, stats_1p)
    share = -(-inputs // devices)
    half_in = ((rows, cols_in, n), BF16)
    xz, x_sum = stage(
        g_xz, [((devices, share, n), BF16), ((inputs, n), F32)],
        [pltpu.VMEM((rows, cols_in, 2 * n), BF16), pltpu.VMEM((devices * share, n), F32)],
    )(k_1a, x_own, x_oth, z_own, z_oth)
    s2, xz, x_sum = tie(s2, xz, x_sum)
    g2 = gather(s2)
    share_1 = -(-n // devices)
    p_rows = ((devices, 2 * share_1, n), BF16)
    own_rows = ((devices, 2 * share_1, n), F32)
    wide_rows = outer // n
    p_at = 2 + wide_rows
    xz_3 = p_at + 2 * share_1
    high_3 = -(-xz_3 // 16) * 16
    xz_6 = p_at + 4 * share_1
    high_6 = -(-xz_6 // 8) * 8
    cut_3 = min(share, high_3 - xz_3)
    cut_6 = min(share, cut_3 + high_6 - xz_6)
    act_1b, z_1c, s3, k_1b, k_p, slope_1b, q_1b, p_1b, own_1b = stage(
        functools.partial(f3, share=share_1, part=(0, cut_3)),
        [maps(n, BF16), maps(outer), ((devices, high_3, n), BF16), mean_scale(n),
         mean_scale(outer), maps(n), ((2, n), F32), p_rows, own_rows],
        [scratch(4 * n, BF16), pltpu.VMEM(p_rows[0], BF16)],
    )(tab, g2, labels, z_1b, norm_1b, w_1c, w_1p, xz)
    g3 = gather(s3)
    high = -(-(8 + 2 * share_1) // 16) * 16
    joined, slope, z_2a, s4, k_cp = stage(
        f4,
        [maps(outer, BF16), maps(outer), maps(n), ((devices, high, n), BF16),
         mean_scale(outer, 2)],
    )(tab, g3, labels, z_1c, z_1p, norm_1c, norm_1p, k_p, w_1c, w_2a, p_1b, q_1b)
    g4 = gather(s4)
    x3, z_2b, s5, k_2a = stage(
        f5, [((rows + 2, COLS, 3 * n), BF16), maps(n), send(2), mean_scale(n)]
    )(tab, g4, labels, z_2a, norm_2a, w_two, w_last)
    g5 = gather(s5)
    act_2b, z_2c, s6, k_2b, slope_2b, q_2b, own_2b = stage(
        functools.partial(f6, share=share_1, part=(cut_3, cut_6)),
        [maps(n, BF16), maps(outer), ((devices, high_6, n), BF16), mean_scale(n), maps(n),
         ((2, n), F32), own_rows],
        [scratch(4 * n, BF16), *(pltpu.VMEM(p_rows[0], BF16) for _ in range(2))],
    )(tab, g5, labels, z_2b, norm_2b, w_2c, xz)
    g6 = gather(s6)
    high_7 = -(-(4 * wide_rows + 8 + 2 * share_1) // 16) * 16
    result, grad_pre, s7, k_2c, d_2b = stage(
        functools.partial(b7, share=share_1, p_at=p_at),
        [(cotangent.shape[1:], BF16), maps(outer), ((devices, high_7, n), BF16),
         mean_scale(outer), maps(n)],
        [pltpu.VMEM((COLS, outer), F32), scratch(outer, BF16)],
    )(tab, g6, labels, joined, z_2c, norm_2c, w_2c, cotangent[0], slope_2b, z_2b, k_2b, q_2b)
    g7 = gather(s7)
    dz_2b, dout_2a, s9, found_2b = stage(
        functools.partial(b9, share=share_1, p_at=p_at),
        [maps(n, BF16), maps(n), ((devices, high, n), BF16), ((2, n), F32)],
        [pltpu.VMEM((rows + 2, COLS, 3 * n), BF16), scratch(n)],
    )(tab, g7, labels, norm_2c, k_2c, w_2c, g6, act_2b, slope_2b, d_2b, z_2b, norm_2b, k_2b,
      b_two, b_last, z_2a, norm_2a, k_2a, x_sum, g4, g3, own_2b)
    g9 = gather(s9)
    dz_2a, grad_pre_2, s10, d_1b = stage(
        b10,
        [maps(n, BF16), maps(outer), ((devices, 2, 3 * outer // 2 + n), F32), maps(n)],
        [scratch(outer), scratch(outer, BF16)],
    )(tab, g9, labels, dout_2a, z_2a, norm_2a, k_2a, w_2a, grad_pre, slope, z_1c, z_1p, k_cp,
      norm_1c, w_1c, slope_1b, z_1b, k_1b)
    g10 = gather(s10)
    half_map = ((rows // 2, COLS, inputs), BF16)
    most_rows = sum(v.size for v in (w_2c, w_2b, w_2a, w_1c, w_1p)) // n
    rows_1b = w_1b.size // n
    piece = 16
    while -(-most_rows // (2 * piece)) - (-rows_1b // (2 * piece)) > devices:
        piece += 16
    first, second = -(-most_rows // (2 * piece)), -(-rows_1b // (2 * piece))
    part, part_1b = ((first, piece, n), BF16), ((second, piece, n), BF16)
    kept, sent, dz_1p, own10 = stage(
        g_most,
        [part, part, maps(outer, BF16), ((1, 2 * outer + 2 * n), F32)],
        [pltpu.VMEM((2 * first * piece, n), BF16), *(scratch(outer, BF16) for _ in range(2))],
    )(tab, act_2b, x3, dz_2b, joined, dz_2a, act_1b, xee,
      g10, labels, norm_1c, norm_1p, k_cp, grad_pre_2, z_1c, z_1p,
      g7, norm_2c, k_2c, grad_pre, z_2c)
    gs_own, gs_send = stage(strided_grad, [half_map, half_map])(tab, dz_1p, w_1p)
    got, gs_for = swap(sent), swap(gs_send)
    half_in = ((rows, cols_in, n), BF16)
    d2, kept_1b, sent_1b, found_1b = stage(
        functools.partial(b12, share=share_1, q_at=4 + 2 * share_1, p_at=4 + 2 * (inputs // n)),
        [((rows + 1, COLS, 2 * n), BF16), part_1b, part_1b, ((2, n), F32)],
        [scratch(n, BF16), pltpu.VMEM((2 * second * piece, n), BF16), scratch(n)],
    )(tab, own10, labels, norm_1c, k_cp, w_1c, g3, g4, g9, own_1b, act_1b, slope_1b, d_1b,
      z_1b, norm_1b, k_1b, xs)
    got_1b = swap(sent_1b)
    sides = []
    for own, z in ((False, z_oth), (True, z_own)):
        sides.append(
            stage(
                functools.partial(b12_images, own=own), [half_in, ((2, n), F32)],
                [pltpu.VMEM((rows // 2, COLS, 2 * n), F32), pltpu.VMEM((rows // 2, COLS, 2 * n), F32),
                 pltpu.VMEM((2, cols_in, n), F32)],
            )(tab, d2, b_even, b_odd, z, norm_1a, k_1a)
        )
        if not own:
            dn_for = swap(sides[0][0])
            d2, _ = tie(d2, sides[0][0])
    (dn_send, sums_send), (dn_own, sums_own) = sides
    stats_at = piece + -(-share // 8) * 8
    high = -(-(stats_at + 4 + share - cut_6) // 16) * 16
    tall, sums_1a = stage(
        g_xd, [((devices * share, n), BF16), ((2, n), F32)], [pltpu.VMEM(half_in[0], BF16)]
    )(tab, sums_own, sums_send, norm_1a, k_1a, x_sum, g9, labels, x_own, x_oth, dn_own, dn_send,
      z_own, z_oth)
    tall, gs_for, dn_for = tie(tall, gs_for, dn_for)
    (s12,) = stage(
        functools.partial(pack_last, stats_at=stats_at, part=(cut_6, share)),
        [((devices, high, n), BF16)]
    )(tall, sums_1a, kept, got, kept_1b, got_1b, xz)
    g12 = gather(s12)
    pixels = 4.0 * images.shape[1] * images.shape[1]
    batch = devices // 2
    far = batch // NEAR
    (mine,) = stage(
        functools.partial(
            add_all, at=stats_at, pixels=pixels,
            parts=((xz_3, 0, cut_3), (xz_6, cut_3, cut_6), (stats_at + 4, cut_6, share)),
        ),
        [((far, 2 * piece + share + 8, n), BF16)],
    )(g12, labels, norm_1a, k_all, g3, g6, found_2b, found_1b)
    columns_of = [[k + NEAR * z for z in range(far)] for k in range(NEAR)]
    along = lax.all_to_all(mine, "batch", 0, 0, axis_index_groups=columns_of)
    near = [
        lax.ppermute(along, "batch", [(i, i ^ k) for i in range(batch)]) for k in range(1, NEAR)
    ]
    late, _ = tie(labels, along)
    grad_norms = stage(norm_tail, params(norm_2c, norm_2a, norm_1c, norm_1p))(late, g7, g9, g10)
    finished = (result, *grad_norms)
    held = len(finished)
    *finished, grad_images, grad_norm_1a = stage(
        functools.partial(b13, at=stats_at, held=held),
        [*((v.shape, v.dtype) for v in finished), (images.shape, BF16), *params(norm_1a)],
        [pltpu.VMEM(half_in[0], BF16), pltpu.VMEM((inputs // n, rows, cols_in, n), F32),
         pltpu.VMEM(images.shape, BF16), pltpu.VMEM(norm_1a.shape, F32),
         pltpu.SemaphoreType.DMA((held + 5,))],
        hbm_out=range(held + 2),
    )(tab, g12, labels, norm_1a, k_1a, w_1a, z_own, z_for, dn_own, dn_for, gs_own, gs_for, *finished)
    result, grad_norm_2c, grad_norm_2a, grad_norm_1c, grad_norm_1p = finished
    *near, grad_images = tie(*near, grad_images)
    parts = [along, *near]
    weights = (w_2c, w_2b.reshape(-1, n), w_2a, w_1c, w_1p, w_1b.reshape(-1, n), w_1a)
    side = [
        ((2, batch, piece, n), BF16), ((batch, share, n), F32), ((batch, 4, n), F32)
    ]
    crossed = [swap(v) for v in parts]
    placed = stage(functools.partial(unpack_own, piece=piece), side)(tab, *parts)
    t_2c, t_2b, t_2a, t_1c, t_1p, t_1b, t_1a, grad_norm_2b, grad_norm_1b = stage(
        functools.partial(unpack, first=first, second=second, piece=piece),
        [(v.shape, F32) for v in (*weights, norm_2b, norm_1b)],
        [*(pltpu.VMEM(v.shape, F32) for v in (*weights, norm_2b, norm_1b)),
         *(pltpu.VMEM(*v) for v in side), pltpu.SemaphoreType.DMA((9,))],
        hbm_out=range(9),
    )(tab, labels, *placed, *crossed)
    grads = (
        grad_norm_1a, grad_norm_1b, grad_norm_1c, grad_norm_1p,
        grad_norm_2a, grad_norm_2b, grad_norm_2c,
    )
    return (
        result[None], grad_images, t_1a, t_1b.reshape(w_1b.shape), t_1c, t_1p, t_2a,
        t_2b.reshape(w_2b.shape), t_2c, *[v.transpose(1, 0, 2) for v in grads],
    )


def solution(mesh):
    return jax.shard_map(
        body,
        mesh=mesh,
        in_specs=(
            P("batch", "rows", None, None),
            *[P()] * 14,
            P(("batch", "rows"), None, None, None),
            P("batch"),
            P(),
            P(),
        ),
        out_specs=(
            P(("batch", "rows"), None, None, None),
            P("batch", "rows", None, None),
            *[P()] * 14,
        ),
        check_vma=False,
    )
```

```python
import functools

import jax
import jax.numpy as jnp
from jax import lax
from jax.experimental import pallas as pl
from jax.experimental.pallas import tpu as pltpu
from jax.sharding import PartitionSpec as P

EPSILON = 1e-05
F32 = jnp.float32
BF16 = jnp.bfloat16
AXES = ("rows", "batch")
VMEM_LIMIT = 14 * 1024 * 1024
LANES = 128
COLS = 32
NEAR = 4


def full(memory=pltpu.VMEM):
    return pl.BlockSpec(memory_space=memory)


def stage(kernel, outs, scratch=(), hbm=(), hbm_out=()):
    def place(i, outside):
        return pltpu.HBM if i in outside else pltpu.VMEM

    def call(*args):
        args = [
            pltpu.with_memory_space_constraint(a, pltpu.HBM) if i in hbm else a
            for i, a in enumerate(args)
        ]
        return pl.pallas_call(
            kernel,
            out_shape=tuple(jax.ShapeDtypeStruct(s, d) for s, d in outs),
            in_specs=[full(place(i, hbm)) for i in range(len(args))],
            out_specs=tuple(
                full(place(i, hbm_out)) for i in range(len(outs))
            ),
            scratch_shapes=list(scratch),
            compiler_params=pltpu.CompilerParams(vmem_limit_bytes=VMEM_LIMIT),
            name=(kernel.func if isinstance(kernel, functools.partial) else kernel).__name__,
        )(*args)

    return call


def silu_of_half(u):
    return u + u * jnp.tanh(u)


def slope_of_half(u):
    t = jnp.tanh(u)
    return (0.5 + 0.5 * t) * (1.0 + u - u * t)


def fold(x):
    return (x[0:8] + x[8:16]) + (x[16:24] + x[24:32])


def row(total, stat):
    blocks = total.shape[0]
    pieces = [total[j : j + 1, LANES * stat : LANES * (stat + 1)] for j in range(blocks)]
    return pieces[0] if blocks == 1 else jnp.concatenate(pieces, axis=1)


def spread(out_ref, rows):
    blocks = out_ref.shape[1]
    for stat, values in enumerate(rows):
        for j in range(blocks):
            piece = values[:, LANES * j : LANES * (j + 1)]
            out_ref[:, j : j + 1, LANES * stat : LANES * (stat + 1)] = jnp.broadcast_to(
                piece[None], (out_ref.shape[0], 1, LANES)
            )


def group_sum(got_ref, labels, label):
    same = (labels == label).astype(F32)
    stats = got_ref.shape[2] // LANES
    parts = [
        jnp.sum(got_ref[:, :, LANES * s : LANES * (s + 1)] * same, axis=0) for s in range(stats)
    ]
    return jnp.concatenate(parts, axis=1) if stats > 1 else parts[0]


def group_count(labels, label):
    return jnp.sum((labels == label).astype(F32), axis=0)


def tiled(values, channels):
    return jnp.concatenate([values] * (channels // LANES), axis=1) if channels > LANES else values


def moments(first, second, pixels):
    mean = first / pixels
    return mean, lax.rsqrt(second / pixels - mean * mean + EPSILON)


def own_of(values, label):
    out = values[0]
    label = tiled(label, out.shape[1])
    for g in range(1, len(values)):
        out = jnp.where(label == float(g), values[g], out)
    return out


def gain_of(norm_ref, label):
    return own_of([norm_ref[g, 0:1, :] for g in range(norm_ref.shape[0])], label)


def shift_of(norm_ref, label):
    return own_of([norm_ref[g, 1:2, :] for g in range(norm_ref.shape[0])], label)


def valid_cols(channels):
    return lax.broadcasted_iota(jnp.int32, (COLS, channels), 0) < COLS - 4


def chan_mask(tab):
    return lax.broadcasted_iota(jnp.int32, (1, LANES), 1).astype(F32) < entry(tab, LIMIT)


def flat(x):
    return x.reshape(x.shape[0] * x.shape[1], x.shape[2])


def mm(a, b):
    return jnp.dot(a, b, preferred_element_type=F32)


def mm_nt(a, b):
    return lax.dot_general(a, b, (((1,), (1,)), ((), ())), preferred_element_type=F32)


def mm_tn(a, b):
    return lax.dot_general(a, b, (((0,), (0,)), ((), ())), preferred_element_type=F32)


def mm_side(a, b):
    turned = mm_tn(b, a)
    blocks = [
        jnp.transpose(turned[:, LANES * j : LANES * (j + 1)]) for j in range(a.shape[1] // LANES)
    ]
    return blocks[0] if len(blocks) == 1 else jnp.concatenate(blocks, axis=0)


def zeros8(channels):
    return jnp.zeros((8, channels), F32)


def down(x):
    return jnp.sum(x, axis=0, keepdims=True)


OWN, OTHER, HALF, LIMIT, GATE, MINOR = range(6)


def entry(tab, k):
    return tab[k : k + 1, :]


def half_of(tab, k=HALF):
    return (jnp.sum(entry(tab, k)) * (1.0 / LANES)).astype(jnp.int32)


def prepare(w1b, w2b, w_even, w_odd, w_two, w_last, b_even, b_odd, b_two, b_last):
    n = LANES
    for k, (y, x) in enumerate(((1, 1), (1, 2), (1, 0))):
        w_even[n * k : n * (k + 1), :] = w1b[y, x]
    for k, (low, high) in enumerate((((2, 1), (0, 1)), ((2, 2), (0, 2)), ((2, 0), (0, 0)))):
        w_odd[n * k : n * (k + 1), 0:n] = w1b[low]
        w_odd[n * k : n * (k + 1), n : 2 * n] = w1b[high]
    for x in range(3):
        w_two[n * x : n * (x + 1), 0:n] = w2b[0, x]
        w_two[n * x : n * (x + 1), n : 2 * n] = w2b[1, x]
        w_last[n * x : n * (x + 1), :] = w2b[2, x]
        b_two[0:n, n * x : n * (x + 1)] = w2b[1, x]
        b_two[n : 2 * n, n * x : n * (x + 1)] = w2b[2, x]
        b_last[:, n * x : n * (x + 1)] = w2b[0, x]
    nothing = jnp.zeros((n, n), BF16)
    b_even[0:n, 0:n] = w1b[1, 1]
    b_even[0:n, n : 2 * n] = nothing
    b_even[n : 2 * n, 0:n] = w1b[1, 2]
    b_even[n : 2 * n, n : 2 * n] = w1b[1, 0]
    for k, top in ((0, 2), (1, 0)):
        b_odd[0:n, 2 * n * k : 2 * n * k + n] = w1b[top, 1]
        b_odd[0:n, 2 * n * k + n : 2 * n * (k + 1)] = nothing
        b_odd[n : 2 * n, 2 * n * k : 2 * n * k + n] = w1b[top, 2]
        b_odd[n : 2 * n, 2 * n * k + n : 2 * n * (k + 1)] = w1b[top, 0]


def widen(source, x_pad):
    rows, cols, chans = source.shape
    gap = x_pad.shape[1] - cols

    def put(i, carry):
        x_pad[i, 0:cols, :] = source[i]
        x_pad[i, cols : cols + gap, :] = jnp.zeros((gap, chans), BF16)
        return carry

    lax.fori_loop(0, rows, put, 0, unroll=7)


def first_project(x_pad, w, z, stats=True):
    rows = x_pad.shape[0]
    step = rows // 4
    sums, squares = zeros8(LANES), zeros8(LANES)
    for c in range(4):
        values = mm(flat(x_pad[step * c : step * (c + 1)]), w[...])
        z[step * c : step * (c + 1)] = values.reshape(step, x_pad.shape[1], LANES)
        if stats:
            parts = values.reshape(-1, 8, LANES)
            sums = sums + jnp.sum(parts, axis=0)
            squares = squares + jnp.sum(parts * parts, axis=0)
    return sums, squares


def f1(
    place_at, group_at, width_at, gate_at, images, w_at, tab, x_own, x_for, z_own, z_for, send,
    place_ref, group, width, gate, raw, w, found, sems, *, batch,
):
    rows = images.shape[1] // 2
    parts = [pl.ds(rows * p, rows) for p in (0, 1)]
    pairs = (
        (place_at, place_ref), (group_at, group), (width_at, width), (gate_at, gate), (w_at, w),
        *((images.at[k, part], raw.at[k, part]) for k in (0, 1) for part in parts),
    )
    copies = [pltpu.make_async_copy(a, b, sems.at[k]) for k, (a, b) in enumerate(pairs)]
    for k in (0, 5, 4, 6, 7, 8, 1, 2, 3):
        copies[k].start()
    for k in (0, 4):
        copies[k].wait()
    half = lax.div(place_ref[0], batch)
    sides = ((x_own, z_own), (x_for, z_for))

    def one(k):
        for p, part in enumerate(parts):
            copies[5 + 2 * k + p].wait()
            for place in (0, 1):

                @pl.when(half == place)
                def _():
                    x_pad, _ = sides[k] if place == 0 else sides[1 - k]
                    widen(raw.at[k, part], x_pad.at[part])

        for place in (0, 1):

            @pl.when(half == place)
            def _():
                x_pad, z = sides[k] if place == 0 else sides[1 - k]
                sums, squares = first_project(x_pad, w, z)
                at = 2 * (k if place == 0 else 1 - k)
                found[at : at + 1, :] = down(sums)
                found[at + 1 : at + 2, :] = down(squares)

    one(0)
    one(1)
    for k in (1, 2, 3):
        copies[k].wait()
    rows = [found[k : k + 1, :] for k in range(4)]
    own, other = group[half], group[1 - half]
    values = {
        OWN: own, OTHER: other, HALF: half, LIMIT: w.shape[1] // 4 * width[own], GATE: gate[own],
        MINOR: lax.rem(lax.rem(place_ref[0], batch), NEAR),
    }
    tab[...] = jnp.zeros(tab.shape, F32)
    for k, v in values.items():
        tab[k : k + 1, :] = jnp.full((1, LANES), v.astype(F32))
    spread(send, [*rows, jnp.full((1, LANES), (own + 4 * other).astype(F32))])


def f1_strided(tab, x_own, x_oth, w, xee, z, stats, wide):
    half = half_of(tab)
    rows = x_own.shape[0] // 2
    for k, x_pad in enumerate((x_own, x_oth)):
        first = rows * (half if k == 0 else 1 - half)

        def put(i, carry, x_pad=x_pad, first=first):
            for b in range(wide.shape[0]):
                lanes = slice(LANES * b, LANES * (b + 1))
                wide[b] = x_pad[2 * i, :, lanes].astype(F32)
                xee[first + i, :, lanes] = wide[b, pl.ds(0, COLS, stride=2), :].astype(BF16)
            return carry

        lax.fori_loop(0, rows, put, 0, unroll=7)
    total = 2 * rows
    step = total // 7
    chans = z.shape[2]
    squares = zeros8(chans)
    for c in range(7):
        values = mm(flat(xee[step * c : step * (c + 1)]), w[...])
        z[step * c : step * (c + 1)] = values.reshape(step, COLS, chans)
        parts = values.reshape(-1, 8, chans)
        squares = squares + jnp.sum(parts * parts, axis=0)
    ones = jnp.ones((8, total * COLS), BF16)
    stats[:, 0 : w.shape[0]] = mm(ones, flat(xee[...]))[0:1]
    stats[:, w.shape[0] :] = down(squares)


def scale_shift(got, labels, tab, norm, pixels, slot=0):
    label = entry(tab, OWN)
    total = group_sum(got, labels, label)
    chans = norm.shape[2]
    count = tiled(group_count(labels, label), chans) * pixels
    mean, rstd = moments(row(total, 2 * slot), row(total, 2 * slot + 1), count)
    gain, shift = gain_of(norm, entry(tab, OWN)), shift_of(norm, entry(tab, OWN))
    return mean, rstd, gain, shift, count


def conv_stats(z, source, pair, single, send, extra=()):
    keep = valid_cols(LANES)[None]
    rows = z.shape[0]
    step = rows // 4
    (lanes_2, w_2, offsets), (lanes_1, w_1, offset) = pair, single
    sums, squares = zeros8(LANES), zeros8(LANES)
    base = min(offsets)
    for c in range(4):
        at = step * c
        both = mm(flat(source[at + base : at + base + step + 1, :, lanes_2]), w_2)
        values = mm(flat(source[at + offset : at + offset + step, :, lanes_1]), w_1)
        for k, own in enumerate(offsets):
            skip = COLS * (own - base)
            values = values + both[skip : skip + step * COLS, LANES * k : LANES * (k + 1)]
        values = jnp.where(keep, values.reshape(step, COLS, LANES), 0.0)
        z[at : at + step] = values
        parts = values.reshape(-1, 8, LANES)
        sums = sums + jnp.sum(parts, axis=0)
        squares = squares + jnp.sum(parts * parts, axis=0)
    spread(send, [down(sums), down(squares), *extra])


def f2(
    tab, got, z_own, x_oth, w, norm, w_even, w_odd, stats_p,
    xs, z, send, labels, keeps, keeps_all, z_oth,
):
    codes = got[:, :, 4 * LANES : 5 * LANES]
    others = jnp.floor(0.25 * codes)
    marks = codes - 4.0 * others
    labels[...] = marks
    rows = xs.shape[0] - 1
    pixels = 4.0 * rows * (COLS - 4)
    first_project(x_oth, w, z_oth, False)
    for g in range(norm.shape[0]):
        mine, theirs = (marks == float(g)).astype(F32), (others == float(g)).astype(F32)
        totals = [
            jnp.sum(
                got[:, :, LANES * s : LANES * (s + 1)] * mine
                + got[:, :, LANES * (s + 2) : LANES * (s + 3)] * theirs,
                axis=0,
            )
            for s in (0, 1)
        ]
        mean, rstd = moments(*totals, group_count(marks, float(g)) * pixels)
        keeps_all[2 * g : 2 * g + 1, :] = mean
        keeps_all[2 * g + 1 : 2 * g + 2, :] = rstd
    for k, slot in enumerate((OWN, OTHER)):
        for q in (0, 1):
            choices = [keeps_all[2 * g + q : 2 * g + q + 1, :] for g in range(norm.shape[0])]
            keeps[2 * k + q : 2 * k + q + 1, :] = own_of(choices, entry(tab, slot))
    mean, rstd = keeps[0:1, :], keeps[1:2, :]
    gain, shift = gain_of(norm, entry(tab, OWN)), shift_of(norm, entry(tab, OWN))
    scale = rstd * gain
    bias = 0.5 * (shift - mean * scale)
    scale = 0.5 * scale
    keep = valid_cols(LANES) & chan_mask(tab)
    half = half_of(tab)
    xs[0] = jnp.zeros(xs.shape[1:], BF16)
    n = LANES
    for k, zz in enumerate((z_own, z_oth)):
        first = 1 + (rows // 2) * (half if k == 0 else 1 - half)

        def put(i, carry, zz=zz, first=first):
            lane = 0
            for a in (0, 1):
                for b in (0, 1):
                    u = zz[2 * i + a, pl.ds(b, COLS, stride=2), :] * scale + bias
                    act = jnp.where(keep, silu_of_half(u), 0.0)
                    xs[first + i, :, lane : lane + n] = act.astype(BF16)
                    lane += n
                    if b == 1:
                        moved = pltpu.roll(act, 1, 0)
                        xs[first + i, :, lane : lane + n] = moved.astype(BF16)
                        lane += n
            return carry

        lax.fori_loop(0, rows // 2, put, 0, unroll=7)
    extra = [stats_p[:, lanes] for lanes in columns(stats_p.shape[1])]
    pair = (slice(3 * n, 6 * n), w_odd[...], (1, 0))
    conv_stats(z, xs, pair, (slice(0, 3 * n), w_even[...], 1), send, extra)


def project(act, w, z):
    rows, chans = z.shape[0], z.shape[2]
    step = rows // 7
    squares = zeros8(chans)
    for c in range(7):
        values = mm(flat(act[step * c : step * (c + 1)]), w[...])
        z[step * c : step * (c + 1)] = values.reshape(step, COLS, chans)
        parts = values.reshape(-1, 8, chans)
        squares = squares + jnp.sum(parts * parts, axis=0)
    return down(squares)


def join(pieces):
    return pieces[0] if len(pieces) == 1 else jnp.concatenate(pieces, axis=1)


def columns(channels):
    return [slice(LANES * j, LANES * (j + 1)) for j in range(channels // LANES)]


def three_parts(sums):
    high = sums.astype(BF16)
    rest = sums - high.astype(F32)
    mid = rest.astype(BF16)
    low = (rest - mid.astype(F32)).astype(BF16)
    lines = [v.astype(F32) for v in (high, mid, low)]
    lines.append(jnp.zeros((13, sums.shape[1]), F32))
    return jnp.concatenate(lines, axis=0).astype(BF16)


def through(sums, w):
    return down(mm(three_parts(sums), w))


def put_split(send, at, values):
    rows = values.shape[0]
    high = values.astype(BF16)
    rest = (values - high.astype(F32)).astype(BF16)
    for k, part in enumerate((high, rest)):
        send[:, at + rows * k : at + rows * (k + 1), :] = jnp.broadcast_to(
            part[None], (send.shape[0], rows, LANES)
        )


def get_split(got, at, rows):
    return got[:, at : at + rows, :].astype(F32) + got[:, at + rows : at + 2 * rows, :].astype(F32)


def over_group(values, marks, label):
    return jnp.sum(values * (marks == label).astype(F32), axis=0)


def stack(rows):
    return jnp.concatenate(rows, axis=0)


def activate_pair(tab, got, labels, z, norm, act, keeps, slope, both):
    rows = z.shape[0]
    pixels = 1.0 * rows * (COLS - 4)
    mean, rstd, gain, shift, _ = scale_shift(got, labels[...], tab, norm, pixels)
    keeps[0:1, :] = mean
    keeps[1:2, :] = rstd
    scale = rstd * gain
    bias = 0.5 * (shift - mean * scale)
    scale = 0.5 * scale
    keep = valid_cols(LANES) & chan_mask(tab)

    def put(i, carry):
        zz = z[i]
        u = zz * scale + bias
        t = jnp.tanh(u)
        p = u * t
        low = jnp.where(keep, u + p, 0.0).astype(BF16)
        act[i] = low
        s = jnp.where(keep, (0.5 + 0.5 * t) * (1.0 + u - p), 0.0)
        sx = s * ((zz - mean) * rstd)
        slope[i] = s
        for k, v in enumerate((s, sx)):
            high = v.astype(BF16)
            both[i, :, LANES * k : LANES * (k + 1)] = high
            both[i, :, LANES * (k + 2) : LANES * (k + 3)] = (v - high.astype(F32)).astype(BF16)
        return carry[0] + fold(low.astype(F32)), carry[1] + fold(s), carry[2] + fold(sx)

    start = zeros8(LANES)
    sums = lax.fori_loop(0, rows, put, (start, start, start), unroll=7)
    act_sum, *sums = [down(v) for v in sums]
    product = mm_tn(flat(act[...]), flat(both[...]))
    product = product[:, 0 : 2 * LANES] + product[:, 2 * LANES :]
    middle = jnp.broadcast_to(act_sum * (1.0 / pixels), (8, LANES))
    return act_sum, product - jnp.transpose(middle)[:, 0:1] * join(sums), stack(sums)


def rows_of(line):
    return stack([line[:, lanes] for lanes in columns(line.shape[1])])


def line_of(rows):
    return join([rows[k : k + 1, :] for k in range(rows.shape[0])])


def put_part(send, at, rows, part):
    first, last = part
    if last > first:
        send[:, at : at + last - first, :] = rows[:, first:last, :]


def pair_rows(product, devices, share, high, low, own):
    n = LANES
    missing = devices * share - n
    for h in (0, 1):
        values = product[:, n * h : n * (h + 1)]
        if missing:
            values = stack([values, jnp.zeros((missing, n), F32)])
        values = values.reshape(devices, share, n)
        first, last = share * h, share * (h + 1)
        top = values.astype(BF16)
        rest = (values - top.astype(F32)).astype(BF16)
        high[:, first:last, :] = top
        low[:, first:last, :] = rest
        own[:, first:last, :] = top.astype(F32) + rest.astype(F32)


def pass_pair(send, at, high, low, marks, groups):
    rows = high.astype(F32) + low.astype(F32)
    out = -rows
    for g in range(groups):
        same = (marks == float(g)).astype(F32)
        images = jnp.maximum(jnp.sum(same, axis=0), 1.0)
        out = out + (jnp.sum(rows * same, axis=0) / images)[None] * same
    send[:, at : at + rows.shape[1], :] = out.astype(BF16)


def pair_solve(tab, marks, outer, inner, sums, w, act_sums, q_rows, p_rows, pixels):
    label, n = entry(tab, OWN), LANES
    (norm_o, keeps_o), (norm_i, keeps_i) = outer, inner
    shift_o, gain_o, shift_i, gain_i = sums
    images = group_count(marks, label)
    count, count_o = images * pixels, tiled(images, norm_o.shape[2]) * pixels
    rstd_o = keeps_o[1:2, :]
    a_o = rstd_o * gain_of(norm_o, label)
    b_o, c_o = -(a_o * rstd_o) * gain_o / count_o, -a_o * shift_o / count_o
    scaled = w[...].astype(F32) * b_o
    high = scaled.astype(BF16)
    low = (scaled - high.astype(F32)).astype(BF16)
    got = mm_nt(jnp.concatenate([high, low, three_parts(c_o)], axis=0), w[...])
    m, e = got[0:n] + got[n : 2 * n], down(got[2 * n :])
    m_high = m.astype(BF16)
    m_low = (m - m_high.astype(F32)).astype(BF16)
    m = m_high.astype(F32) + m_low.astype(F32)
    same = (marks == label).astype(F32)
    middle = jnp.sum(act_sums * same, axis=0) / count
    spread_out = ((act_sums * (1.0 / pixels) - middle[None]) * same).reshape(-1, n).astype(BF16)
    share = p_rows.shape[1] // 2
    p_rows = p_rows * images[None]
    found = []
    q = join([q_rows[:, h : h + 1, :].reshape(-1, n) for h in (0, 1)])
    away = mm_tn(spread_out, q.astype(BF16))
    q = down(q * join([same.reshape(-1, n)] * 2))
    for h, start in enumerate((shift_i, gain_i)):
        lanes = slice(n * h, n * (h + 1))
        p = p_rows[:, share * h : share * (h + 1), :].reshape(-1, n)[0:n] + away[:, lanes]
        found.append(start + down(m * p) + e * q[:, lanes])
    rstd_i = keeps_i[1:2, :]
    a = rstd_i * gain_of(norm_i, label)
    coefs = a, -(a * rstd_i) * found[1] / count, -a * found[0] / count
    both = join([m_high, m_low])
    line = through(middle, both)
    return both, e - line[:, 0:n] - line[:, n:], coefs, found


def f3(
    tab, got, labels, z_in, norm, w, w_p, xz,
    act, z, send, keeps, keeps_p, slope, q, high, own, both, low, *, share, part,
):
    got_1 = got.at[:, :, 0 : 2 * LANES]
    found = activate_pair(tab, got_1, labels, z_in, norm, act, keeps, slope, both)
    at = expand_pair(found, act, w, z, send, q, high, low, own, share)
    send[:, at : at + 2 * share, :] = low[...]
    put_part(send, at + 2 * share, xz, part)
    marks, label = labels[...], entry(tab, OWN)
    total = group_sum(got, marks, label)
    outer, first = z.shape[2], 2 * LANES
    second = first + w_p.shape[0]
    count = tiled(group_count(marks, label), outer) * (1.0 * z.shape[0] * (COLS - 4))
    mean, rstd = moments(through(total[:, first:second], w_p[...]), total[:, second:], count)
    keeps_p[0:1, :] = mean
    keeps_p[1:2, :] = rstd


def expand_pair(found, act, w, z, send, q, high, low, own, share):
    sums, product, q[...] = found
    pixels = 1.0 * z.shape[0] * (COLS - 4)
    squares = project(act, w, z)
    first = through(sums, w[...])
    second = squares - first * first / pixels
    pair_rows(product, send.shape[0], share, high, low, own)
    put_split(send, 0, sums)
    moved = rows_of(second).astype(BF16)
    send[:, 2 : 2 + moved.shape[0], :] = jnp.broadcast_to(moved[None], (send.shape[0], *moved.shape))
    return 2 + moved.shape[0]


def f4(
    tab, got, labels, zc, zp, norm_c, norm_p, keeps_p, w_c, w, high, q,
    joined, slope, z, send, keeps,
):
    rows, chans = zc.shape[0], zc.shape[2]
    pixels = 1.0 * rows * (COLS - 4)
    mean_c, rstd_c = gathered_moments(got, labels[...], entry(tab, OWN), w_c, pixels)
    mean_p, rstd_p = keeps_p[0:1, :], keeps_p[1:2, :]
    for k, v in enumerate((mean_c, rstd_c, mean_p, rstd_p)):
        keeps[k : k + 1, :] = v
    group = entry(tab, OWN)
    scale_c = rstd_c * gain_of(norm_c, group)
    scale_p = rstd_p * gain_of(norm_p, group)
    bias = (shift_of(norm_c, group) - mean_c * scale_c) + (
        shift_of(norm_p, group) - mean_p * scale_p
    )
    keep = valid_cols(chans)
    scale_c, scale_p, bias = 0.5 * scale_c, 0.5 * scale_p, 0.5 * bias

    def put(i, carry):
        u = zc[i] * scale_c + zp[i] * scale_p + bias
        t = jnp.tanh(u)
        p = u * t
        joined[i] = jnp.where(keep, u + p, 0.0).astype(BF16)
        slope[i] = (0.5 + 0.5 * t) * (1.0 + u - p)
        return carry

    lax.fori_loop(0, rows, put, 0, unroll=7)
    step = rows // 4
    sums, squares = zeros8(LANES), zeros8(LANES)
    for c in range(4):
        values = mm(flat(joined[step * c : step * (c + 1)]), w[...])
        z[step * c : step * (c + 1)] = values.reshape(step, COLS, LANES)
        parts = values.reshape(-1, 8, LANES)
        sums = sums + jnp.sum(parts, axis=0)
        squares = squares + jnp.sum(parts * parts, axis=0)
    put_split(send, 0, stack([down(sums), down(squares)]))
    send[:, 4 : 4 + high.shape[1], :] = high[...]
    put_split(send, 4 + high.shape[1], q[...])


def f5(tab, got, labels, z_in, norm, w_two, w_last, x3, z, send, keeps):
    rows = z_in.shape[0]
    pixels = 1.0 * rows * (COLS - 4)
    marks, label = labels[...], entry(tab, OWN)
    total = over_group(get_split(got, 0, 2), marks, label)
    mean, rstd = moments(total[0:1], total[1:2], group_count(marks, label) * pixels)
    gain, shift = gain_of(norm, label), shift_of(norm, label)
    keeps[0:1, :] = mean
    keeps[1:2, :] = rstd
    scale = rstd * gain
    bias = 0.5 * (shift - mean * scale)
    scale = 0.5 * scale
    keep = valid_cols(LANES) & chan_mask(tab)
    x3[0] = jnp.zeros(x3.shape[1:], BF16)
    x3[rows + 1] = jnp.zeros(x3.shape[1:], BF16)
    n = LANES

    def put(i, carry):
        act = jnp.where(keep, silu_of_half(z_in[i] * scale + bias), 0.0)
        x3[i + 1, :, 0:n] = pltpu.roll(act, 1, 0).astype(BF16)
        x3[i + 1, :, n : 2 * n] = act.astype(BF16)
        x3[i + 1, :, 2 * n : 3 * n] = pltpu.roll(act, COLS - 1, 0).astype(BF16)
        return carry

    lax.fori_loop(0, rows, put, 0, unroll=7)
    lanes = slice(0, 3 * n)
    conv_stats(
        z, x3, (lanes, w_two[...], (0, 1)), (lanes, w_last[...], 2), send
    )


def f6(
    tab, got, labels, z_in, norm, w, xz,
    act, z, send, keeps, slope, q, own, both, high, low, *, share, part,
):
    got_1 = got.at[:, :, 0 : 2 * LANES]
    found = activate_pair(tab, got_1, labels, z_in, norm, act, keeps, slope, both)
    at = expand_pair(found, act, w, z, send, q, high, low, own, share)
    send[:, at : at + 2 * share, :] = high[...]
    send[:, at + 2 * share : at + 4 * share, :] = low[...]
    put_part(send, at + 4 * share, xz, part)


def gathered_moments(got, marks, label, w, pixels):
    devices, chans = got.shape[0], w.shape[1]
    low = stack([got[:, k : k + 1, :].astype(F32).reshape(devices, LANES) for k in (0, 1)])
    means = mm(low.astype(BF16), w[...]) * (1.0 / pixels)
    means = means[0:devices] + means[devices:]
    blocks = chans // LANES
    moments_2 = join(
        [got[:, 2 + k : 3 + k, :].astype(F32).reshape(devices, LANES) for k in range(blocks)]
    )
    same = join([(marks == label).astype(F32).reshape(devices, LANES)] * blocks)
    images = tiled(group_count(marks, label), chans)
    mean = down(means * same) / images
    away = means - mean
    variance = down((moments_2 + pixels * (away * away)) * same) / (images * pixels)
    return mean, lax.rsqrt(variance + EPSILON)


def b7(
    tab, got, labels, joined, z, norm, w, cot, slope_in, z_in, keeps_in, q,
    result, grad_pre, send, keeps, d_in, wide, low, *, share, p_at,
):
    rows, chans = z.shape[0], z.shape[2]
    cols = COLS - 4
    pixels = 1.0 * rows * cols
    marks, label = labels[...], entry(tab, OWN)
    mean, rstd = gathered_moments(got, marks, label, w, pixels)
    gain, shift = gain_of(norm, label), shift_of(norm, label)
    keeps[0:1, :] = mean
    keeps[1:2, :] = rstd
    gate = 0.25 * tiled(entry(tab, GATE), chans)
    scale = 0.5 * rstd * gain * gate
    bias = 0.5 * (shift - mean * rstd * gain) * gate
    wide[...] = jnp.zeros(wide.shape, F32)
    a_gate = rstd * gain * gate

    def put(i, carry):
        sums, products = carry
        wide[0:cols, :] = cot[i].astype(F32)
        zz = z[i]
        u = 0.5 * joined[i].astype(F32) + zz * scale + bias
        t = jnp.tanh(u)
        p = u * t
        result[i] = (u + p)[0:cols].astype(BF16)
        g = wide[...] * ((0.5 + 0.5 * t) * (1.0 + u - p))
        grad_pre[i] = g
        low[i] = (a_gate * g).astype(BF16)
        return sums + fold(g), products + fold(g * (zz - mean))

    start = zeros8(chans)
    sums, products = lax.fori_loop(0, rows, put, (start, start), unroll=7)
    inner = inner_sums(low, w, slope_in, z_in, keeps_in, d_in)
    blocks = chans // LANES
    put_split(send, 0, rows_of(down(sums) * gate))
    put_split(send, 2 * blocks, rows_of(down(products) * rstd * gate))
    put_split(send, 4 * blocks, stack(inner))
    put_split(send, 4 * blocks + 4, q[...])
    high = got[:, p_at : p_at + 2 * share, :]
    low_p = got[:, p_at + 2 * share : p_at + 4 * share, :]
    pass_pair(send, 4 * blocks + 8, high, low_p, marks, norm.shape[0])


def own_coefs(tab, marks, norm, keeps, pixels, shift_sum, gain_sum):
    group = entry(tab, OWN)
    count = tiled(group_count(marks, group), norm.shape[2]) * pixels
    mean, rstd = keeps[0:1, :], keeps[1:2, :]
    a = rstd * gain_of(norm, group)
    return mean, a, -(a * rstd) * gain_sum / count, -a * shift_sum / count


def wide_lines(total, outer):
    side = outer // 2
    return [join([total[h : h + 1, side * k : side * (k + 1)] for h in (0, 1)]) for k in range(3)]


def norm_tail(labels, got_2c, got_2a, got_1, grad_2c, grad_2a, grad_1c, grad_1p):
    marks = labels[...]
    outer = grad_2c.shape[2]
    blocks = outer // LANES
    for g in range(grad_2c.shape[0]):
        label = float(g)
        rows = [
            line_of(over_group(get_split(got_2c, 2 * blocks * k, blocks), marks, label))
            for k in (0, 1)
        ]
        pair = over_group(get_split(got_2a, 0, 2), marks, label)
        lines = wide_lines(group_sum(got_1, marks, label), outer)
        for out, shift_sum, gain_sum in (
            (grad_2c, rows[0], rows[1]),
            (grad_2a, pair[0:1], pair[1:2]),
            (grad_1c, lines[0], lines[1]),
            (grad_1p, lines[0], lines[2]),
        ):
            out[g, 0:1, :] = gain_sum
            out[g, 1:2, :] = shift_sum


def slope_sums(tab, d, z_in, norm, keeps, dout):
    rows = z_in.shape[0]
    mean, rstd = keeps[0:1, :], keeps[1:2, :]
    group = entry(tab, OWN)
    scale = rstd * gain_of(norm, group)
    bias = 0.5 * (shift_of(norm, group) - mean * scale)
    scale = 0.5 * scale
    keep = valid_cols(LANES) & chan_mask(tab)

    def put(i, carry):
        sums, products = carry
        zz = z_in[i]
        g = jnp.where(keep, d[i] * slope_of_half(zz * scale + bias), 0.0)
        dout[i] = g
        return sums + fold(g), products + fold(g * (zz - mean))

    sums, products = lax.fori_loop(
        0, rows, put, (zeros8(LANES), zeros8(LANES)), unroll=4
    )
    return down(sums), down(products) * rstd


def b9(
    tab, got, labels, norm_c, keeps_c, w_c, got_act, act, slope, d_in, z, norm, keeps,
    b_two, b_last, z_in, norm_in, keeps_in, x_sum, pair_high, pair_low, own_p,
    dz, dout, send, own_sums, d3, d, *, share, p_at,
):
    rows = z.shape[0]
    pixels = 1.0 * rows * (COLS - 4)
    marks, label = labels[...], entry(tab, OWN)
    blocks = norm_c.shape[2] // LANES
    at = 4 * blocks
    wide = [
        line_of(over_group(get_split(got, 2 * blocks * k, blocks), marks, label)) for k in (0, 1)
    ]
    inner = over_group(get_split(got, at, 2), marks, label)
    m, line, (a, b, c), found = pair_solve(
        tab, marks, (norm_c, keeps_c), (norm, keeps), [*wide, inner[0:1], inner[1:2]], w_c,
        get_split(got_act, 0, 1), get_split(got, at + 4, 2),
        got[:, at + 8 : at + 8 + 2 * share, :].astype(F32) + own_p[...], pixels,
    )
    own_sums[0:1, :] = found[0]
    own_sums[1:2, :] = found[1]
    inner_part(act, m, d_in, d)
    mean = keeps[0:1, :]
    keep = valid_cols(LANES)
    n = LANES
    d3[0] = jnp.zeros(d3.shape[1:], BF16)
    d3[rows + 1] = jnp.zeros(d3.shape[1:], BF16)

    def put(i, carry):
        v = a * (slope[i] * (d[i] + line)) + b * (z[i] - mean) + c
        v = jnp.where(keep, v, 0.0)
        d3[i + 1, :, 0:n] = pltpu.roll(v, COLS - 1, 0).astype(BF16)
        low = v.astype(BF16)
        d3[i + 1, :, n : 2 * n] = low
        dz[i] = low
        d3[i + 1, :, 2 * n : 3 * n] = pltpu.roll(v, 1, 0).astype(BF16)
        return carry

    lax.fori_loop(0, rows, put, 0, unroll=7)
    step = rows // 4
    for k in range(4):
        both = mm_nt(flat(d3[step * k : step * (k + 1) + 1]), b_two[...])
        value = mm_nt(flat(d3[step * k + 2 : step * (k + 1) + 2]), b_last[...])
        value = value + both[COLS:, 0:n] + both[0 : step * COLS, n : 2 * n]
        d[step * k : step * (k + 1)] = value.reshape(step, COLS, LANES)
    put_split(send, 0, stack(slope_sums(tab, d, z_in, norm_in, keeps_in, dout)))
    blocks = columns(x_sum.shape[0])
    put_split(send, 4, stack([jnp.transpose(x_sum[lanes, :])[0:1] for lanes in blocks]))
    high, low = pair_high[:, 4 : 4 + 2 * share, :], pair_low[:, p_at : p_at + 2 * share, :]
    pass_pair(send, 4 + 2 * len(blocks), high, low, marks, norm.shape[0])


def b10(
    tab, got, labels, dout_in, z, norm, keeps, w, grad_pre, slope, zc, zp, keeps_cp,
    norm_c, w_c, slope_in, z_in, keeps_in,
    dz, grad_pre_2, send, d_in, d, low,
):
    rows, chans = zc.shape[0], zc.shape[2]
    pixels = 1.0 * rows * (COLS - 4)
    marks = labels[...]
    total = over_group(get_split(got, 0, 2), marks, entry(tab, OWN))
    coefs = own_coefs(tab, marks, norm, keeps, pixels, total[0:1], total[1:2])
    normed_grad(dout_in, (dz, z, *coefs))
    d[...] = mm_nt(flat(dz[...]), w[...]).reshape(d.shape)
    mean_c, rstd_c, mean_p, rstd_p = (keeps_cp[k : k + 1, :] for k in range(4))
    a_c = rstd_c * gain_of(norm_c, entry(tab, OWN))

    def sum_up(i, carry):
        sums, prod_c, prod_p = carry
        g = (grad_pre[i] + d[i]) * slope[i]
        grad_pre_2[i] = g
        low[i] = (a_c * g).astype(BF16)
        return (
            sums + fold(g),
            prod_c + fold(g * (zc[i] - mean_c)),
            prod_p + fold(g * (zp[i] - mean_p)),
        )

    start = zeros8(chans)
    sums, prod_c, prod_p = lax.fori_loop(0, rows, sum_up, (start, start, start), unroll=7)
    wide = [down(sums), down(prod_c) * rstd_c, down(prod_p) * rstd_p]
    inner = inner_sums(low, w_c, slope_in, z_in, keeps_in, d_in)
    parts = [stack([v[:, 0 : chans // 2], v[:, chans // 2 :]]) for v in wide]
    values = join([*parts, stack(inner)])
    send[...] = jnp.broadcast_to(values[None], send.shape)


def inner_sums(low, w, slope, z, keeps, d_in):
    d_in[...] = mm_nt(flat(low[...]), w[...]).reshape(d_in.shape)
    mean, rstd = keeps[0:1, :], keeps[1:2, :]

    def add(i, carry):
        g = slope[i] * d_in[i]
        return carry[0] + fold(g), carry[1] + fold(g * (z[i] - mean))

    sums = lax.fori_loop(0, z.shape[0], add, (zeros8(LANES), zeros8(LANES)), unroll=7)
    return down(sums[0]), down(sums[1]) * rstd


def inner_part(act, m, d_in, d):
    both = mm(flat(act[...]), m)
    d[...] = d_in[...] + (both[:, 0:LANES] + both[:, LANES:]).reshape(d.shape)


def normed_grad(dout, *parts):
    keep = valid_cols(dout.shape[2])

    def put(i, carry):
        g = dout[i]
        for dz, z, mean, a, b, c in parts:
            v = a * g + b * (z[i] - mean) + c
            dz[i] = jnp.where(keep, v, 0.0).astype(BF16)
        return carry

    lax.fori_loop(0, dout.shape[0], put, 0, unroll=7)


def b12(
    tab, own10, labels, norm_c, keeps_c, w_c, got_act, got_q, got_p, own_p, act, slope, d_in,
    z, norm, keeps, xs, d2, kept, sent, own_sums, dz, packed, dout, *, share, q_at, p_at,
):
    rows = z.shape[0]
    pixels = 1.0 * rows * (COLS - 4)
    outer, n = norm_c.shape[2], LANES
    marks = labels[...]
    total = own10[...]
    cuts = (0, outer, 2 * outer, 2 * outer + n, 2 * outer + 2 * n)
    m, line, (a, b, c), found = pair_solve(
        tab, marks, (norm_c, keeps_c.at[0:2]), (norm, keeps),
        [total[:, u:v] for u, v in zip(cuts, cuts[1:])], w_c, get_split(got_act, 0, 1),
        get_split(got_q, q_at, 2),
        got_p[:, p_at : p_at + 2 * share, :].astype(F32) + own_p[...], pixels,
    )
    own_sums[0:1, :] = found[0]
    own_sums[1:2, :] = found[1]
    inner_part(act, m, d_in, dout)
    mean = keeps[0:1, :]
    keep = valid_cols(LANES)
    d2[rows] = jnp.zeros(d2.shape[1:], BF16)

    def put(i, carry):
        v = a * (slope[i] * (dout[i] + line)) + b * (z[i] - mean) + c
        v = jnp.where(keep, v, 0.0)
        low = v.astype(BF16)
        dz[i] = low
        d2[i, :, 0:n] = low
        d2[i, :, n : 2 * n] = pltpu.roll(v, COLS - 1, 0).astype(BF16)
        return carry

    lax.fori_loop(0, rows, put, 0, unroll=7)
    low = flat(dz[...])
    cur = mm_side(flat(xs[1 : rows + 1]), low)
    for k, (y, x) in enumerate(((1, 1), (1, 2), (1, 0), (2, 1), (2, 2), (2, 0))):
        put_rows(packed, n * (3 * y + x), cur[n * k : n * (k + 1)])
    up = mm_side(flat(xs[0:rows, :, 3 * n : 6 * n]), low)
    for k, (y, x) in enumerate(((0, 1), (0, 2), (0, 0))):
        put_rows(packed, n * (3 * y + x), up[n * k : n * (k + 1)])
    share_out(tab, packed, 9 * n, kept, sent)


def b12_images(
    tab, d2, b_even, b_odd, zz, norm_in, keeps_in, dn, sums_out, de, do, wide, *, own
):
    rows = de.shape[0]
    n = LANES
    half = half_of(tab)
    first = rows * (half if own else 1 - half)
    step = rows // 2
    for k in range(2):
        here = flat(d2[pl.ds(first + step * k, step)])
        below = flat(d2[pl.ds(first + step * k + 1, step)])
        de[step * k : step * (k + 1)] = mm_nt(here, b_even[...]).reshape(step, COLS, 2 * n)
        odd = mm_nt(here, b_odd[:, 0 : 2 * n]) + mm_nt(below, b_odd[:, 2 * n : 4 * n])
        do[step * k : step * (k + 1)] = odd.reshape(step, COLS, 2 * n)
    mean_1, rstd_1 = keeps_in[0:1, :], keeps_in[1:2, :]
    group = entry(tab, OWN)
    scale = rstd_1 * gain_of(norm_in, group)
    bias = 0.5 * (shift_of(norm_in, group) - mean_1 * scale)
    scale = 0.5 * scale
    keep = valid_cols(LANES) & chan_mask(tab)

    def emit(i, carry):
        sums, products = carry
        for ra in (0, 1):
            planes = (de, do)[ra]
            for cb in (0, 1):
                zv = zz[2 * i + ra, pl.ds(cb, COLS, stride=2), :]
                g = planes[i, :, n * cb : n * (cb + 1)] * slope_of_half(zv * scale + bias)
                g = jnp.where(keep, g, 0.0)
                sums = sums + fold(g)
                products = products + fold(g * (zv - mean_1))
                wide[ra, pl.ds(cb, COLS, stride=2), :] = g
            dn[2 * i + ra] = wide[ra].astype(BF16)
        return sums, products

    totals = lax.fori_loop(0, rows, emit, (zeros8(n), zeros8(n)), unroll=7)
    sums_out[0:1, :] = down(totals[0])
    sums_out[1:2, :] = down(totals[1]) * rstd_1


def b13(
    tab, got, labels, norm, keeps, w, z_own, z_for, dn_own, dn_for, gs_own, gs_for, *rest, at, held
):
    finished, outs = rest[:held], rest[held : 2 * held]
    grad, grad_norm, dz, wide, grad_v, norm_v, sems = rest[2 * held :]
    copies = [
        pltpu.make_async_copy(a, b, sems.at[k]) for k, (a, b) in enumerate(zip(finished, outs))
    ]
    for copy in copies:
        copy.start()
    rows, cols = grad.shape[1], grad.shape[2]
    half = half_of(tab)
    pixels = 2.0 * rows * cols
    marks = labels[...]
    totals = last_sums(got.at[:, at : at + 4, :], marks, norm.shape[0])
    for g in range(norm.shape[0]):
        norm_v[g, 0:1, :] = totals[g][1]
        norm_v[g, 1:2, :] = totals[g][0]
    copies.append(pltpu.make_async_copy(norm_v, grad_norm, sems.at[held]))
    copies[-1].start()
    keep = lax.broadcasted_iota(jnp.int32, (z_own.shape[1], LANES), 0) < cols
    for k, (z, dn, gs) in enumerate(((z_own, dn_own, gs_own), (z_for, dn_for, gs_for))):
        group = entry(tab, OWN if k == 0 else OTHER)
        shift_sum = own_of([t[0] for t in totals], group)
        gain_sum = own_of([t[1] for t in totals], group)
        count = group_count(marks, group) * pixels
        mean, rstd = keeps[2 * k : 2 * k + 1, :], keeps[2 * k + 1 : 2 * k + 2, :]
        a = rstd * gain_of(norm, group)
        b = -(a * rstd) * gain_sum / count
        c = -a * shift_sum / count

        def put(i, carry, z=z, dn=dn, mean=mean, a=a, b=b, c=c):
            v = a * dn[i].astype(F32) + b * (z[i] - mean) + c
            dz[i] = jnp.where(keep, v, 0.0).astype(BF16)
            return carry

        lax.fori_loop(0, rows, put, 0, unroll=7)
        place = half if k == 0 else 1 - half
        step = rows // 2
        for q in range(2):
            low = flat(dz[step * q : step * (q + 1)])
            for p in range(wide.shape[0]):
                values = mm_nt(low, w[LANES * p : LANES * (p + 1), :])
                wide[p, step * q : step * (q + 1)] = values.reshape(step, -1, LANES)

            def emit(i, carry, gs=gs, place=place):
                even = pl.ds(0, COLS, stride=2)
                for p in range(wide.shape[0]):
                    lanes = slice(LANES * p, LANES * (p + 1))
                    wide[p, 2 * i, even, :] = wide[p, 2 * i, even, :] + gs[i, :, lanes].astype(F32)
                    grad_v[place, 2 * i, :, lanes] = wide[p, 2 * i, 0:cols, :].astype(BF16)
                    grad_v[place, 2 * i + 1, :, lanes] = wide[p, 2 * i + 1, 0:cols, :].astype(BF16)
                return carry

            lax.fori_loop(step // 2 * q, step // 2 * (q + 1), emit, 0, unroll=True)
            part = pl.ds(step * q, step)
            copies.append(
                pltpu.make_async_copy(
                    grad_v.at[place, part], grad.at[place, part], sems.at[held + 1 + 2 * k + q]
                )
            )
            copies[-1].start()
    for copy in copies:
        copy.wait()


def put_rows(out, at, value):
    for j in range(value.shape[1] // LANES):
        out[at : at + value.shape[0], :] = value[:, LANES * j : LANES * (j + 1)].astype(BF16)
        at += value.shape[0]
    return at


def take_rows(source, at, out):
    rows = out.shape[0]
    for j in range(out.shape[1] // LANES):
        out[:, LANES * j : LANES * (j + 1)] = source(at, rows)
        at += rows
    return at


def share_out(tab, packed, used, kept, sent):
    if used < packed.shape[0]:
        packed[used:, :] = jnp.zeros((packed.shape[0] - used, LANES), BF16)
    half = half_of(tab)
    size = kept.shape[0] * kept.shape[1]
    for out, place in ((kept, half), (sent, 1 - half)):
        out[...] = packed[pl.ds(pl.multiple_of(size * place, 16), size), :].reshape(out.shape)


def g_most(
    tab, act_2b, x3, dz_2b, joined, dz_2a, act_1b, xee,
    got, labels, norm_c, norm_p, keeps, grad_pre_2, zc, zp,
    got_2c, norm_2c, keeps_2c, grad_pre, z_2c,
    kept, sent, dz_p, own10, packed, dz_1c, dz_2c,
):
    rows, outer = dz_2b.shape[0], zc.shape[2]
    pixels = 1.0 * rows * (COLS - 4)
    marks, label = labels[...], entry(tab, OWN)
    blocks = outer // LANES
    total = group_sum(got, marks, label)
    lines = wide_lines(total, outer)
    for k in range(2):
        own10[:, outer * k : outer * (k + 1)] = lines[k]
        at = 2 * outer + LANES * k
        own10[:, at : at + LANES] = total[k : k + 1, 3 * outer // 2 :]
    wide = [
        line_of(over_group(get_split(got_2c, 2 * blocks * k, blocks), marks, label)) for k in (0, 1)
    ]
    mean, a, b, c = own_coefs(tab, marks, norm_2c, keeps_2c, pixels, *wide)
    gate = 0.25 * tiled(entry(tab, GATE), outer)
    normed_grad(grad_pre, (dz_2c, z_2c, mean, a * gate, b, c))
    coefs_c = own_coefs(tab, marks, norm_c, keeps.at[0:2], pixels, lines[0], lines[1])
    coefs_p = own_coefs(tab, marks, norm_p, keeps.at[2:4], pixels, lines[0], lines[2])
    normed_grad(grad_pre_2, (dz_1c, zc, *coefs_c), (dz_p, zp, *coefs_p))
    at = put_rows(packed, 0, mm_tn(flat(act_2b[...]), flat(dz_2c[...])))
    low = flat(dz_2b[...])
    for y in range(3):
        at = put_rows(packed, at, mm_side(flat(x3[y : y + rows]), low))
    at = put_rows(packed, at, mm_side(flat(joined[...]), flat(dz_2a[...])))
    at = put_rows(packed, at, mm_tn(flat(act_1b[...]), flat(dz_1c[...])))
    at = put_rows(packed, at, mm_tn(flat(xee[...]), flat(dz_p[...])))
    share_out(tab, packed, at, kept, sent)


def strided_grad(tab, dz_p, w_p, gs_own, gs_oth):
    half = half_of(tab)
    count = gs_own.shape[0]
    for k, gs in enumerate((gs_own, gs_oth)):
        first = count * (half if k == 0 else 1 - half)
        got = mm_nt(flat(dz_p[pl.ds(first, count)]), w_p[...])
        gs[...] = got.reshape(gs.shape).astype(BF16)


def g_xz(keeps, x_own, x_oth, z_own, z_oth, out, x_sum, low, tall):
    rows, n = z_own.shape[0], LANES
    mean = keeps[0:1, :]
    low[:, :, n : 2 * n] = jnp.ones((rows, z_own.shape[1], n), BF16)
    value = None
    for x, z in ((x_own, z_own), (x_oth, z_oth)):

        def put(i, carry, z=z):
            low[i, :, 0:n] = (z[i] - mean).astype(BF16)
            return carry

        lax.fori_loop(0, rows, put, 0, unroll=7)
        term = mm_tn(flat(x[...]), flat(low[...]))
        value = term if value is None else value + term
    at = value.shape[0]
    tall[0:at, :] = value[:, 0:n]
    if at < tall.shape[0]:
        tall[at:, :] = jnp.zeros((tall.shape[0] - at, n), F32)
    out[...] = tall[...].reshape(out.shape).astype(BF16)
    x_sum[...] = value[:, n : 2 * n]


def g_xd(
    tab, sums_own, sums_oth, norm, keeps, x_sum, got_x, labels, x_own, x_oth, dn_own, dn_oth,
    z_own, z_oth, out, sums, low,
):
    rows = dn_own.shape[0]
    n = LANES
    pixels = 1.0 * (2 * rows) * (2 * (COLS - 4))
    sums[...] = sums_own[...] + sums_oth[...]
    a = keeps[1:2, :] * gain_of(norm, entry(tab, OWN))
    local = sums[0:1, :] / pixels
    mean = keeps[0:1, :]
    b = -(a * keeps[1:2, :]) * sums[1:2, :] / pixels
    value = None
    for x, dn, z in ((x_own, dn_own, z_own), (x_oth, dn_oth, z_oth)):

        def put(i, carry, dn=dn, z=z):
            low[i] = (a * (dn[i].astype(F32) - local) + b * (z[i] - mean)).astype(BF16)
            return carry

        lax.fori_loop(0, rows, put, 0, unroll=7)
        term = mm_tn(flat(low[...]), flat(x[...]))
        value = term if value is None else value + term
    value = stack([jnp.transpose(value[:, lanes]) for lanes in columns(value.shape[1])])
    marks, label = labels[...], entry(tab, OWN)
    total = over_group(get_split(got_x, 4, x_sum.shape[0] // n), marks, label)
    total = join([total[k : k + 1] for k in range(total.shape[0])])
    total = total / tiled(group_count(marks, label), total.shape[1])
    total = jnp.broadcast_to(total, (8, total.shape[1]))
    means = jnp.concatenate(
        [jnp.transpose(total[:, lanes])[:, 0:1] for lanes in columns(total.shape[1])], axis=0
    )
    value = value + (x_sum[...] - means) * (a * local)
    at = value.shape[0]
    out[0:at, :] = value.astype(BF16)
    if at < out.shape[0]:
        out[at:, :] = jnp.zeros((out.shape[0] - at, n), BF16)


def pack_last(tall, sums, kept, got, kept_1b, got_1b, xz, send, *, stats_at, part):
    n = LANES
    devices = send.shape[0]
    piece, share = kept.shape[1], tall.shape[0] // devices
    first = kept.shape[0]
    second = first + kept_1b.shape[0]
    send[0:first, 0:piece, :] = (kept[...].astype(F32) + got[...].astype(F32)).astype(BF16)
    send[first:second, 0:piece, :] = (kept_1b[...].astype(F32) + got_1b[...].astype(F32)).astype(BF16)
    if second < devices:
        send[second:, 0:piece, :] = jnp.zeros((devices - second, piece, n), BF16)
    send[:, piece : piece + share, :] = tall[...].reshape(devices, share, n)
    put_split(send, stats_at, sums[...])
    put_part(send, stats_at + 4, xz, part)


def last_sums(stats, marks, groups):
    values = stats[:, 0:2, :].astype(F32) + stats[:, 2:4, :].astype(F32)
    out = []
    for g in range(groups):
        total = jnp.sum(values * (marks == float(g)).astype(F32), axis=0)
        out.append((total[0:1], total[1:2]))
    return out


def add_all(
    got, labels, norm, keeps_all, got_a, got_b, found_2b, found_1b, out, *, at, pixels, parts
):
    devices, n = got.shape[0], LANES
    half = devices // 2
    share = parts[-1][2]
    piece = (out.shape[1] - share - 8) // 2
    marks = labels[...]
    value = jnp.sum(got[:, piece : piece + share, :].astype(F32), axis=0)
    products = get_split(got, at, 2)[:, 1:2, :]
    lack = jnp.zeros(products.shape, F32)
    for g in range(norm.shape[0]):
        rstd = keeps_all[2 * g + 1 : 2 * g + 2, :]
        factor = -(rstd * rstd * norm[g, 0:1, :]) / pixels
        same = (marks == float(g)).astype(F32)
        middle = jnp.sum(products * same, axis=0) / jnp.sum(same, axis=0)
        lack = lack + (middle[None] - products) * (factor[None] * same)
    rows = [
        jnp.sum(source[:, start : start + last - first, :].astype(F32) * lack, axis=0)
        for source, (start, first, last) in zip((got_a, got_b, got), parts)
        if last > first
    ]
    value = value + jnp.concatenate(rows, axis=0)
    for k in (0, 1):
        total = jnp.sum(got[half * k : half * (k + 1), 0:piece, :].astype(F32), axis=0).astype(BF16)
        out[:, piece * k : piece * (k + 1), :] = jnp.broadcast_to(
            total[None], (out.shape[0], piece, n)
        )
    out[:, 2 * piece : 2 * piece + share, :] = jnp.broadcast_to(
        value.astype(BF16)[None], (out.shape[0], share, n)
    )
    put_split(out, 2 * piece + share, stack([found_2b[...], found_1b[...]]))


def place_parts(minor, parts, packed, tall, found, piece):
    far, share = parts[0].shape[0], tall.shape[1]
    for k, part in enumerate(parts):
        base = lax.bitwise_xor(minor, jnp.int32(k))

        def place(z, carry, part=part, base=base):
            owner = base + NEAR * z
            for h in (0, 1):
                packed[h, owner] = part[z, piece * h : piece * (h + 1), :]
            tall[owner] = part[z, 2 * piece : 2 * piece + share, :].astype(F32)
            sums = part[z, 2 * piece + share :, :].astype(F32)
            found[owner] = sums[0:4] + sums[4:8]
            return carry

        lax.fori_loop(0, far, place, 0, unroll=min(far, 4))


def unpack_own(tab, *refs, piece):
    place_parts(half_of(tab, MINOR), refs[:NEAR], *refs[NEAR:], piece)


def unpack(tab, labels, packed_own, tall_own, found_own, *refs, first, second, piece):
    parts, outs, values = refs[:NEAR], refs[NEAR : NEAR + 9], refs[NEAR + 9 :]
    *values, packed_oth, tall_oth, found_oth, sems = values
    place_parts(half_of(tab, MINOR), parts, packed_oth, tall_oth, found_oth, piece)
    half = half_of(tab)
    copies = [
        pltpu.make_async_copy(value, out, sems.at[k]) for k, (value, out) in enumerate(zip(values, outs))
    ]
    w_1b, w_1a, *grad_norms = values[5:9]
    own, oth = (packed_own, tall_own, found_own), (packed_oth, tall_oth, found_oth)
    for core in (0, 1):

        @pl.when(half == core)
        def _():
            packed, tall, found = zip(*((own, oth) if core == 0 else (oth, own)))
            most, last = [], []
            for h in (0, 1):
                pieces = [flat(v[h]) for v in packed]
                middle = pieces[0].shape[0]
                cut = first * piece
                most.append((pieces, middle))
                last.append((cut, pieces, middle))

            def span(pieces, middle, at, rows):
                found_rows = []
                if at < middle:
                    found_rows.append(pieces[0][at : min(at + rows, middle)])
                if at + rows > middle:
                    found_rows.append(pieces[1][max(at - middle, 0) : at + rows - middle])
                return [v.astype(F32) for v in found_rows]

            size = first * piece

            def source(at, rows):
                out = []
                if at < size:
                    out += span(*most[0], at, min(rows, size - at))
                if at + rows > size:
                    start = max(at - size, 0)
                    out += span(*most[1], start, at + rows - size - start)
                return out[0] if len(out) == 1 else stack(out)

            starts = [0]
            for value in values[0:4]:
                starts.append(starts[-1] + value.shape[0] * value.shape[1] // LANES)
            for k in (1, 4):
                take_rows(source, starts[k], values[k])
                copies[k].start()
            left = w_1b.shape[0]
            for k, (cut, pieces, middle) in enumerate(last):
                rows = min(second * piece, left)
                lines = span(pieces, middle, cut, rows)
                start = second * piece * k
                w_1b[start : start + rows, :] = lines[0] if len(lines) == 1 else stack(lines)
                left -= rows
            copies[5].start()
            for k in (0, 2, 3):
                take_rows(source, starts[k], values[k])
                copies[k].start()
            lines = stack([flat(v[...]) for v in tall])
            w_1a[...] = lines[0 : w_1a.shape[0]]
            copies[6].start()
            sums = jnp.concatenate([v[...] for v in found], axis=0)
            for k, grad_norm in enumerate(grad_norms):
                norm_from_owners(sums[:, 2 * k : 2 * k + 2, :], labels[...], grad_norm)
                copies[7 + k].start()

    for copy in copies:
        copy.wait()


def norm_from_owners(found, marks, grad_norm):
    for g in range(grad_norm.shape[0]):
        total = over_group(found, marks, float(g)) / group_count(marks, float(g))
        grad_norm[g, 0:1, :] = total[1:2]
        grad_norm[g, 1:2, :] = total[0:1]


def gather(send):
    return lax.all_to_all(send, AXES, 0, 0)


def tie(*values):
    return lax.optimization_barrier(values)


def swap(block):
    return lax.ppermute(block, "rows", [(0, 1), (1, 0)])


def body(
    images, w_1a, w_1b, w_1c, w_1p, w_2a, w_2b, w_2c,
    norm_1a, norm_1b, norm_1c, norm_1p, norm_2a, norm_2b, norm_2c,
    cotangent, group, width, gate,
):
    devices = lax.axis_size("rows") * lax.axis_size("batch")
    place = lax.axis_index(AXES).astype(jnp.int32).reshape(1)
    norms = (norm_1a, norm_1b, norm_1c, norm_1p, norm_2a, norm_2b, norm_2c)
    norm_1a, norm_1b, norm_1c, norm_1p, norm_2a, norm_2b, norm_2c = (
        v.transpose(1, 0, 2) for v in norms
    )
    outer, inputs = w_1c.shape[1], w_1a.shape[0]
    rows = cotangent.shape[1]
    cols_in = 2 * COLS
    n, m = LANES, devices

    def send(stats, channels=LANES):
        return ((m, channels // LANES, stats * LANES), F32)

    def maps(channels, dtype=F32):
        return ((rows, COLS, channels), dtype)

    def scratch(channels, dtype=F32):
        return pltpu.VMEM((rows, COLS, channels), dtype)

    def params(*arrays):
        return [(a.shape, F32) for a in arrays]

    def mean_scale(channels, count=1):
        return ((2 * count, channels), F32)

    wide_in = ((rows, cols_in, inputs), BF16)
    wide_z = ((rows, cols_in, n), F32)
    raw = images.shape
    tab, x_own, x_for, z_own, z_for, s1 = stage(
        functools.partial(f1, batch=devices // 2), [((8, n), F32), wide_in, wide_in, wide_z, wide_z, send(5)],
        [*(pltpu.SMEM(v.shape, jnp.int32) for v in (place, group, width, gate)),
         pltpu.VMEM(raw, BF16), pltpu.VMEM(w_1a.shape, BF16), pltpu.VMEM((8, n), F32),
         pltpu.SemaphoreType.DMA((9,))],
        hbm=(0, 1, 2, 3, 4, 5),
    )(place, group, width, gate, images, w_1a)
    s1, v_1b, v_2b = tie(s1, w_1b, w_2b)
    built = stage(
        prepare,
        [(v, BF16) for v in (
            (3 * n, n), (3 * n, 2 * n), (3 * n, 2 * n), (3 * n, n),
            (2 * n, 2 * n), (2 * n, 4 * n), (2 * n, 3 * n), (n, 3 * n),
        )],
    )(v_1b, v_2b)
    s1, x_for, w_even, w_odd, w_two, w_last, b_even, b_odd, b_two, b_last = tie(s1, x_for, *built)
    x_oth = swap(x_for)
    g1 = gather(s1)
    g1, x_oth = tie(g1, x_oth)
    xee, z_1p, stats_1p = stage(
        f1_strided,
        [maps(inputs, BF16), maps(outer), ((1, inputs + outer), F32)],
        [pltpu.VMEM((inputs // n, cols_in, n), F32)],
    )(tab, x_own, x_oth, w_1p)
    xs, z_1b, s2, labels, k_1a, k_all, z_oth = stage(
        f2,
        [((rows + 1, COLS, 6 * n), BF16), maps(n), send(2 + (inputs + outer) // n),
         ((m, 1, n), F32), mean_scale(n, 2), mean_scale(n, norm_1a.shape[0]), wide_z],
    )(tab, g1, z_own, x_oth, w_1a, norm_1a, w_even, w_odd, stats_1p)
    share = -(-inputs // devices)
    half_in = ((rows, cols_in, n), BF16)
    xz, x_sum = stage(
        g_xz, [((devices, share, n), BF16), ((inputs, n), F32)],
        [pltpu.VMEM((rows, cols_in, 2 * n), BF16), pltpu.VMEM((devices * share, n), F32)],
    )(k_1a, x_own, x_oth, z_own, z_oth)
    s2, xz, x_sum = tie(s2, xz, x_sum)
    g2 = gather(s2)
    share_1 = -(-n // devices)
    p_rows = ((devices, 2 * share_1, n), BF16)
    own_rows = ((devices, 2 * share_1, n), F32)
    wide_rows = outer // n
    p_at = 2 + wide_rows
    xz_3 = p_at + 2 * share_1
    high_3 = -(-xz_3 // 16) * 16
    xz_6 = p_at + 4 * share_1
    high_6 = -(-xz_6 // 8) * 8
    cut_3 = min(share, high_3 - xz_3)
    cut_6 = min(share, cut_3 + high_6 - xz_6)
    act_1b, z_1c, s3, k_1b, k_p, slope_1b, q_1b, p_1b, own_1b = stage(
        functools.partial(f3, share=share_1, part=(0, cut_3)),
        [maps(n, BF16), maps(outer), ((devices, high_3, n), BF16), mean_scale(n),
         mean_scale(outer), maps(n), ((2, n), F32), p_rows, own_rows],
        [scratch(4 * n, BF16), pltpu.VMEM(p_rows[0], BF16)],
    )(tab, g2, labels, z_1b, norm_1b, w_1c, w_1p, xz)
    g3 = gather(s3)
    high = -(-(8 + 2 * share_1) // 16) * 16
    joined, slope, z_2a, s4, k_cp = stage(
        f4,
        [maps(outer, BF16), maps(outer), maps(n), ((devices, high, n), BF16),
         mean_scale(outer, 2)],
    )(tab, g3, labels, z_1c, z_1p, norm_1c, norm_1p, k_p, w_1c, w_2a, p_1b, q_1b)
    g4 = gather(s4)
    x3, z_2b, s5, k_2a = stage(
        f5, [((rows + 2, COLS, 3 * n), BF16), maps(n), send(2), mean_scale(n)]
    )(tab, g4, labels, z_2a, norm_2a, w_two, w_last)
    g5 = gather(s5)
    act_2b, z_2c, s6, k_2b, slope_2b, q_2b, own_2b = stage(
        functools.partial(f6, share=share_1, part=(cut_3, cut_6)),
        [maps(n, BF16), maps(outer), ((devices, high_6, n), BF16), mean_scale(n), maps(n),
         ((2, n), F32), own_rows],
        [scratch(4 * n, BF16), *(pltpu.VMEM(p_rows[0], BF16) for _ in range(2))],
    )(tab, g5, labels, z_2b, norm_2b, w_2c, xz)
    g6 = gather(s6)
    high_7 = -(-(4 * wide_rows + 8 + 2 * share_1) // 16) * 16
    result, grad_pre, s7, k_2c, d_2b = stage(
        functools.partial(b7, share=share_1, p_at=p_at),
        [(cotangent.shape[1:], BF16), maps(outer), ((devices, high_7, n), BF16),
         mean_scale(outer), maps(n)],
        [pltpu.VMEM((COLS, outer), F32), scratch(outer, BF16)],
    )(tab, g6, labels, joined, z_2c, norm_2c, w_2c, cotangent[0], slope_2b, z_2b, k_2b, q_2b)
    g7 = gather(s7)
    dz_2b, dout_2a, s9, found_2b = stage(
        functools.partial(b9, share=share_1, p_at=p_at),
        [maps(n, BF16), maps(n), ((devices, high, n), BF16), ((2, n), F32)],
        [pltpu.VMEM((rows + 2, COLS, 3 * n), BF16), scratch(n)],
    )(tab, g7, labels, norm_2c, k_2c, w_2c, g6, act_2b, slope_2b, d_2b, z_2b, norm_2b, k_2b,
      b_two, b_last, z_2a, norm_2a, k_2a, x_sum, g4, g3, own_2b)
    g9 = gather(s9)
    dz_2a, grad_pre_2, s10, d_1b = stage(
        b10,
        [maps(n, BF16), maps(outer), ((devices, 2, 3 * outer // 2 + n), F32), maps(n)],
        [scratch(outer), scratch(outer, BF16)],
    )(tab, g9, labels, dout_2a, z_2a, norm_2a, k_2a, w_2a, grad_pre, slope, z_1c, z_1p, k_cp,
      norm_1c, w_1c, slope_1b, z_1b, k_1b)
    g10 = gather(s10)
    half_map = ((rows // 2, COLS, inputs), BF16)
    most_rows = sum(v.size for v in (w_2c, w_2b, w_2a, w_1c, w_1p)) // n
    rows_1b = w_1b.size // n
    piece = 16
    while -(-most_rows // (2 * piece)) - (-rows_1b // (2 * piece)) > devices:
        piece += 16
    first, second = -(-most_rows // (2 * piece)), -(-rows_1b // (2 * piece))
    part, part_1b = ((first, piece, n), BF16), ((second, piece, n), BF16)
    kept, sent, dz_1p, own10 = stage(
        g_most,
        [part, part, maps(outer, BF16), ((1, 2 * outer + 2 * n), F32)],
        [pltpu.VMEM((2 * first * piece, n), BF16), *(scratch(outer, BF16) for _ in range(2))],
    )(tab, act_2b, x3, dz_2b, joined, dz_2a, act_1b, xee,
      g10, labels, norm_1c, norm_1p, k_cp, grad_pre_2, z_1c, z_1p,
      g7, norm_2c, k_2c, grad_pre, z_2c)
    gs_own, gs_send = stage(strided_grad, [half_map, half_map])(tab, dz_1p, w_1p)
    got, gs_for = swap(sent), swap(gs_send)
    half_in = ((rows, cols_in, n), BF16)
    d2, kept_1b, sent_1b, found_1b = stage(
        functools.partial(b12, share=share_1, q_at=4 + 2 * share_1, p_at=4 + 2 * (inputs // n)),
        [((rows + 1, COLS, 2 * n), BF16), part_1b, part_1b, ((2, n), F32)],
        [scratch(n, BF16), pltpu.VMEM((2 * second * piece, n), BF16), scratch(n)],
    )(tab, own10, labels, norm_1c, k_cp, w_1c, g3, g4, g9, own_1b, act_1b, slope_1b, d_1b,
      z_1b, norm_1b, k_1b, xs)
    got_1b = swap(sent_1b)
    sides = []
    for own, z in ((False, z_oth), (True, z_own)):
        sides.append(
            stage(
                functools.partial(b12_images, own=own), [half_in, ((2, n), F32)],
                [pltpu.VMEM((rows // 2, COLS, 2 * n), F32), pltpu.VMEM((rows // 2, COLS, 2 * n), F32),
                 pltpu.VMEM((2, cols_in, n), F32)],
            )(tab, d2, b_even, b_odd, z, norm_1a, k_1a)
        )
        if not own:
            dn_for = swap(sides[0][0])
            d2, _ = tie(d2, sides[0][0])
    (dn_send, sums_send), (dn_own, sums_own) = sides
    stats_at = piece + -(-share // 8) * 8
    high = -(-(stats_at + 4 + share - cut_6) // 16) * 16
    tall, sums_1a = stage(
        g_xd, [((devices * share, n), BF16), ((2, n), F32)], [pltpu.VMEM(half_in[0], BF16)]
    )(tab, sums_own, sums_send, norm_1a, k_1a, x_sum, g9, labels, x_own, x_oth, dn_own, dn_send,
      z_own, z_oth)
    tall, gs_for, dn_for = tie(tall, gs_for, dn_for)
    (s12,) = stage(
        functools.partial(pack_last, stats_at=stats_at, part=(cut_6, share)),
        [((devices, high, n), BF16)]
    )(tall, sums_1a, kept, got, kept_1b, got_1b, xz)
    g12 = gather(s12)
    pixels = 4.0 * images.shape[1] * images.shape[1]
    batch = devices // 2
    far = batch // NEAR
    (mine,) = stage(
        functools.partial(
            add_all, at=stats_at, pixels=pixels,
            parts=((xz_3, 0, cut_3), (xz_6, cut_3, cut_6), (stats_at + 4, cut_6, share)),
        ),
        [((far, 2 * piece + share + 8, n), BF16)],
    )(g12, labels, norm_1a, k_all, g3, g6, found_2b, found_1b)
    columns_of = [[k + NEAR * z for z in range(far)] for k in range(NEAR)]
    along = lax.all_to_all(mine, "batch", 0, 0, axis_index_groups=columns_of)
    near = [
        lax.ppermute(along, "batch", [(i, i ^ k) for i in range(batch)]) for k in range(1, NEAR)
    ]
    late, _ = tie(labels, along)
    grad_norms = stage(norm_tail, params(norm_2c, norm_2a, norm_1c, norm_1p))(late, g7, g9, g10)
    finished = (result, *grad_norms)
    held = len(finished)
    *finished, grad_images, grad_norm_1a = stage(
        functools.partial(b13, at=stats_at, held=held),
        [*((v.shape, v.dtype) for v in finished), (images.shape, BF16), *params(norm_1a)],
        [pltpu.VMEM(half_in[0], BF16), pltpu.VMEM((inputs // n, rows, cols_in, n), F32),
         pltpu.VMEM(images.shape, BF16), pltpu.VMEM(norm_1a.shape, F32),
         pltpu.SemaphoreType.DMA((held + 5,))],
        hbm_out=range(held + 2),
    )(tab, g12, labels, norm_1a, k_1a, w_1a, z_own, z_for, dn_own, dn_for, gs_own, gs_for, *finished)
    result, grad_norm_2c, grad_norm_2a, grad_norm_1c, grad_norm_1p = finished
    *near, grad_images = tie(*near, grad_images)
    parts = [along, *near]
    weights = (w_2c, w_2b.reshape(-1, n), w_2a, w_1c, w_1p, w_1b.reshape(-1, n), w_1a)
    side = [
        ((2, batch, piece, n), BF16), ((batch, share, n), F32), ((batch, 4, n), F32)
    ]
    crossed = [swap(v) for v in parts]
    placed = stage(functools.partial(unpack_own, piece=piece), side)(tab, *parts)
    t_2c, t_2b, t_2a, t_1c, t_1p, t_1b, t_1a, grad_norm_2b, grad_norm_1b = stage(
        functools.partial(unpack, first=first, second=second, piece=piece),
        [(v.shape, F32) for v in (*weights, norm_2b, norm_1b)],
        [*(pltpu.VMEM(v.shape, F32) for v in (*weights, norm_2b, norm_1b)),
         *(pltpu.VMEM(*v) for v in side), pltpu.SemaphoreType.DMA((9,))],
        hbm_out=range(9),
    )(tab, labels, *placed, *crossed)
    grads = (
        grad_norm_1a, grad_norm_1b, grad_norm_1c, grad_norm_1p,
        grad_norm_2a, grad_norm_2b, grad_norm_2c,
    )
    return (
        result[None], grad_images, t_1a, t_1b.reshape(w_1b.shape), t_1c, t_1p, t_2a,
        t_2b.reshape(w_2b.shape), t_2c, *[v.transpose(1, 0, 2) for v in grads],
    )


def solution(mesh):
    return jax.shard_map(
        body,
        mesh=mesh,
        in_specs=(
            P("batch", "rows", None, None),
            *[P()] * 14,
            P(("batch", "rows"), None, None, None),
            P("batch"),
            P(),
            P(),
        ),
        out_specs=(
            P(("batch", "rows"), None, None, None),
            P("batch", "rows", None, None),
            *[P()] * 14,
        ),
        check_vma=False,
    )
```

```python
import functools

import jax
import jax.numpy as jnp
from jax import lax
from jax.experimental import pallas as pl
from jax.experimental.pallas import tpu as pltpu
from jax.sharding import PartitionSpec as P

EPSILON = 1e-05
F32 = jnp.float32
BF16 = jnp.bfloat16
AXES = ("rows", "batch")
VMEM_LIMIT = 14 * 1024 * 1024
LANES = 128
COLS = 32
NEAR = 4


def full(memory=pltpu.VMEM):
    return pl.BlockSpec(memory_space=memory)


def stage(kernel, outs, scratch=(), hbm=(), hbm_out=()):
    def place(i, outside):
        return pltpu.HBM if i in outside else pltpu.VMEM

    def call(*args):
        args = [
            pltpu.with_memory_space_constraint(a, pltpu.HBM) if i in hbm else a
            for i, a in enumerate(args)
        ]
        return pl.pallas_call(
            kernel,
            out_shape=tuple(jax.ShapeDtypeStruct(s, d) for s, d in outs),
            in_specs=[full(place(i, hbm)) for i in range(len(args))],
            out_specs=tuple(
                full(place(i, hbm_out)) for i in range(len(outs))
            ),
            scratch_shapes=list(scratch),
            compiler_params=pltpu.CompilerParams(vmem_limit_bytes=VMEM_LIMIT),
            name=(kernel.func if isinstance(kernel, functools.partial) else kernel).__name__,
        )(*args)

    return call


def silu_of_half(u):
    return u + u * jnp.tanh(u)


def slope_of_half(u):
    t = jnp.tanh(u)
    return (0.5 + 0.5 * t) * (1.0 + u - u * t)


def fold(x):
    return (x[0:8] + x[8:16]) + (x[16:24] + x[24:32])


def row(total, stat):
    blocks = total.shape[0]
    pieces = [total[j : j + 1, LANES * stat : LANES * (stat + 1)] for j in range(blocks)]
    return pieces[0] if blocks == 1 else jnp.concatenate(pieces, axis=1)


def spread(out_ref, rows):
    blocks = out_ref.shape[1]
    for stat, values in enumerate(rows):
        for j in range(blocks):
            piece = values[:, LANES * j : LANES * (j + 1)]
            out_ref[:, j : j + 1, LANES * stat : LANES * (stat + 1)] = jnp.broadcast_to(
                piece[None], (out_ref.shape[0], 1, LANES)
            )


def group_sum(got_ref, labels, label):
    same = (labels == label).astype(F32)
    stats = got_ref.shape[2] // LANES
    parts = [
        jnp.sum(got_ref[:, :, LANES * s : LANES * (s + 1)] * same, axis=0) for s in range(stats)
    ]
    return jnp.concatenate(parts, axis=1) if stats > 1 else parts[0]


def group_count(labels, label):
    return jnp.sum((labels == label).astype(F32), axis=0)


def tiled(values, channels):
    return jnp.concatenate([values] * (channels // LANES), axis=1) if channels > LANES else values


def moments(first, second, pixels):
    mean = first / pixels
    return mean, lax.rsqrt(second / pixels - mean * mean + EPSILON)


def own_of(values, label):
    out = values[0]
    label = tiled(label, out.shape[1])
    for g in range(1, len(values)):
        out = jnp.where(label == float(g), values[g], out)
    return out


def gain_of(norm_ref, label):
    return own_of([norm_ref[g, 0:1, :] for g in range(norm_ref.shape[0])], label)


def shift_of(norm_ref, label):
    return own_of([norm_ref[g, 1:2, :] for g in range(norm_ref.shape[0])], label)


def valid_cols(channels):
    return lax.broadcasted_iota(jnp.int32, (COLS, channels), 0) < COLS - 4


def chan_mask(tab):
    return lax.broadcasted_iota(jnp.int32, (1, LANES), 1).astype(F32) < entry(tab, LIMIT)


def flat(x):
    return x.reshape(x.shape[0] * x.shape[1], x.shape[2])


def mm(a, b):
    return jnp.dot(a, b, preferred_element_type=F32)


def mm_nt(a, b):
    return lax.dot_general(a, b, (((1,), (1,)), ((), ())), preferred_element_type=F32)


def mm_tn(a, b):
    return lax.dot_general(a, b, (((0,), (0,)), ((), ())), preferred_element_type=F32)


def mm_side(a, b):
    turned = mm_tn(b, a)
    blocks = [
        jnp.transpose(turned[:, LANES * j : LANES * (j + 1)]) for j in range(a.shape[1] // LANES)
    ]
    return blocks[0] if len(blocks) == 1 else jnp.concatenate(blocks, axis=0)


def zeros8(channels):
    return jnp.zeros((8, channels), F32)


def down(x):
    return jnp.sum(x, axis=0, keepdims=True)


OWN, OTHER, HALF, LIMIT, GATE, MINOR, MAJOR = range(7)


def entry(tab, k):
    return tab[k : k + 1, :]


def half_of(tab, k=HALF):
    return (jnp.sum(entry(tab, k)) * (1.0 / LANES)).astype(jnp.int32)


def prepare(w1b, w2b, w_even, w_odd, w_two, w_last, b_even, b_odd, b_two, b_last):
    n = LANES
    for k, (y, x) in enumerate(((1, 1), (1, 2), (1, 0))):
        w_even[n * k : n * (k + 1), :] = w1b[y, x]
    for k, (low, high) in enumerate((((2, 1), (0, 1)), ((2, 2), (0, 2)), ((2, 0), (0, 0)))):
        w_odd[n * k : n * (k + 1), 0:n] = w1b[low]
        w_odd[n * k : n * (k + 1), n : 2 * n] = w1b[high]
    for x in range(3):
        w_two[n * x : n * (x + 1), 0:n] = w2b[0, x]
        w_two[n * x : n * (x + 1), n : 2 * n] = w2b[1, x]
        w_last[n * x : n * (x + 1), :] = w2b[2, x]
        b_two[0:n, n * x : n * (x + 1)] = w2b[1, x]
        b_two[n : 2 * n, n * x : n * (x + 1)] = w2b[2, x]
        b_last[:, n * x : n * (x + 1)] = w2b[0, x]
    nothing = jnp.zeros((n, n), BF16)
    b_even[0:n, 0:n] = w1b[1, 1]
    b_even[0:n, n : 2 * n] = nothing
    b_even[n : 2 * n, 0:n] = w1b[1, 2]
    b_even[n : 2 * n, n : 2 * n] = w1b[1, 0]
    for k, top in ((0, 2), (1, 0)):
        b_odd[0:n, 2 * n * k : 2 * n * k + n] = w1b[top, 1]
        b_odd[0:n, 2 * n * k + n : 2 * n * (k + 1)] = nothing
        b_odd[n : 2 * n, 2 * n * k : 2 * n * k + n] = w1b[top, 2]
        b_odd[n : 2 * n, 2 * n * k + n : 2 * n * (k + 1)] = w1b[top, 0]


def widen(source, x_pad):
    rows, cols, chans = source.shape
    gap = x_pad.shape[1] - cols

    def put(i, carry):
        x_pad[i, 0:cols, :] = source[i]
        x_pad[i, cols : cols + gap, :] = jnp.zeros((gap, chans), BF16)
        return carry

    lax.fori_loop(0, rows, put, 0, unroll=7)


def first_project(x_pad, w, z, stats=True):
    rows = x_pad.shape[0]
    step = rows // 4
    sums, squares = zeros8(LANES), zeros8(LANES)
    for c in range(4):
        values = mm(flat(x_pad[step * c : step * (c + 1)]), w[...])
        z[step * c : step * (c + 1)] = values.reshape(step, x_pad.shape[1], LANES)
        if stats:
            parts = values.reshape(-1, 8, LANES)
            sums = sums + jnp.sum(parts, axis=0)
            squares = squares + jnp.sum(parts * parts, axis=0)
    return sums, squares


def f1(
    place_at, group_at, width_at, gate_at, images, w_at, tab, x_own, x_for, z_own, z_for, send,
    place_ref, group, width, gate, raw, w, found, sems, *, batch,
):
    rows = images.shape[1] // 2
    parts = [pl.ds(rows * p, rows) for p in (0, 1)]
    pairs = (
        (place_at, place_ref), (group_at, group), (width_at, width), (gate_at, gate), (w_at, w),
        *((images.at[k, part], raw.at[k, part]) for k in (0, 1) for part in parts),
    )
    copies = [pltpu.make_async_copy(a, b, sems.at[k]) for k, (a, b) in enumerate(pairs)]
    for k in (0, 5, 4, 6, 7, 8, 1, 2, 3):
        copies[k].start()
    for k in (0, 4):
        copies[k].wait()
    half = lax.div(place_ref[0], batch)
    sides = ((x_own, z_own), (x_for, z_for))

    def one(k):
        for p, part in enumerate(parts):
            copies[5 + 2 * k + p].wait()
            for place in (0, 1):

                @pl.when(half == place)
                def _():
                    x_pad, _ = sides[k] if place == 0 else sides[1 - k]
                    widen(raw.at[k, part], x_pad.at[part])

        for place in (0, 1):

            @pl.when(half == place)
            def _():
                x_pad, z = sides[k] if place == 0 else sides[1 - k]
                sums, squares = first_project(x_pad, w, z)
                at = 2 * (k if place == 0 else 1 - k)
                found[at : at + 1, :] = down(sums)
                found[at + 1 : at + 2, :] = down(squares)

    one(0)
    one(1)
    for k in (1, 2, 3):
        copies[k].wait()
    rows = [found[k : k + 1, :] for k in range(4)]
    own, other = group[half], group[1 - half]
    values = {
        OWN: own, OTHER: other, HALF: half, LIMIT: w.shape[1] // 4 * width[own], GATE: gate[own],
        MINOR: lax.rem(lax.rem(place_ref[0], batch), NEAR),
        MAJOR: lax.div(lax.rem(place_ref[0], batch), NEAR),
    }
    tab[...] = jnp.zeros(tab.shape, F32)
    for k, v in values.items():
        tab[k : k + 1, :] = jnp.full((1, LANES), v.astype(F32))
    spread(send, [*rows, jnp.full((1, LANES), (own + 4 * other).astype(F32))])


def f1_strided(tab, x_own, x_oth, w, xee, z, stats, wide):
    half = half_of(tab)
    rows = x_own.shape[0] // 2
    sums = tuple(zeros8(LANES) for _ in range(wide.shape[0]))
    for k, x_pad in enumerate((x_own, x_oth)):
        first = rows * (half if k == 0 else 1 - half)

        def put(i, carry, x_pad=x_pad, first=first):
            out = []
            for b in range(wide.shape[0]):
                lanes = slice(LANES * b, LANES * (b + 1))
                wide[b, i] = x_pad[2 * i, :, lanes].astype(F32)
                even = wide[b, i, pl.ds(0, COLS, stride=2), :]
                xee[first + i, :, lanes] = even.astype(BF16)
                out.append(carry[b] + fold(even))
            return tuple(out)

        sums = lax.fori_loop(0, rows, put, sums, unroll=7)
    total = 2 * rows
    step = total // 7
    chans = z.shape[2]
    squares = zeros8(chans)
    for c in range(7):
        values = mm(flat(xee[step * c : step * (c + 1)]), w[...])
        z[step * c : step * (c + 1)] = values.reshape(step, COLS, chans)
        parts = values.reshape(-1, 8, chans)
        squares = squares + jnp.sum(parts * parts, axis=0)
    stats[:, 0 : w.shape[0]] = join([down(v) for v in sums])
    stats[:, w.shape[0] :] = down(squares)


def scale_shift(got, labels, tab, norm, pixels, slot=0):
    label = entry(tab, OWN)
    total = group_sum(got, labels, label)
    chans = norm.shape[2]
    count = tiled(group_count(labels, label), chans) * pixels
    mean, rstd = moments(row(total, 2 * slot), row(total, 2 * slot + 1), count)
    gain, shift = gain_of(norm, entry(tab, OWN)), shift_of(norm, entry(tab, OWN))
    return mean, rstd, gain, shift, count


def conv_stats(z, source, pair, single, send, extra=()):
    keep = valid_cols(LANES)[None]
    rows = z.shape[0]
    step = rows // 4
    (lanes_2, w_2, offsets), (lanes_1, w_1, offset) = pair, single
    sums, squares = zeros8(LANES), zeros8(LANES)
    base = min(offsets)
    for c in range(4):
        at = step * c
        both = mm(flat(source[at + base : at + base + step + 1, :, lanes_2]), w_2)
        values = mm(flat(source[at + offset : at + offset + step, :, lanes_1]), w_1)
        for k, own in enumerate(offsets):
            skip = COLS * (own - base)
            values = values + both[skip : skip + step * COLS, LANES * k : LANES * (k + 1)]
        values = jnp.where(keep, values.reshape(step, COLS, LANES), 0.0)
        z[at : at + step] = values
        parts = values.reshape(-1, 8, LANES)
        sums = sums + jnp.sum(parts, axis=0)
        squares = squares + jnp.sum(parts * parts, axis=0)
    spread(send, [down(sums), down(squares), *extra])


def f2(
    tab, got, z_own, x_oth, w, norm, w_even, w_odd, stats_p,
    xs, z, send, labels, keeps, keeps_all, z_oth,
):
    codes = got[:, :, 4 * LANES : 5 * LANES]
    others = jnp.floor(0.25 * codes)
    marks = codes - 4.0 * others
    labels[...] = marks
    rows = xs.shape[0] - 1
    pixels = 4.0 * rows * (COLS - 4)
    first_project(x_oth, w, z_oth, False)
    for g in range(norm.shape[0]):
        mine, theirs = (marks == float(g)).astype(F32), (others == float(g)).astype(F32)
        totals = [
            jnp.sum(
                got[:, :, LANES * s : LANES * (s + 1)] * mine
                + got[:, :, LANES * (s + 2) : LANES * (s + 3)] * theirs,
                axis=0,
            )
            for s in (0, 1)
        ]
        mean, rstd = moments(*totals, group_count(marks, float(g)) * pixels)
        keeps_all[2 * g : 2 * g + 1, :] = mean
        keeps_all[2 * g + 1 : 2 * g + 2, :] = rstd
    for k, slot in enumerate((OWN, OTHER)):
        for q in (0, 1):
            choices = [keeps_all[2 * g + q : 2 * g + q + 1, :] for g in range(norm.shape[0])]
            keeps[2 * k + q : 2 * k + q + 1, :] = own_of(choices, entry(tab, slot))
    mean, rstd = keeps[0:1, :], keeps[1:2, :]
    gain, shift = gain_of(norm, entry(tab, OWN)), shift_of(norm, entry(tab, OWN))
    scale = rstd * gain
    bias = 0.5 * (shift - mean * scale)
    scale = 0.5 * scale
    keep = valid_cols(LANES) & chan_mask(tab)
    half = half_of(tab)
    xs[0] = jnp.zeros(xs.shape[1:], BF16)
    n = LANES
    for k, zz in enumerate((z_own, z_oth)):
        first = 1 + (rows // 2) * (half if k == 0 else 1 - half)

        def put(i, carry, zz=zz, first=first):
            lane = 0
            for a in (0, 1):
                for b in (0, 1):
                    u = zz[2 * i + a, pl.ds(b, COLS, stride=2), :] * scale + bias
                    act = jnp.where(keep, silu_of_half(u), 0.0)
                    xs[first + i, :, lane : lane + n] = act.astype(BF16)
                    lane += n
                    if b == 1:
                        moved = pltpu.roll(act, 1, 0)
                        xs[first + i, :, lane : lane + n] = moved.astype(BF16)
                        lane += n
            return carry

        lax.fori_loop(0, rows // 2, put, 0, unroll=7)
    extra = [stats_p[:, lanes] for lanes in columns(stats_p.shape[1])]
    pair = (slice(3 * n, 6 * n), w_odd[...], (1, 0))
    conv_stats(z, xs, pair, (slice(0, 3 * n), w_even[...], 1), send, extra)


def project(act, w, z):
    rows, chans = z.shape[0], z.shape[2]
    step = rows // 7
    squares = zeros8(chans)
    for c in range(7):
        values = mm(flat(act[step * c : step * (c + 1)]), w[...])
        z[step * c : step * (c + 1)] = values.reshape(step, COLS, chans)
        parts = values.reshape(-1, 8, chans)
        squares = squares + jnp.sum(parts * parts, axis=0)
    return down(squares)


def join(pieces):
    return pieces[0] if len(pieces) == 1 else jnp.concatenate(pieces, axis=1)


def columns(channels):
    return [slice(LANES * j, LANES * (j + 1)) for j in range(channels // LANES)]


def three_parts(sums):
    high = sums.astype(BF16)
    rest = sums - high.astype(F32)
    mid = rest.astype(BF16)
    low = (rest - mid.astype(F32)).astype(BF16)
    lines = [v.astype(F32) for v in (high, mid, low)]
    lines.append(jnp.zeros((13, sums.shape[1]), F32))
    return jnp.concatenate(lines, axis=0).astype(BF16)


def through(sums, w):
    return down(mm(three_parts(sums), w))


def put_split(send, at, values):
    rows = values.shape[0]
    high = values.astype(BF16)
    rest = (values - high.astype(F32)).astype(BF16)
    for k, part in enumerate((high, rest)):
        send[:, at + rows * k : at + rows * (k + 1), :] = jnp.broadcast_to(
            part[None], (send.shape[0], rows, LANES)
        )


def get_split(got, at, rows):
    return got[:, at : at + rows, :].astype(F32) + got[:, at + rows : at + 2 * rows, :].astype(F32)


def over_group(values, marks, label):
    return jnp.sum(values * (marks == label).astype(F32), axis=0)


def stack(rows):
    return jnp.concatenate(rows, axis=0)


def activate_pair(tab, got, labels, z, norm, act, keeps, slope, both):
    rows = z.shape[0]
    pixels = 1.0 * rows * (COLS - 4)
    mean, rstd, gain, shift, _ = scale_shift(got, labels[...], tab, norm, pixels)
    keeps[0:1, :] = mean
    keeps[1:2, :] = rstd
    scale = rstd * gain
    bias = 0.5 * (shift - mean * scale)
    scale = 0.5 * scale
    keep = valid_cols(LANES) & chan_mask(tab)

    def put(i, carry):
        zz = z[i]
        u = zz * scale + bias
        t = jnp.tanh(u)
        p = u * t
        low = jnp.where(keep, u + p, 0.0).astype(BF16)
        act[i] = low
        s = jnp.where(keep, (0.5 + 0.5 * t) * (1.0 + u - p), 0.0)
        sx = s * ((zz - mean) * rstd)
        slope[i] = s
        for k, v in enumerate((s, sx)):
            high = v.astype(BF16)
            both[i, :, LANES * k : LANES * (k + 1)] = high
            both[i, :, LANES * (k + 2) : LANES * (k + 3)] = (v - high.astype(F32)).astype(BF16)
        return carry[0] + fold(low.astype(F32)), carry[1] + fold(s), carry[2] + fold(sx)

    start = zeros8(LANES)
    sums = lax.fori_loop(0, rows, put, (start, start, start), unroll=7)
    act_sum, *sums = [down(v) for v in sums]
    product = mm_tn(flat(act[...]), flat(both[...]))
    product = product[:, 0 : 2 * LANES] + product[:, 2 * LANES :]
    middle = jnp.broadcast_to(act_sum * (1.0 / pixels), (8, LANES))
    return act_sum, product - jnp.transpose(middle)[:, 0:1] * join(sums), stack(sums)


def rows_of(line):
    return stack([line[:, lanes] for lanes in columns(line.shape[1])])


def line_of(rows):
    return join([rows[k : k + 1, :] for k in range(rows.shape[0])])


def put_part(send, at, rows, part):
    first, last = part
    if last > first:
        send[:, at : at + last - first, :] = rows[:, first:last, :]


def pair_rows(product, devices, share, high, low, own):
    n = LANES
    missing = devices * share - n
    for h in (0, 1):
        values = product[:, n * h : n * (h + 1)]
        if missing:
            values = stack([values, jnp.zeros((missing, n), F32)])
        values = values.reshape(devices, share, n)
        first, last = share * h, share * (h + 1)
        top = values.astype(BF16)
        rest = (values - top.astype(F32)).astype(BF16)
        high[:, first:last, :] = top
        low[:, first:last, :] = rest
        own[:, first:last, :] = top.astype(F32) + rest.astype(F32)


def pass_pair(send, at, high, low, marks, groups):
    rows = high.astype(F32) + low.astype(F32)
    out = -rows
    for g in range(groups):
        same = (marks == float(g)).astype(F32)
        images = jnp.maximum(jnp.sum(same, axis=0), 1.0)
        out = out + (jnp.sum(rows * same, axis=0) / images)[None] * same
    send[:, at : at + rows.shape[1], :] = out.astype(BF16)


def pair_solve(tab, marks, outer, inner, sums, w, act_sums, q_rows, p_rows, pixels):
    label, n = entry(tab, OWN), LANES
    (norm_o, keeps_o), (norm_i, keeps_i) = outer, inner
    shift_o, gain_o, shift_i, gain_i = sums
    images = group_count(marks, label)
    count, count_o = images * pixels, tiled(images, norm_o.shape[2]) * pixels
    rstd_o = keeps_o[1:2, :]
    a_o = rstd_o * gain_of(norm_o, label)
    b_o, c_o = -(a_o * rstd_o) * gain_o / count_o, -a_o * shift_o / count_o
    scaled = w[...].astype(F32) * b_o
    high = scaled.astype(BF16)
    low = (scaled - high.astype(F32)).astype(BF16)
    got = mm_nt(jnp.concatenate([high, low, three_parts(c_o)], axis=0), w[...])
    m, e = got[0:n] + got[n : 2 * n], down(got[2 * n :])
    m_high = m.astype(BF16)
    m_low = (m - m_high.astype(F32)).astype(BF16)
    m = m_high.astype(F32) + m_low.astype(F32)
    same = (marks == label).astype(F32)
    middle = jnp.sum(act_sums * same, axis=0) / count
    spread_out = ((act_sums * (1.0 / pixels) - middle[None]) * same).reshape(-1, n).astype(BF16)
    share = p_rows.shape[1] // 2
    p_rows = p_rows * images[None]
    found = []
    q = join([q_rows[:, h : h + 1, :].reshape(-1, n) for h in (0, 1)])
    away = mm_tn(spread_out, q.astype(BF16))
    q = down(q * join([same.reshape(-1, n)] * 2))
    for h, start in enumerate((shift_i, gain_i)):
        lanes = slice(n * h, n * (h + 1))
        p = p_rows[:, share * h : share * (h + 1), :].reshape(-1, n)[0:n] + away[:, lanes]
        found.append(start + down(m * p) + e * q[:, lanes])
    rstd_i = keeps_i[1:2, :]
    a = rstd_i * gain_of(norm_i, label)
    coefs = a, -(a * rstd_i) * found[1] / count, -a * found[0] / count
    both = join([m_high, m_low])
    line = through(middle, both)
    return both, e - line[:, 0:n] - line[:, n:], coefs, found


def f3(
    tab, got, labels, z_in, norm, w, w_p, xz,
    act, z, send, keeps, keeps_p, slope, q, high, own, both, low, *, share, part,
):
    got_1 = got.at[:, :, 0 : 2 * LANES]
    found = activate_pair(tab, got_1, labels, z_in, norm, act, keeps, slope, both)
    at = expand_pair(found, act, w, z, send, q, high, low, own, share)
    send[:, at : at + 2 * share, :] = low[...]
    put_part(send, at + 2 * share, xz, part)
    marks, label = labels[...], entry(tab, OWN)
    total = group_sum(got, marks, label)
    outer, first = z.shape[2], 2 * LANES
    second = first + w_p.shape[0]
    count = tiled(group_count(marks, label), outer) * (1.0 * z.shape[0] * (COLS - 4))
    mean, rstd = moments(through(total[:, first:second], w_p[...]), total[:, second:], count)
    keeps_p[0:1, :] = mean
    keeps_p[1:2, :] = rstd


def expand_pair(found, act, w, z, send, q, high, low, own, share):
    sums, product, q[...] = found
    pixels = 1.0 * z.shape[0] * (COLS - 4)
    squares = project(act, w, z)
    first = through(sums, w[...])
    second = squares - first * first / pixels
    pair_rows(product, send.shape[0], share, high, low, own)
    put_split(send, 0, sums)
    moved = rows_of(second).astype(BF16)
    send[:, 2 : 2 + moved.shape[0], :] = jnp.broadcast_to(moved[None], (send.shape[0], *moved.shape))
    return 2 + moved.shape[0]


def f4(
    tab, got, labels, zc, zp, norm_c, norm_p, keeps_p, w_c, w, high, q,
    joined, slope, z, send, keeps,
):
    rows, chans = zc.shape[0], zc.shape[2]
    pixels = 1.0 * rows * (COLS - 4)
    mean_c, rstd_c = gathered_moments(got, labels[...], entry(tab, OWN), w_c, pixels)
    mean_p, rstd_p = keeps_p[0:1, :], keeps_p[1:2, :]
    for k, v in enumerate((mean_c, rstd_c, mean_p, rstd_p)):
        keeps[k : k + 1, :] = v
    group = entry(tab, OWN)
    scale_c = rstd_c * gain_of(norm_c, group)
    scale_p = rstd_p * gain_of(norm_p, group)
    bias = (shift_of(norm_c, group) - mean_c * scale_c) + (
        shift_of(norm_p, group) - mean_p * scale_p
    )
    keep = valid_cols(chans)
    scale_c, scale_p, bias = 0.5 * scale_c, 0.5 * scale_p, 0.5 * bias

    def put(i, carry):
        u = zc[i] * scale_c + zp[i] * scale_p + bias
        t = jnp.tanh(u)
        p = u * t
        joined[i] = jnp.where(keep, u + p, 0.0).astype(BF16)
        slope[i] = (0.5 + 0.5 * t) * (1.0 + u - p)
        return carry

    lax.fori_loop(0, rows, put, 0, unroll=7)
    step = rows // 4
    sums, squares = zeros8(LANES), zeros8(LANES)
    for c in range(4):
        values = mm(flat(joined[step * c : step * (c + 1)]), w[...])
        z[step * c : step * (c + 1)] = values.reshape(step, COLS, LANES)
        parts = values.reshape(-1, 8, LANES)
        sums = sums + jnp.sum(parts, axis=0)
        squares = squares + jnp.sum(parts * parts, axis=0)
    put_split(send, 0, stack([down(sums), down(squares)]))
    send[:, 4 : 4 + high.shape[1], :] = high[...]
    put_split(send, 4 + high.shape[1], q[...])


def f5(tab, got, labels, z_in, norm, w_two, w_last, x3, z, send, keeps):
    rows = z_in.shape[0]
    pixels = 1.0 * rows * (COLS - 4)
    marks, label = labels[...], entry(tab, OWN)
    total = over_group(get_split(got, 0, 2), marks, label)
    mean, rstd = moments(total[0:1], total[1:2], group_count(marks, label) * pixels)
    gain, shift = gain_of(norm, label), shift_of(norm, label)
    keeps[0:1, :] = mean
    keeps[1:2, :] = rstd
    scale = rstd * gain
    bias = 0.5 * (shift - mean * scale)
    scale = 0.5 * scale
    keep = valid_cols(LANES) & chan_mask(tab)
    x3[0] = jnp.zeros(x3.shape[1:], BF16)
    x3[rows + 1] = jnp.zeros(x3.shape[1:], BF16)
    n = LANES

    def put(i, carry):
        act = jnp.where(keep, silu_of_half(z_in[i] * scale + bias), 0.0)
        x3[i + 1, :, 0:n] = pltpu.roll(act, 1, 0).astype(BF16)
        x3[i + 1, :, n : 2 * n] = act.astype(BF16)
        x3[i + 1, :, 2 * n : 3 * n] = pltpu.roll(act, COLS - 1, 0).astype(BF16)
        return carry

    lax.fori_loop(0, rows, put, 0, unroll=7)
    lanes = slice(0, 3 * n)
    conv_stats(
        z, x3, (lanes, w_two[...], (0, 1)), (lanes, w_last[...], 2), send
    )


def f6(
    tab, got, labels, z_in, norm, w, xz,
    act, z, send, keeps, slope, q, own, both, high, low, *, share, part,
):
    got_1 = got.at[:, :, 0 : 2 * LANES]
    found = activate_pair(tab, got_1, labels, z_in, norm, act, keeps, slope, both)
    at = expand_pair(found, act, w, z, send, q, high, low, own, share)
    send[:, at : at + 2 * share, :] = high[...]
    send[:, at + 2 * share : at + 4 * share, :] = low[...]
    put_part(send, at + 4 * share, xz, part)


def gathered_moments(got, marks, label, w, pixels):
    devices, chans = got.shape[0], w.shape[1]
    low = stack([got[:, k : k + 1, :].astype(F32).reshape(devices, LANES) for k in (0, 1)])
    means = mm(low.astype(BF16), w[...]) * (1.0 / pixels)
    means = means[0:devices] + means[devices:]
    blocks = chans // LANES
    moments_2 = join(
        [got[:, 2 + k : 3 + k, :].astype(F32).reshape(devices, LANES) for k in range(blocks)]
    )
    same = join([(marks == label).astype(F32).reshape(devices, LANES)] * blocks)
    images = tiled(group_count(marks, label), chans)
    mean = down(means * same) / images
    away = means - mean
    variance = down((moments_2 + pixels * (away * away)) * same) / (images * pixels)
    return mean, lax.rsqrt(variance + EPSILON)


def b7(
    tab, got, labels, joined, z, norm, w, cot, slope_in, z_in, keeps_in, q,
    result, grad_pre, send, keeps, d_in, wide, low, *, share, p_at,
):
    rows, chans = z.shape[0], z.shape[2]
    cols = COLS - 4
    pixels = 1.0 * rows * cols
    marks, label = labels[...], entry(tab, OWN)
    mean, rstd = gathered_moments(got, marks, label, w, pixels)
    gain, shift = gain_of(norm, label), shift_of(norm, label)
    keeps[0:1, :] = mean
    keeps[1:2, :] = rstd
    gate = 0.25 * tiled(entry(tab, GATE), chans)
    scale = 0.5 * rstd * gain * gate
    bias = 0.5 * (shift - mean * rstd * gain) * gate
    wide[:, cols:, :] = jnp.zeros((rows, COLS - cols, chans), F32)
    a_gate = rstd * gain * gate

    def put(i, carry):
        sums, products = carry
        wide[i, 0:cols, :] = cot[i].astype(F32)
        zz = z[i]
        u = 0.5 * joined[i].astype(F32) + zz * scale + bias
        t = jnp.tanh(u)
        p = u * t
        result[i] = (u + p)[0:cols].astype(BF16)
        g = wide[i] * ((0.5 + 0.5 * t) * (1.0 + u - p))
        grad_pre[i] = g
        low[i] = (a_gate * g).astype(BF16)
        return sums + fold(g), products + fold(g * (zz - mean))

    start = zeros8(chans)
    sums, products = lax.fori_loop(0, rows, put, (start, start), unroll=7)
    inner = inner_sums(low, w, slope_in, z_in, keeps_in, d_in)
    blocks = chans // LANES
    put_split(send, 0, rows_of(down(sums) * gate))
    put_split(send, 2 * blocks, rows_of(down(products) * rstd * gate))
    put_split(send, 4 * blocks, stack(inner))
    put_split(send, 4 * blocks + 4, q[...])
    high = got[:, p_at : p_at + 2 * share, :]
    low_p = got[:, p_at + 2 * share : p_at + 4 * share, :]
    pass_pair(send, 4 * blocks + 8, high, low_p, marks, norm.shape[0])


def own_coefs(tab, marks, norm, keeps, pixels, shift_sum, gain_sum):
    group = entry(tab, OWN)
    count = tiled(group_count(marks, group), norm.shape[2]) * pixels
    mean, rstd = keeps[0:1, :], keeps[1:2, :]
    a = rstd * gain_of(norm, group)
    return mean, a, -(a * rstd) * gain_sum / count, -a * shift_sum / count


def wide_lines(total, outer):
    side = outer // 2
    return [join([total[h : h + 1, side * k : side * (k + 1)] for h in (0, 1)]) for k in range(3)]


def norm_tail(labels, got_2c, got_2a, got_1, grad_2c, grad_2a, grad_1c, grad_1p):
    marks = labels[...]
    outer = grad_2c.shape[2]
    blocks = outer // LANES
    for g in range(grad_2c.shape[0]):
        label = float(g)
        rows = [
            line_of(over_group(get_split(got_2c, 2 * blocks * k, blocks), marks, label))
            for k in (0, 1)
        ]
        pair = over_group(get_split(got_2a, 0, 2), marks, label)
        lines = wide_lines(group_sum(got_1, marks, label), outer)
        for out, shift_sum, gain_sum in (
            (grad_2c, rows[0], rows[1]),
            (grad_2a, pair[0:1], pair[1:2]),
            (grad_1c, lines[0], lines[1]),
            (grad_1p, lines[0], lines[2]),
        ):
            out[g, 0:1, :] = gain_sum
            out[g, 1:2, :] = shift_sum


def slope_sums(tab, d, z_in, norm, keeps, dout):
    rows = z_in.shape[0]
    mean, rstd = keeps[0:1, :], keeps[1:2, :]
    group = entry(tab, OWN)
    scale = rstd * gain_of(norm, group)
    bias = 0.5 * (shift_of(norm, group) - mean * scale)
    scale = 0.5 * scale
    keep = valid_cols(LANES) & chan_mask(tab)

    def put(i, carry):
        sums, products = carry
        zz = z_in[i]
        g = jnp.where(keep, d[i] * slope_of_half(zz * scale + bias), 0.0)
        dout[i] = g
        return sums + fold(g), products + fold(g * (zz - mean))

    sums, products = lax.fori_loop(
        0, rows, put, (zeros8(LANES), zeros8(LANES)), unroll=4
    )
    return down(sums), down(products) * rstd


def b9(
    tab, got, labels, norm_c, keeps_c, w_c, got_act, act, slope, d_in, z, norm, keeps,
    b_two, b_last, z_in, norm_in, keeps_in, x_sum, pair_high, pair_low, own_p,
    dz, dout, send, own_sums, d3, d, *, share, p_at,
):
    rows = z.shape[0]
    pixels = 1.0 * rows * (COLS - 4)
    marks, label = labels[...], entry(tab, OWN)
    blocks = norm_c.shape[2] // LANES
    at = 4 * blocks
    wide = [
        line_of(over_group(get_split(got, 2 * blocks * k, blocks), marks, label)) for k in (0, 1)
    ]
    inner = over_group(get_split(got, at, 2), marks, label)
    m, line, (a, b, c), found = pair_solve(
        tab, marks, (norm_c, keeps_c), (norm, keeps), [*wide, inner[0:1], inner[1:2]], w_c,
        get_split(got_act, 0, 1), get_split(got, at + 4, 2),
        got[:, at + 8 : at + 8 + 2 * share, :].astype(F32) + own_p[...], pixels,
    )
    own_sums[0:1, :] = found[0]
    own_sums[1:2, :] = found[1]
    inner_part(act, m, d_in, d)
    mean = keeps[0:1, :]
    keep = valid_cols(LANES)
    n = LANES
    d3[0] = jnp.zeros(d3.shape[1:], BF16)
    d3[rows + 1] = jnp.zeros(d3.shape[1:], BF16)

    def put(i, carry):
        v = a * (slope[i] * (d[i] + line)) + b * (z[i] - mean) + c
        v = jnp.where(keep, v, 0.0)
        d3[i + 1, :, 0:n] = pltpu.roll(v, COLS - 1, 0).astype(BF16)
        low = v.astype(BF16)
        d3[i + 1, :, n : 2 * n] = low
        dz[i] = low
        d3[i + 1, :, 2 * n : 3 * n] = pltpu.roll(v, 1, 0).astype(BF16)
        return carry

    lax.fori_loop(0, rows, put, 0, unroll=7)
    step = rows // 4
    for k in range(4):
        both = mm_nt(flat(d3[step * k : step * (k + 1) + 1]), b_two[...])
        value = mm_nt(flat(d3[step * k + 2 : step * (k + 1) + 2]), b_last[...])
        value = value + both[COLS:, 0:n] + both[0 : step * COLS, n : 2 * n]
        d[step * k : step * (k + 1)] = value.reshape(step, COLS, LANES)
    put_split(send, 0, stack(slope_sums(tab, d, z_in, norm_in, keeps_in, dout)))
    blocks = columns(x_sum.shape[0])
    put_split(send, 4, stack([jnp.transpose(x_sum[lanes, :])[0:1] for lanes in blocks]))
    high, low = pair_high[:, 4 : 4 + 2 * share, :], pair_low[:, p_at : p_at + 2 * share, :]
    pass_pair(send, 4 + 2 * len(blocks), high, low, marks, norm.shape[0])


def b10(
    tab, got, labels, dout_in, z, norm, keeps, w, grad_pre, slope, zc, zp, keeps_cp,
    norm_c, w_c, slope_in, z_in, keeps_in,
    dz, grad_pre_2, send, d_in, d, low,
):
    rows, chans = zc.shape[0], zc.shape[2]
    pixels = 1.0 * rows * (COLS - 4)
    marks = labels[...]
    total = over_group(get_split(got, 0, 2), marks, entry(tab, OWN))
    coefs = own_coefs(tab, marks, norm, keeps, pixels, total[0:1], total[1:2])
    normed_grad(dout_in, (dz, z, *coefs))
    d[...] = mm_nt(flat(dz[...]), w[...]).reshape(d.shape)
    mean_c, rstd_c, mean_p, rstd_p = (keeps_cp[k : k + 1, :] for k in range(4))
    a_c = rstd_c * gain_of(norm_c, entry(tab, OWN))

    def sum_up(i, carry):
        sums, prod_c, prod_p = carry
        g = (grad_pre[i] + d[i]) * slope[i]
        grad_pre_2[i] = g
        low[i] = (a_c * g).astype(BF16)
        return (
            sums + fold(g),
            prod_c + fold(g * (zc[i] - mean_c)),
            prod_p + fold(g * (zp[i] - mean_p)),
        )

    start = zeros8(chans)
    sums, prod_c, prod_p = lax.fori_loop(0, rows, sum_up, (start, start, start), unroll=7)
    wide = [down(sums), down(prod_c) * rstd_c, down(prod_p) * rstd_p]
    inner = inner_sums(low, w_c, slope_in, z_in, keeps_in, d_in)
    parts = [stack([v[:, 0 : chans // 2], v[:, chans // 2 :]]) for v in wide]
    values = join([*parts, stack(inner)])
    send[...] = jnp.broadcast_to(values[None], send.shape)


def inner_sums(low, w, slope, z, keeps, d_in):
    d_in[...] = mm_nt(flat(low[...]), w[...]).reshape(d_in.shape)
    mean, rstd = keeps[0:1, :], keeps[1:2, :]

    def add(i, carry):
        g = slope[i] * d_in[i]
        return carry[0] + fold(g), carry[1] + fold(g * (z[i] - mean))

    sums = lax.fori_loop(0, z.shape[0], add, (zeros8(LANES), zeros8(LANES)), unroll=7)
    return down(sums[0]), down(sums[1]) * rstd


def inner_part(act, m, d_in, d):
    both = mm(flat(act[...]), m)
    d[...] = d_in[...] + (both[:, 0:LANES] + both[:, LANES:]).reshape(d.shape)


def normed_grad(dout, *parts):
    keep = valid_cols(dout.shape[2])

    def put(i, carry):
        g = dout[i]
        for dz, z, mean, a, b, c in parts:
            v = a * g + b * (z[i] - mean) + c
            dz[i] = jnp.where(keep, v, 0.0).astype(BF16)
        return carry

    lax.fori_loop(0, dout.shape[0], put, 0, unroll=7)


def b12(
    tab, own10, labels, norm_c, keeps_c, w_c, got_act, got_q, got_p, own_p, act, slope, d_in,
    z, norm, keeps, xs, d2, kept, sent, own_sums, dz, packed, dout, *, share, q_at, p_at,
):
    rows = z.shape[0]
    pixels = 1.0 * rows * (COLS - 4)
    outer, n = norm_c.shape[2], LANES
    marks = labels[...]
    total = own10[...]
    cuts = (0, outer, 2 * outer, 2 * outer + n, 2 * outer + 2 * n)
    m, line, (a, b, c), found = pair_solve(
        tab, marks, (norm_c, keeps_c.at[0:2]), (norm, keeps),
        [total[:, u:v] for u, v in zip(cuts, cuts[1:])], w_c, get_split(got_act, 0, 1),
        get_split(got_q, q_at, 2),
        got_p[:, p_at : p_at + 2 * share, :].astype(F32) + own_p[...], pixels,
    )
    own_sums[0:1, :] = found[0]
    own_sums[1:2, :] = found[1]
    inner_part(act, m, d_in, dout)
    mean = keeps[0:1, :]
    keep = valid_cols(LANES)
    d2[rows] = jnp.zeros(d2.shape[1:], BF16)

    def put(i, carry):
        v = a * (slope[i] * (dout[i] + line)) + b * (z[i] - mean) + c
        v = jnp.where(keep, v, 0.0)
        low = v.astype(BF16)
        dz[i] = low
        d2[i, :, 0:n] = low
        d2[i, :, n : 2 * n] = pltpu.roll(v, COLS - 1, 0).astype(BF16)
        return carry

    lax.fori_loop(0, rows, put, 0, unroll=7)
    low = flat(dz[...])
    cur = mm_side(flat(xs[1 : rows + 1]), low)
    for k, (y, x) in enumerate(((1, 1), (1, 2), (1, 0), (2, 1), (2, 2), (2, 0))):
        put_rows(packed, n * (3 * y + x), cur[n * k : n * (k + 1)])
    up = mm_side(flat(xs[0:rows, :, 3 * n : 6 * n]), low)
    for k, (y, x) in enumerate(((0, 1), (0, 2), (0, 0))):
        put_rows(packed, n * (3 * y + x), up[n * k : n * (k + 1)])
    share_out(tab, packed, 9 * n, kept, sent)


def b12_images(
    tab, d2, b_even, b_odd, zz, norm_in, keeps_in, dn, sums_out, de, do, wide, *, own
):
    rows = de.shape[0]
    n = LANES
    half = half_of(tab)
    first = rows * (half if own else 1 - half)
    step = rows // 2
    for k in range(2):
        here = flat(d2[pl.ds(first + step * k, step)])
        below = flat(d2[pl.ds(first + step * k + 1, step)])
        de[step * k : step * (k + 1)] = mm_nt(here, b_even[...]).reshape(step, COLS, 2 * n)
        odd = mm_nt(here, b_odd[:, 0 : 2 * n]) + mm_nt(below, b_odd[:, 2 * n : 4 * n])
        do[step * k : step * (k + 1)] = odd.reshape(step, COLS, 2 * n)
    mean_1, rstd_1 = keeps_in[0:1, :], keeps_in[1:2, :]
    group = entry(tab, OWN)
    scale = rstd_1 * gain_of(norm_in, group)
    bias = 0.5 * (shift_of(norm_in, group) - mean_1 * scale)
    scale = 0.5 * scale
    keep = valid_cols(LANES) & chan_mask(tab)

    def emit(i, carry):
        sums, products = carry
        for ra in (0, 1):
            planes = (de, do)[ra]
            for cb in (0, 1):
                zv = zz[2 * i + ra, pl.ds(cb, COLS, stride=2), :]
                g = planes[i, :, n * cb : n * (cb + 1)] * slope_of_half(zv * scale + bias)
                g = jnp.where(keep, g, 0.0)
                sums = sums + fold(g)
                products = products + fold(g * (zv - mean_1))
                wide[2 * i + ra, pl.ds(cb, COLS, stride=2), :] = g
            dn[2 * i + ra] = wide[2 * i + ra].astype(BF16)
        return sums, products

    totals = lax.fori_loop(0, rows, emit, (zeros8(n), zeros8(n)), unroll=7)
    sums_out[0:1, :] = down(totals[0])
    sums_out[1:2, :] = down(totals[1]) * rstd_1


def b13(
    tab, got, labels, norm, keeps, w, z_own, z_for, dn_own, dn_for, gs_own, gs_for, *rest, at, held
):
    finished, outs = rest[:held], rest[held : 2 * held]
    grad, grad_norm, dz, wide, grad_v, norm_v, sems = rest[2 * held :]
    copies = [
        pltpu.make_async_copy(a, b, sems.at[k]) for k, (a, b) in enumerate(zip(finished, outs))
    ]
    for copy in copies:
        copy.start()
    rows, cols = grad.shape[1], grad.shape[2]
    half = half_of(tab)
    pixels = 2.0 * rows * cols
    marks = labels[...]
    totals = last_sums(got.at[:, at : at + 4, :], marks, norm.shape[0])
    for g in range(norm.shape[0]):
        norm_v[g, 0:1, :] = totals[g][1]
        norm_v[g, 1:2, :] = totals[g][0]
    copies.append(pltpu.make_async_copy(norm_v, grad_norm, sems.at[held]))
    copies[-1].start()
    keep = lax.broadcasted_iota(jnp.int32, (z_own.shape[1], LANES), 0) < cols
    for k, (z, dn, gs) in enumerate(((z_own, dn_own, gs_own), (z_for, dn_for, gs_for))):
        group = entry(tab, OWN if k == 0 else OTHER)
        shift_sum = own_of([t[0] for t in totals], group)
        gain_sum = own_of([t[1] for t in totals], group)
        count = group_count(marks, group) * pixels
        mean, rstd = keeps[2 * k : 2 * k + 1, :], keeps[2 * k + 1 : 2 * k + 2, :]
        a = rstd * gain_of(norm, group)
        b = -(a * rstd) * gain_sum / count
        c = -a * shift_sum / count

        def put(i, carry, z=z, dn=dn, mean=mean, a=a, b=b, c=c):
            v = a * dn[i].astype(F32) + b * (z[i] - mean) + c
            dz[i] = jnp.where(keep, v, 0.0).astype(BF16)
            return carry

        lax.fori_loop(0, rows, put, 0, unroll=7)
        place = half if k == 0 else 1 - half
        step = rows // 2
        for q in range(2):
            low = flat(dz[step * q : step * (q + 1)])
            for p in range(wide.shape[0]):
                values = mm_nt(low, w[LANES * p : LANES * (p + 1), :])
                wide[p, step * q : step * (q + 1)] = values.reshape(step, -1, LANES)

            def emit(i, carry, gs=gs, place=place):
                even = pl.ds(0, COLS, stride=2)
                for p in range(wide.shape[0]):
                    lanes = slice(LANES * p, LANES * (p + 1))
                    wide[p, 2 * i, even, :] = wide[p, 2 * i, even, :] + gs[i, :, lanes].astype(F32)
                    grad_v[place, 2 * i, :, lanes] = wide[p, 2 * i, 0:cols, :].astype(BF16)
                    grad_v[place, 2 * i + 1, :, lanes] = wide[p, 2 * i + 1, 0:cols, :].astype(BF16)
                return carry

            lax.fori_loop(step // 2 * q, step // 2 * (q + 1), emit, 0, unroll=True)
            part = pl.ds(step * q, step)
            copies.append(
                pltpu.make_async_copy(
                    grad_v.at[place, part], grad.at[place, part], sems.at[held + 1 + 2 * k + q]
                )
            )
            copies[-1].start()
    for copy in copies:
        copy.wait()


def put_rows(out, at, value):
    for j in range(value.shape[1] // LANES):
        out[at : at + value.shape[0], :] = value[:, LANES * j : LANES * (j + 1)].astype(BF16)
        at += value.shape[0]
    return at


def take_rows(source, at, out):
    rows = out.shape[0]
    for j in range(out.shape[1] // LANES):
        out[:, LANES * j : LANES * (j + 1)] = source(at, rows)
        at += rows
    return at


def share_out(tab, packed, used, kept, sent):
    if used < packed.shape[0]:
        packed[used:, :] = jnp.zeros((packed.shape[0] - used, LANES), BF16)
    half = half_of(tab)
    size = kept.shape[0] * kept.shape[1]
    for out, place in ((kept, half), (sent, 1 - half)):
        out[...] = packed[pl.ds(pl.multiple_of(size * place, 16), size), :].reshape(out.shape)


def g_most(
    tab, act_2b, x3, dz_2b, joined, dz_2a, act_1b, xee,
    got, labels, norm_c, norm_p, keeps, grad_pre_2, zc, zp,
    got_2c, norm_2c, keeps_2c, grad_pre, z_2c,
    kept, sent, dz_p, own10, packed, dz_1c, dz_2c,
):
    rows, outer = dz_2b.shape[0], zc.shape[2]
    pixels = 1.0 * rows * (COLS - 4)
    marks, label = labels[...], entry(tab, OWN)
    blocks = outer // LANES
    total = group_sum(got, marks, label)
    lines = wide_lines(total, outer)
    for k in range(2):
        own10[:, outer * k : outer * (k + 1)] = lines[k]
        at = 2 * outer + LANES * k
        own10[:, at : at + LANES] = total[k : k + 1, 3 * outer // 2 :]
    wide = [
        line_of(over_group(get_split(got_2c, 2 * blocks * k, blocks), marks, label)) for k in (0, 1)
    ]
    mean, a, b, c = own_coefs(tab, marks, norm_2c, keeps_2c, pixels, *wide)
    gate = 0.25 * tiled(entry(tab, GATE), outer)
    normed_grad(grad_pre, (dz_2c, z_2c, mean, a * gate, b, c))
    coefs_c = own_coefs(tab, marks, norm_c, keeps.at[0:2], pixels, lines[0], lines[1])
    coefs_p = own_coefs(tab, marks, norm_p, keeps.at[2:4], pixels, lines[0], lines[2])
    normed_grad(grad_pre_2, (dz_1c, zc, *coefs_c), (dz_p, zp, *coefs_p))
    at = put_rows(packed, 0, mm_tn(flat(act_2b[...]), flat(dz_2c[...])))
    low = flat(dz_2b[...])
    for y in range(3):
        at = put_rows(packed, at, mm_side(flat(x3[y : y + rows]), low))
    at = put_rows(packed, at, mm_side(flat(joined[...]), flat(dz_2a[...])))
    at = put_rows(packed, at, mm_tn(flat(act_1b[...]), flat(dz_1c[...])))
    at = put_rows(packed, at, mm_tn(flat(xee[...]), flat(dz_p[...])))
    share_out(tab, packed, at, kept, sent)


def strided_grad(tab, dz_p, w_p, gs_own, gs_oth):
    half = half_of(tab)
    count = gs_own.shape[0]
    for k, gs in enumerate((gs_own, gs_oth)):
        first = count * (half if k == 0 else 1 - half)
        got = mm_nt(flat(dz_p[pl.ds(first, count)]), w_p[...])
        gs[...] = got.reshape(gs.shape).astype(BF16)


def g_xz(keeps, x_own, x_oth, z_own, z_oth, out, x_sum, low, tall):
    rows, n = z_own.shape[0], LANES
    mean = keeps[0:1, :]
    low[:, :, n : 2 * n] = jnp.ones((rows, z_own.shape[1], n), BF16)
    value = None
    for x, z in ((x_own, z_own), (x_oth, z_oth)):

        def put(i, carry, z=z):
            low[i, :, 0:n] = (z[i] - mean).astype(BF16)
            return carry

        lax.fori_loop(0, rows, put, 0, unroll=7)
        term = mm_tn(flat(x[...]), flat(low[...]))
        value = term if value is None else value + term
    at = value.shape[0]
    tall[0:at, :] = value[:, 0:n]
    if at < tall.shape[0]:
        tall[at:, :] = jnp.zeros((tall.shape[0] - at, n), F32)
    out[...] = tall[...].reshape(out.shape).astype(BF16)
    x_sum[...] = value[:, n : 2 * n]


def g_xd(
    tab, sums_own, sums_oth, norm, keeps, x_sum, got_x, labels, x_own, x_oth, dn_own, dn_oth,
    z_own, z_oth, out, sums, low,
):
    rows = dn_own.shape[0]
    n = LANES
    pixels = 1.0 * (2 * rows) * (2 * (COLS - 4))
    sums[...] = sums_own[...] + sums_oth[...]
    a = keeps[1:2, :] * gain_of(norm, entry(tab, OWN))
    local = sums[0:1, :] / pixels
    mean = keeps[0:1, :]
    b = -(a * keeps[1:2, :]) * sums[1:2, :] / pixels
    value = None
    for x, dn, z in ((x_own, dn_own, z_own), (x_oth, dn_oth, z_oth)):

        def put(i, carry, dn=dn, z=z):
            low[i] = (a * (dn[i].astype(F32) - local) + b * (z[i] - mean)).astype(BF16)
            return carry

        lax.fori_loop(0, rows, put, 0, unroll=7)
        term = mm_tn(flat(low[...]), flat(x[...]))
        value = term if value is None else value + term
    value = stack([jnp.transpose(value[:, lanes]) for lanes in columns(value.shape[1])])
    marks, label = labels[...], entry(tab, OWN)
    total = over_group(get_split(got_x, 4, x_sum.shape[0] // n), marks, label)
    total = join([total[k : k + 1] for k in range(total.shape[0])])
    total = total / tiled(group_count(marks, label), total.shape[1])
    total = jnp.broadcast_to(total, (8, total.shape[1]))
    means = jnp.concatenate(
        [jnp.transpose(total[:, lanes])[:, 0:1] for lanes in columns(total.shape[1])], axis=0
    )
    value = value + (x_sum[...] - means) * (a * local)
    at = value.shape[0]
    out[0:at, :] = value.astype(BF16)
    if at < out.shape[0]:
        out[at:, :] = jnp.zeros((out.shape[0] - at, n), BF16)


def pack_last(tall, sums, kept, got, kept_1b, got_1b, xz, send, *, stats_at, part):
    n = LANES
    devices = send.shape[0]
    piece, share = kept.shape[1], tall.shape[0] // devices
    first = kept.shape[0]
    second = first + kept_1b.shape[0]
    send[0:first, 0:piece, :] = (kept[...].astype(F32) + got[...].astype(F32)).astype(BF16)
    send[first:second, 0:piece, :] = (kept_1b[...].astype(F32) + got_1b[...].astype(F32)).astype(BF16)
    if second < devices:
        send[second:, 0:piece, :] = jnp.zeros((devices - second, piece, n), BF16)
    send[:, piece : piece + share, :] = tall[...].reshape(devices, share, n)
    put_split(send, stats_at, sums[...])
    put_part(send, stats_at + 4, xz, part)


def last_sums(stats, marks, groups):
    values = stats[:, 0:2, :].astype(F32) + stats[:, 2:4, :].astype(F32)
    out = []
    for g in range(groups):
        total = jnp.sum(values * (marks == float(g)).astype(F32), axis=0)
        out.append((total[0:1], total[1:2]))
    return out


def add_all(
    got, labels, norm, keeps_all, got_a, got_b, found_2b, found_1b, out, *, at, pixels, parts
):
    devices, n = got.shape[0], LANES
    half = devices // 2
    share = parts[-1][2]
    piece = (out.shape[1] - share - 8) // 2
    marks = labels[...]
    value = jnp.sum(got[:, piece : piece + share, :].astype(F32), axis=0)
    products = get_split(got, at, 2)[:, 1:2, :]
    lack = jnp.zeros(products.shape, F32)
    for g in range(norm.shape[0]):
        rstd = keeps_all[2 * g + 1 : 2 * g + 2, :]
        factor = -(rstd * rstd * norm[g, 0:1, :]) / pixels
        same = (marks == float(g)).astype(F32)
        middle = jnp.sum(products * same, axis=0) / jnp.sum(same, axis=0)
        lack = lack + (middle[None] - products) * (factor[None] * same)
    rows = [
        jnp.sum(source[:, start : start + last - first, :].astype(F32) * lack, axis=0)
        for source, (start, first, last) in zip((got_a, got_b, got), parts)
        if last > first
    ]
    value = value + jnp.concatenate(rows, axis=0)
    for k in (0, 1):
        total = jnp.sum(got[half * k : half * (k + 1), 0:piece, :].astype(F32), axis=0).astype(BF16)
        out[:, piece * k : piece * (k + 1), :] = jnp.broadcast_to(
            total[None], (out.shape[0], piece, n)
        )
    out[:, 2 * piece : 2 * piece + share, :] = jnp.broadcast_to(
        value.astype(BF16)[None], (out.shape[0], share, n)
    )
    put_split(out, 2 * piece + share, stack([found_2b[...], found_1b[...]]))


def place_parts(minor, major, parts, packed, tall, found, piece):
    far, share = parts[0].shape[0], tall.shape[1]
    for k, part in enumerate(parts):
        base = lax.bitwise_xor(minor, jnp.int32(k))

        def place(z, carry, part=part, base=base):
            owner = base + NEAR * lax.bitwise_xor(major, jnp.int32(z))
            for h in (0, 1):
                packed[h, owner] = part[z, piece * h : piece * (h + 1), :]
            tall[owner] = part[z, 2 * piece : 2 * piece + share, :].astype(F32)
            sums = part[z, 2 * piece + share :, :].astype(F32)
            found[owner] = sums[0:4] + sums[4:8]
            return carry

        lax.fori_loop(0, far, place, 0, unroll=min(far, 4))


def stack_parts(*refs):
    for k, ref in enumerate(refs[:-1]):
        refs[-1][k] = ref[0]


def unpack_own(tab, *refs, piece):
    place_parts(half_of(tab, MINOR), half_of(tab, MAJOR), refs[:NEAR], *refs[NEAR:], piece)


def unpack(tab, labels, packed_own, tall_own, found_own, *refs, first, second, piece):
    parts, outs, values = refs[:NEAR], refs[NEAR : NEAR + 9], refs[NEAR + 9 :]
    *values, packed_oth, tall_oth, found_oth, sems = values
    place_parts(half_of(tab, MINOR), half_of(tab, MAJOR), parts, packed_oth, tall_oth, found_oth, piece)
    half = half_of(tab)
    copies = [
        pltpu.make_async_copy(value, out, sems.at[k]) for k, (value, out) in enumerate(zip(values, outs))
    ]
    w_1b, w_1a, *grad_norms = values[5:9]
    own, oth = (packed_own, tall_own, found_own), (packed_oth, tall_oth, found_oth)
    for core in (0, 1):

        @pl.when(half == core)
        def _():
            packed, tall, found = zip(*((own, oth) if core == 0 else (oth, own)))
            most, last = [], []
            for h in (0, 1):
                pieces = [flat(v[h]) for v in packed]
                middle = pieces[0].shape[0]
                cut = first * piece
                most.append((pieces, middle))
                last.append((cut, pieces, middle))

            def span(pieces, middle, at, rows):
                found_rows = []
                if at < middle:
                    found_rows.append(pieces[0][at : min(at + rows, middle)])
                if at + rows > middle:
                    found_rows.append(pieces[1][max(at - middle, 0) : at + rows - middle])
                return [v.astype(F32) for v in found_rows]

            size = first * piece

            def source(at, rows):
                out = []
                if at < size:
                    out += span(*most[0], at, min(rows, size - at))
                if at + rows > size:
                    start = max(at - size, 0)
                    out += span(*most[1], start, at + rows - size - start)
                return out[0] if len(out) == 1 else stack(out)

            starts = [0]
            for value in values[0:4]:
                starts.append(starts[-1] + value.shape[0] * value.shape[1] // LANES)
            for k in (1, 4):
                take_rows(source, starts[k], values[k])
                copies[k].start()
            left = w_1b.shape[0]
            for k, (cut, pieces, middle) in enumerate(last):
                rows = min(second * piece, left)
                lines = span(pieces, middle, cut, rows)
                start = second * piece * k
                w_1b[start : start + rows, :] = lines[0] if len(lines) == 1 else stack(lines)
                left -= rows
            copies[5].start()
            for k in (0, 2, 3):
                take_rows(source, starts[k], values[k])
                copies[k].start()
            lines = stack([flat(v[...]) for v in tall])
            w_1a[...] = lines[0 : w_1a.shape[0]]
            copies[6].start()
            sums = jnp.concatenate([v[...] for v in found], axis=0)
            for k, grad_norm in enumerate(grad_norms):
                norm_from_owners(sums[:, 2 * k : 2 * k + 2, :], labels[...], grad_norm)
                copies[7 + k].start()

    for copy in copies:
        copy.wait()


def norm_from_owners(found, marks, grad_norm):
    for g in range(grad_norm.shape[0]):
        total = over_group(found, marks, float(g)) / group_count(marks, float(g))
        grad_norm[g, 0:1, :] = total[1:2]
        grad_norm[g, 1:2, :] = total[0:1]


def gather(send):
    return lax.all_to_all(send, AXES, 0, 0)


def tie(*values):
    return lax.optimization_barrier(values)


def swap(block):
    return lax.ppermute(block, "rows", [(0, 1), (1, 0)])


def body(
    images, w_1a, w_1b, w_1c, w_1p, w_2a, w_2b, w_2c,
    norm_1a, norm_1b, norm_1c, norm_1p, norm_2a, norm_2b, norm_2c,
    cotangent, group, width, gate,
):
    devices = lax.axis_size("rows") * lax.axis_size("batch")
    place = lax.axis_index(AXES).astype(jnp.int32).reshape(1)
    norms = (norm_1a, norm_1b, norm_1c, norm_1p, norm_2a, norm_2b, norm_2c)
    norm_1a, norm_1b, norm_1c, norm_1p, norm_2a, norm_2b, norm_2c = (
        v.transpose(1, 0, 2) for v in norms
    )
    outer, inputs = w_1c.shape[1], w_1a.shape[0]
    rows = cotangent.shape[1]
    cols_in = 2 * COLS
    n, m = LANES, devices

    def send(stats, channels=LANES):
        return ((m, channels // LANES, stats * LANES), F32)

    def maps(channels, dtype=F32):
        return ((rows, COLS, channels), dtype)

    def scratch(channels, dtype=F32):
        return pltpu.VMEM((rows, COLS, channels), dtype)

    def params(*arrays):
        return [(a.shape, F32) for a in arrays]

    def mean_scale(channels, count=1):
        return ((2 * count, channels), F32)

    wide_in = ((rows, cols_in, inputs), BF16)
    wide_z = ((rows, cols_in, n), F32)
    raw = images.shape
    tab, x_own, x_for, z_own, z_for, s1 = stage(
        functools.partial(f1, batch=devices // 2), [((8, n), F32), wide_in, wide_in, wide_z, wide_z, send(5)],
        [*(pltpu.SMEM(v.shape, jnp.int32) for v in (place, group, width, gate)),
         pltpu.VMEM(raw, BF16), pltpu.VMEM(w_1a.shape, BF16), pltpu.VMEM((8, n), F32),
         pltpu.SemaphoreType.DMA((9,))],
        hbm=(0, 1, 2, 3, 4, 5),
    )(place, group, width, gate, images, w_1a)
    s1, v_1b, v_2b = tie(s1, w_1b, w_2b)
    built = stage(
        prepare,
        [(v, BF16) for v in (
            (3 * n, n), (3 * n, 2 * n), (3 * n, 2 * n), (3 * n, n),
            (2 * n, 2 * n), (2 * n, 4 * n), (2 * n, 3 * n), (n, 3 * n),
        )],
    )(v_1b, v_2b)
    s1, x_for, w_even, w_odd, w_two, w_last, b_even, b_odd, b_two, b_last = tie(s1, x_for, *built)
    x_oth = swap(x_for)
    g1 = gather(s1)
    g1, x_oth = tie(g1, x_oth)
    xee, z_1p, stats_1p = stage(
        f1_strided,
        [maps(inputs, BF16), maps(outer), ((1, inputs + outer), F32)],
        [pltpu.VMEM((inputs // n, rows // 2, cols_in, n), F32)],
    )(tab, x_own, x_oth, w_1p)
    xs, z_1b, s2, labels, k_1a, k_all, z_oth = stage(
        f2,
        [((rows + 1, COLS, 6 * n), BF16), maps(n), send(2 + (inputs + outer) // n),
         ((m, 1, n), F32), mean_scale(n, 2), mean_scale(n, norm_1a.shape[0]), wide_z],
    )(tab, g1, z_own, x_oth, w_1a, norm_1a, w_even, w_odd, stats_1p)
    share = -(-inputs // devices)
    half_in = ((rows, cols_in, n), BF16)
    xz, x_sum = stage(
        g_xz, [((devices, share, n), BF16), ((inputs, n), F32)],
        [pltpu.VMEM((rows, cols_in, 2 * n), BF16), pltpu.VMEM((devices * share, n), F32)],
    )(k_1a, x_own, x_oth, z_own, z_oth)
    s2, xz, x_sum = tie(s2, xz, x_sum)
    g2 = gather(s2)
    share_1 = -(-n // devices)
    p_rows = ((devices, 2 * share_1, n), BF16)
    own_rows = ((devices, 2 * share_1, n), F32)
    wide_rows = outer // n
    p_at = 2 + wide_rows
    xz_3 = p_at + 2 * share_1
    high_3 = -(-xz_3 // 16) * 16
    xz_6 = p_at + 4 * share_1
    high_6 = -(-xz_6 // 8) * 8
    cut_3 = min(share, high_3 - xz_3)
    cut_6 = min(share, cut_3 + high_6 - xz_6)
    act_1b, z_1c, s3, k_1b, k_p, slope_1b, q_1b, p_1b, own_1b = stage(
        functools.partial(f3, share=share_1, part=(0, cut_3)),
        [maps(n, BF16), maps(outer), ((devices, high_3, n), BF16), mean_scale(n),
         mean_scale(outer), maps(n), ((2, n), F32), p_rows, own_rows],
        [scratch(4 * n, BF16), pltpu.VMEM(p_rows[0], BF16)],
    )(tab, g2, labels, z_1b, norm_1b, w_1c, w_1p, xz)
    g3 = gather(s3)
    high = -(-(8 + 2 * share_1) // 16) * 16
    joined, slope, z_2a, s4, k_cp = stage(
        f4,
        [maps(outer, BF16), maps(outer), maps(n), ((devices, high, n), BF16),
         mean_scale(outer, 2)],
    )(tab, g3, labels, z_1c, z_1p, norm_1c, norm_1p, k_p, w_1c, w_2a, p_1b, q_1b)
    g4 = gather(s4)
    x3, z_2b, s5, k_2a = stage(
        f5, [((rows + 2, COLS, 3 * n), BF16), maps(n), send(2), mean_scale(n)]
    )(tab, g4, labels, z_2a, norm_2a, w_two, w_last)
    g5 = gather(s5)
    act_2b, z_2c, s6, k_2b, slope_2b, q_2b, own_2b = stage(
        functools.partial(f6, share=share_1, part=(cut_3, cut_6)),
        [maps(n, BF16), maps(outer), ((devices, high_6, n), BF16), mean_scale(n), maps(n),
         ((2, n), F32), own_rows],
        [scratch(4 * n, BF16), *(pltpu.VMEM(p_rows[0], BF16) for _ in range(2))],
    )(tab, g5, labels, z_2b, norm_2b, w_2c, xz)
    g6 = gather(s6)
    high_7 = -(-(4 * wide_rows + 8 + 2 * share_1) // 16) * 16
    result, grad_pre, s7, k_2c, d_2b = stage(
        functools.partial(b7, share=share_1, p_at=p_at),
        [(cotangent.shape[1:], BF16), maps(outer), ((devices, high_7, n), BF16),
         mean_scale(outer), maps(n)],
        [scratch(outer), scratch(outer, BF16)],
    )(tab, g6, labels, joined, z_2c, norm_2c, w_2c, cotangent[0], slope_2b, z_2b, k_2b, q_2b)
    g7 = gather(s7)
    dz_2b, dout_2a, s9, found_2b = stage(
        functools.partial(b9, share=share_1, p_at=p_at),
        [maps(n, BF16), maps(n), ((devices, high, n), BF16), ((2, n), F32)],
        [pltpu.VMEM((rows + 2, COLS, 3 * n), BF16), scratch(n)],
    )(tab, g7, labels, norm_2c, k_2c, w_2c, g6, act_2b, slope_2b, d_2b, z_2b, norm_2b, k_2b,
      b_two, b_last, z_2a, norm_2a, k_2a, x_sum, g4, g3, own_2b)
    g9 = gather(s9)
    dz_2a, grad_pre_2, s10, d_1b = stage(
        b10,
        [maps(n, BF16), maps(outer), ((devices, 2, 3 * outer // 2 + n), F32), maps(n)],
        [scratch(outer), scratch(outer, BF16)],
    )(tab, g9, labels, dout_2a, z_2a, norm_2a, k_2a, w_2a, grad_pre, slope, z_1c, z_1p, k_cp,
      norm_1c, w_1c, slope_1b, z_1b, k_1b)
    g10 = gather(s10)
    half_map = ((rows // 2, COLS, inputs), BF16)
    most_rows = sum(v.size for v in (w_2c, w_2b, w_2a, w_1c, w_1p)) // n
    rows_1b = w_1b.size // n
    piece = 16
    while -(-most_rows // (2 * piece)) - (-rows_1b // (2 * piece)) > devices:
        piece += 16
    first, second = -(-most_rows // (2 * piece)), -(-rows_1b // (2 * piece))
    part, part_1b = ((first, piece, n), BF16), ((second, piece, n), BF16)
    kept, sent, dz_1p, own10 = stage(
        g_most,
        [part, part, maps(outer, BF16), ((1, 2 * outer + 2 * n), F32)],
        [pltpu.VMEM((2 * first * piece, n), BF16), *(scratch(outer, BF16) for _ in range(2))],
    )(tab, act_2b, x3, dz_2b, joined, dz_2a, act_1b, xee,
      g10, labels, norm_1c, norm_1p, k_cp, grad_pre_2, z_1c, z_1p,
      g7, norm_2c, k_2c, grad_pre, z_2c)
    gs_own, gs_send = stage(strided_grad, [half_map, half_map])(tab, dz_1p, w_1p)
    got, gs_for = swap(sent), swap(gs_send)
    half_in = ((rows, cols_in, n), BF16)
    d2, kept_1b, sent_1b, found_1b = stage(
        functools.partial(b12, share=share_1, q_at=4 + 2 * share_1, p_at=4 + 2 * (inputs // n)),
        [((rows + 1, COLS, 2 * n), BF16), part_1b, part_1b, ((2, n), F32)],
        [scratch(n, BF16), pltpu.VMEM((2 * second * piece, n), BF16), scratch(n)],
    )(tab, own10, labels, norm_1c, k_cp, w_1c, g3, g4, g9, own_1b, act_1b, slope_1b, d_1b,
      z_1b, norm_1b, k_1b, xs)
    got_1b = swap(sent_1b)
    sides = []
    for own, z in ((False, z_oth), (True, z_own)):
        sides.append(
            stage(
                functools.partial(b12_images, own=own), [half_in, ((2, n), F32)],
                [pltpu.VMEM((rows // 2, COLS, 2 * n), F32), pltpu.VMEM((rows // 2, COLS, 2 * n), F32),
                 pltpu.VMEM((rows, cols_in, n), F32)],
            )(tab, d2, b_even, b_odd, z, norm_1a, k_1a)
        )
        if not own:
            dn_for = swap(sides[0][0])
            d2, _ = tie(d2, sides[0][0])
    (dn_send, sums_send), (dn_own, sums_own) = sides
    stats_at = piece + -(-share // 8) * 8
    high = -(-(stats_at + 4 + share - cut_6) // 16) * 16
    tall, sums_1a = stage(
        g_xd, [((devices * share, n), BF16), ((2, n), F32)], [pltpu.VMEM(half_in[0], BF16)]
    )(tab, sums_own, sums_send, norm_1a, k_1a, x_sum, g9, labels, x_own, x_oth, dn_own, dn_send,
      z_own, z_oth)
    tall, gs_for, dn_for = tie(tall, gs_for, dn_for)
    (s12,) = stage(
        functools.partial(pack_last, stats_at=stats_at, part=(cut_6, share)),
        [((devices, high, n), BF16)]
    )(tall, sums_1a, kept, got, kept_1b, got_1b, xz)
    g12 = gather(s12)
    pixels = 4.0 * images.shape[1] * images.shape[1]
    batch = devices // 2
    far = batch // NEAR
    (mine,) = stage(
        functools.partial(
            add_all, at=stats_at, pixels=pixels,
            parts=((xz_3, 0, cut_3), (xz_6, cut_3, cut_6), (stats_at + 4, cut_6, share)),
        ),
        [((1, 2 * piece + share + 8, n), BF16)],
    )(g12, labels, norm_1a, k_all, g3, g6, found_2b, found_1b)
    others = [
        lax.ppermute(mine, "batch", [(i, i ^ (NEAR * k)) for i in range(batch)])
        for k in range(1, far)
    ]
    late, _ = tie(labels, mine)
    grad_norms = stage(norm_tail, params(norm_2c, norm_2a, norm_1c, norm_1p))(late, g7, g9, g10)
    finished = (result, *grad_norms)
    held = len(finished)
    *finished, grad_images, grad_norm_1a = stage(
        functools.partial(b13, at=stats_at, held=held),
        [*((v.shape, v.dtype) for v in finished), (images.shape, BF16), *params(norm_1a)],
        [pltpu.VMEM(half_in[0], BF16), pltpu.VMEM((inputs // n, rows, cols_in, n), F32),
         pltpu.VMEM(images.shape, BF16), pltpu.VMEM(norm_1a.shape, F32),
         pltpu.SemaphoreType.DMA((held + 5,))],
        hbm_out=range(held + 2),
    )(tab, g12, labels, norm_1a, k_1a, w_1a, z_own, z_for, dn_own, dn_for, gs_own, gs_for, *finished)
    result, grad_norm_2c, grad_norm_2a, grad_norm_1c, grad_norm_1p = finished
    *others, grad_images = tie(*others, grad_images)
    (along,) = stage(stack_parts, [((far, *mine.shape[1:]), BF16)])(mine, *others)
    near = [
        lax.ppermute(along, "batch", [(i, i ^ k) for i in range(batch)]) for k in range(1, NEAR)
    ]
    parts = [along, *near]
    weights = (w_2c, w_2b.reshape(-1, n), w_2a, w_1c, w_1p, w_1b.reshape(-1, n), w_1a)
    side = [
        ((2, batch, piece, n), BF16), ((batch, share, n), F32), ((batch, 4, n), F32)
    ]
    crossed = [swap(v) for v in parts]
    placed = stage(functools.partial(unpack_own, piece=piece), side)(tab, *parts)
    t_2c, t_2b, t_2a, t_1c, t_1p, t_1b, t_1a, grad_norm_2b, grad_norm_1b = stage(
        functools.partial(unpack, first=first, second=second, piece=piece),
        [(v.shape, F32) for v in (*weights, norm_2b, norm_1b)],
        [*(pltpu.VMEM(v.shape, F32) for v in (*weights, norm_2b, norm_1b)),
         *(pltpu.VMEM(*v) for v in side), pltpu.SemaphoreType.DMA((9,))],
        hbm_out=range(9),
    )(tab, labels, *placed, *crossed)
    grads = (
        grad_norm_1a, grad_norm_1b, grad_norm_1c, grad_norm_1p,
        grad_norm_2a, grad_norm_2b, grad_norm_2c,
    )
    return (
        result[None], grad_images, t_1a, t_1b.reshape(w_1b.shape), t_1c, t_1p, t_2a,
        t_2b.reshape(w_2b.shape), t_2c, *[v.transpose(1, 0, 2) for v in grads],
    )


def solution(mesh):
    return jax.shard_map(
        body,
        mesh=mesh,
        in_specs=(
            P("batch", "rows", None, None),
            *[P()] * 14,
            P(("batch", "rows"), None, None, None),
            P("batch"),
            P(),
            P(),
        ),
        out_specs=(
            P(("batch", "rows"), None, None, None),
            P("batch", "rows", None, None),
            *[P()] * 14,
        ),
        check_vma=False,
    )
```

```python
import functools

import jax
import jax.numpy as jnp
from jax import lax
from jax.experimental import pallas as pl
from jax.experimental.pallas import tpu as pltpu
from jax.sharding import PartitionSpec as P

EPSILON = 1e-05
F32 = jnp.float32
BF16 = jnp.bfloat16
AXES = ("rows", "batch")
VMEM_LIMIT = 14 * 1024 * 1024
LANES = 128
COLS = 32
NEAR = 4


def full(memory=pltpu.VMEM):
    return pl.BlockSpec(memory_space=memory)


def stage(kernel, outs, scratch=(), hbm=(), hbm_out=()):
    def place(i, outside):
        return pltpu.HBM if i in outside else pltpu.VMEM

    def call(*args):
        args = [
            pltpu.with_memory_space_constraint(a, pltpu.HBM) if i in hbm else a
            for i, a in enumerate(args)
        ]
        return pl.pallas_call(
            kernel,
            out_shape=tuple(jax.ShapeDtypeStruct(s, d) for s, d in outs),
            in_specs=[full(place(i, hbm)) for i in range(len(args))],
            out_specs=tuple(
                full(place(i, hbm_out)) for i in range(len(outs))
            ),
            scratch_shapes=list(scratch),
            compiler_params=pltpu.CompilerParams(vmem_limit_bytes=VMEM_LIMIT),
            name=(kernel.func if isinstance(kernel, functools.partial) else kernel).__name__,
        )(*args)

    return call


def silu_of_half(u):
    return u + u * jnp.tanh(u)


def slope_of_half(u):
    t = jnp.tanh(u)
    return (0.5 + 0.5 * t) * (1.0 + u - u * t)


def fold(x):
    return (x[0:8] + x[8:16]) + (x[16:24] + x[24:32])


def row(total, stat):
    blocks = total.shape[0]
    pieces = [total[j : j + 1, LANES * stat : LANES * (stat + 1)] for j in range(blocks)]
    return pieces[0] if blocks == 1 else jnp.concatenate(pieces, axis=1)


def spread(out_ref, rows):
    blocks = out_ref.shape[1]
    for stat, values in enumerate(rows):
        for j in range(blocks):
            piece = values[:, LANES * j : LANES * (j + 1)]
            out_ref[:, j : j + 1, LANES * stat : LANES * (stat + 1)] = jnp.broadcast_to(
                piece[None], (out_ref.shape[0], 1, LANES)
            )


def group_sum(got_ref, labels, label):
    same = (labels == label).astype(F32)
    stats = got_ref.shape[2] // LANES
    parts = [
        jnp.sum(got_ref[:, :, LANES * s : LANES * (s + 1)] * same, axis=0) for s in range(stats)
    ]
    return jnp.concatenate(parts, axis=1) if stats > 1 else parts[0]


def group_count(labels, label):
    return jnp.sum((labels == label).astype(F32), axis=0)


def tiled(values, channels):
    return jnp.concatenate([values] * (channels // LANES), axis=1) if channels > LANES else values


def moments(first, second, pixels):
    mean = first / pixels
    return mean, lax.rsqrt(second / pixels - mean * mean + EPSILON)


def own_of(values, label):
    out = values[0]
    label = tiled(label, out.shape[1])
    for g in range(1, len(values)):
        out = jnp.where(label == float(g), values[g], out)
    return out


def gain_of(norm_ref, label):
    return own_of([norm_ref[g, 0:1, :] for g in range(norm_ref.shape[0])], label)


def shift_of(norm_ref, label):
    return own_of([norm_ref[g, 1:2, :] for g in range(norm_ref.shape[0])], label)


def valid_cols(channels):
    return lax.broadcasted_iota(jnp.int32, (COLS, channels), 0) < COLS - 4


def chan_mask(tab):
    return lax.broadcasted_iota(jnp.int32, (1, LANES), 1).astype(F32) < entry(tab, LIMIT)


def flat(x):
    return x.reshape(x.shape[0] * x.shape[1], x.shape[2])


def mm(a, b):
    return jnp.dot(a, b, preferred_element_type=F32)


def mm_nt(a, b):
    return lax.dot_general(a, b, (((1,), (1,)), ((), ())), preferred_element_type=F32)


def mm_tn(a, b):
    return lax.dot_general(a, b, (((0,), (0,)), ((), ())), preferred_element_type=F32)


def mm_side(a, b):
    turned = mm_tn(b, a)
    blocks = [
        jnp.transpose(turned[:, LANES * j : LANES * (j + 1)]) for j in range(a.shape[1] // LANES)
    ]
    return blocks[0] if len(blocks) == 1 else jnp.concatenate(blocks, axis=0)


def zeros8(channels):
    return jnp.zeros((8, channels), F32)


def down(x):
    return jnp.sum(x, axis=0, keepdims=True)


OWN, OTHER, HALF, LIMIT, GATE, MINOR, MAJOR = range(7)


def entry(tab, k):
    return tab[k : k + 1, :]


def half_of(tab, k=HALF):
    return (jnp.sum(entry(tab, k)) * (1.0 / LANES)).astype(jnp.int32)


def prepare(w1b, w2b, w_even, w_odd, w_two, w_last, b_even, b_odd, b_two, b_last):
    n = LANES
    for k, (y, x) in enumerate(((1, 1), (1, 2), (1, 0))):
        w_even[n * k : n * (k + 1), :] = w1b[y, x]
    for k, (low, high) in enumerate((((2, 1), (0, 1)), ((2, 2), (0, 2)), ((2, 0), (0, 0)))):
        w_odd[n * k : n * (k + 1), 0:n] = w1b[low]
        w_odd[n * k : n * (k + 1), n : 2 * n] = w1b[high]
    for x in range(3):
        w_two[n * x : n * (x + 1), 0:n] = w2b[0, x]
        w_two[n * x : n * (x + 1), n : 2 * n] = w2b[1, x]
        w_last[n * x : n * (x + 1), :] = w2b[2, x]
        b_two[0:n, n * x : n * (x + 1)] = w2b[1, x]
        b_two[n : 2 * n, n * x : n * (x + 1)] = w2b[2, x]
        b_last[:, n * x : n * (x + 1)] = w2b[0, x]
    nothing = jnp.zeros((n, n), BF16)
    b_even[0:n, 0:n] = w1b[1, 1]
    b_even[0:n, n : 2 * n] = nothing
    b_even[n : 2 * n, 0:n] = w1b[1, 2]
    b_even[n : 2 * n, n : 2 * n] = w1b[1, 0]
    for k, top in ((0, 2), (1, 0)):
        b_odd[0:n, 2 * n * k : 2 * n * k + n] = w1b[top, 1]
        b_odd[0:n, 2 * n * k + n : 2 * n * (k + 1)] = nothing
        b_odd[n : 2 * n, 2 * n * k : 2 * n * k + n] = w1b[top, 2]
        b_odd[n : 2 * n, 2 * n * k + n : 2 * n * (k + 1)] = w1b[top, 0]


def widen(source, x_pad):
    rows, cols, chans = source.shape
    gap = x_pad.shape[1] - cols

    def put(i, carry):
        x_pad[i, 0:cols, :] = source[i]
        x_pad[i, cols : cols + gap, :] = jnp.zeros((gap, chans), BF16)
        return carry

    lax.fori_loop(0, rows, put, 0, unroll=7)


def first_project(x_pad, w, z, stats=True):
    rows = x_pad.shape[0]
    step = rows // 4
    sums, squares = zeros8(LANES), zeros8(LANES)
    for c in range(4):
        values = mm(flat(x_pad[step * c : step * (c + 1)]), w[...])
        z[step * c : step * (c + 1)] = values.reshape(step, x_pad.shape[1], LANES)
        if stats:
            parts = values.reshape(-1, 8, LANES)
            sums = sums + jnp.sum(parts, axis=0)
            squares = squares + jnp.sum(parts * parts, axis=0)
    return sums, squares


def f1(
    place_at, group_at, width_at, gate_at, images, w_at, tab, x_own, x_for, z_own, z_for, send,
    place_ref, group, width, gate, raw, w, found, sems, *, batch,
):
    rows = images.shape[1] // 2
    parts = [pl.ds(rows * p, rows) for p in (0, 1)]
    pairs = (
        (place_at, place_ref), (group_at, group), (width_at, width), (gate_at, gate), (w_at, w),
        *((images.at[k, part], raw.at[k, part]) for k in (0, 1) for part in parts),
    )
    copies = [pltpu.make_async_copy(a, b, sems.at[k]) for k, (a, b) in enumerate(pairs)]
    for k in (0, 5, 4, 6, 7, 8, 1, 2, 3):
        copies[k].start()
    for k in (0, 4):
        copies[k].wait()
    half = lax.div(place_ref[0], batch)
    sides = ((x_own, z_own), (x_for, z_for))

    def one(k):
        for p, part in enumerate(parts):
            copies[5 + 2 * k + p].wait()
            for place in (0, 1):

                @pl.when(half == place)
                def _():
                    x_pad, _ = sides[k] if place == 0 else sides[1 - k]
                    widen(raw.at[k, part], x_pad.at[part])

        for place in (0, 1):

            @pl.when(half == place)
            def _():
                x_pad, z = sides[k] if place == 0 else sides[1 - k]
                sums, squares = first_project(x_pad, w, z)
                at = 2 * (k if place == 0 else 1 - k)
                found[at : at + 1, :] = down(sums)
                found[at + 1 : at + 2, :] = down(squares)

    one(0)
    one(1)
    for k in (1, 2, 3):
        copies[k].wait()
    rows = [found[k : k + 1, :] for k in range(4)]
    own, other = group[half], group[1 - half]
    values = {
        OWN: own, OTHER: other, HALF: half, LIMIT: w.shape[1] // 4 * width[own], GATE: gate[own],
        MINOR: lax.rem(lax.rem(place_ref[0], batch), NEAR),
        MAJOR: lax.div(lax.rem(place_ref[0], batch), NEAR),
    }
    tab[...] = jnp.zeros(tab.shape, F32)
    for k, v in values.items():
        tab[k : k + 1, :] = jnp.full((1, LANES), v.astype(F32))
    spread(send, [*rows, jnp.full((1, LANES), (own + 4 * other).astype(F32))])


def f1_strided(tab, x_own, x_oth, w, xee, z, stats, wide):
    half = half_of(tab)
    rows = x_own.shape[0] // 2
    sums = tuple(zeros8(LANES) for _ in range(wide.shape[0]))
    for k, x_pad in enumerate((x_own, x_oth)):
        first = rows * (half if k == 0 else 1 - half)

        def put(i, carry, x_pad=x_pad, first=first):
            out = []
            for b in range(wide.shape[0]):
                lanes = slice(LANES * b, LANES * (b + 1))
                wide[b, i] = x_pad[2 * i, :, lanes].astype(F32)
                even = wide[b, i, pl.ds(0, COLS, stride=2), :]
                xee[first + i, :, lanes] = even.astype(BF16)
                out.append(carry[b] + fold(even))
            return tuple(out)

        sums = lax.fori_loop(0, rows, put, sums, unroll=7)
    total = 2 * rows
    step = total // 7
    chans = z.shape[2]
    squares = zeros8(chans)
    for c in range(7):
        values = mm(flat(xee[step * c : step * (c + 1)]), w[...])
        z[step * c : step * (c + 1)] = values.reshape(step, COLS, chans)
        parts = values.reshape(-1, 8, chans)
        squares = squares + jnp.sum(parts * parts, axis=0)
    stats[:, 0 : w.shape[0]] = join([down(v) for v in sums])
    stats[:, w.shape[0] :] = down(squares)


def scale_shift(got, labels, tab, norm, pixels, slot=0):
    label = entry(tab, OWN)
    total = group_sum(got, labels, label)
    chans = norm.shape[2]
    count = tiled(group_count(labels, label), chans) * pixels
    mean, rstd = moments(row(total, 2 * slot), row(total, 2 * slot + 1), count)
    gain, shift = gain_of(norm, entry(tab, OWN)), shift_of(norm, entry(tab, OWN))
    return mean, rstd, gain, shift, count


def conv_stats(z, source, pair, single, send, extra=()):
    keep = valid_cols(LANES)[None]
    rows = z.shape[0]
    step = rows // 4
    (lanes_2, w_2, offsets), (lanes_1, w_1, offset) = pair, single
    sums, squares = zeros8(LANES), zeros8(LANES)
    base = min(offsets)
    for c in range(4):
        at = step * c
        both = mm(flat(source[at + base : at + base + step + 1, :, lanes_2]), w_2)
        values = mm(flat(source[at + offset : at + offset + step, :, lanes_1]), w_1)
        for k, own in enumerate(offsets):
            skip = COLS * (own - base)
            values = values + both[skip : skip + step * COLS, LANES * k : LANES * (k + 1)]
        values = jnp.where(keep, values.reshape(step, COLS, LANES), 0.0)
        z[at : at + step] = values
        parts = values.reshape(-1, 8, LANES)
        sums = sums + jnp.sum(parts, axis=0)
        squares = squares + jnp.sum(parts * parts, axis=0)
    spread(send, [down(sums), down(squares), *extra])


def f2(
    tab, got, z_own, x_oth, w, norm, w_even, w_odd, stats_p,
    xs, z, send, labels, keeps, keeps_all, z_oth,
):
    codes = got[:, :, 4 * LANES : 5 * LANES]
    others = jnp.floor(0.25 * codes)
    marks = codes - 4.0 * others
    labels[...] = marks
    rows = xs.shape[0] - 1
    pixels = 4.0 * rows * (COLS - 4)
    first_project(x_oth, w, z_oth, False)
    for g in range(norm.shape[0]):
        mine, theirs = (marks == float(g)).astype(F32), (others == float(g)).astype(F32)
        totals = [
            jnp.sum(
                got[:, :, LANES * s : LANES * (s + 1)] * mine
                + got[:, :, LANES * (s + 2) : LANES * (s + 3)] * theirs,
                axis=0,
            )
            for s in (0, 1)
        ]
        mean, rstd = moments(*totals, group_count(marks, float(g)) * pixels)
        keeps_all[2 * g : 2 * g + 1, :] = mean
        keeps_all[2 * g + 1 : 2 * g + 2, :] = rstd
    for k, slot in enumerate((OWN, OTHER)):
        for q in (0, 1):
            choices = [keeps_all[2 * g + q : 2 * g + q + 1, :] for g in range(norm.shape[0])]
            keeps[2 * k + q : 2 * k + q + 1, :] = own_of(choices, entry(tab, slot))
    mean, rstd = keeps[0:1, :], keeps[1:2, :]
    gain, shift = gain_of(norm, entry(tab, OWN)), shift_of(norm, entry(tab, OWN))
    scale = rstd * gain
    bias = 0.5 * (shift - mean * scale)
    scale = 0.5 * scale
    keep = valid_cols(LANES) & chan_mask(tab)
    half = half_of(tab)
    xs[0] = jnp.zeros(xs.shape[1:], BF16)
    n = LANES
    for k, zz in enumerate((z_own, z_oth)):
        first = 1 + (rows // 2) * (half if k == 0 else 1 - half)

        def put(i, carry, zz=zz, first=first):
            lane = 0
            for a in (0, 1):
                for b in (0, 1):
                    u = zz[2 * i + a, pl.ds(b, COLS, stride=2), :] * scale + bias
                    act = jnp.where(keep, silu_of_half(u), 0.0)
                    xs[first + i, :, lane : lane + n] = act.astype(BF16)
                    lane += n
                    if b == 1:
                        moved = pltpu.roll(act, 1, 0)
                        xs[first + i, :, lane : lane + n] = moved.astype(BF16)
                        lane += n
            return carry

        lax.fori_loop(0, rows // 2, put, 0, unroll=7)
    extra = [stats_p[:, lanes] for lanes in columns(stats_p.shape[1])]
    pair = (slice(3 * n, 6 * n), w_odd[...], (1, 0))
    conv_stats(z, xs, pair, (slice(0, 3 * n), w_even[...], 1), send, extra)


def project(act, w, z):
    rows, chans = z.shape[0], z.shape[2]
    step = rows // 7
    squares = zeros8(chans)
    for c in range(7):
        values = mm(flat(act[step * c : step * (c + 1)]), w[...])
        z[step * c : step * (c + 1)] = values.reshape(step, COLS, chans)
        parts = values.reshape(-1, 8, chans)
        squares = squares + jnp.sum(parts * parts, axis=0)
    return down(squares)


def join(pieces):
    return pieces[0] if len(pieces) == 1 else jnp.concatenate(pieces, axis=1)


def columns(channels):
    return [slice(LANES * j, LANES * (j + 1)) for j in range(channels // LANES)]


def three_parts(sums):
    high = sums.astype(BF16)
    rest = sums - high.astype(F32)
    mid = rest.astype(BF16)
    low = (rest - mid.astype(F32)).astype(BF16)
    lines = [v.astype(F32) for v in (high, mid, low)]
    lines.append(jnp.zeros((13, sums.shape[1]), F32))
    return jnp.concatenate(lines, axis=0).astype(BF16)


def through(sums, w):
    return down(mm(three_parts(sums), w))


def put_split(send, at, values):
    rows = values.shape[0]
    high = values.astype(BF16)
    rest = (values - high.astype(F32)).astype(BF16)
    for k, part in enumerate((high, rest)):
        send[:, at + rows * k : at + rows * (k + 1), :] = jnp.broadcast_to(
            part[None], (send.shape[0], rows, LANES)
        )


def get_split(got, at, rows):
    return got[:, at : at + rows, :].astype(F32) + got[:, at + rows : at + 2 * rows, :].astype(F32)


def over_group(values, marks, label):
    return jnp.sum(values * (marks == label).astype(F32), axis=0)


def stack(rows):
    return jnp.concatenate(rows, axis=0)


def activate_pair(tab, got, labels, z, norm, act, keeps, slope, both):
    rows = z.shape[0]
    pixels = 1.0 * rows * (COLS - 4)
    mean, rstd, gain, shift, _ = scale_shift(got, labels[...], tab, norm, pixels)
    keeps[0:1, :] = mean
    keeps[1:2, :] = rstd
    scale = rstd * gain
    bias = 0.5 * (shift - mean * scale)
    scale = 0.5 * scale
    keep = valid_cols(LANES) & chan_mask(tab)

    def put(i, carry):
        zz = z[i]
        u = zz * scale + bias
        t = jnp.tanh(u)
        p = u * t
        low = jnp.where(keep, u + p, 0.0).astype(BF16)
        act[i] = low
        s = jnp.where(keep, (0.5 + 0.5 * t) * (1.0 + u - p), 0.0)
        sx = s * ((zz - mean) * rstd)
        slope[i] = s
        for k, v in enumerate((s, sx)):
            high = v.astype(BF16)
            both[i, :, LANES * k : LANES * (k + 1)] = high
            both[i, :, LANES * (k + 2) : LANES * (k + 3)] = (v - high.astype(F32)).astype(BF16)
        return carry[0] + fold(low.astype(F32)), carry[1] + fold(s), carry[2] + fold(sx)

    start = zeros8(LANES)
    sums = lax.fori_loop(0, rows, put, (start, start, start), unroll=7)
    act_sum, *sums = [down(v) for v in sums]
    product = mm_tn(flat(act[...]), flat(both[...]))
    product = product[:, 0 : 2 * LANES] + product[:, 2 * LANES :]
    middle = jnp.broadcast_to(act_sum * (1.0 / pixels), (8, LANES))
    return act_sum, product - jnp.transpose(middle)[:, 0:1] * join(sums), stack(sums)


def rows_of(line):
    return stack([line[:, lanes] for lanes in columns(line.shape[1])])


def line_of(rows):
    return join([rows[k : k + 1, :] for k in range(rows.shape[0])])


def put_part(send, at, rows, part):
    first, last = part
    if last > first:
        send[:, at : at + last - first, :] = rows[:, first:last, :]


def pair_rows(product, devices, share, high, low, own):
    n = LANES
    missing = devices * share - n
    for h in (0, 1):
        values = product[:, n * h : n * (h + 1)]
        if missing:
            values = stack([values, jnp.zeros((missing, n), F32)])
        values = values.reshape(devices, share, n)
        first, last = share * h, share * (h + 1)
        top = values.astype(BF16)
        rest = (values - top.astype(F32)).astype(BF16)
        high[:, first:last, :] = top
        low[:, first:last, :] = rest
        own[:, first:last, :] = top.astype(F32) + rest.astype(F32)


def pass_pair(send, at, high, low, marks, groups):
    rows = high.astype(F32) + low.astype(F32)
    out = -rows
    for g in range(groups):
        same = (marks == float(g)).astype(F32)
        images = jnp.maximum(jnp.sum(same, axis=0), 1.0)
        out = out + (jnp.sum(rows * same, axis=0) / images)[None] * same
    send[:, at : at + rows.shape[1], :] = out.astype(BF16)


def pair_solve(tab, marks, outer, inner, sums, w, act_sums, q_rows, p_rows, pixels):
    label, n = entry(tab, OWN), LANES
    (norm_o, keeps_o), (norm_i, keeps_i) = outer, inner
    shift_o, gain_o, shift_i, gain_i = sums
    images = group_count(marks, label)
    count, count_o = images * pixels, tiled(images, norm_o.shape[2]) * pixels
    rstd_o = keeps_o[1:2, :]
    a_o = rstd_o * gain_of(norm_o, label)
    b_o, c_o = -(a_o * rstd_o) * gain_o / count_o, -a_o * shift_o / count_o
    scaled = w[...].astype(F32) * b_o
    high = scaled.astype(BF16)
    low = (scaled - high.astype(F32)).astype(BF16)
    got = mm_nt(jnp.concatenate([high, low, three_parts(c_o)], axis=0), w[...])
    m, e = got[0:n] + got[n : 2 * n], down(got[2 * n :])
    m_high = m.astype(BF16)
    m_low = (m - m_high.astype(F32)).astype(BF16)
    m = m_high.astype(F32) + m_low.astype(F32)
    same = (marks == label).astype(F32)
    middle = jnp.sum(act_sums * same, axis=0) / count
    spread_out = ((act_sums * (1.0 / pixels) - middle[None]) * same).reshape(-1, n).astype(BF16)
    share = p_rows.shape[1] // 2
    p_rows = p_rows * images[None]
    found = []
    q = join([q_rows[:, h : h + 1, :].reshape(-1, n) for h in (0, 1)])
    away = mm_tn(spread_out, q.astype(BF16))
    q = down(q * join([same.reshape(-1, n)] * 2))
    for h, start in enumerate((shift_i, gain_i)):
        lanes = slice(n * h, n * (h + 1))
        p = p_rows[:, share * h : share * (h + 1), :].reshape(-1, n)[0:n] + away[:, lanes]
        found.append(start + down(m * p) + e * q[:, lanes])
    rstd_i = keeps_i[1:2, :]
    a = rstd_i * gain_of(norm_i, label)
    coefs = a, -(a * rstd_i) * found[1] / count, -a * found[0] / count
    both = join([m_high, m_low])
    line = through(middle, both)
    return both, e - line[:, 0:n] - line[:, n:], coefs, found


def f3(
    tab, got, labels, z_in, norm, w, w_p, xz,
    act, z, send, keeps, keeps_p, slope, q, high, own, both, low, *, share, part,
):
    got_1 = got.at[:, :, 0 : 2 * LANES]
    found = activate_pair(tab, got_1, labels, z_in, norm, act, keeps, slope, both)
    at = expand_pair(found, act, w, z, send, q, high, low, own, share)
    send[:, at : at + 2 * share, :] = low[...]
    put_part(send, at + 2 * share, xz, part)
    marks, label = labels[...], entry(tab, OWN)
    total = group_sum(got, marks, label)
    outer, first = z.shape[2], 2 * LANES
    second = first + w_p.shape[0]
    count = tiled(group_count(marks, label), outer) * (1.0 * z.shape[0] * (COLS - 4))
    mean, rstd = moments(through(total[:, first:second], w_p[...]), total[:, second:], count)
    keeps_p[0:1, :] = mean
    keeps_p[1:2, :] = rstd


def expand_pair(found, act, w, z, send, q, high, low, own, share):
    sums, product, q[...] = found
    pixels = 1.0 * z.shape[0] * (COLS - 4)
    squares = project(act, w, z)
    first = through(sums, w[...])
    second = squares - first * first / pixels
    pair_rows(product, send.shape[0], share, high, low, own)
    put_split(send, 0, sums)
    moved = rows_of(second).astype(BF16)
    send[:, 2 : 2 + moved.shape[0], :] = jnp.broadcast_to(moved[None], (send.shape[0], *moved.shape))
    return 2 + moved.shape[0]


def f4(
    tab, got, labels, zc, zp, norm_c, norm_p, keeps_p, w_c, w, high, q,
    joined, slope, z, send, keeps,
):
    rows, chans = zc.shape[0], zc.shape[2]
    pixels = 1.0 * rows * (COLS - 4)
    mean_c, rstd_c = gathered_moments(got, labels[...], entry(tab, OWN), w_c, pixels)
    mean_p, rstd_p = keeps_p[0:1, :], keeps_p[1:2, :]
    for k, v in enumerate((mean_c, rstd_c, mean_p, rstd_p)):
        keeps[k : k + 1, :] = v
    group = entry(tab, OWN)
    scale_c = rstd_c * gain_of(norm_c, group)
    scale_p = rstd_p * gain_of(norm_p, group)
    bias = (shift_of(norm_c, group) - mean_c * scale_c) + (
        shift_of(norm_p, group) - mean_p * scale_p
    )
    keep = valid_cols(chans)
    scale_c, scale_p, bias = 0.5 * scale_c, 0.5 * scale_p, 0.5 * bias

    def put(i, carry):
        u = zc[i] * scale_c + zp[i] * scale_p + bias
        t = jnp.tanh(u)
        p = u * t
        joined[i] = jnp.where(keep, u + p, 0.0).astype(BF16)
        slope[i] = (0.5 + 0.5 * t) * (1.0 + u - p)
        return carry

    lax.fori_loop(0, rows, put, 0, unroll=7)
    step = rows // 4
    sums, squares = zeros8(LANES), zeros8(LANES)
    for c in range(4):
        values = mm(flat(joined[step * c : step * (c + 1)]), w[...])
        z[step * c : step * (c + 1)] = values.reshape(step, COLS, LANES)
        parts = values.reshape(-1, 8, LANES)
        sums = sums + jnp.sum(parts, axis=0)
        squares = squares + jnp.sum(parts * parts, axis=0)
    put_split(send, 0, stack([down(sums), down(squares)]))
    send[:, 4 : 4 + high.shape[1], :] = high[...]
    put_split(send, 4 + high.shape[1], q[...])


def f5(tab, got, labels, z_in, norm, w_two, w_last, x3, z, send, keeps):
    rows = z_in.shape[0]
    pixels = 1.0 * rows * (COLS - 4)
    marks, label = labels[...], entry(tab, OWN)
    total = over_group(get_split(got, 0, 2), marks, label)
    mean, rstd = moments(total[0:1], total[1:2], group_count(marks, label) * pixels)
    gain, shift = gain_of(norm, label), shift_of(norm, label)
    keeps[0:1, :] = mean
    keeps[1:2, :] = rstd
    scale = rstd * gain
    bias = 0.5 * (shift - mean * scale)
    scale = 0.5 * scale
    keep = valid_cols(LANES) & chan_mask(tab)
    x3[0] = jnp.zeros(x3.shape[1:], BF16)
    x3[rows + 1] = jnp.zeros(x3.shape[1:], BF16)
    n = LANES

    def put(i, carry):
        act = jnp.where(keep, silu_of_half(z_in[i] * scale + bias), 0.0)
        x3[i + 1, :, 0:n] = pltpu.roll(act, 1, 0).astype(BF16)
        x3[i + 1, :, n : 2 * n] = act.astype(BF16)
        x3[i + 1, :, 2 * n : 3 * n] = pltpu.roll(act, COLS - 1, 0).astype(BF16)
        return carry

    lax.fori_loop(0, rows, put, 0, unroll=7)
    lanes = slice(0, 3 * n)
    conv_stats(
        z, x3, (lanes, w_two[...], (0, 1)), (lanes, w_last[...], 2), send
    )


def f6(
    tab, got, labels, z_in, norm, w, xz,
    act, z, send, keeps, slope, q, own, both, high, low, *, share, part,
):
    got_1 = got.at[:, :, 0 : 2 * LANES]
    found = activate_pair(tab, got_1, labels, z_in, norm, act, keeps, slope, both)
    at = expand_pair(found, act, w, z, send, q, high, low, own, share)
    send[:, at : at + 2 * share, :] = high[...]
    send[:, at + 2 * share : at + 4 * share, :] = low[...]
    put_part(send, at + 4 * share, xz, part)


def gathered_moments(got, marks, label, w, pixels):
    devices, chans = got.shape[0], w.shape[1]
    low = stack([got[:, k : k + 1, :].astype(F32).reshape(devices, LANES) for k in (0, 1)])
    means = mm(low.astype(BF16), w[...]) * (1.0 / pixels)
    means = means[0:devices] + means[devices:]
    blocks = chans // LANES
    moments_2 = join(
        [got[:, 2 + k : 3 + k, :].astype(F32).reshape(devices, LANES) for k in range(blocks)]
    )
    same = join([(marks == label).astype(F32).reshape(devices, LANES)] * blocks)
    images = tiled(group_count(marks, label), chans)
    mean = down(means * same) / images
    away = means - mean
    variance = down((moments_2 + pixels * (away * away)) * same) / (images * pixels)
    return mean, lax.rsqrt(variance + EPSILON)


def b7(
    tab, got, labels, joined, z, norm, w, cot, slope_in, z_in, keeps_in, q,
    result, grad_pre, send, keeps, d_in, wide, low, *, share, p_at,
):
    rows, chans = z.shape[0], z.shape[2]
    cols = COLS - 4
    pixels = 1.0 * rows * cols
    marks, label = labels[...], entry(tab, OWN)
    mean, rstd = gathered_moments(got, marks, label, w, pixels)
    gain, shift = gain_of(norm, label), shift_of(norm, label)
    keeps[0:1, :] = mean
    keeps[1:2, :] = rstd
    gate = 0.25 * tiled(entry(tab, GATE), chans)
    scale = 0.5 * rstd * gain * gate
    bias = 0.5 * (shift - mean * rstd * gain) * gate
    wide[:, cols:, :] = jnp.zeros((rows, COLS - cols, chans), F32)
    a_gate = rstd * gain * gate

    def put(i, carry):
        sums, products = carry
        wide[i, 0:cols, :] = cot[i].astype(F32)
        zz = z[i]
        u = 0.5 * joined[i].astype(F32) + zz * scale + bias
        t = jnp.tanh(u)
        p = u * t
        result[i] = (u + p)[0:cols].astype(BF16)
        g = wide[i] * ((0.5 + 0.5 * t) * (1.0 + u - p))
        grad_pre[i] = g
        low[i] = (a_gate * g).astype(BF16)
        return sums + fold(g), products + fold(g * (zz - mean))

    start = zeros8(chans)
    sums, products = lax.fori_loop(0, rows, put, (start, start), unroll=7)
    inner = inner_sums(low, w, slope_in, z_in, keeps_in, d_in)
    blocks = chans // LANES
    put_split(send, 0, rows_of(down(sums) * gate))
    put_split(send, 2 * blocks, rows_of(down(products) * rstd * gate))
    put_split(send, 4 * blocks, stack(inner))
    put_split(send, 4 * blocks + 4, q[...])
    high = got[:, p_at : p_at + 2 * share, :]
    low_p = got[:, p_at + 2 * share : p_at + 4 * share, :]
    pass_pair(send, 4 * blocks + 8, high, low_p, marks, norm.shape[0])


def own_coefs(tab, marks, norm, keeps, pixels, shift_sum, gain_sum):
    group = entry(tab, OWN)
    count = tiled(group_count(marks, group), norm.shape[2]) * pixels
    mean, rstd = keeps[0:1, :], keeps[1:2, :]
    a = rstd * gain_of(norm, group)
    return mean, a, -(a * rstd) * gain_sum / count, -a * shift_sum / count


def wide_lines(total, outer):
    side = outer // 2
    return [join([total[h : h + 1, side * k : side * (k + 1)] for h in (0, 1)]) for k in range(3)]


def norm_tail(labels, got_2c, got_2a, got_1, grad_2c, grad_2a, grad_1c, grad_1p):
    marks = labels[...]
    outer = grad_2c.shape[2]
    blocks = outer // LANES
    for g in range(grad_2c.shape[0]):
        label = float(g)
        rows = [
            line_of(over_group(get_split(got_2c, 2 * blocks * k, blocks), marks, label))
            for k in (0, 1)
        ]
        pair = over_group(get_split(got_2a, 0, 2), marks, label)
        lines = wide_lines(group_sum(got_1, marks, label), outer)
        for out, shift_sum, gain_sum in (
            (grad_2c, rows[0], rows[1]),
            (grad_2a, pair[0:1], pair[1:2]),
            (grad_1c, lines[0], lines[1]),
            (grad_1p, lines[0], lines[2]),
        ):
            out[g, 0:1, :] = gain_sum
            out[g, 1:2, :] = shift_sum


def slope_sums(tab, d, z_in, norm, keeps, dout):
    rows = z_in.shape[0]
    mean, rstd = keeps[0:1, :], keeps[1:2, :]
    group = entry(tab, OWN)
    scale = rstd * gain_of(norm, group)
    bias = 0.5 * (shift_of(norm, group) - mean * scale)
    scale = 0.5 * scale
    keep = valid_cols(LANES) & chan_mask(tab)

    def put(i, carry):
        sums, products = carry
        zz = z_in[i]
        g = jnp.where(keep, d[i] * slope_of_half(zz * scale + bias), 0.0)
        dout[i] = g
        return sums + fold(g), products + fold(g * (zz - mean))

    sums, products = lax.fori_loop(
        0, rows, put, (zeros8(LANES), zeros8(LANES)), unroll=4
    )
    return down(sums), down(products) * rstd


def b9(
    tab, got, labels, norm_c, keeps_c, w_c, got_act, act, slope, d_in, z, norm, keeps,
    b_two, b_last, z_in, norm_in, keeps_in, x_sum, pair_high, pair_low, own_p,
    dz, dout, send, own_sums, d3, d, *, share, p_at,
):
    rows = z.shape[0]
    pixels = 1.0 * rows * (COLS - 4)
    marks, label = labels[...], entry(tab, OWN)
    blocks = norm_c.shape[2] // LANES
    at = 4 * blocks
    wide = [
        line_of(over_group(get_split(got, 2 * blocks * k, blocks), marks, label)) for k in (0, 1)
    ]
    inner = over_group(get_split(got, at, 2), marks, label)
    m, line, (a, b, c), found = pair_solve(
        tab, marks, (norm_c, keeps_c), (norm, keeps), [*wide, inner[0:1], inner[1:2]], w_c,
        get_split(got_act, 0, 1), get_split(got, at + 4, 2),
        got[:, at + 8 : at + 8 + 2 * share, :].astype(F32) + own_p[...], pixels,
    )
    own_sums[0:1, :] = found[0]
    own_sums[1:2, :] = found[1]
    inner_part(act, m, d_in, d)
    mean = keeps[0:1, :]
    keep = valid_cols(LANES)
    n = LANES
    d3[0] = jnp.zeros(d3.shape[1:], BF16)
    d3[rows + 1] = jnp.zeros(d3.shape[1:], BF16)

    def put(i, carry):
        v = a * (slope[i] * (d[i] + line)) + b * (z[i] - mean) + c
        v = jnp.where(keep, v, 0.0)
        d3[i + 1, :, 0:n] = pltpu.roll(v, COLS - 1, 0).astype(BF16)
        low = v.astype(BF16)
        d3[i + 1, :, n : 2 * n] = low
        dz[i] = low
        d3[i + 1, :, 2 * n : 3 * n] = pltpu.roll(v, 1, 0).astype(BF16)
        return carry

    lax.fori_loop(0, rows, put, 0, unroll=7)
    step = rows // 4
    for k in range(4):
        both = mm_nt(flat(d3[step * k : step * (k + 1) + 1]), b_two[...])
        value = mm_nt(flat(d3[step * k + 2 : step * (k + 1) + 2]), b_last[...])
        value = value + both[COLS:, 0:n] + both[0 : step * COLS, n : 2 * n]
        d[step * k : step * (k + 1)] = value.reshape(step, COLS, LANES)
    put_split(send, 0, stack(slope_sums(tab, d, z_in, norm_in, keeps_in, dout)))
    blocks = columns(x_sum.shape[0])
    put_split(send, 4, stack([jnp.transpose(x_sum[lanes, :])[0:1] for lanes in blocks]))
    high, low = pair_high[:, 4 : 4 + 2 * share, :], pair_low[:, p_at : p_at + 2 * share, :]
    pass_pair(send, 4 + 2 * len(blocks), high, low, marks, norm.shape[0])


def b10(
    tab, got, labels, dout_in, z, norm, keeps, w, grad_pre, slope, zc, zp, keeps_cp,
    norm_c, w_c, slope_in, z_in, keeps_in,
    dz, grad_pre_2, send, d_in, d, low,
):
    rows, chans = zc.shape[0], zc.shape[2]
    pixels = 1.0 * rows * (COLS - 4)
    marks = labels[...]
    total = over_group(get_split(got, 0, 2), marks, entry(tab, OWN))
    coefs = own_coefs(tab, marks, norm, keeps, pixels, total[0:1], total[1:2])
    normed_grad(dout_in, (dz, z, *coefs))
    d[...] = mm_nt(flat(dz[...]), w[...]).reshape(d.shape)
    mean_c, rstd_c, mean_p, rstd_p = (keeps_cp[k : k + 1, :] for k in range(4))
    a_c = rstd_c * gain_of(norm_c, entry(tab, OWN))

    def sum_up(i, carry):
        sums, prod_c, prod_p = carry
        g = (grad_pre[i] + d[i]) * slope[i]
        grad_pre_2[i] = g
        low[i] = (a_c * g).astype(BF16)
        return (
            sums + fold(g),
            prod_c + fold(g * (zc[i] - mean_c)),
            prod_p + fold(g * (zp[i] - mean_p)),
        )

    start = zeros8(chans)
    sums, prod_c, prod_p = lax.fori_loop(0, rows, sum_up, (start, start, start), unroll=7)
    wide = [down(sums), down(prod_c) * rstd_c, down(prod_p) * rstd_p]
    inner = inner_sums(low, w_c, slope_in, z_in, keeps_in, d_in)
    parts = [stack([v[:, 0 : chans // 2], v[:, chans // 2 :]]) for v in wide]
    values = join([*parts, stack(inner)])
    send[...] = jnp.broadcast_to(values[None], send.shape)


def inner_sums(low, w, slope, z, keeps, d_in):
    d_in[...] = mm_nt(flat(low[...]), w[...]).reshape(d_in.shape)
    mean, rstd = keeps[0:1, :], keeps[1:2, :]

    def add(i, carry):
        g = slope[i] * d_in[i]
        return carry[0] + fold(g), carry[1] + fold(g * (z[i] - mean))

    sums = lax.fori_loop(0, z.shape[0], add, (zeros8(LANES), zeros8(LANES)), unroll=7)
    return down(sums[0]), down(sums[1]) * rstd


def inner_part(act, m, d_in, d):
    both = mm(flat(act[...]), m)
    d[...] = d_in[...] + (both[:, 0:LANES] + both[:, LANES:]).reshape(d.shape)


def normed_grad(dout, *parts):
    keep = valid_cols(dout.shape[2])

    def put(i, carry):
        g = dout[i]
        for dz, z, mean, a, b, c in parts:
            v = a * g + b * (z[i] - mean) + c
            dz[i] = jnp.where(keep, v, 0.0).astype(BF16)
        return carry

    lax.fori_loop(0, dout.shape[0], put, 0, unroll=7)


def b12(
    tab, own10, labels, norm_c, keeps_c, w_c, got_act, got_q, got_p, own_p, act, slope, d_in,
    z, norm, keeps, xs, d2, kept, sent, own_sums, dz, packed, dout, *, share, q_at, p_at,
):
    rows = z.shape[0]
    pixels = 1.0 * rows * (COLS - 4)
    outer, n = norm_c.shape[2], LANES
    marks = labels[...]
    total = own10[...]
    cuts = (0, outer, 2 * outer, 2 * outer + n, 2 * outer + 2 * n)
    m, line, (a, b, c), found = pair_solve(
        tab, marks, (norm_c, keeps_c.at[0:2]), (norm, keeps),
        [total[:, u:v] for u, v in zip(cuts, cuts[1:])], w_c, get_split(got_act, 0, 1),
        get_split(got_q, q_at, 2),
        got_p[:, p_at : p_at + 2 * share, :].astype(F32) + own_p[...], pixels,
    )
    own_sums[0:1, :] = found[0]
    own_sums[1:2, :] = found[1]
    inner_part(act, m, d_in, dout)
    mean = keeps[0:1, :]
    keep = valid_cols(LANES)
    d2[rows] = jnp.zeros(d2.shape[1:], BF16)

    def put(i, carry):
        v = a * (slope[i] * (dout[i] + line)) + b * (z[i] - mean) + c
        v = jnp.where(keep, v, 0.0)
        low = v.astype(BF16)
        dz[i] = low
        d2[i, :, 0:n] = low
        d2[i, :, n : 2 * n] = pltpu.roll(v, COLS - 1, 0).astype(BF16)
        return carry

    lax.fori_loop(0, rows, put, 0, unroll=7)
    low = flat(dz[...])
    cur = mm_side(flat(xs[1 : rows + 1]), low)
    for k, (y, x) in enumerate(((1, 1), (1, 2), (1, 0), (2, 1), (2, 2), (2, 0))):
        put_rows(packed, n * (3 * y + x), cur[n * k : n * (k + 1)])
    up = mm_side(flat(xs[0:rows, :, 3 * n : 6 * n]), low)
    for k, (y, x) in enumerate(((0, 1), (0, 2), (0, 0))):
        put_rows(packed, n * (3 * y + x), up[n * k : n * (k + 1)])
    share_out(tab, packed, 9 * n, kept, sent)


def b12_images(
    tab, d2, b_even, b_odd, zz, norm_in, keeps_in, dn, sums_out, de, do, wide, *, own
):
    rows = de.shape[0]
    n = LANES
    half = half_of(tab)
    first = rows * (half if own else 1 - half)
    step = rows // 2
    for k in range(2):
        here = flat(d2[pl.ds(first + step * k, step)])
        below = flat(d2[pl.ds(first + step * k + 1, step)])
        de[step * k : step * (k + 1)] = mm_nt(here, b_even[...]).reshape(step, COLS, 2 * n)
        odd = mm_nt(here, b_odd[:, 0 : 2 * n]) + mm_nt(below, b_odd[:, 2 * n : 4 * n])
        do[step * k : step * (k + 1)] = odd.reshape(step, COLS, 2 * n)
    mean_1, rstd_1 = keeps_in[0:1, :], keeps_in[1:2, :]
    group = entry(tab, OWN)
    scale = rstd_1 * gain_of(norm_in, group)
    bias = 0.5 * (shift_of(norm_in, group) - mean_1 * scale)
    scale = 0.5 * scale
    keep = valid_cols(LANES) & chan_mask(tab)

    def emit(i, carry):
        sums, products = carry
        for ra in (0, 1):
            planes = (de, do)[ra]
            for cb in (0, 1):
                zv = zz[2 * i + ra, pl.ds(cb, COLS, stride=2), :]
                g = planes[i, :, n * cb : n * (cb + 1)] * slope_of_half(zv * scale + bias)
                g = jnp.where(keep, g, 0.0)
                sums = sums + fold(g)
                products = products + fold(g * (zv - mean_1))
                wide[2 * i + ra, pl.ds(cb, COLS, stride=2), :] = g
            dn[2 * i + ra] = wide[2 * i + ra].astype(BF16)
        return sums, products

    totals = lax.fori_loop(0, rows, emit, (zeros8(n), zeros8(n)), unroll=7)
    sums_out[0:1, :] = down(totals[0])
    sums_out[1:2, :] = down(totals[1]) * rstd_1


def b13(
    tab, got, labels, norm, keeps, w, z_own, z_for, dn_own, dn_for, gs_own, gs_for, *rest, at, held
):
    finished, outs = rest[:held], rest[held : 2 * held]
    grad, grad_norm, dz, wide, grad_v, norm_v, sems = rest[2 * held :]
    copies = [
        pltpu.make_async_copy(a, b, sems.at[k]) for k, (a, b) in enumerate(zip(finished, outs))
    ]
    for copy in copies:
        copy.start()
    rows, cols = grad.shape[1], grad.shape[2]
    half = half_of(tab)
    pixels = 2.0 * rows * cols
    marks = labels[...]
    totals = last_sums(got.at[:, at : at + 4, :], marks, norm.shape[0])
    for g in range(norm.shape[0]):
        norm_v[g, 0:1, :] = totals[g][1]
        norm_v[g, 1:2, :] = totals[g][0]
    copies.append(pltpu.make_async_copy(norm_v, grad_norm, sems.at[held]))
    copies[-1].start()
    keep = lax.broadcasted_iota(jnp.int32, (z_own.shape[1], LANES), 0) < cols
    for k, (z, dn, gs) in enumerate(((z_own, dn_own, gs_own), (z_for, dn_for, gs_for))):
        group = entry(tab, OWN if k == 0 else OTHER)
        shift_sum = own_of([t[0] for t in totals], group)
        gain_sum = own_of([t[1] for t in totals], group)
        count = group_count(marks, group) * pixels
        mean, rstd = keeps[2 * k : 2 * k + 1, :], keeps[2 * k + 1 : 2 * k + 2, :]
        a = rstd * gain_of(norm, group)
        b = -(a * rstd) * gain_sum / count
        c = -a * shift_sum / count

        def put(i, carry, z=z, dn=dn, mean=mean, a=a, b=b, c=c):
            v = a * dn[i].astype(F32) + b * (z[i] - mean) + c
            dz[i] = jnp.where(keep, v, 0.0).astype(BF16)
            return carry

        lax.fori_loop(0, rows, put, 0, unroll=7)
        place = half if k == 0 else 1 - half
        step = rows // 2
        for q in range(2):
            low = flat(dz[step * q : step * (q + 1)])
            for p in range(wide.shape[0]):
                values = mm_nt(low, w[LANES * p : LANES * (p + 1), :])
                wide[p, step * q : step * (q + 1)] = values.reshape(step, -1, LANES)

            def emit(i, carry, gs=gs, place=place):
                even = pl.ds(0, COLS, stride=2)
                for p in range(wide.shape[0]):
                    lanes = slice(LANES * p, LANES * (p + 1))
                    wide[p, 2 * i, even, :] = wide[p, 2 * i, even, :] + gs[i, :, lanes].astype(F32)
                    grad_v[place, 2 * i, :, lanes] = wide[p, 2 * i, 0:cols, :].astype(BF16)
                    grad_v[place, 2 * i + 1, :, lanes] = wide[p, 2 * i + 1, 0:cols, :].astype(BF16)
                return carry

            lax.fori_loop(step // 2 * q, step // 2 * (q + 1), emit, 0, unroll=True)
            part = pl.ds(step * q, step)
            copies.append(
                pltpu.make_async_copy(
                    grad_v.at[place, part], grad.at[place, part], sems.at[held + 1 + 2 * k + q]
                )
            )
            copies[-1].start()
    for copy in copies:
        copy.wait()


def put_rows(out, at, value):
    for j in range(value.shape[1] // LANES):
        out[at : at + value.shape[0], :] = value[:, LANES * j : LANES * (j + 1)].astype(BF16)
        at += value.shape[0]
    return at


def take_rows(source, at, out):
    rows = out.shape[0]
    for j in range(out.shape[1] // LANES):
        out[:, LANES * j : LANES * (j + 1)] = source(at, rows)
        at += rows
    return at


def share_out(tab, packed, used, kept, sent):
    if used < packed.shape[0]:
        packed[used:, :] = jnp.zeros((packed.shape[0] - used, LANES), BF16)
    half = half_of(tab)
    size = kept.shape[0] * kept.shape[1]
    for out, place in ((kept, half), (sent, 1 - half)):
        out[...] = packed[pl.ds(pl.multiple_of(size * place, 16), size), :].reshape(out.shape)


def g_most(
    tab, act_2b, x3, dz_2b, joined, dz_2a, act_1b, xee,
    got, labels, norm_c, norm_p, keeps, grad_pre_2, zc, zp,
    got_2c, norm_2c, keeps_2c, grad_pre, z_2c,
    kept, sent, dz_p, own10, packed, dz_1c, dz_2c,
):
    rows, outer = dz_2b.shape[0], zc.shape[2]
    pixels = 1.0 * rows * (COLS - 4)
    marks, label = labels[...], entry(tab, OWN)
    blocks = outer // LANES
    total = group_sum(got, marks, label)
    lines = wide_lines(total, outer)
    for k in range(2):
        own10[:, outer * k : outer * (k + 1)] = lines[k]
        at = 2 * outer + LANES * k
        own10[:, at : at + LANES] = total[k : k + 1, 3 * outer // 2 :]
    wide = [
        line_of(over_group(get_split(got_2c, 2 * blocks * k, blocks), marks, label)) for k in (0, 1)
    ]
    mean, a, b, c = own_coefs(tab, marks, norm_2c, keeps_2c, pixels, *wide)
    gate = 0.25 * tiled(entry(tab, GATE), outer)
    normed_grad(grad_pre, (dz_2c, z_2c, mean, a * gate, b, c))
    coefs_c = own_coefs(tab, marks, norm_c, keeps.at[0:2], pixels, lines[0], lines[1])
    coefs_p = own_coefs(tab, marks, norm_p, keeps.at[2:4], pixels, lines[0], lines[2])
    normed_grad(grad_pre_2, (dz_1c, zc, *coefs_c), (dz_p, zp, *coefs_p))
    at = put_rows(packed, 0, mm_tn(flat(act_2b[...]), flat(dz_2c[...])))
    low = flat(dz_2b[...])
    for y in range(3):
        at = put_rows(packed, at, mm_side(flat(x3[y : y + rows]), low))
    at = put_rows(packed, at, mm_side(flat(joined[...]), flat(dz_2a[...])))
    at = put_rows(packed, at, mm_tn(flat(act_1b[...]), flat(dz_1c[...])))
    at = put_rows(packed, at, mm_tn(flat(xee[...]), flat(dz_p[...])))
    share_out(tab, packed, at, kept, sent)


def strided_grad(tab, dz_p, w_p, gs_own, gs_oth):
    half = half_of(tab)
    count = gs_own.shape[0]
    for k, gs in enumerate((gs_own, gs_oth)):
        first = count * (half if k == 0 else 1 - half)
        got = mm_nt(flat(dz_p[pl.ds(first, count)]), w_p[...])
        gs[...] = got.reshape(gs.shape).astype(BF16)


def g_xz(keeps, x_own, x_oth, z_own, z_oth, out, x_sum, low, tall):
    rows, n = z_own.shape[0], LANES
    mean = keeps[0:1, :]
    low[:, :, n : 2 * n] = jnp.ones((rows, z_own.shape[1], n), BF16)
    value = None
    for x, z in ((x_own, z_own), (x_oth, z_oth)):

        def put(i, carry, z=z):
            low[i, :, 0:n] = (z[i] - mean).astype(BF16)
            return carry

        lax.fori_loop(0, rows, put, 0, unroll=7)
        term = mm_tn(flat(x[...]), flat(low[...]))
        value = term if value is None else value + term
    at = value.shape[0]
    tall[0:at, :] = value[:, 0:n]
    if at < tall.shape[0]:
        tall[at:, :] = jnp.zeros((tall.shape[0] - at, n), F32)
    out[...] = tall[...].reshape(out.shape).astype(BF16)
    x_sum[...] = value[:, n : 2 * n]


def g_xd(
    tab, sums_own, sums_oth, norm, keeps, x_sum, got_x, labels, x_own, x_oth, dn_own, dn_oth,
    z_own, z_oth, out, sums, low,
):
    rows = dn_own.shape[0]
    n = LANES
    pixels = 1.0 * (2 * rows) * (2 * (COLS - 4))
    sums[...] = sums_own[...] + sums_oth[...]
    a = keeps[1:2, :] * gain_of(norm, entry(tab, OWN))
    local = sums[0:1, :] / pixels
    mean = keeps[0:1, :]
    b = -(a * keeps[1:2, :]) * sums[1:2, :] / pixels
    value = None
    for x, dn, z in ((x_own, dn_own, z_own), (x_oth, dn_oth, z_oth)):

        def put(i, carry, dn=dn, z=z):
            low[i] = (a * (dn[i].astype(F32) - local) + b * (z[i] - mean)).astype(BF16)
            return carry

        lax.fori_loop(0, rows, put, 0, unroll=7)
        term = mm_tn(flat(low[...]), flat(x[...]))
        value = term if value is None else value + term
    value = stack([jnp.transpose(value[:, lanes]) for lanes in columns(value.shape[1])])
    marks, label = labels[...], entry(tab, OWN)
    total = over_group(get_split(got_x, 4, x_sum.shape[0] // n), marks, label)
    total = join([total[k : k + 1] for k in range(total.shape[0])])
    total = total / tiled(group_count(marks, label), total.shape[1])
    total = jnp.broadcast_to(total, (8, total.shape[1]))
    means = jnp.concatenate(
        [jnp.transpose(total[:, lanes])[:, 0:1] for lanes in columns(total.shape[1])], axis=0
    )
    value = value + (x_sum[...] - means) * (a * local)
    at = value.shape[0]
    out[0:at, :] = value.astype(BF16)
    if at < out.shape[0]:
        out[at:, :] = jnp.zeros((out.shape[0] - at, n), BF16)


def pack_last(tall, sums, kept, got, kept_1b, got_1b, xz, send, *, stats_at, part):
    n = LANES
    devices = send.shape[0]
    piece, share = kept.shape[1], tall.shape[0] // devices
    first = kept.shape[0]
    second = first + kept_1b.shape[0]
    send[0:first, 0:piece, :] = (kept[...].astype(F32) + got[...].astype(F32)).astype(BF16)
    send[first:second, 0:piece, :] = (kept_1b[...].astype(F32) + got_1b[...].astype(F32)).astype(BF16)
    if second < devices:
        send[second:, 0:piece, :] = jnp.zeros((devices - second, piece, n), BF16)
    send[:, piece : piece + share, :] = tall[...].reshape(devices, share, n)
    put_split(send, stats_at, sums[...])
    put_part(send, stats_at + 4, xz, part)


def last_sums(stats, marks, groups):
    values = stats[:, 0:2, :].astype(F32) + stats[:, 2:4, :].astype(F32)
    out = []
    for g in range(groups):
        total = jnp.sum(values * (marks == float(g)).astype(F32), axis=0)
        out.append((total[0:1], total[1:2]))
    return out


def add_all(
    got, labels, norm, keeps_all, got_a, got_b, found_2b, found_1b, out, *, at, pixels, parts
):
    devices, n = got.shape[0], LANES
    half = devices // 2
    share = parts[-1][2]
    piece = (out.shape[1] - share - 8) // 2
    marks = labels[...]
    value = jnp.sum(got[:, piece : piece + share, :].astype(F32), axis=0)
    products = get_split(got, at, 2)[:, 1:2, :]
    lack = jnp.zeros(products.shape, F32)
    for g in range(norm.shape[0]):
        rstd = keeps_all[2 * g + 1 : 2 * g + 2, :]
        factor = -(rstd * rstd * norm[g, 0:1, :]) / pixels
        same = (marks == float(g)).astype(F32)
        middle = jnp.sum(products * same, axis=0) / jnp.sum(same, axis=0)
        lack = lack + (middle[None] - products) * (factor[None] * same)
    rows = [
        jnp.sum(source[:, start : start + last - first, :].astype(F32) * lack, axis=0)
        for source, (start, first, last) in zip((got_a, got_b, got), parts)
        if last > first
    ]
    value = value + jnp.concatenate(rows, axis=0)
    for k in (0, 1):
        total = jnp.sum(got[half * k : half * (k + 1), 0:piece, :].astype(F32), axis=0).astype(BF16)
        out[:, piece * k : piece * (k + 1), :] = jnp.broadcast_to(
            total[None], (out.shape[0], piece, n)
        )
    out[:, 2 * piece : 2 * piece + share, :] = jnp.broadcast_to(
        value.astype(BF16)[None], (out.shape[0], share, n)
    )
    put_split(out, 2 * piece + share, stack([found_2b[...], found_1b[...]]))


def place_parts(minor, major, parts, packed, tall, found, piece):
    far, share = parts[0].shape[0], tall.shape[1]
    for k, part in enumerate(parts):
        base = lax.bitwise_xor(minor, jnp.int32(k))

        def place(z, carry, part=part, base=base):
            owner = base + NEAR * lax.bitwise_xor(major, jnp.int32(z))
            for h in (0, 1):
                packed[h, owner] = part[z, piece * h : piece * (h + 1), :]
            tall[owner] = part[z, 2 * piece : 2 * piece + share, :].astype(F32)
            sums = part[z, 2 * piece + share :, :].astype(F32)
            found[owner] = sums[0:4] + sums[4:8]
            return carry

        lax.fori_loop(0, far, place, 0, unroll=min(far, 4))


def stack_parts(*refs):
    for k, ref in enumerate(refs[:-1]):
        refs[-1][k] = ref[0]


def unpack_own(tab, *refs, piece):
    place_parts(half_of(tab, MINOR), half_of(tab, MAJOR), refs[:NEAR], *refs[NEAR:], piece)


def unpack(tab, labels, packed_own, tall_own, found_own, *refs, first, second, piece):
    parts, outs, values = refs[:NEAR], refs[NEAR : NEAR + 9], refs[NEAR + 9 :]
    *values, packed_oth, tall_oth, found_oth, sems = values
    place_parts(half_of(tab, MINOR), half_of(tab, MAJOR), parts, packed_oth, tall_oth, found_oth, piece)
    half = half_of(tab)
    copies = [
        pltpu.make_async_copy(value, out, sems.at[k]) for k, (value, out) in enumerate(zip(values, outs))
    ]
    w_1b, w_1a, *grad_norms = values[5:9]
    own, oth = (packed_own, tall_own, found_own), (packed_oth, tall_oth, found_oth)
    for core in (0, 1):

        @pl.when(half == core)
        def _():
            packed, tall, found = zip(*((own, oth) if core == 0 else (oth, own)))
            most, last = [], []
            for h in (0, 1):
                pieces = [flat(v[h]) for v in packed]
                middle = pieces[0].shape[0]
                cut = first * piece
                most.append((pieces, middle))
                last.append((cut, pieces, middle))

            def span(pieces, middle, at, rows):
                found_rows = []
                if at < middle:
                    found_rows.append(pieces[0][at : min(at + rows, middle)])
                if at + rows > middle:
                    found_rows.append(pieces[1][max(at - middle, 0) : at + rows - middle])
                return [v.astype(F32) for v in found_rows]

            size = first * piece

            def source(at, rows):
                out = []
                if at < size:
                    out += span(*most[0], at, min(rows, size - at))
                if at + rows > size:
                    start = max(at - size, 0)
                    out += span(*most[1], start, at + rows - size - start)
                return out[0] if len(out) == 1 else stack(out)

            starts = [0]
            for value in values[0:4]:
                starts.append(starts[-1] + value.shape[0] * value.shape[1] // LANES)
            for k in (1, 4):
                take_rows(source, starts[k], values[k])
                copies[k].start()
            left = w_1b.shape[0]
            for k, (cut, pieces, middle) in enumerate(last):
                rows = min(second * piece, left)
                lines = span(pieces, middle, cut, rows)
                start = second * piece * k
                w_1b[start : start + rows, :] = lines[0] if len(lines) == 1 else stack(lines)
                left -= rows
            copies[5].start()
            for k in (0, 2, 3):
                take_rows(source, starts[k], values[k])
                copies[k].start()
            lines = stack([flat(v[...]) for v in tall])
            w_1a[...] = lines[0 : w_1a.shape[0]]
            copies[6].start()
            sums = jnp.concatenate([v[...] for v in found], axis=0)
            for k, grad_norm in enumerate(grad_norms):
                norm_from_owners(sums[:, 2 * k : 2 * k + 2, :], labels[...], grad_norm)
                copies[7 + k].start()

    for copy in copies:
        copy.wait()


def norm_from_owners(found, marks, grad_norm):
    for g in range(grad_norm.shape[0]):
        total = over_group(found, marks, float(g)) / group_count(marks, float(g))
        grad_norm[g, 0:1, :] = total[1:2]
        grad_norm[g, 1:2, :] = total[0:1]


def gather(send):
    return lax.all_to_all(send, AXES, 0, 0)


def tie(*values):
    return lax.optimization_barrier(values)


def swap(block):
    return lax.ppermute(block, "rows", [(0, 1), (1, 0)])


def body(
    images, w_1a, w_1b, w_1c, w_1p, w_2a, w_2b, w_2c,
    norm_1a, norm_1b, norm_1c, norm_1p, norm_2a, norm_2b, norm_2c,
    cotangent, group, width, gate,
):
    devices = lax.axis_size("rows") * lax.axis_size("batch")
    place = lax.axis_index(AXES).astype(jnp.int32).reshape(1)
    norms = (norm_1a, norm_1b, norm_1c, norm_1p, norm_2a, norm_2b, norm_2c)
    norm_1a, norm_1b, norm_1c, norm_1p, norm_2a, norm_2b, norm_2c = (
        v.transpose(1, 0, 2) for v in norms
    )
    outer, inputs = w_1c.shape[1], w_1a.shape[0]
    rows = cotangent.shape[1]
    cols_in = 2 * COLS
    n, m = LANES, devices

    def send(stats, channels=LANES):
        return ((m, channels // LANES, stats * LANES), F32)

    def maps(channels, dtype=F32):
        return ((rows, COLS, channels), dtype)

    def scratch(channels, dtype=F32):
        return pltpu.VMEM((rows, COLS, channels), dtype)

    def params(*arrays):
        return [(a.shape, F32) for a in arrays]

    def mean_scale(channels, count=1):
        return ((2 * count, channels), F32)

    wide_in = ((rows, cols_in, inputs), BF16)
    wide_z = ((rows, cols_in, n), F32)
    raw = images.shape
    tab, x_own, x_for, z_own, z_for, s1 = stage(
        functools.partial(f1, batch=devices // 2), [((8, n), F32), wide_in, wide_in, wide_z, wide_z, send(5)],
        [*(pltpu.SMEM(v.shape, jnp.int32) for v in (place, group, width, gate)),
         pltpu.VMEM(raw, BF16), pltpu.VMEM(w_1a.shape, BF16), pltpu.VMEM((8, n), F32),
         pltpu.SemaphoreType.DMA((9,))],
        hbm=(0, 1, 2, 3, 4, 5),
    )(place, group, width, gate, images, w_1a)
    s1, v_1b, v_2b = tie(s1, w_1b, w_2b)
    built = stage(
        prepare,
        [(v, BF16) for v in (
            (3 * n, n), (3 * n, 2 * n), (3 * n, 2 * n), (3 * n, n),
            (2 * n, 2 * n), (2 * n, 4 * n), (2 * n, 3 * n), (n, 3 * n),
        )],
    )(v_1b, v_2b)
    s1, x_for, w_even, w_odd, w_two, w_last, b_even, b_odd, b_two, b_last = tie(s1, x_for, *built)
    x_oth = swap(x_for)
    g1 = gather(s1)
    g1, x_oth = tie(g1, x_oth)
    xee, z_1p, stats_1p = stage(
        f1_strided,
        [maps(inputs, BF16), maps(outer), ((1, inputs + outer), F32)],
        [pltpu.VMEM((inputs // n, rows // 2, cols_in, n), F32)],
    )(tab, x_own, x_oth, w_1p)
    xs, z_1b, s2, labels, k_1a, k_all, z_oth = stage(
        f2,
        [((rows + 1, COLS, 6 * n), BF16), maps(n), send(2 + (inputs + outer) // n),
         ((m, 1, n), F32), mean_scale(n, 2), mean_scale(n, norm_1a.shape[0]), wide_z],
    )(tab, g1, z_own, x_oth, w_1a, norm_1a, w_even, w_odd, stats_1p)
    share = -(-inputs // devices)
    half_in = ((rows, cols_in, n), BF16)
    xz, x_sum = stage(
        g_xz, [((devices, share, n), BF16), ((inputs, n), F32)],
        [pltpu.VMEM((rows, cols_in, 2 * n), BF16), pltpu.VMEM((devices * share, n), F32)],
    )(k_1a, x_own, x_oth, z_own, z_oth)
    s2, xz, x_sum = tie(s2, xz, x_sum)
    g2 = gather(s2)
    share_1 = -(-n // devices)
    p_rows = ((devices, 2 * share_1, n), BF16)
    own_rows = ((devices, 2 * share_1, n), F32)
    wide_rows = outer // n
    p_at = 2 + wide_rows
    xz_3 = p_at + 2 * share_1
    high_3 = -(-xz_3 // 16) * 16
    xz_6 = p_at + 4 * share_1
    high_6 = -(-xz_6 // 8) * 8
    cut_3 = min(share, high_3 - xz_3)
    cut_6 = min(share, cut_3 + high_6 - xz_6)
    act_1b, z_1c, s3, k_1b, k_p, slope_1b, q_1b, p_1b, own_1b = stage(
        functools.partial(f3, share=share_1, part=(0, cut_3)),
        [maps(n, BF16), maps(outer), ((devices, high_3, n), BF16), mean_scale(n),
         mean_scale(outer), maps(n), ((2, n), F32), p_rows, own_rows],
        [scratch(4 * n, BF16), pltpu.VMEM(p_rows[0], BF16)],
    )(tab, g2, labels, z_1b, norm_1b, w_1c, w_1p, xz)
    g3 = gather(s3)
    high = -(-(8 + 2 * share_1) // 16) * 16
    joined, slope, z_2a, s4, k_cp = stage(
        f4,
        [maps(outer, BF16), maps(outer), maps(n), ((devices, high, n), BF16),
         mean_scale(outer, 2)],
    )(tab, g3, labels, z_1c, z_1p, norm_1c, norm_1p, k_p, w_1c, w_2a, p_1b, q_1b)
    g4 = gather(s4)
    x3, z_2b, s5, k_2a = stage(
        f5, [((rows + 2, COLS, 3 * n), BF16), maps(n), send(2), mean_scale(n)]
    )(tab, g4, labels, z_2a, norm_2a, w_two, w_last)
    g5 = gather(s5)
    act_2b, z_2c, s6, k_2b, slope_2b, q_2b, own_2b = stage(
        functools.partial(f6, share=share_1, part=(cut_3, cut_6)),
        [maps(n, BF16), maps(outer), ((devices, high_6, n), BF16), mean_scale(n), maps(n),
         ((2, n), F32), own_rows],
        [scratch(4 * n, BF16), *(pltpu.VMEM(p_rows[0], BF16) for _ in range(2))],
    )(tab, g5, labels, z_2b, norm_2b, w_2c, xz)
    g6 = gather(s6)
    high_7 = -(-(4 * wide_rows + 8 + 2 * share_1) // 16) * 16
    result, grad_pre, s7, k_2c, d_2b = stage(
        functools.partial(b7, share=share_1, p_at=p_at),
        [(cotangent.shape[1:], BF16), maps(outer), ((devices, high_7, n), BF16),
         mean_scale(outer), maps(n)],
        [scratch(outer), scratch(outer, BF16)],
    )(tab, g6, labels, joined, z_2c, norm_2c, w_2c, cotangent[0], slope_2b, z_2b, k_2b, q_2b)
    g7 = gather(s7)
    dz_2b, dout_2a, s9, found_2b = stage(
        functools.partial(b9, share=share_1, p_at=p_at),
        [maps(n, BF16), maps(n), ((devices, high, n), BF16), ((2, n), F32)],
        [pltpu.VMEM((rows + 2, COLS, 3 * n), BF16), scratch(n)],
    )(tab, g7, labels, norm_2c, k_2c, w_2c, g6, act_2b, slope_2b, d_2b, z_2b, norm_2b, k_2b,
      b_two, b_last, z_2a, norm_2a, k_2a, x_sum, g4, g3, own_2b)
    g9 = gather(s9)
    dz_2a, grad_pre_2, s10, d_1b = stage(
        b10,
        [maps(n, BF16), maps(outer), ((devices, 2, 3 * outer // 2 + n), F32), maps(n)],
        [scratch(outer), scratch(outer, BF16)],
    )(tab, g9, labels, dout_2a, z_2a, norm_2a, k_2a, w_2a, grad_pre, slope, z_1c, z_1p, k_cp,
      norm_1c, w_1c, slope_1b, z_1b, k_1b)
    g10 = gather(s10)
    half_map = ((rows // 2, COLS, inputs), BF16)
    most_rows = sum(v.size for v in (w_2c, w_2b, w_2a, w_1c, w_1p)) // n
    rows_1b = w_1b.size // n
    piece = 16
    while -(-most_rows // (2 * piece)) - (-rows_1b // (2 * piece)) > devices:
        piece += 16
    first, second = -(-most_rows // (2 * piece)), -(-rows_1b // (2 * piece))
    part, part_1b = ((first, piece, n), BF16), ((second, piece, n), BF16)
    kept, sent, dz_1p, own10 = stage(
        g_most,
        [part, part, maps(outer, BF16), ((1, 2 * outer + 2 * n), F32)],
        [pltpu.VMEM((2 * first * piece, n), BF16), *(scratch(outer, BF16) for _ in range(2))],
    )(tab, act_2b, x3, dz_2b, joined, dz_2a, act_1b, xee,
      g10, labels, norm_1c, norm_1p, k_cp, grad_pre_2, z_1c, z_1p,
      g7, norm_2c, k_2c, grad_pre, z_2c)
    gs_own, gs_send = stage(strided_grad, [half_map, half_map])(tab, dz_1p, w_1p)
    got, gs_for = swap(sent), swap(gs_send)
    half_in = ((rows, cols_in, n), BF16)
    d2, kept_1b, sent_1b, found_1b = stage(
        functools.partial(b12, share=share_1, q_at=4 + 2 * share_1, p_at=4 + 2 * (inputs // n)),
        [((rows + 1, COLS, 2 * n), BF16), part_1b, part_1b, ((2, n), F32)],
        [scratch(n, BF16), pltpu.VMEM((2 * second * piece, n), BF16), scratch(n)],
    )(tab, own10, labels, norm_1c, k_cp, w_1c, g3, g4, g9, own_1b, act_1b, slope_1b, d_1b,
      z_1b, norm_1b, k_1b, xs)
    got_1b = swap(sent_1b)
    sides = []
    for own, z in ((False, z_oth), (True, z_own)):
        sides.append(
            stage(
                functools.partial(b12_images, own=own), [half_in, ((2, n), F32)],
                [pltpu.VMEM((rows // 2, COLS, 2 * n), F32), pltpu.VMEM((rows // 2, COLS, 2 * n), F32),
                 pltpu.VMEM((rows, cols_in, n), F32)],
            )(tab, d2, b_even, b_odd, z, norm_1a, k_1a)
        )
        if not own:
            dn_for = swap(sides[0][0])
            d2, _ = tie(d2, sides[0][0])
    (dn_send, sums_send), (dn_own, sums_own) = sides
    stats_at = piece + -(-share // 8) * 8
    high = -(-(stats_at + 4 + share - cut_6) // 16) * 16
    tall, sums_1a = stage(
        g_xd, [((devices * share, n), BF16), ((2, n), F32)], [pltpu.VMEM(half_in[0], BF16)]
    )(tab, sums_own, sums_send, norm_1a, k_1a, x_sum, g9, labels, x_own, x_oth, dn_own, dn_send,
      z_own, z_oth)
    tall, gs_for, dn_for = tie(tall, gs_for, dn_for)
    (s12,) = stage(
        functools.partial(pack_last, stats_at=stats_at, part=(cut_6, share)),
        [((devices, high, n), BF16)]
    )(tall, sums_1a, kept, got, kept_1b, got_1b, xz)
    g12 = gather(s12)
    pixels = 4.0 * images.shape[1] * images.shape[1]
    batch = devices // 2
    far = batch // NEAR
    (mine,) = stage(
        functools.partial(
            add_all, at=stats_at, pixels=pixels,
            parts=((xz_3, 0, cut_3), (xz_6, cut_3, cut_6), (stats_at + 4, cut_6, share)),
        ),
        [((1, 2 * piece + share + 8, n), BF16)],
    )(g12, labels, norm_1a, k_all, g3, g6, found_2b, found_1b)
    others = [
        lax.ppermute(mine, "batch", [(i, i ^ (NEAR * k)) for i in range(batch)])
        for k in range(1, far)
    ]
    finished = (result,)
    held = len(finished)
    *finished, grad_images, grad_norm_1a = stage(
        functools.partial(b13, at=stats_at, held=held),
        [*((v.shape, v.dtype) for v in finished), (images.shape, BF16), *params(norm_1a)],
        [pltpu.VMEM(half_in[0], BF16), pltpu.VMEM((inputs // n, rows, cols_in, n), F32),
         pltpu.VMEM(images.shape, BF16), pltpu.VMEM(norm_1a.shape, F32),
         pltpu.SemaphoreType.DMA((held + 5,))],
        hbm_out=range(held + 2),
    )(tab, g12, labels, norm_1a, k_1a, w_1a, z_own, z_for, dn_own, dn_for, gs_own, gs_for, *finished)
    (result,) = finished
    *others, grad_images = tie(*others, grad_images)
    (along,) = stage(stack_parts, [((far, *mine.shape[1:]), BF16)])(mine, *others)
    near = [
        lax.ppermute(along, "batch", [(i, i ^ k) for i in range(batch)]) for k in range(1, NEAR)
    ]
    late, _ = tie(labels, along)
    grad_norms = stage(norm_tail, params(norm_2c, norm_2a, norm_1c, norm_1p))(late, g7, g9, g10)
    grad_norm_2c, *near, grad_norm_2a, grad_norm_1c, grad_norm_1p = tie(
        grad_norms[0], *near, *grad_norms[1:]
    )
    parts = [along, *near]
    weights = (w_2c, w_2b.reshape(-1, n), w_2a, w_1c, w_1p, w_1b.reshape(-1, n), w_1a)
    side = [
        ((2, batch, piece, n), BF16), ((batch, share, n), F32), ((batch, 4, n), F32)
    ]
    crossed = [swap(v) for v in parts]
    placed = stage(functools.partial(unpack_own, piece=piece), side)(tab, *parts)
    t_2c, t_2b, t_2a, t_1c, t_1p, t_1b, t_1a, grad_norm_2b, grad_norm_1b = stage(
        functools.partial(unpack, first=first, second=second, piece=piece),
        [(v.shape, F32) for v in (*weights, norm_2b, norm_1b)],
        [*(pltpu.VMEM(v.shape, F32) for v in (*weights, norm_2b, norm_1b)),
         *(pltpu.VMEM(*v) for v in side), pltpu.SemaphoreType.DMA((9,))],
        hbm_out=range(9),
    )(tab, labels, *placed, *crossed)
    grads = (
        grad_norm_1a, grad_norm_1b, grad_norm_1c, grad_norm_1p,
        grad_norm_2a, grad_norm_2b, grad_norm_2c,
    )
    return (
        result[None], grad_images, t_1a, t_1b.reshape(w_1b.shape), t_1c, t_1p, t_2a,
        t_2b.reshape(w_2b.shape), t_2c, *[v.transpose(1, 0, 2) for v in grads],
    )


def solution(mesh):
    return jax.shard_map(
        body,
        mesh=mesh,
        in_specs=(
            P("batch", "rows", None, None),
            *[P()] * 14,
            P(("batch", "rows"), None, None, None),
            P("batch"),
            P(),
            P(),
        ),
        out_specs=(
            P(("batch", "rows"), None, None, None),
            P("batch", "rows", None, None),
            *[P()] * 14,
        ),
        check_vma=False,
    )
```
